32 devices in a mesh: gy: 4 (over z), gx: 4 (over y, x), gz: 2 (over core).
Axes of the slice: x: 2, y: 2, z: 4, core: 2. Of those that a mesh axis runs over, the one named last changes fastest.
Arguments:
- velocity: float32 [3, 8, 768, 256], P(None, 'gx', 'gy', 'gz'), may hold values from -36 to 36
- tendency: float32 [3, 8, 768, 256], P(None, 'gx', 'gy', 'gz'), may hold values from -6 to 6
Outputs:
- new_velocity: float32 [3, 8, 768, 256], P(None, 'gx', 'gy', 'gz')
- eddy_viscosity: float32 [8, 768, 256], P('gx', 'gy', 'gz')
The draws below stay inside these ranges and needn't reach their ends.
All inputs are finite; a program needn't handle non-finite values.
Results may differ from the reference program's by a relative error of at most 0.0003.
Values sent between devices are 32-bit elements; how exact they have to be, the bound alone decides.
No kernel may reach another device: no remote copies, remote signals or barrier semaphores. Data moves between devices by JAX's collectives and lax.ppermute only.
A program may use at most 128 MiB of HBM per device.

```python
import jax
import jax.numpy as jnp
from jax import lax

CY = 192
NX = 8
NY = 768
NZ = 256
N_GY = 4


def draw_velocity(key, part):
    key = jax.random.fold_in(key, 11)
    key_fluct, key_level, key_mean = jax.random.split(key, 3)
    fluctuation = jax.random.truncated_normal(key_fluct, -4.0, 4.0, (3, NX, NY, NZ), jnp.float32)
    peak_flow = 4.0
    row_level = jnp.exp(jax.random.uniform(key_level, (1, 1, NY, 1), jnp.float32, -0.7, 0.7))
    along_x = 1.0 + 2.0 * jnp.arange(NX, dtype=jnp.float32) / max(NX - 1, 1)
    along_z = 1.0 + 2.0 * jnp.arange(NZ, dtype=jnp.float32) / max(NZ - 1, 1)
    amplitude = jnp.sqrt(along_x[None, :, None, None] * along_z[None, None, None, :])
    height = (2.0 * jnp.arange(NY, dtype=jnp.float32) + 1.0) / NY
    roughness = jax.random.uniform(key_mean, (NY,), jnp.float32, 0.5, 1.5)
    profile = peak_flow * height * (2.0 - height) * roughness
    mean_flow = jnp.zeros((3, 1, NY, 1), jnp.float32).at[0, 0, :, 0].set(profile)
    return fluctuation * row_level * amplitude + mean_flow


def steps_of(own_key, shape, pieces, low, largest):
    factor_of = 1.0
    for dim, shards_of in pieces:
        draws = jax.random.uniform(jax.random.fold_in(jax.random.fold_in(own_key, 6), dim), (shards_of,), jnp.float32, low / len(pieces), largest / len(pieces))
        factor_of = factor_of * jnp.repeat(jnp.exp(draws), shape[dim] // shards_of).reshape((-1,) + (1,) * (len(shape) - 1 - dim))
    return factor_of


def gaussian(key, shape, deviation, reach, pieces=(), kind=jnp.bfloat16):
    values = deviation * jax.random.normal(key, shape, jnp.float32)
    if pieces:
        values = values * steps_of(key, shape, pieces, -0.22, 0.18)
    return jnp.clip(values, -reach, reach).astype(kind)


def setup_inputs(seed: int = 0) -> dict:
    seeds = jax.random.split(jax.random.key(seed), 3)
    velocity = draw_velocity(jax.random.fold_in(seeds[2], 71), 0)
    tendency = gaussian(seeds[1], (3, NX, NY, NZ), 1.0, 6.0, ((1, 4), (2, 4), (3, 2)), jnp.float32)
    return {"velocity": velocity, "tendency": tendency}


def contract(left_tensor, right_tensor):
    diagonal_part = left_tensor[0] * right_tensor[0] + left_tensor[1] * right_tensor[1] + left_tensor[2] * right_tensor[2]
    return diagonal_part + 2.0 * (left_tensor[3] * right_tensor[3] + left_tensor[4] * right_tensor[4] + left_tensor[5] * right_tensor[5])

def products(vectors):
    return jnp.stack([vectors[0] * vectors[0], vectors[1] * vectors[1], vectors[2] * vectors[2], vectors[0] * vectors[1], vectors[0] * vectors[2], vectors[1] * vectors[2]])

def derivatives(extended):
    grad_x = (extended[:, 2:, 1:-1, 1:-1] - extended[:, :-2, 1:-1, 1:-1]) * 0.5
    grad_y = (extended[:, 1:-1, 2:, 1:-1] - extended[:, 1:-1, :-2, 1:-1]) * 0.5
    grad_z = (extended[:, 1:-1, 1:-1, 2:] - extended[:, 1:-1, 1:-1, :-2]) * 0.5
    strain = jnp.stack([grad_x[0], grad_y[1], grad_z[2], 0.5 * (grad_y[0] + grad_x[1]), 0.5 * (grad_z[0] + grad_x[2]), 0.5 * (grad_z[1] + grad_y[2])])
    return (strain, jnp.sqrt(2.0 * contract(strain, strain)))

def build_fields(vectors, strain, magnitude):
    return jnp.concatenate([vectors, products(vectors), strain, magnitude[None] * strain], axis=0)

def test_filter(fields):
    along_x = (fields[:, :-2] + 2.0 * fields[:, 1:-1] + fields[:, 2:]) * 0.25
    return (along_x[..., :-2] + 2.0 * along_x[..., 1:-1] + along_x[..., 2:]) * 0.25

def germano(filtered):
    mean_vel = filtered[0:3]
    mean_prod = filtered[3:9]
    mean_strain = filtered[9:15]
    mean_scaled = filtered[15:21]
    leonard = mean_prod - products(mean_vel)
    filtered_mag = jnp.sqrt(2.0 * contract(mean_strain, mean_strain))
    model_term = 2.0 * (mean_scaled - 4.0 * filtered_mag[None] * mean_strain)
    return (contract(leonard, model_term), contract(model_term, model_term))

def diffusion(visc_ext, vel_ext, tendency):
    upward = 1500.0 * (visc_ext[:, 1:-1] + visc_ext[:, 2:])
    downward = 1500.0 * (visc_ext[:, :-2] + visc_ext[:, 1:-1])
    centre = vel_ext[:, :, 1:-1]
    source = centre + tendency + 0.5 * (upward * (vel_ext[:, :, 2:] - centre) - downward * (centre - vel_ext[:, :, :-2]))
    lower_band = jnp.broadcast_to(-0.5 * downward, centre.shape)
    middle = jnp.broadcast_to(1.0 + 0.5 * (upward + downward), centre.shape)
    higher = jnp.broadcast_to(-0.5 * upward, centre.shape)
    return (lower_band, middle, higher, source)

def reference(velocity, tendency):
    vel_padded = jnp.pad(velocity, ((0, 0), (0, 0), (1, 1), (0, 0)))
    planes = jnp.arange(NX, dtype=jnp.int32)
    slabs = jnp.arange(N_GY, dtype=jnp.int32)

    def first_pass(plane):
        plane_idx = ((plane - 2 + jnp.arange(5, dtype=jnp.int32)) % NX).astype(jnp.int32)
        window_vel = jnp.take(vel_padded, plane_idx, axis=1)
        window_vel = jnp.concatenate([window_vel[..., -2:], window_vel, window_vel[..., :2]], axis=3)

        def slab_pass(slab):
            start_row = (slab * CY).astype(jnp.int32)
            part_vel = lax.dynamic_slice_in_dim(window_vel, start_row, CY + 2, 2)
            strain, magnitude = derivatives(part_vel)
            fields = build_fields(part_vel[:, 1:-1, 1:-1, 1:-1], strain, magnitude)
            leo_model, model_model = germano(test_filter(fields))
            return (lax.optimization_barrier(jnp.sum(leo_model, axis=(0, 2))), lax.optimization_barrier(jnp.sum(model_model, axis=(0, 2))), magnitude[1, :, 1:-1])
        return lax.map(slab_pass, slabs)
    lm_parts, mm_parts, magnitudes = lax.map(first_pass, planes)
    plane_lm = lax.optimization_barrier(jnp.sum(lm_parts, axis=0)).reshape(NY)
    plane_mm = lax.optimization_barrier(jnp.sum(mm_parts, axis=0)).reshape(NY)
    cell_count = NX * NZ
    coefficient = jnp.maximum(plane_lm / cell_count / (plane_mm / cell_count + 1e-06), 0.0)
    blocks = jnp.arange(NX // 2, dtype=jnp.int32)
    mag_blocks = magnitudes.reshape(NX // 2, 2, NY, NZ)

    def second_pass(inputs):
        block_idx, magnitude = inputs
        start_row = (block_idx * 2).astype(jnp.int32)
        vel_block = lax.dynamic_slice_in_dim(velocity, start_row, 2, 1)
        tend_block = lax.dynamic_slice_in_dim(tendency, start_row, 2, 1)
        eddy_visc = coefficient[None, :, None] * magnitude
        visc_ext = jnp.pad(1.0 + eddy_visc, ((0, 0), (1, 1), (0, 0)))
        vel_ext = jnp.pad(vel_block, ((0, 0), (0, 0), (1, 1), (0, 0)))
        lower_band, middle, higher, source = diffusion(visc_ext, vel_ext, tend_block)
        band_low = jnp.moveaxis(lower_band, 2, -1).at[..., 0].set(0.0)
        band_mid = jnp.moveaxis(middle, 2, -1)
        band_high = jnp.moveaxis(higher, 2, -1).at[..., -1].set(0.0)
        solved = lax.linalg.tridiagonal_solve(band_low, band_mid, band_high, jnp.moveaxis(source, 2, -1)[..., None])
        return (jnp.moveaxis(solved[..., 0], -1, 2), eddy_visc)
    solved_blocks, eddy_blocks = lax.map(second_pass, (blocks, mag_blocks))
    solution = jnp.transpose(solved_blocks, (1, 0, 2, 3, 4)).reshape(3, NX, NY, NZ)
    return (solution, eddy_blocks.reshape(NX, NY, NZ))
```

```python
import functools

import jax
import jax.numpy as jnp
from jax import lax
from jax.experimental import pallas as pl
from jax.experimental.pallas import tpu as pltpu
from jax.sharding import PartitionSpec as P

LANES = 128
SEGMENTS = 8
VMEM_BYTES = 24 * 2**20


def strain_parts(centre, below, above):
    nx, nz = centre[0].shape
    grad_x = [pltpu.roll(f, nx - 1, 0) - pltpu.roll(f, 1, 0) for f in centre]
    grad_z = [pltpu.roll(f, nz - 1, 1) - pltpu.roll(f, 1, 1) for f in centre]
    grad_y = [up - down for up, down in zip(above, below)]
    return (
        grad_x[0],
        grad_y[1],
        grad_z[2],
        grad_y[0] + grad_x[1],
        grad_z[0] + grad_x[2],
        grad_z[1] + grad_y[2],
    )


def strain_size(parts):
    diagonal = parts[0] * parts[0] + parts[1] * parts[1] + parts[2] * parts[2]
    mixed = parts[3] * parts[3] + parts[4] * parts[4] + parts[5] * parts[5]
    return jnp.sqrt(0.5 * diagonal + 0.25 * mixed)


def smooth(field):
    field = field + pltpu.roll(field, 1, 0)
    field = field + pltpu.roll(field, 1, 0)
    field = field + pltpu.roll(field, 1, 1)
    return field + pltpu.roll(field, 1, 1)


def products(v):
    return (v[0] * v[0], v[1] * v[1], v[2] * v[2], v[0] * v[1], v[0] * v[2], v[1] * v[2])


def germano_kernel(nz_parts, recv, below, above, out, planes, vel, filt, mag, lm, mm):
    count, _, width, rows, _ = recv.shape
    nx = (count // nz_parts) * width
    nz = nz_parts * LANES
    for k in range(count):
        x0, zb = (k // nz_parts) * width, k % nz_parts
        lanes = slice(zb * LANES, (zb + 1) * LANES)
        for c in range(3):
            for x in range(width):
                planes[c, zb, (x0 + x) * rows : (x0 + x + 1) * rows, :] = recv[k, c, x]
            vel[c, 0, x0 : x0 + width, lanes] = below[k, c]
            vel[c, rows + 1, x0 : x0 + width, lanes] = above[k, c]
    for c in range(3):
        for y in range(rows):
            for zb in range(nz_parts):
                lanes = slice(zb * LANES, (zb + 1) * LANES)
                vel[c, y + 1, :, lanes] = planes[c, zb, pl.ds(y, nx, stride=rows), :]
    for c in range(3):
        for y in range(rows + 2):
            filt[c, y] = smooth(vel[c, y])

    for y in range(rows):
        centre = [vel[c, y + 1] for c in range(3)]
        strain = strain_parts(centre, [vel[c, y] for c in range(3)], [vel[c, y + 2] for c in range(3)])
        size = strain_size(strain)
        for zb in range(nz_parts):
            mag[zb, y * nx : (y + 1) * nx, :] = size[:, zb * LANES : (zb + 1) * LANES]
        mean = [filt[c, y + 1] for c in range(3)]
        mean_strain = strain_parts(mean, [filt[c, y] for c in range(3)], [filt[c, y + 2] for c in range(3)])
        mean_size = 0.25 * strain_size(mean_strain)
        model = [smooth(size * s) - mean_size * f for s, f in zip(strain, mean_strain)]
        scaled = [0.0625 * f for f in mean]
        pairs = (
            (mean[0], scaled[0]),
            (mean[1], scaled[1]),
            (mean[2], scaled[2]),
            (mean[0], scaled[1]),
            (mean[0], scaled[2]),
            (mean[1], scaled[2]),
        )
        leonard = [smooth(p) - f * g for p, (f, g) in zip(products(centre), pairs)]
        left = leonard[0] * model[0]
        for i in range(1, 6):
            left = left + leonard[i] * model[i]
        right = (model[0] * model[0] + model[1] * model[1] + model[2] * model[2]) + 0.5 * (
            model[3] * model[3] + model[4] * model[4] + model[5] * model[5]
        )
        for total, ref in ((left, lm), (right, mm)):
            part = total[:, :LANES]
            for zb in range(1, nz_parts):
                part = part + total[:, zb * LANES : (zb + 1) * LANES]
            ref[y * nx : (y + 1) * nx, :] = part

    def plane_sum(ref):
        part = ref[pl.ds(0, rows, stride=nx), :]
        for x in range(1, nx):
            part = part + ref[pl.ds(x, rows, stride=nx), :]
        return jnp.sum(part, axis=1, keepdims=True) * (1.0 / (256.0 * nx * nz))

    coefficient = jnp.maximum(plane_sum(lm) / (plane_sum(mm) + 1e-06), 0.0)
    for k in range(count):
        x0, zb = (k // nz_parts) * width, k % nz_parts
        for x in range(width):
            out[k, x] = coefficient * mag[zb, pl.ds(x0 + x, rows, stride=nx), :]


def sweep_kernel(back, velocity, tendency, eddy, reduced, factors, tree):
    count, width, rows, _ = back.shape
    length = count * rows // SEGMENTS
    for k in range(count):
        for x in range(width):
            eddy[x, k * rows : (k + 1) * rows, :] = back[k, x]

    def row(ref, index, j):
        return ref[(*index, pl.ds(j, SEGMENTS, stride=length), slice(None))]

    for x in range(width):
        visc = 1.0 + row(eddy, (x,), 0)
        visc_first = visc
        q = jnp.ones_like(visc)
        m = jnp.ones_like(visc)
        corner = jnp.zeros_like(visc)
        first = [jnp.zeros_like(visc)] * 3
        value = None
        for j in range(length):
            if j < length - 1:
                visc_next = 1.0 + row(eddy, (x,), j + 1)
                link = 750.0 * (visc + visc_next)
                inverse = 1.0 / (q + link)
            else:
                visc_next = None
                link = None
                inverse = 1.0 / q
            left = m * inverse
            corner = corner + m * left
            source = [
                2.0 * row(velocity, (c, x), j) + row(tendency, (c, x), j) for c in range(3)
            ]
            if j > 0:
                source = [s + link_before * v for s, v in zip(source, value)]
            value = [s * inverse for s in source]
            first = [f + m * v for f, v in zip(first, value)]
            for c in range(3):
                factors[x, j, c] = value[c]
            factors[x, j, 3] = left
            if j < length - 1:
                ratio = link * inverse
                factors[x, j, 4] = ratio
                q = 1.0 + link * (q * inverse)
                m = m * ratio
                link_before = link
                visc = visc_next
            else:
                factors[x, j, 4] = inverse
        last = value
        across = left
        end = inverse
        links = 750.0 * (visc + pltpu.roll(visc_first, SEGMENTS - 1, 0))
        level, step = 0, 1
        while step < SEGMENTS:
            def other(v):
                return pltpu.roll(v, SEGMENTS - step, 0)

            link = links if step == 1 else pltpu.roll(links, SEGMENTS - (step - 1), 0)
            across_b = other(across)
            stiff = link / (1.0 + link * (end + other(corner)))
            flux = [stiff * (g - other(f)) for g, f in zip(last, first)]
            from_left = stiff * across
            from_right = stiff * across_b
            for c in range(3):
                tree[x, level, c] = flux[c]
            tree[x, level, 3] = from_left
            tree[x, level, 4] = from_right
            first = [f - across * t for f, t in zip(first, flux)]
            last = [other(g) + across_b * t for g, t in zip(last, flux)]
            corner = corner - across * from_left
            end = other(end) - across_b * from_right
            across = from_left * across_b
            level, step = level + 1, step * 2
        rows_out = [*first, *last, corner, across, end, visc_first]
        for i, v in enumerate(rows_out):
            reduced[i * width + x : i * width + x + 1, :] = v[0:1, :]
        i = len(rows_out)
        reduced[i * width + x : i * width + x + 1, :] = visc[SEGMENTS - 1 :, :]


def finish_kernel(devices, position, factors, tree, velocity, *rest):
    reduced, (out, gathered, fluxes) = rest[:devices], rest[devices:]
    width, length = factors.shape[:2]
    here = position[0]
    for shift in range(devices):
        gathered[lax.rem(here - shift + devices, devices)] = reduced[shift][...]

    def part(device, i):
        return gathered[device, i * width : (i + 1) * width, :]

    ratios, values = [], []
    for i in range(devices + 1):
        if i == 0:
            link = 750.0 * part(0, 9)
            total = part(0, 6)
            source = [-part(0, c) for c in range(3)]
        elif i == devices:
            link = 750.0 * part(i - 1, 10)
            total = part(i - 1, 8)
            source = [part(i - 1, 3 + c) for c in range(3)]
        else:
            link = 750.0 * (part(i - 1, 10) + part(i, 9))
            total = part(i - 1, 8) + part(i, 6)
            source = [part(i - 1, 3 + c) - part(i, c) for c in range(3)]
        pivot = 1.0 + link * total
        if i > 0:
            before = part(i - 1, 7)
            pivot = pivot - link * before * ratios[-1]
            source = [s + before * v for s, v in zip(source, values[-1])]
        scale = link / pivot
        values.append([scale * s for s in source])
        if i < devices:
            ratios.append(scale * part(i, 7))
    flux = values[devices]
    for i in range(devices, -1, -1):
        if i < devices:
            flux = [v + ratios[i] * f for v, f in zip(values[i], flux)]
        for c in range(3):
            fluxes[i, c * width : (c + 1) * width, :] = flux[c]

    sublane = lax.broadcasted_iota(jnp.int32, (SEGMENTS, LANES), 0)
    levels = tree.shape[1]
    for x in range(width):
        for c in range(3):
            r = c * width + x
            left = jnp.broadcast_to(fluxes[here, r : r + 1, :], (SEGMENTS, LANES))
            right = -jnp.broadcast_to(fluxes[here + 1, r : r + 1, :], (SEGMENTS, LANES))
            for level in range(levels - 1, -1, -1):
                step = 2**level
                through = tree[x, level, c] + tree[x, level, 3] * left - tree[x, level, 4] * right
                second = lax.rem(sublane, 2 * step) == step
                left = jnp.where(second, pltpu.roll(through, step, 0), left)
                right = jnp.where(second, pltpu.roll(right, step, 0), -through)
            value = right
            for j in range(length - 1, -1, -1):
                value = (factors[x, j, c] + factors[x, j, 3] * left) + factors[x, j, 4] * value
                rows = pl.ds(j, SEGMENTS, stride=length)
                out[c, x, rows, :] = value - velocity[c, x, rows, :]


def in_vmem(count):
    return [pl.BlockSpec(memory_space=pltpu.VMEM)] * count


def params():
    return pltpu.CompilerParams(vmem_limit_bytes=VMEM_BYTES)


def body(velocity, tendency):
    _, width, cells, lanes = velocity.shape
    nz_parts = lax.axis_size("gz")
    count = lax.axis_size("gx") * nz_parts
    walls = lax.axis_size("gy")
    rows = cells // count
    nx = lax.axis_size("gx") * width
    nz = nz_parts * lanes
    f32 = jnp.float32

    chunks = velocity.reshape(3, width, count, rows, lanes).transpose(2, 0, 1, 3, 4)
    recv = lax.all_to_all(chunks, ("gx", "gz"), split_axis=0, concat_axis=0, tiled=True)
    total = walls * count
    everyone = ("gy", "gx", "gz")
    below = lax.ppermute(recv[:, :, :, rows - 1], everyone, [(i, i + 1) for i in range(total - 1)])
    above = lax.ppermute(recv[:, :, :, 0], everyone, [(i + 1, i) for i in range(total - 1)])
    eddy_chunks = pl.pallas_call(
        functools.partial(germano_kernel, nz_parts),
        out_shape=jax.ShapeDtypeStruct((count, width, rows, lanes), f32),
        in_specs=in_vmem(3),
        out_specs=pl.BlockSpec(memory_space=pltpu.VMEM),
        scratch_shapes=[
            pltpu.VMEM((3, nz_parts, nx * rows, lanes), f32),
            pltpu.VMEM((3, rows + 2, nx, nz), f32),
            pltpu.VMEM((3, rows + 2, nx, nz), f32),
            pltpu.VMEM((nz_parts, rows * nx, lanes), f32),
            pltpu.VMEM((rows * nx, lanes), f32),
            pltpu.VMEM((rows * nx, lanes), f32),
        ],
        compiler_params=params(),
        name="germano",
    )(recv, below, above)
    back = lax.all_to_all(eddy_chunks, ("gx", "gz"), split_axis=0, concat_axis=0, tiled=True)

    length = cells // SEGMENTS
    levels = SEGMENTS.bit_length() - 1
    packed = -(-11 * width // 8) * 8
    eddy, reduced, factors, tree = pl.pallas_call(
        sweep_kernel,
        out_shape=(
            jax.ShapeDtypeStruct((width, cells, lanes), f32),
            jax.ShapeDtypeStruct((packed, lanes), f32),
            jax.ShapeDtypeStruct((width, length, 5, SEGMENTS, lanes), f32),
            jax.ShapeDtypeStruct((width, levels, 5, SEGMENTS, lanes), f32),
        ),
        in_specs=in_vmem(3),
        out_specs=tuple(in_vmem(4)),
        compiler_params=params(),
        name="sweep",
    )(back, velocity, tendency)

    others = [
        lax.ppermute(reduced, "gy", [(i, (i + shift) % walls) for i in range(walls)])
        for shift in range(1, walls)
    ]
    position = lax.axis_index("gy").astype(jnp.int32).reshape(1)
    new_velocity = pl.pallas_call(
        functools.partial(finish_kernel, walls),
        out_shape=jax.ShapeDtypeStruct(velocity.shape, f32),
        in_specs=[pl.BlockSpec(memory_space=pltpu.SMEM)] + in_vmem(3 + walls),
        out_specs=pl.BlockSpec(memory_space=pltpu.VMEM),
        scratch_shapes=[
            pltpu.VMEM((walls, packed, lanes), f32),
            pltpu.VMEM((walls + 1, -(-3 * width // 8) * 8, lanes), f32),
        ],
        compiler_params=params(),
        name="finish",
    )(position, factors, tree, velocity, reduced, *others)
    return (new_velocity, eddy)


def solution(mesh):
    return jax.shard_map(
        body,
        mesh=mesh,
        in_specs=(P(None, "gx", "gy", "gz"), P(None, "gx", "gy", "gz")),
        out_specs=(P(None, "gx", "gy", "gz"), P("gx", "gy", "gz")),
        check_vma=False,
    )
```

```python
import functools

import jax
import jax.numpy as jnp
from jax import lax
from jax.experimental import pallas as pl
from jax.experimental.pallas import tpu as pltpu
from jax.sharding import PartitionSpec as P

LANES = 128
SEGMENTS = 8
VMEM_BYTES = 24 * 2**20


def strain_parts(grad_x, grad_y, grad_z):
    return (
        grad_x[0],
        grad_y[1],
        grad_z[2],
        grad_y[0] + grad_x[1],
        grad_z[0] + grad_x[2],
        grad_z[1] + grad_y[2],
    )


def strain_size(parts):
    diagonal = parts[0] * parts[0] + parts[1] * parts[1] + parts[2] * parts[2]
    mixed = parts[3] * parts[3] + parts[4] * parts[4] + parts[5] * parts[5]
    return jnp.sqrt(0.5 * diagonal + 0.25 * mixed)


def beside(blocks):
    count = len(blocks)
    lanes = blocks[0].shape[1]
    down = [pltpu.roll(f, 1, 1) for f in blocks]
    up = [pltpu.roll(f, lanes - 1, 1) for f in blocks]
    if count > 1:
        lane = lax.broadcasted_iota(jnp.int32, blocks[0].shape, 1)
        first, last = lane == 0, lane == lanes - 1
        down, up = (
            [jnp.where(first, down[i - 1], down[i]) for i in range(count)],
            [jnp.where(last, up[(i + 1) % count], up[i]) for i in range(count)],
        )
    return down, up


def slope_z(blocks):
    down, up = beside(blocks)
    return [u - d for u, d in zip(up, down)]


def smooth_z(blocks):
    down, up = beside(blocks)
    return [(u + d) + 2.0 * f for f, u, d in zip(blocks, up, down)]


def products(v):
    return (v[0] * v[0], v[1] * v[1], v[2] * v[2], v[0] * v[1], v[0] * v[2], v[1] * v[2])


def germano_kernel(nz_parts, recv, below, above, out, vel, filt, ends, mag, part):
    count, _, width, rows, lanes = recv.shape
    nx = (count // nz_parts) * width
    nz = nz_parts * lanes
    blocks = range(nz_parts)
    lead = 8
    inner = slice(lead, lead + rows)
    lower = slice(lead - 1, lead - 1 + rows)
    upper = slice(lead + 1, lead + 1 + rows)
    for k in range(count):
        x0, zb = (k // nz_parts) * width, k % nz_parts
        for c in range(3):
            for x in range(width):
                vel[c, x0 + x, zb, inner, :] = recv[k, c, x]
                for i, (ref, at) in enumerate(((below, lead - 1), (above, lead + rows))):
                    edge = ref[k, c, x : x + 1, :]
                    vel[c, x0 + x, zb, at : at + 1, :] = edge
                    ends[c, x0 + x, zb, i : i + 1, :] = edge

    for x in range(nx):
        left, right = (x - 1) % nx, (x + 1) % nx
        centre = [[vel[c, x, zb, inner, :] for zb in blocks] for c in range(3)]
        grad_x = [[vel[c, right, zb, inner, :] - vel[c, left, zb, inner, :] for zb in blocks] for c in range(3)]
        grad_y = [[vel[c, x, zb, upper, :] - vel[c, x, zb, lower, :] for zb in blocks] for c in range(3)]
        grad_z = []
        for c in range(3):
            down, up = beside(centre[c])
            grad_z.append([u - d for u, d in zip(up, down)])
            for zb in blocks:
                part[c, x, zb] = (up[zb] + down[zb]) + 2.0 * centre[c][zb]
        strain = [
            strain_parts(*([g[c][zb] for c in range(3)] for g in (grad_x, grad_y, grad_z)))
            for zb in blocks
        ]
        size = [strain_size(s) for s in strain]
        for zb in blocks:
            mag[x, zb] = size[zb]
        pairs = [products([centre[c][zb] for c in range(3)]) for zb in blocks]
        for i in range(6):
            for base, fields in (
                (3, [pairs[zb][i] for zb in blocks]),
                (9, [size[zb] * strain[zb][i] for zb in blocks]),
            ):
                for zb, f in enumerate(smooth_z(fields)):
                    part[base + i, x, zb] = f

    def smooth_x(read, x):
        return (read((x - 1) % nx) + read((x + 1) % nx)) + 2.0 * read(x)

    for c in range(3):
        rims = []
        for x in range(nx):
            rims.append(smooth_z([ends[c, x, zb] for zb in blocks]))
        for x in range(nx):
            for zb in blocks:
                rim = smooth_x(lambda at: rims[at][zb], x)
                filt[c, x, zb, lead - 1 : lead, :] = rim[0:1, :]
                filt[c, x, zb, lead + rows : lead + rows + 1, :] = rim[1:2, :]
                filt[c, x, zb, inner, :] = smooth_x(lambda at: part[c, at, zb], x)

    sum_lm = sum_mm = None
    for x in range(nx):
        left, right = (x - 1) % nx, (x + 1) % nx
        mean = [[filt[c, x, zb, inner, :] for zb in blocks] for c in range(3)]
        grad_x = [[filt[c, right, zb, inner, :] - filt[c, left, zb, inner, :] for zb in blocks] for c in range(3)]
        grad_y = [[filt[c, x, zb, upper, :] - filt[c, x, zb, lower, :] for zb in blocks] for c in range(3)]
        grad_z = [slope_z(mean[c]) for c in range(3)]
        for zb in blocks:
            strain = strain_parts(*([g[c][zb] for c in range(3)] for g in (grad_x, grad_y, grad_z)))
            size = 0.25 * strain_size(strain)
            v = [mean[c][zb] for c in range(3)]
            scaled = [0.0625 * f for f in v]
            pairs = (
                v[0] * scaled[0],
                v[1] * scaled[1],
                v[2] * scaled[2],
                v[0] * scaled[1],
                v[0] * scaled[2],
                v[1] * scaled[2],
            )
            lm = mm = None
            for i in range(6):
                leonard = smooth_x(lambda at: part[3 + i, at, zb], x) - pairs[i]
                model = smooth_x(lambda at: part[9 + i, at, zb], x) - size * strain[i]
                square = model * model if i < 3 else (0.5 * model) * model
                lm = leonard * model if lm is None else lm + leonard * model
                mm = square if mm is None else mm + square
            sum_lm = lm if sum_lm is None else sum_lm + lm
            sum_mm = mm if sum_mm is None else sum_mm + mm

    def plane_mean(total):
        return jnp.sum(total, axis=1, keepdims=True) * (1.0 / (256.0 * nx * nz))

    coefficient = jnp.maximum(plane_mean(sum_lm) / (plane_mean(sum_mm) + 1e-06), 0.0)
    for k in range(count):
        x0, zb = (k // nz_parts) * width, k % nz_parts
        for x in range(width):
            out[k, x] = coefficient * mag[x0 + x, zb]


def sweep_kernel(back, velocity, tendency, eddy, reduced, factors, tree):
    count, width, rows, _ = back.shape
    length = count * rows // SEGMENTS
    for k in range(count):
        for x in range(width):
            eddy[x, k * rows : (k + 1) * rows, :] = back[k, x]

    def row(ref, index, j):
        return ref[(*index, pl.ds(j, SEGMENTS, stride=length), slice(None))]

    for x in range(width):
        visc = 1.0 + row(eddy, (x,), 0)
        visc_first = visc
        q = jnp.ones_like(visc)
        m = jnp.ones_like(visc)
        corner = jnp.zeros_like(visc)
        first = [jnp.zeros_like(visc)] * 3
        value = None
        for j in range(length):
            if j < length - 1:
                visc_next = 1.0 + row(eddy, (x,), j + 1)
                link = 750.0 * (visc + visc_next)
                inverse = 1.0 / (q + link)
            else:
                visc_next = None
                link = None
                inverse = 1.0 / q
            left = m * inverse
            corner = corner + m * left
            source = [
                2.0 * row(velocity, (c, x), j) + row(tendency, (c, x), j) for c in range(3)
            ]
            if j > 0:
                source = [s + link_before * v for s, v in zip(source, value)]
            value = [s * inverse for s in source]
            first = [f + m * v for f, v in zip(first, value)]
            for c in range(3):
                factors[x, j, c] = value[c]
            factors[x, j, 3] = left
            if j < length - 1:
                ratio = link * inverse
                factors[x, j, 4] = ratio
                q = 1.0 + link * (q * inverse)
                m = m * ratio
                link_before = link
                visc = visc_next
            else:
                factors[x, j, 4] = inverse
        last = value
        across = left
        end = inverse
        links = 750.0 * (visc + pltpu.roll(visc_first, SEGMENTS - 1, 0))
        level, step = 0, 1
        while step < SEGMENTS:
            def other(v):
                return pltpu.roll(v, SEGMENTS - step, 0)

            link = links if step == 1 else pltpu.roll(links, SEGMENTS - (step - 1), 0)
            across_b = other(across)
            stiff = link / (1.0 + link * (end + other(corner)))
            flux = [stiff * (g - other(f)) for g, f in zip(last, first)]
            from_left = stiff * across
            from_right = stiff * across_b
            for c in range(3):
                tree[x, level, c] = flux[c]
            tree[x, level, 3] = from_left
            tree[x, level, 4] = from_right
            first = [f - across * t for f, t in zip(first, flux)]
            last = [other(g) + across_b * t for g, t in zip(last, flux)]
            corner = corner - across * from_left
            end = other(end) - across_b * from_right
            across = from_left * across_b
            level, step = level + 1, step * 2
        rows_out = [*first, *last, corner, across, end, visc_first]
        for i, v in enumerate(rows_out):
            reduced[i * width + x : i * width + x + 1, :] = v[0:1, :]
        i = len(rows_out)
        reduced[i * width + x : i * width + x + 1, :] = visc[SEGMENTS - 1 :, :]


def finish_kernel(devices, position, factors, tree, velocity, *rest):
    reduced, (out, gathered, fluxes) = rest[:devices], rest[devices:]
    width, length = factors.shape[:2]
    here = position[0]
    for shift in range(devices):
        gathered[lax.rem(here - shift + devices, devices)] = reduced[shift][...]

    def part(device, i):
        return gathered[device, i * width : (i + 1) * width, :]

    ratios, values = [], []
    for i in range(devices + 1):
        if i == 0:
            link = 750.0 * part(0, 9)
            total = part(0, 6)
            source = [-part(0, c) for c in range(3)]
        elif i == devices:
            link = 750.0 * part(i - 1, 10)
            total = part(i - 1, 8)
            source = [part(i - 1, 3 + c) for c in range(3)]
        else:
            link = 750.0 * (part(i - 1, 10) + part(i, 9))
            total = part(i - 1, 8) + part(i, 6)
            source = [part(i - 1, 3 + c) - part(i, c) for c in range(3)]
        pivot = 1.0 + link * total
        if i > 0:
            before = part(i - 1, 7)
            pivot = pivot - link * before * ratios[-1]
            source = [s + before * v for s, v in zip(source, values[-1])]
        scale = link / pivot
        values.append([scale * s for s in source])
        if i < devices:
            ratios.append(scale * part(i, 7))
    flux = values[devices]
    for i in range(devices, -1, -1):
        if i < devices:
            flux = [v + ratios[i] * f for v, f in zip(values[i], flux)]
        for c in range(3):
            fluxes[i, c * width : (c + 1) * width, :] = flux[c]

    sublane = lax.broadcasted_iota(jnp.int32, (SEGMENTS, LANES), 0)
    levels = tree.shape[1]
    for x in range(width):
        for c in range(3):
            r = c * width + x
            left = jnp.broadcast_to(fluxes[here, r : r + 1, :], (SEGMENTS, LANES))
            right = -jnp.broadcast_to(fluxes[here + 1, r : r + 1, :], (SEGMENTS, LANES))
            for level in range(levels - 1, -1, -1):
                step = 2**level
                through = tree[x, level, c] + tree[x, level, 3] * left - tree[x, level, 4] * right
                second = lax.rem(sublane, 2 * step) == step
                left = jnp.where(second, pltpu.roll(through, step, 0), left)
                right = jnp.where(second, pltpu.roll(right, step, 0), -through)
            value = right
            for j in range(length - 1, -1, -1):
                value = (factors[x, j, c] + factors[x, j, 3] * left) + factors[x, j, 4] * value
                rows = pl.ds(j, SEGMENTS, stride=length)
                out[c, x, rows, :] = value - velocity[c, x, rows, :]


def in_vmem(count):
    return [pl.BlockSpec(memory_space=pltpu.VMEM)] * count


def params():
    return pltpu.CompilerParams(vmem_limit_bytes=VMEM_BYTES)


def body(velocity, tendency):
    _, width, cells, lanes = velocity.shape
    nz_parts = lax.axis_size("gz")
    count = lax.axis_size("gx") * nz_parts
    walls = lax.axis_size("gy")
    rows = cells // count
    nx = lax.axis_size("gx") * width
    padded = 16 + -(-rows // 8) * 8
    f32 = jnp.float32

    chunks = velocity.reshape(3, width, count, rows, lanes).transpose(2, 0, 1, 3, 4)
    recv = lax.all_to_all(chunks, ("gx", "gz"), split_axis=0, concat_axis=0, tiled=True)
    total = walls * count
    everyone = ("gy", "gx", "gz")
    below = lax.ppermute(recv[:, :, :, rows - 1], everyone, [(i, i + 1) for i in range(total - 1)])
    above = lax.ppermute(recv[:, :, :, 0], everyone, [(i + 1, i) for i in range(total - 1)])
    eddy_chunks = pl.pallas_call(
        functools.partial(germano_kernel, nz_parts),
        out_shape=jax.ShapeDtypeStruct((count, width, rows, lanes), f32),
        in_specs=in_vmem(3),
        out_specs=pl.BlockSpec(memory_space=pltpu.VMEM),
        scratch_shapes=[
            pltpu.VMEM((3, nx, nz_parts, padded, lanes), f32),
            pltpu.VMEM((3, nx, nz_parts, padded, lanes), f32),
            pltpu.VMEM((3, nx, nz_parts, 8, lanes), f32),
            pltpu.VMEM((nx, nz_parts, rows, lanes), f32),
            pltpu.VMEM((15, nx, nz_parts, rows, lanes), f32),
        ],
        compiler_params=params(),
        name="germano",
    )(recv, below, above)
    back = lax.all_to_all(eddy_chunks, ("gx", "gz"), split_axis=0, concat_axis=0, tiled=True)

    length = cells // SEGMENTS
    levels = SEGMENTS.bit_length() - 1
    packed = -(-11 * width // 8) * 8
    eddy, reduced, factors, tree = pl.pallas_call(
        sweep_kernel,
        out_shape=(
            jax.ShapeDtypeStruct((width, cells, lanes), f32),
            jax.ShapeDtypeStruct((packed, lanes), f32),
            jax.ShapeDtypeStruct((width, length, 5, SEGMENTS, lanes), f32),
            jax.ShapeDtypeStruct((width, levels, 5, SEGMENTS, lanes), f32),
        ),
        in_specs=in_vmem(3),
        out_specs=tuple(in_vmem(4)),
        compiler_params=params(),
        name="sweep",
    )(back, velocity, tendency)

    others = [
        lax.ppermute(reduced, "gy", [(i, (i + shift) % walls) for i in range(walls)])
        for shift in range(1, walls)
    ]
    position = lax.axis_index("gy").astype(jnp.int32).reshape(1)
    new_velocity = pl.pallas_call(
        functools.partial(finish_kernel, walls),
        out_shape=jax.ShapeDtypeStruct(velocity.shape, f32),
        in_specs=[pl.BlockSpec(memory_space=pltpu.SMEM)] + in_vmem(3 + walls),
        out_specs=pl.BlockSpec(memory_space=pltpu.VMEM),
        scratch_shapes=[
            pltpu.VMEM((walls, packed, lanes), f32),
            pltpu.VMEM((walls + 1, -(-3 * width // 8) * 8, lanes), f32),
        ],
        compiler_params=params(),
        name="finish",
    )(position, factors, tree, velocity, reduced, *others)
    return (new_velocity, eddy)


def solution(mesh):
    return jax.shard_map(
        body,
        mesh=mesh,
        in_specs=(P(None, "gx", "gy", "gz"), P(None, "gx", "gy", "gz")),
        out_specs=(P(None, "gx", "gy", "gz"), P("gx", "gy", "gz")),
        check_vma=False,
    )
```

```python
import functools

import jax
import jax.numpy as jnp
from jax import lax
from jax.experimental import pallas as pl
from jax.experimental.pallas import tpu as pltpu
from jax.sharding import PartitionSpec as P

LANES = 128
SEGMENTS = 8
VMEM_BYTES = 24 * 2**20


def strain_parts(grad_x, grad_y, grad_z):
    return (
        grad_x[0],
        grad_y[1],
        grad_z[2],
        grad_y[0] + grad_x[1],
        grad_z[0] + grad_x[2],
        grad_z[1] + grad_y[2],
    )


def strain_size(parts):
    diagonal = parts[0] * parts[0] + parts[1] * parts[1] + parts[2] * parts[2]
    mixed = parts[3] * parts[3] + parts[4] * parts[4] + parts[5] * parts[5]
    return jnp.sqrt(0.5 * diagonal + 0.25 * mixed)


def beside(blocks):
    count = len(blocks)
    lanes = blocks[0].shape[1]
    down = [pltpu.roll(f, 1, 1) for f in blocks]
    up = [pltpu.roll(f, lanes - 1, 1) for f in blocks]
    if count > 1:
        lane = lax.broadcasted_iota(jnp.int32, blocks[0].shape, 1)
        first, last = lane == 0, lane == lanes - 1
        down, up = (
            [jnp.where(first, down[i - 1], down[i]) for i in range(count)],
            [jnp.where(last, up[(i + 1) % count], up[i]) for i in range(count)],
        )
    return down, up


def slope_z(blocks):
    down, up = beside(blocks)
    return [u - d for u, d in zip(up, down)]


def smooth_z(blocks):
    down, up = beside(blocks)
    return [(u + d) + 2.0 * f for f, u, d in zip(blocks, up, down)]


def products(v):
    return (v[0] * v[0], v[1] * v[1], v[2] * v[2], v[0] * v[1], v[0] * v[2], v[1] * v[2])


def row_order(count):
    return [0, count - 1, *range(1, count - 1)]


def pack_kernel(rows, velocity, out):
    _, width, cells, _ = velocity.shape
    count, depth, lanes = out.shape
    planes = 3 * width
    for rank, place in enumerate(row_order(count)):
        first = place * rows
        before = max(first - 1, 0)
        after = min(first + rows, cells - 1)
        for i in range(planes):
            c, x = divmod(i, width)
            out[rank, i * rows : (i + 1) * rows, :] = velocity[c, x, first : first + rows, :]
            at = planes * rows + i
            out[rank, at : at + 1, :] = velocity[c, x, before : before + 1, :]
            at += planes
            out[rank, at : at + 1, :] = velocity[c, x, after : after + 1, :]
        filled = planes * (rows + 2)
        if filled < depth:
            out[rank, filled:, :] = jnp.zeros((depth - filled, lanes), jnp.float32)


def germano_kernel(nz_parts, width, rows, rank, recv, swapped, out, vel, filt, ends, mag, part):
    count, _, lanes = recv.shape
    planes = 3 * width
    outer = (rank[0] == 0, rank[0] == 1)
    nx = (count // nz_parts) * width
    nz = nz_parts * lanes
    blocks = range(nz_parts)
    lead = 8
    inner = slice(lead, lead + rows)
    lower = slice(lead - 1, lead - 1 + rows)
    upper = slice(lead + 1, lead + 1 + rows)
    for k in range(count):
        x0, zb = (k // nz_parts) * width, k % nz_parts
        for c in range(3):
            for x in range(width):
                i = c * width + x
                vel[c, x0 + x, zb, inner, :] = recv[k, i * rows : (i + 1) * rows, :]
                for side, at in ((0, lead - 1), (1, lead + rows)):
                    own = planes * rows + side * planes + i
                    far = (1 - side) * planes + i
                    edge = jnp.where(outer[side], swapped[k, far : far + 1, :], recv[k, own : own + 1, :])
                    vel[c, x0 + x, zb, at : at + 1, :] = edge
                    ends[c, x0 + x, zb, side : side + 1, :] = edge

    for x in range(nx):
        left, right = (x - 1) % nx, (x + 1) % nx
        centre = [[vel[c, x, zb, inner, :] for zb in blocks] for c in range(3)]
        grad_x = [[vel[c, right, zb, inner, :] - vel[c, left, zb, inner, :] for zb in blocks] for c in range(3)]
        grad_y = [[vel[c, x, zb, upper, :] - vel[c, x, zb, lower, :] for zb in blocks] for c in range(3)]
        grad_z = []
        for c in range(3):
            down, up = beside(centre[c])
            grad_z.append([u - d for u, d in zip(up, down)])
            for zb in blocks:
                part[c, x, zb] = (up[zb] + down[zb]) + 2.0 * centre[c][zb]
        strain = [
            strain_parts(*([g[c][zb] for c in range(3)] for g in (grad_x, grad_y, grad_z)))
            for zb in blocks
        ]
        size = [strain_size(s) for s in strain]
        for zb in blocks:
            mag[x, zb] = size[zb]
        pairs = [products([centre[c][zb] for c in range(3)]) for zb in blocks]
        for i in range(6):
            for base, fields in (
                (3, [pairs[zb][i] for zb in blocks]),
                (9, [size[zb] * strain[zb][i] for zb in blocks]),
            ):
                for zb, f in enumerate(smooth_z(fields)):
                    part[base + i, x, zb] = f

    def smooth_x(read, x):
        return (read((x - 1) % nx) + read((x + 1) % nx)) + 2.0 * read(x)

    for c in range(3):
        rims = []
        for x in range(nx):
            rims.append(smooth_z([ends[c, x, zb] for zb in blocks]))
        for x in range(nx):
            for zb in blocks:
                rim = smooth_x(lambda at: rims[at][zb], x)
                filt[c, x, zb, lead - 1 : lead, :] = rim[0:1, :]
                filt[c, x, zb, lead + rows : lead + rows + 1, :] = rim[1:2, :]
                filt[c, x, zb, inner, :] = smooth_x(lambda at: part[c, at, zb], x)

    sum_lm = sum_mm = None
    for x in range(nx):
        left, right = (x - 1) % nx, (x + 1) % nx
        mean = [[filt[c, x, zb, inner, :] for zb in blocks] for c in range(3)]
        grad_x = [[filt[c, right, zb, inner, :] - filt[c, left, zb, inner, :] for zb in blocks] for c in range(3)]
        grad_y = [[filt[c, x, zb, upper, :] - filt[c, x, zb, lower, :] for zb in blocks] for c in range(3)]
        grad_z = [slope_z(mean[c]) for c in range(3)]
        for zb in blocks:
            strain = strain_parts(*([g[c][zb] for c in range(3)] for g in (grad_x, grad_y, grad_z)))
            size = 0.25 * strain_size(strain)
            v = [mean[c][zb] for c in range(3)]
            scaled = [0.0625 * f for f in v]
            pairs = (
                v[0] * scaled[0],
                v[1] * scaled[1],
                v[2] * scaled[2],
                v[0] * scaled[1],
                v[0] * scaled[2],
                v[1] * scaled[2],
            )
            lm = mm = None
            for i in range(6):
                leonard = smooth_x(lambda at: part[3 + i, at, zb], x) - pairs[i]
                model = smooth_x(lambda at: part[9 + i, at, zb], x) - size * strain[i]
                square = model * model if i < 3 else (0.5 * model) * model
                lm = leonard * model if lm is None else lm + leonard * model
                mm = square if mm is None else mm + square
            sum_lm = lm if sum_lm is None else sum_lm + lm
            sum_mm = mm if sum_mm is None else sum_mm + mm

    def plane_mean(total):
        return jnp.sum(total, axis=1, keepdims=True) * (1.0 / (256.0 * nx * nz))

    coefficient = jnp.maximum(plane_mean(sum_lm) / (plane_mean(sum_mm) + 1e-06), 0.0)
    for k in range(count):
        x0, zb = (k // nz_parts) * width, k % nz_parts
        for x in range(width):
            out[k, x] = coefficient * mag[x0 + x, zb]


def sweep_kernel(back, velocity, tendency, eddy, reduced, factors, tree):
    count, width, rows, _ = back.shape
    length = count * rows // SEGMENTS
    for k, place in enumerate(row_order(count)):
        for x in range(width):
            eddy[x, place * rows : (place + 1) * rows, :] = back[k, x]

    def row(ref, index, j):
        return ref[(*index, pl.ds(j, SEGMENTS, stride=length), slice(None))]

    for x in range(width):
        visc = 1.0 + row(eddy, (x,), 0)
        visc_first = visc
        q = jnp.ones_like(visc)
        m = jnp.ones_like(visc)
        corner = jnp.zeros_like(visc)
        first = [jnp.zeros_like(visc)] * 3
        value = None
        for j in range(length):
            if j < length - 1:
                visc_next = 1.0 + row(eddy, (x,), j + 1)
                link = 750.0 * (visc + visc_next)
                inverse = 1.0 / (q + link)
            else:
                visc_next = None
                link = None
                inverse = 1.0 / q
            left = m * inverse
            corner = corner + m * left
            source = [
                2.0 * row(velocity, (c, x), j) + row(tendency, (c, x), j) for c in range(3)
            ]
            if j > 0:
                source = [s + link_before * v for s, v in zip(source, value)]
            value = [s * inverse for s in source]
            first = [f + m * v for f, v in zip(first, value)]
            for c in range(3):
                factors[x, j, c] = value[c]
            factors[x, j, 3] = left
            if j < length - 1:
                ratio = link * inverse
                factors[x, j, 4] = ratio
                q = 1.0 + link * (q * inverse)
                m = m * ratio
                link_before = link
                visc = visc_next
            else:
                factors[x, j, 4] = inverse
        last = value
        across = left
        end = inverse
        links = 750.0 * (visc + pltpu.roll(visc_first, SEGMENTS - 1, 0))
        level, step = 0, 1
        while step < SEGMENTS:
            def other(v):
                return pltpu.roll(v, SEGMENTS - step, 0)

            link = links if step == 1 else pltpu.roll(links, SEGMENTS - (step - 1), 0)
            across_b = other(across)
            stiff = link / (1.0 + link * (end + other(corner)))
            flux = [stiff * (g - other(f)) for g, f in zip(last, first)]
            from_left = stiff * across
            from_right = stiff * across_b
            for c in range(3):
                tree[x, level, c] = flux[c]
            tree[x, level, 3] = from_left
            tree[x, level, 4] = from_right
            first = [f - across * t for f, t in zip(first, flux)]
            last = [other(g) + across_b * t for g, t in zip(last, flux)]
            corner = corner - across * from_left
            end = other(end) - across_b * from_right
            across = from_left * across_b
            level, step = level + 1, step * 2
        rows_out = [*first, *last, corner, across, end, visc_first]
        for i, v in enumerate(rows_out):
            reduced[i * width + x : i * width + x + 1, :] = v[0:1, :]
        i = len(rows_out)
        reduced[i * width + x : i * width + x + 1, :] = visc[SEGMENTS - 1 :, :]


def finish_kernel(devices, position, factors, tree, velocity, *rest):
    reduced, (out, gathered, fluxes) = rest[:devices], rest[devices:]
    width, length = factors.shape[:2]
    here = position[0]
    for shift in range(devices):
        gathered[lax.rem(here - shift + devices, devices)] = reduced[shift][...]

    def part(device, i):
        return gathered[device, i * width : (i + 1) * width, :]

    ratios, values = [], []
    for i in range(devices + 1):
        if i == 0:
            link = 750.0 * part(0, 9)
            total = part(0, 6)
            source = [-part(0, c) for c in range(3)]
        elif i == devices:
            link = 750.0 * part(i - 1, 10)
            total = part(i - 1, 8)
            source = [part(i - 1, 3 + c) for c in range(3)]
        else:
            link = 750.0 * (part(i - 1, 10) + part(i, 9))
            total = part(i - 1, 8) + part(i, 6)
            source = [part(i - 1, 3 + c) - part(i, c) for c in range(3)]
        pivot = 1.0 + link * total
        if i > 0:
            before = part(i - 1, 7)
            pivot = pivot - link * before * ratios[-1]
            source = [s + before * v for s, v in zip(source, values[-1])]
        scale = link / pivot
        values.append([scale * s for s in source])
        if i < devices:
            ratios.append(scale * part(i, 7))
    flux = values[devices]
    for i in range(devices, -1, -1):
        if i < devices:
            flux = [v + ratios[i] * f for v, f in zip(values[i], flux)]
        for c in range(3):
            fluxes[i, c * width : (c + 1) * width, :] = flux[c]

    sublane = lax.broadcasted_iota(jnp.int32, (SEGMENTS, LANES), 0)
    levels = tree.shape[1]
    for x in range(width):
        for c in range(3):
            r = c * width + x
            left = jnp.broadcast_to(fluxes[here, r : r + 1, :], (SEGMENTS, LANES))
            right = -jnp.broadcast_to(fluxes[here + 1, r : r + 1, :], (SEGMENTS, LANES))
            for level in range(levels - 1, -1, -1):
                step = 2**level
                through = tree[x, level, c] + tree[x, level, 3] * left - tree[x, level, 4] * right
                second = lax.rem(sublane, 2 * step) == step
                left = jnp.where(second, pltpu.roll(through, step, 0), left)
                right = jnp.where(second, pltpu.roll(right, step, 0), -through)
            value = right
            for j in range(length - 1, -1, -1):
                value = (factors[x, j, c] + factors[x, j, 3] * left) + factors[x, j, 4] * value
                rows = pl.ds(j, SEGMENTS, stride=length)
                out[c, x, rows, :] = value - velocity[c, x, rows, :]


def in_vmem(count):
    return [pl.BlockSpec(memory_space=pltpu.VMEM)] * count


def params():
    return pltpu.CompilerParams(vmem_limit_bytes=VMEM_BYTES)


def body(velocity, tendency):
    _, width, cells, lanes = velocity.shape
    nz_parts = lax.axis_size("gz")
    count = lax.axis_size("gx") * nz_parts
    walls = lax.axis_size("gy")
    rows = cells // count
    nx = lax.axis_size("gx") * width
    padded = 16 + -(-rows // 8) * 8
    f32 = jnp.float32

    filled = 3 * width * (rows + 2)
    depth = -(-filled // 8) * 8
    chunks = pl.pallas_call(
        functools.partial(pack_kernel, rows),
        out_shape=jax.ShapeDtypeStruct((count, depth, lanes), f32),
        in_specs=in_vmem(1),
        out_specs=pl.BlockSpec(memory_space=pltpu.VMEM),
        compiler_params=params(),
        name="pack",
    )(velocity)
    recv = lax.all_to_all(chunks, ("gx", "gz"), split_axis=0, concat_axis=0, tiled=True)
    pairs = []
    for wall in range(walls - 1):
        upper, lower = wall * count + 1, (wall + 1) * count
        pairs += [(upper, lower), (lower, upper)]
    swapped = lax.ppermute(recv[:, 3 * width * rows :], ("gy", "gx", "gz"), pairs)
    rank = lax.axis_index(("gx", "gz")).astype(jnp.int32).reshape(1)
    eddy_chunks = pl.pallas_call(
        functools.partial(germano_kernel, nz_parts, width, rows),
        out_shape=jax.ShapeDtypeStruct((count, width, rows, lanes), f32),
        in_specs=[pl.BlockSpec(memory_space=pltpu.SMEM)] + in_vmem(2),
        out_specs=pl.BlockSpec(memory_space=pltpu.VMEM),
        scratch_shapes=[
            pltpu.VMEM((3, nx, nz_parts, padded, lanes), f32),
            pltpu.VMEM((3, nx, nz_parts, padded, lanes), f32),
            pltpu.VMEM((3, nx, nz_parts, 8, lanes), f32),
            pltpu.VMEM((nx, nz_parts, rows, lanes), f32),
            pltpu.VMEM((15, nx, nz_parts, rows, lanes), f32),
        ],
        compiler_params=params(),
        name="germano",
    )(rank, recv, swapped)
    back = lax.all_to_all(eddy_chunks, ("gx", "gz"), split_axis=0, concat_axis=0, tiled=True)

    length = cells // SEGMENTS
    levels = SEGMENTS.bit_length() - 1
    packed = -(-11 * width // 8) * 8
    eddy, reduced, factors, tree = pl.pallas_call(
        sweep_kernel,
        out_shape=(
            jax.ShapeDtypeStruct((width, cells, lanes), f32),
            jax.ShapeDtypeStruct((packed, lanes), f32),
            jax.ShapeDtypeStruct((width, length, 5, SEGMENTS, lanes), f32),
            jax.ShapeDtypeStruct((width, levels, 5, SEGMENTS, lanes), f32),
        ),
        in_specs=in_vmem(3),
        out_specs=tuple(in_vmem(4)),
        compiler_params=params(),
        name="sweep",
    )(back, velocity, tendency)

    others = [
        lax.ppermute(reduced, "gy", [(i, (i + shift) % walls) for i in range(walls)])
        for shift in range(1, walls)
    ]
    position = lax.axis_index("gy").astype(jnp.int32).reshape(1)
    new_velocity = pl.pallas_call(
        functools.partial(finish_kernel, walls),
        out_shape=jax.ShapeDtypeStruct(velocity.shape, f32),
        in_specs=[pl.BlockSpec(memory_space=pltpu.SMEM)] + in_vmem(3 + walls),
        out_specs=pl.BlockSpec(memory_space=pltpu.VMEM),
        scratch_shapes=[
            pltpu.VMEM((walls, packed, lanes), f32),
            pltpu.VMEM((walls + 1, -(-3 * width // 8) * 8, lanes), f32),
        ],
        compiler_params=params(),
        name="finish",
    )(position, factors, tree, velocity, reduced, *others)
    return (new_velocity, eddy)


def solution(mesh):
    return jax.shard_map(
        body,
        mesh=mesh,
        in_specs=(P(None, "gx", "gy", "gz"), P(None, "gx", "gy", "gz")),
        out_specs=(P(None, "gx", "gy", "gz"), P("gx", "gy", "gz")),
        check_vma=False,
    )
```

```python
import functools

import jax
import jax.numpy as jnp
from jax import lax
from jax.experimental import pallas as pl
from jax.experimental.pallas import tpu as pltpu
from jax.sharding import PartitionSpec as P

LANES = 128
SEGMENTS = 8
VMEM_BYTES = 24 * 2**20


def strain_parts(grad_x, grad_y, grad_z):
    return (
        grad_x[0],
        grad_y[1],
        grad_z[2],
        grad_y[0] + grad_x[1],
        grad_z[0] + grad_x[2],
        grad_z[1] + grad_y[2],
    )


def strain_size(parts):
    diagonal = parts[0] * parts[0] + parts[1] * parts[1] + parts[2] * parts[2]
    mixed = parts[3] * parts[3] + parts[4] * parts[4] + parts[5] * parts[5]
    return jnp.sqrt(0.5 * diagonal + 0.25 * mixed)


def beside(blocks):
    count = len(blocks)
    lanes = blocks[0].shape[1]
    down = [pltpu.roll(f, 1, 1) for f in blocks]
    up = [pltpu.roll(f, lanes - 1, 1) for f in blocks]
    if count > 1:
        lane = lax.broadcasted_iota(jnp.int32, blocks[0].shape, 1)
        first, last = lane == 0, lane == lanes - 1
        down, up = (
            [jnp.where(first, down[i - 1], down[i]) for i in range(count)],
            [jnp.where(last, up[(i + 1) % count], up[i]) for i in range(count)],
        )
    return down, up


def slope_z(blocks):
    down, up = beside(blocks)
    return [u - d for u, d in zip(up, down)]


def smooth_z(blocks):
    down, up = beside(blocks)
    return [(u + d) + 2.0 * f for f, u, d in zip(blocks, up, down)]


def products(v):
    return (v[0] * v[0], v[1] * v[1], v[2] * v[2], v[0] * v[1], v[0] * v[2], v[1] * v[2])


def row_order(count):
    return [0, count - 1, *range(1, count - 1)]


def pack_kernel(rows, velocity, out):
    _, width, cells, _ = velocity.shape
    count, depth, lanes = out.shape
    planes = 3 * width
    for rank, place in enumerate(row_order(count)):
        first = place * rows
        before = max(first - 1, 0)
        after = min(first + rows, cells - 1)
        for i in range(planes):
            c, x = divmod(i, width)
            out[rank, i * rows : (i + 1) * rows, :] = velocity[c, x, first : first + rows, :]
            at = planes * rows + i
            out[rank, at : at + 1, :] = velocity[c, x, before : before + 1, :]
            at += planes
            out[rank, at : at + 1, :] = velocity[c, x, after : after + 1, :]
        filled = planes * (rows + 2)
        if filled < depth:
            out[rank, filled:, :] = jnp.zeros((depth - filled, lanes), jnp.float32)


def germano_kernel(nz_parts, width, rows, rank, recv, swapped, out, vel, filt, ends, mag, part):
    count, _, lanes = recv.shape
    planes = 3 * width
    outer = (rank[0] == 0, rank[0] == 1)
    nx = (count // nz_parts) * width
    nz = nz_parts * lanes
    blocks = range(nz_parts)
    lead = 8
    inner = slice(lead, lead + rows)
    lower = slice(lead - 1, lead - 1 + rows)
    upper = slice(lead + 1, lead + 1 + rows)
    for k in range(count):
        x0, zb = (k // nz_parts) * width, k % nz_parts
        for c in range(3):
            for x in range(width):
                i = c * width + x
                vel[c, x0 + x, zb, inner, :] = recv[k, i * rows : (i + 1) * rows, :]
                for side, at in ((0, lead - 1), (1, lead + rows)):
                    own = planes * rows + side * planes + i
                    far = (1 - side) * planes + i
                    edge = jnp.where(outer[side], swapped[k, far : far + 1, :], recv[k, own : own + 1, :])
                    vel[c, x0 + x, zb, at : at + 1, :] = edge
                    ends[c, x0 + x, zb, side : side + 1, :] = edge

    for x in range(nx):
        left, right = (x - 1) % nx, (x + 1) % nx
        centre = [[vel[c, x, zb, inner, :] for zb in blocks] for c in range(3)]
        grad_x = [[vel[c, right, zb, inner, :] - vel[c, left, zb, inner, :] for zb in blocks] for c in range(3)]
        grad_y = [[vel[c, x, zb, upper, :] - vel[c, x, zb, lower, :] for zb in blocks] for c in range(3)]
        grad_z = []
        for c in range(3):
            down, up = beside(centre[c])
            grad_z.append([u - d for u, d in zip(up, down)])
            for zb in blocks:
                part[c, x, zb] = (up[zb] + down[zb]) + 2.0 * centre[c][zb]
        strain = [
            strain_parts(*([g[c][zb] for c in range(3)] for g in (grad_x, grad_y, grad_z)))
            for zb in blocks
        ]
        size = [strain_size(s) for s in strain]
        for zb in blocks:
            mag[x, zb] = size[zb]
        pairs = [products([centre[c][zb] for c in range(3)]) for zb in blocks]
        for i in range(6):
            for base, fields in (
                (3, [pairs[zb][i] for zb in blocks]),
                (9, [size[zb] * strain[zb][i] for zb in blocks]),
            ):
                for zb, f in enumerate(smooth_z(fields)):
                    part[base + i, x, zb] = f

    def smooth_x(read, x):
        return (read((x - 1) % nx) + read((x + 1) % nx)) + 2.0 * read(x)

    for c in range(3):
        rims = []
        for x in range(nx):
            rims.append(smooth_z([ends[c, x, zb] for zb in blocks]))
        for x in range(nx):
            for zb in blocks:
                rim = smooth_x(lambda at: rims[at][zb], x)
                filt[c, x, zb, lead - 1 : lead, :] = rim[0:1, :]
                filt[c, x, zb, lead + rows : lead + rows + 1, :] = rim[1:2, :]
                filt[c, x, zb, inner, :] = smooth_x(lambda at: part[c, at, zb], x)

    sum_lm = sum_mm = None
    for x in range(nx):
        left, right = (x - 1) % nx, (x + 1) % nx
        mean = [[filt[c, x, zb, inner, :] for zb in blocks] for c in range(3)]
        grad_x = [[filt[c, right, zb, inner, :] - filt[c, left, zb, inner, :] for zb in blocks] for c in range(3)]
        grad_y = [[filt[c, x, zb, upper, :] - filt[c, x, zb, lower, :] for zb in blocks] for c in range(3)]
        grad_z = [slope_z(mean[c]) for c in range(3)]
        for zb in blocks:
            strain = strain_parts(*([g[c][zb] for c in range(3)] for g in (grad_x, grad_y, grad_z)))
            size = 0.25 * strain_size(strain)
            v = [mean[c][zb] for c in range(3)]
            scaled = [0.0625 * f for f in v]
            pairs = (
                v[0] * scaled[0],
                v[1] * scaled[1],
                v[2] * scaled[2],
                v[0] * scaled[1],
                v[0] * scaled[2],
                v[1] * scaled[2],
            )
            lm = mm = None
            for i in range(6):
                leonard = smooth_x(lambda at: part[3 + i, at, zb], x) - pairs[i]
                model = smooth_x(lambda at: part[9 + i, at, zb], x) - size * strain[i]
                square = model * model if i < 3 else (0.5 * model) * model
                lm = leonard * model if lm is None else lm + leonard * model
                mm = square if mm is None else mm + square
            sum_lm = lm if sum_lm is None else sum_lm + lm
            sum_mm = mm if sum_mm is None else sum_mm + mm

    def plane_mean(total):
        return jnp.sum(total, axis=1, keepdims=True) * (1.0 / (256.0 * nx * nz))

    coefficient = jnp.maximum(plane_mean(sum_lm) / (plane_mean(sum_mm) + 1e-06), 0.0)
    for k in range(count):
        x0, zb = (k // nz_parts) * width, k % nz_parts
        for x in range(width):
            out[k, x] = coefficient * mag[x0 + x, zb]


def sweep_kernel(back, velocity, tendency, eddy, reduced, factors, tree):
    count, width, rows, _ = back.shape
    length = count * rows // SEGMENTS
    for k, place in enumerate(row_order(count)):
        for x in range(width):
            eddy[x, place * rows : (place + 1) * rows, :] = back[k, x]

    def row(ref, index, j):
        return ref[(*index, pl.ds(j, SEGMENTS, stride=length), slice(None))]

    for x in range(width):
        visc = 1.0 + row(eddy, (x,), 0)
        visc_first = visc
        q = jnp.ones_like(visc)
        m = jnp.ones_like(visc)
        corner = jnp.zeros_like(visc)
        first = [jnp.zeros_like(visc)] * 3
        value = None
        for j in range(length):
            if j < length - 1:
                visc_next = 1.0 + row(eddy, (x,), j + 1)
                link = 750.0 * (visc + visc_next)
                inverse = 1.0 / (q + link)
            else:
                visc_next = None
                link = None
                inverse = 1.0 / q
            left = m * inverse
            corner = corner + m * left
            source = [
                2.0 * row(velocity, (c, x), j) + row(tendency, (c, x), j) for c in range(3)
            ]
            if j > 0:
                source = [s + link_before * v for s, v in zip(source, value)]
            value = [s * inverse for s in source]
            first = [f + m * v for f, v in zip(first, value)]
            for c in range(3):
                factors[x, j, c] = value[c]
            factors[x, j, 3] = left
            if j < length - 1:
                ratio = link * inverse
                factors[x, j, 4] = ratio
                q = 1.0 + link * (q * inverse)
                m = m * ratio
                link_before = link
                visc = visc_next
            else:
                factors[x, j, 4] = inverse
        last = value
        across = left
        end = inverse
        links = 750.0 * (visc + pltpu.roll(visc_first, SEGMENTS - 1, 0))
        level, step = 0, 1
        while step < SEGMENTS:
            def other(v):
                return pltpu.roll(v, SEGMENTS - step, 0)

            link = links if step == 1 else pltpu.roll(links, SEGMENTS - (step - 1), 0)
            across_b = other(across)
            stiff = link / (1.0 + link * (end + other(corner)))
            flux = [stiff * (g - other(f)) for g, f in zip(last, first)]
            from_left = stiff * across
            from_right = stiff * across_b
            for c in range(3):
                tree[x, level, c] = flux[c]
            tree[x, level, 3] = from_left
            tree[x, level, 4] = from_right
            first = [f - across * t for f, t in zip(first, flux)]
            last = [other(g) + across_b * t for g, t in zip(last, flux)]
            corner = corner - across * from_left
            end = other(end) - across_b * from_right
            across = from_left * across_b
            level, step = level + 1, step * 2
        rows_out = [*first, *last, corner, across, end, visc_first]
        rows_out = [v[0:1, :] for v in rows_out] + [visc[SEGMENTS - 1 :, :]]
        for i, v in enumerate(rows_out):
            for device in range(reduced.shape[0]):
                reduced[device, i * width + x : i * width + x + 1, :] = v


def finish_kernel(position, factors, tree, velocity, gathered, out, fluxes):
    devices = gathered.shape[0]
    width, length = factors.shape[:2]
    here = position[0]

    def part(device, i):
        return gathered[device, i * width : (i + 1) * width, :]

    ratios, values = [], []
    for i in range(devices + 1):
        if i == 0:
            link = 750.0 * part(0, 9)
            total = part(0, 6)
            source = [-part(0, c) for c in range(3)]
        elif i == devices:
            link = 750.0 * part(i - 1, 10)
            total = part(i - 1, 8)
            source = [part(i - 1, 3 + c) for c in range(3)]
        else:
            link = 750.0 * (part(i - 1, 10) + part(i, 9))
            total = part(i - 1, 8) + part(i, 6)
            source = [part(i - 1, 3 + c) - part(i, c) for c in range(3)]
        pivot = 1.0 + link * total
        if i > 0:
            before = part(i - 1, 7)
            pivot = pivot - link * before * ratios[-1]
            source = [s + before * v for s, v in zip(source, values[-1])]
        scale = link / pivot
        values.append([scale * s for s in source])
        if i < devices:
            ratios.append(scale * part(i, 7))
    flux = values[devices]
    for i in range(devices, -1, -1):
        if i < devices:
            flux = [v + ratios[i] * f for v, f in zip(values[i], flux)]
        for c in range(3):
            fluxes[i, c * width : (c + 1) * width, :] = flux[c]

    sublane = lax.broadcasted_iota(jnp.int32, (SEGMENTS, LANES), 0)
    levels = tree.shape[1]
    for x in range(width):
        for c in range(3):
            r = c * width + x
            left = jnp.broadcast_to(fluxes[here, r : r + 1, :], (SEGMENTS, LANES))
            right = -jnp.broadcast_to(fluxes[here + 1, r : r + 1, :], (SEGMENTS, LANES))
            for level in range(levels - 1, -1, -1):
                step = 2**level
                through = tree[x, level, c] + tree[x, level, 3] * left - tree[x, level, 4] * right
                second = lax.rem(sublane, 2 * step) == step
                left = jnp.where(second, pltpu.roll(through, step, 0), left)
                right = jnp.where(second, pltpu.roll(right, step, 0), -through)
            value = right
            for j in range(length - 1, -1, -1):
                value = (factors[x, j, c] + factors[x, j, 3] * left) + factors[x, j, 4] * value
                rows = pl.ds(j, SEGMENTS, stride=length)
                out[c, x, rows, :] = value - velocity[c, x, rows, :]


def in_vmem(count):
    return [pl.BlockSpec(memory_space=pltpu.VMEM)] * count


def params():
    return pltpu.CompilerParams(vmem_limit_bytes=VMEM_BYTES)


def body(velocity, tendency):
    _, width, cells, lanes = velocity.shape
    nz_parts = lax.axis_size("gz")
    count = lax.axis_size("gx") * nz_parts
    walls = lax.axis_size("gy")
    rows = cells // count
    nx = lax.axis_size("gx") * width
    padded = 16 + -(-rows // 8) * 8
    f32 = jnp.float32

    filled = 3 * width * (rows + 2)
    depth = -(-filled // 8) * 8
    chunks = pl.pallas_call(
        functools.partial(pack_kernel, rows),
        out_shape=jax.ShapeDtypeStruct((count, depth, lanes), f32),
        in_specs=in_vmem(1),
        out_specs=pl.BlockSpec(memory_space=pltpu.VMEM),
        compiler_params=params(),
        name="pack",
    )(velocity)
    recv = lax.all_to_all(chunks, ("gx", "gz"), split_axis=0, concat_axis=0, tiled=True)
    pairs = []
    for wall in range(walls - 1):
        upper, lower = wall * count + 1, (wall + 1) * count
        pairs += [(upper, lower), (lower, upper)]
    swapped = lax.ppermute(recv[:, 3 * width * rows :], ("gy", "gx", "gz"), pairs)
    rank = lax.axis_index(("gx", "gz")).astype(jnp.int32).reshape(1)
    eddy_chunks = pl.pallas_call(
        functools.partial(germano_kernel, nz_parts, width, rows),
        out_shape=jax.ShapeDtypeStruct((count, width, rows, lanes), f32),
        in_specs=[pl.BlockSpec(memory_space=pltpu.SMEM)] + in_vmem(2),
        out_specs=pl.BlockSpec(memory_space=pltpu.VMEM),
        scratch_shapes=[
            pltpu.VMEM((3, nx, nz_parts, padded, lanes), f32),
            pltpu.VMEM((3, nx, nz_parts, padded, lanes), f32),
            pltpu.VMEM((3, nx, nz_parts, 8, lanes), f32),
            pltpu.VMEM((nx, nz_parts, rows, lanes), f32),
            pltpu.VMEM((15, nx, nz_parts, rows, lanes), f32),
        ],
        compiler_params=params(),
        name="germano",
    )(rank, recv, swapped)
    back = lax.all_to_all(eddy_chunks, ("gx", "gz"), split_axis=0, concat_axis=0, tiled=True)

    length = cells // SEGMENTS
    levels = SEGMENTS.bit_length() - 1
    packed = -(-11 * width // 8) * 8
    eddy, reduced, factors, tree = pl.pallas_call(
        sweep_kernel,
        out_shape=(
            jax.ShapeDtypeStruct((width, cells, lanes), f32),
            jax.ShapeDtypeStruct((walls, packed, lanes), f32),
            jax.ShapeDtypeStruct((width, length, 5, SEGMENTS, lanes), f32),
            jax.ShapeDtypeStruct((width, levels, 5, SEGMENTS, lanes), f32),
        ),
        in_specs=in_vmem(3),
        out_specs=tuple(in_vmem(4)),
        compiler_params=params(),
        name="sweep",
    )(back, velocity, tendency)

    gathered = lax.all_to_all(reduced, "gy", split_axis=0, concat_axis=0, tiled=True)
    position = lax.axis_index("gy").astype(jnp.int32).reshape(1)
    new_velocity = pl.pallas_call(
        finish_kernel,
        out_shape=jax.ShapeDtypeStruct(velocity.shape, f32),
        in_specs=[pl.BlockSpec(memory_space=pltpu.SMEM)] + in_vmem(4),
        out_specs=pl.BlockSpec(memory_space=pltpu.VMEM),
        scratch_shapes=[
            pltpu.VMEM((walls + 1, -(-3 * width // 8) * 8, lanes), f32),
        ],
        compiler_params=params(),
        name="finish",
    )(position, factors, tree, velocity, gathered)
    return (new_velocity, eddy)


def solution(mesh):
    return jax.shard_map(
        body,
        mesh=mesh,
        in_specs=(P(None, "gx", "gy", "gz"), P(None, "gx", "gy", "gz")),
        out_specs=(P(None, "gx", "gy", "gz"), P("gx", "gy", "gz")),
        check_vma=False,
    )
```

```python
import functools

import jax
import jax.numpy as jnp
from jax import lax
from jax.experimental import pallas as pl
from jax.experimental.pallas import tpu as pltpu
from jax.sharding import PartitionSpec as P

LANES = 128
SEGMENTS = 8
VMEM_BYTES = 24 * 2**20


def strain_parts(grad_x, grad_y, grad_z):
    return (
        grad_x[0],
        grad_y[1],
        grad_z[2],
        grad_y[0] + grad_x[1],
        grad_z[0] + grad_x[2],
        grad_z[1] + grad_y[2],
    )


def strain_size(parts):
    diagonal = parts[0] * parts[0] + parts[1] * parts[1] + parts[2] * parts[2]
    mixed = parts[3] * parts[3] + parts[4] * parts[4] + parts[5] * parts[5]
    return jnp.sqrt(0.5 * diagonal + 0.25 * mixed)


def beside(blocks):
    count = len(blocks)
    lanes = blocks[0].shape[1]
    down = [pltpu.roll(f, 1, 1) for f in blocks]
    up = [pltpu.roll(f, lanes - 1, 1) for f in blocks]
    if count > 1:
        lane = lax.broadcasted_iota(jnp.int32, blocks[0].shape, 1)
        first, last = lane == 0, lane == lanes - 1
        down, up = (
            [jnp.where(first, down[i - 1], down[i]) for i in range(count)],
            [jnp.where(last, up[(i + 1) % count], up[i]) for i in range(count)],
        )
    return down, up


def slope_z(blocks):
    down, up = beside(blocks)
    return [u - d for u, d in zip(up, down)]


def smooth_z(blocks):
    down, up = beside(blocks)
    return [(u + d) + 2.0 * f for f, u, d in zip(blocks, up, down)]


def products(v):
    return (v[0] * v[0], v[1] * v[1], v[2] * v[2], v[0] * v[1], v[0] * v[2], v[1] * v[2])


def place_of(rank, parity, count):
    if rank >= 2:
        return rank - 1
    return 0 if rank == parity else count - 1


def by_parity(parity, count, fill):
    for rank in range(2, count):
        fill(rank, place_of(rank, 0, count))
    for turn in range(2):

        @pl.when(parity[0] == turn)
        def _():
            for rank in range(2):
                fill(rank, place_of(rank, turn, count))


def aligned(n):
    return -(-n // 8) * 8


def pack_kernel(rows, parity, velocity, out):
    _, width, cells, _ = velocity.shape
    count, depth, lanes = out.shape
    planes = 3 * width
    slots = planes * rows

    def fill(rank, place):
        first = place * rows
        beside = [first - 1, first + rows]
        if place == 0:
            beside = [first, first + rows]
        if place == count - 1:
            beside = [first + rows - 1, first - 1]
        for i in range(planes):
            c, x = divmod(i, width)
            out[rank, i * rows : (i + 1) * rows, :] = velocity[c, x, first : first + rows, :]
            for slot, row in enumerate(beside):
                at = slots + slot * aligned(planes) + i
                out[rank, at : at + 1, :] = velocity[c, x, row : row + 1, :]

    by_parity(parity, count, fill)
    blank = aligned(planes) - planes
    for rank in range(count):
        for slot in range(2):
            at = slots + slot * aligned(planes) + planes
            out[rank, at : at + blank, :] = jnp.zeros((blank, lanes), jnp.float32)
        at = slots + 2 * aligned(planes)
        if at < depth:
            out[rank, at:, :] = jnp.zeros((depth - at, lanes), jnp.float32)


def germano_kernel(nz_parts, width, rows, rank, parity, recv, swapped, out, vel, filt, ends, mag, part):
    count, _, lanes = recv.shape
    planes = 3 * width
    bottom = rank[0] == parity[0]
    top = rank[0] == 1 - parity[0]
    nx = (count // nz_parts) * width
    nz = nz_parts * lanes
    blocks = range(nz_parts)
    lead = 8
    inner = slice(lead, lead + rows)
    lower = slice(lead - 1, lead - 1 + rows)
    upper = slice(lead + 1, lead + 1 + rows)
    for k in range(count):
        x0, zb = (k // nz_parts) * width, k % nz_parts
        for c in range(3):
            for x in range(width):
                i = c * width + x
                vel[c, x0 + x, zb, inner, :] = recv[k, i * rows : (i + 1) * rows, :]
                slots = planes * rows + i
                near = recv[k, slots : slots + 1, :]
                slots += aligned(planes)
                other = recv[k, slots : slots + 1, :]
                far = swapped[k, i : i + 1, :]
                below = jnp.where(bottom, far, jnp.where(top, other, near))
                above = jnp.where(top, far, other)
                for side, (edge, at) in enumerate(((below, lead - 1), (above, lead + rows))):
                    vel[c, x0 + x, zb, at : at + 1, :] = edge
                    ends[c, x0 + x, zb, side : side + 1, :] = edge

    for x in range(nx):
        left, right = (x - 1) % nx, (x + 1) % nx
        centre = [[vel[c, x, zb, inner, :] for zb in blocks] for c in range(3)]
        grad_x = [[vel[c, right, zb, inner, :] - vel[c, left, zb, inner, :] for zb in blocks] for c in range(3)]
        grad_y = [[vel[c, x, zb, upper, :] - vel[c, x, zb, lower, :] for zb in blocks] for c in range(3)]
        grad_z = []
        for c in range(3):
            down, up = beside(centre[c])
            grad_z.append([u - d for u, d in zip(up, down)])
            for zb in blocks:
                part[c, x, zb] = (up[zb] + down[zb]) + 2.0 * centre[c][zb]
        strain = [
            strain_parts(*([g[c][zb] for c in range(3)] for g in (grad_x, grad_y, grad_z)))
            for zb in blocks
        ]
        size = [strain_size(s) for s in strain]
        for zb in blocks:
            mag[x, zb] = size[zb]
        pairs = [products([centre[c][zb] for c in range(3)]) for zb in blocks]
        for i in range(6):
            for base, fields in (
                (3, [pairs[zb][i] for zb in blocks]),
                (9, [size[zb] * strain[zb][i] for zb in blocks]),
            ):
                for zb, f in enumerate(smooth_z(fields)):
                    part[base + i, x, zb] = f

    def smooth_x(read, x):
        return (read((x - 1) % nx) + read((x + 1) % nx)) + 2.0 * read(x)

    for c in range(3):
        rims = []
        for x in range(nx):
            rims.append(smooth_z([ends[c, x, zb] for zb in blocks]))
        for x in range(nx):
            for zb in blocks:
                rim = smooth_x(lambda at: rims[at][zb], x)
                filt[c, x, zb, lead - 1 : lead, :] = rim[0:1, :]
                filt[c, x, zb, lead + rows : lead + rows + 1, :] = rim[1:2, :]
                filt[c, x, zb, inner, :] = smooth_x(lambda at: part[c, at, zb], x)

    sum_lm = sum_mm = None
    for x in range(nx):
        left, right = (x - 1) % nx, (x + 1) % nx
        mean = [[filt[c, x, zb, inner, :] for zb in blocks] for c in range(3)]
        grad_x = [[filt[c, right, zb, inner, :] - filt[c, left, zb, inner, :] for zb in blocks] for c in range(3)]
        grad_y = [[filt[c, x, zb, upper, :] - filt[c, x, zb, lower, :] for zb in blocks] for c in range(3)]
        grad_z = [slope_z(mean[c]) for c in range(3)]
        for zb in blocks:
            strain = strain_parts(*([g[c][zb] for c in range(3)] for g in (grad_x, grad_y, grad_z)))
            size = 0.25 * strain_size(strain)
            v = [mean[c][zb] for c in range(3)]
            scaled = [0.0625 * f for f in v]
            pairs = (
                v[0] * scaled[0],
                v[1] * scaled[1],
                v[2] * scaled[2],
                v[0] * scaled[1],
                v[0] * scaled[2],
                v[1] * scaled[2],
            )
            lm = mm = None
            for i in range(6):
                leonard = smooth_x(lambda at: part[3 + i, at, zb], x) - pairs[i]
                model = smooth_x(lambda at: part[9 + i, at, zb], x) - size * strain[i]
                square = model * model if i < 3 else (0.5 * model) * model
                lm = leonard * model if lm is None else lm + leonard * model
                mm = square if mm is None else mm + square
            sum_lm = lm if sum_lm is None else sum_lm + lm
            sum_mm = mm if sum_mm is None else sum_mm + mm

    def plane_mean(total):
        return jnp.sum(total, axis=1, keepdims=True) * (1.0 / (256.0 * nx * nz))

    coefficient = jnp.maximum(plane_mean(sum_lm) / (plane_mean(sum_mm) + 1e-06), 0.0)
    for k in range(count):
        x0, zb = (k // nz_parts) * width, k % nz_parts
        for x in range(width):
            out[k, x] = coefficient * mag[x0 + x, zb]


def sweep_kernel(parity, back, velocity, tendency, eddy, reduced, factors, tree):
    count, width, rows, _ = back.shape
    length = count * rows // SEGMENTS

    def fill(rank, place):
        for x in range(width):
            eddy[x, place * rows : (place + 1) * rows, :] = back[rank, x]

    by_parity(parity, count, fill)

    def row(ref, index, j):
        return ref[(*index, pl.ds(j, SEGMENTS, stride=length), slice(None))]

    for x in range(width):
        visc = 1.0 + row(eddy, (x,), 0)
        visc_first = visc
        q = jnp.ones_like(visc)
        m = jnp.ones_like(visc)
        corner = jnp.zeros_like(visc)
        first = [jnp.zeros_like(visc)] * 3
        value = None
        for j in range(length):
            if j < length - 1:
                visc_next = 1.0 + row(eddy, (x,), j + 1)
                link = 750.0 * (visc + visc_next)
                inverse = 1.0 / (q + link)
            else:
                visc_next = None
                link = None
                inverse = 1.0 / q
            left = m * inverse
            corner = corner + m * left
            source = [
                2.0 * row(velocity, (c, x), j) + row(tendency, (c, x), j) for c in range(3)
            ]
            if j > 0:
                source = [s + link_before * v for s, v in zip(source, value)]
            value = [s * inverse for s in source]
            first = [f + m * v for f, v in zip(first, value)]
            for c in range(3):
                factors[x, j, c] = value[c]
            factors[x, j, 3] = left
            if j < length - 1:
                ratio = link * inverse
                factors[x, j, 4] = ratio
                q = 1.0 + link * (q * inverse)
                m = m * ratio
                link_before = link
                visc = visc_next
            else:
                factors[x, j, 4] = inverse
        last = value
        across = left
        end = inverse
        links = 750.0 * (visc + pltpu.roll(visc_first, SEGMENTS - 1, 0))
        level, step = 0, 1
        while step < SEGMENTS:
            def other(v):
                return pltpu.roll(v, SEGMENTS - step, 0)

            link = links if step == 1 else pltpu.roll(links, SEGMENTS - (step - 1), 0)
            across_b = other(across)
            stiff = link / (1.0 + link * (end + other(corner)))
            flux = [stiff * (g - other(f)) for g, f in zip(last, first)]
            from_left = stiff * across
            from_right = stiff * across_b
            for c in range(3):
                tree[x, level, c] = flux[c]
            tree[x, level, 3] = from_left
            tree[x, level, 4] = from_right
            first = [f - across * t for f, t in zip(first, flux)]
            last = [other(g) + across_b * t for g, t in zip(last, flux)]
            corner = corner - across * from_left
            end = other(end) - across_b * from_right
            across = from_left * across_b
            level, step = level + 1, step * 2
        rows_out = [*first, *last, corner, across, end, visc_first]
        for i, v in enumerate(rows_out):
            reduced[i * width + x : i * width + x + 1, :] = v[0:1, :]
        i = len(rows_out)
        reduced[i * width + x : i * width + x + 1, :] = visc[SEGMENTS - 1 :, :]


def finish_kernel(devices, position, factors, tree, velocity, *rest):
    reduced, (out, gathered, fluxes) = rest[:devices], rest[devices:]
    width, length = factors.shape[:2]
    here = position[0]
    for shift in range(devices):
        gathered[lax.rem(here - shift + devices, devices)] = reduced[shift][...]

    def part(device, i):
        return gathered[device, i * width : (i + 1) * width, :]

    ratios, values = [], []
    for i in range(devices + 1):
        if i == 0:
            link = 750.0 * part(0, 9)
            total = part(0, 6)
            source = [-part(0, c) for c in range(3)]
        elif i == devices:
            link = 750.0 * part(i - 1, 10)
            total = part(i - 1, 8)
            source = [part(i - 1, 3 + c) for c in range(3)]
        else:
            link = 750.0 * (part(i - 1, 10) + part(i, 9))
            total = part(i - 1, 8) + part(i, 6)
            source = [part(i - 1, 3 + c) - part(i, c) for c in range(3)]
        pivot = 1.0 + link * total
        if i > 0:
            before = part(i - 1, 7)
            pivot = pivot - link * before * ratios[-1]
            source = [s + before * v for s, v in zip(source, values[-1])]
        scale = link / pivot
        values.append([scale * s for s in source])
        if i < devices:
            ratios.append(scale * part(i, 7))
    flux = values[devices]
    for i in range(devices, -1, -1):
        if i < devices:
            flux = [v + ratios[i] * f for v, f in zip(values[i], flux)]
        for c in range(3):
            fluxes[i, c * width : (c + 1) * width, :] = flux[c]

    sublane = lax.broadcasted_iota(jnp.int32, (SEGMENTS, LANES), 0)
    levels = tree.shape[1]
    for x in range(width):
        for c in range(3):
            r = c * width + x
            left = jnp.broadcast_to(fluxes[here, r : r + 1, :], (SEGMENTS, LANES))
            right = -jnp.broadcast_to(fluxes[here + 1, r : r + 1, :], (SEGMENTS, LANES))
            for level in range(levels - 1, -1, -1):
                step = 2**level
                through = tree[x, level, c] + tree[x, level, 3] * left - tree[x, level, 4] * right
                second = lax.rem(sublane, 2 * step) == step
                left = jnp.where(second, pltpu.roll(through, step, 0), left)
                right = jnp.where(second, pltpu.roll(right, step, 0), -through)
            value = right
            for j in range(length - 1, -1, -1):
                value = (factors[x, j, c] + factors[x, j, 3] * left) + factors[x, j, 4] * value
                rows = pl.ds(j, SEGMENTS, stride=length)
                out[c, x, rows, :] = value - velocity[c, x, rows, :]


def in_vmem(count):
    return [pl.BlockSpec(memory_space=pltpu.VMEM)] * count


def in_smem(count):
    return [pl.BlockSpec(memory_space=pltpu.SMEM)] * count


def params():
    return pltpu.CompilerParams(vmem_limit_bytes=VMEM_BYTES)


def body(velocity, tendency):
    _, width, cells, lanes = velocity.shape
    nz_parts = lax.axis_size("gz")
    count = lax.axis_size("gx") * nz_parts
    walls = lax.axis_size("gy")
    rows = cells // count
    nx = lax.axis_size("gx") * width
    padded = 16 + aligned(rows)
    f32 = jnp.float32

    planes = 3 * width
    depth = aligned(planes * rows + 2 * aligned(planes))
    position = lax.axis_index("gy").astype(jnp.int32).reshape(1)
    parity = lax.rem(position, 2)
    chunks = pl.pallas_call(
        functools.partial(pack_kernel, rows),
        out_shape=jax.ShapeDtypeStruct((count, depth, lanes), f32),
        in_specs=in_smem(1) + in_vmem(1),
        out_specs=pl.BlockSpec(memory_space=pltpu.VMEM),
        compiler_params=params(),
        name="pack",
    )(parity, velocity)
    recv = lax.all_to_all(chunks, ("gx", "gz"), split_axis=0, concat_axis=0, tiled=True)
    pairs = []
    for wall in range(walls - 1):
        outer = wall * count + (1 - wall % 2)
        pairs += [(outer, outer + count), (outer + count, outer)]
    slot = lax.slice_in_dim(recv, planes * rows, planes * rows + aligned(planes), axis=1)
    swapped = lax.ppermute(slot, ("gy", "gx", "gz"), pairs)
    rank = lax.axis_index(("gx", "gz")).astype(jnp.int32).reshape(1)
    eddy_chunks = pl.pallas_call(
        functools.partial(germano_kernel, nz_parts, width, rows),
        out_shape=jax.ShapeDtypeStruct((count, width, rows, lanes), f32),
        in_specs=in_smem(2) + in_vmem(2),
        out_specs=pl.BlockSpec(memory_space=pltpu.VMEM),
        scratch_shapes=[
            pltpu.VMEM((3, nx, nz_parts, padded, lanes), f32),
            pltpu.VMEM((3, nx, nz_parts, padded, lanes), f32),
            pltpu.VMEM((3, nx, nz_parts, 8, lanes), f32),
            pltpu.VMEM((nx, nz_parts, rows, lanes), f32),
            pltpu.VMEM((15, nx, nz_parts, rows, lanes), f32),
        ],
        compiler_params=params(),
        name="germano",
    )(rank, parity, recv, swapped)
    back = lax.all_to_all(eddy_chunks, ("gx", "gz"), split_axis=0, concat_axis=0, tiled=True)

    length = cells // SEGMENTS
    levels = SEGMENTS.bit_length() - 1
    packed = aligned(11 * width)
    eddy, reduced, factors, tree = pl.pallas_call(
        sweep_kernel,
        out_shape=(
            jax.ShapeDtypeStruct((width, cells, lanes), f32),
            jax.ShapeDtypeStruct((packed, lanes), f32),
            jax.ShapeDtypeStruct((width, length, 5, SEGMENTS, lanes), f32),
            jax.ShapeDtypeStruct((width, levels, 5, SEGMENTS, lanes), f32),
        ),
        in_specs=in_smem(1) + in_vmem(3),
        out_specs=tuple(in_vmem(4)),
        compiler_params=params(),
        name="sweep",
    )(parity, back, velocity, tendency)

    others = [
        lax.ppermute(reduced, "gy", [(i, (i + shift) % walls) for i in range(walls)])
        for shift in range(1, walls)
    ]
    new_velocity = pl.pallas_call(
        functools.partial(finish_kernel, walls),
        out_shape=jax.ShapeDtypeStruct(velocity.shape, f32),
        in_specs=in_smem(1) + in_vmem(3 + walls),
        out_specs=pl.BlockSpec(memory_space=pltpu.VMEM),
        scratch_shapes=[
            pltpu.VMEM((walls, packed, lanes), f32),
            pltpu.VMEM((walls + 1, aligned(3 * width), lanes), f32),
        ],
        compiler_params=params(),
        name="finish",
    )(position, factors, tree, velocity, reduced, *others)
    return (new_velocity, eddy)


def solution(mesh):
    return jax.shard_map(
        body,
        mesh=mesh,
        in_specs=(P(None, "gx", "gy", "gz"), P(None, "gx", "gy", "gz")),
        out_specs=(P(None, "gx", "gy", "gz"), P("gx", "gy", "gz")),
        check_vma=False,
    )
```

```python
import functools

import jax
import jax.numpy as jnp
from jax import lax
from jax.experimental import pallas as pl
from jax.experimental.pallas import tpu as pltpu
from jax.sharding import PartitionSpec as P

LANES = 128
SEGMENTS = 8
VMEM_BYTES = 24 * 2**20


def strain_parts(grad_x, grad_y, grad_z):
    return (
        grad_x[0],
        grad_y[1],
        grad_z[2],
        grad_y[0] + grad_x[1],
        grad_z[0] + grad_x[2],
        grad_z[1] + grad_y[2],
    )


def strain_size(parts):
    diagonal = parts[0] * parts[0] + parts[1] * parts[1] + parts[2] * parts[2]
    mixed = parts[3] * parts[3] + parts[4] * parts[4] + parts[5] * parts[5]
    return jnp.sqrt(0.5 * diagonal + 0.25 * mixed)


def beside(blocks):
    count = len(blocks)
    lanes = blocks[0].shape[1]
    down = [pltpu.roll(f, 1, 1) for f in blocks]
    up = [pltpu.roll(f, lanes - 1, 1) for f in blocks]
    if count > 1:
        lane = lax.broadcasted_iota(jnp.int32, blocks[0].shape, 1)
        first, last = lane == 0, lane == lanes - 1
        down, up = (
            [jnp.where(first, down[i - 1], down[i]) for i in range(count)],
            [jnp.where(last, up[(i + 1) % count], up[i]) for i in range(count)],
        )
    return down, up


def slope_z(blocks):
    down, up = beside(blocks)
    return [u - d for u, d in zip(up, down)]


def smooth_z(blocks):
    down, up = beside(blocks)
    return [(u + d) + 2.0 * f for f, u, d in zip(blocks, up, down)]


def products(v):
    return (v[0] * v[0], v[1] * v[1], v[2] * v[2], v[0] * v[1], v[0] * v[2], v[1] * v[2])


def outer_ranks(count):
    return (count - 1, count - 3)


def places(parity, count):
    outer = outer_ranks(count)
    inner = iter(range(1, count - 1))
    return [
        (0 if outer[parity] == rank else count - 1) if rank in outer else next(inner)
        for rank in range(count)
    ]


def by_parity(parity, count, fill):
    outer = outer_ranks(count)
    for rank, place in enumerate(places(0, count)):
        if rank not in outer:
            fill(rank, place)
    for turn in range(2):

        @pl.when(parity[0] == turn)
        def _():
            for rank in outer:
                fill(rank, places(turn, count)[rank])


def aligned(n):
    return -(-n // 8) * 8


def pack_kernel(rows, parity, velocity, out):
    _, width, cells, _ = velocity.shape
    count, depth, lanes = out.shape
    planes = 3 * width
    slots = planes * rows

    def fill(rank, place):
        first = place * rows
        beside = [first - 1, first + rows]
        if place == 0:
            beside = [first, first + rows]
        if place == count - 1:
            beside = [first + rows - 1, first - 1]
        for i in range(planes):
            c, x = divmod(i, width)
            out[rank, i * rows : (i + 1) * rows, :] = velocity[c, x, first : first + rows, :]
            for slot, row in enumerate(beside):
                at = slots + slot * aligned(planes) + i
                out[rank, at : at + 1, :] = velocity[c, x, row : row + 1, :]

    by_parity(parity, count, fill)
    blank = aligned(planes) - planes
    for rank in range(count):
        for slot in range(2):
            at = slots + slot * aligned(planes) + planes
            out[rank, at : at + blank, :] = jnp.zeros((blank, lanes), jnp.float32)
        at = slots + 2 * aligned(planes)
        if at < depth:
            out[rank, at:, :] = jnp.zeros((depth - at, lanes), jnp.float32)


def germano_kernel(nz_parts, width, rows, rank, parity, recv, swapped, out, vel, filt, ends, mag, part):
    count, _, lanes = recv.shape
    planes = 3 * width
    outer = outer_ranks(count)
    even = parity[0] == 0
    bottom = rank[0] == jnp.where(even, outer[0], outer[1])
    top = rank[0] == jnp.where(even, outer[1], outer[0])
    nx = (count // nz_parts) * width
    nz = nz_parts * lanes
    blocks = range(nz_parts)
    lead = 8
    inner = slice(lead, lead + rows)
    lower = slice(lead - 1, lead - 1 + rows)
    upper = slice(lead + 1, lead + 1 + rows)
    for k in range(count):
        x0, zb = (k // nz_parts) * width, k % nz_parts
        for c in range(3):
            for x in range(width):
                i = c * width + x
                vel[c, x0 + x, zb, inner, :] = recv[k, i * rows : (i + 1) * rows, :]
                slots = planes * rows + i
                near = recv[k, slots : slots + 1, :]
                slots += aligned(planes)
                other = recv[k, slots : slots + 1, :]
                far = swapped[k, i : i + 1, :]
                below = jnp.where(bottom, far, jnp.where(top, other, near))
                above = jnp.where(top, far, other)
                for side, (edge, at) in enumerate(((below, lead - 1), (above, lead + rows))):
                    vel[c, x0 + x, zb, at : at + 1, :] = edge
                    ends[c, x0 + x, zb, side : side + 1, :] = edge

    for x in range(nx):
        left, right = (x - 1) % nx, (x + 1) % nx
        centre = [[vel[c, x, zb, inner, :] for zb in blocks] for c in range(3)]
        grad_x = [[vel[c, right, zb, inner, :] - vel[c, left, zb, inner, :] for zb in blocks] for c in range(3)]
        grad_y = [[vel[c, x, zb, upper, :] - vel[c, x, zb, lower, :] for zb in blocks] for c in range(3)]
        grad_z = []
        for c in range(3):
            down, up = beside(centre[c])
            grad_z.append([u - d for u, d in zip(up, down)])
            for zb in blocks:
                part[c, x, zb] = (up[zb] + down[zb]) + 2.0 * centre[c][zb]
        strain = [
            strain_parts(*([g[c][zb] for c in range(3)] for g in (grad_x, grad_y, grad_z)))
            for zb in blocks
        ]
        size = [strain_size(s) for s in strain]
        for zb in blocks:
            mag[x, zb] = size[zb]
        pairs = [products([centre[c][zb] for c in range(3)]) for zb in blocks]
        for i in range(6):
            for base, fields in (
                (3, [pairs[zb][i] for zb in blocks]),
                (9, [size[zb] * strain[zb][i] for zb in blocks]),
            ):
                for zb, f in enumerate(smooth_z(fields)):
                    part[base + i, x, zb] = f

    def smooth_x(read, x):
        return (read((x - 1) % nx) + read((x + 1) % nx)) + 2.0 * read(x)

    for c in range(3):
        rims = []
        for x in range(nx):
            rims.append(smooth_z([ends[c, x, zb] for zb in blocks]))
        for x in range(nx):
            for zb in blocks:
                rim = smooth_x(lambda at: rims[at][zb], x)
                filt[c, x, zb, lead - 1 : lead, :] = rim[0:1, :]
                filt[c, x, zb, lead + rows : lead + rows + 1, :] = rim[1:2, :]
                filt[c, x, zb, inner, :] = smooth_x(lambda at: part[c, at, zb], x)

    sum_lm = sum_mm = None
    for x in range(nx):
        left, right = (x - 1) % nx, (x + 1) % nx
        mean = [[filt[c, x, zb, inner, :] for zb in blocks] for c in range(3)]
        grad_x = [[filt[c, right, zb, inner, :] - filt[c, left, zb, inner, :] for zb in blocks] for c in range(3)]
        grad_y = [[filt[c, x, zb, upper, :] - filt[c, x, zb, lower, :] for zb in blocks] for c in range(3)]
        grad_z = [slope_z(mean[c]) for c in range(3)]
        for zb in blocks:
            strain = strain_parts(*([g[c][zb] for c in range(3)] for g in (grad_x, grad_y, grad_z)))
            size = 0.25 * strain_size(strain)
            v = [mean[c][zb] for c in range(3)]
            scaled = [0.0625 * f for f in v]
            pairs = (
                v[0] * scaled[0],
                v[1] * scaled[1],
                v[2] * scaled[2],
                v[0] * scaled[1],
                v[0] * scaled[2],
                v[1] * scaled[2],
            )
            lm = mm = None
            for i in range(6):
                leonard = smooth_x(lambda at: part[3 + i, at, zb], x) - pairs[i]
                model = smooth_x(lambda at: part[9 + i, at, zb], x) - size * strain[i]
                square = model * model if i < 3 else (0.5 * model) * model
                lm = leonard * model if lm is None else lm + leonard * model
                mm = square if mm is None else mm + square
            sum_lm = lm if sum_lm is None else sum_lm + lm
            sum_mm = mm if sum_mm is None else sum_mm + mm

    def plane_mean(total):
        return jnp.sum(total, axis=1, keepdims=True) * (1.0 / (256.0 * nx * nz))

    coefficient = jnp.maximum(plane_mean(sum_lm) / (plane_mean(sum_mm) + 1e-06), 0.0)
    for k in range(count):
        x0, zb = (k // nz_parts) * width, k % nz_parts
        for x in range(width):
            out[k, x] = coefficient * mag[x0 + x, zb]


def sweep_kernel(parity, back, velocity, tendency, eddy, reduced, factors, tree):
    count, width, rows, _ = back.shape
    length = count * rows // SEGMENTS

    def fill(rank, place):
        for x in range(width):
            eddy[x, place * rows : (place + 1) * rows, :] = back[rank, x]

    by_parity(parity, count, fill)

    def row(ref, index, j):
        return ref[(*index, pl.ds(j, SEGMENTS, stride=length), slice(None))]

    for x in range(width):
        visc = 1.0 + row(eddy, (x,), 0)
        visc_first = visc
        q = jnp.ones_like(visc)
        m = jnp.ones_like(visc)
        corner = jnp.zeros_like(visc)
        first = [jnp.zeros_like(visc)] * 3
        value = None
        for j in range(length):
            if j < length - 1:
                visc_next = 1.0 + row(eddy, (x,), j + 1)
                link = 750.0 * (visc + visc_next)
                inverse = 1.0 / (q + link)
            else:
                visc_next = None
                link = None
                inverse = 1.0 / q
            left = m * inverse
            corner = corner + m * left
            source = [
                2.0 * row(velocity, (c, x), j) + row(tendency, (c, x), j) for c in range(3)
            ]
            if j > 0:
                source = [s + link_before * v for s, v in zip(source, value)]
            value = [s * inverse for s in source]
            first = [f + m * v for f, v in zip(first, value)]
            for c in range(3):
                factors[x, j, c] = value[c]
            factors[x, j, 3] = left
            if j < length - 1:
                ratio = link * inverse
                factors[x, j, 4] = ratio
                q = 1.0 + link * (q * inverse)
                m = m * ratio
                link_before = link
                visc = visc_next
            else:
                factors[x, j, 4] = inverse
        last = value
        across = left
        end = inverse
        links = 750.0 * (visc + pltpu.roll(visc_first, SEGMENTS - 1, 0))
        level, step = 0, 1
        while step < SEGMENTS:
            def other(v):
                return pltpu.roll(v, SEGMENTS - step, 0)

            link = links if step == 1 else pltpu.roll(links, SEGMENTS - (step - 1), 0)
            across_b = other(across)
            stiff = link / (1.0 + link * (end + other(corner)))
            flux = [stiff * (g - other(f)) for g, f in zip(last, first)]
            from_left = stiff * across
            from_right = stiff * across_b
            for c in range(3):
                tree[x, level, c] = flux[c]
            tree[x, level, 3] = from_left
            tree[x, level, 4] = from_right
            first = [f - across * t for f, t in zip(first, flux)]
            last = [other(g) + across_b * t for g, t in zip(last, flux)]
            corner = corner - across * from_left
            end = other(end) - across_b * from_right
            across = from_left * across_b
            level, step = level + 1, step * 2
        rows_out = [*first, *last, corner, across, end, visc_first]
        for i, v in enumerate(rows_out):
            reduced[i * width + x : i * width + x + 1, :] = v[0:1, :]
        i = len(rows_out)
        reduced[i * width + x : i * width + x + 1, :] = visc[SEGMENTS - 1 :, :]


def finish_kernel(devices, position, factors, tree, velocity, *rest):
    reduced, (out, gathered, fluxes) = rest[:devices], rest[devices:]
    width, length = factors.shape[:2]
    here = position[0]
    for shift in range(devices):
        gathered[lax.rem(here - shift + devices, devices)] = reduced[shift][...]

    def part(device, i):
        return gathered[device, i * width : (i + 1) * width, :]

    ratios, values = [], []
    for i in range(devices + 1):
        if i == 0:
            link = 750.0 * part(0, 9)
            total = part(0, 6)
            source = [-part(0, c) for c in range(3)]
        elif i == devices:
            link = 750.0 * part(i - 1, 10)
            total = part(i - 1, 8)
            source = [part(i - 1, 3 + c) for c in range(3)]
        else:
            link = 750.0 * (part(i - 1, 10) + part(i, 9))
            total = part(i - 1, 8) + part(i, 6)
            source = [part(i - 1, 3 + c) - part(i, c) for c in range(3)]
        pivot = 1.0 + link * total
        if i > 0:
            before = part(i - 1, 7)
            pivot = pivot - link * before * ratios[-1]
            source = [s + before * v for s, v in zip(source, values[-1])]
        scale = link / pivot
        values.append([scale * s for s in source])
        if i < devices:
            ratios.append(scale * part(i, 7))
    flux = values[devices]
    for i in range(devices, -1, -1):
        if i < devices:
            flux = [v + ratios[i] * f for v, f in zip(values[i], flux)]
        for c in range(3):
            fluxes[i, c * width : (c + 1) * width, :] = flux[c]

    sublane = lax.broadcasted_iota(jnp.int32, (SEGMENTS, LANES), 0)
    levels = tree.shape[1]
    for x in range(width):
        for c in range(3):
            r = c * width + x
            left = jnp.broadcast_to(fluxes[here, r : r + 1, :], (SEGMENTS, LANES))
            right = -jnp.broadcast_to(fluxes[here + 1, r : r + 1, :], (SEGMENTS, LANES))
            for level in range(levels - 1, -1, -1):
                step = 2**level
                through = tree[x, level, c] + tree[x, level, 3] * left - tree[x, level, 4] * right
                second = lax.rem(sublane, 2 * step) == step
                left = jnp.where(second, pltpu.roll(through, step, 0), left)
                right = jnp.where(second, pltpu.roll(right, step, 0), -through)
            value = right
            for j in range(length - 1, -1, -1):
                value = (factors[x, j, c] + factors[x, j, 3] * left) + factors[x, j, 4] * value
                rows = pl.ds(j, SEGMENTS, stride=length)
                out[c, x, rows, :] = value - velocity[c, x, rows, :]


def in_vmem(count):
    return [pl.BlockSpec(memory_space=pltpu.VMEM)] * count


def in_smem(count):
    return [pl.BlockSpec(memory_space=pltpu.SMEM)] * count


def params():
    return pltpu.CompilerParams(vmem_limit_bytes=VMEM_BYTES)


def body(velocity, tendency):
    _, width, cells, lanes = velocity.shape
    nz_parts = lax.axis_size("gz")
    count = lax.axis_size("gx") * nz_parts
    walls = lax.axis_size("gy")
    rows = cells // count
    nx = lax.axis_size("gx") * width
    padded = 16 + aligned(rows)
    f32 = jnp.float32

    planes = 3 * width
    depth = aligned(planes * rows + 2 * aligned(planes))
    position = lax.axis_index("gy").astype(jnp.int32).reshape(1)
    parity = lax.rem(position, 2)
    chunks = pl.pallas_call(
        functools.partial(pack_kernel, rows),
        out_shape=jax.ShapeDtypeStruct((count, depth, lanes), f32),
        in_specs=in_smem(1) + in_vmem(1),
        out_specs=pl.BlockSpec(memory_space=pltpu.VMEM),
        compiler_params=params(),
        name="pack",
    )(parity, velocity)
    recv = lax.all_to_all(chunks, ("gx", "gz"), split_axis=0, concat_axis=0, tiled=True)
    pairs = []
    for wall in range(walls - 1):
        outer = wall * count + outer_ranks(count)[1 - wall % 2]
        pairs += [(outer, outer + count), (outer + count, outer)]
    slot = lax.slice_in_dim(recv, planes * rows, planes * rows + aligned(planes), axis=1)
    swapped = lax.ppermute(slot, ("gy", "gx", "gz"), pairs)
    rank = lax.axis_index(("gx", "gz")).astype(jnp.int32).reshape(1)
    eddy_chunks = pl.pallas_call(
        functools.partial(germano_kernel, nz_parts, width, rows),
        out_shape=jax.ShapeDtypeStruct((count, width, rows, lanes), f32),
        in_specs=in_smem(2) + in_vmem(2),
        out_specs=pl.BlockSpec(memory_space=pltpu.VMEM),
        scratch_shapes=[
            pltpu.VMEM((3, nx, nz_parts, padded, lanes), f32),
            pltpu.VMEM((3, nx, nz_parts, padded, lanes), f32),
            pltpu.VMEM((3, nx, nz_parts, 8, lanes), f32),
            pltpu.VMEM((nx, nz_parts, rows, lanes), f32),
            pltpu.VMEM((15, nx, nz_parts, rows, lanes), f32),
        ],
        compiler_params=params(),
        name="germano",
    )(rank, parity, recv, swapped)
    back = lax.all_to_all(eddy_chunks, ("gx", "gz"), split_axis=0, concat_axis=0, tiled=True)

    length = cells // SEGMENTS
    levels = SEGMENTS.bit_length() - 1
    packed = aligned(11 * width)
    eddy, reduced, factors, tree = pl.pallas_call(
        sweep_kernel,
        out_shape=(
            jax.ShapeDtypeStruct((width, cells, lanes), f32),
            jax.ShapeDtypeStruct((packed, lanes), f32),
            jax.ShapeDtypeStruct((width, length, 5, SEGMENTS, lanes), f32),
            jax.ShapeDtypeStruct((width, levels, 5, SEGMENTS, lanes), f32),
        ),
        in_specs=in_smem(1) + in_vmem(3),
        out_specs=tuple(in_vmem(4)),
        compiler_params=params(),
        name="sweep",
    )(parity, back, velocity, tendency)

    others = [
        lax.ppermute(reduced, "gy", [(i, (i + shift) % walls) for i in range(walls)])
        for shift in range(1, walls)
    ]
    new_velocity = pl.pallas_call(
        functools.partial(finish_kernel, walls),
        out_shape=jax.ShapeDtypeStruct(velocity.shape, f32),
        in_specs=in_smem(1) + in_vmem(3 + walls),
        out_specs=pl.BlockSpec(memory_space=pltpu.VMEM),
        scratch_shapes=[
            pltpu.VMEM((walls, packed, lanes), f32),
            pltpu.VMEM((walls + 1, aligned(3 * width), lanes), f32),
        ],
        compiler_params=params(),
        name="finish",
    )(position, factors, tree, velocity, reduced, *others)
    return (new_velocity, eddy)


def solution(mesh):
    return jax.shard_map(
        body,
        mesh=mesh,
        in_specs=(P(None, "gx", "gy", "gz"), P(None, "gx", "gy", "gz")),
        out_specs=(P(None, "gx", "gy", "gz"), P("gx", "gy", "gz")),
        check_vma=False,
    )
```

```python
import functools

import jax
import jax.numpy as jnp
from jax import lax
from jax.experimental import pallas as pl
from jax.experimental.pallas import tpu as pltpu
from jax.sharding import PartitionSpec as P

LANES = 128
SEGMENTS = 8
VMEM_BYTES = 24 * 2**20


def strain_parts(grad_x, grad_y, grad_z):
    return (
        grad_x[0],
        grad_y[1],
        grad_z[2],
        grad_y[0] + grad_x[1],
        grad_z[0] + grad_x[2],
        grad_z[1] + grad_y[2],
    )


def strain_size(parts):
    diagonal = parts[0] * parts[0] + parts[1] * parts[1] + parts[2] * parts[2]
    mixed = parts[3] * parts[3] + parts[4] * parts[4] + parts[5] * parts[5]
    return jnp.sqrt(0.5 * diagonal + 0.25 * mixed)


def beside(blocks):
    count = len(blocks)
    lanes = blocks[0].shape[1]
    down = [pltpu.roll(f, 1, 1) for f in blocks]
    up = [pltpu.roll(f, lanes - 1, 1) for f in blocks]
    if count > 1:
        lane = lax.broadcasted_iota(jnp.int32, blocks[0].shape, 1)
        first, last = lane == 0, lane == lanes - 1
        down, up = (
            [jnp.where(first, down[i - 1], down[i]) for i in range(count)],
            [jnp.where(last, up[(i + 1) % count], up[i]) for i in range(count)],
        )
    return down, up


def slope_z(blocks):
    down, up = beside(blocks)
    return [u - d for u, d in zip(up, down)]


def smooth_z(blocks):
    down, up = beside(blocks)
    return [(u + d) + 2.0 * f for f, u, d in zip(blocks, up, down)]


def products(v):
    return (v[0] * v[0], v[1] * v[1], v[2] * v[2], v[0] * v[1], v[0] * v[2], v[1] * v[2])


def outer_ranks(count):
    return (count - 1, count - 3)


def places(parity, count):
    outer = outer_ranks(count)
    inner = iter(range(1, count - 1))
    return [
        (0 if outer[parity] == rank else count - 1) if rank in outer else next(inner)
        for rank in range(count)
    ]


def by_parity(parity, count, fill):
    outer = outer_ranks(count)
    for rank, place in enumerate(places(0, count)):
        if rank not in outer:
            fill(rank, place)
    for turn in range(2):

        @pl.when(parity[0] == turn)
        def _():
            for rank in outer:
                fill(rank, places(turn, count)[rank])


def aligned(n):
    return -(-n // 8) * 8


def pack_kernel(rows, parity, velocity, out):
    _, width, cells, _ = velocity.shape
    count, depth, lanes = out.shape
    planes = 3 * width
    slots = planes * rows

    def fill(rank, place):
        first = place * rows
        beside = [first - 1, first + rows]
        if place == 0:
            beside = [first, first + rows]
        if place == count - 1:
            beside = [first + rows - 1, first - 1]
        for i in range(planes):
            c, x = divmod(i, width)
            out[rank, i * rows : (i + 1) * rows, :] = velocity[c, x, first : first + rows, :]
            for slot, row in enumerate(beside):
                at = slots + slot * aligned(planes) + i
                out[rank, at : at + 1, :] = velocity[c, x, row : row + 1, :]

    by_parity(parity, count, fill)
    blank = aligned(planes) - planes
    for rank in range(count):
        for slot in range(2):
            at = slots + slot * aligned(planes) + planes
            out[rank, at : at + blank, :] = jnp.zeros((blank, lanes), jnp.float32)
        at = slots + 2 * aligned(planes)
        if at < depth:
            out[rank, at:, :] = jnp.zeros((depth - at, lanes), jnp.float32)


def outer_sides(rank, parity, count):
    outer = outer_ranks(count)
    even = parity[0] == 0
    bottom = rank[0] == jnp.where(even, outer[0], outer[1])
    top = rank[0] == jnp.where(even, outer[1], outer[0])
    return bottom, top


def edge_kernel(nz_parts, width, rows, rank, parity, recv, swapped, given, out, vel):
    count, _, lanes = recv.shape
    planes = 3 * width
    nx = (count // nz_parts) * width
    nz = nz_parts * lanes
    bottom, top = outer_sides(rank, parity, count)

    def rows_of(k, i):
        first = i * rows
        own = [recv[k, first + j : first + j + 1, :] for j in (0, 1, rows - 2, rows - 1)]
        far = swapped[k, i : i + 1, :]
        return (
            jnp.where(bottom, far, own[2]),
            jnp.where(bottom, own[0], own[3]),
            jnp.where(bottom, own[1], far),
        )

    def roll_x(f, shift):
        return pltpu.roll(f, shift % nx, 0)

    def roll_z(f, shift):
        return pltpu.roll(f, shift % nz, 1)

    def smooth_x(f):
        return (roll_x(f, 1) + roll_x(f, -1)) + 2.0 * f

    def smooth(f):
        f = smooth_x(f)
        return (roll_z(f, 1) + roll_z(f, -1)) + 2.0 * f

    def slopes(below, centre, above):
        return strain_parts(
            [roll_x(f, -1) - roll_x(f, 1) for f in centre],
            [a - b for a, b in zip(above, below)],
            [roll_z(f, -1) - roll_z(f, 1) for f in centre],
        )

    @pl.when(jnp.logical_or(bottom, top))
    def _():
        for k in range(count):
            x0, zb = (k // nz_parts) * width, k % nz_parts
            for i in range(planes):
                c, x = divmod(i, width)
                for j, row in enumerate(rows_of(k, i)):
                    vel[j, c, x0 + x : x0 + x + 1, zb * lanes : (zb + 1) * lanes] = row
        u = [[vel[j, c] for c in range(3)] for j in range(3)]
        v = [[smooth(f) for f in row] for row in u]
        strain = slopes(*u)
        size = strain_size(strain)
        mean_strain = slopes(*v)
        mean_size = 0.25 * strain_size(mean_strain)
        scaled = [0.0625 * f for f in v[1]]
        pairs = [v[1][i] * scaled[j] for i, j in ((0, 0), (1, 1), (2, 2), (0, 1), (0, 2), (1, 2))]
        leonard = [smooth(p) - q for p, q in zip(products(u[1]), pairs)]
        model = [smooth(size * s) - mean_size * f for s, f in zip(strain, mean_strain)]
        lm, mm = contracted(leonard, model)
        coefficient = coefficient_of(
            *(jnp.sum(f, axis=(0, 1), keepdims=True) for f in (lm, mm)), nx * nz
        )
        eddy = coefficient * size

        def put(at):
            for k in range(count):
                x0, zb = (k // nz_parts) * width, k % nz_parts
                for x in range(width):
                    out[k, x, at : at + 1, :] = eddy[x0 + x : x0 + x + 1, zb * lanes : (zb + 1) * lanes]

        pl.when(bottom)(lambda: put(0))
        pl.when(top)(lambda: put(rows - 1))


def contracted(leonard, model):
    lm = mm = None
    for i in range(6):
        square = model[i] * model[i] if i < 3 else (0.5 * model[i]) * model[i]
        product = leonard[i] * model[i]
        lm = product if lm is None else lm + product
        mm = square if mm is None else mm + square
    return lm, mm


def coefficient_of(plane_lm, plane_mm, cells):
    scale = 1.0 / (256.0 * cells)
    return jnp.maximum(plane_lm * scale / (plane_mm * scale + 1e-06), 0.0)


def germano_kernel(nz_parts, width, rows, rank, parity, recv, out, vel, filt, ends, mag, part):
    count, _, lanes = recv.shape
    planes = 3 * width
    _, top = outer_sides(rank, parity, count)
    nx = (count // nz_parts) * width
    nz = nz_parts * lanes
    blocks = range(nz_parts)
    lead = 8
    inner = slice(lead, lead + rows)
    lower = slice(lead - 1, lead - 1 + rows)
    upper = slice(lead + 1, lead + 1 + rows)
    for k in range(count):
        x0, zb = (k // nz_parts) * width, k % nz_parts
        for c in range(3):
            for x in range(width):
                i = c * width + x
                vel[c, x0 + x, zb, inner, :] = recv[k, i * rows : (i + 1) * rows, :]
                slots = planes * rows + i
                near = recv[k, slots : slots + 1, :]
                slots += aligned(planes)
                other = recv[k, slots : slots + 1, :]
                below = jnp.where(top, other, near)
                for side, (edge, at) in enumerate(((below, lead - 1), (other, lead + rows))):
                    vel[c, x0 + x, zb, at : at + 1, :] = edge
                    ends[c, x0 + x, zb, side : side + 1, :] = edge

    for x in range(nx):
        left, right = (x - 1) % nx, (x + 1) % nx
        centre = [[vel[c, x, zb, inner, :] for zb in blocks] for c in range(3)]
        grad_x = [[vel[c, right, zb, inner, :] - vel[c, left, zb, inner, :] for zb in blocks] for c in range(3)]
        grad_y = [[vel[c, x, zb, upper, :] - vel[c, x, zb, lower, :] for zb in blocks] for c in range(3)]
        grad_z = []
        for c in range(3):
            down, up = beside(centre[c])
            grad_z.append([u - d for u, d in zip(up, down)])
            for zb in blocks:
                part[c, x, zb] = (up[zb] + down[zb]) + 2.0 * centre[c][zb]
        strain = [
            strain_parts(*([g[c][zb] for c in range(3)] for g in (grad_x, grad_y, grad_z)))
            for zb in blocks
        ]
        size = [strain_size(s) for s in strain]
        for zb in blocks:
            mag[x, zb] = size[zb]
        pairs = [products([centre[c][zb] for c in range(3)]) for zb in blocks]
        for i in range(6):
            for base, fields in (
                (3, [pairs[zb][i] for zb in blocks]),
                (9, [size[zb] * strain[zb][i] for zb in blocks]),
            ):
                for zb, f in enumerate(smooth_z(fields)):
                    part[base + i, x, zb] = f

    def smooth_x(read, x):
        return (read((x - 1) % nx) + read((x + 1) % nx)) + 2.0 * read(x)

    for c in range(3):
        rims = []
        for x in range(nx):
            rims.append(smooth_z([ends[c, x, zb] for zb in blocks]))
        for x in range(nx):
            for zb in blocks:
                rim = smooth_x(lambda at: rims[at][zb], x)
                filt[c, x, zb, lead - 1 : lead, :] = rim[0:1, :]
                filt[c, x, zb, lead + rows : lead + rows + 1, :] = rim[1:2, :]
                filt[c, x, zb, inner, :] = smooth_x(lambda at: part[c, at, zb], x)

    sum_lm = sum_mm = None
    for x in range(nx):
        left, right = (x - 1) % nx, (x + 1) % nx
        mean = [[filt[c, x, zb, inner, :] for zb in blocks] for c in range(3)]
        grad_x = [[filt[c, right, zb, inner, :] - filt[c, left, zb, inner, :] for zb in blocks] for c in range(3)]
        grad_y = [[filt[c, x, zb, upper, :] - filt[c, x, zb, lower, :] for zb in blocks] for c in range(3)]
        grad_z = [slope_z(mean[c]) for c in range(3)]
        for zb in blocks:
            strain = strain_parts(*([g[c][zb] for c in range(3)] for g in (grad_x, grad_y, grad_z)))
            size = 0.25 * strain_size(strain)
            v = [mean[c][zb] for c in range(3)]
            scaled = [0.0625 * f for f in v]
            pairs = (
                v[0] * scaled[0],
                v[1] * scaled[1],
                v[2] * scaled[2],
                v[0] * scaled[1],
                v[0] * scaled[2],
                v[1] * scaled[2],
            )
            leonard = [smooth_x(lambda at: part[3 + i, at, zb], x) - pairs[i] for i in range(6)]
            model = [smooth_x(lambda at: part[9 + i, at, zb], x) - size * strain[i] for i in range(6)]
            lm, mm = contracted(leonard, model)
            sum_lm = lm if sum_lm is None else sum_lm + lm
            sum_mm = mm if sum_mm is None else sum_mm + mm

    coefficient = coefficient_of(
        *(jnp.sum(total, axis=1, keepdims=True) for total in (sum_lm, sum_mm)), nx * nz
    )
    for k in range(count):
        x0, zb = (k // nz_parts) * width, k % nz_parts
        for x in range(width):
            out[k, x] = coefficient * mag[x0 + x, zb]


def sweep_kernel(parity, back, velocity, tendency, eddy, reduced, factors, tree):
    count, width, rows, _ = back.shape
    length = count * rows // SEGMENTS

    def fill(rank, place):
        for x in range(width):
            eddy[x, place * rows : (place + 1) * rows, :] = back[rank, x]

    by_parity(parity, count, fill)

    def row(ref, index, j):
        return ref[(*index, pl.ds(j, SEGMENTS, stride=length), slice(None))]

    for x in range(width):
        visc = 1.0 + row(eddy, (x,), 0)
        visc_first = visc
        q = jnp.ones_like(visc)
        m = jnp.ones_like(visc)
        corner = jnp.zeros_like(visc)
        first = [jnp.zeros_like(visc)] * 3
        value = None
        for j in range(length):
            if j < length - 1:
                visc_next = 1.0 + row(eddy, (x,), j + 1)
                link = 750.0 * (visc + visc_next)
                inverse = 1.0 / (q + link)
            else:
                visc_next = None
                link = None
                inverse = 1.0 / q
            left = m * inverse
            corner = corner + m * left
            source = [
                2.0 * row(velocity, (c, x), j) + row(tendency, (c, x), j) for c in range(3)
            ]
            if j > 0:
                source = [s + link_before * v for s, v in zip(source, value)]
            value = [s * inverse for s in source]
            first = [f + m * v for f, v in zip(first, value)]
            for c in range(3):
                factors[x, j, c] = value[c]
            factors[x, j, 3] = left
            if j < length - 1:
                ratio = link * inverse
                factors[x, j, 4] = ratio
                q = 1.0 + link * (q * inverse)
                m = m * ratio
                link_before = link
                visc = visc_next
            else:
                factors[x, j, 4] = inverse
        last = value
        across = left
        end = inverse
        links = 750.0 * (visc + pltpu.roll(visc_first, SEGMENTS - 1, 0))
        level, step = 0, 1
        while step < SEGMENTS:
            def other(v):
                return pltpu.roll(v, SEGMENTS - step, 0)

            link = links if step == 1 else pltpu.roll(links, SEGMENTS - (step - 1), 0)
            across_b = other(across)
            stiff = link / (1.0 + link * (end + other(corner)))
            flux = [stiff * (g - other(f)) for g, f in zip(last, first)]
            from_left = stiff * across
            from_right = stiff * across_b
            for c in range(3):
                tree[x, level, c] = flux[c]
            tree[x, level, 3] = from_left
            tree[x, level, 4] = from_right
            first = [f - across * t for f, t in zip(first, flux)]
            last = [other(g) + across_b * t for g, t in zip(last, flux)]
            corner = corner - across * from_left
            end = other(end) - across_b * from_right
            across = from_left * across_b
            level, step = level + 1, step * 2
        rows_out = [*first, *last, corner, across, end, visc_first]
        for i, v in enumerate(rows_out):
            reduced[i * width + x : i * width + x + 1, :] = v[0:1, :]
        i = len(rows_out)
        reduced[i * width + x : i * width + x + 1, :] = visc[SEGMENTS - 1 :, :]


def finish_kernel(devices, position, factors, tree, velocity, *rest):
    reduced, (out, gathered, fluxes) = rest[:devices], rest[devices:]
    width, length = factors.shape[:2]
    here = position[0]
    for shift in range(devices):
        gathered[lax.rem(here - shift + devices, devices)] = reduced[shift][...]

    def part(device, i):
        return gathered[device, i * width : (i + 1) * width, :]

    ratios, values = [], []
    for i in range(devices + 1):
        if i == 0:
            link = 750.0 * part(0, 9)
            total = part(0, 6)
            source = [-part(0, c) for c in range(3)]
        elif i == devices:
            link = 750.0 * part(i - 1, 10)
            total = part(i - 1, 8)
            source = [part(i - 1, 3 + c) for c in range(3)]
        else:
            link = 750.0 * (part(i - 1, 10) + part(i, 9))
            total = part(i - 1, 8) + part(i, 6)
            source = [part(i - 1, 3 + c) - part(i, c) for c in range(3)]
        pivot = 1.0 + link * total
        if i > 0:
            before = part(i - 1, 7)
            pivot = pivot - link * before * ratios[-1]
            source = [s + before * v for s, v in zip(source, values[-1])]
        scale = link / pivot
        values.append([scale * s for s in source])
        if i < devices:
            ratios.append(scale * part(i, 7))
    flux = values[devices]
    for i in range(devices, -1, -1):
        if i < devices:
            flux = [v + ratios[i] * f for v, f in zip(values[i], flux)]
        for c in range(3):
            fluxes[i, c * width : (c + 1) * width, :] = flux[c]

    sublane = lax.broadcasted_iota(jnp.int32, (SEGMENTS, LANES), 0)
    levels = tree.shape[1]
    for x in range(width):
        for c in range(3):
            r = c * width + x
            left = jnp.broadcast_to(fluxes[here, r : r + 1, :], (SEGMENTS, LANES))
            right = -jnp.broadcast_to(fluxes[here + 1, r : r + 1, :], (SEGMENTS, LANES))
            for level in range(levels - 1, -1, -1):
                step = 2**level
                through = tree[x, level, c] + tree[x, level, 3] * left - tree[x, level, 4] * right
                second = lax.rem(sublane, 2 * step) == step
                left = jnp.where(second, pltpu.roll(through, step, 0), left)
                right = jnp.where(second, pltpu.roll(right, step, 0), -through)
            value = right
            for j in range(length - 1, -1, -1):
                value = (factors[x, j, c] + factors[x, j, 3] * left) + factors[x, j, 4] * value
                rows = pl.ds(j, SEGMENTS, stride=length)
                out[c, x, rows, :] = value - velocity[c, x, rows, :]


def in_vmem(count):
    return [pl.BlockSpec(memory_space=pltpu.VMEM)] * count


def in_smem(count):
    return [pl.BlockSpec(memory_space=pltpu.SMEM)] * count


def params():
    return pltpu.CompilerParams(vmem_limit_bytes=VMEM_BYTES)


def body(velocity, tendency):
    _, width, cells, lanes = velocity.shape
    nz_parts = lax.axis_size("gz")
    count = lax.axis_size("gx") * nz_parts
    walls = lax.axis_size("gy")
    rows = cells // count
    nx = lax.axis_size("gx") * width
    padded = 16 + aligned(rows)
    f32 = jnp.float32

    planes = 3 * width
    depth = aligned(planes * rows + 2 * aligned(planes))
    position = lax.axis_index("gy").astype(jnp.int32).reshape(1)
    parity = lax.rem(position, 2)
    chunks = pl.pallas_call(
        functools.partial(pack_kernel, rows),
        out_shape=jax.ShapeDtypeStruct((count, depth, lanes), f32),
        in_specs=in_smem(1) + in_vmem(1),
        out_specs=pl.BlockSpec(memory_space=pltpu.VMEM),
        compiler_params=params(),
        name="pack",
    )(parity, velocity)
    recv = lax.all_to_all(chunks, ("gx", "gz"), split_axis=0, concat_axis=0, tiled=True)
    pairs = []
    for wall in range(walls - 1):
        outer = wall * count + outer_ranks(count)[1 - wall % 2]
        pairs += [(outer, outer + count), (outer + count, outer)]
    slot = lax.slice_in_dim(recv, planes * rows, planes * rows + aligned(planes), axis=1)
    swapped = lax.ppermute(slot, ("gy", "gx", "gz"), pairs)
    rank = lax.axis_index(("gx", "gz")).astype(jnp.int32).reshape(1)
    chunk_shape = jax.ShapeDtypeStruct((count, width, rows, lanes), f32)
    cells_here = nx * nz_parts * rows * lanes
    provisional = pl.pallas_call(
        functools.partial(germano_kernel, nz_parts, width, rows),
        out_shape=chunk_shape,
        in_specs=in_smem(2) + in_vmem(1),
        out_specs=pl.BlockSpec(memory_space=pltpu.VMEM),
        scratch_shapes=[
            pltpu.VMEM((3, nx, nz_parts, padded, lanes), f32),
            pltpu.VMEM((3, nx, nz_parts, padded, lanes), f32),
            pltpu.VMEM((3, nx, nz_parts, 8, lanes), f32),
            pltpu.VMEM((nx, nz_parts, rows, lanes), f32),
            pltpu.VMEM((15, nx, nz_parts, rows, lanes), f32),
        ],
        compiler_params=params(),
        cost_estimate=pl.CostEstimate(
            flops=300 * cells_here, bytes_accessed=16 * cells_here, transcendentals=2 * cells_here
        ),
        name="germano",
    )(rank, parity, recv)
    eddy_chunks = pl.pallas_call(
        functools.partial(edge_kernel, nz_parts, width, rows),
        out_shape=chunk_shape,
        in_specs=in_smem(2) + in_vmem(3),
        out_specs=pl.BlockSpec(memory_space=pltpu.VMEM),
        scratch_shapes=[pltpu.VMEM((3, 3, nx, nz_parts * lanes), f32)],
        input_output_aliases={4: 0},
        compiler_params=params(),
        name="edge",
    )(rank, parity, recv, swapped, provisional)
    back = lax.all_to_all(eddy_chunks, ("gx", "gz"), split_axis=0, concat_axis=0, tiled=True)

    length = cells // SEGMENTS
    levels = SEGMENTS.bit_length() - 1
    packed = aligned(11 * width)
    eddy, reduced, factors, tree = pl.pallas_call(
        sweep_kernel,
        out_shape=(
            jax.ShapeDtypeStruct((width, cells, lanes), f32),
            jax.ShapeDtypeStruct((packed, lanes), f32),
            jax.ShapeDtypeStruct((width, length, 5, SEGMENTS, lanes), f32),
            jax.ShapeDtypeStruct((width, levels, 5, SEGMENTS, lanes), f32),
        ),
        in_specs=in_smem(1) + in_vmem(3),
        out_specs=tuple(in_vmem(4)),
        compiler_params=params(),
        name="sweep",
    )(parity, back, velocity, tendency)

    others = [
        lax.ppermute(reduced, "gy", [(i, (i + shift) % walls) for i in range(walls)])
        for shift in range(1, walls)
    ]
    new_velocity = pl.pallas_call(
        functools.partial(finish_kernel, walls),
        out_shape=jax.ShapeDtypeStruct(velocity.shape, f32),
        in_specs=in_smem(1) + in_vmem(3 + walls),
        out_specs=pl.BlockSpec(memory_space=pltpu.VMEM),
        scratch_shapes=[
            pltpu.VMEM((walls, packed, lanes), f32),
            pltpu.VMEM((walls + 1, aligned(3 * width), lanes), f32),
        ],
        compiler_params=params(),
        name="finish",
    )(position, factors, tree, velocity, reduced, *others)
    return (new_velocity, eddy)


def solution(mesh):
    return jax.shard_map(
        body,
        mesh=mesh,
        in_specs=(P(None, "gx", "gy", "gz"), P(None, "gx", "gy", "gz")),
        out_specs=(P(None, "gx", "gy", "gz"), P("gx", "gy", "gz")),
        check_vma=False,
    )
```

```python
import functools

import jax
import jax.numpy as jnp
from jax import lax
from jax.experimental import pallas as pl
from jax.experimental.pallas import tpu as pltpu
from jax.sharding import PartitionSpec as P

LANES = 128
SEGMENTS = 8
VMEM_BYTES = 24 * 2**20


def strain_parts(grad_x, grad_y, grad_z):
    return (
        grad_x[0],
        grad_y[1],
        grad_z[2],
        grad_y[0] + grad_x[1],
        grad_z[0] + grad_x[2],
        grad_z[1] + grad_y[2],
    )


def strain_size(parts):
    diagonal = parts[0] * parts[0] + parts[1] * parts[1] + parts[2] * parts[2]
    mixed = parts[3] * parts[3] + parts[4] * parts[4] + parts[5] * parts[5]
    return jnp.sqrt(0.5 * diagonal + 0.25 * mixed)


def beside(blocks):
    count = len(blocks)
    lanes = blocks[0].shape[1]
    down = [pltpu.roll(f, 1, 1) for f in blocks]
    up = [pltpu.roll(f, lanes - 1, 1) for f in blocks]
    if count > 1:
        lane = lax.broadcasted_iota(jnp.int32, blocks[0].shape, 1)
        first, last = lane == 0, lane == lanes - 1
        down, up = (
            [jnp.where(first, down[i - 1], down[i]) for i in range(count)],
            [jnp.where(last, up[(i + 1) % count], up[i]) for i in range(count)],
        )
    return down, up


def slope_z(blocks):
    down, up = beside(blocks)
    return [u - d for u, d in zip(up, down)]


def smooth_z(blocks):
    down, up = beside(blocks)
    return [(u + d) + 2.0 * f for f, u, d in zip(blocks, up, down)]


def products(v):
    return (v[0] * v[0], v[1] * v[1], v[2] * v[2], v[0] * v[1], v[0] * v[2], v[1] * v[2])


def outer_ranks(count):
    return (count - 1, count - 3)


def places(parity, count):
    outer = outer_ranks(count)
    inner = iter(range(1, count - 1))
    return [
        (0 if outer[parity] == rank else count - 1) if rank in outer else next(inner)
        for rank in range(count)
    ]


def by_parity(parity, count, fill):
    outer = outer_ranks(count)
    for rank, place in enumerate(places(0, count)):
        if rank not in outer:
            fill(rank, place)
    for turn in range(2):

        @pl.when(parity[0] == turn)
        def _():
            for rank in outer:
                fill(rank, places(turn, count)[rank])


def aligned(n):
    return -(-n // 8) * 8


def pack_kernel(rows, parity, velocity, out):
    _, width, cells, _ = velocity.shape
    count, depth, lanes = out.shape
    planes = 3 * width
    slots = planes * rows

    def fill(rank, place):
        first = place * rows
        beside = [first - 1, first + rows]
        if place == 0:
            beside = [first, first + rows]
        if place == count - 1:
            beside = [first + rows - 1, first - 1]
        for i in range(planes):
            c, x = divmod(i, width)
            out[rank, i * rows : (i + 1) * rows, :] = velocity[c, x, first : first + rows, :]
            for slot, row in enumerate(beside):
                at = slots + slot * aligned(planes) + i
                out[rank, at : at + 1, :] = velocity[c, x, row : row + 1, :]

    by_parity(parity, count, fill)
    blank = aligned(planes) - planes
    for rank in range(count):
        for slot in range(2):
            at = slots + slot * aligned(planes) + planes
            out[rank, at : at + blank, :] = jnp.zeros((blank, lanes), jnp.float32)
        at = slots + 2 * aligned(planes)
        if at < depth:
            out[rank, at:, :] = jnp.zeros((depth - at, lanes), jnp.float32)


def outer_sides(rank, parity, count):
    outer = outer_ranks(count)
    even = parity[0] == 0
    bottom = rank[0] == jnp.where(even, outer[0], outer[1])
    top = rank[0] == jnp.where(even, outer[1], outer[0])
    return bottom, top


def edge_kernel(nz_parts, width, rows, rank, parity, recv, swapped, given, out, vel):
    count, _, lanes = recv.shape
    planes = 3 * width
    nx = (count // nz_parts) * width
    nz = nz_parts * lanes
    bottom, top = outer_sides(rank, parity, count)

    def rows_of(k, i):
        first = i * rows
        own = [recv[k, first + j : first + j + 1, :] for j in (0, 1, rows - 2, rows - 1)]
        far = swapped[k, i : i + 1, :]
        return (
            jnp.where(bottom, far, own[2]),
            jnp.where(bottom, own[0], own[3]),
            jnp.where(bottom, own[1], far),
        )

    def roll_x(f, shift):
        return pltpu.roll(f, shift % nx, 0)

    def roll_z(f, shift):
        return pltpu.roll(f, shift % nz, 1)

    def smooth_x(f):
        return (roll_x(f, 1) + roll_x(f, -1)) + 2.0 * f

    def smooth(f):
        f = smooth_x(f)
        return (roll_z(f, 1) + roll_z(f, -1)) + 2.0 * f

    def slopes(below, centre, above):
        return strain_parts(
            [roll_x(f, -1) - roll_x(f, 1) for f in centre],
            [a - b for a, b in zip(above, below)],
            [roll_z(f, -1) - roll_z(f, 1) for f in centre],
        )

    @pl.when(jnp.logical_or(bottom, top))
    def _():
        for k in range(count):
            x0, zb = (k // nz_parts) * width, k % nz_parts
            for i in range(planes):
                c, x = divmod(i, width)
                for j, row in enumerate(rows_of(k, i)):
                    vel[j, c, x0 + x : x0 + x + 1, zb * lanes : (zb + 1) * lanes] = row
        u = [[vel[j, c] for c in range(3)] for j in range(3)]
        v = [[smooth(f) for f in row] for row in u]
        strain = slopes(*u)
        size = strain_size(strain)
        mean_strain = slopes(*v)
        mean_size = 0.25 * strain_size(mean_strain)
        scaled = [0.0625 * f for f in v[1]]
        pairs = [v[1][i] * scaled[j] for i, j in ((0, 0), (1, 1), (2, 2), (0, 1), (0, 2), (1, 2))]
        leonard = [smooth(p) - q for p, q in zip(products(u[1]), pairs)]
        model = [smooth(size * s) - mean_size * f for s, f in zip(strain, mean_strain)]
        lm, mm = contracted(leonard, model)
        coefficient = coefficient_of(
            *(jnp.sum(f, axis=(0, 1), keepdims=True) for f in (lm, mm)), nx * nz
        )
        eddy = coefficient * size

        def put(at):
            for k in range(count):
                x0, zb = (k // nz_parts) * width, k % nz_parts
                for x in range(width):
                    out[k, x, at : at + 1, :] = eddy[x0 + x : x0 + x + 1, zb * lanes : (zb + 1) * lanes]

        pl.when(bottom)(lambda: put(0))
        pl.when(top)(lambda: put(rows - 1))


def contracted(leonard, model):
    lm = mm = None
    for i in range(6):
        square = model[i] * model[i] if i < 3 else (0.5 * model[i]) * model[i]
        product = leonard[i] * model[i]
        lm = product if lm is None else lm + product
        mm = square if mm is None else mm + square
    return lm, mm


def coefficient_of(plane_lm, plane_mm, cells):
    scale = 1.0 / (256.0 * cells)
    return jnp.maximum(plane_lm * scale / (plane_mm * scale + 1e-06), 0.0)


def germano_kernel(nz_parts, width, rows, rank, parity, recv, out, vel, filt, ends, mag, part):
    count, _, lanes = recv.shape
    planes = 3 * width
    _, top = outer_sides(rank, parity, count)
    nx = (count // nz_parts) * width
    nz = nz_parts * lanes
    blocks = range(nz_parts)
    lead = 8
    inner = slice(lead, lead + rows)
    lower = slice(lead - 1, lead - 1 + rows)
    upper = slice(lead + 1, lead + 1 + rows)
    for k in range(count):
        x0, zb = (k // nz_parts) * width, k % nz_parts
        for c in range(3):
            for x in range(width):
                i = c * width + x
                vel[c, x0 + x, zb, inner, :] = recv[k, i * rows : (i + 1) * rows, :]
                slots = planes * rows + i
                near = recv[k, slots : slots + 1, :]
                slots += aligned(planes)
                other = recv[k, slots : slots + 1, :]
                below = jnp.where(top, other, near)
                for side, (edge, at) in enumerate(((below, lead - 1), (other, lead + rows))):
                    vel[c, x0 + x, zb, at : at + 1, :] = edge
                    ends[c, x0 + x, zb, side : side + 1, :] = edge

    for x in range(nx):
        left, right = (x - 1) % nx, (x + 1) % nx
        centre = [[vel[c, x, zb, inner, :] for zb in blocks] for c in range(3)]
        grad_x = [[vel[c, right, zb, inner, :] - vel[c, left, zb, inner, :] for zb in blocks] for c in range(3)]
        grad_y = [[vel[c, x, zb, upper, :] - vel[c, x, zb, lower, :] for zb in blocks] for c in range(3)]
        grad_z = []
        for c in range(3):
            down, up = beside(centre[c])
            grad_z.append([u - d for u, d in zip(up, down)])
            for zb in blocks:
                part[c, x, zb] = (up[zb] + down[zb]) + 2.0 * centre[c][zb]
        strain = [
            strain_parts(*([g[c][zb] for c in range(3)] for g in (grad_x, grad_y, grad_z)))
            for zb in blocks
        ]
        size = [strain_size(s) for s in strain]
        for zb in blocks:
            mag[x, zb] = size[zb]
        pairs = [products([centre[c][zb] for c in range(3)]) for zb in blocks]
        for i in range(6):
            for base, fields in (
                (3, [pairs[zb][i] for zb in blocks]),
                (9, [size[zb] * strain[zb][i] for zb in blocks]),
            ):
                for zb, f in enumerate(smooth_z(fields)):
                    part[base + i, x, zb] = f

    def smooth_x(read, x):
        return (read((x - 1) % nx) + read((x + 1) % nx)) + 2.0 * read(x)

    for c in range(3):
        rims = []
        for x in range(nx):
            rims.append(smooth_z([ends[c, x, zb] for zb in blocks]))
        for x in range(nx):
            for zb in blocks:
                rim = smooth_x(lambda at: rims[at][zb], x)
                filt[c, x, zb, lead - 1 : lead, :] = rim[0:1, :]
                filt[c, x, zb, lead + rows : lead + rows + 1, :] = rim[1:2, :]
                filt[c, x, zb, inner, :] = smooth_x(lambda at: part[c, at, zb], x)

    sum_lm = sum_mm = None
    for x in range(nx):
        left, right = (x - 1) % nx, (x + 1) % nx
        mean = [[filt[c, x, zb, inner, :] for zb in blocks] for c in range(3)]
        grad_x = [[filt[c, right, zb, inner, :] - filt[c, left, zb, inner, :] for zb in blocks] for c in range(3)]
        grad_y = [[filt[c, x, zb, upper, :] - filt[c, x, zb, lower, :] for zb in blocks] for c in range(3)]
        grad_z = [slope_z(mean[c]) for c in range(3)]
        for zb in blocks:
            strain = strain_parts(*([g[c][zb] for c in range(3)] for g in (grad_x, grad_y, grad_z)))
            size = 0.25 * strain_size(strain)
            v = [mean[c][zb] for c in range(3)]
            scaled = [0.0625 * f for f in v]
            pairs = (
                v[0] * scaled[0],
                v[1] * scaled[1],
                v[2] * scaled[2],
                v[0] * scaled[1],
                v[0] * scaled[2],
                v[1] * scaled[2],
            )
            leonard = [smooth_x(lambda at: part[3 + i, at, zb], x) - pairs[i] for i in range(6)]
            model = [smooth_x(lambda at: part[9 + i, at, zb], x) - size * strain[i] for i in range(6)]
            lm, mm = contracted(leonard, model)
            sum_lm = lm if sum_lm is None else sum_lm + lm
            sum_mm = mm if sum_mm is None else sum_mm + mm

    coefficient = coefficient_of(
        *(jnp.sum(total, axis=1, keepdims=True) for total in (sum_lm, sum_mm)), nx * nz
    )
    for k in range(count):
        x0, zb = (k // nz_parts) * width, k % nz_parts
        for x in range(width):
            out[k, x] = coefficient * mag[x0 + x, zb]


def sweep_kernel(parity, back, velocity, tendency, eddy, reduced, factors, tree):
    count, width, rows, _ = back.shape
    length = count * rows // SEGMENTS

    def fill(rank, place):
        for x in range(width):
            eddy[x, place * rows : (place + 1) * rows, :] = back[rank, x]

    by_parity(parity, count, fill)

    def row(ref, index, j):
        return ref[(*index, pl.ds(j, SEGMENTS, stride=length), slice(None))]

    for x in range(width):
        visc = 1.0 + row(eddy, (x,), 0)
        visc_first = visc
        q = jnp.ones_like(visc)
        m = jnp.ones_like(visc)
        corner = jnp.zeros_like(visc)
        first = [jnp.zeros_like(visc)] * 3
        value = None
        for j in range(length):
            if j < length - 1:
                visc_next = 1.0 + row(eddy, (x,), j + 1)
                link = 750.0 * (visc + visc_next)
                inverse = 1.0 / (q + link)
            else:
                visc_next = None
                link = None
                inverse = 1.0 / q
            left = m * inverse
            corner = corner + m * left
            source = [
                2.0 * row(velocity, (c, x), j) + row(tendency, (c, x), j) for c in range(3)
            ]
            if j > 0:
                source = [s + link_before * v for s, v in zip(source, value)]
            value = [s * inverse for s in source]
            first = [f + m * v for f, v in zip(first, value)]
            for c in range(3):
                factors[x, j, c] = value[c]
            factors[x, j, 3] = left
            if j < length - 1:
                ratio = link * inverse
                factors[x, j, 4] = ratio
                q = 1.0 + link * (q * inverse)
                m = m * ratio
                link_before = link
                visc = visc_next
            else:
                factors[x, j, 4] = inverse
        last = value
        across = left
        end = inverse
        links = 750.0 * (visc + pltpu.roll(visc_first, SEGMENTS - 1, 0))
        level, step = 0, 1
        while step < SEGMENTS:
            def other(v):
                return pltpu.roll(v, SEGMENTS - step, 0)

            link = links if step == 1 else pltpu.roll(links, SEGMENTS - (step - 1), 0)
            across_b = other(across)
            stiff = link / (1.0 + link * (end + other(corner)))
            flux = [stiff * (g - other(f)) for g, f in zip(last, first)]
            from_left = stiff * across
            from_right = stiff * across_b
            for c in range(3):
                tree[x, level, c] = flux[c]
            tree[x, level, 3] = from_left
            tree[x, level, 4] = from_right
            first = [f - across * t for f, t in zip(first, flux)]
            last = [other(g) + across_b * t for g, t in zip(last, flux)]
            corner = corner - across * from_left
            end = other(end) - across_b * from_right
            across = from_left * across_b
            level, step = level + 1, step * 2
        rows_out = [*first, *last, corner, across, end, visc_first]
        for i, v in enumerate(rows_out):
            reduced[i * width + x : i * width + x + 1, :] = v[0:1, :]
        i = len(rows_out)
        reduced[i * width + x : i * width + x + 1, :] = visc[SEGMENTS - 1 :, :]


def partner(i, step, count):
    if count & (count - 1) == 0:
        return i ^ step
    return (i - step + count) % count


def finish_kernel(devices, position, factors, tree, velocity, *rest):
    reduced, (out, gathered, fluxes) = rest[:devices], rest[devices:]
    width, length = factors.shape[:2]
    here = position[0]
    for step in range(devices):
        gathered[partner(here, step, devices)] = reduced[step][...]

    def part(device, i):
        return gathered[device, i * width : (i + 1) * width, :]

    ratios, values = [], []
    for i in range(devices + 1):
        if i == 0:
            link = 750.0 * part(0, 9)
            total = part(0, 6)
            source = [-part(0, c) for c in range(3)]
        elif i == devices:
            link = 750.0 * part(i - 1, 10)
            total = part(i - 1, 8)
            source = [part(i - 1, 3 + c) for c in range(3)]
        else:
            link = 750.0 * (part(i - 1, 10) + part(i, 9))
            total = part(i - 1, 8) + part(i, 6)
            source = [part(i - 1, 3 + c) - part(i, c) for c in range(3)]
        pivot = 1.0 + link * total
        if i > 0:
            before = part(i - 1, 7)
            pivot = pivot - link * before * ratios[-1]
            source = [s + before * v for s, v in zip(source, values[-1])]
        scale = link / pivot
        values.append([scale * s for s in source])
        if i < devices:
            ratios.append(scale * part(i, 7))
    flux = values[devices]
    for i in range(devices, -1, -1):
        if i < devices:
            flux = [v + ratios[i] * f for v, f in zip(values[i], flux)]
        for c in range(3):
            fluxes[i, c * width : (c + 1) * width, :] = flux[c]

    sublane = lax.broadcasted_iota(jnp.int32, (SEGMENTS, LANES), 0)
    levels = tree.shape[1]
    for x in range(width):
        for c in range(3):
            r = c * width + x
            left = jnp.broadcast_to(fluxes[here, r : r + 1, :], (SEGMENTS, LANES))
            right = -jnp.broadcast_to(fluxes[here + 1, r : r + 1, :], (SEGMENTS, LANES))
            for level in range(levels - 1, -1, -1):
                step = 2**level
                through = tree[x, level, c] + tree[x, level, 3] * left - tree[x, level, 4] * right
                second = lax.rem(sublane, 2 * step) == step
                left = jnp.where(second, pltpu.roll(through, step, 0), left)
                right = jnp.where(second, pltpu.roll(right, step, 0), -through)
            value = right
            for j in range(length - 1, -1, -1):
                value = (factors[x, j, c] + factors[x, j, 3] * left) + factors[x, j, 4] * value
                rows = pl.ds(j, SEGMENTS, stride=length)
                out[c, x, rows, :] = value - velocity[c, x, rows, :]


def in_vmem(count):
    return [pl.BlockSpec(memory_space=pltpu.VMEM)] * count


def in_smem(count):
    return [pl.BlockSpec(memory_space=pltpu.SMEM)] * count


def params():
    return pltpu.CompilerParams(vmem_limit_bytes=VMEM_BYTES)


def body(velocity, tendency):
    _, width, cells, lanes = velocity.shape
    nz_parts = lax.axis_size("gz")
    count = lax.axis_size("gx") * nz_parts
    walls = lax.axis_size("gy")
    rows = cells // count
    nx = lax.axis_size("gx") * width
    padded = 16 + aligned(rows)
    f32 = jnp.float32

    planes = 3 * width
    depth = aligned(planes * rows + 2 * aligned(planes))
    position = lax.axis_index("gy").astype(jnp.int32).reshape(1)
    parity = lax.rem(position, 2)
    chunks = pl.pallas_call(
        functools.partial(pack_kernel, rows),
        out_shape=jax.ShapeDtypeStruct((count, depth, lanes), f32),
        in_specs=in_smem(1) + in_vmem(1),
        out_specs=pl.BlockSpec(memory_space=pltpu.VMEM),
        compiler_params=params(),
        name="pack",
    )(parity, velocity)
    recv = lax.all_to_all(chunks, ("gx", "gz"), split_axis=0, concat_axis=0, tiled=True)
    pairs = []
    for wall in range(walls - 1):
        outer = wall * count + outer_ranks(count)[1 - wall % 2]
        pairs += [(outer, outer + count), (outer + count, outer)]
    slot = lax.slice_in_dim(recv, planes * rows, planes * rows + aligned(planes), axis=1)
    swapped = lax.ppermute(slot, ("gy", "gx", "gz"), pairs)
    rank = lax.axis_index(("gx", "gz")).astype(jnp.int32).reshape(1)
    chunk_shape = jax.ShapeDtypeStruct((count, width, rows, lanes), f32)
    cells_here = nx * nz_parts * rows * lanes
    provisional = pl.pallas_call(
        functools.partial(germano_kernel, nz_parts, width, rows),
        out_shape=chunk_shape,
        in_specs=in_smem(2) + in_vmem(1),
        out_specs=pl.BlockSpec(memory_space=pltpu.VMEM),
        scratch_shapes=[
            pltpu.VMEM((3, nx, nz_parts, padded, lanes), f32),
            pltpu.VMEM((3, nx, nz_parts, padded, lanes), f32),
            pltpu.VMEM((3, nx, nz_parts, 8, lanes), f32),
            pltpu.VMEM((nx, nz_parts, rows, lanes), f32),
            pltpu.VMEM((15, nx, nz_parts, rows, lanes), f32),
        ],
        compiler_params=params(),
        cost_estimate=pl.CostEstimate(
            flops=300 * cells_here, bytes_accessed=16 * cells_here, transcendentals=2 * cells_here
        ),
        name="germano",
    )(rank, parity, recv)
    eddy_chunks = pl.pallas_call(
        functools.partial(edge_kernel, nz_parts, width, rows),
        out_shape=chunk_shape,
        in_specs=in_smem(2) + in_vmem(3),
        out_specs=pl.BlockSpec(memory_space=pltpu.VMEM),
        scratch_shapes=[pltpu.VMEM((3, 3, nx, nz_parts * lanes), f32)],
        input_output_aliases={4: 0},
        compiler_params=params(),
        name="edge",
    )(rank, parity, recv, swapped, provisional)
    back = lax.all_to_all(eddy_chunks, ("gx", "gz"), split_axis=0, concat_axis=0, tiled=True)

    length = cells // SEGMENTS
    levels = SEGMENTS.bit_length() - 1
    packed = aligned(11 * width)
    eddy, reduced, factors, tree = pl.pallas_call(
        sweep_kernel,
        out_shape=(
            jax.ShapeDtypeStruct((width, cells, lanes), f32),
            jax.ShapeDtypeStruct((packed, lanes), f32),
            jax.ShapeDtypeStruct((width, length, 5, SEGMENTS, lanes), f32),
            jax.ShapeDtypeStruct((width, levels, 5, SEGMENTS, lanes), f32),
        ),
        in_specs=in_smem(1) + in_vmem(3),
        out_specs=tuple(in_vmem(4)),
        compiler_params=params(),
        name="sweep",
    )(parity, back, velocity, tendency)

    others = [
        lax.ppermute(reduced, "gy", [(partner(i, step, walls), i) for i in range(walls)])
        for step in range(1, walls)
    ]
    new_velocity = pl.pallas_call(
        functools.partial(finish_kernel, walls),
        out_shape=jax.ShapeDtypeStruct(velocity.shape, f32),
        in_specs=in_smem(1) + in_vmem(3 + walls),
        out_specs=pl.BlockSpec(memory_space=pltpu.VMEM),
        scratch_shapes=[
            pltpu.VMEM((walls, packed, lanes), f32),
            pltpu.VMEM((walls + 1, aligned(3 * width), lanes), f32),
        ],
        compiler_params=params(),
        name="finish",
    )(position, factors, tree, velocity, reduced, *others)
    return (new_velocity, eddy)


def solution(mesh):
    return jax.shard_map(
        body,
        mesh=mesh,
        in_specs=(P(None, "gx", "gy", "gz"), P(None, "gx", "gy", "gz")),
        out_specs=(P(None, "gx", "gy", "gz"), P("gx", "gy", "gz")),
        check_vma=False,
    )
```

```python
import functools

import jax
import jax.numpy as jnp
from jax import lax
from jax.experimental import pallas as pl
from jax.experimental.pallas import tpu as pltpu
from jax.sharding import PartitionSpec as P

LANES = 128
SEGMENTS = 8
VMEM_BYTES = 24 * 2**20


def strain_parts(grad_x, grad_y, grad_z):
    return (
        grad_x[0],
        grad_y[1],
        grad_z[2],
        grad_y[0] + grad_x[1],
        grad_z[0] + grad_x[2],
        grad_z[1] + grad_y[2],
    )


def strain_size(parts):
    diagonal = parts[0] * parts[0] + parts[1] * parts[1] + parts[2] * parts[2]
    mixed = parts[3] * parts[3] + parts[4] * parts[4] + parts[5] * parts[5]
    return jnp.sqrt(0.5 * diagonal + 0.25 * mixed)


def beside(blocks):
    count = len(blocks)
    lanes = blocks[0].shape[1]
    down = [pltpu.roll(f, 1, 1) for f in blocks]
    up = [pltpu.roll(f, lanes - 1, 1) for f in blocks]
    if count > 1:
        lane = lax.broadcasted_iota(jnp.int32, blocks[0].shape, 1)
        first, last = lane == 0, lane == lanes - 1
        down, up = (
            [jnp.where(first, down[i - 1], down[i]) for i in range(count)],
            [jnp.where(last, up[(i + 1) % count], up[i]) for i in range(count)],
        )
    return down, up


def slope_z(blocks):
    down, up = beside(blocks)
    return [u - d for u, d in zip(up, down)]


def smooth_z(blocks):
    down, up = beside(blocks)
    return [(u + d) + 2.0 * f for f, u, d in zip(blocks, up, down)]


def products(v):
    return (v[0] * v[0], v[1] * v[1], v[2] * v[2], v[0] * v[1], v[0] * v[2], v[1] * v[2])


def outer_ranks(count):
    return (count - 1, count - 3)


def places(parity, count):
    outer = outer_ranks(count)
    inner = iter(range(1, count - 1))
    return [
        (0 if outer[parity] == rank else count - 1) if rank in outer else next(inner)
        for rank in range(count)
    ]


def by_parity(parity, count, fill):
    outer = outer_ranks(count)
    for rank, place in enumerate(places(0, count)):
        if rank not in outer:
            fill(rank, place)
    for turn in range(2):

        @pl.when(parity[0] == turn)
        def _():
            for rank in outer:
                fill(rank, places(turn, count)[rank])


def aligned(n):
    return -(-n // 8) * 8


def pack_kernel(rows, parity, velocity, out):
    _, width, cells, _ = velocity.shape
    count, depth, lanes = out.shape
    planes = 3 * width
    slots = planes * rows

    def fill(rank, place):
        first = place * rows
        beside = [first - 1, first + rows]
        if place == 0:
            beside = [first, first + rows]
        if place == count - 1:
            beside = [first + rows - 1, first - 1]
        for i in range(planes):
            c, x = divmod(i, width)
            out[rank, i * rows : (i + 1) * rows, :] = velocity[c, x, first : first + rows, :]
            for slot, row in enumerate(beside):
                at = slots + slot * aligned(planes) + i
                out[rank, at : at + 1, :] = velocity[c, x, row : row + 1, :]

    by_parity(parity, count, fill)
    blank = aligned(planes) - planes
    for rank in range(count):
        for slot in range(2):
            at = slots + slot * aligned(planes) + planes
            out[rank, at : at + blank, :] = jnp.zeros((blank, lanes), jnp.float32)
        at = slots + 2 * aligned(planes)
        if at < depth:
            out[rank, at:, :] = jnp.zeros((depth - at, lanes), jnp.float32)


def outer_sides(rank, parity, count):
    outer = outer_ranks(count)
    even = parity[0] == 0
    bottom = rank[0] == jnp.where(even, outer[0], outer[1])
    top = rank[0] == jnp.where(even, outer[1], outer[0])
    return bottom, top


def edge_kernel(nz_parts, width, rows, walls, rank, position, recv, swapped, given, out, vel):
    count, _, lanes = recv.shape
    planes = 3 * width
    nx = (count // nz_parts) * width
    nz = nz_parts * lanes
    bottom, top = outer_sides(rank, [lax.rem(position[0], 2)], count)
    at_wall = jnp.logical_or(
        jnp.logical_and(bottom, position[0] == 0), jnp.logical_and(top, position[0] == walls - 1)
    )

    def rows_of(k, i):
        first = i * rows
        own = [recv[k, first + j : first + j + 1, :] for j in (0, 1, rows - 2, rows - 1)]
        far = jnp.where(at_wall, 0.0, swapped[k, i : i + 1, :])
        return (
            jnp.where(bottom, far, own[2]),
            jnp.where(bottom, own[0], own[3]),
            jnp.where(bottom, own[1], far),
        )

    def roll_x(f, shift):
        return pltpu.roll(f, shift % nx, 0)

    def roll_z(f, shift):
        return pltpu.roll(f, shift % nz, 1)

    def smooth_x(f):
        return (roll_x(f, 1) + roll_x(f, -1)) + 2.0 * f

    def smooth(f):
        f = smooth_x(f)
        return (roll_z(f, 1) + roll_z(f, -1)) + 2.0 * f

    def slopes(below, centre, above):
        return strain_parts(
            [roll_x(f, -1) - roll_x(f, 1) for f in centre],
            [a - b for a, b in zip(above, below)],
            [roll_z(f, -1) - roll_z(f, 1) for f in centre],
        )

    @pl.when(jnp.logical_or(bottom, top))
    def _():
        for k in range(count):
            x0, zb = (k // nz_parts) * width, k % nz_parts
            for i in range(planes):
                c, x = divmod(i, width)
                for j, row in enumerate(rows_of(k, i)):
                    vel[j, c, x0 + x : x0 + x + 1, zb * lanes : (zb + 1) * lanes] = row
        u = [[vel[j, c] for c in range(3)] for j in range(3)]
        v = [[smooth(f) for f in row] for row in u]
        strain = slopes(*u)
        size = strain_size(strain)
        mean_strain = slopes(*v)
        mean_size = 0.25 * strain_size(mean_strain)
        scaled = [0.0625 * f for f in v[1]]
        pairs = [v[1][i] * scaled[j] for i, j in ((0, 0), (1, 1), (2, 2), (0, 1), (0, 2), (1, 2))]
        leonard = [smooth(p) - q for p, q in zip(products(u[1]), pairs)]
        model = [smooth(size * s) - mean_size * f for s, f in zip(strain, mean_strain)]
        lm, mm = contracted(leonard, model)
        coefficient = coefficient_of(
            *(jnp.sum(f, axis=(0, 1), keepdims=True) for f in (lm, mm)), nx * nz
        )
        eddy = coefficient * size

        def put(at):
            for k in range(count):
                x0, zb = (k // nz_parts) * width, k % nz_parts
                for x in range(width):
                    out[k, x, at : at + 1, :] = eddy[x0 + x : x0 + x + 1, zb * lanes : (zb + 1) * lanes]

        pl.when(bottom)(lambda: put(0))
        pl.when(top)(lambda: put(rows - 1))


def contracted(leonard, model):
    lm = mm = None
    for i in range(6):
        square = model[i] * model[i] if i < 3 else (0.5 * model[i]) * model[i]
        product = leonard[i] * model[i]
        lm = product if lm is None else lm + product
        mm = square if mm is None else mm + square
    return lm, mm


def coefficient_of(plane_lm, plane_mm, cells):
    scale = 1.0 / (256.0 * cells)
    return jnp.maximum(plane_lm * scale / (plane_mm * scale + 1e-06), 0.0)


def germano_kernel(nz_parts, width, rows, rank, parity, recv, out, vel, filt, ends, mag, part):
    count, _, lanes = recv.shape
    planes = 3 * width
    _, top = outer_sides(rank, parity, count)
    nx = (count // nz_parts) * width
    nz = nz_parts * lanes
    blocks = range(nz_parts)
    lead = 8
    inner = slice(lead, lead + rows)
    lower = slice(lead - 1, lead - 1 + rows)
    upper = slice(lead + 1, lead + 1 + rows)
    for k in range(count):
        x0, zb = (k // nz_parts) * width, k % nz_parts
        for c in range(3):
            for x in range(width):
                i = c * width + x
                vel[c, x0 + x, zb, inner, :] = recv[k, i * rows : (i + 1) * rows, :]
                slots = planes * rows + i
                near = recv[k, slots : slots + 1, :]
                slots += aligned(planes)
                other = recv[k, slots : slots + 1, :]
                below = jnp.where(top, other, near)
                for side, (edge, at) in enumerate(((below, lead - 1), (other, lead + rows))):
                    vel[c, x0 + x, zb, at : at + 1, :] = edge
                    ends[c, x0 + x, zb, side : side + 1, :] = edge

    for x in range(nx):
        left, right = (x - 1) % nx, (x + 1) % nx
        centre = [[vel[c, x, zb, inner, :] for zb in blocks] for c in range(3)]
        grad_x = [[vel[c, right, zb, inner, :] - vel[c, left, zb, inner, :] for zb in blocks] for c in range(3)]
        grad_y = [[vel[c, x, zb, upper, :] - vel[c, x, zb, lower, :] for zb in blocks] for c in range(3)]
        grad_z = []
        for c in range(3):
            down, up = beside(centre[c])
            grad_z.append([u - d for u, d in zip(up, down)])
            for zb in blocks:
                part[c, x, zb] = (up[zb] + down[zb]) + 2.0 * centre[c][zb]
        strain = [
            strain_parts(*([g[c][zb] for c in range(3)] for g in (grad_x, grad_y, grad_z)))
            for zb in blocks
        ]
        size = [strain_size(s) for s in strain]
        for zb in blocks:
            mag[x, zb] = size[zb]
        pairs = [products([centre[c][zb] for c in range(3)]) for zb in blocks]
        for i in range(6):
            for base, fields in (
                (3, [pairs[zb][i] for zb in blocks]),
                (9, [size[zb] * strain[zb][i] for zb in blocks]),
            ):
                for zb, f in enumerate(smooth_z(fields)):
                    part[base + i, x, zb] = f

    def smooth_x(read, x):
        return (read((x - 1) % nx) + read((x + 1) % nx)) + 2.0 * read(x)

    for c in range(3):
        rims = []
        for x in range(nx):
            rims.append(smooth_z([ends[c, x, zb] for zb in blocks]))
        for x in range(nx):
            for zb in blocks:
                rim = smooth_x(lambda at: rims[at][zb], x)
                filt[c, x, zb, lead - 1 : lead, :] = rim[0:1, :]
                filt[c, x, zb, lead + rows : lead + rows + 1, :] = rim[1:2, :]
                filt[c, x, zb, inner, :] = smooth_x(lambda at: part[c, at, zb], x)

    sum_lm = sum_mm = None
    for x in range(nx):
        left, right = (x - 1) % nx, (x + 1) % nx
        mean = [[filt[c, x, zb, inner, :] for zb in blocks] for c in range(3)]
        grad_x = [[filt[c, right, zb, inner, :] - filt[c, left, zb, inner, :] for zb in blocks] for c in range(3)]
        grad_y = [[filt[c, x, zb, upper, :] - filt[c, x, zb, lower, :] for zb in blocks] for c in range(3)]
        grad_z = [slope_z(mean[c]) for c in range(3)]
        for zb in blocks:
            strain = strain_parts(*([g[c][zb] for c in range(3)] for g in (grad_x, grad_y, grad_z)))
            size = 0.25 * strain_size(strain)
            v = [mean[c][zb] for c in range(3)]
            scaled = [0.0625 * f for f in v]
            pairs = (
                v[0] * scaled[0],
                v[1] * scaled[1],
                v[2] * scaled[2],
                v[0] * scaled[1],
                v[0] * scaled[2],
                v[1] * scaled[2],
            )
            leonard = [smooth_x(lambda at: part[3 + i, at, zb], x) - pairs[i] for i in range(6)]
            model = [smooth_x(lambda at: part[9 + i, at, zb], x) - size * strain[i] for i in range(6)]
            lm, mm = contracted(leonard, model)
            sum_lm = lm if sum_lm is None else sum_lm + lm
            sum_mm = mm if sum_mm is None else sum_mm + mm

    coefficient = coefficient_of(
        *(jnp.sum(total, axis=1, keepdims=True) for total in (sum_lm, sum_mm)), nx * nz
    )
    for k in range(count):
        x0, zb = (k // nz_parts) * width, k % nz_parts
        for x in range(width):
            out[k, x] = coefficient * mag[x0 + x, zb]


def sweep_kernel(parity, back, velocity, tendency, eddy, reduced, factors, tree):
    count, width, rows, _ = back.shape
    length = count * rows // SEGMENTS

    def fill(rank, place):
        for x in range(width):
            eddy[x, place * rows : (place + 1) * rows, :] = back[rank, x]

    by_parity(parity, count, fill)

    def row(ref, index, j):
        return ref[(*index, pl.ds(j, SEGMENTS, stride=length), slice(None))]

    for x in range(width):
        visc = 1.0 + row(eddy, (x,), 0)
        visc_first = visc
        q = jnp.ones_like(visc)
        m = jnp.ones_like(visc)
        corner = jnp.zeros_like(visc)
        first = [jnp.zeros_like(visc)] * 3
        value = None
        for j in range(length):
            if j < length - 1:
                visc_next = 1.0 + row(eddy, (x,), j + 1)
                link = 750.0 * (visc + visc_next)
                inverse = 1.0 / (q + link)
            else:
                visc_next = None
                link = None
                inverse = 1.0 / q
            left = m * inverse
            corner = corner + m * left
            source = [
                2.0 * row(velocity, (c, x), j) + row(tendency, (c, x), j) for c in range(3)
            ]
            if j > 0:
                source = [s + link_before * v for s, v in zip(source, value)]
            value = [s * inverse for s in source]
            first = [f + m * v for f, v in zip(first, value)]
            for c in range(3):
                factors[x, j, c] = value[c]
            factors[x, j, 3] = left
            if j < length - 1:
                ratio = link * inverse
                factors[x, j, 4] = ratio
                q = 1.0 + link * (q * inverse)
                m = m * ratio
                link_before = link
                visc = visc_next
            else:
                factors[x, j, 4] = inverse
        last = value
        across = left
        end = inverse
        links = 750.0 * (visc + pltpu.roll(visc_first, SEGMENTS - 1, 0))
        level, step = 0, 1
        while step < SEGMENTS:
            def other(v):
                return pltpu.roll(v, SEGMENTS - step, 0)

            link = links if step == 1 else pltpu.roll(links, SEGMENTS - (step - 1), 0)
            across_b = other(across)
            stiff = link / (1.0 + link * (end + other(corner)))
            flux = [stiff * (g - other(f)) for g, f in zip(last, first)]
            from_left = stiff * across
            from_right = stiff * across_b
            for c in range(3):
                tree[x, level, c] = flux[c]
            tree[x, level, 3] = from_left
            tree[x, level, 4] = from_right
            first = [f - across * t for f, t in zip(first, flux)]
            last = [other(g) + across_b * t for g, t in zip(last, flux)]
            corner = corner - across * from_left
            end = other(end) - across_b * from_right
            across = from_left * across_b
            level, step = level + 1, step * 2
        rows_out = [*first, *last, corner, across, end, visc_first]
        for i, v in enumerate(rows_out):
            reduced[i * width + x : i * width + x + 1, :] = v[0:1, :]
        i = len(rows_out)
        reduced[i * width + x : i * width + x + 1, :] = visc[SEGMENTS - 1 :, :]


def partner(i, step, count):
    if count & (count - 1) == 0:
        return i ^ step
    return (i - step + count) % count


def finish_kernel(devices, position, factors, tree, velocity, *rest):
    reduced, (out, gathered, fluxes) = rest[:devices], rest[devices:]
    width, length = factors.shape[:2]
    here = position[0]
    for step in range(devices):
        gathered[partner(here, step, devices)] = reduced[step][...]

    def part(device, i):
        return gathered[device, i * width : (i + 1) * width, :]

    ratios, values = [], []
    for i in range(devices + 1):
        if i == 0:
            link = 750.0 * part(0, 9)
            total = part(0, 6)
            source = [-part(0, c) for c in range(3)]
        elif i == devices:
            link = 750.0 * part(i - 1, 10)
            total = part(i - 1, 8)
            source = [part(i - 1, 3 + c) for c in range(3)]
        else:
            link = 750.0 * (part(i - 1, 10) + part(i, 9))
            total = part(i - 1, 8) + part(i, 6)
            source = [part(i - 1, 3 + c) - part(i, c) for c in range(3)]
        pivot = 1.0 + link * total
        if i > 0:
            before = part(i - 1, 7)
            pivot = pivot - link * before * ratios[-1]
            source = [s + before * v for s, v in zip(source, values[-1])]
        scale = link / pivot
        values.append([scale * s for s in source])
        if i < devices:
            ratios.append(scale * part(i, 7))
    flux = values[devices]
    for i in range(devices, -1, -1):
        if i < devices:
            flux = [v + ratios[i] * f for v, f in zip(values[i], flux)]
        for c in range(3):
            fluxes[i, c * width : (c + 1) * width, :] = flux[c]

    sublane = lax.broadcasted_iota(jnp.int32, (SEGMENTS, LANES), 0)
    levels = tree.shape[1]
    for x in range(width):
        for c in range(3):
            r = c * width + x
            left = jnp.broadcast_to(fluxes[here, r : r + 1, :], (SEGMENTS, LANES))
            right = -jnp.broadcast_to(fluxes[here + 1, r : r + 1, :], (SEGMENTS, LANES))
            for level in range(levels - 1, -1, -1):
                step = 2**level
                through = tree[x, level, c] + tree[x, level, 3] * left - tree[x, level, 4] * right
                second = lax.rem(sublane, 2 * step) == step
                left = jnp.where(second, pltpu.roll(through, step, 0), left)
                right = jnp.where(second, pltpu.roll(right, step, 0), -through)
            value = right
            for j in range(length - 1, -1, -1):
                value = (factors[x, j, c] + factors[x, j, 3] * left) + factors[x, j, 4] * value
                rows = pl.ds(j, SEGMENTS, stride=length)
                out[c, x, rows, :] = value - velocity[c, x, rows, :]


def in_vmem(count):
    return [pl.BlockSpec(memory_space=pltpu.VMEM)] * count


def in_smem(count):
    return [pl.BlockSpec(memory_space=pltpu.SMEM)] * count


def params():
    return pltpu.CompilerParams(vmem_limit_bytes=VMEM_BYTES)


def body(velocity, tendency):
    _, width, cells, lanes = velocity.shape
    nz_parts = lax.axis_size("gz")
    count = lax.axis_size("gx") * nz_parts
    walls = lax.axis_size("gy")
    rows = cells // count
    nx = lax.axis_size("gx") * width
    padded = 16 + aligned(rows)
    f32 = jnp.float32

    planes = 3 * width
    depth = aligned(planes * rows + 2 * aligned(planes))
    position = lax.axis_index("gy").astype(jnp.int32).reshape(1)
    parity = lax.rem(position, 2)
    chunks = pl.pallas_call(
        functools.partial(pack_kernel, rows),
        out_shape=jax.ShapeDtypeStruct((count, depth, lanes), f32),
        in_specs=in_smem(1) + in_vmem(1),
        out_specs=pl.BlockSpec(memory_space=pltpu.VMEM),
        compiler_params=params(),
        name="pack",
    )(parity, velocity)
    recv = lax.all_to_all(chunks, ("gx", "gz"), split_axis=0, concat_axis=0, tiled=True)
    pairs = []
    for r in range(count):
        shift = 1 if r == outer_ranks(count)[0] else 0
        for wall in range(walls):
            beside = (wall + 1) % walls if (wall - shift) % 2 == 0 else (wall - 1) % walls
            pairs.append((wall * count + r, beside * count + r))
    slot = lax.slice_in_dim(recv, planes * rows, planes * rows + aligned(planes), axis=1)
    swapped = lax.ppermute(slot, ("gy", "gx", "gz"), pairs)
    rank = lax.axis_index(("gx", "gz")).astype(jnp.int32).reshape(1)
    chunk_shape = jax.ShapeDtypeStruct((count, width, rows, lanes), f32)
    cells_here = nx * nz_parts * rows * lanes
    provisional = pl.pallas_call(
        functools.partial(germano_kernel, nz_parts, width, rows),
        out_shape=chunk_shape,
        in_specs=in_smem(2) + in_vmem(1),
        out_specs=pl.BlockSpec(memory_space=pltpu.VMEM),
        scratch_shapes=[
            pltpu.VMEM((3, nx, nz_parts, padded, lanes), f32),
            pltpu.VMEM((3, nx, nz_parts, padded, lanes), f32),
            pltpu.VMEM((3, nx, nz_parts, 8, lanes), f32),
            pltpu.VMEM((nx, nz_parts, rows, lanes), f32),
            pltpu.VMEM((15, nx, nz_parts, rows, lanes), f32),
        ],
        compiler_params=params(),
        cost_estimate=pl.CostEstimate(
            flops=300 * cells_here, bytes_accessed=16 * cells_here, transcendentals=2 * cells_here
        ),
        name="germano",
    )(rank, parity, recv)
    eddy_chunks = pl.pallas_call(
        functools.partial(edge_kernel, nz_parts, width, rows, walls),
        out_shape=chunk_shape,
        in_specs=in_smem(2) + in_vmem(3),
        out_specs=pl.BlockSpec(memory_space=pltpu.VMEM),
        scratch_shapes=[pltpu.VMEM((3, 3, nx, nz_parts * lanes), f32)],
        input_output_aliases={4: 0},
        compiler_params=params(),
        name="edge",
    )(rank, position, recv, swapped, provisional)
    back = lax.all_to_all(eddy_chunks, ("gx", "gz"), split_axis=0, concat_axis=0, tiled=True)

    length = cells // SEGMENTS
    levels = SEGMENTS.bit_length() - 1
    packed = aligned(11 * width)
    eddy, reduced, factors, tree = pl.pallas_call(
        sweep_kernel,
        out_shape=(
            jax.ShapeDtypeStruct((width, cells, lanes), f32),
            jax.ShapeDtypeStruct((packed, lanes), f32),
            jax.ShapeDtypeStruct((width, length, 5, SEGMENTS, lanes), f32),
            jax.ShapeDtypeStruct((width, levels, 5, SEGMENTS, lanes), f32),
        ),
        in_specs=in_smem(1) + in_vmem(3),
        out_specs=tuple(in_vmem(4)),
        compiler_params=params(),
        name="sweep",
    )(parity, back, velocity, tendency)

    others = [
        lax.ppermute(reduced, "gy", [(partner(i, step, walls), i) for i in range(walls)])
        for step in range(1, walls)
    ]
    new_velocity = pl.pallas_call(
        functools.partial(finish_kernel, walls),
        out_shape=jax.ShapeDtypeStruct(velocity.shape, f32),
        in_specs=in_smem(1) + in_vmem(3 + walls),
        out_specs=pl.BlockSpec(memory_space=pltpu.VMEM),
        scratch_shapes=[
            pltpu.VMEM((walls, packed, lanes), f32),
            pltpu.VMEM((walls + 1, aligned(3 * width), lanes), f32),
        ],
        compiler_params=params(),
        name="finish",
    )(position, factors, tree, velocity, reduced, *others)
    return (new_velocity, eddy)


def solution(mesh):
    return jax.shard_map(
        body,
        mesh=mesh,
        in_specs=(P(None, "gx", "gy", "gz"), P(None, "gx", "gy", "gz")),
        out_specs=(P(None, "gx", "gy", "gz"), P("gx", "gy", "gz")),
        check_vma=False,
    )
```

```python
import functools

import jax
import jax.numpy as jnp
from jax import lax
from jax.experimental import pallas as pl
from jax.experimental.pallas import tpu as pltpu
from jax.sharding import PartitionSpec as P

LANES = 128
SEGMENTS = 8
VMEM_BYTES = 24 * 2**20


def strain_parts(grad_x, grad_y, grad_z):
    return (
        grad_x[0],
        grad_y[1],
        grad_z[2],
        grad_y[0] + grad_x[1],
        grad_z[0] + grad_x[2],
        grad_z[1] + grad_y[2],
    )


def strain_size(parts):
    diagonal = parts[0] * parts[0] + parts[1] * parts[1] + parts[2] * parts[2]
    mixed = parts[3] * parts[3] + parts[4] * parts[4] + parts[5] * parts[5]
    return jnp.sqrt(0.5 * diagonal + 0.25 * mixed)


def beside(blocks):
    count = len(blocks)
    lanes = blocks[0].shape[1]
    down = [pltpu.roll(f, 1, 1) for f in blocks]
    up = [pltpu.roll(f, lanes - 1, 1) for f in blocks]
    if count > 1:
        lane = lax.broadcasted_iota(jnp.int32, blocks[0].shape, 1)
        first, last = lane == 0, lane == lanes - 1
        down, up = (
            [jnp.where(first, down[i - 1], down[i]) for i in range(count)],
            [jnp.where(last, up[(i + 1) % count], up[i]) for i in range(count)],
        )
    return down, up


def slope_z(blocks):
    down, up = beside(blocks)
    return [u - d for u, d in zip(up, down)]


def smooth_z(blocks):
    down, up = beside(blocks)
    return [(u + d) + 2.0 * f for f, u, d in zip(blocks, up, down)]


def products(v):
    return (v[0] * v[0], v[1] * v[1], v[2] * v[2], v[0] * v[1], v[0] * v[2], v[1] * v[2])


def outer_ranks(count):
    return (count - 1, count - 3)


def places(parity, count):
    outer = outer_ranks(count)
    inner = iter(range(1, count - 1))
    return [
        (0 if outer[parity] == rank else count - 1) if rank in outer else next(inner)
        for rank in range(count)
    ]


def by_parity(parity, count, fill):
    outer = outer_ranks(count)
    for rank, place in enumerate(places(0, count)):
        if rank not in outer:
            fill(rank, place)
    for turn in range(2):

        @pl.when(parity[0] == turn)
        def _():
            for rank in outer:
                fill(rank, places(turn, count)[rank])


def aligned(n):
    return -(-n // 8) * 8


def pack_kernel(rows, parity, velocity, out):
    _, width, cells, _ = velocity.shape
    count, depth, lanes = out.shape
    planes = 3 * width
    slots = planes * rows

    def fill(rank, place):
        first = place * rows
        beside = [first - 1, first + rows]
        if place == 0:
            beside = [first, first + rows]
        if place == count - 1:
            beside = [first + rows - 1, first - 1]
        for i in range(planes):
            c, x = divmod(i, width)
            out[rank, i * rows : (i + 1) * rows, :] = velocity[c, x, first : first + rows, :]
            for slot, row in enumerate(beside):
                at = slots + slot * aligned(planes) + i
                out[rank, at : at + 1, :] = velocity[c, x, row : row + 1, :]

    by_parity(parity, count, fill)
    blank = aligned(planes) - planes
    for rank in range(count):
        for slot in range(2):
            at = slots + slot * aligned(planes) + planes
            out[rank, at : at + blank, :] = jnp.zeros((blank, lanes), jnp.float32)
        at = slots + 2 * aligned(planes)
        if at < depth:
            out[rank, at:, :] = jnp.zeros((depth - at, lanes), jnp.float32)


def outer_sides(rank, parity, count):
    outer = outer_ranks(count)
    even = parity[0] == 0
    bottom = rank[0] == jnp.where(even, outer[0], outer[1])
    top = rank[0] == jnp.where(even, outer[1], outer[0])
    return bottom, top


def edge_kernel(nz_parts, width, rows, walls, rank, position, recv, swapped, given, out, vel):
    count, _, lanes = recv.shape
    planes = 3 * width
    nx = (count // nz_parts) * width
    nz = nz_parts * lanes
    bottom, top = outer_sides(rank, [lax.rem(position[0], 2)], count)
    at_wall = jnp.logical_or(
        jnp.logical_and(bottom, position[0] == 0), jnp.logical_and(top, position[0] == walls - 1)
    )

    def rows_of(k, i):
        first = i * rows
        own = [recv[k, first + j : first + j + 1, :] for j in (0, 1, rows - 2, rows - 1)]
        far = jnp.where(at_wall, 0.0, swapped[k, i : i + 1, :])
        return (
            jnp.where(bottom, far, own[2]),
            jnp.where(bottom, own[0], own[3]),
            jnp.where(bottom, own[1], far),
        )

    def roll_x(f, shift):
        return pltpu.roll(f, shift % nx, 0)

    def roll_z(f, shift):
        return pltpu.roll(f, shift % nz, 1)

    def smooth_x(f):
        return (roll_x(f, 1) + roll_x(f, -1)) + 2.0 * f

    def smooth(f):
        f = smooth_x(f)
        return (roll_z(f, 1) + roll_z(f, -1)) + 2.0 * f

    def slopes(below, centre, above):
        return strain_parts(
            [roll_x(f, -1) - roll_x(f, 1) for f in centre],
            [a - b for a, b in zip(above, below)],
            [roll_z(f, -1) - roll_z(f, 1) for f in centre],
        )

    @pl.when(jnp.logical_or(bottom, top))
    def _():
        for k in range(count):
            x0, zb = (k // nz_parts) * width, k % nz_parts
            for i in range(planes):
                c, x = divmod(i, width)
                for j, row in enumerate(rows_of(k, i)):
                    vel[j, c, x0 + x : x0 + x + 1, zb * lanes : (zb + 1) * lanes] = row
        u = [[vel[j, c] for c in range(3)] for j in range(3)]
        v = [[smooth(f) for f in row] for row in u]
        strain = slopes(*u)
        size = strain_size(strain)
        mean_strain = slopes(*v)
        mean_size = 0.25 * strain_size(mean_strain)
        scaled = [0.0625 * f for f in v[1]]
        pairs = [v[1][i] * scaled[j] for i, j in ((0, 0), (1, 1), (2, 2), (0, 1), (0, 2), (1, 2))]
        leonard = [smooth(p) - q for p, q in zip(products(u[1]), pairs)]
        model = [smooth(size * s) - mean_size * f for s, f in zip(strain, mean_strain)]
        lm, mm = contracted(leonard, model)
        coefficient = coefficient_of(
            *(jnp.sum(f, axis=(0, 1), keepdims=True) for f in (lm, mm)), nx * nz
        )
        eddy = coefficient * size

        def put(at):
            for k in range(count):
                x0, zb = (k // nz_parts) * width, k % nz_parts
                for x in range(width):
                    out[k, x, at : at + 1, :] = eddy[x0 + x : x0 + x + 1, zb * lanes : (zb + 1) * lanes]

        pl.when(bottom)(lambda: put(0))
        pl.when(top)(lambda: put(rows - 1))


def contracted(leonard, model):
    lm = mm = None
    for i in range(6):
        square = model[i] * model[i] if i < 3 else (0.5 * model[i]) * model[i]
        product = leonard[i] * model[i]
        lm = product if lm is None else lm + product
        mm = square if mm is None else mm + square
    return lm, mm


def coefficient_of(plane_lm, plane_mm, cells):
    scale = 1.0 / (256.0 * cells)
    return jnp.maximum(plane_lm * scale / (plane_mm * scale + 1e-06), 0.0)


def germano_kernel(nz_parts, width, rows, rank, parity, recv, out, vel, filt, ends, mag, part):
    count, _, lanes = recv.shape
    planes = 3 * width
    _, top = outer_sides(rank, parity, count)
    nx = (count // nz_parts) * width
    nz = nz_parts * lanes
    blocks = range(nz_parts)
    lead = 8
    inner = slice(lead, lead + rows)
    lower = slice(lead - 1, lead - 1 + rows)
    upper = slice(lead + 1, lead + 1 + rows)
    for k in range(count):
        x0, zb = (k // nz_parts) * width, k % nz_parts
        for c in range(3):
            for x in range(width):
                i = c * width + x
                vel[c, x0 + x, zb, inner, :] = recv[k, i * rows : (i + 1) * rows, :]
                slots = planes * rows + i
                near = recv[k, slots : slots + 1, :]
                slots += aligned(planes)
                other = recv[k, slots : slots + 1, :]
                below = jnp.where(top, other, near)
                for side, (edge, at) in enumerate(((below, lead - 1), (other, lead + rows))):
                    vel[c, x0 + x, zb, at : at + 1, :] = edge
                    ends[c, x0 + x, zb, side : side + 1, :] = edge

    for x in range(nx):
        left, right = (x - 1) % nx, (x + 1) % nx
        centre = [[vel[c, x, zb, inner, :] for zb in blocks] for c in range(3)]
        grad_x = [[vel[c, right, zb, inner, :] - vel[c, left, zb, inner, :] for zb in blocks] for c in range(3)]
        grad_y = [[vel[c, x, zb, upper, :] - vel[c, x, zb, lower, :] for zb in blocks] for c in range(3)]
        grad_z = []
        for c in range(3):
            down, up = beside(centre[c])
            grad_z.append([u - d for u, d in zip(up, down)])
            for zb in blocks:
                part[c, x, zb] = (up[zb] + down[zb]) + 2.0 * centre[c][zb]
        strain = [
            strain_parts(*([g[c][zb] for c in range(3)] for g in (grad_x, grad_y, grad_z)))
            for zb in blocks
        ]
        size = [strain_size(s) for s in strain]
        for zb in blocks:
            mag[x, zb] = size[zb]
        pairs = [products([centre[c][zb] for c in range(3)]) for zb in blocks]
        for i in range(6):
            for base, fields in (
                (3, [pairs[zb][i] for zb in blocks]),
                (9, [size[zb] * strain[zb][i] for zb in blocks]),
            ):
                for zb, f in enumerate(smooth_z(fields)):
                    part[base + i, x, zb] = f

    def smooth_x(read, x):
        return (read((x - 1) % nx) + read((x + 1) % nx)) + 2.0 * read(x)

    for c in range(3):
        rims = []
        for x in range(nx):
            rims.append(smooth_z([ends[c, x, zb] for zb in blocks]))
        for x in range(nx):
            for zb in blocks:
                rim = smooth_x(lambda at: rims[at][zb], x)
                filt[c, x, zb, lead - 1 : lead, :] = rim[0:1, :]
                filt[c, x, zb, lead + rows : lead + rows + 1, :] = rim[1:2, :]
                filt[c, x, zb, inner, :] = smooth_x(lambda at: part[c, at, zb], x)

    sum_lm = sum_mm = None
    for x in range(nx):
        left, right = (x - 1) % nx, (x + 1) % nx
        mean = [[filt[c, x, zb, inner, :] for zb in blocks] for c in range(3)]
        grad_x = [[filt[c, right, zb, inner, :] - filt[c, left, zb, inner, :] for zb in blocks] for c in range(3)]
        grad_y = [[filt[c, x, zb, upper, :] - filt[c, x, zb, lower, :] for zb in blocks] for c in range(3)]
        grad_z = [slope_z(mean[c]) for c in range(3)]
        for zb in blocks:
            strain = strain_parts(*([g[c][zb] for c in range(3)] for g in (grad_x, grad_y, grad_z)))
            size = 0.25 * strain_size(strain)
            v = [mean[c][zb] for c in range(3)]
            scaled = [0.0625 * f for f in v]
            pairs = (
                v[0] * scaled[0],
                v[1] * scaled[1],
                v[2] * scaled[2],
                v[0] * scaled[1],
                v[0] * scaled[2],
                v[1] * scaled[2],
            )
            leonard = [smooth_x(lambda at: part[3 + i, at, zb], x) - pairs[i] for i in range(6)]
            model = [smooth_x(lambda at: part[9 + i, at, zb], x) - size * strain[i] for i in range(6)]
            lm, mm = contracted(leonard, model)
            sum_lm = lm if sum_lm is None else sum_lm + lm
            sum_mm = mm if sum_mm is None else sum_mm + mm

    coefficient = coefficient_of(
        *(jnp.sum(total, axis=1, keepdims=True) for total in (sum_lm, sum_mm)), nx * nz
    )
    for k in range(count):
        x0, zb = (k // nz_parts) * width, k % nz_parts
        for x in range(width):
            out[k, x] = coefficient * mag[x0 + x, zb]


def sweep_kernel(parity, back, velocity, tendency, eddy, reduced, factors, tree):
    count, width, rows, _ = back.shape
    length = count * rows // SEGMENTS

    def fill(rank, place):
        for x in range(width):
            eddy[x, place * rows : (place + 1) * rows, :] = back[rank, x]

    by_parity(parity, count, fill)

    def row(ref, index, j):
        return ref[(*index, pl.ds(j, SEGMENTS, stride=length), slice(None))]

    for x in range(width):
        visc = 1.0 + row(eddy, (x,), 0)
        visc_first = visc
        q = jnp.ones_like(visc)
        m = jnp.ones_like(visc)
        corner = jnp.zeros_like(visc)
        first = [jnp.zeros_like(visc)] * 3
        value = None
        for j in range(length):
            if j < length - 1:
                visc_next = 1.0 + row(eddy, (x,), j + 1)
                link = 750.0 * (visc + visc_next)
                inverse = 1.0 / (q + link)
            else:
                visc_next = None
                link = None
                inverse = 1.0 / q
            left = m * inverse
            corner = corner + m * left
            source = [
                2.0 * row(velocity, (c, x), j) + row(tendency, (c, x), j) for c in range(3)
            ]
            if j > 0:
                source = [s + link_before * v for s, v in zip(source, value)]
            value = [s * inverse for s in source]
            first = [f + m * v for f, v in zip(first, value)]
            for c in range(3):
                factors[x, j, c] = value[c]
            factors[x, j, 3] = left
            if j < length - 1:
                ratio = link * inverse
                factors[x, j, 4] = ratio
                q = 1.0 + link * (q * inverse)
                m = m * ratio
                link_before = link
                visc = visc_next
            else:
                factors[x, j, 4] = inverse
        last = value
        across = left
        end = inverse
        links = 750.0 * (visc + pltpu.roll(visc_first, SEGMENTS - 1, 0))
        level, step = 0, 1
        while step < SEGMENTS:
            def other(v):
                return pltpu.roll(v, SEGMENTS - step, 0)

            link = links if step == 1 else pltpu.roll(links, SEGMENTS - (step - 1), 0)
            across_b = other(across)
            stiff = link / (1.0 + link * (end + other(corner)))
            flux = [stiff * (g - other(f)) for g, f in zip(last, first)]
            from_left = stiff * across
            from_right = stiff * across_b
            for c in range(3):
                tree[x, level, c] = flux[c]
            tree[x, level, 3] = from_left
            tree[x, level, 4] = from_right
            first = [f - across * t for f, t in zip(first, flux)]
            last = [other(g) + across_b * t for g, t in zip(last, flux)]
            corner = corner - across * from_left
            end = other(end) - across_b * from_right
            across = from_left * across_b
            level, step = level + 1, step * 2
        rows_out = [*first, *last, corner, across, end, visc_first]
        for i, v in enumerate(rows_out):
            reduced[i * width + x : i * width + x + 1, :] = v[0:1, :]
        i = len(rows_out)
        reduced[i * width + x : i * width + x + 1, :] = visc[SEGMENTS - 1 :, :]


def partner(i, step, count):
    if count & (count - 1) == 0:
        return i ^ step
    return (i - step + count) % count


def finish_kernel(devices, position, factors, tree, velocity, *rest):
    reduced, (out, gathered, fluxes) = rest[:devices], rest[devices:]
    width, length = factors.shape[:2]
    here = position[0]
    for step in range(devices):
        gathered[partner(here, step, devices)] = reduced[step][...]

    def part(device, i):
        return gathered[device, i * width : (i + 1) * width, :]

    ratios, values = [], []
    for i in range(devices + 1):
        if i == 0:
            link = 750.0 * part(0, 9)
            total = part(0, 6)
            source = [-part(0, c) for c in range(3)]
        elif i == devices:
            link = 750.0 * part(i - 1, 10)
            total = part(i - 1, 8)
            source = [part(i - 1, 3 + c) for c in range(3)]
        else:
            link = 750.0 * (part(i - 1, 10) + part(i, 9))
            total = part(i - 1, 8) + part(i, 6)
            source = [part(i - 1, 3 + c) - part(i, c) for c in range(3)]
        pivot = 1.0 + link * total
        if i > 0:
            before = part(i - 1, 7)
            pivot = pivot - link * before * ratios[-1]
            source = [s + before * v for s, v in zip(source, values[-1])]
        scale = link / pivot
        values.append([scale * s for s in source])
        if i < devices:
            ratios.append(scale * part(i, 7))
    flux = values[devices]
    for i in range(devices, -1, -1):
        if i < devices:
            flux = [v + ratios[i] * f for v, f in zip(values[i], flux)]
        for c in range(3):
            fluxes[i, c * width : (c + 1) * width, :] = flux[c]

    sublane = lax.broadcasted_iota(jnp.int32, (SEGMENTS, LANES), 0)
    levels = tree.shape[1]
    for x in range(width):
        for c in range(3):
            r = c * width + x
            left = jnp.broadcast_to(fluxes[here, r : r + 1, :], (SEGMENTS, LANES))
            right = -jnp.broadcast_to(fluxes[here + 1, r : r + 1, :], (SEGMENTS, LANES))
            for level in range(levels - 1, -1, -1):
                step = 2**level
                through = tree[x, level, c] + tree[x, level, 3] * left - tree[x, level, 4] * right
                second = lax.rem(sublane, 2 * step) == step
                left = jnp.where(second, pltpu.roll(through, step, 0), left)
                right = jnp.where(second, pltpu.roll(right, step, 0), -through)
            value = right
            for j in range(length - 1, -1, -1):
                value = (factors[x, j, c] + factors[x, j, 3] * left) + factors[x, j, 4] * value
                rows = pl.ds(j, SEGMENTS, stride=length)
                out[c, x, rows, :] = value - velocity[c, x, rows, :]


def in_vmem(count):
    return [pl.BlockSpec(memory_space=pltpu.VMEM)] * count


def in_smem(count):
    return [pl.BlockSpec(memory_space=pltpu.SMEM)] * count


def params():
    return pltpu.CompilerParams(vmem_limit_bytes=VMEM_BYTES)


def body(velocity, tendency):
    _, width, cells, lanes = velocity.shape
    nz_parts = lax.axis_size("gz")
    count = lax.axis_size("gx") * nz_parts
    walls = lax.axis_size("gy")
    rows = cells // count
    nx = lax.axis_size("gx") * width
    padded = 16 + aligned(rows)
    f32 = jnp.float32

    planes = 3 * width
    depth = aligned(planes * rows + 2 * aligned(planes))
    position = lax.axis_index("gy").astype(jnp.int32).reshape(1)
    parity = lax.rem(position, 2)
    chunks = pl.pallas_call(
        functools.partial(pack_kernel, rows),
        out_shape=jax.ShapeDtypeStruct((count, depth, lanes), f32),
        in_specs=in_smem(1) + in_vmem(1),
        out_specs=pl.BlockSpec(memory_space=pltpu.VMEM),
        compiler_params=params(),
        name="pack",
    )(parity, velocity)
    recv = lax.all_to_all(chunks, ("gx", "gz"), split_axis=0, concat_axis=0, tiled=True)
    pairs = []
    for r in range(count):
        for wall in range(walls):
            beside = wall
            if r in outer_ranks(count):
                up = (wall - outer_ranks(count)[::-1].index(r)) % 2 == 0
                beside = wall + 1 if up else wall - 1
            beside = beside if 0 <= beside < walls else wall
            pairs.append((wall * count + r, beside * count + r))
    slot = lax.slice_in_dim(recv, planes * rows, planes * rows + aligned(planes), axis=1)
    swapped = lax.ppermute(slot, ("gy", "gx", "gz"), pairs)
    rank = lax.axis_index(("gx", "gz")).astype(jnp.int32).reshape(1)
    chunk_shape = jax.ShapeDtypeStruct((count, width, rows, lanes), f32)
    cells_here = nx * nz_parts * rows * lanes
    provisional = pl.pallas_call(
        functools.partial(germano_kernel, nz_parts, width, rows),
        out_shape=chunk_shape,
        in_specs=in_smem(2) + in_vmem(1),
        out_specs=pl.BlockSpec(memory_space=pltpu.VMEM),
        scratch_shapes=[
            pltpu.VMEM((3, nx, nz_parts, padded, lanes), f32),
            pltpu.VMEM((3, nx, nz_parts, padded, lanes), f32),
            pltpu.VMEM((3, nx, nz_parts, 8, lanes), f32),
            pltpu.VMEM((nx, nz_parts, rows, lanes), f32),
            pltpu.VMEM((15, nx, nz_parts, rows, lanes), f32),
        ],
        compiler_params=params(),
        cost_estimate=pl.CostEstimate(
            flops=300 * cells_here, bytes_accessed=16 * cells_here, transcendentals=2 * cells_here
        ),
        name="germano",
    )(rank, parity, recv)
    eddy_chunks = pl.pallas_call(
        functools.partial(edge_kernel, nz_parts, width, rows, walls),
        out_shape=chunk_shape,
        in_specs=in_smem(2) + in_vmem(3),
        out_specs=pl.BlockSpec(memory_space=pltpu.VMEM),
        scratch_shapes=[pltpu.VMEM((3, 3, nx, nz_parts * lanes), f32)],
        input_output_aliases={4: 0},
        compiler_params=params(),
        name="edge",
    )(rank, position, recv, swapped, provisional)
    back = lax.all_to_all(eddy_chunks, ("gx", "gz"), split_axis=0, concat_axis=0, tiled=True)

    length = cells // SEGMENTS
    levels = SEGMENTS.bit_length() - 1
    packed = aligned(11 * width)
    eddy, reduced, factors, tree = pl.pallas_call(
        sweep_kernel,
        out_shape=(
            jax.ShapeDtypeStruct((width, cells, lanes), f32),
            jax.ShapeDtypeStruct((packed, lanes), f32),
            jax.ShapeDtypeStruct((width, length, 5, SEGMENTS, lanes), f32),
            jax.ShapeDtypeStruct((width, levels, 5, SEGMENTS, lanes), f32),
        ),
        in_specs=in_smem(1) + in_vmem(3),
        out_specs=tuple(in_vmem(4)),
        compiler_params=params(),
        name="sweep",
    )(parity, back, velocity, tendency)

    others = [
        lax.ppermute(reduced, "gy", [(partner(i, step, walls), i) for i in range(walls)])
        for step in range(1, walls)
    ]
    new_velocity = pl.pallas_call(
        functools.partial(finish_kernel, walls),
        out_shape=jax.ShapeDtypeStruct(velocity.shape, f32),
        in_specs=in_smem(1) + in_vmem(3 + walls),
        out_specs=pl.BlockSpec(memory_space=pltpu.VMEM),
        scratch_shapes=[
            pltpu.VMEM((walls, packed, lanes), f32),
            pltpu.VMEM((walls + 1, aligned(3 * width), lanes), f32),
        ],
        compiler_params=params(),
        name="finish",
    )(position, factors, tree, velocity, reduced, *others)
    return (new_velocity, eddy)


def solution(mesh):
    return jax.shard_map(
        body,
        mesh=mesh,
        in_specs=(P(None, "gx", "gy", "gz"), P(None, "gx", "gy", "gz")),
        out_specs=(P(None, "gx", "gy", "gz"), P("gx", "gy", "gz")),
        check_vma=False,
    )
```

```python
import functools

import jax
import jax.numpy as jnp
from jax import lax
from jax.experimental import pallas as pl
from jax.experimental.pallas import tpu as pltpu
from jax.sharding import PartitionSpec as P

LANES = 128
SEGMENTS = 8
VMEM_BYTES = 24 * 2**20


def strain_parts(grad_x, grad_y, grad_z):
    return (
        grad_x[0],
        grad_y[1],
        grad_z[2],
        grad_y[0] + grad_x[1],
        grad_z[0] + grad_x[2],
        grad_z[1] + grad_y[2],
    )


def strain_size(parts):
    diagonal = parts[0] * parts[0] + parts[1] * parts[1] + parts[2] * parts[2]
    mixed = parts[3] * parts[3] + parts[4] * parts[4] + parts[5] * parts[5]
    return jnp.sqrt(0.5 * diagonal + 0.25 * mixed)


def beside(blocks):
    count = len(blocks)
    lanes = blocks[0].shape[1]
    down = [pltpu.roll(f, 1, 1) for f in blocks]
    up = [pltpu.roll(f, lanes - 1, 1) for f in blocks]
    if count > 1:
        lane = lax.broadcasted_iota(jnp.int32, blocks[0].shape, 1)
        first, last = lane == 0, lane == lanes - 1
        down, up = (
            [jnp.where(first, down[i - 1], down[i]) for i in range(count)],
            [jnp.where(last, up[(i + 1) % count], up[i]) for i in range(count)],
        )
    return down, up


def slope_z(blocks):
    down, up = beside(blocks)
    return [u - d for u, d in zip(up, down)]


def smooth_z(blocks):
    down, up = beside(blocks)
    return [(u + d) + 2.0 * f for f, u, d in zip(blocks, up, down)]


def products(v):
    return (v[0] * v[0], v[1] * v[1], v[2] * v[2], v[0] * v[1], v[0] * v[2], v[1] * v[2])


def outer_ranks(count):
    return (count - 1, count - 3)


def places(parity, count):
    outer = outer_ranks(count)
    inner = iter(range(1, count - 1))
    return [
        (0 if outer[parity] == rank else count - 1) if rank in outer else next(inner)
        for rank in range(count)
    ]


def swap_pairs(walls, count):
    odd, even = outer_ranks(count)
    spare = count - 5
    partners = {}

    def join(a, b):
        partners[a], partners[b] = b, a

    def join_walls(rank, first):
        for wall in range(first, walls - 1, 2):
            join((wall, rank), (wall + 1, rank))

    join_walls(even, 0)
    join_walls(odd, 1)
    join_walls(spare, 1)
    join((0, odd), (0, spare))
    if walls % 2 == 0:
        join((walls - 1, odd), (walls - 1, spare))
    others = [r for r in range(count) if r not in (odd, even, spare)]
    for core in range(2):
        ranks = [r for r in others if r % 2 == core]
        half = len(ranks) // 2
        for wall in range(walls):
            for a, b in zip(ranks[:half], ranks[half : 2 * half]):
                join((wall, a), (wall, b))
        for rank in ranks[2 * half :]:
            join_walls(rank, 0)
    return [
        (wall * count + rank, to[0] * count + to[1])
        for wall in range(walls)
        for rank in range(count)
        for to in [partners.get((wall, rank), (wall, rank))]
    ]


def by_parity(parity, count, fill):
    outer = outer_ranks(count)
    for rank, place in enumerate(places(0, count)):
        if rank not in outer:
            fill(rank, place)
    for turn in range(2):

        @pl.when(parity[0] == turn)
        def _():
            for rank in outer:
                fill(rank, places(turn, count)[rank])


def aligned(n):
    return -(-n // 8) * 8


def pack_kernel(rows, parity, velocity, out):
    _, width, cells, _ = velocity.shape
    count, depth, lanes = out.shape
    planes = 3 * width
    slots = planes * rows

    def fill(rank, place):
        first = place * rows
        beside = [first - 1, first + rows]
        if place == 0:
            beside = [first, first + rows]
        if place == count - 1:
            beside = [first + rows - 1, first - 1]
        for i in range(planes):
            c, x = divmod(i, width)
            out[rank, i * rows : (i + 1) * rows, :] = velocity[c, x, first : first + rows, :]
            for slot, row in enumerate(beside):
                at = slots + slot * aligned(planes) + i
                out[rank, at : at + 1, :] = velocity[c, x, row : row + 1, :]

    by_parity(parity, count, fill)
    blank = aligned(planes) - planes
    for rank in range(count):
        for slot in range(2):
            at = slots + slot * aligned(planes) + planes
            out[rank, at : at + blank, :] = jnp.zeros((blank, lanes), jnp.float32)
        at = slots + 2 * aligned(planes)
        if at < depth:
            out[rank, at:, :] = jnp.zeros((depth - at, lanes), jnp.float32)


def outer_sides(rank, parity, count):
    outer = outer_ranks(count)
    even = parity[0] == 0
    bottom = rank[0] == jnp.where(even, outer[0], outer[1])
    top = rank[0] == jnp.where(even, outer[1], outer[0])
    return bottom, top


def edge_kernel(nz_parts, width, rows, walls, rank, position, recv, swapped, given, out, vel):
    count, _, lanes = recv.shape
    planes = 3 * width
    nx = (count // nz_parts) * width
    nz = nz_parts * lanes
    bottom, top = outer_sides(rank, [lax.rem(position[0], 2)], count)
    at_wall = jnp.logical_or(
        jnp.logical_and(bottom, position[0] == 0), jnp.logical_and(top, position[0] == walls - 1)
    )

    def rows_of(k, i):
        first = i * rows
        own = [recv[k, first + j : first + j + 1, :] for j in (0, 1, rows - 2, rows - 1)]
        far = jnp.where(at_wall, 0.0, swapped[k, i : i + 1, :])
        return (
            jnp.where(bottom, far, own[2]),
            jnp.where(bottom, own[0], own[3]),
            jnp.where(bottom, own[1], far),
        )

    def roll_x(f, shift):
        return pltpu.roll(f, shift % nx, 0)

    def roll_z(f, shift):
        return pltpu.roll(f, shift % nz, 1)

    def smooth_x(f):
        return (roll_x(f, 1) + roll_x(f, -1)) + 2.0 * f

    def smooth(f):
        f = smooth_x(f)
        return (roll_z(f, 1) + roll_z(f, -1)) + 2.0 * f

    def slopes(below, centre, above):
        return strain_parts(
            [roll_x(f, -1) - roll_x(f, 1) for f in centre],
            [a - b for a, b in zip(above, below)],
            [roll_z(f, -1) - roll_z(f, 1) for f in centre],
        )

    @pl.when(jnp.logical_or(bottom, top))
    def _():
        for k in range(count):
            x0, zb = (k // nz_parts) * width, k % nz_parts
            for i in range(planes):
                c, x = divmod(i, width)
                for j, row in enumerate(rows_of(k, i)):
                    vel[j, c, x0 + x : x0 + x + 1, zb * lanes : (zb + 1) * lanes] = row
        u = [[vel[j, c] for c in range(3)] for j in range(3)]
        v = [[smooth(f) for f in row] for row in u]
        strain = slopes(*u)
        size = strain_size(strain)
        mean_strain = slopes(*v)
        mean_size = 0.25 * strain_size(mean_strain)
        scaled = [0.0625 * f for f in v[1]]
        pairs = [v[1][i] * scaled[j] for i, j in ((0, 0), (1, 1), (2, 2), (0, 1), (0, 2), (1, 2))]
        leonard = [smooth(p) - q for p, q in zip(products(u[1]), pairs)]
        model = [smooth(size * s) - mean_size * f for s, f in zip(strain, mean_strain)]
        lm, mm = contracted(leonard, model)
        coefficient = coefficient_of(
            *(jnp.sum(f, axis=(0, 1), keepdims=True) for f in (lm, mm)), nx * nz
        )
        eddy = coefficient * size

        def put(at):
            for k in range(count):
                x0, zb = (k // nz_parts) * width, k % nz_parts
                for x in range(width):
                    out[k, x, at : at + 1, :] = eddy[x0 + x : x0 + x + 1, zb * lanes : (zb + 1) * lanes]

        pl.when(bottom)(lambda: put(0))
        pl.when(top)(lambda: put(rows - 1))


def contracted(leonard, model):
    lm = mm = None
    for i in range(6):
        square = model[i] * model[i] if i < 3 else (0.5 * model[i]) * model[i]
        product = leonard[i] * model[i]
        lm = product if lm is None else lm + product
        mm = square if mm is None else mm + square
    return lm, mm


def coefficient_of(plane_lm, plane_mm, cells):
    scale = 1.0 / (256.0 * cells)
    return jnp.maximum(plane_lm * scale / (plane_mm * scale + 1e-06), 0.0)


def germano_kernel(nz_parts, width, rows, rank, parity, recv, out, vel, filt, ends, mag, part):
    count, _, lanes = recv.shape
    planes = 3 * width
    _, top = outer_sides(rank, parity, count)
    nx = (count // nz_parts) * width
    nz = nz_parts * lanes
    blocks = range(nz_parts)
    lead = 8
    inner = slice(lead, lead + rows)
    lower = slice(lead - 1, lead - 1 + rows)
    upper = slice(lead + 1, lead + 1 + rows)
    for k in range(count):
        x0, zb = (k // nz_parts) * width, k % nz_parts
        for c in range(3):
            for x in range(width):
                i = c * width + x
                vel[c, x0 + x, zb, inner, :] = recv[k, i * rows : (i + 1) * rows, :]
                slots = planes * rows + i
                near = recv[k, slots : slots + 1, :]
                slots += aligned(planes)
                other = recv[k, slots : slots + 1, :]
                below = jnp.where(top, other, near)
                for side, (edge, at) in enumerate(((below, lead - 1), (other, lead + rows))):
                    vel[c, x0 + x, zb, at : at + 1, :] = edge
                    ends[c, x0 + x, zb, side : side + 1, :] = edge

    for x in range(nx):
        left, right = (x - 1) % nx, (x + 1) % nx
        centre = [[vel[c, x, zb, inner, :] for zb in blocks] for c in range(3)]
        grad_x = [[vel[c, right, zb, inner, :] - vel[c, left, zb, inner, :] for zb in blocks] for c in range(3)]
        grad_y = [[vel[c, x, zb, upper, :] - vel[c, x, zb, lower, :] for zb in blocks] for c in range(3)]
        grad_z = []
        for c in range(3):
            down, up = beside(centre[c])
            grad_z.append([u - d for u, d in zip(up, down)])
            for zb in blocks:
                part[c, x, zb] = (up[zb] + down[zb]) + 2.0 * centre[c][zb]
        strain = [
            strain_parts(*([g[c][zb] for c in range(3)] for g in (grad_x, grad_y, grad_z)))
            for zb in blocks
        ]
        size = [strain_size(s) for s in strain]
        for zb in blocks:
            mag[x, zb] = size[zb]
        pairs = [products([centre[c][zb] for c in range(3)]) for zb in blocks]
        for i in range(6):
            for base, fields in (
                (3, [pairs[zb][i] for zb in blocks]),
                (9, [size[zb] * strain[zb][i] for zb in blocks]),
            ):
                for zb, f in enumerate(smooth_z(fields)):
                    part[base + i, x, zb] = f

    def smooth_x(read, x):
        return (read((x - 1) % nx) + read((x + 1) % nx)) + 2.0 * read(x)

    for c in range(3):
        rims = []
        for x in range(nx):
            rims.append(smooth_z([ends[c, x, zb] for zb in blocks]))
        for x in range(nx):
            for zb in blocks:
                rim = smooth_x(lambda at: rims[at][zb], x)
                filt[c, x, zb, lead - 1 : lead, :] = rim[0:1, :]
                filt[c, x, zb, lead + rows : lead + rows + 1, :] = rim[1:2, :]
                filt[c, x, zb, inner, :] = smooth_x(lambda at: part[c, at, zb], x)

    sum_lm = sum_mm = None
    for x in range(nx):
        left, right = (x - 1) % nx, (x + 1) % nx
        mean = [[filt[c, x, zb, inner, :] for zb in blocks] for c in range(3)]
        grad_x = [[filt[c, right, zb, inner, :] - filt[c, left, zb, inner, :] for zb in blocks] for c in range(3)]
        grad_y = [[filt[c, x, zb, upper, :] - filt[c, x, zb, lower, :] for zb in blocks] for c in range(3)]
        grad_z = [slope_z(mean[c]) for c in range(3)]
        for zb in blocks:
            strain = strain_parts(*([g[c][zb] for c in range(3)] for g in (grad_x, grad_y, grad_z)))
            size = 0.25 * strain_size(strain)
            v = [mean[c][zb] for c in range(3)]
            scaled = [0.0625 * f for f in v]
            pairs = (
                v[0] * scaled[0],
                v[1] * scaled[1],
                v[2] * scaled[2],
                v[0] * scaled[1],
                v[0] * scaled[2],
                v[1] * scaled[2],
            )
            leonard = [smooth_x(lambda at: part[3 + i, at, zb], x) - pairs[i] for i in range(6)]
            model = [smooth_x(lambda at: part[9 + i, at, zb], x) - size * strain[i] for i in range(6)]
            lm, mm = contracted(leonard, model)
            sum_lm = lm if sum_lm is None else sum_lm + lm
            sum_mm = mm if sum_mm is None else sum_mm + mm

    coefficient = coefficient_of(
        *(jnp.sum(total, axis=1, keepdims=True) for total in (sum_lm, sum_mm)), nx * nz
    )
    for k in range(count):
        x0, zb = (k // nz_parts) * width, k % nz_parts
        for x in range(width):
            out[k, x] = coefficient * mag[x0 + x, zb]


def sweep_kernel(parity, back, velocity, tendency, eddy, reduced, factors, tree):
    count, width, rows, _ = back.shape
    length = count * rows // SEGMENTS

    def fill(rank, place):
        for x in range(width):
            eddy[x, place * rows : (place + 1) * rows, :] = back[rank, x]

    by_parity(parity, count, fill)

    def row(ref, index, j):
        return ref[(*index, pl.ds(j, SEGMENTS, stride=length), slice(None))]

    for x in range(width):
        visc = 1.0 + row(eddy, (x,), 0)
        visc_first = visc
        q = jnp.ones_like(visc)
        m = jnp.ones_like(visc)
        corner = jnp.zeros_like(visc)
        first = [jnp.zeros_like(visc)] * 3
        value = None
        for j in range(length):
            if j < length - 1:
                visc_next = 1.0 + row(eddy, (x,), j + 1)
                link = 750.0 * (visc + visc_next)
                inverse = 1.0 / (q + link)
            else:
                visc_next = None
                link = None
                inverse = 1.0 / q
            left = m * inverse
            corner = corner + m * left
            source = [
                2.0 * row(velocity, (c, x), j) + row(tendency, (c, x), j) for c in range(3)
            ]
            if j > 0:
                source = [s + link_before * v for s, v in zip(source, value)]
            value = [s * inverse for s in source]
            first = [f + m * v for f, v in zip(first, value)]
            for c in range(3):
                factors[x, j, c] = value[c]
            factors[x, j, 3] = left
            if j < length - 1:
                ratio = link * inverse
                factors[x, j, 4] = ratio
                q = 1.0 + link * (q * inverse)
                m = m * ratio
                link_before = link
                visc = visc_next
            else:
                factors[x, j, 4] = inverse
        last = value
        across = left
        end = inverse
        links = 750.0 * (visc + pltpu.roll(visc_first, SEGMENTS - 1, 0))
        level, step = 0, 1
        while step < SEGMENTS:
            def other(v):
                return pltpu.roll(v, SEGMENTS - step, 0)

            link = links if step == 1 else pltpu.roll(links, SEGMENTS - (step - 1), 0)
            across_b = other(across)
            stiff = link / (1.0 + link * (end + other(corner)))
            flux = [stiff * (g - other(f)) for g, f in zip(last, first)]
            from_left = stiff * across
            from_right = stiff * across_b
            for c in range(3):
                tree[x, level, c] = flux[c]
            tree[x, level, 3] = from_left
            tree[x, level, 4] = from_right
            first = [f - across * t for f, t in zip(first, flux)]
            last = [other(g) + across_b * t for g, t in zip(last, flux)]
            corner = corner - across * from_left
            end = other(end) - across_b * from_right
            across = from_left * across_b
            level, step = level + 1, step * 2
        rows_out = [*first, *last, corner, across, end, visc_first]
        for i, v in enumerate(rows_out):
            reduced[i * width + x : i * width + x + 1, :] = v[0:1, :]
        i = len(rows_out)
        reduced[i * width + x : i * width + x + 1, :] = visc[SEGMENTS - 1 :, :]


def partner(i, step, count):
    if count & (count - 1) == 0:
        return i ^ step
    return (i - step + count) % count


def finish_kernel(devices, position, factors, tree, velocity, *rest):
    reduced, (out, gathered, fluxes) = rest[:devices], rest[devices:]
    width, length = factors.shape[:2]
    here = position[0]
    for step in range(devices):
        gathered[partner(here, step, devices)] = reduced[step][...]

    def part(device, i):
        return gathered[device, i * width : (i + 1) * width, :]

    ratios, values = [], []
    for i in range(devices + 1):
        if i == 0:
            link = 750.0 * part(0, 9)
            total = part(0, 6)
            source = [-part(0, c) for c in range(3)]
        elif i == devices:
            link = 750.0 * part(i - 1, 10)
            total = part(i - 1, 8)
            source = [part(i - 1, 3 + c) for c in range(3)]
        else:
            link = 750.0 * (part(i - 1, 10) + part(i, 9))
            total = part(i - 1, 8) + part(i, 6)
            source = [part(i - 1, 3 + c) - part(i, c) for c in range(3)]
        pivot = 1.0 + link * total
        if i > 0:
            before = part(i - 1, 7)
            pivot = pivot - link * before * ratios[-1]
            source = [s + before * v for s, v in zip(source, values[-1])]
        scale = link / pivot
        values.append([scale * s for s in source])
        if i < devices:
            ratios.append(scale * part(i, 7))
    flux = values[devices]
    for i in range(devices, -1, -1):
        if i < devices:
            flux = [v + ratios[i] * f for v, f in zip(values[i], flux)]
        for c in range(3):
            fluxes[i, c * width : (c + 1) * width, :] = flux[c]

    sublane = lax.broadcasted_iota(jnp.int32, (SEGMENTS, LANES), 0)
    levels = tree.shape[1]
    for x in range(width):
        for c in range(3):
            r = c * width + x
            left = jnp.broadcast_to(fluxes[here, r : r + 1, :], (SEGMENTS, LANES))
            right = -jnp.broadcast_to(fluxes[here + 1, r : r + 1, :], (SEGMENTS, LANES))
            for level in range(levels - 1, -1, -1):
                step = 2**level
                through = tree[x, level, c] + tree[x, level, 3] * left - tree[x, level, 4] * right
                second = lax.rem(sublane, 2 * step) == step
                left = jnp.where(second, pltpu.roll(through, step, 0), left)
                right = jnp.where(second, pltpu.roll(right, step, 0), -through)
            value = right
            for j in range(length - 1, -1, -1):
                value = (factors[x, j, c] + factors[x, j, 3] * left) + factors[x, j, 4] * value
                rows = pl.ds(j, SEGMENTS, stride=length)
                out[c, x, rows, :] = value - velocity[c, x, rows, :]


def in_vmem(count):
    return [pl.BlockSpec(memory_space=pltpu.VMEM)] * count


def in_smem(count):
    return [pl.BlockSpec(memory_space=pltpu.SMEM)] * count


def params():
    return pltpu.CompilerParams(vmem_limit_bytes=VMEM_BYTES)


def body(velocity, tendency):
    _, width, cells, lanes = velocity.shape
    nz_parts = lax.axis_size("gz")
    count = lax.axis_size("gx") * nz_parts
    walls = lax.axis_size("gy")
    rows = cells // count
    nx = lax.axis_size("gx") * width
    padded = 16 + aligned(rows)
    f32 = jnp.float32

    planes = 3 * width
    depth = aligned(planes * rows + 2 * aligned(planes))
    position = lax.axis_index("gy").astype(jnp.int32).reshape(1)
    parity = lax.rem(position, 2)
    chunks = pl.pallas_call(
        functools.partial(pack_kernel, rows),
        out_shape=jax.ShapeDtypeStruct((count, depth, lanes), f32),
        in_specs=in_smem(1) + in_vmem(1),
        out_specs=pl.BlockSpec(memory_space=pltpu.VMEM),
        compiler_params=params(),
        name="pack",
    )(parity, velocity)
    recv = lax.all_to_all(chunks, ("gx", "gz"), split_axis=0, concat_axis=0, tiled=True)
    slot = lax.slice_in_dim(recv, planes * rows, planes * rows + aligned(planes), axis=1)
    swapped = lax.ppermute(slot, ("gy", "gx", "gz"), swap_pairs(walls, count))
    rank = lax.axis_index(("gx", "gz")).astype(jnp.int32).reshape(1)
    chunk_shape = jax.ShapeDtypeStruct((count, width, rows, lanes), f32)
    cells_here = nx * nz_parts * rows * lanes
    provisional = pl.pallas_call(
        functools.partial(germano_kernel, nz_parts, width, rows),
        out_shape=chunk_shape,
        in_specs=in_smem(2) + in_vmem(1),
        out_specs=pl.BlockSpec(memory_space=pltpu.VMEM),
        scratch_shapes=[
            pltpu.VMEM((3, nx, nz_parts, padded, lanes), f32),
            pltpu.VMEM((3, nx, nz_parts, padded, lanes), f32),
            pltpu.VMEM((3, nx, nz_parts, 8, lanes), f32),
            pltpu.VMEM((nx, nz_parts, rows, lanes), f32),
            pltpu.VMEM((15, nx, nz_parts, rows, lanes), f32),
        ],
        compiler_params=params(),
        cost_estimate=pl.CostEstimate(
            flops=300 * cells_here, bytes_accessed=16 * cells_here, transcendentals=2 * cells_here
        ),
        name="germano",
    )(rank, parity, recv)
    eddy_chunks = pl.pallas_call(
        functools.partial(edge_kernel, nz_parts, width, rows, walls),
        out_shape=chunk_shape,
        in_specs=in_smem(2) + in_vmem(3),
        out_specs=pl.BlockSpec(memory_space=pltpu.VMEM),
        scratch_shapes=[pltpu.VMEM((3, 3, nx, nz_parts * lanes), f32)],
        input_output_aliases={4: 0},
        compiler_params=params(),
        name="edge",
    )(rank, position, recv, swapped, provisional)
    back = lax.all_to_all(eddy_chunks, ("gx", "gz"), split_axis=0, concat_axis=0, tiled=True)

    length = cells // SEGMENTS
    levels = SEGMENTS.bit_length() - 1
    packed = aligned(11 * width)
    eddy, reduced, factors, tree = pl.pallas_call(
        sweep_kernel,
        out_shape=(
            jax.ShapeDtypeStruct((width, cells, lanes), f32),
            jax.ShapeDtypeStruct((packed, lanes), f32),
            jax.ShapeDtypeStruct((width, length, 5, SEGMENTS, lanes), f32),
            jax.ShapeDtypeStruct((width, levels, 5, SEGMENTS, lanes), f32),
        ),
        in_specs=in_smem(1) + in_vmem(3),
        out_specs=tuple(in_vmem(4)),
        compiler_params=params(),
        name="sweep",
    )(parity, back, velocity, tendency)

    others = [
        lax.ppermute(reduced, "gy", [(partner(i, step, walls), i) for i in range(walls)])
        for step in range(1, walls)
    ]
    new_velocity = pl.pallas_call(
        functools.partial(finish_kernel, walls),
        out_shape=jax.ShapeDtypeStruct(velocity.shape, f32),
        in_specs=in_smem(1) + in_vmem(3 + walls),
        out_specs=pl.BlockSpec(memory_space=pltpu.VMEM),
        scratch_shapes=[
            pltpu.VMEM((walls, packed, lanes), f32),
            pltpu.VMEM((walls + 1, aligned(3 * width), lanes), f32),
        ],
        compiler_params=params(),
        name="finish",
    )(position, factors, tree, velocity, reduced, *others)
    return (new_velocity, eddy)


def solution(mesh):
    return jax.shard_map(
        body,
        mesh=mesh,
        in_specs=(P(None, "gx", "gy", "gz"), P(None, "gx", "gy", "gz")),
        out_specs=(P(None, "gx", "gy", "gz"), P("gx", "gy", "gz")),
        check_vma=False,
    )
```

```python
import functools

import jax
import jax.numpy as jnp
from jax import lax
from jax.experimental import pallas as pl
from jax.experimental.pallas import tpu as pltpu
from jax.sharding import PartitionSpec as P

LANES = 128
SEGMENTS = 8
VMEM_BYTES = 24 * 2**20


def strain_parts(grad_x, grad_y, grad_z):
    return (
        grad_x[0],
        grad_y[1],
        grad_z[2],
        grad_y[0] + grad_x[1],
        grad_z[0] + grad_x[2],
        grad_z[1] + grad_y[2],
    )


def strain_size(parts):
    diagonal = parts[0] * parts[0] + parts[1] * parts[1] + parts[2] * parts[2]
    mixed = parts[3] * parts[3] + parts[4] * parts[4] + parts[5] * parts[5]
    return jnp.sqrt(0.5 * diagonal + 0.25 * mixed)


def beside(blocks):
    count = len(blocks)
    lanes = blocks[0].shape[1]
    down = [pltpu.roll(f, 1, 1) for f in blocks]
    up = [pltpu.roll(f, lanes - 1, 1) for f in blocks]
    if count > 1:
        lane = lax.broadcasted_iota(jnp.int32, blocks[0].shape, 1)
        first, last = lane == 0, lane == lanes - 1
        down, up = (
            [jnp.where(first, down[i - 1], down[i]) for i in range(count)],
            [jnp.where(last, up[(i + 1) % count], up[i]) for i in range(count)],
        )
    return down, up


def slope_z(blocks):
    down, up = beside(blocks)
    return [u - d for u, d in zip(up, down)]


def smooth_z(blocks):
    down, up = beside(blocks)
    return [(u + d) + 2.0 * f for f, u, d in zip(blocks, up, down)]


def products(v):
    return (v[0] * v[0], v[1] * v[1], v[2] * v[2], v[0] * v[1], v[0] * v[2], v[1] * v[2])


def outer_ranks(count):
    return (count - 1, count - 3)


def places(parity, count):
    outer = outer_ranks(count)
    inner = iter(range(1, count - 1))
    return [
        (0 if outer[parity] == rank else count - 1) if rank in outer else next(inner)
        for rank in range(count)
    ]


def swap_pairs(walls, count):
    odd, even = outer_ranks(count)
    spare = count - 5
    partners = {}

    def join(a, b):
        partners[a], partners[b] = b, a

    def join_walls(rank, first):
        for wall in range(first, walls - 1, 2):
            join((wall, rank), (wall + 1, rank))

    join_walls(even, 0)
    join_walls(odd, 1)
    join_walls(spare, 1)
    join((0, odd), (0, spare))
    if walls % 2 == 0:
        join((walls - 1, odd), (walls - 1, spare))
    others = [r for r in range(count) if r not in (odd, even, spare)]
    for core in range(2):
        ranks = [r for r in others if r % 2 == core]
        half = len(ranks) // 2
        for wall in range(walls):
            for a, b in zip(ranks[:half], ranks[half : 2 * half]):
                join((wall, a), (wall, b))
        for rank in ranks[2 * half :]:
            join_walls(rank, 0)
    return [
        (wall * count + rank, to[0] * count + to[1])
        for wall in range(walls)
        for rank in range(count)
        for to in [partners.get((wall, rank), (wall, rank))]
    ]


def by_parity(parity, count, fill):
    outer = outer_ranks(count)
    for rank, place in enumerate(places(0, count)):
        if rank not in outer:
            fill(rank, place)
    for turn in range(2):

        @pl.when(parity[0] == turn)
        def _():
            for rank in outer:
                fill(rank, places(turn, count)[rank])


def aligned(n):
    return -(-n // 8) * 8


def pack_kernel(rows, parity, velocity, out):
    _, width, cells, _ = velocity.shape
    count, depth, lanes = out.shape
    planes = 3 * width
    slots = planes * rows

    def fill(rank, place):
        first = place * rows
        beside = [first - 1, first + rows]
        if place == 0:
            beside = [first, first + rows]
        if place == count - 1:
            beside = [first + rows - 1, first - 1]
        for i in range(planes):
            c, x = divmod(i, width)
            out[rank, i * rows : (i + 1) * rows, :] = velocity[c, x, first : first + rows, :]
            for slot, row in enumerate(beside):
                at = slots + slot * aligned(planes) + i
                out[rank, at : at + 1, :] = velocity[c, x, row : row + 1, :]

    by_parity(parity, count, fill)
    blank = aligned(planes) - planes
    for rank in range(count):
        for slot in range(2):
            at = slots + slot * aligned(planes) + planes
            out[rank, at : at + blank, :] = jnp.zeros((blank, lanes), jnp.float32)
        at = slots + 2 * aligned(planes)
        if at < depth:
            out[rank, at:, :] = jnp.zeros((depth - at, lanes), jnp.float32)


def outer_sides(rank, parity, count):
    outer = outer_ranks(count)
    even = parity[0] == 0
    bottom = rank[0] == jnp.where(even, outer[0], outer[1])
    top = rank[0] == jnp.where(even, outer[1], outer[0])
    return bottom, top


def edge_kernel(nz_parts, width, rows, walls, rank, position, recv, swapped, given, out, vel):
    count, _, lanes = recv.shape
    planes = 3 * width
    nx = (count // nz_parts) * width
    nz = nz_parts * lanes
    bottom, top = outer_sides(rank, [lax.rem(position[0], 2)], count)
    at_wall = jnp.logical_or(
        jnp.logical_and(bottom, position[0] == 0), jnp.logical_and(top, position[0] == walls - 1)
    )

    def rows_of(k, i):
        first = i * rows
        own = [recv[k, first + j : first + j + 1, :] for j in (0, 1, rows - 2, rows - 1)]
        far = jnp.where(at_wall, 0.0, swapped[k, i : i + 1, :])
        return (
            jnp.where(bottom, far, own[2]),
            jnp.where(bottom, own[0], own[3]),
            jnp.where(bottom, own[1], far),
        )

    def roll_x(f, shift):
        return pltpu.roll(f, shift % nx, 0)

    def roll_z(f, shift):
        return pltpu.roll(f, shift % nz, 1)

    def smooth_x(f):
        return (roll_x(f, 1) + roll_x(f, -1)) + 2.0 * f

    def smooth(f):
        f = smooth_x(f)
        return (roll_z(f, 1) + roll_z(f, -1)) + 2.0 * f

    def slopes(below, centre, above):
        return strain_parts(
            [roll_x(f, -1) - roll_x(f, 1) for f in centre],
            [a - b for a, b in zip(above, below)],
            [roll_z(f, -1) - roll_z(f, 1) for f in centre],
        )

    @pl.when(jnp.logical_or(bottom, top))
    def _():
        for k in range(count):
            x0, zb = (k // nz_parts) * width, k % nz_parts
            for i in range(planes):
                c, x = divmod(i, width)
                for j, row in enumerate(rows_of(k, i)):
                    vel[j, c, x0 + x : x0 + x + 1, zb * lanes : (zb + 1) * lanes] = row
        u = [[vel[j, c] for c in range(3)] for j in range(3)]
        v = [[smooth(f) for f in row] for row in u]
        strain = slopes(*u)
        size = strain_size(strain)
        mean_strain = slopes(*v)
        mean_size = 0.25 * strain_size(mean_strain)
        scaled = [0.0625 * f for f in v[1]]
        pairs = [v[1][i] * scaled[j] for i, j in ((0, 0), (1, 1), (2, 2), (0, 1), (0, 2), (1, 2))]
        leonard = [smooth(p) - q for p, q in zip(products(u[1]), pairs)]
        model = [smooth(size * s) - mean_size * f for s, f in zip(strain, mean_strain)]
        lm, mm = contracted(leonard, model)
        coefficient = coefficient_of(
            *(jnp.sum(f, axis=(0, 1), keepdims=True) for f in (lm, mm)), nx * nz
        )
        eddy = coefficient * size

        def put(at):
            for k in range(count):
                x0, zb = (k // nz_parts) * width, k % nz_parts
                for x in range(width):
                    out[k, x, at : at + 1, :] = eddy[x0 + x : x0 + x + 1, zb * lanes : (zb + 1) * lanes]

        pl.when(bottom)(lambda: put(0))
        pl.when(top)(lambda: put(rows - 1))


def contracted(leonard, model):
    lm = mm = None
    for i in range(6):
        square = model[i] * model[i] if i < 3 else (0.5 * model[i]) * model[i]
        product = leonard[i] * model[i]
        lm = product if lm is None else lm + product
        mm = square if mm is None else mm + square
    return lm, mm


def coefficient_of(plane_lm, plane_mm, cells):
    scale = 1.0 / (256.0 * cells)
    return jnp.maximum(plane_lm * scale / (plane_mm * scale + 1e-06), 0.0)


def germano_kernel(nz_parts, width, rows, rank, parity, recv, out, vel, filt, ends, mag, part):
    count, _, lanes = recv.shape
    planes = 3 * width
    _, top = outer_sides(rank, parity, count)
    nx = (count // nz_parts) * width
    nz = nz_parts * lanes
    blocks = range(nz_parts)
    lead = 8
    inner = slice(lead, lead + rows)
    lower = slice(lead - 1, lead - 1 + rows)
    upper = slice(lead + 1, lead + 1 + rows)
    for k in range(count):
        x0, zb = (k // nz_parts) * width, k % nz_parts
        for c in range(3):
            for x in range(width):
                i = c * width + x
                vel[c, x0 + x, zb, inner, :] = recv[k, i * rows : (i + 1) * rows, :]
                slots = planes * rows + i
                near = recv[k, slots : slots + 1, :]
                slots += aligned(planes)
                other = recv[k, slots : slots + 1, :]
                below = jnp.where(top, other, near)
                for side, (edge, at) in enumerate(((below, lead - 1), (other, lead + rows))):
                    vel[c, x0 + x, zb, at : at + 1, :] = edge
                    ends[c, x0 + x, zb, side : side + 1, :] = edge

    for x in range(nx):
        left, right = (x - 1) % nx, (x + 1) % nx
        centre = [[vel[c, x, zb, inner, :] for zb in blocks] for c in range(3)]
        grad_x = [[vel[c, right, zb, inner, :] - vel[c, left, zb, inner, :] for zb in blocks] for c in range(3)]
        grad_y = [[vel[c, x, zb, upper, :] - vel[c, x, zb, lower, :] for zb in blocks] for c in range(3)]
        grad_z = []
        for c in range(3):
            down, up = beside(centre[c])
            grad_z.append([u - d for u, d in zip(up, down)])
            for zb in blocks:
                part[c, x, zb] = (up[zb] + down[zb]) + 2.0 * centre[c][zb]
        strain = [
            strain_parts(*([g[c][zb] for c in range(3)] for g in (grad_x, grad_y, grad_z)))
            for zb in blocks
        ]
        size = [strain_size(s) for s in strain]
        for zb in blocks:
            mag[x, zb] = size[zb]
        pairs = [products([centre[c][zb] for c in range(3)]) for zb in blocks]
        for i in range(6):
            for base, fields in (
                (3, [pairs[zb][i] for zb in blocks]),
                (9, [size[zb] * strain[zb][i] for zb in blocks]),
            ):
                for zb, f in enumerate(smooth_z(fields)):
                    part[base + i, x, zb] = f

    def smooth_x(read, x):
        return (read((x - 1) % nx) + read((x + 1) % nx)) + 2.0 * read(x)

    for c in range(3):
        rims = []
        for x in range(nx):
            rims.append(smooth_z([ends[c, x, zb] for zb in blocks]))
        for x in range(nx):
            for zb in blocks:
                rim = smooth_x(lambda at: rims[at][zb], x)
                filt[c, x, zb, lead - 1 : lead, :] = rim[0:1, :]
                filt[c, x, zb, lead + rows : lead + rows + 1, :] = rim[1:2, :]
                filt[c, x, zb, inner, :] = smooth_x(lambda at: part[c, at, zb], x)

    sum_lm = sum_mm = None
    for x in range(nx):
        left, right = (x - 1) % nx, (x + 1) % nx
        mean = [[filt[c, x, zb, inner, :] for zb in blocks] for c in range(3)]
        grad_x = [[filt[c, right, zb, inner, :] - filt[c, left, zb, inner, :] for zb in blocks] for c in range(3)]
        grad_y = [[filt[c, x, zb, upper, :] - filt[c, x, zb, lower, :] for zb in blocks] for c in range(3)]
        grad_z = [slope_z(mean[c]) for c in range(3)]
        for zb in blocks:
            strain = strain_parts(*([g[c][zb] for c in range(3)] for g in (grad_x, grad_y, grad_z)))
            size = 0.25 * strain_size(strain)
            v = [mean[c][zb] for c in range(3)]
            scaled = [0.0625 * f for f in v]
            pairs = (
                v[0] * scaled[0],
                v[1] * scaled[1],
                v[2] * scaled[2],
                v[0] * scaled[1],
                v[0] * scaled[2],
                v[1] * scaled[2],
            )
            leonard = [smooth_x(lambda at: part[3 + i, at, zb], x) - pairs[i] for i in range(6)]
            model = [smooth_x(lambda at: part[9 + i, at, zb], x) - size * strain[i] for i in range(6)]
            lm, mm = contracted(leonard, model)
            sum_lm = lm if sum_lm is None else sum_lm + lm
            sum_mm = mm if sum_mm is None else sum_mm + mm

    coefficient = coefficient_of(
        *(jnp.sum(total, axis=1, keepdims=True) for total in (sum_lm, sum_mm)), nx * nz
    )
    for k in range(count):
        x0, zb = (k // nz_parts) * width, k % nz_parts
        for x in range(width):
            out[k, x] = coefficient * mag[x0 + x, zb]


def sweep_kernel(parity, back, velocity, tendency, eddy_out, reduced, factors, tree, eddy, sent):
    count, width, rows, _ = back.shape
    length = count * rows // SEGMENTS

    def fill(rank, place):
        for x in range(width):
            eddy[x, place * rows : (place + 1) * rows, :] = back[rank, x]

    by_parity(parity, count, fill)
    write = pltpu.make_async_copy(eddy, eddy_out, sent)
    write.start()

    def row(ref, index, j):
        return ref[(*index, pl.ds(j, SEGMENTS, stride=length), slice(None))]

    for x in range(width):
        visc = 1.0 + row(eddy, (x,), 0)
        visc_first = visc
        q = jnp.ones_like(visc)
        m = jnp.ones_like(visc)
        corner = jnp.zeros_like(visc)
        first = [jnp.zeros_like(visc)] * 3
        value = None
        for j in range(length):
            if j < length - 1:
                visc_next = 1.0 + row(eddy, (x,), j + 1)
                link = 750.0 * (visc + visc_next)
                inverse = 1.0 / (q + link)
            else:
                visc_next = None
                link = None
                inverse = 1.0 / q
            left = m * inverse
            corner = corner + m * left
            source = [
                2.0 * row(velocity, (c, x), j) + row(tendency, (c, x), j) for c in range(3)
            ]
            if j > 0:
                source = [s + link_before * v for s, v in zip(source, value)]
            value = [s * inverse for s in source]
            first = [f + m * v for f, v in zip(first, value)]
            for c in range(3):
                factors[x, j, c] = value[c]
            factors[x, j, 3] = left
            if j < length - 1:
                ratio = link * inverse
                factors[x, j, 4] = ratio
                q = 1.0 + link * (q * inverse)
                m = m * ratio
                link_before = link
                visc = visc_next
            else:
                factors[x, j, 4] = inverse
        last = value
        across = left
        end = inverse
        links = 750.0 * (visc + pltpu.roll(visc_first, SEGMENTS - 1, 0))
        level, step = 0, 1
        while step < SEGMENTS:
            def other(v):
                return pltpu.roll(v, SEGMENTS - step, 0)

            link = links if step == 1 else pltpu.roll(links, SEGMENTS - (step - 1), 0)
            across_b = other(across)
            stiff = link / (1.0 + link * (end + other(corner)))
            flux = [stiff * (g - other(f)) for g, f in zip(last, first)]
            from_left = stiff * across
            from_right = stiff * across_b
            for c in range(3):
                tree[x, level, c] = flux[c]
            tree[x, level, 3] = from_left
            tree[x, level, 4] = from_right
            first = [f - across * t for f, t in zip(first, flux)]
            last = [other(g) + across_b * t for g, t in zip(last, flux)]
            corner = corner - across * from_left
            end = other(end) - across_b * from_right
            across = from_left * across_b
            level, step = level + 1, step * 2
        rows_out = [*first, *last, corner, across, end, visc_first]
        for i, v in enumerate(rows_out):
            reduced[i * width + x : i * width + x + 1, :] = v[0:1, :]
        i = len(rows_out)
        reduced[i * width + x : i * width + x + 1, :] = visc[SEGMENTS - 1 :, :]
    write.wait()


def partner(i, step, count):
    if count & (count - 1) == 0:
        return i ^ step
    return (i - step + count) % count


def finish_kernel(devices, position, factors, tree, velocity, *rest):
    reduced, (result, gathered, fluxes, out, sent) = rest[:devices], rest[devices:]
    width, length = factors.shape[:2]
    here = position[0]
    for step in range(devices):
        gathered[partner(here, step, devices)] = reduced[step][...]

    def part(device, i):
        return gathered[device, i * width : (i + 1) * width, :]

    ratios, values = [], []
    for i in range(devices + 1):
        if i == 0:
            link = 750.0 * part(0, 9)
            total = part(0, 6)
            source = [-part(0, c) for c in range(3)]
        elif i == devices:
            link = 750.0 * part(i - 1, 10)
            total = part(i - 1, 8)
            source = [part(i - 1, 3 + c) for c in range(3)]
        else:
            link = 750.0 * (part(i - 1, 10) + part(i, 9))
            total = part(i - 1, 8) + part(i, 6)
            source = [part(i - 1, 3 + c) - part(i, c) for c in range(3)]
        pivot = 1.0 + link * total
        if i > 0:
            before = part(i - 1, 7)
            pivot = pivot - link * before * ratios[-1]
            source = [s + before * v for s, v in zip(source, values[-1])]
        scale = link / pivot
        values.append([scale * s for s in source])
        if i < devices:
            ratios.append(scale * part(i, 7))
    flux = values[devices]
    for i in range(devices, -1, -1):
        if i < devices:
            flux = [v + ratios[i] * f for v, f in zip(values[i], flux)]
        for c in range(3):
            fluxes[i, c * width : (c + 1) * width, :] = flux[c]

    sublane = lax.broadcasted_iota(jnp.int32, (SEGMENTS, LANES), 0)
    levels = tree.shape[1]
    writes = []
    for c in range(3):
        for x in range(width):
            r = c * width + x
            left = jnp.broadcast_to(fluxes[here, r : r + 1, :], (SEGMENTS, LANES))
            right = -jnp.broadcast_to(fluxes[here + 1, r : r + 1, :], (SEGMENTS, LANES))
            for level in range(levels - 1, -1, -1):
                step = 2**level
                through = tree[x, level, c] + tree[x, level, 3] * left - tree[x, level, 4] * right
                second = lax.rem(sublane, 2 * step) == step
                left = jnp.where(second, pltpu.roll(through, step, 0), left)
                right = jnp.where(second, pltpu.roll(right, step, 0), -through)
            value = right
            for j in range(length - 1, -1, -1):
                value = (factors[x, j, c] + factors[x, j, 3] * left) + factors[x, j, 4] * value
                rows = pl.ds(j, SEGMENTS, stride=length)
                out[c, x, rows, :] = value - velocity[c, x, rows, :]
            writes.append(pltpu.make_async_copy(out.at[c, x], result.at[c, x], sent.at[r]))
            writes[-1].start()
    for write in writes:
        write.wait()


def in_vmem(count):
    return [pl.BlockSpec(memory_space=pltpu.VMEM)] * count


def in_hbm(count):
    return [pl.BlockSpec(memory_space=pltpu.HBM)] * count


def in_smem(count):
    return [pl.BlockSpec(memory_space=pltpu.SMEM)] * count


def params():
    return pltpu.CompilerParams(vmem_limit_bytes=VMEM_BYTES)


def body(velocity, tendency):
    _, width, cells, lanes = velocity.shape
    nz_parts = lax.axis_size("gz")
    count = lax.axis_size("gx") * nz_parts
    walls = lax.axis_size("gy")
    rows = cells // count
    nx = lax.axis_size("gx") * width
    padded = 16 + aligned(rows)
    f32 = jnp.float32

    planes = 3 * width
    depth = aligned(planes * rows + 2 * aligned(planes))
    position = lax.axis_index("gy").astype(jnp.int32).reshape(1)
    parity = lax.rem(position, 2)
    chunks = pl.pallas_call(
        functools.partial(pack_kernel, rows),
        out_shape=jax.ShapeDtypeStruct((count, depth, lanes), f32),
        in_specs=in_smem(1) + in_vmem(1),
        out_specs=pl.BlockSpec(memory_space=pltpu.VMEM),
        compiler_params=params(),
        name="pack",
    )(parity, velocity)
    recv = lax.all_to_all(chunks, ("gx", "gz"), split_axis=0, concat_axis=0, tiled=True)
    slot = lax.slice_in_dim(recv, planes * rows, planes * rows + aligned(planes), axis=1)
    swapped = lax.ppermute(slot, ("gy", "gx", "gz"), swap_pairs(walls, count))
    rank = lax.axis_index(("gx", "gz")).astype(jnp.int32).reshape(1)
    chunk_shape = jax.ShapeDtypeStruct((count, width, rows, lanes), f32)
    cells_here = nx * nz_parts * rows * lanes
    provisional = pl.pallas_call(
        functools.partial(germano_kernel, nz_parts, width, rows),
        out_shape=chunk_shape,
        in_specs=in_smem(2) + in_vmem(1),
        out_specs=pl.BlockSpec(memory_space=pltpu.VMEM),
        scratch_shapes=[
            pltpu.VMEM((3, nx, nz_parts, padded, lanes), f32),
            pltpu.VMEM((3, nx, nz_parts, padded, lanes), f32),
            pltpu.VMEM((3, nx, nz_parts, 8, lanes), f32),
            pltpu.VMEM((nx, nz_parts, rows, lanes), f32),
            pltpu.VMEM((15, nx, nz_parts, rows, lanes), f32),
        ],
        compiler_params=params(),
        cost_estimate=pl.CostEstimate(
            flops=300 * cells_here, bytes_accessed=16 * cells_here, transcendentals=2 * cells_here
        ),
        name="germano",
    )(rank, parity, recv)
    eddy_chunks = pl.pallas_call(
        functools.partial(edge_kernel, nz_parts, width, rows, walls),
        out_shape=chunk_shape,
        in_specs=in_smem(2) + in_vmem(3),
        out_specs=pl.BlockSpec(memory_space=pltpu.VMEM),
        scratch_shapes=[pltpu.VMEM((3, 3, nx, nz_parts * lanes), f32)],
        input_output_aliases={4: 0},
        compiler_params=params(),
        name="edge",
    )(rank, position, recv, swapped, provisional)
    back = lax.all_to_all(eddy_chunks, ("gx", "gz"), split_axis=0, concat_axis=0, tiled=True)

    length = cells // SEGMENTS
    levels = SEGMENTS.bit_length() - 1
    packed = aligned(11 * width)
    eddy, reduced, factors, tree = pl.pallas_call(
        sweep_kernel,
        out_shape=(
            jax.ShapeDtypeStruct((width, cells, lanes), f32),
            jax.ShapeDtypeStruct((packed, lanes), f32),
            jax.ShapeDtypeStruct((width, length, 5, SEGMENTS, lanes), f32),
            jax.ShapeDtypeStruct((width, levels, 5, SEGMENTS, lanes), f32),
        ),
        in_specs=in_smem(1) + in_vmem(3),
        out_specs=tuple(in_hbm(1) + in_vmem(3)),
        scratch_shapes=[pltpu.VMEM((width, cells, lanes), f32), pltpu.SemaphoreType.DMA],
        compiler_params=params(),
        name="sweep",
    )(parity, back, velocity, tendency)

    others = [
        lax.ppermute(reduced, "gy", [(partner(i, step, walls), i) for i in range(walls)])
        for step in range(1, walls)
    ]
    new_velocity = pl.pallas_call(
        functools.partial(finish_kernel, walls),
        out_shape=jax.ShapeDtypeStruct(velocity.shape, f32),
        in_specs=in_smem(1) + in_vmem(3 + walls),
        out_specs=in_hbm(1)[0],
        scratch_shapes=[
            pltpu.VMEM((walls, packed, lanes), f32),
            pltpu.VMEM((walls + 1, aligned(3 * width), lanes), f32),
            pltpu.VMEM(velocity.shape, f32),
            pltpu.SemaphoreType.DMA((planes,)),
        ],
        compiler_params=params(),
        name="finish",
    )(position, factors, tree, velocity, reduced, *others)
    return (new_velocity, eddy)


def solution(mesh):
    return jax.shard_map(
        body,
        mesh=mesh,
        in_specs=(P(None, "gx", "gy", "gz"), P(None, "gx", "gy", "gz")),
        out_specs=(P(None, "gx", "gy", "gz"), P("gx", "gy", "gz")),
        check_vma=False,
    )
```

```python
import functools

import jax
import jax.numpy as jnp
from jax import lax
from jax.experimental import pallas as pl
from jax.experimental.pallas import tpu as pltpu
from jax.sharding import PartitionSpec as P

LANES = 128
SEGMENTS = 8
VMEM_BYTES = 24 * 2**20


def strain_parts(grad_x, grad_y, grad_z):
    return (
        grad_x[0],
        grad_y[1],
        grad_z[2],
        grad_y[0] + grad_x[1],
        grad_z[0] + grad_x[2],
        grad_z[1] + grad_y[2],
    )


def strain_size(parts):
    diagonal = parts[0] * parts[0] + parts[1] * parts[1] + parts[2] * parts[2]
    mixed = parts[3] * parts[3] + parts[4] * parts[4] + parts[5] * parts[5]
    return jnp.sqrt(0.5 * diagonal + 0.25 * mixed)


def lane_of(shape):
    return lax.broadcasted_iota(jnp.int32, shape, len(shape) - 1)


def picked(f, lanes):
    return jnp.take_along_axis(f, lanes, axis=1)


def to_phases(blocks):
    count = len(blocks)
    if count == 1:
        return blocks
    lanes = blocks[0].shape[1]
    phases = []
    for j in range(count):
        z = lane_of(blocks[0].shape) * count + j
        phase = picked(blocks[0], lax.rem(z, lanes))
        for b in range(1, count):
            phase = jnp.where(z >= b * lanes, picked(blocks[b], lax.rem(z, lanes)), phase)
        phases.append(phase)
    return phases


def to_blocks(phases):
    count = len(phases)
    if count == 1:
        return phases
    lanes = phases[0].shape[1]
    blocks = []
    for b in range(count):
        z = lane_of(phases[0].shape) + b * lanes
        block = picked(phases[0], lax.div(z, count))
        for j in range(1, count):
            block = jnp.where(lax.rem(z, count) == j, picked(phases[j], lax.div(z, count)), block)
        blocks.append(block)
    return blocks


def after(phases):
    return [*phases[1:], pltpu.roll(phases[0], phases[0].shape[1] - 1, 1)]


def before(phases):
    return [pltpu.roll(phases[-1], 1, 1), *phases[:-1]]


def smooth_z(phases, up=None):
    sums = [f + u for f, u in zip(phases, after(phases) if up is None else up)]
    return [f + d for f, d in zip(sums, before(sums))]


def smooth_pair(a, b, c, d):
    middle = b + c
    return (a + b) + middle, middle + (c + d)


def products(v):
    return (v[0] * v[0], v[1] * v[1], v[2] * v[2], v[0] * v[1], v[0] * v[2], v[1] * v[2])


def outer_ranks(count):
    return (count - 1, count - 3)


def places(parity, count):
    outer = outer_ranks(count)
    inner = iter(range(1, count - 1))
    return [
        (0 if outer[parity] == rank else count - 1) if rank in outer else next(inner)
        for rank in range(count)
    ]


def swap_pairs(walls, count):
    odd, even = outer_ranks(count)
    spare = count - 5
    partners = {}

    def join(a, b):
        partners[a], partners[b] = b, a

    def join_walls(rank, first):
        for wall in range(first, walls - 1, 2):
            join((wall, rank), (wall + 1, rank))

    join_walls(even, 0)
    join_walls(odd, 1)
    join_walls(spare, 1)
    join((0, odd), (0, spare))
    if walls % 2 == 0:
        join((walls - 1, odd), (walls - 1, spare))
    others = [r for r in range(count) if r not in (odd, even, spare)]
    for core in range(2):
        ranks = [r for r in others if r % 2 == core]
        half = len(ranks) // 2
        for wall in range(walls):
            for a, b in zip(ranks[:half], ranks[half : 2 * half]):
                join((wall, a), (wall, b))
        for rank in ranks[2 * half :]:
            join_walls(rank, 0)
    return [
        (wall * count + rank, to[0] * count + to[1])
        for wall in range(walls)
        for rank in range(count)
        for to in [partners.get((wall, rank), (wall, rank))]
    ]


def by_parity(parity, count, fill):
    outer = outer_ranks(count)
    for rank, place in enumerate(places(0, count)):
        if rank not in outer:
            fill(rank, place)
    for turn in range(2):

        @pl.when(parity[0] == turn)
        def _():
            for rank in outer:
                fill(rank, places(turn, count)[rank])


def aligned(n):
    return -(-n // 8) * 8


def pack_kernel(rows, parity, velocity, out):
    _, width, cells, _ = velocity.shape
    count, depth, lanes = out.shape
    planes = 3 * width
    slots = planes * rows

    def fill(rank, place):
        first = place * rows
        beside = [first - 1, first + rows]
        if place == 0:
            beside = [first, first + rows]
        if place == count - 1:
            beside = [first + rows - 1, first - 1]
        for i in range(planes):
            c, x = divmod(i, width)
            out[rank, i * rows : (i + 1) * rows, :] = velocity[c, x, first : first + rows, :]
            for slot, row in enumerate(beside):
                at = slots + slot * aligned(planes) + i
                out[rank, at : at + 1, :] = velocity[c, x, row : row + 1, :]

    by_parity(parity, count, fill)
    blank = aligned(planes) - planes
    for rank in range(count):
        for slot in range(2):
            at = slots + slot * aligned(planes) + planes
            out[rank, at : at + blank, :] = jnp.zeros((blank, lanes), jnp.float32)
        at = slots + 2 * aligned(planes)
        if at < depth:
            out[rank, at:, :] = jnp.zeros((depth - at, lanes), jnp.float32)


def outer_sides(rank, parity, count):
    outer = outer_ranks(count)
    even = parity[0] == 0
    bottom = rank[0] == jnp.where(even, outer[0], outer[1])
    top = rank[0] == jnp.where(even, outer[1], outer[0])
    return bottom, top


def edge_kernel(nz_parts, width, rows, walls, rank, position, recv, swapped, given, out, vel):
    count, _, lanes = recv.shape
    planes = 3 * width
    nx = (count // nz_parts) * width
    nz = nz_parts * lanes
    bottom, top = outer_sides(rank, [lax.rem(position[0], 2)], count)
    at_wall = jnp.logical_or(
        jnp.logical_and(bottom, position[0] == 0), jnp.logical_and(top, position[0] == walls - 1)
    )

    def rows_of(k, i):
        first = i * rows
        own = [recv[k, first + j : first + j + 1, :] for j in (0, 1, rows - 2, rows - 1)]
        far = jnp.where(at_wall, 0.0, swapped[k, i : i + 1, :])
        return (
            jnp.where(bottom, far, own[2]),
            jnp.where(bottom, own[0], own[3]),
            jnp.where(bottom, own[1], far),
        )

    def roll_x(f, shift):
        return pltpu.roll(f, shift % nx, 0)

    def roll_z(f, shift):
        return pltpu.roll(f, shift % nz, 1)

    def smooth_x(f):
        return (roll_x(f, 1) + roll_x(f, -1)) + 2.0 * f

    def smooth(f):
        f = smooth_x(f)
        return (roll_z(f, 1) + roll_z(f, -1)) + 2.0 * f

    def slopes(below, centre, above):
        return strain_parts(
            [roll_x(f, -1) - roll_x(f, 1) for f in centre],
            [a - b for a, b in zip(above, below)],
            [roll_z(f, -1) - roll_z(f, 1) for f in centre],
        )

    @pl.when(jnp.logical_or(bottom, top))
    def _():
        for k in range(count):
            x0, zb = (k // nz_parts) * width, k % nz_parts
            for i in range(planes):
                c, x = divmod(i, width)
                for j, row in enumerate(rows_of(k, i)):
                    vel[j, c, x0 + x : x0 + x + 1, zb * lanes : (zb + 1) * lanes] = row
        u = [[vel[j, c] for c in range(3)] for j in range(3)]
        v = [[smooth(f) for f in row] for row in u]
        strain = slopes(*u)
        size = strain_size(strain)
        mean_strain = slopes(*v)
        mean_size = 0.25 * strain_size(mean_strain)
        scaled = [0.0625 * f for f in v[1]]
        pairs = [v[1][i] * scaled[j] for i, j in ((0, 0), (1, 1), (2, 2), (0, 1), (0, 2), (1, 2))]
        leonard = [smooth(p) - q for p, q in zip(products(u[1]), pairs)]
        model = [smooth(size * s) - mean_size * f for s, f in zip(strain, mean_strain)]
        lm, mm = contracted(leonard, model)
        coefficient = coefficient_of(
            *(jnp.sum(f, axis=(0, 1), keepdims=True) for f in (lm, mm)), nx * nz
        )
        eddy = coefficient * size

        def put(at):
            for k in range(count):
                x0, zb = (k // nz_parts) * width, k % nz_parts
                for x in range(width):
                    out[k, x, at : at + 1, :] = eddy[x0 + x : x0 + x + 1, zb * lanes : (zb + 1) * lanes]

        pl.when(bottom)(lambda: put(0))
        pl.when(top)(lambda: put(rows - 1))


def contracted(leonard, model):
    lm = mm = None
    for i in range(6):
        square = model[i] * model[i] if i < 3 else (0.5 * model[i]) * model[i]
        product = leonard[i] * model[i]
        lm = product if lm is None else lm + product
        mm = square if mm is None else mm + square
    return lm, mm


def coefficient_of(plane_lm, plane_mm, cells):
    scale = 1.0 / (256.0 * cells)
    return jnp.maximum(plane_lm * scale / (plane_mm * scale + 1e-06), 0.0)


def germano_kernel(nz_parts, width, rows, rank, parity, recv, out, vel, filt, ends, mag, part):
    count, _, lanes = recv.shape
    planes = 3 * width
    _, top = outer_sides(rank, parity, count)
    nx = (count // nz_parts) * width
    nz = nz_parts * lanes
    phases = range(nz_parts)
    lead = 8
    tile = min(rows, 8)
    tiles = [lead + t for t in range(0, rows, tile)]

    for c in range(3):
        for x in range(nx):
            i = c * width + x % width
            ranks = [x // width * nz_parts + zb for zb in phases]
            for t in tiles:
                first = i * rows + t - lead
                blocks = [recv[k, first : first + tile, :] for k in ranks]
                for j, f in enumerate(to_phases(blocks)):
                    vel[c, x, j, t : t + tile, :] = f
            for zb, k in enumerate(ranks):
                slots = planes * rows + i
                near = recv[k, slots : slots + 1, :]
                slots += aligned(planes)
                other = recv[k, slots : slots + 1, :]
                ends[c, x, zb, 0:1, :] = jnp.where(top, other, near)
                ends[c, x, zb, 1:2, :] = other
            for j, f in enumerate(to_phases([ends[c, x, zb] for zb in phases])):
                ends[c, x, j] = f
                vel[c, x, j, lead - 1 : lead, :] = f[0:1, :]
                vel[c, x, j, lead + rows : lead + rows + 1, :] = f[1:2, :]

    for x in range(nx):
        left, right = (x - 1) % nx, (x + 1) % nx
        for t in tiles:
            at = slice(t, t + tile)
            lower, upper = slice(t - 1, t - 1 + tile), slice(t + 1, t + 1 + tile)
            own = slice(t - lead, t - lead + tile)
            centre = [[vel[c, x, j, at, :] for j in phases] for c in range(3)]
            grad_x = [[vel[c, right, j, at, :] - vel[c, left, j, at, :] for j in phases] for c in range(3)]
            grad_y = [[vel[c, x, j, upper, :] - vel[c, x, j, lower, :] for j in phases] for c in range(3)]
            grad_z = []
            for c in range(3):
                up, down = after(centre[c]), before(centre[c])
                grad_z.append([u - d for u, d in zip(up, down)])
                for j, f in enumerate(smooth_z(centre[c], up)):
                    part[c, x, j, own, :] = f
            strain = [
                strain_parts(*([g[c][j] for c in range(3)] for g in (grad_x, grad_y, grad_z)))
                for j in phases
            ]
            size = [strain_size(s) for s in strain]
            for j in phases:
                mag[x, j, own, :] = size[j]
            pairs = [products([centre[c][j] for c in range(3)]) for j in phases]
            for i in range(6):
                for base, fields in (
                    (3, [pairs[j][i] for j in phases]),
                    (9, [size[j] * strain[j][i] for j in phases]),
                ):
                    for j, f in enumerate(smooth_z(fields)):
                        part[base + i, x, j, own, :] = f

    for c in range(3):
        rims = [smooth_z([ends[c, x, j] for j in phases]) for x in range(nx)]
        for x in range(0, nx, 2):
            around = [(x - 1) % nx, x, x + 1, (x + 2) % nx]
            for j in phases:
                for at, rim in zip(around[1:3], smooth_pair(*(rims[a][j] for a in around))):
                    filt[c, at, j, lead - 1 : lead, :] = rim[0:1, :]
                    filt[c, at, j, lead + rows : lead + rows + 1, :] = rim[1:2, :]
                for t in tiles:
                    own = slice(t - lead, t - lead + tile)
                    pair = smooth_pair(*(part[c, a, j, own, :] for a in around))
                    for at, f in zip(around[1:3], pair):
                        filt[c, at, j, t : t + tile, :] = f

    sums = [[None, None] for _ in tiles]
    for x in range(0, nx, 2):
        around = [(x - 1) % nx, x, x + 1, (x + 2) % nx]
        for n, t in enumerate(tiles):
            lower, upper = slice(t - 1, t - 1 + tile), slice(t + 1, t + 1 + tile)
            own = slice(t - lead, t - lead + tile)
            mean = [[[filt[c, a, j, t : t + tile, :] for j in phases] for a in around] for c in range(3)]
            slopes_z = [
                [[u - d for u, d in zip(after(m), before(m))] for m in mean[c][1:3]] for c in range(3)
            ]
            for j in phases:
                leonard = [smooth_pair(*(part[3 + i, a, j, own, :] for a in around)) for i in range(6)]
                scaled = [smooth_pair(*(part[9 + i, a, j, own, :] for a in around)) for i in range(6)]
                for w in range(2):
                    at = around[1 + w]
                    grad_x = [mean[c][2 + w][j] - mean[c][w][j] for c in range(3)]
                    grad_y = [filt[c, at, j, upper, :] - filt[c, at, j, lower, :] for c in range(3)]
                    strain = strain_parts(grad_x, grad_y, [slopes_z[c][w][j] for c in range(3)])
                    size = 0.25 * strain_size(strain)
                    v = [mean[c][1 + w][j] for c in range(3)]
                    q = [0.0625 * f for f in v]
                    pairs = [v[a] * q[b] for a, b in ((0, 0), (1, 1), (2, 2), (0, 1), (0, 2), (1, 2))]
                    totals = contracted(
                        [leonard[i][w] - pairs[i] for i in range(6)],
                        [scaled[i][w] - size * strain[i] for i in range(6)],
                    )
                    sums[n] = [f if s is None else s + f for s, f in zip(sums[n], totals)]

    for n, t in enumerate(tiles):
        own = slice(t - lead, t - lead + tile)
        coefficient = coefficient_of(
            *(jnp.sum(total, axis=1, keepdims=True) for total in sums[n]), nx * nz
        )
        for x in range(nx):
            blocks = to_blocks([coefficient * mag[x, j, own, :] for j in phases])
            for zb, f in enumerate(blocks):
                out[x // width * nz_parts + zb, x % width, own, :] = f


def sweep_kernel(parity, back, velocity, tendency, eddy_out, reduced, factors, tree, eddy, sent):
    count, width, rows, _ = back.shape
    length = count * rows // SEGMENTS

    def fill(rank, place):
        for x in range(width):
            eddy[x, place * rows : (place + 1) * rows, :] = back[rank, x]

    by_parity(parity, count, fill)
    write = pltpu.make_async_copy(eddy, eddy_out, sent)
    write.start()

    def row(ref, index, j):
        return ref[(*index, pl.ds(j, SEGMENTS, stride=length), slice(None))]

    for x in range(width):
        visc = 1.0 + row(eddy, (x,), 0)
        visc_first = visc
        q = jnp.ones_like(visc)
        m = jnp.ones_like(visc)
        corner = jnp.zeros_like(visc)
        first = [jnp.zeros_like(visc)] * 3
        value = None
        for j in range(length):
            if j < length - 1:
                visc_next = 1.0 + row(eddy, (x,), j + 1)
                link = 750.0 * (visc + visc_next)
                inverse = 1.0 / (q + link)
            else:
                visc_next = None
                link = None
                inverse = 1.0 / q
            left = m * inverse
            corner = corner + m * left
            source = [
                2.0 * row(velocity, (c, x), j) + row(tendency, (c, x), j) for c in range(3)
            ]
            if j > 0:
                source = [s + link_before * v for s, v in zip(source, value)]
            value = [s * inverse for s in source]
            first = [f + m * v for f, v in zip(first, value)]
            for c in range(3):
                factors[x, j, c] = value[c]
            factors[x, j, 3] = left
            if j < length - 1:
                ratio = link * inverse
                factors[x, j, 4] = ratio
                q = 1.0 + link * (q * inverse)
                m = m * ratio
                link_before = link
                visc = visc_next
            else:
                factors[x, j, 4] = inverse
        last = value
        across = left
        end = inverse
        links = 750.0 * (visc + pltpu.roll(visc_first, SEGMENTS - 1, 0))
        level, step = 0, 1
        while step < SEGMENTS:
            def other(v):
                return pltpu.roll(v, SEGMENTS - step, 0)

            link = links if step == 1 else pltpu.roll(links, SEGMENTS - (step - 1), 0)
            across_b = other(across)
            stiff = link / (1.0 + link * (end + other(corner)))
            flux = [stiff * (g - other(f)) for g, f in zip(last, first)]
            from_left = stiff * across
            from_right = stiff * across_b
            for c in range(3):
                tree[x, level, c] = flux[c]
            tree[x, level, 3] = from_left
            tree[x, level, 4] = from_right
            first = [f - across * t for f, t in zip(first, flux)]
            last = [other(g) + across_b * t for g, t in zip(last, flux)]
            corner = corner - across * from_left
            end = other(end) - across_b * from_right
            across = from_left * across_b
            level, step = level + 1, step * 2
        rows_out = [*first, *last, corner, across, end, visc_first]
        for i, v in enumerate(rows_out):
            reduced[i * width + x : i * width + x + 1, :] = v[0:1, :]
        i = len(rows_out)
        reduced[i * width + x : i * width + x + 1, :] = visc[SEGMENTS - 1 :, :]
    write.wait()


def partner(i, step, count):
    if count & (count - 1) == 0:
        return i ^ step
    return (i - step + count) % count


def finish_kernel(devices, position, factors, tree, velocity, *rest):
    reduced, (result, gathered, fluxes, out, sent) = rest[:devices], rest[devices:]
    width, length = factors.shape[:2]
    here = position[0]
    for step in range(devices):
        gathered[partner(here, step, devices)] = reduced[step][...]

    def part(device, i):
        return gathered[device, i * width : (i + 1) * width, :]

    ratios, values = [], []
    for i in range(devices + 1):
        if i == 0:
            link = 750.0 * part(0, 9)
            total = part(0, 6)
            source = [-part(0, c) for c in range(3)]
        elif i == devices:
            link = 750.0 * part(i - 1, 10)
            total = part(i - 1, 8)
            source = [part(i - 1, 3 + c) for c in range(3)]
        else:
            link = 750.0 * (part(i - 1, 10) + part(i, 9))
            total = part(i - 1, 8) + part(i, 6)
            source = [part(i - 1, 3 + c) - part(i, c) for c in range(3)]
        pivot = 1.0 + link * total
        if i > 0:
            before = part(i - 1, 7)
            pivot = pivot - link * before * ratios[-1]
            source = [s + before * v for s, v in zip(source, values[-1])]
        scale = link / pivot
        values.append([scale * s for s in source])
        if i < devices:
            ratios.append(scale * part(i, 7))
    flux = values[devices]
    for i in range(devices, -1, -1):
        if i < devices:
            flux = [v + ratios[i] * f for v, f in zip(values[i], flux)]
        for c in range(3):
            fluxes[i, c * width : (c + 1) * width, :] = flux[c]

    sublane = lax.broadcasted_iota(jnp.int32, (SEGMENTS, LANES), 0)
    levels = tree.shape[1]
    writes = []
    for c in range(3):
        for x in range(width):
            r = c * width + x
            left = jnp.broadcast_to(fluxes[here, r : r + 1, :], (SEGMENTS, LANES))
            right = -jnp.broadcast_to(fluxes[here + 1, r : r + 1, :], (SEGMENTS, LANES))
            for level in range(levels - 1, -1, -1):
                step = 2**level
                through = tree[x, level, c] + tree[x, level, 3] * left - tree[x, level, 4] * right
                second = lax.rem(sublane, 2 * step) == step
                left = jnp.where(second, pltpu.roll(through, step, 0), left)
                right = jnp.where(second, pltpu.roll(right, step, 0), -through)
            value = right
            for j in range(length - 1, -1, -1):
                value = (factors[x, j, c] + factors[x, j, 3] * left) + factors[x, j, 4] * value
                rows = pl.ds(j, SEGMENTS, stride=length)
                out[c, x, rows, :] = value - velocity[c, x, rows, :]
            writes.append(pltpu.make_async_copy(out.at[c, x], result.at[c, x], sent.at[r]))
            writes[-1].start()
    for write in writes:
        write.wait()


def in_vmem(count):
    return [pl.BlockSpec(memory_space=pltpu.VMEM)] * count


def in_hbm(count):
    return [pl.BlockSpec(memory_space=pltpu.HBM)] * count


def in_smem(count):
    return [pl.BlockSpec(memory_space=pltpu.SMEM)] * count


def params():
    return pltpu.CompilerParams(vmem_limit_bytes=VMEM_BYTES)


def body(velocity, tendency):
    _, width, cells, lanes = velocity.shape
    nz_parts = lax.axis_size("gz")
    count = lax.axis_size("gx") * nz_parts
    walls = lax.axis_size("gy")
    rows = cells // count
    nx = lax.axis_size("gx") * width
    padded = 16 + aligned(rows)
    f32 = jnp.float32

    planes = 3 * width
    depth = aligned(planes * rows + 2 * aligned(planes))
    position = lax.axis_index("gy").astype(jnp.int32).reshape(1)
    parity = lax.rem(position, 2)
    chunks = pl.pallas_call(
        functools.partial(pack_kernel, rows),
        out_shape=jax.ShapeDtypeStruct((count, depth, lanes), f32),
        in_specs=in_smem(1) + in_vmem(1),
        out_specs=pl.BlockSpec(memory_space=pltpu.VMEM),
        compiler_params=params(),
        name="pack",
    )(parity, velocity)
    recv = lax.all_to_all(chunks, ("gx", "gz"), split_axis=0, concat_axis=0, tiled=True)
    slot = lax.slice_in_dim(recv, planes * rows, planes * rows + aligned(planes), axis=1)
    swapped = lax.ppermute(slot, ("gy", "gx", "gz"), swap_pairs(walls, count))
    rank = lax.axis_index(("gx", "gz")).astype(jnp.int32).reshape(1)
    chunk_shape = jax.ShapeDtypeStruct((count, width, rows, lanes), f32)
    cells_here = nx * nz_parts * rows * lanes
    provisional = pl.pallas_call(
        functools.partial(germano_kernel, nz_parts, width, rows),
        out_shape=chunk_shape,
        in_specs=in_smem(2) + in_vmem(1),
        out_specs=pl.BlockSpec(memory_space=pltpu.VMEM),
        scratch_shapes=[
            pltpu.VMEM((3, nx, nz_parts, padded, lanes), f32),
            pltpu.VMEM((3, nx, nz_parts, padded, lanes), f32),
            pltpu.VMEM((3, nx, nz_parts, 8, lanes), f32),
            pltpu.VMEM((nx, nz_parts, rows, lanes), f32),
            pltpu.VMEM((15, nx, nz_parts, rows, lanes), f32),
        ],
        compiler_params=params(),
        cost_estimate=pl.CostEstimate(
            flops=300 * cells_here, bytes_accessed=16 * cells_here, transcendentals=2 * cells_here
        ),
        name="germano",
    )(rank, parity, recv)
    eddy_chunks = pl.pallas_call(
        functools.partial(edge_kernel, nz_parts, width, rows, walls),
        out_shape=chunk_shape,
        in_specs=in_smem(2) + in_vmem(3),
        out_specs=pl.BlockSpec(memory_space=pltpu.VMEM),
        scratch_shapes=[pltpu.VMEM((3, 3, nx, nz_parts * lanes), f32)],
        input_output_aliases={4: 0},
        compiler_params=params(),
        name="edge",
    )(rank, position, recv, swapped, provisional)
    back = lax.all_to_all(eddy_chunks, ("gx", "gz"), split_axis=0, concat_axis=0, tiled=True)

    length = cells // SEGMENTS
    levels = SEGMENTS.bit_length() - 1
    packed = aligned(11 * width)
    eddy, reduced, factors, tree = pl.pallas_call(
        sweep_kernel,
        out_shape=(
            jax.ShapeDtypeStruct((width, cells, lanes), f32),
            jax.ShapeDtypeStruct((packed, lanes), f32),
            jax.ShapeDtypeStruct((width, length, 5, SEGMENTS, lanes), f32),
            jax.ShapeDtypeStruct((width, levels, 5, SEGMENTS, lanes), f32),
        ),
        in_specs=in_smem(1) + in_vmem(3),
        out_specs=tuple(in_hbm(1) + in_vmem(3)),
        scratch_shapes=[pltpu.VMEM((width, cells, lanes), f32), pltpu.SemaphoreType.DMA],
        compiler_params=params(),
        name="sweep",
    )(parity, back, velocity, tendency)

    others = [
        lax.ppermute(reduced, "gy", [(partner(i, step, walls), i) for i in range(walls)])
        for step in range(1, walls)
    ]
    new_velocity = pl.pallas_call(
        functools.partial(finish_kernel, walls),
        out_shape=jax.ShapeDtypeStruct(velocity.shape, f32),
        in_specs=in_smem(1) + in_vmem(3 + walls),
        out_specs=in_hbm(1)[0],
        scratch_shapes=[
            pltpu.VMEM((walls, packed, lanes), f32),
            pltpu.VMEM((walls + 1, aligned(3 * width), lanes), f32),
            pltpu.VMEM(velocity.shape, f32),
            pltpu.SemaphoreType.DMA((planes,)),
        ],
        compiler_params=params(),
        name="finish",
    )(position, factors, tree, velocity, reduced, *others)
    return (new_velocity, eddy)


def solution(mesh):
    return jax.shard_map(
        body,
        mesh=mesh,
        in_specs=(P(None, "gx", "gy", "gz"), P(None, "gx", "gy", "gz")),
        out_specs=(P(None, "gx", "gy", "gz"), P("gx", "gy", "gz")),
        check_vma=False,
    )
```

```python
import functools

import jax
import jax.numpy as jnp
from jax import lax
from jax.experimental import pallas as pl
from jax.experimental.pallas import tpu as pltpu
from jax.sharding import PartitionSpec as P

LANES = 128
SEGMENTS = 8
VMEM_BYTES = 24 * 2**20


def strain_parts(grad_x, grad_y, grad_z):
    return (
        grad_x[0],
        grad_y[1],
        grad_z[2],
        grad_y[0] + grad_x[1],
        grad_z[0] + grad_x[2],
        grad_z[1] + grad_y[2],
    )


def strain_size(parts):
    diagonal = parts[0] * parts[0] + parts[1] * parts[1] + parts[2] * parts[2]
    mixed = parts[3] * parts[3] + parts[4] * parts[4] + parts[5] * parts[5]
    return jnp.sqrt(0.5 * diagonal + 0.25 * mixed)


def lane_of(shape):
    return lax.broadcasted_iota(jnp.int32, shape, len(shape) - 1)


def picked(f, lanes):
    return jnp.take_along_axis(f, lanes, axis=1)


def to_phases(blocks):
    count = len(blocks)
    if count == 1:
        return blocks
    lanes = blocks[0].shape[1]
    phases = []
    for j in range(count):
        z = lane_of(blocks[0].shape) * count + j
        phase = picked(blocks[0], lax.rem(z, lanes))
        for b in range(1, count):
            phase = jnp.where(z >= b * lanes, picked(blocks[b], lax.rem(z, lanes)), phase)
        phases.append(phase)
    return phases


def to_blocks(phases):
    count = len(phases)
    if count == 1:
        return phases
    lanes = phases[0].shape[1]
    blocks = []
    for b in range(count):
        z = lane_of(phases[0].shape) + b * lanes
        block = picked(phases[0], lax.div(z, count))
        for j in range(1, count):
            block = jnp.where(lax.rem(z, count) == j, picked(phases[j], lax.div(z, count)), block)
        blocks.append(block)
    return blocks


def after(phases):
    return [*phases[1:], pltpu.roll(phases[0], phases[0].shape[1] - 1, 1)]


def before(phases):
    return [pltpu.roll(phases[-1], 1, 1), *phases[:-1]]


def smooth_z(phases, up=None):
    sums = [f + u for f, u in zip(phases, after(phases) if up is None else up)]
    return [f + d for f, d in zip(sums, before(sums))]


def smooth_pair(a, b, c, d):
    middle = b + c
    return (a + b) + middle, middle + (c + d)


def products(v):
    return (v[0] * v[0], v[1] * v[1], v[2] * v[2], v[0] * v[1], v[0] * v[2], v[1] * v[2])


def outer_ranks(count):
    return (count - 1, count - 3)


def places(parity, count):
    outer = outer_ranks(count)
    inner = iter(range(1, count - 1))
    return [
        (0 if outer[parity] == rank else count - 1) if rank in outer else next(inner)
        for rank in range(count)
    ]


def swap_pairs(walls, count):
    odd, even = outer_ranks(count)
    spare = count - 5
    partners = {}

    def join(a, b):
        partners[a], partners[b] = b, a

    def join_walls(rank, first):
        for wall in range(first, walls - 1, 2):
            join((wall, rank), (wall + 1, rank))

    join_walls(even, 0)
    join_walls(odd, 1)
    join_walls(spare, 1)
    join((0, odd), (0, spare))
    if walls % 2 == 0:
        join((walls - 1, odd), (walls - 1, spare))
    others = [r for r in range(count) if r not in (odd, even, spare)]
    for core in range(2):
        ranks = [r for r in others if r % 2 == core]
        half = len(ranks) // 2
        for wall in range(walls):
            for a, b in zip(ranks[:half], ranks[half : 2 * half]):
                join((wall, a), (wall, b))
        for rank in ranks[2 * half :]:
            join_walls(rank, 0)
    return [
        (wall * count + rank, to[0] * count + to[1])
        for wall in range(walls)
        for rank in range(count)
        for to in [partners.get((wall, rank), (wall, rank))]
    ]


def by_parity(parity, count, fill):
    outer = outer_ranks(count)
    for rank, place in enumerate(places(0, count)):
        if rank not in outer:
            fill(rank, place)
    for turn in range(2):

        @pl.when(parity[0] == turn)
        def _():
            for rank in outer:
                fill(rank, places(turn, count)[rank])


def aligned(n):
    return -(-n // 8) * 8


def pack_kernel(rows, parity, velocity, out):
    _, width, cells, _ = velocity.shape
    count, depth, lanes = out.shape
    planes = 3 * width
    slots = planes * rows

    def fill(rank, place):
        first = place * rows
        beside = [first - 1, first + rows]
        if place == 0:
            beside = [first, first + rows]
        if place == count - 1:
            beside = [first + rows - 1, first - 1]
        for i in range(planes):
            c, x = divmod(i, width)
            out[rank, i * rows : (i + 1) * rows, :] = velocity[c, x, first : first + rows, :]
            for slot, row in enumerate(beside):
                at = slots + slot * aligned(planes) + i
                out[rank, at : at + 1, :] = velocity[c, x, row : row + 1, :]

    by_parity(parity, count, fill)
    blank = aligned(planes) - planes
    for rank in range(count):
        for slot in range(2):
            at = slots + slot * aligned(planes) + planes
            out[rank, at : at + blank, :] = jnp.zeros((blank, lanes), jnp.float32)
        at = slots + 2 * aligned(planes)
        if at < depth:
            out[rank, at:, :] = jnp.zeros((depth - at, lanes), jnp.float32)


def outer_sides(rank, parity, count):
    outer = outer_ranks(count)
    even = parity[0] == 0
    bottom = rank[0] == jnp.where(even, outer[0], outer[1])
    top = rank[0] == jnp.where(even, outer[1], outer[0])
    return bottom, top


def edge_kernel(nz_parts, width, rows, walls, rank, position, recv, swapped, given, out, vel):
    count, _, lanes = recv.shape
    planes = 3 * width
    nx = (count // nz_parts) * width
    nz = nz_parts * lanes
    bottom, top = outer_sides(rank, [lax.rem(position[0], 2)], count)
    at_wall = jnp.logical_or(
        jnp.logical_and(bottom, position[0] == 0), jnp.logical_and(top, position[0] == walls - 1)
    )

    def rows_of(k, i):
        first = i * rows
        own = [recv[k, first + j : first + j + 1, :] for j in (0, 1, rows - 2, rows - 1)]
        far = jnp.where(at_wall, 0.0, swapped[k, i : i + 1, :])
        return (
            jnp.where(bottom, far, own[2]),
            jnp.where(bottom, own[0], own[3]),
            jnp.where(bottom, own[1], far),
        )

    def roll_x(f, shift):
        return pltpu.roll(f, shift % nx, 0)

    def roll_z(f, shift):
        return pltpu.roll(f, shift % nz, 1)

    def smooth_x(f):
        return (roll_x(f, 1) + roll_x(f, -1)) + 2.0 * f

    def smooth(f):
        f = smooth_x(f)
        return (roll_z(f, 1) + roll_z(f, -1)) + 2.0 * f

    def slopes(below, centre, above):
        return strain_parts(
            [roll_x(f, -1) - roll_x(f, 1) for f in centre],
            [a - b for a, b in zip(above, below)],
            [roll_z(f, -1) - roll_z(f, 1) for f in centre],
        )

    @pl.when(jnp.logical_or(bottom, top))
    def _():
        for k in range(count):
            x0, zb = (k // nz_parts) * width, k % nz_parts
            for i in range(planes):
                c, x = divmod(i, width)
                for j, row in enumerate(rows_of(k, i)):
                    vel[j, c, x0 + x : x0 + x + 1, zb * lanes : (zb + 1) * lanes] = row
        u = [[vel[j, c] for c in range(3)] for j in range(3)]
        v = [[smooth(f) for f in row] for row in u]
        strain = slopes(*u)
        size = strain_size(strain)
        mean_strain = slopes(*v)
        mean_size = 0.25 * strain_size(mean_strain)
        scaled = [0.0625 * f for f in v[1]]
        pairs = [v[1][i] * scaled[j] for i, j in ((0, 0), (1, 1), (2, 2), (0, 1), (0, 2), (1, 2))]
        leonard = [smooth(p) - q for p, q in zip(products(u[1]), pairs)]
        model = [smooth(size * s) - mean_size * f for s, f in zip(strain, mean_strain)]
        lm, mm = contracted(leonard, model)
        coefficient = coefficient_of(
            *(jnp.sum(f, axis=(0, 1), keepdims=True) for f in (lm, mm)), nx * nz
        )
        eddy = coefficient * size

        def put(at):
            for k in range(count):
                x0, zb = (k // nz_parts) * width, k % nz_parts
                for x in range(width):
                    out[k, x, at : at + 1, :] = eddy[x0 + x : x0 + x + 1, zb * lanes : (zb + 1) * lanes]

        pl.when(bottom)(lambda: put(0))
        pl.when(top)(lambda: put(rows - 1))


def contracted(leonard, model):
    lm = mm = None
    for i in range(6):
        square = model[i] * model[i] if i < 3 else (0.5 * model[i]) * model[i]
        product = leonard[i] * model[i]
        lm = product if lm is None else lm + product
        mm = square if mm is None else mm + square
    return lm, mm


def coefficient_of(plane_lm, plane_mm, cells):
    scale = 1.0 / (256.0 * cells)
    return jnp.maximum(plane_lm * scale / (plane_mm * scale + 1e-06), 0.0)


def germano_kernel(nz_parts, width, rows, rank, parity, recv, out, vel, filt, ends, mag, part):
    count, _, lanes = recv.shape
    planes = 3 * width
    _, top = outer_sides(rank, parity, count)
    nx = (count // nz_parts) * width
    nz = nz_parts * lanes
    phases = range(nz_parts)
    lead = 8
    tile = rows
    tiles = [lead + t for t in range(0, rows, tile)]

    for c in range(3):
        for x in range(nx):
            i = c * width + x % width
            ranks = [x // width * nz_parts + zb for zb in phases]
            for t in tiles:
                first = i * rows + t - lead
                blocks = [recv[k, first : first + tile, :] for k in ranks]
                for j, f in enumerate(to_phases(blocks)):
                    vel[c, x, j, t : t + tile, :] = f
            for zb, k in enumerate(ranks):
                slots = planes * rows + i
                near = recv[k, slots : slots + 1, :]
                slots += aligned(planes)
                other = recv[k, slots : slots + 1, :]
                ends[c, x, zb, 0:1, :] = jnp.where(top, other, near)
                ends[c, x, zb, 1:2, :] = other
            for j, f in enumerate(to_phases([ends[c, x, zb] for zb in phases])):
                ends[c, x, j] = f
                vel[c, x, j, lead - 1 : lead, :] = f[0:1, :]
                vel[c, x, j, lead + rows : lead + rows + 1, :] = f[1:2, :]

    for x in range(nx):
        left, right = (x - 1) % nx, (x + 1) % nx
        for t in tiles:
            at = slice(t, t + tile)
            lower, upper = slice(t - 1, t - 1 + tile), slice(t + 1, t + 1 + tile)
            own = slice(t - lead, t - lead + tile)
            centre = [[vel[c, x, j, at, :] for j in phases] for c in range(3)]
            grad_x = [[vel[c, right, j, at, :] - vel[c, left, j, at, :] for j in phases] for c in range(3)]
            grad_y = [[vel[c, x, j, upper, :] - vel[c, x, j, lower, :] for j in phases] for c in range(3)]
            grad_z = []
            for c in range(3):
                up, down = after(centre[c]), before(centre[c])
                grad_z.append([u - d for u, d in zip(up, down)])
                for j, f in enumerate(smooth_z(centre[c], up)):
                    part[c, x, j, own, :] = f
            strain = [
                strain_parts(*([g[c][j] for c in range(3)] for g in (grad_x, grad_y, grad_z)))
                for j in phases
            ]
            size = [strain_size(s) for s in strain]
            for j in phases:
                mag[x, j, own, :] = size[j]
            pairs = [products([centre[c][j] for c in range(3)]) for j in phases]
            for i in range(6):
                for base, fields in (
                    (3, [pairs[j][i] for j in phases]),
                    (9, [size[j] * strain[j][i] for j in phases]),
                ):
                    for j, f in enumerate(smooth_z(fields)):
                        part[base + i, x, j, own, :] = f

    for c in range(3):
        rims = [smooth_z([ends[c, x, j] for j in phases]) for x in range(nx)]
        for x in range(0, nx, 2):
            around = [(x - 1) % nx, x, x + 1, (x + 2) % nx]
            for j in phases:
                for at, rim in zip(around[1:3], smooth_pair(*(rims[a][j] for a in around))):
                    filt[c, at, j, lead - 1 : lead, :] = rim[0:1, :]
                    filt[c, at, j, lead + rows : lead + rows + 1, :] = rim[1:2, :]
                for t in tiles:
                    own = slice(t - lead, t - lead + tile)
                    pair = smooth_pair(*(part[c, a, j, own, :] for a in around))
                    for at, f in zip(around[1:3], pair):
                        filt[c, at, j, t : t + tile, :] = f

    sums = [[None, None] for _ in tiles]
    for x in range(0, nx, 2):
        around = [(x - 1) % nx, x, x + 1, (x + 2) % nx]
        for n, t in enumerate(tiles):
            lower, upper = slice(t - 1, t - 1 + tile), slice(t + 1, t + 1 + tile)
            own = slice(t - lead, t - lead + tile)
            mean = [[[filt[c, a, j, t : t + tile, :] for j in phases] for a in around] for c in range(3)]
            slopes_z = [
                [[u - d for u, d in zip(after(m), before(m))] for m in mean[c][1:3]] for c in range(3)
            ]
            for j in phases:
                leonard = [smooth_pair(*(part[3 + i, a, j, own, :] for a in around)) for i in range(6)]
                scaled = [smooth_pair(*(part[9 + i, a, j, own, :] for a in around)) for i in range(6)]
                for w in range(2):
                    at = around[1 + w]
                    grad_x = [mean[c][2 + w][j] - mean[c][w][j] for c in range(3)]
                    grad_y = [filt[c, at, j, upper, :] - filt[c, at, j, lower, :] for c in range(3)]
                    strain = strain_parts(grad_x, grad_y, [slopes_z[c][w][j] for c in range(3)])
                    size = 0.25 * strain_size(strain)
                    v = [mean[c][1 + w][j] for c in range(3)]
                    q = [0.0625 * f for f in v]
                    pairs = [v[a] * q[b] for a, b in ((0, 0), (1, 1), (2, 2), (0, 1), (0, 2), (1, 2))]
                    totals = contracted(
                        [leonard[i][w] - pairs[i] for i in range(6)],
                        [scaled[i][w] - size * strain[i] for i in range(6)],
                    )
                    sums[n] = [f if s is None else s + f for s, f in zip(sums[n], totals)]

    for n, t in enumerate(tiles):
        own = slice(t - lead, t - lead + tile)
        coefficient = coefficient_of(
            *(jnp.sum(total, axis=1, keepdims=True) for total in sums[n]), nx * nz
        )
        for x in range(nx):
            blocks = to_blocks([coefficient * mag[x, j, own, :] for j in phases])
            for zb, f in enumerate(blocks):
                out[x // width * nz_parts + zb, x % width, own, :] = f


def sweep_kernel(parity, back, velocity, tendency, eddy_out, reduced, factors, tree, eddy, sent):
    count, width, rows, _ = back.shape
    length = count * rows // SEGMENTS

    def fill(rank, place):
        for x in range(width):
            eddy[x, place * rows : (place + 1) * rows, :] = back[rank, x]

    by_parity(parity, count, fill)
    write = pltpu.make_async_copy(eddy, eddy_out, sent)
    write.start()

    def row(ref, index, j):
        return ref[(*index, pl.ds(j, SEGMENTS, stride=length), slice(None))]

    for x in range(width):
        visc = 1.0 + row(eddy, (x,), 0)
        visc_first = visc
        q = jnp.ones_like(visc)
        m = jnp.ones_like(visc)
        corner = jnp.zeros_like(visc)
        first = [jnp.zeros_like(visc)] * 3
        value = None
        for j in range(length):
            if j < length - 1:
                visc_next = 1.0 + row(eddy, (x,), j + 1)
                link = 750.0 * (visc + visc_next)
                inverse = 1.0 / (q + link)
            else:
                visc_next = None
                link = None
                inverse = 1.0 / q
            left = m * inverse
            corner = corner + m * left
            source = [
                2.0 * row(velocity, (c, x), j) + row(tendency, (c, x), j) for c in range(3)
            ]
            if j > 0:
                source = [s + link_before * v for s, v in zip(source, value)]
            value = [s * inverse for s in source]
            first = [f + m * v for f, v in zip(first, value)]
            for c in range(3):
                factors[x, j, c] = value[c]
            factors[x, j, 3] = left
            if j < length - 1:
                ratio = link * inverse
                factors[x, j, 4] = ratio
                q = 1.0 + link * (q * inverse)
                m = m * ratio
                link_before = link
                visc = visc_next
            else:
                factors[x, j, 4] = inverse
        last = value
        across = left
        end = inverse
        links = 750.0 * (visc + pltpu.roll(visc_first, SEGMENTS - 1, 0))
        level, step = 0, 1
        while step < SEGMENTS:
            def other(v):
                return pltpu.roll(v, SEGMENTS - step, 0)

            link = links if step == 1 else pltpu.roll(links, SEGMENTS - (step - 1), 0)
            across_b = other(across)
            stiff = link / (1.0 + link * (end + other(corner)))
            flux = [stiff * (g - other(f)) for g, f in zip(last, first)]
            from_left = stiff * across
            from_right = stiff * across_b
            for c in range(3):
                tree[x, level, c] = flux[c]
            tree[x, level, 3] = from_left
            tree[x, level, 4] = from_right
            first = [f - across * t for f, t in zip(first, flux)]
            last = [other(g) + across_b * t for g, t in zip(last, flux)]
            corner = corner - across * from_left
            end = other(end) - across_b * from_right
            across = from_left * across_b
            level, step = level + 1, step * 2
        rows_out = [*first, *last, corner, across, end, visc_first]
        for i, v in enumerate(rows_out):
            reduced[i * width + x : i * width + x + 1, :] = v[0:1, :]
        i = len(rows_out)
        reduced[i * width + x : i * width + x + 1, :] = visc[SEGMENTS - 1 :, :]
    write.wait()


def partner(i, step, count):
    if count & (count - 1) == 0:
        return i ^ step
    return (i - step + count) % count


def finish_kernel(devices, position, factors, tree, velocity, *rest):
    reduced, (result, gathered, fluxes, out, sent) = rest[:devices], rest[devices:]
    width, length = factors.shape[:2]
    here = position[0]
    for step in range(devices):
        gathered[partner(here, step, devices)] = reduced[step][...]

    def part(device, i):
        return gathered[device, i * width : (i + 1) * width, :]

    ratios, values = [], []
    for i in range(devices + 1):
        if i == 0:
            link = 750.0 * part(0, 9)
            total = part(0, 6)
            source = [-part(0, c) for c in range(3)]
        elif i == devices:
            link = 750.0 * part(i - 1, 10)
            total = part(i - 1, 8)
            source = [part(i - 1, 3 + c) for c in range(3)]
        else:
            link = 750.0 * (part(i - 1, 10) + part(i, 9))
            total = part(i - 1, 8) + part(i, 6)
            source = [part(i - 1, 3 + c) - part(i, c) for c in range(3)]
        pivot = 1.0 + link * total
        if i > 0:
            before = part(i - 1, 7)
            pivot = pivot - link * before * ratios[-1]
            source = [s + before * v for s, v in zip(source, values[-1])]
        scale = link / pivot
        values.append([scale * s for s in source])
        if i < devices:
            ratios.append(scale * part(i, 7))
    flux = values[devices]
    for i in range(devices, -1, -1):
        if i < devices:
            flux = [v + ratios[i] * f for v, f in zip(values[i], flux)]
        for c in range(3):
            fluxes[i, c * width : (c + 1) * width, :] = flux[c]

    sublane = lax.broadcasted_iota(jnp.int32, (SEGMENTS, LANES), 0)
    levels = tree.shape[1]
    writes = []
    for c in range(3):
        for x in range(width):
            r = c * width + x
            left = jnp.broadcast_to(fluxes[here, r : r + 1, :], (SEGMENTS, LANES))
            right = -jnp.broadcast_to(fluxes[here + 1, r : r + 1, :], (SEGMENTS, LANES))
            for level in range(levels - 1, -1, -1):
                step = 2**level
                through = tree[x, level, c] + tree[x, level, 3] * left - tree[x, level, 4] * right
                second = lax.rem(sublane, 2 * step) == step
                left = jnp.where(second, pltpu.roll(through, step, 0), left)
                right = jnp.where(second, pltpu.roll(right, step, 0), -through)
            value = right
            for j in range(length - 1, -1, -1):
                value = (factors[x, j, c] + factors[x, j, 3] * left) + factors[x, j, 4] * value
                rows = pl.ds(j, SEGMENTS, stride=length)
                out[c, x, rows, :] = value - velocity[c, x, rows, :]
            writes.append(pltpu.make_async_copy(out.at[c, x], result.at[c, x], sent.at[r]))
            writes[-1].start()
    for write in writes:
        write.wait()


def in_vmem(count):
    return [pl.BlockSpec(memory_space=pltpu.VMEM)] * count


def in_hbm(count):
    return [pl.BlockSpec(memory_space=pltpu.HBM)] * count


def in_smem(count):
    return [pl.BlockSpec(memory_space=pltpu.SMEM)] * count


def params():
    return pltpu.CompilerParams(vmem_limit_bytes=VMEM_BYTES)


def body(velocity, tendency):
    _, width, cells, lanes = velocity.shape
    nz_parts = lax.axis_size("gz")
    count = lax.axis_size("gx") * nz_parts
    walls = lax.axis_size("gy")
    rows = cells // count
    nx = lax.axis_size("gx") * width
    padded = 16 + aligned(rows)
    f32 = jnp.float32

    planes = 3 * width
    depth = aligned(planes * rows + 2 * aligned(planes))
    position = lax.axis_index("gy").astype(jnp.int32).reshape(1)
    parity = lax.rem(position, 2)
    chunks = pl.pallas_call(
        functools.partial(pack_kernel, rows),
        out_shape=jax.ShapeDtypeStruct((count, depth, lanes), f32),
        in_specs=in_smem(1) + in_vmem(1),
        out_specs=pl.BlockSpec(memory_space=pltpu.VMEM),
        compiler_params=params(),
        name="pack",
    )(parity, velocity)
    recv = lax.all_to_all(chunks, ("gx", "gz"), split_axis=0, concat_axis=0, tiled=True)
    slot = lax.slice_in_dim(recv, planes * rows, planes * rows + aligned(planes), axis=1)
    swapped = lax.ppermute(slot, ("gy", "gx", "gz"), swap_pairs(walls, count))
    rank = lax.axis_index(("gx", "gz")).astype(jnp.int32).reshape(1)
    chunk_shape = jax.ShapeDtypeStruct((count, width, rows, lanes), f32)
    cells_here = nx * nz_parts * rows * lanes
    provisional = pl.pallas_call(
        functools.partial(germano_kernel, nz_parts, width, rows),
        out_shape=chunk_shape,
        in_specs=in_smem(2) + in_vmem(1),
        out_specs=pl.BlockSpec(memory_space=pltpu.VMEM),
        scratch_shapes=[
            pltpu.VMEM((3, nx, nz_parts, padded, lanes), f32),
            pltpu.VMEM((3, nx, nz_parts, padded, lanes), f32),
            pltpu.VMEM((3, nx, nz_parts, 8, lanes), f32),
            pltpu.VMEM((nx, nz_parts, rows, lanes), f32),
            pltpu.VMEM((15, nx, nz_parts, rows, lanes), f32),
        ],
        compiler_params=params(),
        cost_estimate=pl.CostEstimate(
            flops=300 * cells_here, bytes_accessed=16 * cells_here, transcendentals=2 * cells_here
        ),
        name="germano",
    )(rank, parity, recv)
    eddy_chunks = pl.pallas_call(
        functools.partial(edge_kernel, nz_parts, width, rows, walls),
        out_shape=chunk_shape,
        in_specs=in_smem(2) + in_vmem(3),
        out_specs=pl.BlockSpec(memory_space=pltpu.VMEM),
        scratch_shapes=[pltpu.VMEM((3, 3, nx, nz_parts * lanes), f32)],
        input_output_aliases={4: 0},
        compiler_params=params(),
        name="edge",
    )(rank, position, recv, swapped, provisional)
    back = lax.all_to_all(eddy_chunks, ("gx", "gz"), split_axis=0, concat_axis=0, tiled=True)

    length = cells // SEGMENTS
    levels = SEGMENTS.bit_length() - 1
    packed = aligned(11 * width)
    eddy, reduced, factors, tree = pl.pallas_call(
        sweep_kernel,
        out_shape=(
            jax.ShapeDtypeStruct((width, cells, lanes), f32),
            jax.ShapeDtypeStruct((packed, lanes), f32),
            jax.ShapeDtypeStruct((width, length, 5, SEGMENTS, lanes), f32),
            jax.ShapeDtypeStruct((width, levels, 5, SEGMENTS, lanes), f32),
        ),
        in_specs=in_smem(1) + in_vmem(3),
        out_specs=tuple(in_hbm(1) + in_vmem(3)),
        scratch_shapes=[pltpu.VMEM((width, cells, lanes), f32), pltpu.SemaphoreType.DMA],
        compiler_params=params(),
        name="sweep",
    )(parity, back, velocity, tendency)

    others = [
        lax.ppermute(reduced, "gy", [(partner(i, step, walls), i) for i in range(walls)])
        for step in range(1, walls)
    ]
    new_velocity = pl.pallas_call(
        functools.partial(finish_kernel, walls),
        out_shape=jax.ShapeDtypeStruct(velocity.shape, f32),
        in_specs=in_smem(1) + in_vmem(3 + walls),
        out_specs=in_hbm(1)[0],
        scratch_shapes=[
            pltpu.VMEM((walls, packed, lanes), f32),
            pltpu.VMEM((walls + 1, aligned(3 * width), lanes), f32),
            pltpu.VMEM(velocity.shape, f32),
            pltpu.SemaphoreType.DMA((planes,)),
        ],
        compiler_params=params(),
        name="finish",
    )(position, factors, tree, velocity, reduced, *others)
    return (new_velocity, eddy)


def solution(mesh):
    return jax.shard_map(
        body,
        mesh=mesh,
        in_specs=(P(None, "gx", "gy", "gz"), P(None, "gx", "gy", "gz")),
        out_specs=(P(None, "gx", "gy", "gz"), P("gx", "gy", "gz")),
        check_vma=False,
    )
```

```python
import functools

import jax
import jax.numpy as jnp
from jax import lax
from jax.experimental import pallas as pl
from jax.experimental.pallas import tpu as pltpu
from jax.sharding import PartitionSpec as P

LANES = 128
SEGMENTS = 8
VMEM_BYTES = 24 * 2**20


def strain_parts(grad_x, grad_y, grad_z):
    return (
        grad_x[0],
        grad_y[1],
        grad_z[2],
        grad_y[0] + grad_x[1],
        grad_z[0] + grad_x[2],
        grad_z[1] + grad_y[2],
    )


def strain_size(parts):
    diagonal = parts[0] * parts[0] + parts[1] * parts[1] + parts[2] * parts[2]
    mixed = parts[3] * parts[3] + parts[4] * parts[4] + parts[5] * parts[5]
    return jnp.sqrt(0.5 * diagonal + 0.25 * mixed)


def beside(blocks):
    count = len(blocks)
    lanes = blocks[0].shape[1]
    down = [pltpu.roll(f, 1, 1) for f in blocks]
    up = [pltpu.roll(f, lanes - 1, 1) for f in blocks]
    if count > 1:
        lane = lax.broadcasted_iota(jnp.int32, blocks[0].shape, 1)
        first, last = lane == 0, lane == lanes - 1
        down, up = (
            [jnp.where(first, down[i - 1], down[i]) for i in range(count)],
            [jnp.where(last, up[(i + 1) % count], up[i]) for i in range(count)],
        )
    return down, up


def slope_z(blocks):
    down, up = beside(blocks)
    return [u - d for u, d in zip(up, down)]


def smooth_z(blocks):
    down, up = beside(blocks)
    return [(u + d) + 2.0 * f for f, u, d in zip(blocks, up, down)]


def products(v):
    return (v[0] * v[0], v[1] * v[1], v[2] * v[2], v[0] * v[1], v[0] * v[2], v[1] * v[2])


def outer_ranks(count):
    return (count - 1, count - 3)


def places(parity, count):
    outer = outer_ranks(count)
    inner = iter(range(1, count - 1))
    return [
        (0 if outer[parity] == rank else count - 1) if rank in outer else next(inner)
        for rank in range(count)
    ]


def swap_pairs(walls, count):
    odd, even = outer_ranks(count)
    spare = count - 5
    partners = {}

    def join(a, b):
        partners[a], partners[b] = b, a

    def join_walls(rank, first):
        for wall in range(first, walls - 1, 2):
            join((wall, rank), (wall + 1, rank))

    join_walls(even, 0)
    join_walls(odd, 1)
    join_walls(spare, 1)
    join((0, odd), (0, spare))
    if walls % 2 == 0:
        join((walls - 1, odd), (walls - 1, spare))
    others = [r for r in range(count) if r not in (odd, even, spare)]
    for core in range(2):
        ranks = [r for r in others if r % 2 == core]
        half = len(ranks) // 2
        for wall in range(walls):
            for a, b in zip(ranks[:half], ranks[half : 2 * half]):
                join((wall, a), (wall, b))
        for rank in ranks[2 * half :]:
            join_walls(rank, 0)
    return [
        (wall * count + rank, to[0] * count + to[1])
        for wall in range(walls)
        for rank in range(count)
        for to in [partners.get((wall, rank), (wall, rank))]
    ]


def by_parity(parity, count, fill):
    outer = outer_ranks(count)
    for rank, place in enumerate(places(0, count)):
        if rank not in outer:
            fill(rank, place)
    for turn in range(2):

        @pl.when(parity[0] == turn)
        def _():
            for rank in outer:
                fill(rank, places(turn, count)[rank])


def aligned(n):
    return -(-n // 8) * 8


def pack_kernel(rows, parity, velocity, out):
    _, width, cells, _ = velocity.shape
    count, depth, lanes = out.shape
    planes = 3 * width
    slots = planes * rows

    def fill(rank, place):
        first = place * rows
        beside = [first - 1, first + rows]
        if place == 0:
            beside = [first, first + rows]
        if place == count - 1:
            beside = [first + rows - 1, first - 1]
        for i in range(planes):
            c, x = divmod(i, width)
            out[rank, i * rows : (i + 1) * rows, :] = velocity[c, x, first : first + rows, :]
            for slot, row in enumerate(beside):
                at = slots + slot * aligned(planes) + i
                out[rank, at : at + 1, :] = velocity[c, x, row : row + 1, :]

    by_parity(parity, count, fill)
    blank = aligned(planes) - planes
    for rank in range(count):
        for slot in range(2):
            at = slots + slot * aligned(planes) + planes
            out[rank, at : at + blank, :] = jnp.zeros((blank, lanes), jnp.float32)
        at = slots + 2 * aligned(planes)
        if at < depth:
            out[rank, at:, :] = jnp.zeros((depth - at, lanes), jnp.float32)


def outer_sides(rank, parity, count):
    outer = outer_ranks(count)
    even = parity[0] == 0
    bottom = rank[0] == jnp.where(even, outer[0], outer[1])
    top = rank[0] == jnp.where(even, outer[1], outer[0])
    return bottom, top


def edge_kernel(nz_parts, width, rows, walls, rank, position, recv, swapped, given, out, vel):
    count, _, lanes = recv.shape
    planes = 3 * width
    nx = (count // nz_parts) * width
    nz = nz_parts * lanes
    bottom, top = outer_sides(rank, [lax.rem(position[0], 2)], count)
    at_wall = jnp.logical_or(
        jnp.logical_and(bottom, position[0] == 0), jnp.logical_and(top, position[0] == walls - 1)
    )

    def rows_of(k, i):
        first = i * rows
        own = [recv[k, first + j : first + j + 1, :] for j in (0, 1, rows - 2, rows - 1)]
        far = jnp.where(at_wall, 0.0, swapped[k, i : i + 1, :])
        return (
            jnp.where(bottom, far, own[2]),
            jnp.where(bottom, own[0], own[3]),
            jnp.where(bottom, own[1], far),
        )

    def roll_x(f, shift):
        return pltpu.roll(f, shift % nx, 0)

    def roll_z(f, shift):
        return pltpu.roll(f, shift % nz, 1)

    def smooth_x(f):
        return (roll_x(f, 1) + roll_x(f, -1)) + 2.0 * f

    def smooth(f):
        f = smooth_x(f)
        return (roll_z(f, 1) + roll_z(f, -1)) + 2.0 * f

    def slopes(below, centre, above):
        return strain_parts(
            [roll_x(f, -1) - roll_x(f, 1) for f in centre],
            [a - b for a, b in zip(above, below)],
            [roll_z(f, -1) - roll_z(f, 1) for f in centre],
        )

    @pl.when(jnp.logical_or(bottom, top))
    def _():
        for k in range(count):
            x0, zb = (k // nz_parts) * width, k % nz_parts
            for i in range(planes):
                c, x = divmod(i, width)
                for j, row in enumerate(rows_of(k, i)):
                    vel[j, c, x0 + x : x0 + x + 1, zb * lanes : (zb + 1) * lanes] = row
        u = [[vel[j, c] for c in range(3)] for j in range(3)]
        v = [[smooth(f) for f in row] for row in u]
        strain = slopes(*u)
        size = strain_size(strain)
        mean_strain = slopes(*v)
        mean_size = 0.25 * strain_size(mean_strain)
        scaled = [0.0625 * f for f in v[1]]
        pairs = [v[1][i] * scaled[j] for i, j in ((0, 0), (1, 1), (2, 2), (0, 1), (0, 2), (1, 2))]
        leonard = [smooth(p) - q for p, q in zip(products(u[1]), pairs)]
        model = [smooth(size * s) - mean_size * f for s, f in zip(strain, mean_strain)]
        lm, mm = contracted(leonard, model)
        coefficient = coefficient_of(
            *(jnp.sum(f, axis=(0, 1), keepdims=True) for f in (lm, mm)), nx * nz
        )
        eddy = coefficient * size

        def put(at):
            for k in range(count):
                x0, zb = (k // nz_parts) * width, k % nz_parts
                for x in range(width):
                    out[k, x, at : at + 1, :] = eddy[x0 + x : x0 + x + 1, zb * lanes : (zb + 1) * lanes]

        pl.when(bottom)(lambda: put(0))
        pl.when(top)(lambda: put(rows - 1))


def contracted(leonard, model):
    lm = mm = None
    for i in range(6):
        square = model[i] * model[i] if i < 3 else (0.5 * model[i]) * model[i]
        product = leonard[i] * model[i]
        lm = product if lm is None else lm + product
        mm = square if mm is None else mm + square
    return lm, mm


def coefficient_of(plane_lm, plane_mm, cells):
    scale = 1.0 / (256.0 * cells)
    return jnp.maximum(plane_lm * scale / (plane_mm * scale + 1e-06), 0.0)


def germano_kernel(nz_parts, width, rows, rank, parity, recv, out, vel, filt, ends, mag, part):
    count, _, lanes = recv.shape
    planes = 3 * width
    _, top = outer_sides(rank, parity, count)
    nx = (count // nz_parts) * width
    nz = nz_parts * lanes
    blocks = range(nz_parts)
    lead = 8
    inner = slice(lead, lead + rows)
    lower = slice(lead - 1, lead - 1 + rows)
    upper = slice(lead + 1, lead + 1 + rows)
    for k in range(count):
        x0, zb = (k // nz_parts) * width, k % nz_parts
        for c in range(3):
            for x in range(width):
                i = c * width + x
                vel[c, x0 + x, zb, inner, :] = recv[k, i * rows : (i + 1) * rows, :]
                slots = planes * rows + i
                near = recv[k, slots : slots + 1, :]
                slots += aligned(planes)
                other = recv[k, slots : slots + 1, :]
                below = jnp.where(top, other, near)
                for side, (edge, at) in enumerate(((below, lead - 1), (other, lead + rows))):
                    vel[c, x0 + x, zb, at : at + 1, :] = edge
                    ends[c, x0 + x, zb, side : side + 1, :] = edge

    for x in range(nx):
        left, right = (x - 1) % nx, (x + 1) % nx
        centre = [[vel[c, x, zb, inner, :] for zb in blocks] for c in range(3)]
        grad_x = [[vel[c, right, zb, inner, :] - vel[c, left, zb, inner, :] for zb in blocks] for c in range(3)]
        grad_y = [[vel[c, x, zb, upper, :] - vel[c, x, zb, lower, :] for zb in blocks] for c in range(3)]
        grad_z = []
        for c in range(3):
            down, up = beside(centre[c])
            grad_z.append([u - d for u, d in zip(up, down)])
            for zb in blocks:
                part[c, x, zb] = (up[zb] + down[zb]) + 2.0 * centre[c][zb]
        strain = [
            strain_parts(*([g[c][zb] for c in range(3)] for g in (grad_x, grad_y, grad_z)))
            for zb in blocks
        ]
        size = [strain_size(s) for s in strain]
        for zb in blocks:
            mag[x, zb] = size[zb]
        pairs = [products([centre[c][zb] for c in range(3)]) for zb in blocks]
        for i in range(6):
            for base, fields in (
                (3, [pairs[zb][i] for zb in blocks]),
                (9, [size[zb] * strain[zb][i] for zb in blocks]),
            ):
                for zb, f in enumerate(smooth_z(fields)):
                    part[base + i, x, zb] = f

    def smooth_x(read, x):
        return (read((x - 1) % nx) + read((x + 1) % nx)) + 2.0 * read(x)

    for c in range(3):
        rims = []
        for x in range(nx):
            rims.append(smooth_z([ends[c, x, zb] for zb in blocks]))
        for x in range(nx):
            for zb in blocks:
                rim = smooth_x(lambda at: rims[at][zb], x)
                filt[c, x, zb, lead - 1 : lead, :] = rim[0:1, :]
                filt[c, x, zb, lead + rows : lead + rows + 1, :] = rim[1:2, :]
                filt[c, x, zb, inner, :] = smooth_x(lambda at: part[c, at, zb], x)

    sum_lm = sum_mm = None
    for x in range(nx):
        left, right = (x - 1) % nx, (x + 1) % nx
        mean = [[filt[c, x, zb, inner, :] for zb in blocks] for c in range(3)]
        grad_x = [[filt[c, right, zb, inner, :] - filt[c, left, zb, inner, :] for zb in blocks] for c in range(3)]
        grad_y = [[filt[c, x, zb, upper, :] - filt[c, x, zb, lower, :] for zb in blocks] for c in range(3)]
        grad_z = [slope_z(mean[c]) for c in range(3)]
        for zb in blocks:
            strain = strain_parts(*([g[c][zb] for c in range(3)] for g in (grad_x, grad_y, grad_z)))
            size = 0.25 * strain_size(strain)
            v = [mean[c][zb] for c in range(3)]
            scaled = [0.0625 * f for f in v]
            pairs = (
                v[0] * scaled[0],
                v[1] * scaled[1],
                v[2] * scaled[2],
                v[0] * scaled[1],
                v[0] * scaled[2],
                v[1] * scaled[2],
            )
            leonard = [smooth_x(lambda at: part[3 + i, at, zb], x) - pairs[i] for i in range(6)]
            model = [smooth_x(lambda at: part[9 + i, at, zb], x) - size * strain[i] for i in range(6)]
            lm, mm = contracted(leonard, model)
            sum_lm = lm if sum_lm is None else sum_lm + lm
            sum_mm = mm if sum_mm is None else sum_mm + mm

    coefficient = coefficient_of(
        *(jnp.sum(total, axis=1, keepdims=True) for total in (sum_lm, sum_mm)), nx * nz
    )
    for k in range(count):
        x0, zb = (k // nz_parts) * width, k % nz_parts
        for x in range(width):
            out[k, x] = coefficient * mag[x0 + x, zb]


def sweep_kernel(parity, back, velocity, tendency, eddy_out, reduced, factors, tree, eddy, sent):
    count, width, rows, _ = back.shape
    length = count * rows // SEGMENTS

    def fill(rank, place):
        for x in range(width):
            eddy[x, place * rows : (place + 1) * rows, :] = back[rank, x]

    by_parity(parity, count, fill)
    write = pltpu.make_async_copy(eddy, eddy_out, sent)
    write.start()

    def row(ref, index, j):
        return ref[(*index, pl.ds(j, SEGMENTS, stride=length), slice(None))]

    planes = range(width)
    last_row = length - 1
    visc = [[1.0 + row(eddy, (x,), j) for x in planes] for j in range(length)]
    links = [[750.0 * (v + w) for v, w in zip(visc[j], visc[j + 1])] for j in range(last_row)]

    over = [jnp.ones_like(v) for v in visc[0]]
    under = [jnp.ones_like(v) for v in visc[0]]
    inverses = []
    for j in range(last_row):
        inverses.append([u / (o + e * u) for o, u, e in zip(over, under, links[j])])
        steps = [o * (1.0 / e) for o, e in zip(over, links[j])]
        under, over = (
            [u + t for u, t in zip(under, steps)],
            [(o + u) + t for o, u, t in zip(over, under, steps)],
        )
    inverses.append([u / o for o, u in zip(over, under)])

    value = first = corner = left = None
    reach = [jnp.ones_like(v) for v in visc[0]]
    for j in range(length):
        inverse = inverses[j]
        before = value
        source = [[2.0 * row(velocity, (c, x), j) + row(tendency, (c, x), j) for x in planes] for c in range(3)]
        value = [[f * r for f, r in zip(source[c], inverse)] for c in range(3)]
        if j > 0:
            carry = [e * r for e, r in zip(links[j - 1], inverse)]
            value = [[v + k * w for v, k, w in zip(value[c], carry, before[c])] for c in range(3)]
        left = [m * r for m, r in zip(reach, inverse)]
        if j == 0:
            first, corner = value, left
        else:
            first = [[f + m * v for f, m, v in zip(first[c], reach, value[c])] for c in range(3)]
            corner = [a + m * v for a, m, v in zip(corner, reach, left)]
        ratio = inverse
        if j < last_row:
            ratio = [e * r for e, r in zip(links[j], inverse)]
            reach = [m * r for m, r in zip(reach, ratio)]
        for x in planes:
            for c in range(3):
                factors[x, j, c] = value[c][x]
            factors[x, j, 3] = left[x]
            factors[x, j, 4] = ratio[x]

    def other(fields, step):
        return [pltpu.roll(f, (SEGMENTS - step) % SEGMENTS, 0) if step else f for f in fields]

    last, across, end = value, left, inverse
    seams = [750.0 * (v + w) for v, w in zip(visc[last_row], other(visc[0], 1))]
    level, step = 0, 1
    while step < SEGMENTS:
        link = other(seams, step - 1)
        first_b = [other(f, step) for f in first]
        last_b = [other(f, step) for f in last]
        corner_b, end_b, across_b = other(corner, step), other(end, step), other(across, step)
        stiff = [e / (1.0 + e * (d + a)) for e, d, a in zip(link, end, corner_b)]
        flux = [[k * (g - f) for k, g, f in zip(stiff, last[c], first_b[c])] for c in range(3)]
        from_left = [k * b for k, b in zip(stiff, across)]
        from_right = [k * b for k, b in zip(stiff, across_b)]
        for x in planes:
            for c in range(3):
                tree[x, level, c] = flux[c][x]
            tree[x, level, 3] = from_left[x]
            tree[x, level, 4] = from_right[x]
        first = [[f - b * t for f, b, t in zip(first[c], across, flux[c])] for c in range(3)]
        last = [[g + b * t for g, b, t in zip(last_b[c], across_b, flux[c])] for c in range(3)]
        corner = [a - b * k for a, b, k in zip(corner, across, from_left)]
        end = [d - b * k for d, b, k in zip(end_b, across_b, from_right)]
        across = [k * b for k, b in zip(from_left, across_b)]
        level, step = level + 1, step * 2
    for x in planes:
        rows_out = [f[x][0:1, :] for f in (*first, *last, corner, across, end, visc[0])]
        rows_out.append(visc[last_row][x][SEGMENTS - 1 :, :])
        for i, v in enumerate(rows_out):
            reduced[i * width + x : i * width + x + 1, :] = v
    write.wait()


def spread_kernel(factors, tree, velocity, particular, response):
    width, length = factors.shape[:2]
    levels = tree.shape[1]
    sublane = lax.broadcasted_iota(jnp.int32, (SEGMENTS, LANES), 0)
    one, zero = (jnp.full((SEGMENTS, LANES), v, jnp.float32) for v in (1.0, 0.0))
    sides = [(c, zero, zero) for c in range(3)] + [(None, one, zero), (None, zero, one)]
    lefts = [[side[1]] * width for side in sides]
    rights = [[side[2]] * width for side in sides]
    for level in range(levels - 1, -1, -1):
        step = 2**level
        second = lax.rem(sublane, 2 * step) == step
        for n, (c, _, _) in enumerate(sides):
            for x in range(width):
                left, right = lefts[n][x], rights[n][x]
                through = tree[x, level, 3] * left - tree[x, level, 4] * right
                if c is not None:
                    through = tree[x, level, c] + through
                lefts[n][x] = jnp.where(second, pltpu.roll(through, step, 0), left)
                rights[n][x] = jnp.where(second, pltpu.roll(right, step, 0), -through)
    values = rights
    for j in range(length - 1, -1, -1):
        rows = pl.ds(j, SEGMENTS, stride=length)
        for n, (c, _, _) in enumerate(sides):
            for x in range(width):
                value = factors[x, j, 3] * lefts[n][x] + factors[x, j, 4] * values[n][x]
                if c is not None:
                    value = factors[x, j, c] + value
                    particular[c, x, rows, :] = value - velocity[c, x, rows, :]
                else:
                    response[n - 3, x, rows, :] = value
                values[n][x] = value


def partner(i, step, count):
    if count & (count - 1) == 0:
        return i ^ step
    return (i - step + count) % count


def finish_kernel(devices, position, particular, response, *rest):
    reduced, (result, gathered, fluxes, out, sent) = rest[:devices], rest[devices:]
    width = particular.shape[1]
    here = position[0]
    for step in range(devices):
        gathered[partner(here, step, devices)] = reduced[step][...]

    def part(device, i):
        return gathered[device, i * width : (i + 1) * width, :]

    ratios, values = [], []
    for i in range(devices + 1):
        if i == 0:
            link = 750.0 * part(0, 9)
            total = part(0, 6)
            source = [-part(0, c) for c in range(3)]
        elif i == devices:
            link = 750.0 * part(i - 1, 10)
            total = part(i - 1, 8)
            source = [part(i - 1, 3 + c) for c in range(3)]
        else:
            link = 750.0 * (part(i - 1, 10) + part(i, 9))
            total = part(i - 1, 8) + part(i, 6)
            source = [part(i - 1, 3 + c) - part(i, c) for c in range(3)]
        pivot = 1.0 + link * total
        if i > 0:
            before = part(i - 1, 7)
            pivot = pivot - link * before * ratios[-1]
            source = [s + before * v for s, v in zip(source, values[-1])]
        scale = link / pivot
        values.append([scale * s for s in source])
        if i < devices:
            ratios.append(scale * part(i, 7))
    flux = values[devices]
    for i in range(devices, -1, -1):
        if i < devices:
            flux = [v + ratios[i] * f for v, f in zip(values[i], flux)]
        for c in range(3):
            fluxes[i, c * width : (c + 1) * width, :] = flux[c]

    writes = []
    for c in range(3):
        for x in range(width):
            r = c * width + x
            left, right = fluxes[here, r : r + 1, :], fluxes[here + 1, r : r + 1, :]
            out[c, x] = particular[c, x] + (response[0, x] * left - response[1, x] * right)
            writes.append(pltpu.make_async_copy(out.at[c, x], result.at[c, x], sent.at[r]))
            writes[-1].start()
    for write in writes:
        write.wait()


def in_vmem(count):
    return [pl.BlockSpec(memory_space=pltpu.VMEM)] * count


def in_hbm(count):
    return [pl.BlockSpec(memory_space=pltpu.HBM)] * count


def in_smem(count):
    return [pl.BlockSpec(memory_space=pltpu.SMEM)] * count


def params():
    return pltpu.CompilerParams(vmem_limit_bytes=VMEM_BYTES)


def body(velocity, tendency):
    _, width, cells, lanes = velocity.shape
    nz_parts = lax.axis_size("gz")
    count = lax.axis_size("gx") * nz_parts
    walls = lax.axis_size("gy")
    rows = cells // count
    nx = lax.axis_size("gx") * width
    padded = 16 + aligned(rows)
    f32 = jnp.float32

    planes = 3 * width
    depth = aligned(planes * rows + 2 * aligned(planes))
    position = lax.axis_index("gy").astype(jnp.int32).reshape(1)
    parity = lax.rem(position, 2)
    chunks = pl.pallas_call(
        functools.partial(pack_kernel, rows),
        out_shape=jax.ShapeDtypeStruct((count, depth, lanes), f32),
        in_specs=in_smem(1) + in_vmem(1),
        out_specs=pl.BlockSpec(memory_space=pltpu.VMEM),
        compiler_params=params(),
        name="pack",
    )(parity, velocity)
    recv = lax.all_to_all(chunks, ("gx", "gz"), split_axis=0, concat_axis=0, tiled=True)
    slot = lax.slice_in_dim(recv, planes * rows, planes * rows + aligned(planes), axis=1)
    swapped = lax.ppermute(slot, ("gy", "gx", "gz"), swap_pairs(walls, count))
    rank = lax.axis_index(("gx", "gz")).astype(jnp.int32).reshape(1)
    chunk_shape = jax.ShapeDtypeStruct((count, width, rows, lanes), f32)
    cells_here = nx * nz_parts * rows * lanes
    provisional = pl.pallas_call(
        functools.partial(germano_kernel, nz_parts, width, rows),
        out_shape=chunk_shape,
        in_specs=in_smem(2) + in_vmem(1),
        out_specs=pl.BlockSpec(memory_space=pltpu.VMEM),
        scratch_shapes=[
            pltpu.VMEM((3, nx, nz_parts, padded, lanes), f32),
            pltpu.VMEM((3, nx, nz_parts, padded, lanes), f32),
            pltpu.VMEM((3, nx, nz_parts, 8, lanes), f32),
            pltpu.VMEM((nx, nz_parts, rows, lanes), f32),
            pltpu.VMEM((15, nx, nz_parts, rows, lanes), f32),
        ],
        compiler_params=params(),
        cost_estimate=pl.CostEstimate(
            flops=300 * cells_here, bytes_accessed=16 * cells_here, transcendentals=2 * cells_here
        ),
        name="germano",
    )(rank, parity, recv)
    eddy_chunks = pl.pallas_call(
        functools.partial(edge_kernel, nz_parts, width, rows, walls),
        out_shape=chunk_shape,
        in_specs=in_smem(2) + in_vmem(3),
        out_specs=pl.BlockSpec(memory_space=pltpu.VMEM),
        scratch_shapes=[pltpu.VMEM((3, 3, nx, nz_parts * lanes), f32)],
        input_output_aliases={4: 0},
        compiler_params=params(),
        name="edge",
    )(rank, position, recv, swapped, provisional)
    back = lax.all_to_all(eddy_chunks, ("gx", "gz"), split_axis=0, concat_axis=0, tiled=True)

    length = cells // SEGMENTS
    levels = SEGMENTS.bit_length() - 1
    packed = aligned(11 * width)
    eddy, reduced, factors, tree = pl.pallas_call(
        sweep_kernel,
        out_shape=(
            jax.ShapeDtypeStruct((width, cells, lanes), f32),
            jax.ShapeDtypeStruct((packed, lanes), f32),
            jax.ShapeDtypeStruct((width, length, 5, SEGMENTS, lanes), f32),
            jax.ShapeDtypeStruct((width, levels, 5, SEGMENTS, lanes), f32),
        ),
        in_specs=in_smem(1) + in_vmem(3),
        out_specs=tuple(in_hbm(1) + in_vmem(3)),
        scratch_shapes=[pltpu.VMEM((width, cells, lanes), f32), pltpu.SemaphoreType.DMA],
        compiler_params=params(),
        name="sweep",
    )(parity, back, velocity, tendency)

    others = [
        lax.ppermute(reduced, "gy", [(partner(i, step, walls), i) for i in range(walls)])
        for step in range(1, walls)
    ]
    particular, response = pl.pallas_call(
        spread_kernel,
        out_shape=(
            jax.ShapeDtypeStruct(velocity.shape, f32),
            jax.ShapeDtypeStruct((2, *velocity.shape[1:]), f32),
        ),
        in_specs=in_vmem(3),
        out_specs=tuple(in_vmem(2)),
        compiler_params=params(),
        cost_estimate=pl.CostEstimate(
            flops=20 * velocity.size, bytes_accessed=16 * velocity.size, transcendentals=0
        ),
        name="spread",
    )(factors, tree, velocity)
    new_velocity = pl.pallas_call(
        functools.partial(finish_kernel, walls),
        out_shape=jax.ShapeDtypeStruct(velocity.shape, f32),
        in_specs=in_smem(1) + in_vmem(2 + walls),
        out_specs=in_hbm(1)[0],
        scratch_shapes=[
            pltpu.VMEM((walls, packed, lanes), f32),
            pltpu.VMEM((walls + 1, aligned(3 * width), lanes), f32),
            pltpu.VMEM(velocity.shape, f32),
            pltpu.SemaphoreType.DMA((planes,)),
        ],
        compiler_params=params(),
        name="finish",
    )(position, particular, response, reduced, *others)
    return (new_velocity, eddy)


def solution(mesh):
    return jax.shard_map(
        body,
        mesh=mesh,
        in_specs=(P(None, "gx", "gy", "gz"), P(None, "gx", "gy", "gz")),
        out_specs=(P(None, "gx", "gy", "gz"), P("gx", "gy", "gz")),
        check_vma=False,
    )
```

```python
import functools

import jax
import jax.numpy as jnp
from jax import lax
from jax.experimental import pallas as pl
from jax.experimental.pallas import tpu as pltpu
from jax.sharding import PartitionSpec as P

LANES = 128
SEGMENTS = 8
VMEM_BYTES = 24 * 2**20


def strain_parts(grad_x, grad_y, grad_z):
    return (
        grad_x[0],
        grad_y[1],
        grad_z[2],
        grad_y[0] + grad_x[1],
        grad_z[0] + grad_x[2],
        grad_z[1] + grad_y[2],
    )


def strain_size(parts):
    diagonal = parts[0] * parts[0] + parts[1] * parts[1] + parts[2] * parts[2]
    mixed = parts[3] * parts[3] + parts[4] * parts[4] + parts[5] * parts[5]
    return jnp.sqrt(0.5 * diagonal + 0.25 * mixed)


def beside(blocks):
    count = len(blocks)
    lanes = blocks[0].shape[1]
    down = [pltpu.roll(f, 1, 1) for f in blocks]
    up = [pltpu.roll(f, lanes - 1, 1) for f in blocks]
    if count > 1:
        lane = lax.broadcasted_iota(jnp.int32, blocks[0].shape, 1)
        first, last = lane == 0, lane == lanes - 1
        down, up = (
            [jnp.where(first, down[i - 1], down[i]) for i in range(count)],
            [jnp.where(last, up[(i + 1) % count], up[i]) for i in range(count)],
        )
    return down, up


def slope_z(blocks):
    down, up = beside(blocks)
    return [u - d for u, d in zip(up, down)]


def smooth_z(blocks):
    down, up = beside(blocks)
    return [(u + d) + 2.0 * f for f, u, d in zip(blocks, up, down)]


def products(v):
    return (v[0] * v[0], v[1] * v[1], v[2] * v[2], v[0] * v[1], v[0] * v[2], v[1] * v[2])


def outer_ranks(count):
    return (count - 1, count - 3)


def places(parity, count):
    outer = outer_ranks(count)
    inner = iter(range(1, count - 1))
    return [
        (0 if outer[parity] == rank else count - 1) if rank in outer else next(inner)
        for rank in range(count)
    ]


def swap_pairs(walls, count):
    odd, even = outer_ranks(count)
    spare = count - 5
    partners = {}

    def join(a, b):
        partners[a], partners[b] = b, a

    def join_walls(rank, first):
        for wall in range(first, walls - 1, 2):
            join((wall, rank), (wall + 1, rank))

    join_walls(even, 0)
    join_walls(odd, 1)
    join_walls(spare, 1)
    join((0, odd), (0, spare))
    if walls % 2 == 0:
        join((walls - 1, odd), (walls - 1, spare))
    others = [r for r in range(count) if r not in (odd, even, spare)]
    for core in range(2):
        ranks = [r for r in others if r % 2 == core]
        half = len(ranks) // 2
        for wall in range(walls):
            for a, b in zip(ranks[:half], ranks[half : 2 * half]):
                join((wall, a), (wall, b))
        for rank in ranks[2 * half :]:
            join_walls(rank, 0)
    return [
        (wall * count + rank, to[0] * count + to[1])
        for wall in range(walls)
        for rank in range(count)
        for to in [partners.get((wall, rank), (wall, rank))]
    ]


def by_parity(parity, count, fill):
    outer = outer_ranks(count)
    for rank, place in enumerate(places(0, count)):
        if rank not in outer:
            fill(rank, place)
    for turn in range(2):

        @pl.when(parity[0] == turn)
        def _():
            for rank in outer:
                fill(rank, places(turn, count)[rank])


def aligned(n):
    return -(-n // 8) * 8


def pack_kernel(rows, parity, velocity, out):
    _, width, cells, _ = velocity.shape
    count, depth, lanes = out.shape
    planes = 3 * width
    slots = planes * rows

    def fill(rank, place):
        first = place * rows
        beside = [first - 1, first + rows]
        if place == 0:
            beside = [first, first + rows]
        if place == count - 1:
            beside = [first + rows - 1, first - 1]
        for i in range(planes):
            c, x = divmod(i, width)
            out[rank, i * rows : (i + 1) * rows, :] = velocity[c, x, first : first + rows, :]
            for slot, row in enumerate(beside):
                at = slots + slot * aligned(planes) + i
                out[rank, at : at + 1, :] = velocity[c, x, row : row + 1, :]

    by_parity(parity, count, fill)
    blank = aligned(planes) - planes
    for rank in range(count):
        for slot in range(2):
            at = slots + slot * aligned(planes) + planes
            out[rank, at : at + blank, :] = jnp.zeros((blank, lanes), jnp.float32)
        at = slots + 2 * aligned(planes)
        if at < depth:
            out[rank, at:, :] = jnp.zeros((depth - at, lanes), jnp.float32)


def outer_sides(rank, parity, count):
    outer = outer_ranks(count)
    even = parity[0] == 0
    bottom = rank[0] == jnp.where(even, outer[0], outer[1])
    top = rank[0] == jnp.where(even, outer[1], outer[0])
    return bottom, top


def edge_kernel(nz_parts, width, rows, walls, rank, position, recv, swapped, given, out, vel):
    count, _, lanes = recv.shape
    planes = 3 * width
    nx = (count // nz_parts) * width
    nz = nz_parts * lanes
    bottom, top = outer_sides(rank, [lax.rem(position[0], 2)], count)
    at_wall = jnp.logical_or(
        jnp.logical_and(bottom, position[0] == 0), jnp.logical_and(top, position[0] == walls - 1)
    )

    def rows_of(k, i):
        first = i * rows
        own = [recv[k, first + j : first + j + 1, :] for j in (0, 1, rows - 2, rows - 1)]
        far = jnp.where(at_wall, 0.0, swapped[k, i : i + 1, :])
        return (
            jnp.where(bottom, far, own[2]),
            jnp.where(bottom, own[0], own[3]),
            jnp.where(bottom, own[1], far),
        )

    def roll_x(f, shift):
        return pltpu.roll(f, shift % nx, 0)

    def roll_z(f, shift):
        return pltpu.roll(f, shift % nz, 1)

    def smooth_x(f):
        return (roll_x(f, 1) + roll_x(f, -1)) + 2.0 * f

    def smooth(f):
        f = smooth_x(f)
        return (roll_z(f, 1) + roll_z(f, -1)) + 2.0 * f

    def slopes(below, centre, above):
        return strain_parts(
            [roll_x(f, -1) - roll_x(f, 1) for f in centre],
            [a - b for a, b in zip(above, below)],
            [roll_z(f, -1) - roll_z(f, 1) for f in centre],
        )

    @pl.when(jnp.logical_or(bottom, top))
    def _():
        for k in range(count):
            x0, zb = (k // nz_parts) * width, k % nz_parts
            for i in range(planes):
                c, x = divmod(i, width)
                for j, row in enumerate(rows_of(k, i)):
                    vel[j, c, x0 + x : x0 + x + 1, zb * lanes : (zb + 1) * lanes] = row
        u = [[vel[j, c] for c in range(3)] for j in range(3)]
        v = [[smooth(f) for f in row] for row in u]
        strain = slopes(*u)
        size = strain_size(strain)
        mean_strain = slopes(*v)
        mean_size = 0.25 * strain_size(mean_strain)
        scaled = [0.0625 * f for f in v[1]]
        pairs = [v[1][i] * scaled[j] for i, j in ((0, 0), (1, 1), (2, 2), (0, 1), (0, 2), (1, 2))]
        leonard = [smooth(p) - q for p, q in zip(products(u[1]), pairs)]
        model = [smooth(size * s) - mean_size * f for s, f in zip(strain, mean_strain)]
        lm, mm = contracted(leonard, model)
        coefficient = coefficient_of(
            *(jnp.sum(f, axis=(0, 1), keepdims=True) for f in (lm, mm)), nx * nz
        )
        eddy = coefficient * size

        def put(at):
            for k in range(count):
                x0, zb = (k // nz_parts) * width, k % nz_parts
                for x in range(width):
                    out[k, x, at : at + 1, :] = eddy[x0 + x : x0 + x + 1, zb * lanes : (zb + 1) * lanes]

        pl.when(bottom)(lambda: put(0))
        pl.when(top)(lambda: put(rows - 1))


def contracted(leonard, model):
    lm = mm = None
    for i in range(6):
        square = model[i] * model[i] if i < 3 else (0.5 * model[i]) * model[i]
        product = leonard[i] * model[i]
        lm = product if lm is None else lm + product
        mm = square if mm is None else mm + square
    return lm, mm


def coefficient_of(plane_lm, plane_mm, cells):
    scale = 1.0 / (256.0 * cells)
    return jnp.maximum(plane_lm * scale / (plane_mm * scale + 1e-06), 0.0)


def germano_kernel(nz_parts, width, rows, rank, parity, recv, out, vel, filt, ends, mag, part):
    count, _, lanes = recv.shape
    planes = 3 * width
    _, top = outer_sides(rank, parity, count)
    nx = (count // nz_parts) * width
    nz = nz_parts * lanes
    blocks = range(nz_parts)
    lead = 8
    inner = slice(lead, lead + rows)
    lower = slice(lead - 1, lead - 1 + rows)
    upper = slice(lead + 1, lead + 1 + rows)
    for k in range(count):
        x0, zb = (k // nz_parts) * width, k % nz_parts
        for c in range(3):
            for x in range(width):
                i = c * width + x
                vel[c, x0 + x, zb, inner, :] = recv[k, i * rows : (i + 1) * rows, :]
                slots = planes * rows + i
                near = recv[k, slots : slots + 1, :]
                slots += aligned(planes)
                other = recv[k, slots : slots + 1, :]
                below = jnp.where(top, other, near)
                for side, (edge, at) in enumerate(((below, lead - 1), (other, lead + rows))):
                    vel[c, x0 + x, zb, at : at + 1, :] = edge
                    ends[c, x0 + x, zb, side : side + 1, :] = edge

    for x in range(nx):
        left, right = (x - 1) % nx, (x + 1) % nx
        centre = [[vel[c, x, zb, inner, :] for zb in blocks] for c in range(3)]
        grad_x = [[vel[c, right, zb, inner, :] - vel[c, left, zb, inner, :] for zb in blocks] for c in range(3)]
        grad_y = [[vel[c, x, zb, upper, :] - vel[c, x, zb, lower, :] for zb in blocks] for c in range(3)]
        grad_z = []
        for c in range(3):
            down, up = beside(centre[c])
            grad_z.append([u - d for u, d in zip(up, down)])
            for zb in blocks:
                part[c, x, zb] = (up[zb] + down[zb]) + 2.0 * centre[c][zb]
        strain = [
            strain_parts(*([g[c][zb] for c in range(3)] for g in (grad_x, grad_y, grad_z)))
            for zb in blocks
        ]
        size = [strain_size(s) for s in strain]
        for zb in blocks:
            mag[x, zb] = size[zb]
        pairs = [products([centre[c][zb] for c in range(3)]) for zb in blocks]
        for i in range(6):
            for base, fields in (
                (3, [pairs[zb][i] for zb in blocks]),
                (9, [size[zb] * strain[zb][i] for zb in blocks]),
            ):
                for zb, f in enumerate(smooth_z(fields)):
                    part[base + i, x, zb] = f

    def smooth_x(read, x):
        return (read((x - 1) % nx) + read((x + 1) % nx)) + 2.0 * read(x)

    for c in range(3):
        rims = []
        for x in range(nx):
            rims.append(smooth_z([ends[c, x, zb] for zb in blocks]))
        for x in range(nx):
            for zb in blocks:
                rim = smooth_x(lambda at: rims[at][zb], x)
                filt[c, x, zb, lead - 1 : lead, :] = rim[0:1, :]
                filt[c, x, zb, lead + rows : lead + rows + 1, :] = rim[1:2, :]
                filt[c, x, zb, inner, :] = smooth_x(lambda at: part[c, at, zb], x)

    sum_lm = sum_mm = None
    for x in range(nx):
        left, right = (x - 1) % nx, (x + 1) % nx
        mean = [[filt[c, x, zb, inner, :] for zb in blocks] for c in range(3)]
        grad_x = [[filt[c, right, zb, inner, :] - filt[c, left, zb, inner, :] for zb in blocks] for c in range(3)]
        grad_y = [[filt[c, x, zb, upper, :] - filt[c, x, zb, lower, :] for zb in blocks] for c in range(3)]
        grad_z = [slope_z(mean[c]) for c in range(3)]
        for zb in blocks:
            strain = strain_parts(*([g[c][zb] for c in range(3)] for g in (grad_x, grad_y, grad_z)))
            size = 0.25 * strain_size(strain)
            v = [mean[c][zb] for c in range(3)]
            scaled = [0.0625 * f for f in v]
            pairs = (
                v[0] * scaled[0],
                v[1] * scaled[1],
                v[2] * scaled[2],
                v[0] * scaled[1],
                v[0] * scaled[2],
                v[1] * scaled[2],
            )
            leonard = [smooth_x(lambda at: part[3 + i, at, zb], x) - pairs[i] for i in range(6)]
            model = [smooth_x(lambda at: part[9 + i, at, zb], x) - size * strain[i] for i in range(6)]
            lm, mm = contracted(leonard, model)
            sum_lm = lm if sum_lm is None else sum_lm + lm
            sum_mm = mm if sum_mm is None else sum_mm + mm

    coefficient = coefficient_of(
        *(jnp.sum(total, axis=1, keepdims=True) for total in (sum_lm, sum_mm)), nx * nz
    )
    for k in range(count):
        x0, zb = (k // nz_parts) * width, k % nz_parts
        for x in range(width):
            out[k, x] = coefficient * mag[x0 + x, zb]


def sweep_kernel(parity, back, velocity, tendency, eddy, reduced, factors, tree):
    count, width, rows, _ = back.shape
    length = count * rows // SEGMENTS

    def fill(rank, place):
        for x in range(width):
            eddy[x, place * rows : (place + 1) * rows, :] = back[rank, x]

    by_parity(parity, count, fill)

    def row(ref, index, j):
        return ref[(*index, pl.ds(j, SEGMENTS, stride=length), slice(None))]

    planes = range(width)
    last_row = length - 1
    visc = [[1.0 + row(eddy, (x,), j) for x in planes] for j in range(length)]
    links = [[750.0 * (v + w) for v, w in zip(visc[j], visc[j + 1])] for j in range(last_row)]

    over = [jnp.ones_like(v) for v in visc[0]]
    under = [jnp.ones_like(v) for v in visc[0]]
    inverses = []
    for j in range(last_row):
        inverses.append([u / (o + e * u) for o, u, e in zip(over, under, links[j])])
        steps = [o * (1.0 / e) for o, e in zip(over, links[j])]
        under, over = (
            [u + t for u, t in zip(under, steps)],
            [(o + u) + t for o, u, t in zip(over, under, steps)],
        )
    inverses.append([u / o for o, u in zip(over, under)])

    value = first = corner = left = None
    reach = [jnp.ones_like(v) for v in visc[0]]
    for j in range(length):
        inverse = inverses[j]
        before = value
        source = [[2.0 * row(velocity, (c, x), j) + row(tendency, (c, x), j) for x in planes] for c in range(3)]
        value = [[f * r for f, r in zip(source[c], inverse)] for c in range(3)]
        if j > 0:
            carry = [e * r for e, r in zip(links[j - 1], inverse)]
            value = [[v + k * w for v, k, w in zip(value[c], carry, before[c])] for c in range(3)]
        left = [m * r for m, r in zip(reach, inverse)]
        if j == 0:
            first, corner = value, left
        else:
            first = [[f + m * v for f, m, v in zip(first[c], reach, value[c])] for c in range(3)]
            corner = [a + m * v for a, m, v in zip(corner, reach, left)]
        ratio = inverse
        if j < last_row:
            ratio = [e * r for e, r in zip(links[j], inverse)]
            reach = [m * r for m, r in zip(reach, ratio)]
        for x in planes:
            for c in range(3):
                factors[x, j, c] = value[c][x]
            factors[x, j, 3] = left[x]
            factors[x, j, 4] = ratio[x]

    def other(fields, step):
        return [pltpu.roll(f, (SEGMENTS - step) % SEGMENTS, 0) if step else f for f in fields]

    last, across, end = value, left, inverse
    seams = [750.0 * (v + w) for v, w in zip(visc[last_row], other(visc[0], 1))]
    level, step = 0, 1
    while step < SEGMENTS:
        link = other(seams, step - 1)
        first_b = [other(f, step) for f in first]
        last_b = [other(f, step) for f in last]
        corner_b, end_b, across_b = other(corner, step), other(end, step), other(across, step)
        stiff = [e / (1.0 + e * (d + a)) for e, d, a in zip(link, end, corner_b)]
        flux = [[k * (g - f) for k, g, f in zip(stiff, last[c], first_b[c])] for c in range(3)]
        from_left = [k * b for k, b in zip(stiff, across)]
        from_right = [k * b for k, b in zip(stiff, across_b)]
        for x in planes:
            for c in range(3):
                tree[x, level, c] = flux[c][x]
            tree[x, level, 3] = from_left[x]
            tree[x, level, 4] = from_right[x]
        first = [[f - b * t for f, b, t in zip(first[c], across, flux[c])] for c in range(3)]
        last = [[g + b * t for g, b, t in zip(last_b[c], across_b, flux[c])] for c in range(3)]
        corner = [a - b * k for a, b, k in zip(corner, across, from_left)]
        end = [d - b * k for d, b, k in zip(end_b, across_b, from_right)]
        across = [k * b for k, b in zip(from_left, across_b)]
        level, step = level + 1, step * 2
    for x in planes:
        rows_out = [f[x][0:1, :] for f in (*first, *last, corner, across, end, visc[0])]
        rows_out.append(visc[last_row][x][SEGMENTS - 1 :, :])
        for i, v in enumerate(rows_out):
            reduced[i * width + x : i * width + x + 1, :] = v


def spread_kernel(factors, tree, velocity, eddy, particular, response, eddy_out, sent):
    write = pltpu.make_async_copy(eddy, eddy_out, sent)
    write.start()
    width, length = factors.shape[:2]
    levels = tree.shape[1]
    sublane = lax.broadcasted_iota(jnp.int32, (SEGMENTS, LANES), 0)
    one, zero = (jnp.full((SEGMENTS, LANES), v, jnp.float32) for v in (1.0, 0.0))
    sides = [(c, zero, zero) for c in range(3)] + [(None, one, zero), (None, zero, one)]
    lefts = [[side[1]] * width for side in sides]
    rights = [[side[2]] * width for side in sides]
    for level in range(levels - 1, -1, -1):
        step = 2**level
        second = lax.rem(sublane, 2 * step) == step
        for n, (c, _, _) in enumerate(sides):
            for x in range(width):
                left, right = lefts[n][x], rights[n][x]
                through = tree[x, level, 3] * left - tree[x, level, 4] * right
                if c is not None:
                    through = tree[x, level, c] + through
                lefts[n][x] = jnp.where(second, pltpu.roll(through, step, 0), left)
                rights[n][x] = jnp.where(second, pltpu.roll(right, step, 0), -through)
    values = rights
    for j in range(length - 1, -1, -1):
        rows = pl.ds(j, SEGMENTS, stride=length)
        for n, (c, _, _) in enumerate(sides):
            for x in range(width):
                value = factors[x, j, 3] * lefts[n][x] + factors[x, j, 4] * values[n][x]
                if c is not None:
                    value = factors[x, j, c] + value
                    particular[c, x, rows, :] = value - velocity[c, x, rows, :]
                else:
                    response[n - 3, x, rows, :] = value
                values[n][x] = value
    write.wait()


def partner(i, step, count):
    if count & (count - 1) == 0:
        return i ^ step
    return (i - step + count) % count


def finish_kernel(devices, position, particular, response, *rest):
    reduced, (result, gathered, fluxes, out, sent) = rest[:devices], rest[devices:]
    width = particular.shape[1]
    here = position[0]
    for step in range(devices):
        gathered[partner(here, step, devices)] = reduced[step][...]

    def part(device, i):
        return gathered[device, i * width : (i + 1) * width, :]

    pivots, sources = [], []
    for i in range(devices + 1):
        visc = [part(i - 1, 10)] if i > 0 else []
        total = [part(i - 1, 8)] if i > 0 else []
        source = [part(i - 1, 3 + c) for c in range(3)] if i > 0 else [0.0] * 3
        if i < devices:
            visc.append(part(i, 9))
            total.append(part(i, 6))
            source = [s - part(i, c) for c, s in enumerate(source)]
        pivots.append(sum(total) + 1.0 / (750.0 * sum(visc)))
        sources.append(source)
    across = [part(i, 7) for i in range(devices)]
    minors = [jnp.ones_like(pivots[0]), pivots[0]]
    for i in range(1, devices + 1):
        minors.append(pivots[i] * minors[i] - (across[i - 1] * across[i - 1]) * minors[i - 1])
    inverses = [minors[i] / minors[i + 1] for i in range(devices + 1)]
    ratios = [b * r for b, r in zip(across, inverses)]
    for i in range(1, devices + 1):
        sources[i] = [s + ratios[i - 1] * t for s, t in zip(sources[i], sources[i - 1])]
    for i in range(devices, -1, -1):
        flux_here = [inverses[i] * s for s in sources[i]]
        flux = flux_here if i == devices else [f + ratios[i] * g for f, g in zip(flux_here, flux)]
        for c in range(3):
            fluxes[i, c * width : (c + 1) * width, :] = flux[c]

    writes = []
    for c in range(3):
        for x in range(width):
            r = c * width + x
            left, right = fluxes[here, r : r + 1, :], fluxes[here + 1, r : r + 1, :]
            out[c, x] = particular[c, x] + (response[0, x] * left - response[1, x] * right)
            writes.append(pltpu.make_async_copy(out.at[c, x], result.at[c, x], sent.at[r]))
            writes[-1].start()
    for write in writes:
        write.wait()


def in_vmem(count):
    return [pl.BlockSpec(memory_space=pltpu.VMEM)] * count


def in_hbm(count):
    return [pl.BlockSpec(memory_space=pltpu.HBM)] * count


def in_smem(count):
    return [pl.BlockSpec(memory_space=pltpu.SMEM)] * count


def params():
    return pltpu.CompilerParams(vmem_limit_bytes=VMEM_BYTES)


def body(velocity, tendency):
    _, width, cells, lanes = velocity.shape
    nz_parts = lax.axis_size("gz")
    count = lax.axis_size("gx") * nz_parts
    walls = lax.axis_size("gy")
    rows = cells // count
    nx = lax.axis_size("gx") * width
    padded = 16 + aligned(rows)
    f32 = jnp.float32

    planes = 3 * width
    depth = aligned(planes * rows + 2 * aligned(planes))
    position = lax.axis_index("gy").astype(jnp.int32).reshape(1)
    parity = lax.rem(position, 2)
    chunks = pl.pallas_call(
        functools.partial(pack_kernel, rows),
        out_shape=jax.ShapeDtypeStruct((count, depth, lanes), f32),
        in_specs=in_smem(1) + in_vmem(1),
        out_specs=pl.BlockSpec(memory_space=pltpu.VMEM),
        compiler_params=params(),
        name="pack",
    )(parity, velocity)
    recv = lax.all_to_all(chunks, ("gx", "gz"), split_axis=0, concat_axis=0, tiled=True)
    slot = lax.slice_in_dim(recv, planes * rows, planes * rows + aligned(planes), axis=1)
    swapped = lax.ppermute(slot, ("gy", "gx", "gz"), swap_pairs(walls, count))
    rank = lax.axis_index(("gx", "gz")).astype(jnp.int32).reshape(1)
    chunk_shape = jax.ShapeDtypeStruct((count, width, rows, lanes), f32)
    cells_here = nx * nz_parts * rows * lanes
    provisional = pl.pallas_call(
        functools.partial(germano_kernel, nz_parts, width, rows),
        out_shape=chunk_shape,
        in_specs=in_smem(2) + in_vmem(1),
        out_specs=pl.BlockSpec(memory_space=pltpu.VMEM),
        scratch_shapes=[
            pltpu.VMEM((3, nx, nz_parts, padded, lanes), f32),
            pltpu.VMEM((3, nx, nz_parts, padded, lanes), f32),
            pltpu.VMEM((3, nx, nz_parts, 8, lanes), f32),
            pltpu.VMEM((nx, nz_parts, rows, lanes), f32),
            pltpu.VMEM((15, nx, nz_parts, rows, lanes), f32),
        ],
        compiler_params=params(),
        cost_estimate=pl.CostEstimate(
            flops=300 * cells_here, bytes_accessed=16 * cells_here, transcendentals=2 * cells_here
        ),
        name="germano",
    )(rank, parity, recv)
    eddy_chunks = pl.pallas_call(
        functools.partial(edge_kernel, nz_parts, width, rows, walls),
        out_shape=chunk_shape,
        in_specs=in_smem(2) + in_vmem(3),
        out_specs=pl.BlockSpec(memory_space=pltpu.VMEM),
        scratch_shapes=[pltpu.VMEM((3, 3, nx, nz_parts * lanes), f32)],
        input_output_aliases={4: 0},
        compiler_params=params(),
        name="edge",
    )(rank, position, recv, swapped, provisional)
    back = lax.all_to_all(eddy_chunks, ("gx", "gz"), split_axis=0, concat_axis=0, tiled=True)

    length = cells // SEGMENTS
    levels = SEGMENTS.bit_length() - 1
    packed = aligned(11 * width)
    eddy_here, reduced, factors, tree = pl.pallas_call(
        sweep_kernel,
        out_shape=(
            jax.ShapeDtypeStruct((width, cells, lanes), f32),
            jax.ShapeDtypeStruct((packed, lanes), f32),
            jax.ShapeDtypeStruct((width, length, 5, SEGMENTS, lanes), f32),
            jax.ShapeDtypeStruct((width, levels, 5, SEGMENTS, lanes), f32),
        ),
        in_specs=in_smem(1) + in_vmem(3),
        out_specs=tuple(in_vmem(4)),
        compiler_params=params(),
        name="sweep",
    )(parity, back, velocity, tendency)

    others = [
        lax.ppermute(reduced, "gy", [(partner(i, step, walls), i) for i in range(walls)])
        for step in range(1, walls)
    ]
    particular, response, eddy = pl.pallas_call(
        spread_kernel,
        out_shape=(
            jax.ShapeDtypeStruct(velocity.shape, f32),
            jax.ShapeDtypeStruct((2, *velocity.shape[1:]), f32),
            jax.ShapeDtypeStruct(eddy_here.shape, f32),
        ),
        in_specs=in_vmem(4),
        out_specs=tuple(in_vmem(2) + in_hbm(1)),
        scratch_shapes=[pltpu.SemaphoreType.DMA],
        compiler_params=params(),
        cost_estimate=pl.CostEstimate(
            flops=20 * velocity.size, bytes_accessed=16 * velocity.size, transcendentals=0
        ),
        name="spread",
    )(factors, tree, velocity, eddy_here)
    new_velocity = pl.pallas_call(
        functools.partial(finish_kernel, walls),
        out_shape=jax.ShapeDtypeStruct(velocity.shape, f32),
        in_specs=in_smem(1) + in_vmem(2 + walls),
        out_specs=in_hbm(1)[0],
        scratch_shapes=[
            pltpu.VMEM((walls, packed, lanes), f32),
            pltpu.VMEM((walls + 1, aligned(3 * width), lanes), f32),
            pltpu.VMEM(velocity.shape, f32),
            pltpu.SemaphoreType.DMA((planes,)),
        ],
        compiler_params=params(),
        name="finish",
    )(position, particular, response, reduced, *others)
    return (new_velocity, eddy)


def solution(mesh):
    return jax.shard_map(
        body,
        mesh=mesh,
        in_specs=(P(None, "gx", "gy", "gz"), P(None, "gx", "gy", "gz")),
        out_specs=(P(None, "gx", "gy", "gz"), P("gx", "gy", "gz")),
        check_vma=False,
    )
```

```python
import functools

import jax
import jax.numpy as jnp
from jax import lax
from jax.experimental import pallas as pl
from jax.experimental.pallas import tpu as pltpu
from jax.sharding import PartitionSpec as P

LANES = 128
SEGMENTS = 8
VMEM_BYTES = 24 * 2**20


def strain_parts(grad_x, grad_y, grad_z):
    return (
        grad_x[0],
        grad_y[1],
        grad_z[2],
        grad_y[0] + grad_x[1],
        grad_z[0] + grad_x[2],
        grad_z[1] + grad_y[2],
    )


def strain_size(parts):
    diagonal = parts[0] * parts[0] + parts[1] * parts[1] + parts[2] * parts[2]
    mixed = parts[3] * parts[3] + parts[4] * parts[4] + parts[5] * parts[5]
    return jnp.sqrt(0.5 * diagonal + 0.25 * mixed)


def beside(blocks):
    count = len(blocks)
    lanes = blocks[0].shape[1]
    down = [pltpu.roll(f, 1, 1) for f in blocks]
    up = [pltpu.roll(f, lanes - 1, 1) for f in blocks]
    if count > 1:
        lane = lax.broadcasted_iota(jnp.int32, blocks[0].shape, 1)
        first, last = lane == 0, lane == lanes - 1
        down, up = (
            [jnp.where(first, down[i - 1], down[i]) for i in range(count)],
            [jnp.where(last, up[(i + 1) % count], up[i]) for i in range(count)],
        )
    return down, up


def slope_z(blocks):
    down, up = beside(blocks)
    return [u - d for u, d in zip(up, down)]


def smooth_z(blocks):
    down, up = beside(blocks)
    return [(u + d) + 2.0 * f for f, u, d in zip(blocks, up, down)]


def products(v):
    return (v[0] * v[0], v[1] * v[1], v[2] * v[2], v[0] * v[1], v[0] * v[2], v[1] * v[2])


def outer_ranks(count):
    return (count - 1, count - 3)


def places(parity, count):
    outer = outer_ranks(count)
    inner = iter(range(1, count - 1))
    return [
        (0 if outer[parity] == rank else count - 1) if rank in outer else next(inner)
        for rank in range(count)
    ]


def swap_pairs(walls, count):
    odd, even = outer_ranks(count)
    spare = count - 5
    partners = {}

    def join(a, b):
        partners[a], partners[b] = b, a

    def join_walls(rank, first):
        for wall in range(first, walls - 1, 2):
            join((wall, rank), (wall + 1, rank))

    join_walls(even, 0)
    join_walls(odd, 1)
    join_walls(spare, 1)
    join((0, odd), (0, spare))
    if walls % 2 == 0:
        join((walls - 1, odd), (walls - 1, spare))
    others = [r for r in range(count) if r not in (odd, even, spare)]
    for core in range(2):
        ranks = [r for r in others if r % 2 == core]
        half = len(ranks) // 2
        for wall in range(walls):
            for a, b in zip(ranks[:half], ranks[half : 2 * half]):
                join((wall, a), (wall, b))
        for rank in ranks[2 * half :]:
            join_walls(rank, 0)
    return [
        (wall * count + rank, to[0] * count + to[1])
        for wall in range(walls)
        for rank in range(count)
        for to in [partners.get((wall, rank), (wall, rank))]
    ]


def by_parity(parity, count, fill):
    outer = outer_ranks(count)
    for rank, place in enumerate(places(0, count)):
        if rank not in outer:
            fill(rank, place)
    for turn in range(2):

        @pl.when(parity[0] == turn)
        def _():
            for rank in outer:
                fill(rank, places(turn, count)[rank])


def aligned(n):
    return -(-n // 8) * 8


def pack_kernel(rows, parity, velocity, out):
    _, width, cells, _ = velocity.shape
    count, depth, lanes = out.shape
    planes = 3 * width
    slots = planes * rows

    def fill(rank, place):
        first = place * rows
        beside = [first - 1, first + rows]
        if place == 0:
            beside = [first, first + rows]
        if place == count - 1:
            beside = [first + rows - 1, first - 1]
        for i in range(planes):
            c, x = divmod(i, width)
            out[rank, i * rows : (i + 1) * rows, :] = velocity[c, x, first : first + rows, :]
            for slot, row in enumerate(beside):
                at = slots + slot * aligned(planes) + i
                out[rank, at : at + 1, :] = velocity[c, x, row : row + 1, :]

    by_parity(parity, count, fill)
    blank = aligned(planes) - planes
    for rank in range(count):
        for slot in range(2):
            at = slots + slot * aligned(planes) + planes
            out[rank, at : at + blank, :] = jnp.zeros((blank, lanes), jnp.float32)
        at = slots + 2 * aligned(planes)
        if at < depth:
            out[rank, at:, :] = jnp.zeros((depth - at, lanes), jnp.float32)


def outer_sides(rank, parity, count):
    outer = outer_ranks(count)
    even = parity[0] == 0
    bottom = rank[0] == jnp.where(even, outer[0], outer[1])
    top = rank[0] == jnp.where(even, outer[1], outer[0])
    return bottom, top


def edge_kernel(nz_parts, width, rows, walls, rank, position, recv, swapped, given, out, vel):
    count, _, lanes = recv.shape
    planes = 3 * width
    nx = (count // nz_parts) * width
    nz = nz_parts * lanes
    bottom, top = outer_sides(rank, [lax.rem(position[0], 2)], count)
    at_wall = jnp.logical_or(
        jnp.logical_and(bottom, position[0] == 0), jnp.logical_and(top, position[0] == walls - 1)
    )

    def rows_of(k, i):
        first = i * rows
        own = [recv[k, first + j : first + j + 1, :] for j in (0, 1, rows - 2, rows - 1)]
        far = jnp.where(at_wall, 0.0, swapped[k, i : i + 1, :])
        return (
            jnp.where(bottom, far, own[2]),
            jnp.where(bottom, own[0], own[3]),
            jnp.where(bottom, own[1], far),
        )

    def roll_x(f, shift):
        return pltpu.roll(f, shift % nx, 0)

    def roll_z(f, shift):
        return pltpu.roll(f, shift % nz, 1)

    def smooth_x(f):
        return (roll_x(f, 1) + roll_x(f, -1)) + 2.0 * f

    def smooth(f):
        f = smooth_x(f)
        return (roll_z(f, 1) + roll_z(f, -1)) + 2.0 * f

    def slopes(below, centre, above):
        return strain_parts(
            [roll_x(f, -1) - roll_x(f, 1) for f in centre],
            [a - b for a, b in zip(above, below)],
            [roll_z(f, -1) - roll_z(f, 1) for f in centre],
        )

    @pl.when(jnp.logical_or(bottom, top))
    def _():
        for k in range(count):
            x0, zb = (k // nz_parts) * width, k % nz_parts
            for i in range(planes):
                c, x = divmod(i, width)
                for j, row in enumerate(rows_of(k, i)):
                    vel[j, c, x0 + x : x0 + x + 1, zb * lanes : (zb + 1) * lanes] = row
        u = [[vel[j, c] for c in range(3)] for j in range(3)]
        v = [[smooth(f) for f in row] for row in u]
        strain = slopes(*u)
        size = strain_size(strain)
        mean_strain = slopes(*v)
        mean_size = 0.25 * strain_size(mean_strain)
        scaled = [0.0625 * f for f in v[1]]
        pairs = [v[1][i] * scaled[j] for i, j in ((0, 0), (1, 1), (2, 2), (0, 1), (0, 2), (1, 2))]
        leonard = [smooth(p) - q for p, q in zip(products(u[1]), pairs)]
        model = [smooth(size * s) - mean_size * f for s, f in zip(strain, mean_strain)]
        lm, mm = contracted(leonard, model)
        coefficient = coefficient_of(
            *(jnp.sum(f, axis=(0, 1), keepdims=True) for f in (lm, mm)), nx * nz
        )
        eddy = coefficient * size

        def put(at):
            for k in range(count):
                x0, zb = (k // nz_parts) * width, k % nz_parts
                for x in range(width):
                    out[k, x, at : at + 1, :] = eddy[x0 + x : x0 + x + 1, zb * lanes : (zb + 1) * lanes]

        pl.when(bottom)(lambda: put(0))
        pl.when(top)(lambda: put(rows - 1))


def contracted(leonard, model):
    lm = mm = None
    for i in range(6):
        square = model[i] * model[i] if i < 3 else (0.5 * model[i]) * model[i]
        product = leonard[i] * model[i]
        lm = product if lm is None else lm + product
        mm = square if mm is None else mm + square
    return lm, mm


def coefficient_of(plane_lm, plane_mm, cells):
    scale = 1.0 / (256.0 * cells)
    return jnp.maximum(plane_lm * scale / (plane_mm * scale + 1e-06), 0.0)


def germano_kernel(nz_parts, width, rows, rank, parity, recv, out, vel, filt, ends, mag, part):
    count, _, lanes = recv.shape
    planes = 3 * width
    _, top = outer_sides(rank, parity, count)
    nx = (count // nz_parts) * width
    nz = nz_parts * lanes
    blocks = range(nz_parts)
    lead = 8
    inner = slice(lead, lead + rows)
    lower = slice(lead - 1, lead - 1 + rows)
    upper = slice(lead + 1, lead + 1 + rows)
    for k in range(count):
        x0, zb = (k // nz_parts) * width, k % nz_parts
        for c in range(3):
            for x in range(width):
                i = c * width + x
                vel[c, x0 + x, zb, inner, :] = recv[k, i * rows : (i + 1) * rows, :]
                slots = planes * rows + i
                near = recv[k, slots : slots + 1, :]
                slots += aligned(planes)
                other = recv[k, slots : slots + 1, :]
                below = jnp.where(top, other, near)
                for side, (edge, at) in enumerate(((below, lead - 1), (other, lead + rows))):
                    vel[c, x0 + x, zb, at : at + 1, :] = edge
                    ends[c, x0 + x, zb, side : side + 1, :] = edge

    for x in range(nx):
        left, right = (x - 1) % nx, (x + 1) % nx
        centre = [[vel[c, x, zb, inner, :] for zb in blocks] for c in range(3)]
        grad_x = [[vel[c, right, zb, inner, :] - vel[c, left, zb, inner, :] for zb in blocks] for c in range(3)]
        grad_y = [[vel[c, x, zb, upper, :] - vel[c, x, zb, lower, :] for zb in blocks] for c in range(3)]
        grad_z = []
        for c in range(3):
            down, up = beside(centre[c])
            grad_z.append([u - d for u, d in zip(up, down)])
            for zb in blocks:
                part[c, x, zb] = (up[zb] + down[zb]) + 2.0 * centre[c][zb]
        strain = [
            strain_parts(*([g[c][zb] for c in range(3)] for g in (grad_x, grad_y, grad_z)))
            for zb in blocks
        ]
        size = [strain_size(s) for s in strain]
        for zb in blocks:
            mag[x, zb] = size[zb]
        pairs = [products([centre[c][zb] for c in range(3)]) for zb in blocks]
        for i in range(6):
            for base, fields in (
                (3, [pairs[zb][i] for zb in blocks]),
                (9, [size[zb] * strain[zb][i] for zb in blocks]),
            ):
                for zb, f in enumerate(smooth_z(fields)):
                    part[base + i, x, zb] = f

    def smooth_x(read, x):
        return (read((x - 1) % nx) + read((x + 1) % nx)) + 2.0 * read(x)

    for c in range(3):
        rims = []
        for x in range(nx):
            rims.append(smooth_z([ends[c, x, zb] for zb in blocks]))
        for x in range(nx):
            for zb in blocks:
                rim = smooth_x(lambda at: rims[at][zb], x)
                filt[c, x, zb, lead - 1 : lead, :] = rim[0:1, :]
                filt[c, x, zb, lead + rows : lead + rows + 1, :] = rim[1:2, :]
                filt[c, x, zb, inner, :] = smooth_x(lambda at: part[c, at, zb], x)

    sum_lm = sum_mm = None
    for x in range(nx):
        left, right = (x - 1) % nx, (x + 1) % nx
        mean = [[filt[c, x, zb, inner, :] for zb in blocks] for c in range(3)]
        grad_x = [[filt[c, right, zb, inner, :] - filt[c, left, zb, inner, :] for zb in blocks] for c in range(3)]
        grad_y = [[filt[c, x, zb, upper, :] - filt[c, x, zb, lower, :] for zb in blocks] for c in range(3)]
        grad_z = [slope_z(mean[c]) for c in range(3)]
        for zb in blocks:
            strain = strain_parts(*([g[c][zb] for c in range(3)] for g in (grad_x, grad_y, grad_z)))
            size = 0.25 * strain_size(strain)
            v = [mean[c][zb] for c in range(3)]
            scaled = [0.0625 * f for f in v]
            pairs = (
                v[0] * scaled[0],
                v[1] * scaled[1],
                v[2] * scaled[2],
                v[0] * scaled[1],
                v[0] * scaled[2],
                v[1] * scaled[2],
            )
            leonard = [smooth_x(lambda at: part[3 + i, at, zb], x) - pairs[i] for i in range(6)]
            model = [smooth_x(lambda at: part[9 + i, at, zb], x) - size * strain[i] for i in range(6)]
            lm, mm = contracted(leonard, model)
            sum_lm = lm if sum_lm is None else sum_lm + lm
            sum_mm = mm if sum_mm is None else sum_mm + mm

    coefficient = coefficient_of(
        *(jnp.sum(total, axis=1, keepdims=True) for total in (sum_lm, sum_mm)), nx * nz
    )
    for k in range(count):
        x0, zb = (k // nz_parts) * width, k % nz_parts
        for x in range(width):
            out[k, x] = coefficient * mag[x0 + x, zb]


def sweep_kernel(parity, back, velocity, tendency, eddy, reduced, factors, tree):
    count, width, rows, _ = back.shape
    length = count * rows // SEGMENTS

    def fill(rank, place):
        for x in range(width):
            eddy[x, place * rows : (place + 1) * rows, :] = back[rank, x]

    by_parity(parity, count, fill)

    def row(ref, index, j):
        return ref[(*index, pl.ds(j, SEGMENTS, stride=length), slice(None))]

    planes = range(width)
    last_row = length - 1
    visc = [[1.0 + row(eddy, (x,), j) for x in planes] for j in range(length)]
    links = [[750.0 * (v + w) for v, w in zip(visc[j], visc[j + 1])] for j in range(last_row)]

    over = [jnp.ones_like(v) for v in visc[0]]
    under = [jnp.ones_like(v) for v in visc[0]]
    inverses = []
    for j in range(last_row):
        inverses.append([u / (o + e * u) for o, u, e in zip(over, under, links[j])])
        steps = [o * (1.0 / e) for o, e in zip(over, links[j])]
        under, over = (
            [u + t for u, t in zip(under, steps)],
            [(o + u) + t for o, u, t in zip(over, under, steps)],
        )
    inverses.append([u / o for o, u in zip(over, under)])

    value = first = corner = left = None
    reach = [jnp.ones_like(v) for v in visc[0]]
    for j in range(length):
        inverse = inverses[j]
        before = value
        source = [[2.0 * row(velocity, (c, x), j) + row(tendency, (c, x), j) for x in planes] for c in range(3)]
        value = [[f * r for f, r in zip(source[c], inverse)] for c in range(3)]
        if j > 0:
            carry = [e * r for e, r in zip(links[j - 1], inverse)]
            value = [[v + k * w for v, k, w in zip(value[c], carry, before[c])] for c in range(3)]
        left = [m * r for m, r in zip(reach, inverse)]
        if j == 0:
            first, corner = value, left
        else:
            first = [[f + m * v for f, m, v in zip(first[c], reach, value[c])] for c in range(3)]
            corner = [a + m * v for a, m, v in zip(corner, reach, left)]
        ratio = inverse
        if j < last_row:
            ratio = [e * r for e, r in zip(links[j], inverse)]
            reach = [m * r for m, r in zip(reach, ratio)]
        for x in planes:
            for c in range(3):
                factors[x, j, c] = value[c][x]
            factors[x, j, 3] = left[x]
            factors[x, j, 4] = ratio[x]

    def other(fields, step):
        return [pltpu.roll(f, (SEGMENTS - step) % SEGMENTS, 0) if step else f for f in fields]

    last, across, end = value, left, inverse
    seams = [750.0 * (v + w) for v, w in zip(visc[last_row], other(visc[0], 1))]
    level, step = 0, 1
    while step < SEGMENTS:
        link = other(seams, step - 1)
        first_b = [other(f, step) for f in first]
        last_b = [other(f, step) for f in last]
        corner_b, end_b, across_b = other(corner, step), other(end, step), other(across, step)
        stiff = [e / (1.0 + e * (d + a)) for e, d, a in zip(link, end, corner_b)]
        flux = [[k * (g - f) for k, g, f in zip(stiff, last[c], first_b[c])] for c in range(3)]
        from_left = [k * b for k, b in zip(stiff, across)]
        from_right = [k * b for k, b in zip(stiff, across_b)]
        for x in planes:
            for c in range(3):
                tree[x, level, c] = flux[c][x]
            tree[x, level, 3] = from_left[x]
            tree[x, level, 4] = from_right[x]
        first = [[f - b * t for f, b, t in zip(first[c], across, flux[c])] for c in range(3)]
        last = [[g + b * t for g, b, t in zip(last_b[c], across_b, flux[c])] for c in range(3)]
        corner = [a - b * k for a, b, k in zip(corner, across, from_left)]
        end = [d - b * k for d, b, k in zip(end_b, across_b, from_right)]
        across = [k * b for k, b in zip(from_left, across_b)]
        level, step = level + 1, step * 2
    for x in planes:
        rows_out = [f[x][0:1, :] for f in (*first, *last, corner, across, end, visc[0])]
        rows_out.append(visc[last_row][x][SEGMENTS - 1 :, :])
        for i, v in enumerate(rows_out):
            reduced[i * width + x : i * width + x + 1, :] = v


def spread_kernel(factors, tree, velocity, eddy, particular, response, eddy_out, sent):
    write = pltpu.make_async_copy(eddy, eddy_out, sent)
    write.start()
    width, length = factors.shape[:2]
    levels = tree.shape[1]
    sublane = lax.broadcasted_iota(jnp.int32, (SEGMENTS, LANES), 0)
    one, zero = (jnp.full((SEGMENTS, LANES), v, jnp.float32) for v in (1.0, 0.0))
    sides = [(c, zero, zero) for c in range(3)] + [(None, one, zero), (None, zero, one)]
    lefts = [[side[1]] * width for side in sides]
    rights = [[side[2]] * width for side in sides]
    for level in range(levels - 1, -1, -1):
        step = 2**level
        second = lax.rem(sublane, 2 * step) == step
        for n, (c, _, _) in enumerate(sides):
            for x in range(width):
                left, right = lefts[n][x], rights[n][x]
                through = tree[x, level, 3] * left - tree[x, level, 4] * right
                if c is not None:
                    through = tree[x, level, c] + through
                lefts[n][x] = jnp.where(second, pltpu.roll(through, step, 0), left)
                rights[n][x] = jnp.where(second, pltpu.roll(right, step, 0), -through)
    values = rights
    for j in range(length - 1, -1, -1):
        rows = pl.ds(j, SEGMENTS, stride=length)
        for n, (c, _, _) in enumerate(sides):
            for x in range(width):
                value = factors[x, j, 3] * lefts[n][x] + factors[x, j, 4] * values[n][x]
                if c is not None:
                    value = factors[x, j, c] + value
                    particular[c, x, rows, :] = value - velocity[c, x, rows, :]
                else:
                    response[n - 3, x, rows, :] = value
                values[n][x] = value
    write.wait()


def sources_of(step, count):
    ring = [0, *range(1, count, 2), *range(count - 2 + count % 2, 0, -2)]
    return [ring[(ring.index(i) - step) % count] for i in range(count)]


def exchange_order(count):
    return [1, *range(count - 1, 1, -1)]


def spread_kernel(factors, tree, velocity, eddy, particular, response, eddy_out, sent):
    write = pltpu.make_async_copy(eddy, eddy_out, sent)
    write.start()
    width, length = factors.shape[:2]
    levels = tree.shape[1]
    sublane = lax.broadcasted_iota(jnp.int32, (SEGMENTS, LANES), 0)
    one, zero = (jnp.full((SEGMENTS, LANES), v, jnp.float32) for v in (1.0, 0.0))
    sides = [(c, zero, zero) for c in range(3)] + [(None, one, zero), (None, zero, one)]
    lefts = [[side[1]] * width for side in sides]
    rights = [[side[2]] * width for side in sides]
    for level in range(levels - 1, -1, -1):
        step = 2**level
        second = lax.rem(sublane, 2 * step) == step
        for n, (c, _, _) in enumerate(sides):
            for x in range(width):
                left, right = lefts[n][x], rights[n][x]
                through = tree[x, level, 3] * left - tree[x, level, 4] * right
                if c is not None:
                    through = tree[x, level, c] + through
                lefts[n][x] = jnp.where(second, pltpu.roll(through, step, 0), left)
                rights[n][x] = jnp.where(second, pltpu.roll(right, step, 0), -through)
    values = rights
    for j in range(length - 1, -1, -1):
        rows = pl.ds(j, SEGMENTS, stride=length)
        for n, (c, _, _) in enumerate(sides):
            for x in range(width):
                value = factors[x, j, 3] * lefts[n][x] + factors[x, j, 4] * values[n][x]
                if c is not None:
                    value = factors[x, j, c] + value
                    particular[c, x, rows, :] = value - velocity[c, x, rows, :]
                else:
                    response[n - 3, x, rows, :] = value
                values[n][x] = value
    write.wait()


def partner(i, step, count):
    if count & (count - 1) == 0:
        return i ^ step
    return (i - step + count) % count


def finish_kernel(devices, position, particular, response, *rest):
    reduced, (result, gathered, fluxes, out, sent) = rest[:devices], rest[devices:]
    width = particular.shape[1]
    here = position[0]
    for step, ref in zip([0, *exchange_order(devices)], reduced):
        source = sum(jnp.where(here == i, s, 0) for i, s in enumerate(sources_of(step, devices)))
        gathered[source] = ref[...]

    def part(device, i):
        return gathered[device, i * width : (i + 1) * width, :]

    pivots, sources = [], []
    for i in range(devices + 1):
        visc = [part(i - 1, 10)] if i > 0 else []
        total = [part(i - 1, 8)] if i > 0 else []
        source = [part(i - 1, 3 + c) for c in range(3)] if i > 0 else [0.0] * 3
        if i < devices:
            visc.append(part(i, 9))
            total.append(part(i, 6))
            source = [s - part(i, c) for c, s in enumerate(source)]
        pivots.append(sum(total) + 1.0 / (750.0 * sum(visc)))
        sources.append(source)
    across = [part(i, 7) for i in range(devices)]
    minors = [jnp.ones_like(pivots[0]), pivots[0]]
    for i in range(1, devices + 1):
        minors.append(pivots[i] * minors[i] - (across[i - 1] * across[i - 1]) * minors[i - 1])
    inverses = [minors[i] / minors[i + 1] for i in range(devices + 1)]
    ratios = [b * r for b, r in zip(across, inverses)]
    for i in range(1, devices + 1):
        sources[i] = [s + ratios[i - 1] * t for s, t in zip(sources[i], sources[i - 1])]
    for i in range(devices, -1, -1):
        flux_here = [inverses[i] * s for s in sources[i]]
        flux = flux_here if i == devices else [f + ratios[i] * g for f, g in zip(flux_here, flux)]
        for c in range(3):
            fluxes[i, c * width : (c + 1) * width, :] = flux[c]

    writes = []
    for c in range(3):
        for x in range(width):
            r = c * width + x
            left, right = fluxes[here, r : r + 1, :], fluxes[here + 1, r : r + 1, :]
            out[c, x] = particular[c, x] + (response[0, x] * left - response[1, x] * right)
            writes.append(pltpu.make_async_copy(out.at[c, x], result.at[c, x], sent.at[r]))
            writes[-1].start()
    for write in writes:
        write.wait()


def in_vmem(count):
    return [pl.BlockSpec(memory_space=pltpu.VMEM)] * count


def in_hbm(count):
    return [pl.BlockSpec(memory_space=pltpu.HBM)] * count


def in_smem(count):
    return [pl.BlockSpec(memory_space=pltpu.SMEM)] * count


def params():
    return pltpu.CompilerParams(vmem_limit_bytes=VMEM_BYTES)


def body(velocity, tendency):
    _, width, cells, lanes = velocity.shape
    nz_parts = lax.axis_size("gz")
    count = lax.axis_size("gx") * nz_parts
    walls = lax.axis_size("gy")
    rows = cells // count
    nx = lax.axis_size("gx") * width
    padded = 16 + aligned(rows)
    f32 = jnp.float32

    planes = 3 * width
    depth = aligned(planes * rows + 2 * aligned(planes))
    position = lax.axis_index("gy").astype(jnp.int32).reshape(1)
    parity = lax.rem(position, 2)
    chunks = pl.pallas_call(
        functools.partial(pack_kernel, rows),
        out_shape=jax.ShapeDtypeStruct((count, depth, lanes), f32),
        in_specs=in_smem(1) + in_vmem(1),
        out_specs=pl.BlockSpec(memory_space=pltpu.VMEM),
        compiler_params=params(),
        name="pack",
    )(parity, velocity)
    recv = lax.all_to_all(chunks, ("gx", "gz"), split_axis=0, concat_axis=0, tiled=True)
    slot = lax.slice_in_dim(recv, planes * rows, planes * rows + aligned(planes), axis=1)
    swapped = lax.ppermute(slot, ("gy", "gx", "gz"), swap_pairs(walls, count))
    rank = lax.axis_index(("gx", "gz")).astype(jnp.int32).reshape(1)
    chunk_shape = jax.ShapeDtypeStruct((count, width, rows, lanes), f32)
    cells_here = nx * nz_parts * rows * lanes
    provisional = pl.pallas_call(
        functools.partial(germano_kernel, nz_parts, width, rows),
        out_shape=chunk_shape,
        in_specs=in_smem(2) + in_vmem(1),
        out_specs=pl.BlockSpec(memory_space=pltpu.VMEM),
        scratch_shapes=[
            pltpu.VMEM((3, nx, nz_parts, padded, lanes), f32),
            pltpu.VMEM((3, nx, nz_parts, padded, lanes), f32),
            pltpu.VMEM((3, nx, nz_parts, 8, lanes), f32),
            pltpu.VMEM((nx, nz_parts, rows, lanes), f32),
            pltpu.VMEM((15, nx, nz_parts, rows, lanes), f32),
        ],
        compiler_params=params(),
        cost_estimate=pl.CostEstimate(
            flops=300 * cells_here, bytes_accessed=16 * cells_here, transcendentals=2 * cells_here
        ),
        name="germano",
    )(rank, parity, recv)
    eddy_chunks = pl.pallas_call(
        functools.partial(edge_kernel, nz_parts, width, rows, walls),
        out_shape=chunk_shape,
        in_specs=in_smem(2) + in_vmem(3),
        out_specs=pl.BlockSpec(memory_space=pltpu.VMEM),
        scratch_shapes=[pltpu.VMEM((3, 3, nx, nz_parts * lanes), f32)],
        input_output_aliases={4: 0},
        compiler_params=params(),
        name="edge",
    )(rank, position, recv, swapped, provisional)
    back = lax.all_to_all(eddy_chunks, ("gx", "gz"), split_axis=0, concat_axis=0, tiled=True)

    length = cells // SEGMENTS
    levels = SEGMENTS.bit_length() - 1
    packed = aligned(11 * width)
    eddy_here, reduced, factors, tree = pl.pallas_call(
        sweep_kernel,
        out_shape=(
            jax.ShapeDtypeStruct((width, cells, lanes), f32),
            jax.ShapeDtypeStruct((packed, lanes), f32),
            jax.ShapeDtypeStruct((width, length, 5, SEGMENTS, lanes), f32),
            jax.ShapeDtypeStruct((width, levels, 5, SEGMENTS, lanes), f32),
        ),
        in_specs=in_smem(1) + in_vmem(3),
        out_specs=tuple(in_vmem(4)),
        compiler_params=params(),
        name="sweep",
    )(parity, back, velocity, tendency)

    others = [
        lax.ppermute(reduced, "gy", [(s, i) for i, s in enumerate(sources_of(step, walls))])
        for step in exchange_order(walls)
    ]
    particular, response, eddy = pl.pallas_call(
        spread_kernel,
        out_shape=(
            jax.ShapeDtypeStruct(velocity.shape, f32),
            jax.ShapeDtypeStruct((2, *velocity.shape[1:]), f32),
            jax.ShapeDtypeStruct(eddy_here.shape, f32),
        ),
        in_specs=in_vmem(4),
        out_specs=tuple(in_vmem(2) + in_hbm(1)),
        scratch_shapes=[pltpu.SemaphoreType.DMA],
        compiler_params=params(),
        cost_estimate=pl.CostEstimate(
            flops=20 * velocity.size, bytes_accessed=16 * velocity.size, transcendentals=0
        ),
        name="spread",
    )(factors, tree, velocity, eddy_here)
    new_velocity = pl.pallas_call(
        functools.partial(finish_kernel, walls),
        out_shape=jax.ShapeDtypeStruct(velocity.shape, f32),
        in_specs=in_smem(1) + in_vmem(2 + walls),
        out_specs=in_hbm(1)[0],
        scratch_shapes=[
            pltpu.VMEM((walls, packed, lanes), f32),
            pltpu.VMEM((walls + 1, aligned(3 * width), lanes), f32),
            pltpu.VMEM(velocity.shape, f32),
            pltpu.SemaphoreType.DMA((planes,)),
        ],
        compiler_params=params(),
        name="finish",
    )(position, particular, response, reduced, *others)
    return (new_velocity, eddy)


def solution(mesh):
    return jax.shard_map(
        body,
        mesh=mesh,
        in_specs=(P(None, "gx", "gy", "gz"), P(None, "gx", "gy", "gz")),
        out_specs=(P(None, "gx", "gy", "gz"), P("gx", "gy", "gz")),
        check_vma=False,
    )
```

```python
import functools

import jax
import jax.numpy as jnp
from jax import lax
from jax.experimental import pallas as pl
from jax.experimental.pallas import tpu as pltpu
from jax.sharding import PartitionSpec as P

LANES = 128
SEGMENTS = 8
VMEM_BYTES = 24 * 2**20


def strain_parts(grad_x, grad_y, grad_z):
    return (
        grad_x[0],
        grad_y[1],
        grad_z[2],
        grad_y[0] + grad_x[1],
        grad_z[0] + grad_x[2],
        grad_z[1] + grad_y[2],
    )


def strain_size(parts):
    diagonal = parts[0] * parts[0] + parts[1] * parts[1] + parts[2] * parts[2]
    mixed = parts[3] * parts[3] + parts[4] * parts[4] + parts[5] * parts[5]
    return jnp.sqrt(0.5 * diagonal + 0.25 * mixed)


def beside(blocks):
    count = len(blocks)
    lanes = blocks[0].shape[1]
    down = [pltpu.roll(f, 1, 1) for f in blocks]
    up = [pltpu.roll(f, lanes - 1, 1) for f in blocks]
    if count > 1:
        lane = lax.broadcasted_iota(jnp.int32, blocks[0].shape, 1)
        first, last = lane == 0, lane == lanes - 1
        down, up = (
            [jnp.where(first, down[i - 1], down[i]) for i in range(count)],
            [jnp.where(last, up[(i + 1) % count], up[i]) for i in range(count)],
        )
    return down, up


def slope_z(blocks):
    down, up = beside(blocks)
    return [u - d for u, d in zip(up, down)]


def smooth_z(blocks):
    down, up = beside(blocks)
    return [(u + d) + 2.0 * f for f, u, d in zip(blocks, up, down)]


def products(v):
    return (v[0] * v[0], v[1] * v[1], v[2] * v[2], v[0] * v[1], v[0] * v[2], v[1] * v[2])


def outer_ranks(count):
    return (count - 1, count - 3)


def places(parity, count):
    outer = outer_ranks(count)
    inner = iter(range(1, count - 1))
    return [
        (0 if outer[parity] == rank else count - 1) if rank in outer else next(inner)
        for rank in range(count)
    ]


def swap_pairs(walls, count):
    odd, even = outer_ranks(count)
    spare = count - 5
    partners = {}

    def join(a, b):
        partners[a], partners[b] = b, a

    def join_walls(rank, first):
        for wall in range(first, walls - 1, 2):
            join((wall, rank), (wall + 1, rank))

    join_walls(even, 0)
    join_walls(odd, 1)
    join_walls(spare, 1)
    join((0, odd), (0, spare))
    if walls % 2 == 0:
        join((walls - 1, odd), (walls - 1, spare))
    others = [r for r in range(count) if r not in (odd, even, spare)]
    for core in range(2):
        ranks = [r for r in others if r % 2 == core]
        half = len(ranks) // 2
        for wall in range(walls):
            for a, b in zip(ranks[:half], ranks[half : 2 * half]):
                join((wall, a), (wall, b))
        for rank in ranks[2 * half :]:
            join_walls(rank, 0)
    return [
        (wall * count + rank, to[0] * count + to[1])
        for wall in range(walls)
        for rank in range(count)
        for to in [partners.get((wall, rank), (wall, rank))]
    ]


def by_parity(parity, count, fill):
    outer = outer_ranks(count)
    for rank, place in enumerate(places(0, count)):
        if rank not in outer:
            fill(rank, place)
    for turn in range(2):

        @pl.when(parity[0] == turn)
        def _():
            for rank in outer:
                fill(rank, places(turn, count)[rank])


def aligned(n):
    return -(-n // 8) * 8


def pack_kernel(rows, parity, velocity, out):
    _, width, cells, _ = velocity.shape
    count, depth, lanes = out.shape
    planes = 3 * width
    slots = planes * rows

    def fill(rank, place):
        first = place * rows
        beside = [first - 1, first + rows]
        if place == 0:
            beside = [first, first + rows]
        if place == count - 1:
            beside = [first + rows - 1, first - 1]
        for i in range(planes):
            c, x = divmod(i, width)
            out[rank, i * rows : (i + 1) * rows, :] = velocity[c, x, first : first + rows, :]
            for slot, row in enumerate(beside):
                at = slots + slot * aligned(planes) + i
                out[rank, at : at + 1, :] = velocity[c, x, row : row + 1, :]

    by_parity(parity, count, fill)
    blank = aligned(planes) - planes
    for rank in range(count):
        for slot in range(2):
            at = slots + slot * aligned(planes) + planes
            out[rank, at : at + blank, :] = jnp.zeros((blank, lanes), jnp.float32)
        at = slots + 2 * aligned(planes)
        if at < depth:
            out[rank, at:, :] = jnp.zeros((depth - at, lanes), jnp.float32)


def outer_sides(rank, parity, count):
    outer = outer_ranks(count)
    even = parity[0] == 0
    bottom = rank[0] == jnp.where(even, outer[0], outer[1])
    top = rank[0] == jnp.where(even, outer[1], outer[0])
    return bottom, top


def edge_kernel(nz_parts, width, rows, walls, rank, position, recv, swapped, given, out, vel):
    count, _, lanes = recv.shape
    planes = 3 * width
    nx = (count // nz_parts) * width
    nz = nz_parts * lanes
    bottom, top = outer_sides(rank, [lax.rem(position[0], 2)], count)
    at_wall = jnp.logical_or(
        jnp.logical_and(bottom, position[0] == 0), jnp.logical_and(top, position[0] == walls - 1)
    )

    def rows_of(k, i):
        first = i * rows
        own = [recv[k, first + j : first + j + 1, :] for j in (0, 1, rows - 2, rows - 1)]
        far = jnp.where(at_wall, 0.0, swapped[k, i : i + 1, :])
        return (
            jnp.where(bottom, far, own[2]),
            jnp.where(bottom, own[0], own[3]),
            jnp.where(bottom, own[1], far),
        )

    def roll_x(f, shift):
        return pltpu.roll(f, shift % nx, 0)

    def roll_z(f, shift):
        return pltpu.roll(f, shift % nz, 1)

    def smooth_x(f):
        return (roll_x(f, 1) + roll_x(f, -1)) + 2.0 * f

    def smooth(f):
        f = smooth_x(f)
        return (roll_z(f, 1) + roll_z(f, -1)) + 2.0 * f

    def slopes(below, centre, above):
        return strain_parts(
            [roll_x(f, -1) - roll_x(f, 1) for f in centre],
            [a - b for a, b in zip(above, below)],
            [roll_z(f, -1) - roll_z(f, 1) for f in centre],
        )

    @pl.when(jnp.logical_or(bottom, top))
    def _():
        for k in range(count):
            x0, zb = (k // nz_parts) * width, k % nz_parts
            for i in range(planes):
                c, x = divmod(i, width)
                for j, row in enumerate(rows_of(k, i)):
                    vel[j, c, x0 + x : x0 + x + 1, zb * lanes : (zb + 1) * lanes] = row
        u = [[vel[j, c] for c in range(3)] for j in range(3)]
        v = [[smooth(f) for f in row] for row in u]
        strain = slopes(*u)
        size = strain_size(strain)
        mean_strain = slopes(*v)
        mean_size = 0.25 * strain_size(mean_strain)
        scaled = [0.0625 * f for f in v[1]]
        pairs = [v[1][i] * scaled[j] for i, j in ((0, 0), (1, 1), (2, 2), (0, 1), (0, 2), (1, 2))]
        leonard = [smooth(p) - q for p, q in zip(products(u[1]), pairs)]
        model = [smooth(size * s) - mean_size * f for s, f in zip(strain, mean_strain)]
        lm, mm = contracted(leonard, model)
        coefficient = coefficient_of(
            *(jnp.sum(f, axis=(0, 1), keepdims=True) for f in (lm, mm)), nx * nz
        )
        eddy = coefficient * size

        def put(at):
            for k in range(count):
                x0, zb = (k // nz_parts) * width, k % nz_parts
                for x in range(width):
                    out[k, x, at : at + 1, :] = eddy[x0 + x : x0 + x + 1, zb * lanes : (zb + 1) * lanes]

        pl.when(bottom)(lambda: put(0))
        pl.when(top)(lambda: put(rows - 1))


def contracted(leonard, model):
    lm = mm = None
    for i in range(6):
        square = model[i] * model[i] if i < 3 else (0.5 * model[i]) * model[i]
        product = leonard[i] * model[i]
        lm = product if lm is None else lm + product
        mm = square if mm is None else mm + square
    return lm, mm


def coefficient_of(plane_lm, plane_mm, cells):
    scale = 1.0 / (256.0 * cells)
    return jnp.maximum(plane_lm * scale / (plane_mm * scale + 1e-06), 0.0)


def germano_kernel(nz_parts, width, rows, rank, parity, recv, out, vel, filt, ends, mag, part):
    count, _, lanes = recv.shape
    planes = 3 * width
    _, top = outer_sides(rank, parity, count)
    nx = (count // nz_parts) * width
    nz = nz_parts * lanes
    blocks = range(nz_parts)
    lead = 8
    inner = slice(lead, lead + rows)
    for k in range(count):
        x0, zb = (k // nz_parts) * width, k % nz_parts
        for c in range(3):
            for x in range(width):
                i = c * width + x
                vel[c, x0 + x, zb, inner, :] = recv[k, i * rows : (i + 1) * rows, :]
                slots = planes * rows + i
                near = recv[k, slots : slots + 1, :]
                slots += aligned(planes)
                other = recv[k, slots : slots + 1, :]
                below = jnp.where(top, other, near)
                for side, (edge, at) in enumerate(((below, lead - 1), (other, lead + rows))):
                    vel[c, x0 + x, zb, at : at + 1, :] = edge
                    ends[c, x0 + x, zb, side : side + 1, :] = edge

    tile = min(rows, 8)
    tiles = [slice(t, t + tile) for t in range(0, rows, tile)]

    def moved(own, by):
        return slice(lead + own.start + by, lead + own.stop + by)

    for x, own in [(x, own) for x in range(nx) for own in tiles]:
        left, right = (x - 1) % nx, (x + 1) % nx
        inner, lower, upper = (moved(own, by) for by in (0, -1, 1))
        centre = [[vel[c, x, zb, inner, :] for zb in blocks] for c in range(3)]
        grad_x = [[vel[c, right, zb, inner, :] - vel[c, left, zb, inner, :] for zb in blocks] for c in range(3)]
        grad_y = [[vel[c, x, zb, upper, :] - vel[c, x, zb, lower, :] for zb in blocks] for c in range(3)]
        grad_z = []
        for c in range(3):
            down, up = beside(centre[c])
            grad_z.append([u - d for u, d in zip(up, down)])
            for zb in blocks:
                part[c, x, zb, own, :] = (up[zb] + down[zb]) + 2.0 * centre[c][zb]
        strain = [
            strain_parts(*([g[c][zb] for c in range(3)] for g in (grad_x, grad_y, grad_z)))
            for zb in blocks
        ]
        size = [strain_size(s) for s in strain]
        for zb in blocks:
            mag[x, zb, own, :] = size[zb]
        pairs = [products([centre[c][zb] for c in range(3)]) for zb in blocks]
        for i in range(6):
            for base, fields in (
                (3, [pairs[zb][i] for zb in blocks]),
                (9, [size[zb] * strain[zb][i] for zb in blocks]),
            ):
                for zb, f in enumerate(smooth_z(fields)):
                    part[base + i, x, zb, own, :] = f

    def smooth_x(read, x):
        return (read((x - 1) % nx) + read((x + 1) % nx)) + 2.0 * read(x)

    for c in range(3):
        rims = []
        for x in range(nx):
            rims.append(smooth_z([ends[c, x, zb] for zb in blocks]))
        for x in range(nx):
            for zb in blocks:
                rim = smooth_x(lambda at: rims[at][zb], x)
                filt[c, x, zb, lead - 1 : lead, :] = rim[0:1, :]
                filt[c, x, zb, lead + rows : lead + rows + 1, :] = rim[1:2, :]
                for own in tiles:
                    filt[c, x, zb, moved(own, 0), :] = smooth_x(lambda at: part[c, at, zb, own, :], x)

    sums = [[None, None] for _ in tiles]
    for x, n in [(x, n) for x in range(nx) for n in range(len(tiles))]:
        own = tiles[n]
        left, right = (x - 1) % nx, (x + 1) % nx
        inner, lower, upper = (moved(own, by) for by in (0, -1, 1))
        mean = [[filt[c, x, zb, inner, :] for zb in blocks] for c in range(3)]
        grad_x = [[filt[c, right, zb, inner, :] - filt[c, left, zb, inner, :] for zb in blocks] for c in range(3)]
        grad_y = [[filt[c, x, zb, upper, :] - filt[c, x, zb, lower, :] for zb in blocks] for c in range(3)]
        grad_z = [slope_z(mean[c]) for c in range(3)]
        for zb in blocks:
            strain = strain_parts(*([g[c][zb] for c in range(3)] for g in (grad_x, grad_y, grad_z)))
            size = 0.25 * strain_size(strain)
            v = [mean[c][zb] for c in range(3)]
            scaled = [0.0625 * f for f in v]
            pairs = [v[i] * scaled[j] for i, j in ((0, 0), (1, 1), (2, 2), (0, 1), (0, 2), (1, 2))]
            leonard = [smooth_x(lambda at: part[3 + i, at, zb, own, :], x) - pairs[i] for i in range(6)]
            model = [smooth_x(lambda at: part[9 + i, at, zb, own, :], x) - size * strain[i] for i in range(6)]
            totals = contracted(leonard, model)
            sums[n] = [f if s is None else s + f for s, f in zip(sums[n], totals)]

    for own, totals in zip(tiles, sums):
        coefficient = coefficient_of(
            *(jnp.sum(total, axis=1, keepdims=True) for total in totals), nx * nz
        )
        for k in range(count):
            x0, zb = (k // nz_parts) * width, k % nz_parts
            for x in range(width):
                out[k, x, own, :] = coefficient * mag[x0 + x, zb, own, :]


def sweep_kernel(parity, back, velocity, tendency, eddy, reduced, factors, tree):
    count, width, rows, _ = back.shape
    length = count * rows // SEGMENTS

    def fill(rank, place):
        for x in range(width):
            eddy[x, place * rows : (place + 1) * rows, :] = back[rank, x]

    by_parity(parity, count, fill)

    def row(ref, index, j):
        return ref[(*index, pl.ds(j, SEGMENTS, stride=length), slice(None))]

    planes = range(width)
    last_row = length - 1
    visc = [[1.0 + row(eddy, (x,), j) for x in planes] for j in range(length)]
    links = [[750.0 * (v + w) for v, w in zip(visc[j], visc[j + 1])] for j in range(last_row)]

    over = [jnp.ones_like(v) for v in visc[0]]
    under = [jnp.ones_like(v) for v in visc[0]]
    inverses = []
    for j in range(last_row):
        inverses.append([u / (o + e * u) for o, u, e in zip(over, under, links[j])])
        steps = [o * (1.0 / e) for o, e in zip(over, links[j])]
        under, over = (
            [u + t for u, t in zip(under, steps)],
            [(o + u) + t for o, u, t in zip(over, under, steps)],
        )
    inverses.append([u / o for o, u in zip(over, under)])

    value = first = corner = left = None
    reach = [jnp.ones_like(v) for v in visc[0]]
    for j in range(length):
        inverse = inverses[j]
        before = value
        source = [[2.0 * row(velocity, (c, x), j) + row(tendency, (c, x), j) for x in planes] for c in range(3)]
        value = [[f * r for f, r in zip(source[c], inverse)] for c in range(3)]
        if j > 0:
            carry = [e * r for e, r in zip(links[j - 1], inverse)]
            value = [[v + k * w for v, k, w in zip(value[c], carry, before[c])] for c in range(3)]
        left = [m * r for m, r in zip(reach, inverse)]
        if j == 0:
            first, corner = value, left
        else:
            first = [[f + m * v for f, m, v in zip(first[c], reach, value[c])] for c in range(3)]
            corner = [a + m * v for a, m, v in zip(corner, reach, left)]
        ratio = inverse
        if j < last_row:
            ratio = [e * r for e, r in zip(links[j], inverse)]
            reach = [m * r for m, r in zip(reach, ratio)]
        for x in planes:
            for c in range(3):
                factors[x, j, c] = value[c][x]
            factors[x, j, 3] = left[x]
            factors[x, j, 4] = ratio[x]

    def other(fields, step):
        return [pltpu.roll(f, (SEGMENTS - step) % SEGMENTS, 0) if step else f for f in fields]

    last, across, end = value, left, inverse
    seams = [750.0 * (v + w) for v, w in zip(visc[last_row], other(visc[0], 1))]
    level, step = 0, 1
    while step < SEGMENTS:
        link = other(seams, step - 1)
        first_b = [other(f, step) for f in first]
        last_b = [other(f, step) for f in last]
        corner_b, end_b, across_b = other(corner, step), other(end, step), other(across, step)
        stiff = [e / (1.0 + e * (d + a)) for e, d, a in zip(link, end, corner_b)]
        flux = [[k * (g - f) for k, g, f in zip(stiff, last[c], first_b[c])] for c in range(3)]
        from_left = [k * b for k, b in zip(stiff, across)]
        from_right = [k * b for k, b in zip(stiff, across_b)]
        for x in planes:
            for c in range(3):
                tree[x, level, c] = flux[c][x]
            tree[x, level, 3] = from_left[x]
            tree[x, level, 4] = from_right[x]
        first = [[f - b * t for f, b, t in zip(first[c], across, flux[c])] for c in range(3)]
        last = [[g + b * t for g, b, t in zip(last_b[c], across_b, flux[c])] for c in range(3)]
        corner = [a - b * k for a, b, k in zip(corner, across, from_left)]
        end = [d - b * k for d, b, k in zip(end_b, across_b, from_right)]
        across = [k * b for k, b in zip(from_left, across_b)]
        level, step = level + 1, step * 2
    for x in planes:
        rows_out = [f[x][0:1, :] for f in (*first, *last, corner, across, end, visc[0])]
        rows_out.append(visc[last_row][x][SEGMENTS - 1 :, :])
        for i, v in enumerate(rows_out):
            reduced[i * width + x : i * width + x + 1, :] = v


def spread_kernel(factors, tree, velocity, eddy, particular, response, eddy_out, sent):
    write = pltpu.make_async_copy(eddy, eddy_out, sent)
    write.start()
    width, length = factors.shape[:2]
    levels = tree.shape[1]
    sublane = lax.broadcasted_iota(jnp.int32, (SEGMENTS, LANES), 0)
    one, zero = (jnp.full((SEGMENTS, LANES), v, jnp.float32) for v in (1.0, 0.0))
    sides = [(c, zero, zero) for c in range(3)] + [(None, one, zero), (None, zero, one)]
    lefts = [[side[1]] * width for side in sides]
    rights = [[side[2]] * width for side in sides]
    for level in range(levels - 1, -1, -1):
        step = 2**level
        second = lax.rem(sublane, 2 * step) == step
        for n, (c, _, _) in enumerate(sides):
            for x in range(width):
                left, right = lefts[n][x], rights[n][x]
                through = tree[x, level, 3] * left - tree[x, level, 4] * right
                if c is not None:
                    through = tree[x, level, c] + through
                lefts[n][x] = jnp.where(second, pltpu.roll(through, step, 0), left)
                rights[n][x] = jnp.where(second, pltpu.roll(right, step, 0), -through)
    values = rights
    for j in range(length - 1, -1, -1):
        rows = pl.ds(j, SEGMENTS, stride=length)
        for n, (c, _, _) in enumerate(sides):
            for x in range(width):
                value = factors[x, j, 3] * lefts[n][x] + factors[x, j, 4] * values[n][x]
                if c is not None:
                    value = factors[x, j, c] + value
                    particular[c, x, rows, :] = value - velocity[c, x, rows, :]
                else:
                    response[n - 3, x, rows, :] = value
                values[n][x] = value
    write.wait()


def sources_of(step, count):
    ring = [0, *range(1, count, 2), *range(count - 2 + count % 2, 0, -2)]
    return [ring[(ring.index(i) - step) % count] for i in range(count)]


def exchange_order(count):
    return range(count - 1, 0, -1)


def spread_kernel(factors, tree, velocity, eddy, particular, response, eddy_out, sent):
    write = pltpu.make_async_copy(eddy, eddy_out, sent)
    write.start()
    width, length = factors.shape[:2]
    levels = tree.shape[1]
    sublane = lax.broadcasted_iota(jnp.int32, (SEGMENTS, LANES), 0)
    one, zero = (jnp.full((SEGMENTS, LANES), v, jnp.float32) for v in (1.0, 0.0))
    sides = [(c, zero, zero) for c in range(3)] + [(None, one, zero), (None, zero, one)]
    lefts = [[side[1]] * width for side in sides]
    rights = [[side[2]] * width for side in sides]
    for level in range(levels - 1, -1, -1):
        step = 2**level
        second = lax.rem(sublane, 2 * step) == step
        for n, (c, _, _) in enumerate(sides):
            for x in range(width):
                left, right = lefts[n][x], rights[n][x]
                through = tree[x, level, 3] * left - tree[x, level, 4] * right
                if c is not None:
                    through = tree[x, level, c] + through
                lefts[n][x] = jnp.where(second, pltpu.roll(through, step, 0), left)
                rights[n][x] = jnp.where(second, pltpu.roll(right, step, 0), -through)
    values = rights
    for j in range(length - 1, -1, -1):
        rows = pl.ds(j, SEGMENTS, stride=length)
        for n, (c, _, _) in enumerate(sides):
            for x in range(width):
                value = factors[x, j, 3] * lefts[n][x] + factors[x, j, 4] * values[n][x]
                if c is not None:
                    value = factors[x, j, c] + value
                    particular[c, x, rows, :] = value - velocity[c, x, rows, :]
                else:
                    response[n - 3, x, rows, :] = value
                values[n][x] = value
    write.wait()


def partner(i, step, count):
    if count & (count - 1) == 0:
        return i ^ step
    return (i - step + count) % count


def finish_kernel(devices, position, particular, response, *rest):
    reduced, (result, gathered, fluxes, out, sent) = rest[:devices], rest[devices:]
    width = particular.shape[1]
    here = position[0]
    for step, ref in zip([0, *exchange_order(devices)], reduced):
        source = sum(jnp.where(here == i, s, 0) for i, s in enumerate(sources_of(step, devices)))
        gathered[source] = ref[...]

    def part(device, i):
        return gathered[device, i * width : (i + 1) * width, :]

    pivots, sources = [], []
    for i in range(devices + 1):
        visc = [part(i - 1, 10)] if i > 0 else []
        total = [part(i - 1, 8)] if i > 0 else []
        source = [part(i - 1, 3 + c) for c in range(3)] if i > 0 else [0.0] * 3
        if i < devices:
            visc.append(part(i, 9))
            total.append(part(i, 6))
            source = [s - part(i, c) for c, s in enumerate(source)]
        pivots.append(sum(total) + 1.0 / (750.0 * sum(visc)))
        sources.append(source)
    across = [part(i, 7) for i in range(devices)]
    minors = [jnp.ones_like(pivots[0]), pivots[0]]
    for i in range(1, devices + 1):
        minors.append(pivots[i] * minors[i] - (across[i - 1] * across[i - 1]) * minors[i - 1])
    inverses = [minors[i] / minors[i + 1] for i in range(devices + 1)]
    ratios = [b * r for b, r in zip(across, inverses)]
    for i in range(1, devices + 1):
        sources[i] = [s + ratios[i - 1] * t for s, t in zip(sources[i], sources[i - 1])]
    for i in range(devices, -1, -1):
        flux_here = [inverses[i] * s for s in sources[i]]
        flux = flux_here if i == devices else [f + ratios[i] * g for f, g in zip(flux_here, flux)]
        for c in range(3):
            fluxes[i, c * width : (c + 1) * width, :] = flux[c]

    writes = []
    for c in range(3):
        for x in range(width):
            r = c * width + x
            left, right = fluxes[here, r : r + 1, :], fluxes[here + 1, r : r + 1, :]
            out[c, x] = particular[c, x] + (response[0, x] * left - response[1, x] * right)
            writes.append(pltpu.make_async_copy(out.at[c, x], result.at[c, x], sent.at[r]))
            writes[-1].start()
    for write in writes:
        write.wait()


def in_vmem(count):
    return [pl.BlockSpec(memory_space=pltpu.VMEM)] * count


def in_hbm(count):
    return [pl.BlockSpec(memory_space=pltpu.HBM)] * count


def in_smem(count):
    return [pl.BlockSpec(memory_space=pltpu.SMEM)] * count


def params():
    return pltpu.CompilerParams(vmem_limit_bytes=VMEM_BYTES)


def body(velocity, tendency):
    _, width, cells, lanes = velocity.shape
    nz_parts = lax.axis_size("gz")
    count = lax.axis_size("gx") * nz_parts
    walls = lax.axis_size("gy")
    rows = cells // count
    nx = lax.axis_size("gx") * width
    padded = 16 + aligned(rows)
    f32 = jnp.float32

    planes = 3 * width
    depth = aligned(planes * rows + 2 * aligned(planes))
    position = lax.axis_index("gy").astype(jnp.int32).reshape(1)
    parity = lax.rem(position, 2)
    chunks = pl.pallas_call(
        functools.partial(pack_kernel, rows),
        out_shape=jax.ShapeDtypeStruct((count, depth, lanes), f32),
        in_specs=in_smem(1) + in_vmem(1),
        out_specs=pl.BlockSpec(memory_space=pltpu.VMEM),
        compiler_params=params(),
        name="pack",
    )(parity, velocity)
    recv = lax.all_to_all(chunks, ("gx", "gz"), split_axis=0, concat_axis=0, tiled=True)
    slot = lax.slice_in_dim(recv, planes * rows, planes * rows + aligned(planes), axis=1)
    swapped = lax.ppermute(slot, ("gy", "gx", "gz"), swap_pairs(walls, count))
    rank = lax.axis_index(("gx", "gz")).astype(jnp.int32).reshape(1)
    chunk_shape = jax.ShapeDtypeStruct((count, width, rows, lanes), f32)
    cells_here = nx * nz_parts * rows * lanes
    provisional = pl.pallas_call(
        functools.partial(germano_kernel, nz_parts, width, rows),
        out_shape=chunk_shape,
        in_specs=in_smem(2) + in_vmem(1),
        out_specs=pl.BlockSpec(memory_space=pltpu.VMEM),
        scratch_shapes=[
            pltpu.VMEM((3, nx, nz_parts, padded, lanes), f32),
            pltpu.VMEM((3, nx, nz_parts, padded, lanes), f32),
            pltpu.VMEM((3, nx, nz_parts, 8, lanes), f32),
            pltpu.VMEM((nx, nz_parts, rows, lanes), f32),
            pltpu.VMEM((15, nx, nz_parts, rows, lanes), f32),
        ],
        compiler_params=params(),
        cost_estimate=pl.CostEstimate(
            flops=300 * cells_here, bytes_accessed=16 * cells_here, transcendentals=2 * cells_here
        ),
        name="germano",
    )(rank, parity, recv)
    eddy_chunks = pl.pallas_call(
        functools.partial(edge_kernel, nz_parts, width, rows, walls),
        out_shape=chunk_shape,
        in_specs=in_smem(2) + in_vmem(3),
        out_specs=pl.BlockSpec(memory_space=pltpu.VMEM),
        scratch_shapes=[pltpu.VMEM((3, 3, nx, nz_parts * lanes), f32)],
        input_output_aliases={4: 0},
        compiler_params=params(),
        name="edge",
    )(rank, position, recv, swapped, provisional)
    back = lax.all_to_all(eddy_chunks, ("gx", "gz"), split_axis=0, concat_axis=0, tiled=True)

    length = cells // SEGMENTS
    levels = SEGMENTS.bit_length() - 1
    packed = aligned(11 * width)
    eddy_here, reduced, factors, tree = pl.pallas_call(
        sweep_kernel,
        out_shape=(
            jax.ShapeDtypeStruct((width, cells, lanes), f32),
            jax.ShapeDtypeStruct((packed, lanes), f32),
            jax.ShapeDtypeStruct((width, length, 5, SEGMENTS, lanes), f32),
            jax.ShapeDtypeStruct((width, levels, 5, SEGMENTS, lanes), f32),
        ),
        in_specs=in_smem(1) + in_vmem(3),
        out_specs=tuple(in_vmem(4)),
        compiler_params=params(),
        name="sweep",
    )(parity, back, velocity, tendency)

    others = [
        lax.ppermute(reduced, "gy", [(s, i) for i, s in enumerate(sources_of(step, walls))])
        for step in exchange_order(walls)
    ]
    particular, response, eddy = pl.pallas_call(
        spread_kernel,
        out_shape=(
            jax.ShapeDtypeStruct(velocity.shape, f32),
            jax.ShapeDtypeStruct((2, *velocity.shape[1:]), f32),
            jax.ShapeDtypeStruct(eddy_here.shape, f32),
        ),
        in_specs=in_vmem(4),
        out_specs=tuple(in_vmem(2) + in_hbm(1)),
        scratch_shapes=[pltpu.SemaphoreType.DMA],
        compiler_params=params(),
        cost_estimate=pl.CostEstimate(
            flops=20 * velocity.size, bytes_accessed=16 * velocity.size, transcendentals=0
        ),
        name="spread",
    )(factors, tree, velocity, eddy_here)
    new_velocity = pl.pallas_call(
        functools.partial(finish_kernel, walls),
        out_shape=jax.ShapeDtypeStruct(velocity.shape, f32),
        in_specs=in_smem(1) + in_vmem(2 + walls),
        out_specs=in_hbm(1)[0],
        scratch_shapes=[
            pltpu.VMEM((walls, packed, lanes), f32),
            pltpu.VMEM((walls + 1, aligned(3 * width), lanes), f32),
            pltpu.VMEM(velocity.shape, f32),
            pltpu.SemaphoreType.DMA((planes,)),
        ],
        compiler_params=params(),
        name="finish",
    )(position, particular, response, reduced, *others)
    return (new_velocity, eddy)


def solution(mesh):
    return jax.shard_map(
        body,
        mesh=mesh,
        in_specs=(P(None, "gx", "gy", "gz"), P(None, "gx", "gy", "gz")),
        out_specs=(P(None, "gx", "gy", "gz"), P("gx", "gy", "gz")),
        check_vma=False,
    )
```

```python
import functools

import jax
import jax.numpy as jnp
from jax import lax
from jax.experimental import pallas as pl
from jax.experimental.pallas import tpu as pltpu
from jax.sharding import PartitionSpec as P

LANES = 128
SEGMENTS = 8
VMEM_BYTES = 24 * 2**20


def strain_parts(grad_x, grad_y, grad_z):
    return (
        grad_x[0],
        grad_y[1],
        grad_z[2],
        grad_y[0] + grad_x[1],
        grad_z[0] + grad_x[2],
        grad_z[1] + grad_y[2],
    )


def strain_size(parts):
    diagonal = parts[0] * parts[0] + parts[1] * parts[1] + parts[2] * parts[2]
    mixed = parts[3] * parts[3] + parts[4] * parts[4] + parts[5] * parts[5]
    return jnp.sqrt(0.5 * diagonal + 0.25 * mixed)


def beside(blocks):
    count = len(blocks)
    lanes = blocks[0].shape[1]
    down = [pltpu.roll(f, 1, 1) for f in blocks]
    up = [pltpu.roll(f, lanes - 1, 1) for f in blocks]
    if count > 1:
        lane = lax.broadcasted_iota(jnp.int32, blocks[0].shape, 1)
        first, last = lane == 0, lane == lanes - 1
        down, up = (
            [jnp.where(first, down[i - 1], down[i]) for i in range(count)],
            [jnp.where(last, up[(i + 1) % count], up[i]) for i in range(count)],
        )
    return down, up


def slope_z(blocks):
    down, up = beside(blocks)
    return [u - d for u, d in zip(up, down)]


def smooth_z(blocks):
    down, up = beside(blocks)
    return [(u + d) + 2.0 * f for f, u, d in zip(blocks, up, down)]


def products(v):
    return (v[0] * v[0], v[1] * v[1], v[2] * v[2], v[0] * v[1], v[0] * v[2], v[1] * v[2])


def outer_ranks(count):
    return (count - 1, count - 3)


def places(parity, count):
    outer = outer_ranks(count)
    inner = iter(range(1, count - 1))
    return [
        (0 if outer[parity] == rank else count - 1) if rank in outer else next(inner)
        for rank in range(count)
    ]


def swap_pairs(walls, count):
    odd, even = outer_ranks(count)
    spare = count - 5
    partners = {}

    def join(a, b):
        partners[a], partners[b] = b, a

    def join_walls(rank, first):
        for wall in range(first, walls - 1, 2):
            join((wall, rank), (wall + 1, rank))

    join_walls(even, 0)
    join_walls(odd, 1)
    join_walls(spare, 1)
    join((0, odd), (0, spare))
    if walls % 2 == 0:
        join((walls - 1, odd), (walls - 1, spare))
    others = [r for r in range(count) if r not in (odd, even, spare)]
    for core in range(2):
        ranks = [r for r in others if r % 2 == core]
        half = len(ranks) // 2
        for wall in range(walls):
            for a, b in zip(ranks[:half], ranks[half : 2 * half]):
                join((wall, a), (wall, b))
        for rank in ranks[2 * half :]:
            join_walls(rank, 0)
    return [
        (wall * count + rank, to[0] * count + to[1])
        for wall in range(walls)
        for rank in range(count)
        for to in [partners.get((wall, rank), (wall, rank))]
    ]


def by_parity(parity, count, fill):
    outer = outer_ranks(count)
    for rank, place in enumerate(places(0, count)):
        if rank not in outer:
            fill(rank, place)
    for turn in range(2):

        @pl.when(parity[0] == turn)
        def _():
            for rank in outer:
                fill(rank, places(turn, count)[rank])


def aligned(n):
    return -(-n // 8) * 8


def pack_kernel(rows, parity, velocity, out):
    _, width, cells, _ = velocity.shape
    count, depth, lanes = out.shape
    planes = 3 * width
    slots = planes * rows

    def fill(rank, place):
        first = place * rows
        beside = [first - 1, first + rows]
        if place == 0:
            beside = [first, first + rows]
        if place == count - 1:
            beside = [first + rows - 1, first - 1]
        for i in range(planes):
            c, x = divmod(i, width)
            out[rank, i * rows : (i + 1) * rows, :] = velocity[c, x, first : first + rows, :]
            for slot, row in enumerate(beside):
                at = slots + slot * aligned(planes) + i
                out[rank, at : at + 1, :] = velocity[c, x, row : row + 1, :]

    by_parity(parity, count, fill)
    blank = aligned(planes) - planes
    for rank in range(count):
        for slot in range(2):
            at = slots + slot * aligned(planes) + planes
            out[rank, at : at + blank, :] = jnp.zeros((blank, lanes), jnp.float32)
        at = slots + 2 * aligned(planes)
        if at < depth:
            out[rank, at:, :] = jnp.zeros((depth - at, lanes), jnp.float32)


def outer_sides(rank, parity, count):
    outer = outer_ranks(count)
    even = parity[0] == 0
    bottom = rank[0] == jnp.where(even, outer[0], outer[1])
    top = rank[0] == jnp.where(even, outer[1], outer[0])
    return bottom, top


def edge_kernel(nz_parts, width, rows, walls, rank, position, recv, swapped, given, out, vel):
    count, _, lanes = recv.shape
    planes = 3 * width
    nx = (count // nz_parts) * width
    nz = nz_parts * lanes
    bottom, top = outer_sides(rank, [lax.rem(position[0], 2)], count)
    at_wall = jnp.logical_or(
        jnp.logical_and(bottom, position[0] == 0), jnp.logical_and(top, position[0] == walls - 1)
    )

    def rows_of(k, i):
        first = i * rows
        own = [recv[k, first + j : first + j + 1, :] for j in (0, 1, rows - 2, rows - 1)]
        far = jnp.where(at_wall, 0.0, swapped[k, i : i + 1, :])
        return (
            jnp.where(bottom, far, own[2]),
            jnp.where(bottom, own[0], own[3]),
            jnp.where(bottom, own[1], far),
        )

    def roll_x(f, shift):
        return pltpu.roll(f, shift % nx, 0)

    def roll_z(f, shift):
        return pltpu.roll(f, shift % nz, 1)

    def smooth_x(f):
        return (roll_x(f, 1) + roll_x(f, -1)) + 2.0 * f

    def smooth(f):
        f = smooth_x(f)
        return (roll_z(f, 1) + roll_z(f, -1)) + 2.0 * f

    def slopes(below, centre, above):
        return strain_parts(
            [roll_x(f, -1) - roll_x(f, 1) for f in centre],
            [a - b for a, b in zip(above, below)],
            [roll_z(f, -1) - roll_z(f, 1) for f in centre],
        )

    @pl.when(jnp.logical_or(bottom, top))
    def _():
        for k in range(count):
            x0, zb = (k // nz_parts) * width, k % nz_parts
            for i in range(planes):
                c, x = divmod(i, width)
                for j, row in enumerate(rows_of(k, i)):
                    vel[j, c, x0 + x : x0 + x + 1, zb * lanes : (zb + 1) * lanes] = row
        u = [[vel[j, c] for c in range(3)] for j in range(3)]
        v = [[smooth(f) for f in row] for row in u]
        strain = slopes(*u)
        size = strain_size(strain)
        mean_strain = slopes(*v)
        mean_size = 0.25 * strain_size(mean_strain)
        scaled = [0.0625 * f for f in v[1]]
        pairs = [v[1][i] * scaled[j] for i, j in ((0, 0), (1, 1), (2, 2), (0, 1), (0, 2), (1, 2))]
        leonard = [smooth(p) - q for p, q in zip(products(u[1]), pairs)]
        model = [smooth(size * s) - mean_size * f for s, f in zip(strain, mean_strain)]
        lm, mm = contracted(leonard, model)
        coefficient = coefficient_of(
            *(jnp.sum(f, axis=(0, 1), keepdims=True) for f in (lm, mm)), nx * nz
        )
        eddy = coefficient * size

        def put(at):
            for k in range(count):
                x0, zb = (k // nz_parts) * width, k % nz_parts
                for x in range(width):
                    out[k, x, at : at + 1, :] = eddy[x0 + x : x0 + x + 1, zb * lanes : (zb + 1) * lanes]

        pl.when(bottom)(lambda: put(0))
        pl.when(top)(lambda: put(rows - 1))


def contracted(leonard, model):
    lm = mm = None
    for i in range(6):
        square = model[i] * model[i] if i < 3 else (0.5 * model[i]) * model[i]
        product = leonard[i] * model[i]
        lm = product if lm is None else lm + product
        mm = square if mm is None else mm + square
    return lm, mm


def coefficient_of(plane_lm, plane_mm, cells):
    scale = 1.0 / (256.0 * cells)
    return jnp.maximum(plane_lm * scale / (plane_mm * scale + 1e-06), 0.0)


def germano_kernel(nz_parts, width, rows, rank, parity, recv, out, vel, filt, ends, strains, means, part):
    count, _, lanes = recv.shape
    planes = 3 * width
    _, top = outer_sides(rank, parity, count)
    nx = (count // nz_parts) * width
    nz = nz_parts * lanes
    blocks = range(nz_parts)
    lead = 8
    inner = slice(lead, lead + rows)
    for k in range(count):
        x0, zb = (k // nz_parts) * width, k % nz_parts
        for c in range(3):
            for x in range(width):
                i = c * width + x
                vel[c, x0 + x, zb, inner, :] = recv[k, i * rows : (i + 1) * rows, :]
                slots = planes * rows + i
                near = recv[k, slots : slots + 1, :]
                slots += aligned(planes)
                other = recv[k, slots : slots + 1, :]
                below = jnp.where(top, other, near)
                for side, (edge, at) in enumerate(((below, lead - 1), (other, lead + rows))):
                    vel[c, x0 + x, zb, at : at + 1, :] = edge
                    ends[c, x0 + x, zb, side : side + 1, :] = edge

    lower = slice(lead - 1, lead - 1 + rows)
    upper = slice(lead + 1, lead + 1 + rows)

    def smooth_x(read, x):
        return (read((x - 1) % nx) + read((x + 1) % nx)) + 2.0 * read(x)

    def keep_strain(field, x, kept, scale):
        left, right = (x - 1) % nx, (x + 1) % nx
        grad_z = [slope_z([field[c, x, zb, inner, :] for zb in blocks]) for c in range(3)]
        for zb in blocks:
            grad_x = [field[c, right, zb, inner, :] - field[c, left, zb, inner, :] for c in range(3)]
            grad_y = [field[c, x, zb, upper, :] - field[c, x, zb, lower, :] for c in range(3)]
            parts = strain_parts(grad_x, grad_y, [grad_z[c][zb] for c in range(3)])
            for i in range(6):
                kept[i, x, zb] = parts[i]
            kept[6, x, zb] = scale * strain_size(parts) if scale != 1.0 else strain_size(parts)

    for x in range(nx):
        keep_strain(vel, x, strains, 1.0)
        for c in range(3):
            for zb, f in enumerate(smooth_z([vel[c, x, zb, inner, :] for zb in blocks])):
                part[c, x, zb] = f
    for c in range(3):
        rims = [smooth_z([ends[c, x, zb] for zb in blocks]) for x in range(nx)]
        for x in range(nx):
            for zb in blocks:
                rim = smooth_x(lambda at: rims[at][zb], x)
                filt[c, x, zb, lead - 1 : lead, :] = rim[0:1, :]
                filt[c, x, zb, lead + rows : lead + rows + 1, :] = rim[1:2, :]
                filt[c, x, zb, inner, :] = smooth_x(lambda at: part[c, at, zb], x)
    for x in range(nx):
        keep_strain(filt, x, means, 0.25)
        for i, (a, b) in enumerate(((0, 0), (1, 1), (2, 2), (0, 1), (0, 2), (1, 2))):
            fields = [vel[a, x, zb, inner, :] * vel[b, x, zb, inner, :] for zb in blocks]
            for zb, f in enumerate(smooth_z(fields)):
                part[3 + i, x, zb] = f
            fields = [strains[6, x, zb] * strains[i, x, zb] for zb in blocks]
            for zb, f in enumerate(smooth_z(fields)):
                part[9 + i, x, zb] = f

    sum_lm = sum_mm = None
    for x in range(nx):
        for zb in blocks:
            v = [filt[c, x, zb, inner, :] for c in range(3)]
            scaled = [0.0625 * f for f in v]
            size = means[6, x, zb]
            for i, (a, b) in enumerate(((0, 0), (1, 1), (2, 2), (0, 1), (0, 2), (1, 2))):
                leonard = smooth_x(lambda at: part[3 + i, at, zb], x) - v[a] * scaled[b]
                model = smooth_x(lambda at: part[9 + i, at, zb], x) - size * means[i, x, zb]
                square = model * model if i < 3 else (0.5 * model) * model
                sum_lm = leonard * model if sum_lm is None else sum_lm + leonard * model
                sum_mm = square if sum_mm is None else sum_mm + square

    coefficient = coefficient_of(
        *(jnp.sum(total, axis=1, keepdims=True) for total in (sum_lm, sum_mm)), nx * nz
    )
    for k in range(count):
        x0, zb = (k // nz_parts) * width, k % nz_parts
        for x in range(width):
            out[k, x] = coefficient * strains[6, x0 + x, zb]


def sweep_kernel(parity, back, velocity, tendency, eddy, reduced, factors, tree):
    count, width, rows, _ = back.shape
    length = count * rows // SEGMENTS

    def fill(rank, place):
        for x in range(width):
            eddy[x, place * rows : (place + 1) * rows, :] = back[rank, x]

    by_parity(parity, count, fill)

    def row(ref, index, j):
        return ref[(*index, pl.ds(j, SEGMENTS, stride=length), slice(None))]

    planes = range(width)
    last_row = length - 1
    visc = [[1.0 + row(eddy, (x,), j) for x in planes] for j in range(length)]
    links = [[750.0 * (v + w) for v, w in zip(visc[j], visc[j + 1])] for j in range(last_row)]

    over = [jnp.ones_like(v) for v in visc[0]]
    under = [jnp.ones_like(v) for v in visc[0]]
    inverses = []
    for j in range(last_row):
        inverses.append([u / (o + e * u) for o, u, e in zip(over, under, links[j])])
        steps = [o * (1.0 / e) for o, e in zip(over, links[j])]
        under, over = (
            [u + t for u, t in zip(under, steps)],
            [(o + u) + t for o, u, t in zip(over, under, steps)],
        )
    inverses.append([u / o for o, u in zip(over, under)])

    value = first = corner = left = None
    reach = [jnp.ones_like(v) for v in visc[0]]
    for j in range(length):
        inverse = inverses[j]
        before = value
        source = [[2.0 * row(velocity, (c, x), j) + row(tendency, (c, x), j) for x in planes] for c in range(3)]
        value = [[f * r for f, r in zip(source[c], inverse)] for c in range(3)]
        if j > 0:
            carry = [e * r for e, r in zip(links[j - 1], inverse)]
            value = [[v + k * w for v, k, w in zip(value[c], carry, before[c])] for c in range(3)]
        left = [m * r for m, r in zip(reach, inverse)]
        if j == 0:
            first, corner = value, left
        else:
            first = [[f + m * v for f, m, v in zip(first[c], reach, value[c])] for c in range(3)]
            corner = [a + m * v for a, m, v in zip(corner, reach, left)]
        ratio = inverse
        if j < last_row:
            ratio = [e * r for e, r in zip(links[j], inverse)]
            reach = [m * r for m, r in zip(reach, ratio)]
        for x in planes:
            for c in range(3):
                factors[x, j, c] = value[c][x]
            factors[x, j, 3] = left[x]
            factors[x, j, 4] = ratio[x]

    def other(fields, step):
        return [pltpu.roll(f, (SEGMENTS - step) % SEGMENTS, 0) if step else f for f in fields]

    last, across, end = value, left, inverse
    seams = [750.0 * (v + w) for v, w in zip(visc[last_row], other(visc[0], 1))]
    level, step = 0, 1
    while step < SEGMENTS:
        link = other(seams, step - 1)
        first_b = [other(f, step) for f in first]
        last_b = [other(f, step) for f in last]
        corner_b, end_b, across_b = other(corner, step), other(end, step), other(across, step)
        stiff = [e / (1.0 + e * (d + a)) for e, d, a in zip(link, end, corner_b)]
        flux = [[k * (g - f) for k, g, f in zip(stiff, last[c], first_b[c])] for c in range(3)]
        from_left = [k * b for k, b in zip(stiff, across)]
        from_right = [k * b for k, b in zip(stiff, across_b)]
        for x in planes:
            for c in range(3):
                tree[x, level, c] = flux[c][x]
            tree[x, level, 3] = from_left[x]
            tree[x, level, 4] = from_right[x]
        first = [[f - b * t for f, b, t in zip(first[c], across, flux[c])] for c in range(3)]
        last = [[g + b * t for g, b, t in zip(last_b[c], across_b, flux[c])] for c in range(3)]
        corner = [a - b * k for a, b, k in zip(corner, across, from_left)]
        end = [d - b * k for d, b, k in zip(end_b, across_b, from_right)]
        across = [k * b for k, b in zip(from_left, across_b)]
        level, step = level + 1, step * 2
    for x in planes:
        rows_out = [f[x][0:1, :] for f in (*first, *last, corner, across, end, visc[0])]
        rows_out.append(visc[last_row][x][SEGMENTS - 1 :, :])
        for i, v in enumerate(rows_out):
            reduced[i * width + x : i * width + x + 1, :] = v


def spread_kernel(factors, tree, velocity, eddy, particular, response, eddy_out, sent):
    write = pltpu.make_async_copy(eddy, eddy_out, sent)
    write.start()
    width, length = factors.shape[:2]
    levels = tree.shape[1]
    sublane = lax.broadcasted_iota(jnp.int32, (SEGMENTS, LANES), 0)
    one, zero = (jnp.full((SEGMENTS, LANES), v, jnp.float32) for v in (1.0, 0.0))
    sides = [(c, zero, zero) for c in range(3)] + [(None, one, zero), (None, zero, one)]
    lefts = [[side[1]] * width for side in sides]
    rights = [[side[2]] * width for side in sides]
    for level in range(levels - 1, -1, -1):
        step = 2**level
        second = lax.rem(sublane, 2 * step) == step
        for n, (c, _, _) in enumerate(sides):
            for x in range(width):
                left, right = lefts[n][x], rights[n][x]
                through = tree[x, level, 3] * left - tree[x, level, 4] * right
                if c is not None:
                    through = tree[x, level, c] + through
                lefts[n][x] = jnp.where(second, pltpu.roll(through, step, 0), left)
                rights[n][x] = jnp.where(second, pltpu.roll(right, step, 0), -through)
    values = rights
    for j in range(length - 1, -1, -1):
        rows = pl.ds(j, SEGMENTS, stride=length)
        for n, (c, _, _) in enumerate(sides):
            for x in range(width):
                value = factors[x, j, 3] * lefts[n][x] + factors[x, j, 4] * values[n][x]
                if c is not None:
                    value = factors[x, j, c] + value
                    particular[c, x, rows, :] = value - velocity[c, x, rows, :]
                else:
                    response[n - 3, x, rows, :] = value
                values[n][x] = value
    write.wait()


def sources_of(step, count):
    ring = [0, *range(1, count, 2), *range(count - 2 + count % 2, 0, -2)]
    return [ring[(ring.index(i) - step) % count] for i in range(count)]


def exchange_order(count):
    return range(count - 1, 0, -1)


def spread_kernel(factors, tree, velocity, eddy, particular, response, eddy_out, sent):
    write = pltpu.make_async_copy(eddy, eddy_out, sent)
    write.start()
    width, length = factors.shape[:2]
    levels = tree.shape[1]
    sublane = lax.broadcasted_iota(jnp.int32, (SEGMENTS, LANES), 0)
    one, zero = (jnp.full((SEGMENTS, LANES), v, jnp.float32) for v in (1.0, 0.0))
    sides = [(c, zero, zero) for c in range(3)] + [(None, one, zero), (None, zero, one)]
    lefts = [[side[1]] * width for side in sides]
    rights = [[side[2]] * width for side in sides]
    for level in range(levels - 1, -1, -1):
        step = 2**level
        second = lax.rem(sublane, 2 * step) == step
        for n, (c, _, _) in enumerate(sides):
            for x in range(width):
                left, right = lefts[n][x], rights[n][x]
                through = tree[x, level, 3] * left - tree[x, level, 4] * right
                if c is not None:
                    through = tree[x, level, c] + through
                lefts[n][x] = jnp.where(second, pltpu.roll(through, step, 0), left)
                rights[n][x] = jnp.where(second, pltpu.roll(right, step, 0), -through)
    values = rights
    for j in range(length - 1, -1, -1):
        rows = pl.ds(j, SEGMENTS, stride=length)
        for n, (c, _, _) in enumerate(sides):
            for x in range(width):
                value = factors[x, j, 3] * lefts[n][x] + factors[x, j, 4] * values[n][x]
                if c is not None:
                    value = factors[x, j, c] + value
                    particular[c, x, rows, :] = value - velocity[c, x, rows, :]
                else:
                    response[n - 3, x, rows, :] = value
                values[n][x] = value
    write.wait()


def partner(i, step, count):
    if count & (count - 1) == 0:
        return i ^ step
    return (i - step + count) % count


def finish_kernel(devices, position, particular, response, *rest):
    reduced, (result, gathered, fluxes, out, sent) = rest[:devices], rest[devices:]
    width = particular.shape[1]
    here = position[0]
    for step, ref in zip([0, *exchange_order(devices)], reduced):
        source = sum(jnp.where(here == i, s, 0) for i, s in enumerate(sources_of(step, devices)))
        gathered[source] = ref[...]

    def part(device, i):
        return gathered[device, i * width : (i + 1) * width, :]

    pivots, sources = [], []
    for i in range(devices + 1):
        visc = [part(i - 1, 10)] if i > 0 else []
        total = [part(i - 1, 8)] if i > 0 else []
        source = [part(i - 1, 3 + c) for c in range(3)] if i > 0 else [0.0] * 3
        if i < devices:
            visc.append(part(i, 9))
            total.append(part(i, 6))
            source = [s - part(i, c) for c, s in enumerate(source)]
        pivots.append(sum(total) + 1.0 / (750.0 * sum(visc)))
        sources.append(source)
    across = [part(i, 7) for i in range(devices)]
    minors = [jnp.ones_like(pivots[0]), pivots[0]]
    for i in range(1, devices + 1):
        minors.append(pivots[i] * minors[i] - (across[i - 1] * across[i - 1]) * minors[i - 1])
    inverses = [minors[i] / minors[i + 1] for i in range(devices + 1)]
    ratios = [b * r for b, r in zip(across, inverses)]
    for i in range(1, devices + 1):
        sources[i] = [s + ratios[i - 1] * t for s, t in zip(sources[i], sources[i - 1])]
    for i in range(devices, -1, -1):
        flux_here = [inverses[i] * s for s in sources[i]]
        flux = flux_here if i == devices else [f + ratios[i] * g for f, g in zip(flux_here, flux)]
        for c in range(3):
            fluxes[i, c * width : (c + 1) * width, :] = flux[c]

    writes = []
    for c in range(3):
        for x in range(width):
            r = c * width + x
            left, right = fluxes[here, r : r + 1, :], fluxes[here + 1, r : r + 1, :]
            out[c, x] = particular[c, x] + (response[0, x] * left - response[1, x] * right)
            writes.append(pltpu.make_async_copy(out.at[c, x], result.at[c, x], sent.at[r]))
            writes[-1].start()
    for write in writes:
        write.wait()


def in_vmem(count):
    return [pl.BlockSpec(memory_space=pltpu.VMEM)] * count


def in_hbm(count):
    return [pl.BlockSpec(memory_space=pltpu.HBM)] * count


def in_smem(count):
    return [pl.BlockSpec(memory_space=pltpu.SMEM)] * count


def params():
    return pltpu.CompilerParams(vmem_limit_bytes=VMEM_BYTES)


def body(velocity, tendency):
    _, width, cells, lanes = velocity.shape
    nz_parts = lax.axis_size("gz")
    count = lax.axis_size("gx") * nz_parts
    walls = lax.axis_size("gy")
    rows = cells // count
    nx = lax.axis_size("gx") * width
    padded = 16 + aligned(rows)
    f32 = jnp.float32

    planes = 3 * width
    depth = aligned(planes * rows + 2 * aligned(planes))
    position = lax.axis_index("gy").astype(jnp.int32).reshape(1)
    parity = lax.rem(position, 2)
    chunks = pl.pallas_call(
        functools.partial(pack_kernel, rows),
        out_shape=jax.ShapeDtypeStruct((count, depth, lanes), f32),
        in_specs=in_smem(1) + in_vmem(1),
        out_specs=pl.BlockSpec(memory_space=pltpu.VMEM),
        compiler_params=params(),
        name="pack",
    )(parity, velocity)
    recv = lax.all_to_all(chunks, ("gx", "gz"), split_axis=0, concat_axis=0, tiled=True)
    slot = lax.slice_in_dim(recv, planes * rows, planes * rows + aligned(planes), axis=1)
    swapped = lax.ppermute(slot, ("gy", "gx", "gz"), swap_pairs(walls, count))
    rank = lax.axis_index(("gx", "gz")).astype(jnp.int32).reshape(1)
    chunk_shape = jax.ShapeDtypeStruct((count, width, rows, lanes), f32)
    cells_here = nx * nz_parts * rows * lanes
    provisional = pl.pallas_call(
        functools.partial(germano_kernel, nz_parts, width, rows),
        out_shape=chunk_shape,
        in_specs=in_smem(2) + in_vmem(1),
        out_specs=pl.BlockSpec(memory_space=pltpu.VMEM),
        scratch_shapes=[
            pltpu.VMEM((3, nx, nz_parts, padded, lanes), f32),
            pltpu.VMEM((3, nx, nz_parts, padded, lanes), f32),
            pltpu.VMEM((3, nx, nz_parts, 8, lanes), f32),
            pltpu.VMEM((7, nx, nz_parts, rows, lanes), f32),
            pltpu.VMEM((7, nx, nz_parts, rows, lanes), f32),
            pltpu.VMEM((15, nx, nz_parts, rows, lanes), f32),
        ],
        compiler_params=params(),
        cost_estimate=pl.CostEstimate(
            flops=300 * cells_here, bytes_accessed=16 * cells_here, transcendentals=2 * cells_here
        ),
        name="germano",
    )(rank, parity, recv)
    eddy_chunks = pl.pallas_call(
        functools.partial(edge_kernel, nz_parts, width, rows, walls),
        out_shape=chunk_shape,
        in_specs=in_smem(2) + in_vmem(3),
        out_specs=pl.BlockSpec(memory_space=pltpu.VMEM),
        scratch_shapes=[pltpu.VMEM((3, 3, nx, nz_parts * lanes), f32)],
        input_output_aliases={4: 0},
        compiler_params=params(),
        name="edge",
    )(rank, position, recv, swapped, provisional)
    back = lax.all_to_all(eddy_chunks, ("gx", "gz"), split_axis=0, concat_axis=0, tiled=True)

    length = cells // SEGMENTS
    levels = SEGMENTS.bit_length() - 1
    packed = aligned(11 * width)
    eddy_here, reduced, factors, tree = pl.pallas_call(
        sweep_kernel,
        out_shape=(
            jax.ShapeDtypeStruct((width, cells, lanes), f32),
            jax.ShapeDtypeStruct((packed, lanes), f32),
            jax.ShapeDtypeStruct((width, length, 5, SEGMENTS, lanes), f32),
            jax.ShapeDtypeStruct((width, levels, 5, SEGMENTS, lanes), f32),
        ),
        in_specs=in_smem(1) + in_vmem(3),
        out_specs=tuple(in_vmem(4)),
        compiler_params=params(),
        name="sweep",
    )(parity, back, velocity, tendency)

    others = [
        lax.ppermute(reduced, "gy", [(s, i) for i, s in enumerate(sources_of(step, walls))])
        for step in exchange_order(walls)
    ]
    particular, response, eddy = pl.pallas_call(
        spread_kernel,
        out_shape=(
            jax.ShapeDtypeStruct(velocity.shape, f32),
            jax.ShapeDtypeStruct((2, *velocity.shape[1:]), f32),
            jax.ShapeDtypeStruct(eddy_here.shape, f32),
        ),
        in_specs=in_vmem(4),
        out_specs=tuple(in_vmem(2) + in_hbm(1)),
        scratch_shapes=[pltpu.SemaphoreType.DMA],
        compiler_params=params(),
        cost_estimate=pl.CostEstimate(
            flops=20 * velocity.size, bytes_accessed=16 * velocity.size, transcendentals=0
        ),
        name="spread",
    )(factors, tree, velocity, eddy_here)
    new_velocity = pl.pallas_call(
        functools.partial(finish_kernel, walls),
        out_shape=jax.ShapeDtypeStruct(velocity.shape, f32),
        in_specs=in_smem(1) + in_vmem(2 + walls),
        out_specs=in_hbm(1)[0],
        scratch_shapes=[
            pltpu.VMEM((walls, packed, lanes), f32),
            pltpu.VMEM((walls + 1, aligned(3 * width), lanes), f32),
            pltpu.VMEM(velocity.shape, f32),
            pltpu.SemaphoreType.DMA((planes,)),
        ],
        compiler_params=params(),
        name="finish",
    )(position, particular, response, reduced, *others)
    return (new_velocity, eddy)


def solution(mesh):
    return jax.shard_map(
        body,
        mesh=mesh,
        in_specs=(P(None, "gx", "gy", "gz"), P(None, "gx", "gy", "gz")),
        out_specs=(P(None, "gx", "gy", "gz"), P("gx", "gy", "gz")),
        check_vma=False,
    )
```

```python
import functools

import jax
import jax.numpy as jnp
from jax import lax
from jax.experimental import pallas as pl
from jax.experimental.pallas import tpu as pltpu
from jax.sharding import PartitionSpec as P

LANES = 128
SEGMENTS = 8
VMEM_BYTES = 24 * 2**20


def strain_parts(grad_x, grad_y, grad_z):
    return (
        grad_x[0],
        grad_y[1],
        grad_z[2],
        grad_y[0] + grad_x[1],
        grad_z[0] + grad_x[2],
        grad_z[1] + grad_y[2],
    )


def strain_size(parts):
    diagonal = parts[0] * parts[0] + parts[1] * parts[1] + parts[2] * parts[2]
    mixed = parts[3] * parts[3] + parts[4] * parts[4] + parts[5] * parts[5]
    return jnp.sqrt(0.5 * diagonal + 0.25 * mixed)


def beside(blocks):
    count = len(blocks)
    lanes = blocks[0].shape[1]
    down = [pltpu.roll(f, 1, 1) for f in blocks]
    up = [pltpu.roll(f, lanes - 1, 1) for f in blocks]
    if count > 1:
        lane = lax.broadcasted_iota(jnp.int32, blocks[0].shape, 1)
        first, last = lane == 0, lane == lanes - 1
        down, up = (
            [jnp.where(first, down[i - 1], down[i]) for i in range(count)],
            [jnp.where(last, up[(i + 1) % count], up[i]) for i in range(count)],
        )
    return down, up


def slope_z(blocks):
    down, up = beside(blocks)
    return [u - d for u, d in zip(up, down)]


def smooth_z(blocks):
    down, up = beside(blocks)
    return [(u + d) + 2.0 * f for f, u, d in zip(blocks, up, down)]


def band_matrix(n):
    shape = (n, n)
    apart = lax.broadcasted_iota(jnp.int32, shape, 0) - lax.broadcasted_iota(jnp.int32, shape, 1)
    apart = jnp.abs(apart)
    near = jnp.logical_or(apart == 1, apart == n - 1)
    return jnp.where(apart == 0, 2.0, jnp.where(near, 1.0, 0.0)).astype(jnp.bfloat16)


def times_band(f, band):
    total = None
    for i in range(3):
        piece = f.astype(jnp.bfloat16)
        product = jnp.dot(piece, band, preferred_element_type=jnp.float32)
        total = product if total is None else total + product
        if i < 2:
            f = f - piece.astype(jnp.float32)
    return total


def products(v):
    return (v[0] * v[0], v[1] * v[1], v[2] * v[2], v[0] * v[1], v[0] * v[2], v[1] * v[2])


def outer_ranks(count):
    return (count - 1, count - 3)


def places(parity, count):
    outer = outer_ranks(count)
    inner = iter(range(1, count - 1))
    return [
        (0 if outer[parity] == rank else count - 1) if rank in outer else next(inner)
        for rank in range(count)
    ]


def swap_pairs(walls, count):
    odd, even = outer_ranks(count)
    spare = count - 5
    partners = {}

    def join(a, b):
        partners[a], partners[b] = b, a

    def join_walls(rank, first):
        for wall in range(first, walls - 1, 2):
            join((wall, rank), (wall + 1, rank))

    join_walls(even, 0)
    join_walls(odd, 1)
    join_walls(spare, 1)
    join((0, odd), (0, spare))
    if walls % 2 == 0:
        join((walls - 1, odd), (walls - 1, spare))
    others = [r for r in range(count) if r not in (odd, even, spare)]
    for core in range(2):
        ranks = [r for r in others if r % 2 == core]
        half = len(ranks) // 2
        for wall in range(walls):
            for a, b in zip(ranks[:half], ranks[half : 2 * half]):
                join((wall, a), (wall, b))
        for rank in ranks[2 * half :]:
            join_walls(rank, 0)
    return [
        (wall * count + rank, to[0] * count + to[1])
        for wall in range(walls)
        for rank in range(count)
        for to in [partners.get((wall, rank), (wall, rank))]
    ]


def by_parity(parity, count, fill):
    outer = outer_ranks(count)
    for rank, place in enumerate(places(0, count)):
        if rank not in outer:
            fill(rank, place)
    for turn in range(2):

        @pl.when(parity[0] == turn)
        def _():
            for rank in outer:
                fill(rank, places(turn, count)[rank])


def aligned(n):
    return -(-n // 8) * 8


def pack_kernel(rows, parity, velocity, out):
    _, width, cells, _ = velocity.shape
    count, depth, lanes = out.shape
    planes = 3 * width
    slots = planes * rows

    def fill(rank, place):
        first = place * rows
        beside = [first - 1, first + rows]
        if place == 0:
            beside = [first, first + rows]
        if place == count - 1:
            beside = [first + rows - 1, first - 1]
        for i in range(planes):
            c, x = divmod(i, width)
            out[rank, i * rows : (i + 1) * rows, :] = velocity[c, x, first : first + rows, :]
            for slot, row in enumerate(beside):
                at = slots + slot * aligned(planes) + i
                out[rank, at : at + 1, :] = velocity[c, x, row : row + 1, :]

    by_parity(parity, count, fill)
    blank = aligned(planes) - planes
    for rank in range(count):
        for slot in range(2):
            at = slots + slot * aligned(planes) + planes
            out[rank, at : at + blank, :] = jnp.zeros((blank, lanes), jnp.float32)
        at = slots + 2 * aligned(planes)
        if at < depth:
            out[rank, at:, :] = jnp.zeros((depth - at, lanes), jnp.float32)


def outer_sides(rank, parity, count):
    outer = outer_ranks(count)
    even = parity[0] == 0
    bottom = rank[0] == jnp.where(even, outer[0], outer[1])
    top = rank[0] == jnp.where(even, outer[1], outer[0])
    return bottom, top


def edge_kernel(nz_parts, width, rows, walls, rank, position, recv, swapped, given, out, vel):
    count, _, lanes = recv.shape
    planes = 3 * width
    nx = (count // nz_parts) * width
    nz = nz_parts * lanes
    bottom, top = outer_sides(rank, [lax.rem(position[0], 2)], count)
    at_wall = jnp.logical_or(
        jnp.logical_and(bottom, position[0] == 0), jnp.logical_and(top, position[0] == walls - 1)
    )

    def rows_of(k, i):
        first = i * rows
        own = [recv[k, first + j : first + j + 1, :] for j in (0, 1, rows - 2, rows - 1)]
        far = jnp.where(at_wall, 0.0, swapped[k, i : i + 1, :])
        return (
            jnp.where(bottom, far, own[2]),
            jnp.where(bottom, own[0], own[3]),
            jnp.where(bottom, own[1], far),
        )

    def roll_x(f, shift):
        return pltpu.roll(f, shift % nx, 0)

    def roll_z(f, shift):
        return pltpu.roll(f, shift % nz, 1)

    def smooth_x(f):
        return (roll_x(f, 1) + roll_x(f, -1)) + 2.0 * f

    def smooth(f):
        f = smooth_x(f)
        return (roll_z(f, 1) + roll_z(f, -1)) + 2.0 * f

    def slopes(below, centre, above):
        return strain_parts(
            [roll_x(f, -1) - roll_x(f, 1) for f in centre],
            [a - b for a, b in zip(above, below)],
            [roll_z(f, -1) - roll_z(f, 1) for f in centre],
        )

    @pl.when(jnp.logical_or(bottom, top))
    def _():
        for k in range(count):
            x0, zb = (k // nz_parts) * width, k % nz_parts
            for i in range(planes):
                c, x = divmod(i, width)
                for j, row in enumerate(rows_of(k, i)):
                    vel[j, c, x0 + x : x0 + x + 1, zb * lanes : (zb + 1) * lanes] = row
        u = [[vel[j, c] for c in range(3)] for j in range(3)]
        v = [[smooth(f) for f in row] for row in u]
        strain = slopes(*u)
        size = strain_size(strain)
        mean_strain = slopes(*v)
        mean_size = 0.25 * strain_size(mean_strain)
        scaled = [0.0625 * f for f in v[1]]
        pairs = [v[1][i] * scaled[j] for i, j in ((0, 0), (1, 1), (2, 2), (0, 1), (0, 2), (1, 2))]
        leonard = [smooth(p) - q for p, q in zip(products(u[1]), pairs)]
        model = [smooth(size * s) - mean_size * f for s, f in zip(strain, mean_strain)]
        lm, mm = contracted(leonard, model)
        coefficient = coefficient_of(
            *(jnp.sum(f, axis=(0, 1), keepdims=True) for f in (lm, mm)), nx * nz
        )
        eddy = coefficient * size

        def put(at):
            for k in range(count):
                x0, zb = (k // nz_parts) * width, k % nz_parts
                for x in range(width):
                    out[k, x, at : at + 1, :] = eddy[x0 + x : x0 + x + 1, zb * lanes : (zb + 1) * lanes]

        pl.when(bottom)(lambda: put(0))
        pl.when(top)(lambda: put(rows - 1))


def contracted(leonard, model):
    lm = mm = None
    for i in range(6):
        square = model[i] * model[i] if i < 3 else (0.5 * model[i]) * model[i]
        product = leonard[i] * model[i]
        lm = product if lm is None else lm + product
        mm = square if mm is None else mm + square
    return lm, mm


def coefficient_of(plane_lm, plane_mm, cells):
    scale = 1.0 / (256.0 * cells)
    return jnp.maximum(plane_lm * scale / (plane_mm * scale + 1e-06), 0.0)


def germano_kernel(nz_parts, width, rows, rank, parity, recv, out, vel, filt, ends, strains, means, part):
    count, _, lanes = recv.shape
    planes = 3 * width
    _, top = outer_sides(rank, parity, count)
    nx = (count // nz_parts) * width
    nz = nz_parts * lanes
    blocks = range(nz_parts)
    lead = 8
    inner = slice(lead, lead + rows)
    for k in range(count):
        x0, zb = (k // nz_parts) * width, k % nz_parts
        for c in range(3):
            for x in range(width):
                i = c * width + x
                vel[c, x0 + x, zb, inner, :] = recv[k, i * rows : (i + 1) * rows, :]
                slots = planes * rows + i
                near = recv[k, slots : slots + 1, :]
                slots += aligned(planes)
                other = recv[k, slots : slots + 1, :]
                below = jnp.where(top, other, near)
                for side, (edge, at) in enumerate(((below, lead - 1), (other, lead + rows))):
                    vel[c, x0 + x, zb, at : at + 1, :] = edge
                    ends[c, x0 + x, zb, side : side + 1, :] = edge

    lower = slice(lead - 1, lead - 1 + rows)
    upper = slice(lead + 1, lead + 1 + rows)

    def smooth_x(read, x):
        return (read((x - 1) % nx) + read((x + 1) % nx)) + 2.0 * read(x)

    def keep_strain(field, x, kept, scale):
        left, right = (x - 1) % nx, (x + 1) % nx
        grad_z = [slope_z([field[c, x, zb, inner, :] for zb in blocks]) for c in range(3)]
        for zb in blocks:
            grad_x = [field[c, right, zb, inner, :] - field[c, left, zb, inner, :] for c in range(3)]
            grad_y = [field[c, x, zb, upper, :] - field[c, x, zb, lower, :] for c in range(3)]
            parts = strain_parts(grad_x, grad_y, [grad_z[c][zb] for c in range(3)])
            for i in range(6):
                kept[i, x, zb] = parts[i]
            kept[6, x, zb] = scale * strain_size(parts) if scale != 1.0 else strain_size(parts)

    for x in range(nx):
        keep_strain(vel, x, strains, 1.0)
        for c in range(3):
            for zb, f in enumerate(smooth_z([vel[c, x, zb, inner, :] for zb in blocks])):
                part[c, x, zb] = f
    for c in range(3):
        rims = [smooth_z([ends[c, x, zb] for zb in blocks]) for x in range(nx)]
        for x in range(nx):
            for zb in blocks:
                rim = smooth_x(lambda at: rims[at][zb], x)
                filt[c, x, zb, lead - 1 : lead, :] = rim[0:1, :]
                filt[c, x, zb, lead + rows : lead + rows + 1, :] = rim[1:2, :]
                filt[c, x, zb, inner, :] = smooth_x(lambda at: part[c, at, zb], x)
    def filter_z(read, kept):
        if not on_matrix_unit:
            for x in range(nx):
                for zb, f in enumerate(smooth_z([read(x, zb) for zb in blocks])):
                    part[kept, x, zb] = f
            return
        half = nx // 2
        for x0 in (0, half):
            planes_here = [
                jnp.concatenate([read(x, zb) for zb in blocks], axis=1) for x in range(x0, x0 + half)
            ]
            total = times_band(jnp.concatenate(planes_here, axis=0), band)
            for x in range(half):
                for zb in blocks:
                    part[kept, x0 + x, zb] = total[x * rows : (x + 1) * rows, zb * lanes : (zb + 1) * lanes]

    on_matrix_unit = nz <= 256 and rows * nx % 32 == 0 and rows % 8 == 0
    band = band_matrix(nz) if on_matrix_unit else None
    for i, (a, b) in enumerate(((0, 0), (1, 1), (2, 2), (0, 1), (0, 2), (1, 2))):
        filter_z(lambda x, zb: vel[a, x, zb, inner, :] * vel[b, x, zb, inner, :], 3 + i)
        filter_z(lambda x, zb: strains[6, x, zb] * strains[i, x, zb], 9 + i)
    for x in range(nx):
        keep_strain(filt, x, means, 0.25)

    sum_lm = sum_mm = None
    for x in range(nx):
        for zb in blocks:
            v = [filt[c, x, zb, inner, :] for c in range(3)]
            scaled = [0.0625 * f for f in v]
            size = means[6, x, zb]
            for i, (a, b) in enumerate(((0, 0), (1, 1), (2, 2), (0, 1), (0, 2), (1, 2))):
                leonard = smooth_x(lambda at: part[3 + i, at, zb], x) - v[a] * scaled[b]
                model = smooth_x(lambda at: part[9 + i, at, zb], x) - size * means[i, x, zb]
                square = model * model if i < 3 else (0.5 * model) * model
                sum_lm = leonard * model if sum_lm is None else sum_lm + leonard * model
                sum_mm = square if sum_mm is None else sum_mm + square

    coefficient = coefficient_of(
        *(jnp.sum(total, axis=1, keepdims=True) for total in (sum_lm, sum_mm)), nx * nz
    )
    for k in range(count):
        x0, zb = (k // nz_parts) * width, k % nz_parts
        for x in range(width):
            out[k, x] = coefficient * strains[6, x0 + x, zb]


def sweep_kernel(parity, back, velocity, tendency, eddy, reduced, factors, tree):
    count, width, rows, _ = back.shape
    length = count * rows // SEGMENTS

    def fill(rank, place):
        for x in range(width):
            eddy[x, place * rows : (place + 1) * rows, :] = back[rank, x]

    by_parity(parity, count, fill)

    def row(ref, index, j):
        return ref[(*index, pl.ds(j, SEGMENTS, stride=length), slice(None))]

    planes = range(width)
    last_row = length - 1
    visc = [[1.0 + row(eddy, (x,), j) for x in planes] for j in range(length)]
    links = [[750.0 * (v + w) for v, w in zip(visc[j], visc[j + 1])] for j in range(last_row)]

    over = [jnp.ones_like(v) for v in visc[0]]
    under = [jnp.ones_like(v) for v in visc[0]]
    inverses = []
    for j in range(last_row):
        inverses.append([u / (o + e * u) for o, u, e in zip(over, under, links[j])])
        steps = [o * (1.0 / e) for o, e in zip(over, links[j])]
        under, over = (
            [u + t for u, t in zip(under, steps)],
            [(o + u) + t for o, u, t in zip(over, under, steps)],
        )
    inverses.append([u / o for o, u in zip(over, under)])

    value = first = corner = left = None
    reach = [jnp.ones_like(v) for v in visc[0]]
    for j in range(length):
        inverse = inverses[j]
        before = value
        source = [[2.0 * row(velocity, (c, x), j) + row(tendency, (c, x), j) for x in planes] for c in range(3)]
        value = [[f * r for f, r in zip(source[c], inverse)] for c in range(3)]
        if j > 0:
            carry = [e * r for e, r in zip(links[j - 1], inverse)]
            value = [[v + k * w for v, k, w in zip(value[c], carry, before[c])] for c in range(3)]
        left = [m * r for m, r in zip(reach, inverse)]
        if j == 0:
            first, corner = value, left
        else:
            first = [[f + m * v for f, m, v in zip(first[c], reach, value[c])] for c in range(3)]
            corner = [a + m * v for a, m, v in zip(corner, reach, left)]
        ratio = inverse
        if j < last_row:
            ratio = [e * r for e, r in zip(links[j], inverse)]
            reach = [m * r for m, r in zip(reach, ratio)]
        for x in planes:
            for c in range(3):
                factors[x, j, c] = value[c][x]
            factors[x, j, 3] = left[x]
            factors[x, j, 4] = ratio[x]

    def other(fields, step):
        return [pltpu.roll(f, (SEGMENTS - step) % SEGMENTS, 0) if step else f for f in fields]

    last, across, end = value, left, inverse
    seams = [750.0 * (v + w) for v, w in zip(visc[last_row], other(visc[0], 1))]
    level, step = 0, 1
    while step < SEGMENTS:
        link = other(seams, step - 1)
        first_b = [other(f, step) for f in first]
        last_b = [other(f, step) for f in last]
        corner_b, end_b, across_b = other(corner, step), other(end, step), other(across, step)
        stiff = [e / (1.0 + e * (d + a)) for e, d, a in zip(link, end, corner_b)]
        flux = [[k * (g - f) for k, g, f in zip(stiff, last[c], first_b[c])] for c in range(3)]
        from_left = [k * b for k, b in zip(stiff, across)]
        from_right = [k * b for k, b in zip(stiff, across_b)]
        for x in planes:
            for c in range(3):
                tree[x, level, c] = flux[c][x]
            tree[x, level, 3] = from_left[x]
            tree[x, level, 4] = from_right[x]
        first = [[f - b * t for f, b, t in zip(first[c], across, flux[c])] for c in range(3)]
        last = [[g + b * t for g, b, t in zip(last_b[c], across_b, flux[c])] for c in range(3)]
        corner = [a - b * k for a, b, k in zip(corner, across, from_left)]
        end = [d - b * k for d, b, k in zip(end_b, across_b, from_right)]
        across = [k * b for k, b in zip(from_left, across_b)]
        level, step = level + 1, step * 2
    for x in planes:
        rows_out = [f[x][0:1, :] for f in (*first, *last, corner, across, end, visc[0])]
        rows_out.append(visc[last_row][x][SEGMENTS - 1 :, :])
        for i, v in enumerate(rows_out):
            reduced[i * width + x : i * width + x + 1, :] = v


def spread_kernel(factors, tree, velocity, eddy, particular, response, eddy_out, sent):
    write = pltpu.make_async_copy(eddy, eddy_out, sent)
    write.start()
    width, length = factors.shape[:2]
    levels = tree.shape[1]
    sublane = lax.broadcasted_iota(jnp.int32, (SEGMENTS, LANES), 0)
    one, zero = (jnp.full((SEGMENTS, LANES), v, jnp.float32) for v in (1.0, 0.0))
    sides = [(c, zero, zero) for c in range(3)] + [(None, one, zero), (None, zero, one)]
    lefts = [[side[1]] * width for side in sides]
    rights = [[side[2]] * width for side in sides]
    for level in range(levels - 1, -1, -1):
        step = 2**level
        second = lax.rem(sublane, 2 * step) == step
        for n, (c, _, _) in enumerate(sides):
            for x in range(width):
                left, right = lefts[n][x], rights[n][x]
                through = tree[x, level, 3] * left - tree[x, level, 4] * right
                if c is not None:
                    through = tree[x, level, c] + through
                lefts[n][x] = jnp.where(second, pltpu.roll(through, step, 0), left)
                rights[n][x] = jnp.where(second, pltpu.roll(right, step, 0), -through)
    values = rights
    for j in range(length - 1, -1, -1):
        rows = pl.ds(j, SEGMENTS, stride=length)
        for n, (c, _, _) in enumerate(sides):
            for x in range(width):
                value = factors[x, j, 3] * lefts[n][x] + factors[x, j, 4] * values[n][x]
                if c is not None:
                    value = factors[x, j, c] + value
                    particular[c, x, rows, :] = value - velocity[c, x, rows, :]
                else:
                    response[n - 3, x, rows, :] = value
                values[n][x] = value
    write.wait()


def sources_of(step, count):
    ring = [0, *range(1, count, 2), *range(count - 2 + count % 2, 0, -2)]
    return [ring[(ring.index(i) - step) % count] for i in range(count)]


def exchange_order(count):
    return range(count - 1, 0, -1)


def spread_kernel(factors, tree, velocity, eddy, particular, response, eddy_out, sent):
    write = pltpu.make_async_copy(eddy, eddy_out, sent)
    write.start()
    width, length = factors.shape[:2]
    levels = tree.shape[1]
    sublane = lax.broadcasted_iota(jnp.int32, (SEGMENTS, LANES), 0)
    one, zero = (jnp.full((SEGMENTS, LANES), v, jnp.float32) for v in (1.0, 0.0))
    sides = [(c, zero, zero) for c in range(3)] + [(None, one, zero), (None, zero, one)]
    lefts = [[side[1]] * width for side in sides]
    rights = [[side[2]] * width for side in sides]
    for level in range(levels - 1, -1, -1):
        step = 2**level
        second = lax.rem(sublane, 2 * step) == step
        for n, (c, _, _) in enumerate(sides):
            for x in range(width):
                left, right = lefts[n][x], rights[n][x]
                through = tree[x, level, 3] * left - tree[x, level, 4] * right
                if c is not None:
                    through = tree[x, level, c] + through
                lefts[n][x] = jnp.where(second, pltpu.roll(through, step, 0), left)
                rights[n][x] = jnp.where(second, pltpu.roll(right, step, 0), -through)
    values = rights
    for j in range(length - 1, -1, -1):
        rows = pl.ds(j, SEGMENTS, stride=length)
        for n, (c, _, _) in enumerate(sides):
            for x in range(width):
                value = factors[x, j, 3] * lefts[n][x] + factors[x, j, 4] * values[n][x]
                if c is not None:
                    value = factors[x, j, c] + value
                    particular[c, x, rows, :] = value - velocity[c, x, rows, :]
                else:
                    response[n - 3, x, rows, :] = value
                values[n][x] = value
    write.wait()


def partner(i, step, count):
    if count & (count - 1) == 0:
        return i ^ step
    return (i - step + count) % count


def finish_kernel(devices, position, particular, response, *rest):
    reduced, (result, gathered, fluxes, out, sent) = rest[:devices], rest[devices:]
    width = particular.shape[1]
    here = position[0]
    for step, ref in zip([0, *exchange_order(devices)], reduced):
        source = sum(jnp.where(here == i, s, 0) for i, s in enumerate(sources_of(step, devices)))
        gathered[source] = ref[...]

    def part(device, i):
        return gathered[device, i * width : (i + 1) * width, :]

    pivots, sources = [], []
    for i in range(devices + 1):
        visc = [part(i - 1, 10)] if i > 0 else []
        total = [part(i - 1, 8)] if i > 0 else []
        source = [part(i - 1, 3 + c) for c in range(3)] if i > 0 else [0.0] * 3
        if i < devices:
            visc.append(part(i, 9))
            total.append(part(i, 6))
            source = [s - part(i, c) for c, s in enumerate(source)]
        pivots.append(sum(total) + 1.0 / (750.0 * sum(visc)))
        sources.append(source)
    across = [part(i, 7) for i in range(devices)]
    minors = [jnp.ones_like(pivots[0]), pivots[0]]
    for i in range(1, devices + 1):
        minors.append(pivots[i] * minors[i] - (across[i - 1] * across[i - 1]) * minors[i - 1])
    inverses = [minors[i] / minors[i + 1] for i in range(devices + 1)]
    ratios = [b * r for b, r in zip(across, inverses)]
    for i in range(1, devices + 1):
        sources[i] = [s + ratios[i - 1] * t for s, t in zip(sources[i], sources[i - 1])]
    for i in range(devices, -1, -1):
        flux_here = [inverses[i] * s for s in sources[i]]
        flux = flux_here if i == devices else [f + ratios[i] * g for f, g in zip(flux_here, flux)]
        for c in range(3):
            fluxes[i, c * width : (c + 1) * width, :] = flux[c]

    writes = []
    for c in range(3):
        for x in range(width):
            r = c * width + x
            left, right = fluxes[here, r : r + 1, :], fluxes[here + 1, r : r + 1, :]
            out[c, x] = particular[c, x] + (response[0, x] * left - response[1, x] * right)
            writes.append(pltpu.make_async_copy(out.at[c, x], result.at[c, x], sent.at[r]))
            writes[-1].start()
    for write in writes:
        write.wait()


def in_vmem(count):
    return [pl.BlockSpec(memory_space=pltpu.VMEM)] * count


def in_hbm(count):
    return [pl.BlockSpec(memory_space=pltpu.HBM)] * count


def in_smem(count):
    return [pl.BlockSpec(memory_space=pltpu.SMEM)] * count


def params():
    return pltpu.CompilerParams(vmem_limit_bytes=VMEM_BYTES)


def body(velocity, tendency):
    _, width, cells, lanes = velocity.shape
    nz_parts = lax.axis_size("gz")
    count = lax.axis_size("gx") * nz_parts
    walls = lax.axis_size("gy")
    rows = cells // count
    nx = lax.axis_size("gx") * width
    padded = 16 + aligned(rows)
    f32 = jnp.float32

    planes = 3 * width
    depth = aligned(planes * rows + 2 * aligned(planes))
    position = lax.axis_index("gy").astype(jnp.int32).reshape(1)
    parity = lax.rem(position, 2)
    chunks = pl.pallas_call(
        functools.partial(pack_kernel, rows),
        out_shape=jax.ShapeDtypeStruct((count, depth, lanes), f32),
        in_specs=in_smem(1) + in_vmem(1),
        out_specs=pl.BlockSpec(memory_space=pltpu.VMEM),
        compiler_params=params(),
        name="pack",
    )(parity, velocity)
    recv = lax.all_to_all(chunks, ("gx", "gz"), split_axis=0, concat_axis=0, tiled=True)
    slot = lax.slice_in_dim(recv, planes * rows, planes * rows + aligned(planes), axis=1)
    swapped = lax.ppermute(slot, ("gy", "gx", "gz"), swap_pairs(walls, count))
    rank = lax.axis_index(("gx", "gz")).astype(jnp.int32).reshape(1)
    chunk_shape = jax.ShapeDtypeStruct((count, width, rows, lanes), f32)
    cells_here = nx * nz_parts * rows * lanes
    provisional = pl.pallas_call(
        functools.partial(germano_kernel, nz_parts, width, rows),
        out_shape=chunk_shape,
        in_specs=in_smem(2) + in_vmem(1),
        out_specs=pl.BlockSpec(memory_space=pltpu.VMEM),
        scratch_shapes=[
            pltpu.VMEM((3, nx, nz_parts, padded, lanes), f32),
            pltpu.VMEM((3, nx, nz_parts, padded, lanes), f32),
            pltpu.VMEM((3, nx, nz_parts, 8, lanes), f32),
            pltpu.VMEM((7, nx, nz_parts, rows, lanes), f32),
            pltpu.VMEM((7, nx, nz_parts, rows, lanes), f32),
            pltpu.VMEM((15, nx, nz_parts, rows, lanes), f32),
        ],
        compiler_params=params(),
        cost_estimate=pl.CostEstimate(
            flops=300 * cells_here, bytes_accessed=16 * cells_here, transcendentals=2 * cells_here
        ),
        name="germano",
    )(rank, parity, recv)
    eddy_chunks = pl.pallas_call(
        functools.partial(edge_kernel, nz_parts, width, rows, walls),
        out_shape=chunk_shape,
        in_specs=in_smem(2) + in_vmem(3),
        out_specs=pl.BlockSpec(memory_space=pltpu.VMEM),
        scratch_shapes=[pltpu.VMEM((3, 3, nx, nz_parts * lanes), f32)],
        input_output_aliases={4: 0},
        compiler_params=params(),
        name="edge",
    )(rank, position, recv, swapped, provisional)
    back = lax.all_to_all(eddy_chunks, ("gx", "gz"), split_axis=0, concat_axis=0, tiled=True)

    length = cells // SEGMENTS
    levels = SEGMENTS.bit_length() - 1
    packed = aligned(11 * width)
    eddy_here, reduced, factors, tree = pl.pallas_call(
        sweep_kernel,
        out_shape=(
            jax.ShapeDtypeStruct((width, cells, lanes), f32),
            jax.ShapeDtypeStruct((packed, lanes), f32),
            jax.ShapeDtypeStruct((width, length, 5, SEGMENTS, lanes), f32),
            jax.ShapeDtypeStruct((width, levels, 5, SEGMENTS, lanes), f32),
        ),
        in_specs=in_smem(1) + in_vmem(3),
        out_specs=tuple(in_vmem(4)),
        compiler_params=params(),
        name="sweep",
    )(parity, back, velocity, tendency)

    others = [
        lax.ppermute(reduced, "gy", [(s, i) for i, s in enumerate(sources_of(step, walls))])
        for step in exchange_order(walls)
    ]
    particular, response, eddy = pl.pallas_call(
        spread_kernel,
        out_shape=(
            jax.ShapeDtypeStruct(velocity.shape, f32),
            jax.ShapeDtypeStruct((2, *velocity.shape[1:]), f32),
            jax.ShapeDtypeStruct(eddy_here.shape, f32),
        ),
        in_specs=in_vmem(4),
        out_specs=tuple(in_vmem(2) + in_hbm(1)),
        scratch_shapes=[pltpu.SemaphoreType.DMA],
        compiler_params=params(),
        cost_estimate=pl.CostEstimate(
            flops=20 * velocity.size, bytes_accessed=16 * velocity.size, transcendentals=0
        ),
        name="spread",
    )(factors, tree, velocity, eddy_here)
    new_velocity = pl.pallas_call(
        functools.partial(finish_kernel, walls),
        out_shape=jax.ShapeDtypeStruct(velocity.shape, f32),
        in_specs=in_smem(1) + in_vmem(2 + walls),
        out_specs=in_hbm(1)[0],
        scratch_shapes=[
            pltpu.VMEM((walls, packed, lanes), f32),
            pltpu.VMEM((walls + 1, aligned(3 * width), lanes), f32),
            pltpu.VMEM(velocity.shape, f32),
            pltpu.SemaphoreType.DMA((planes,)),
        ],
        compiler_params=params(),
        name="finish",
    )(position, particular, response, reduced, *others)
    return (new_velocity, eddy)


def solution(mesh):
    return jax.shard_map(
        body,
        mesh=mesh,
        in_specs=(P(None, "gx", "gy", "gz"), P(None, "gx", "gy", "gz")),
        out_specs=(P(None, "gx", "gy", "gz"), P("gx", "gy", "gz")),
        check_vma=False,
    )
```

```python
import functools

import jax
import jax.numpy as jnp
from jax import lax
from jax.experimental import pallas as pl
from jax.experimental.pallas import tpu as pltpu
from jax.sharding import PartitionSpec as P

LANES = 128
SEGMENTS = 8
VMEM_BYTES = 24 * 2**20


def strain_parts(grad_x, grad_y, grad_z):
    return (
        grad_x[0],
        grad_y[1],
        grad_z[2],
        grad_y[0] + grad_x[1],
        grad_z[0] + grad_x[2],
        grad_z[1] + grad_y[2],
    )


def strain_size(parts):
    diagonal = parts[0] * parts[0] + parts[1] * parts[1] + parts[2] * parts[2]
    mixed = parts[3] * parts[3] + parts[4] * parts[4] + parts[5] * parts[5]
    return jnp.sqrt(0.5 * diagonal + 0.25 * mixed)


def beside(blocks):
    count = len(blocks)
    lanes = blocks[0].shape[1]
    down = [pltpu.roll(f, 1, 1) for f in blocks]
    up = [pltpu.roll(f, lanes - 1, 1) for f in blocks]
    if count > 1:
        lane = lax.broadcasted_iota(jnp.int32, blocks[0].shape, 1)
        first, last = lane == 0, lane == lanes - 1
        down, up = (
            [jnp.where(first, down[i - 1], down[i]) for i in range(count)],
            [jnp.where(last, up[(i + 1) % count], up[i]) for i in range(count)],
        )
    return down, up


def slope_z(blocks):
    down, up = beside(blocks)
    return [u - d for u, d in zip(up, down)]


def smooth_z(blocks):
    down, up = beside(blocks)
    return [(u + d) + 2.0 * f for f, u, d in zip(blocks, up, down)]


def band_matrix(n):
    shape = (n, n)
    apart = lax.broadcasted_iota(jnp.int32, shape, 0) - lax.broadcasted_iota(jnp.int32, shape, 1)
    apart = jnp.abs(apart)
    near = jnp.logical_or(apart == 1, apart == n - 1)
    return jnp.where(apart == 0, 2.0, jnp.where(near, 1.0, 0.0)).astype(jnp.bfloat16)


def times_band(f, band):
    total = None
    for i in range(3):
        piece = f.astype(jnp.bfloat16)
        product = jnp.dot(piece, band, preferred_element_type=jnp.float32)
        total = product if total is None else total + product
        if i < 2:
            f = f - piece.astype(jnp.float32)
    return total


def products(v):
    return (v[0] * v[0], v[1] * v[1], v[2] * v[2], v[0] * v[1], v[0] * v[2], v[1] * v[2])


def outer_ranks(count):
    return (count - 1, count - 3)


def places(parity, count):
    outer = outer_ranks(count)
    inner = iter(range(1, count - 1))
    return [
        (0 if outer[parity] == rank else count - 1) if rank in outer else next(inner)
        for rank in range(count)
    ]


def swap_pairs(walls, count):
    odd, even = outer_ranks(count)
    spare = count - 5
    partners = {}

    def join(a, b):
        partners[a], partners[b] = b, a

    def join_walls(rank, first):
        for wall in range(first, walls - 1, 2):
            join((wall, rank), (wall + 1, rank))

    join_walls(even, 0)
    join_walls(odd, 1)
    join_walls(spare, 1)
    join((0, odd), (0, spare))
    if walls % 2 == 0:
        join((walls - 1, odd), (walls - 1, spare))
    for wall in range(walls):
        join((wall, 0), (wall, 1))
    others = [r for r in range(2, count) if r not in (odd, even, spare)]
    for core in range(2):
        ranks = [r for r in others if r % 2 == core]
        first = len(ranks) % 2
        for wall in range(walls):
            for a, b in zip(ranks[first::2], ranks[first + 1 :: 2]):
                join((wall, a), (wall, b))
        for rank in ranks[:first]:
            join_walls(rank, 0)
    return [
        (wall * count + rank, to[0] * count + to[1])
        for wall in range(walls)
        for rank in range(count)
        for to in [partners.get((wall, rank), (wall, rank))]
    ]


def by_parity(parity, count, fill):
    outer = outer_ranks(count)
    for rank, place in enumerate(places(0, count)):
        if rank not in outer:
            fill(rank, place)
    for turn in range(2):

        @pl.when(parity[0] == turn)
        def _():
            for rank in outer:
                fill(rank, places(turn, count)[rank])


def aligned(n):
    return -(-n // 8) * 8


def pack_kernel(rows, parity, velocity, out):
    _, width, cells, _ = velocity.shape
    count, depth, lanes = out.shape
    planes = 3 * width
    slots = planes * rows

    def fill(rank, place):
        first = place * rows
        beside = [first - 1, first + rows]
        if place == 0:
            beside = [first, first + rows]
        if place == count - 1:
            beside = [first + rows - 1, first - 1]
        for i in range(planes):
            c, x = divmod(i, width)
            out[rank, i * rows : (i + 1) * rows, :] = velocity[c, x, first : first + rows, :]
            for slot, row in enumerate(beside):
                at = slots + slot * aligned(planes) + i
                out[rank, at : at + 1, :] = velocity[c, x, row : row + 1, :]

    by_parity(parity, count, fill)
    blank = aligned(planes) - planes
    for rank in range(count):
        for slot in range(2):
            at = slots + slot * aligned(planes) + planes
            out[rank, at : at + blank, :] = jnp.zeros((blank, lanes), jnp.float32)
        at = slots + 2 * aligned(planes)
        if at < depth:
            out[rank, at:, :] = jnp.zeros((depth - at, lanes), jnp.float32)


def outer_sides(rank, parity, count):
    outer = outer_ranks(count)
    even = parity[0] == 0
    bottom = rank[0] == jnp.where(even, outer[0], outer[1])
    top = rank[0] == jnp.where(even, outer[1], outer[0])
    return bottom, top


def edge_kernel(nz_parts, width, rows, walls, rank, position, recv, swapped, given, out, vel):
    count, _, lanes = recv.shape
    planes = 3 * width
    nx = (count // nz_parts) * width
    nz = nz_parts * lanes
    bottom, top = outer_sides(rank, [lax.rem(position[0], 2)], count)
    at_wall = jnp.logical_or(
        jnp.logical_and(bottom, position[0] == 0), jnp.logical_and(top, position[0] == walls - 1)
    )

    def rows_of(k, i):
        first = i * rows
        own = [recv[k, first + j : first + j + 1, :] for j in (0, 1, rows - 2, rows - 1)]
        far = jnp.where(at_wall, 0.0, swapped[k, i : i + 1, :])
        return (
            jnp.where(bottom, far, own[2]),
            jnp.where(bottom, own[0], own[3]),
            jnp.where(bottom, own[1], far),
        )

    def roll_x(f, shift):
        return pltpu.roll(f, shift % nx, 0)

    def roll_z(f, shift):
        return pltpu.roll(f, shift % nz, 1)

    def smooth_x(f):
        return (roll_x(f, 1) + roll_x(f, -1)) + 2.0 * f

    def smooth(f):
        f = smooth_x(f)
        return (roll_z(f, 1) + roll_z(f, -1)) + 2.0 * f

    def slopes(below, centre, above):
        return strain_parts(
            [roll_x(f, -1) - roll_x(f, 1) for f in centre],
            [a - b for a, b in zip(above, below)],
            [roll_z(f, -1) - roll_z(f, 1) for f in centre],
        )

    @pl.when(jnp.logical_or(bottom, top))
    def _():
        for k in range(count):
            x0, zb = (k // nz_parts) * width, k % nz_parts
            for i in range(planes):
                c, x = divmod(i, width)
                for j, row in enumerate(rows_of(k, i)):
                    vel[j, c, x0 + x : x0 + x + 1, zb * lanes : (zb + 1) * lanes] = row
        u = [[vel[j, c] for c in range(3)] for j in range(3)]
        v = [[smooth(f) for f in row] for row in u]
        strain = slopes(*u)
        size = strain_size(strain)
        mean_strain = slopes(*v)
        mean_size = 0.25 * strain_size(mean_strain)
        scaled = [0.0625 * f for f in v[1]]
        pairs = [v[1][i] * scaled[j] for i, j in ((0, 0), (1, 1), (2, 2), (0, 1), (0, 2), (1, 2))]
        leonard = [smooth(p) - q for p, q in zip(products(u[1]), pairs)]
        model = [smooth(size * s) - mean_size * f for s, f in zip(strain, mean_strain)]
        lm, mm = contracted(leonard, model)
        coefficient = coefficient_of(
            *(jnp.sum(f, axis=(0, 1), keepdims=True) for f in (lm, mm)), nx * nz
        )
        eddy = coefficient * size

        def put(at):
            for k in range(count):
                x0, zb = (k // nz_parts) * width, k % nz_parts
                for x in range(width):
                    out[k, x, at : at + 1, :] = eddy[x0 + x : x0 + x + 1, zb * lanes : (zb + 1) * lanes]

        pl.when(bottom)(lambda: put(0))
        pl.when(top)(lambda: put(rows - 1))


def contracted(leonard, model):
    lm = mm = None
    for i in range(6):
        square = model[i] * model[i] if i < 3 else (0.5 * model[i]) * model[i]
        product = leonard[i] * model[i]
        lm = product if lm is None else lm + product
        mm = square if mm is None else mm + square
    return lm, mm


def coefficient_of(plane_lm, plane_mm, cells):
    scale = 1.0 / (256.0 * cells)
    return jnp.maximum(plane_lm * scale / (plane_mm * scale + 1e-06), 0.0)


def germano_kernel(nz_parts, width, rows, rank, parity, recv, out, vel, filt, ends, strains, means, part):
    count, _, lanes = recv.shape
    planes = 3 * width
    _, top = outer_sides(rank, parity, count)
    nx = (count // nz_parts) * width
    nz = nz_parts * lanes
    blocks = range(nz_parts)
    lead = 8
    inner = slice(lead, lead + rows)
    for k in range(count):
        x0, zb = (k // nz_parts) * width, k % nz_parts
        for c in range(3):
            for x in range(width):
                i = c * width + x
                vel[c, x0 + x, zb, inner, :] = recv[k, i * rows : (i + 1) * rows, :]
                slots = planes * rows + i
                near = recv[k, slots : slots + 1, :]
                slots += aligned(planes)
                other = recv[k, slots : slots + 1, :]
                below = jnp.where(top, other, near)
                for side, (edge, at) in enumerate(((below, lead - 1), (other, lead + rows))):
                    vel[c, x0 + x, zb, at : at + 1, :] = edge
                    ends[c, x0 + x, zb, side : side + 1, :] = edge

    lower = slice(lead - 1, lead - 1 + rows)
    upper = slice(lead + 1, lead + 1 + rows)

    def smooth_x(read, x):
        return (read((x - 1) % nx) + read((x + 1) % nx)) + 2.0 * read(x)

    def keep_strain(field, x, kept, scale):
        left, right = (x - 1) % nx, (x + 1) % nx
        grad_z = [slope_z([field[c, x, zb, inner, :] for zb in blocks]) for c in range(3)]
        for zb in blocks:
            grad_x = [field[c, right, zb, inner, :] - field[c, left, zb, inner, :] for c in range(3)]
            grad_y = [field[c, x, zb, upper, :] - field[c, x, zb, lower, :] for c in range(3)]
            parts = strain_parts(grad_x, grad_y, [grad_z[c][zb] for c in range(3)])
            for i in range(6):
                kept[i, x, zb] = parts[i]
            kept[6, x, zb] = scale * strain_size(parts) if scale != 1.0 else strain_size(parts)

    for x in range(nx):
        keep_strain(vel, x, strains, 1.0)
        for c in range(3):
            for zb, f in enumerate(smooth_z([vel[c, x, zb, inner, :] for zb in blocks])):
                part[c, x, zb] = f
    for c in range(3):
        rims = [smooth_z([ends[c, x, zb] for zb in blocks]) for x in range(nx)]
        for x in range(nx):
            for zb in blocks:
                rim = smooth_x(lambda at: rims[at][zb], x)
                filt[c, x, zb, lead - 1 : lead, :] = rim[0:1, :]
                filt[c, x, zb, lead + rows : lead + rows + 1, :] = rim[1:2, :]
                filt[c, x, zb, inner, :] = smooth_x(lambda at: part[c, at, zb], x)
    def filter_z(read, kept):
        if not on_matrix_unit:
            for x in range(nx):
                for zb, f in enumerate(smooth_z([read(x, zb) for zb in blocks])):
                    part[kept, x, zb] = f
            return
        half = nx // 2
        for x0 in (0, half):
            planes_here = [
                jnp.concatenate([read(x, zb) for zb in blocks], axis=1) for x in range(x0, x0 + half)
            ]
            total = times_band(jnp.concatenate(planes_here, axis=0), band)
            for x in range(half):
                for zb in blocks:
                    part[kept, x0 + x, zb] = total[x * rows : (x + 1) * rows, zb * lanes : (zb + 1) * lanes]

    on_matrix_unit = nz <= 256 and rows * nx % 32 == 0 and rows % 8 == 0
    band = band_matrix(nz) if on_matrix_unit else None
    for i, (a, b) in enumerate(((0, 0), (1, 1), (2, 2), (0, 1), (0, 2), (1, 2))):
        filter_z(lambda x, zb: vel[a, x, zb, inner, :] * vel[b, x, zb, inner, :], 3 + i)
        filter_z(lambda x, zb: strains[6, x, zb] * strains[i, x, zb], 9 + i)
    for x in range(nx):
        keep_strain(filt, x, means, 0.25)

    sum_lm = sum_mm = None
    for x in range(nx):
        for zb in blocks:
            v = [filt[c, x, zb, inner, :] for c in range(3)]
            scaled = [0.0625 * f for f in v]
            size = means[6, x, zb]
            for i, (a, b) in enumerate(((0, 0), (1, 1), (2, 2), (0, 1), (0, 2), (1, 2))):
                leonard = smooth_x(lambda at: part[3 + i, at, zb], x) - v[a] * scaled[b]
                model = smooth_x(lambda at: part[9 + i, at, zb], x) - size * means[i, x, zb]
                square = model * model if i < 3 else (0.5 * model) * model
                sum_lm = leonard * model if sum_lm is None else sum_lm + leonard * model
                sum_mm = square if sum_mm is None else sum_mm + square

    coefficient = coefficient_of(
        *(jnp.sum(total, axis=1, keepdims=True) for total in (sum_lm, sum_mm)), nx * nz
    )
    for k in range(count):
        x0, zb = (k // nz_parts) * width, k % nz_parts
        for x in range(width):
            out[k, x] = coefficient * strains[6, x0 + x, zb]


def sweep_kernel(parity, back, velocity, tendency, eddy, reduced, factors, tree):
    count, width, rows, _ = back.shape
    length = count * rows // SEGMENTS

    def fill(rank, place):
        for x in range(width):
            eddy[x, place * rows : (place + 1) * rows, :] = back[rank, x]

    by_parity(parity, count, fill)

    def row(ref, index, j):
        return ref[(*index, pl.ds(j, SEGMENTS, stride=length), slice(None))]

    planes = range(width)
    last_row = length - 1
    visc = [[1.0 + row(eddy, (x,), j) for x in planes] for j in range(length)]
    links = [[750.0 * (v + w) for v, w in zip(visc[j], visc[j + 1])] for j in range(last_row)]

    over = [jnp.ones_like(v) for v in visc[0]]
    under = [jnp.ones_like(v) for v in visc[0]]
    inverses = []
    for j in range(last_row):
        inverses.append([u / (o + e * u) for o, u, e in zip(over, under, links[j])])
        steps = [o * (1.0 / e) for o, e in zip(over, links[j])]
        under, over = (
            [u + t for u, t in zip(under, steps)],
            [(o + u) + t for o, u, t in zip(over, under, steps)],
        )
    inverses.append([u / o for o, u in zip(over, under)])

    value = first = corner = left = None
    reach = [jnp.ones_like(v) for v in visc[0]]
    for j in range(length):
        inverse = inverses[j]
        before = value
        source = [[2.0 * row(velocity, (c, x), j) + row(tendency, (c, x), j) for x in planes] for c in range(3)]
        value = [[f * r for f, r in zip(source[c], inverse)] for c in range(3)]
        if j > 0:
            carry = [e * r for e, r in zip(links[j - 1], inverse)]
            value = [[v + k * w for v, k, w in zip(value[c], carry, before[c])] for c in range(3)]
        left = [m * r for m, r in zip(reach, inverse)]
        if j == 0:
            first, corner = value, left
        else:
            first = [[f + m * v for f, m, v in zip(first[c], reach, value[c])] for c in range(3)]
            corner = [a + m * v for a, m, v in zip(corner, reach, left)]
        ratio = inverse
        if j < last_row:
            ratio = [e * r for e, r in zip(links[j], inverse)]
            reach = [m * r for m, r in zip(reach, ratio)]
        for x in planes:
            for c in range(3):
                factors[x, j, c] = value[c][x]
            factors[x, j, 3] = left[x]
            factors[x, j, 4] = ratio[x]

    def other(fields, step):
        return [pltpu.roll(f, (SEGMENTS - step) % SEGMENTS, 0) if step else f for f in fields]

    last, across, end = value, left, inverse
    seams = [750.0 * (v + w) for v, w in zip(visc[last_row], other(visc[0], 1))]
    level, step = 0, 1
    while step < SEGMENTS:
        link = other(seams, step - 1)
        first_b = [other(f, step) for f in first]
        last_b = [other(f, step) for f in last]
        corner_b, end_b, across_b = other(corner, step), other(end, step), other(across, step)
        stiff = [e / (1.0 + e * (d + a)) for e, d, a in zip(link, end, corner_b)]
        flux = [[k * (g - f) for k, g, f in zip(stiff, last[c], first_b[c])] for c in range(3)]
        from_left = [k * b for k, b in zip(stiff, across)]
        from_right = [k * b for k, b in zip(stiff, across_b)]
        for x in planes:
            for c in range(3):
                tree[x, level, c] = flux[c][x]
            tree[x, level, 3] = from_left[x]
            tree[x, level, 4] = from_right[x]
        first = [[f - b * t for f, b, t in zip(first[c], across, flux[c])] for c in range(3)]
        last = [[g + b * t for g, b, t in zip(last_b[c], across_b, flux[c])] for c in range(3)]
        corner = [a - b * k for a, b, k in zip(corner, across, from_left)]
        end = [d - b * k for d, b, k in zip(end_b, across_b, from_right)]
        across = [k * b for k, b in zip(from_left, across_b)]
        level, step = level + 1, step * 2
    for x in planes:
        rows_out = [f[x][0:1, :] for f in (*first, *last, corner, across, end, visc[0])]
        rows_out.append(visc[last_row][x][SEGMENTS - 1 :, :])
        for i, v in enumerate(rows_out):
            reduced[i * width + x : i * width + x + 1, :] = v


def spread_kernel(factors, tree, velocity, eddy, particular, response, eddy_out, sent):
    write = pltpu.make_async_copy(eddy, eddy_out, sent)
    write.start()
    width, length = factors.shape[:2]
    levels = tree.shape[1]
    sublane = lax.broadcasted_iota(jnp.int32, (SEGMENTS, LANES), 0)
    one, zero = (jnp.full((SEGMENTS, LANES), v, jnp.float32) for v in (1.0, 0.0))
    sides = [(c, zero, zero) for c in range(3)] + [(None, one, zero), (None, zero, one)]
    lefts = [[side[1]] * width for side in sides]
    rights = [[side[2]] * width for side in sides]
    for level in range(levels - 1, -1, -1):
        step = 2**level
        second = lax.rem(sublane, 2 * step) == step
        for n, (c, _, _) in enumerate(sides):
            for x in range(width):
                left, right = lefts[n][x], rights[n][x]
                through = tree[x, level, 3] * left - tree[x, level, 4] * right
                if c is not None:
                    through = tree[x, level, c] + through
                lefts[n][x] = jnp.where(second, pltpu.roll(through, step, 0), left)
                rights[n][x] = jnp.where(second, pltpu.roll(right, step, 0), -through)
    values = rights
    for j in range(length - 1, -1, -1):
        rows = pl.ds(j, SEGMENTS, stride=length)
        for n, (c, _, _) in enumerate(sides):
            for x in range(width):
                value = factors[x, j, 3] * lefts[n][x] + factors[x, j, 4] * values[n][x]
                if c is not None:
                    value = factors[x, j, c] + value
                    particular[c, x, rows, :] = value - velocity[c, x, rows, :]
                else:
                    response[n - 3, x, rows, :] = value
                values[n][x] = value
    write.wait()


def sources_of(step, count):
    ring = [0, *range(1, count, 2), *range(count - 2 + count % 2, 0, -2)]
    return [ring[(ring.index(i) - step) % count] for i in range(count)]


def exchange_order(count):
    return range(count - 1, 0, -1)


def spread_kernel(factors, tree, velocity, eddy, particular, response, eddy_out, sent):
    write = pltpu.make_async_copy(eddy, eddy_out, sent)
    write.start()
    width, length = factors.shape[:2]
    levels = tree.shape[1]
    sublane = lax.broadcasted_iota(jnp.int32, (SEGMENTS, LANES), 0)
    one, zero = (jnp.full((SEGMENTS, LANES), v, jnp.float32) for v in (1.0, 0.0))
    sides = [(c, zero, zero) for c in range(3)] + [(None, one, zero), (None, zero, one)]
    lefts = [[side[1]] * width for side in sides]
    rights = [[side[2]] * width for side in sides]
    for level in range(levels - 1, -1, -1):
        step = 2**level
        second = lax.rem(sublane, 2 * step) == step
        for n, (c, _, _) in enumerate(sides):
            for x in range(width):
                left, right = lefts[n][x], rights[n][x]
                through = tree[x, level, 3] * left - tree[x, level, 4] * right
                if c is not None:
                    through = tree[x, level, c] + through
                lefts[n][x] = jnp.where(second, pltpu.roll(through, step, 0), left)
                rights[n][x] = jnp.where(second, pltpu.roll(right, step, 0), -through)
    values = rights
    for j in range(length - 1, -1, -1):
        rows = pl.ds(j, SEGMENTS, stride=length)
        for n, (c, _, _) in enumerate(sides):
            for x in range(width):
                value = factors[x, j, 3] * lefts[n][x] + factors[x, j, 4] * values[n][x]
                if c is not None:
                    value = factors[x, j, c] + value
                    particular[c, x, rows, :] = value - velocity[c, x, rows, :]
                else:
                    response[n - 3, x, rows, :] = value
                values[n][x] = value
    write.wait()


def partner(i, step, count):
    if count & (count - 1) == 0:
        return i ^ step
    return (i - step + count) % count


def finish_kernel(devices, position, particular, response, *rest):
    reduced, (result, gathered, fluxes, out, sent) = rest[:devices], rest[devices:]
    width = particular.shape[1]
    here = position[0]
    for step, ref in zip([0, *exchange_order(devices)], reduced):
        source = sum(jnp.where(here == i, s, 0) for i, s in enumerate(sources_of(step, devices)))
        gathered[source] = ref[...]

    def part(device, i):
        return gathered[device, i * width : (i + 1) * width, :]

    pivots, sources = [], []
    for i in range(devices + 1):
        visc = [part(i - 1, 10)] if i > 0 else []
        total = [part(i - 1, 8)] if i > 0 else []
        source = [part(i - 1, 3 + c) for c in range(3)] if i > 0 else [0.0] * 3
        if i < devices:
            visc.append(part(i, 9))
            total.append(part(i, 6))
            source = [s - part(i, c) for c, s in enumerate(source)]
        pivots.append(sum(total) + 1.0 / (750.0 * sum(visc)))
        sources.append(source)
    across = [part(i, 7) for i in range(devices)]
    minors = [jnp.ones_like(pivots[0]), pivots[0]]
    for i in range(1, devices + 1):
        minors.append(pivots[i] * minors[i] - (across[i - 1] * across[i - 1]) * minors[i - 1])
    inverses = [minors[i] / minors[i + 1] for i in range(devices + 1)]
    ratios = [b * r for b, r in zip(across, inverses)]
    for i in range(1, devices + 1):
        sources[i] = [s + ratios[i - 1] * t for s, t in zip(sources[i], sources[i - 1])]
    for i in range(devices, -1, -1):
        flux_here = [inverses[i] * s for s in sources[i]]
        flux = flux_here if i == devices else [f + ratios[i] * g for f, g in zip(flux_here, flux)]
        for c in range(3):
            fluxes[i, c * width : (c + 1) * width, :] = flux[c]

    writes = []
    for c in range(3):
        for x in range(width):
            r = c * width + x
            left, right = fluxes[here, r : r + 1, :], fluxes[here + 1, r : r + 1, :]
            out[c, x] = particular[c, x] + (response[0, x] * left - response[1, x] * right)
            writes.append(pltpu.make_async_copy(out.at[c, x], result.at[c, x], sent.at[r]))
            writes[-1].start()
    for write in writes:
        write.wait()


def in_vmem(count):
    return [pl.BlockSpec(memory_space=pltpu.VMEM)] * count


def in_hbm(count):
    return [pl.BlockSpec(memory_space=pltpu.HBM)] * count


def in_smem(count):
    return [pl.BlockSpec(memory_space=pltpu.SMEM)] * count


def params():
    return pltpu.CompilerParams(vmem_limit_bytes=VMEM_BYTES)


def body(velocity, tendency):
    _, width, cells, lanes = velocity.shape
    nz_parts = lax.axis_size("gz")
    count = lax.axis_size("gx") * nz_parts
    walls = lax.axis_size("gy")
    rows = cells // count
    nx = lax.axis_size("gx") * width
    padded = 16 + aligned(rows)
    f32 = jnp.float32

    planes = 3 * width
    depth = aligned(planes * rows + 2 * aligned(planes))
    position = lax.axis_index("gy").astype(jnp.int32).reshape(1)
    parity = lax.rem(position, 2)
    chunks = pl.pallas_call(
        functools.partial(pack_kernel, rows),
        out_shape=jax.ShapeDtypeStruct((count, depth, lanes), f32),
        in_specs=in_smem(1) + in_vmem(1),
        out_specs=pl.BlockSpec(memory_space=pltpu.VMEM),
        compiler_params=params(),
        name="pack",
    )(parity, velocity)
    recv = lax.all_to_all(chunks, ("gx", "gz"), split_axis=0, concat_axis=0, tiled=True)
    slot = lax.slice_in_dim(recv, planes * rows, planes * rows + aligned(planes), axis=1)
    swapped = lax.ppermute(slot, ("gy", "gx", "gz"), swap_pairs(walls, count))
    rank = lax.axis_index(("gx", "gz")).astype(jnp.int32).reshape(1)
    chunk_shape = jax.ShapeDtypeStruct((count, width, rows, lanes), f32)
    cells_here = nx * nz_parts * rows * lanes
    provisional = pl.pallas_call(
        functools.partial(germano_kernel, nz_parts, width, rows),
        out_shape=chunk_shape,
        in_specs=in_smem(2) + in_vmem(1),
        out_specs=pl.BlockSpec(memory_space=pltpu.VMEM),
        scratch_shapes=[
            pltpu.VMEM((3, nx, nz_parts, padded, lanes), f32),
            pltpu.VMEM((3, nx, nz_parts, padded, lanes), f32),
            pltpu.VMEM((3, nx, nz_parts, 8, lanes), f32),
            pltpu.VMEM((7, nx, nz_parts, rows, lanes), f32),
            pltpu.VMEM((7, nx, nz_parts, rows, lanes), f32),
            pltpu.VMEM((15, nx, nz_parts, rows, lanes), f32),
        ],
        compiler_params=params(),
        cost_estimate=pl.CostEstimate(
            flops=300 * cells_here, bytes_accessed=16 * cells_here, transcendentals=2 * cells_here
        ),
        name="germano",
    )(rank, parity, recv)
    eddy_chunks = pl.pallas_call(
        functools.partial(edge_kernel, nz_parts, width, rows, walls),
        out_shape=chunk_shape,
        in_specs=in_smem(2) + in_vmem(3),
        out_specs=pl.BlockSpec(memory_space=pltpu.VMEM),
        scratch_shapes=[pltpu.VMEM((3, 3, nx, nz_parts * lanes), f32)],
        input_output_aliases={4: 0},
        compiler_params=params(),
        name="edge",
    )(rank, position, recv, swapped, provisional)
    back = lax.all_to_all(eddy_chunks, ("gx", "gz"), split_axis=0, concat_axis=0, tiled=True)

    length = cells // SEGMENTS
    levels = SEGMENTS.bit_length() - 1
    packed = aligned(11 * width)
    eddy_here, reduced, factors, tree = pl.pallas_call(
        sweep_kernel,
        out_shape=(
            jax.ShapeDtypeStruct((width, cells, lanes), f32),
            jax.ShapeDtypeStruct((packed, lanes), f32),
            jax.ShapeDtypeStruct((width, length, 5, SEGMENTS, lanes), f32),
            jax.ShapeDtypeStruct((width, levels, 5, SEGMENTS, lanes), f32),
        ),
        in_specs=in_smem(1) + in_vmem(3),
        out_specs=tuple(in_vmem(4)),
        compiler_params=params(),
        name="sweep",
    )(parity, back, velocity, tendency)

    others = [
        lax.ppermute(reduced, "gy", [(s, i) for i, s in enumerate(sources_of(step, walls))])
        for step in exchange_order(walls)
    ]
    particular, response, eddy = pl.pallas_call(
        spread_kernel,
        out_shape=(
            jax.ShapeDtypeStruct(velocity.shape, f32),
            jax.ShapeDtypeStruct((2, *velocity.shape[1:]), f32),
            jax.ShapeDtypeStruct(eddy_here.shape, f32),
        ),
        in_specs=in_vmem(4),
        out_specs=tuple(in_vmem(2) + in_hbm(1)),
        scratch_shapes=[pltpu.SemaphoreType.DMA],
        compiler_params=params(),
        cost_estimate=pl.CostEstimate(
            flops=20 * velocity.size, bytes_accessed=16 * velocity.size, transcendentals=0
        ),
        name="spread",
    )(factors, tree, velocity, eddy_here)
    new_velocity = pl.pallas_call(
        functools.partial(finish_kernel, walls),
        out_shape=jax.ShapeDtypeStruct(velocity.shape, f32),
        in_specs=in_smem(1) + in_vmem(2 + walls),
        out_specs=in_hbm(1)[0],
        scratch_shapes=[
            pltpu.VMEM((walls, packed, lanes), f32),
            pltpu.VMEM((walls + 1, aligned(3 * width), lanes), f32),
            pltpu.VMEM(velocity.shape, f32),
            pltpu.SemaphoreType.DMA((planes,)),
        ],
        compiler_params=params(),
        name="finish",
    )(position, particular, response, reduced, *others)
    return (new_velocity, eddy)


def solution(mesh):
    return jax.shard_map(
        body,
        mesh=mesh,
        in_specs=(P(None, "gx", "gy", "gz"), P(None, "gx", "gy", "gz")),
        out_specs=(P(None, "gx", "gy", "gz"), P("gx", "gy", "gz")),
        check_vma=False,
    )
```

```python
import functools

import jax
import jax.numpy as jnp
from jax import lax
from jax.experimental import pallas as pl
from jax.experimental.pallas import tpu as pltpu
from jax.sharding import PartitionSpec as P

LANES = 128
SEGMENTS = 8
VMEM_BYTES = 24 * 2**20


def strain_parts(grad_x, grad_y, grad_z):
    return (
        grad_x[0],
        grad_y[1],
        grad_z[2],
        grad_y[0] + grad_x[1],
        grad_z[0] + grad_x[2],
        grad_z[1] + grad_y[2],
    )


def strain_size(parts):
    diagonal = parts[0] * parts[0] + parts[1] * parts[1] + parts[2] * parts[2]
    mixed = parts[3] * parts[3] + parts[4] * parts[4] + parts[5] * parts[5]
    return jnp.sqrt(0.5 * diagonal + 0.25 * mixed)


def beside(blocks):
    count = len(blocks)
    lanes = blocks[0].shape[1]
    down = [pltpu.roll(f, 1, 1) for f in blocks]
    up = [pltpu.roll(f, lanes - 1, 1) for f in blocks]
    if count > 1:
        lane = lax.broadcasted_iota(jnp.int32, blocks[0].shape, 1)
        first, last = lane == 0, lane == lanes - 1
        down, up = (
            [jnp.where(first, down[i - 1], down[i]) for i in range(count)],
            [jnp.where(last, up[(i + 1) % count], up[i]) for i in range(count)],
        )
    return down, up


def slope_z(blocks):
    down, up = beside(blocks)
    return [u - d for u, d in zip(up, down)]


def smooth_z(blocks):
    down, up = beside(blocks)
    return [(u + d) + 2.0 * f for f, u, d in zip(blocks, up, down)]


def band_matrix(n):
    shape = (n, n)
    apart = lax.broadcasted_iota(jnp.int32, shape, 0) - lax.broadcasted_iota(jnp.int32, shape, 1)
    apart = jnp.abs(apart)
    near = jnp.logical_or(apart == 1, apart == n - 1)
    return jnp.where(apart == 0, 2.0, jnp.where(near, 1.0, 0.0)).astype(jnp.bfloat16)


def times_band(f, band):
    total = None
    for i in range(3):
        piece = f.astype(jnp.bfloat16)
        product = jnp.dot(piece, band, preferred_element_type=jnp.float32)
        total = product if total is None else total + product
        if i < 2:
            f = f - piece.astype(jnp.float32)
    return total


def products(v):
    return (v[0] * v[0], v[1] * v[1], v[2] * v[2], v[0] * v[1], v[0] * v[2], v[1] * v[2])


def outer_ranks(count):
    return (count - 3, count - 1)


def places(parity, count):
    outer = outer_ranks(count)
    inner = iter(range(1, count - 1))
    return [
        (0 if outer[parity] == rank else count - 1) if rank in outer else next(inner)
        for rank in range(count)
    ]


def swap_pairs(walls, count):
    odd, even = outer_ranks(count)
    partners = {}

    def join(a, b):
        partners[a], partners[b] = b, a

    for core in range(0, count, 2):
        here = (core, core + 1)
        if odd in here or even in here:
            first = 1 if odd in here else 0
            for wall in range(first, walls - 1, 2):
                for rank in here:
                    join((wall, rank), (wall + 1, rank))
        for wall in range(walls):
            if (wall, core) not in partners:
                join((wall, core), (wall, core + 1))
    return [
        (wall * count + rank, to[0] * count + to[1])
        for wall in range(walls)
        for rank in range(count)
        for to in [partners.get((wall, rank), (wall, rank))]
    ]


def by_parity(parity, count, fill):
    outer = outer_ranks(count)
    for rank, place in enumerate(places(0, count)):
        if rank not in outer:
            fill(rank, place)
    for turn in range(2):

        @pl.when(parity[0] == turn)
        def _():
            for rank in outer:
                fill(rank, places(turn, count)[rank])


def aligned(n):
    return -(-n // 8) * 8


def pack_kernel(rows, parity, velocity, out):
    _, width, cells, _ = velocity.shape
    count, depth, lanes = out.shape
    planes = 3 * width
    slots = planes * rows

    def fill(rank, place):
        first = place * rows
        beside = [first - 1, first + rows]
        if place == 0:
            beside = [first, first + rows]
        if place == count - 1:
            beside = [first + rows - 1, first - 1]
        for i in range(planes):
            c, x = divmod(i, width)
            out[rank, i * rows : (i + 1) * rows, :] = velocity[c, x, first : first + rows, :]
            for slot, row in enumerate(beside):
                at = slots + slot * aligned(planes) + i
                out[rank, at : at + 1, :] = velocity[c, x, row : row + 1, :]

    by_parity(parity, count, fill)
    blank = aligned(planes) - planes
    for rank in range(count):
        for slot in range(2):
            at = slots + slot * aligned(planes) + planes
            out[rank, at : at + blank, :] = jnp.zeros((blank, lanes), jnp.float32)
        at = slots + 2 * aligned(planes)
        if at < depth:
            out[rank, at:, :] = jnp.zeros((depth - at, lanes), jnp.float32)


def outer_sides(rank, parity, count):
    outer = outer_ranks(count)
    even = parity[0] == 0
    bottom = rank[0] == jnp.where(even, outer[0], outer[1])
    top = rank[0] == jnp.where(even, outer[1], outer[0])
    return bottom, top


def edge_kernel(nz_parts, width, rows, walls, rank, position, recv, swapped, given, out, vel):
    count, _, lanes = recv.shape
    planes = 3 * width
    nx = (count // nz_parts) * width
    nz = nz_parts * lanes
    bottom, top = outer_sides(rank, [lax.rem(position[0], 2)], count)
    at_wall = jnp.logical_or(
        jnp.logical_and(bottom, position[0] == 0), jnp.logical_and(top, position[0] == walls - 1)
    )

    def rows_of(k, i):
        first = i * rows
        own = [recv[k, first + j : first + j + 1, :] for j in (0, 1, rows - 2, rows - 1)]
        far = jnp.where(at_wall, 0.0, swapped[k, i : i + 1, :])
        return (
            jnp.where(bottom, far, own[2]),
            jnp.where(bottom, own[0], own[3]),
            jnp.where(bottom, own[1], far),
        )

    def roll_x(f, shift):
        return pltpu.roll(f, shift % nx, 0)

    def roll_z(f, shift):
        return pltpu.roll(f, shift % nz, 1)

    def smooth_x(f):
        return (roll_x(f, 1) + roll_x(f, -1)) + 2.0 * f

    def smooth(f):
        f = smooth_x(f)
        return (roll_z(f, 1) + roll_z(f, -1)) + 2.0 * f

    def slopes(below, centre, above):
        return strain_parts(
            [roll_x(f, -1) - roll_x(f, 1) for f in centre],
            [a - b for a, b in zip(above, below)],
            [roll_z(f, -1) - roll_z(f, 1) for f in centre],
        )

    @pl.when(jnp.logical_or(bottom, top))
    def _():
        for k in range(count):
            x0, zb = (k // nz_parts) * width, k % nz_parts
            for i in range(planes):
                c, x = divmod(i, width)
                for j, row in enumerate(rows_of(k, i)):
                    vel[j, c, x0 + x : x0 + x + 1, zb * lanes : (zb + 1) * lanes] = row
        u = [[vel[j, c] for c in range(3)] for j in range(3)]
        v = [[smooth(f) for f in row] for row in u]
        strain = slopes(*u)
        size = strain_size(strain)
        mean_strain = slopes(*v)
        mean_size = 0.25 * strain_size(mean_strain)
        scaled = [0.0625 * f for f in v[1]]
        pairs = [v[1][i] * scaled[j] for i, j in ((0, 0), (1, 1), (2, 2), (0, 1), (0, 2), (1, 2))]
        leonard = [smooth(p) - q for p, q in zip(products(u[1]), pairs)]
        model = [smooth(size * s) - mean_size * f for s, f in zip(strain, mean_strain)]
        lm, mm = contracted(leonard, model)
        coefficient = coefficient_of(
            *(jnp.sum(f, axis=(0, 1), keepdims=True) for f in (lm, mm)), nx * nz
        )
        eddy = coefficient * size

        def put(at):
            for k in range(count):
                x0, zb = (k // nz_parts) * width, k % nz_parts
                for x in range(width):
                    out[k, x, at : at + 1, :] = eddy[x0 + x : x0 + x + 1, zb * lanes : (zb + 1) * lanes]

        pl.when(bottom)(lambda: put(0))
        pl.when(top)(lambda: put(rows - 1))


def contracted(leonard, model):
    lm = mm = None
    for i in range(6):
        square = model[i] * model[i] if i < 3 else (0.5 * model[i]) * model[i]
        product = leonard[i] * model[i]
        lm = product if lm is None else lm + product
        mm = square if mm is None else mm + square
    return lm, mm


def coefficient_of(plane_lm, plane_mm, cells):
    scale = 1.0 / (256.0 * cells)
    return jnp.maximum(plane_lm * scale / (plane_mm * scale + 1e-06), 0.0)


def germano_kernel(nz_parts, width, rows, rank, parity, recv, out, vel, filt, ends, strains, means, part):
    count, _, lanes = recv.shape
    planes = 3 * width
    _, top = outer_sides(rank, parity, count)
    nx = (count // nz_parts) * width
    nz = nz_parts * lanes
    blocks = range(nz_parts)
    lead = 8
    inner = slice(lead, lead + rows)
    for k in range(count):
        x0, zb = (k // nz_parts) * width, k % nz_parts
        for c in range(3):
            for x in range(width):
                i = c * width + x
                vel[c, x0 + x, zb, inner, :] = recv[k, i * rows : (i + 1) * rows, :]
                slots = planes * rows + i
                near = recv[k, slots : slots + 1, :]
                slots += aligned(planes)
                other = recv[k, slots : slots + 1, :]
                below = jnp.where(top, other, near)
                for side, (edge, at) in enumerate(((below, lead - 1), (other, lead + rows))):
                    vel[c, x0 + x, zb, at : at + 1, :] = edge
                    ends[c, x0 + x, zb, side : side + 1, :] = edge

    lower = slice(lead - 1, lead - 1 + rows)
    upper = slice(lead + 1, lead + 1 + rows)

    def smooth_x(read, x):
        return (read((x - 1) % nx) + read((x + 1) % nx)) + 2.0 * read(x)

    def keep_strain(field, x, kept, scale):
        left, right = (x - 1) % nx, (x + 1) % nx
        grad_z = [slope_z([field[c, x, zb, inner, :] for zb in blocks]) for c in range(3)]
        for zb in blocks:
            grad_x = [field[c, right, zb, inner, :] - field[c, left, zb, inner, :] for c in range(3)]
            grad_y = [field[c, x, zb, upper, :] - field[c, x, zb, lower, :] for c in range(3)]
            parts = strain_parts(grad_x, grad_y, [grad_z[c][zb] for c in range(3)])
            for i in range(6):
                kept[i, x, zb] = parts[i]
            kept[6, x, zb] = scale * strain_size(parts) if scale != 1.0 else strain_size(parts)

    for x in range(nx):
        keep_strain(vel, x, strains, 1.0)
        for c in range(3):
            for zb, f in enumerate(smooth_z([vel[c, x, zb, inner, :] for zb in blocks])):
                part[c, x, zb] = f
    for c in range(3):
        rims = [smooth_z([ends[c, x, zb] for zb in blocks]) for x in range(nx)]
        for x in range(nx):
            for zb in blocks:
                rim = smooth_x(lambda at: rims[at][zb], x)
                filt[c, x, zb, lead - 1 : lead, :] = rim[0:1, :]
                filt[c, x, zb, lead + rows : lead + rows + 1, :] = rim[1:2, :]
                filt[c, x, zb, inner, :] = smooth_x(lambda at: part[c, at, zb], x)
    def filter_z(read, kept):
        if not on_matrix_unit:
            for x in range(nx):
                for zb, f in enumerate(smooth_z([read(x, zb) for zb in blocks])):
                    part[kept, x, zb] = f
            return
        half = nx // 2
        for x0 in (0, half):
            planes_here = [
                jnp.concatenate([read(x, zb) for zb in blocks], axis=1) for x in range(x0, x0 + half)
            ]
            total = times_band(jnp.concatenate(planes_here, axis=0), band)
            for x in range(half):
                for zb in blocks:
                    part[kept, x0 + x, zb] = total[x * rows : (x + 1) * rows, zb * lanes : (zb + 1) * lanes]

    on_matrix_unit = nz <= 256 and rows * nx % 32 == 0 and rows % 8 == 0
    band = band_matrix(nz) if on_matrix_unit else None
    for i, (a, b) in enumerate(((0, 0), (1, 1), (2, 2), (0, 1), (0, 2), (1, 2))):
        filter_z(lambda x, zb: vel[a, x, zb, inner, :] * vel[b, x, zb, inner, :], 3 + i)
        filter_z(lambda x, zb: strains[6, x, zb] * strains[i, x, zb], 9 + i)
    for x in range(nx):
        keep_strain(filt, x, means, 0.25)

    sum_lm = sum_mm = None
    for x in range(nx):
        for zb in blocks:
            v = [filt[c, x, zb, inner, :] for c in range(3)]
            scaled = [0.0625 * f for f in v]
            size = means[6, x, zb]
            for i, (a, b) in enumerate(((0, 0), (1, 1), (2, 2), (0, 1), (0, 2), (1, 2))):
                leonard = smooth_x(lambda at: part[3 + i, at, zb], x) - v[a] * scaled[b]
                model = smooth_x(lambda at: part[9 + i, at, zb], x) - size * means[i, x, zb]
                square = model * model if i < 3 else (0.5 * model) * model
                sum_lm = leonard * model if sum_lm is None else sum_lm + leonard * model
                sum_mm = square if sum_mm is None else sum_mm + square

    coefficient = coefficient_of(
        *(jnp.sum(total, axis=1, keepdims=True) for total in (sum_lm, sum_mm)), nx * nz
    )
    for k in range(count):
        x0, zb = (k // nz_parts) * width, k % nz_parts
        for x in range(width):
            out[k, x] = coefficient * strains[6, x0 + x, zb]


def sweep_kernel(parity, back, velocity, tendency, eddy, reduced, factors, tree):
    count, width, rows, _ = back.shape
    length = count * rows // SEGMENTS

    def fill(rank, place):
        for x in range(width):
            eddy[x, place * rows : (place + 1) * rows, :] = back[rank, x]

    by_parity(parity, count, fill)

    def row(ref, index, j):
        return ref[(*index, pl.ds(j, SEGMENTS, stride=length), slice(None))]

    planes = range(width)
    last_row = length - 1
    visc = [[1.0 + row(eddy, (x,), j) for x in planes] for j in range(length)]
    links = [[750.0 * (v + w) for v, w in zip(visc[j], visc[j + 1])] for j in range(last_row)]

    over = [jnp.ones_like(v) for v in visc[0]]
    under = [jnp.ones_like(v) for v in visc[0]]
    inverses = []
    for j in range(last_row):
        inverses.append([u / (o + e * u) for o, u, e in zip(over, under, links[j])])
        steps = [o * (1.0 / e) for o, e in zip(over, links[j])]
        under, over = (
            [u + t for u, t in zip(under, steps)],
            [(o + u) + t for o, u, t in zip(over, under, steps)],
        )
    inverses.append([u / o for o, u in zip(over, under)])

    value = first = corner = left = None
    reach = [jnp.ones_like(v) for v in visc[0]]
    for j in range(length):
        inverse = inverses[j]
        before = value
        source = [[2.0 * row(velocity, (c, x), j) + row(tendency, (c, x), j) for x in planes] for c in range(3)]
        value = [[f * r for f, r in zip(source[c], inverse)] for c in range(3)]
        if j > 0:
            carry = [e * r for e, r in zip(links[j - 1], inverse)]
            value = [[v + k * w for v, k, w in zip(value[c], carry, before[c])] for c in range(3)]
        left = [m * r for m, r in zip(reach, inverse)]
        if j == 0:
            first, corner = value, left
        else:
            first = [[f + m * v for f, m, v in zip(first[c], reach, value[c])] for c in range(3)]
            corner = [a + m * v for a, m, v in zip(corner, reach, left)]
        ratio = inverse
        if j < last_row:
            ratio = [e * r for e, r in zip(links[j], inverse)]
            reach = [m * r for m, r in zip(reach, ratio)]
        for x in planes:
            for c in range(3):
                factors[x, j, c] = value[c][x]
            factors[x, j, 3] = left[x]
            factors[x, j, 4] = ratio[x]

    def other(fields, step):
        return [pltpu.roll(f, (SEGMENTS - step) % SEGMENTS, 0) if step else f for f in fields]

    last, across, end = value, left, inverse
    seams = [750.0 * (v + w) for v, w in zip(visc[last_row], other(visc[0], 1))]
    level, step = 0, 1
    while step < SEGMENTS:
        link = other(seams, step - 1)
        first_b = [other(f, step) for f in first]
        last_b = [other(f, step) for f in last]
        corner_b, end_b, across_b = other(corner, step), other(end, step), other(across, step)
        stiff = [e / (1.0 + e * (d + a)) for e, d, a in zip(link, end, corner_b)]
        flux = [[k * (g - f) for k, g, f in zip(stiff, last[c], first_b[c])] for c in range(3)]
        from_left = [k * b for k, b in zip(stiff, across)]
        from_right = [k * b for k, b in zip(stiff, across_b)]
        for x in planes:
            for c in range(3):
                tree[x, level, c] = flux[c][x]
            tree[x, level, 3] = from_left[x]
            tree[x, level, 4] = from_right[x]
        first = [[f - b * t for f, b, t in zip(first[c], across, flux[c])] for c in range(3)]
        last = [[g + b * t for g, b, t in zip(last_b[c], across_b, flux[c])] for c in range(3)]
        corner = [a - b * k for a, b, k in zip(corner, across, from_left)]
        end = [d - b * k for d, b, k in zip(end_b, across_b, from_right)]
        across = [k * b for k, b in zip(from_left, across_b)]
        level, step = level + 1, step * 2
    for x in planes:
        rows_out = [f[x][0:1, :] for f in (*first, *last, corner, across, end, visc[0])]
        rows_out.append(visc[last_row][x][SEGMENTS - 1 :, :])
        for i, v in enumerate(rows_out):
            reduced[i * width + x : i * width + x + 1, :] = v


def spread_kernel(factors, tree, velocity, eddy, particular, response, eddy_out, sent):
    write = pltpu.make_async_copy(eddy, eddy_out, sent)
    write.start()
    width, length = factors.shape[:2]
    levels = tree.shape[1]
    sublane = lax.broadcasted_iota(jnp.int32, (SEGMENTS, LANES), 0)
    one, zero = (jnp.full((SEGMENTS, LANES), v, jnp.float32) for v in (1.0, 0.0))
    sides = [(c, zero, zero) for c in range(3)] + [(None, one, zero), (None, zero, one)]
    lefts = [[side[1]] * width for side in sides]
    rights = [[side[2]] * width for side in sides]
    for level in range(levels - 1, -1, -1):
        step = 2**level
        second = lax.rem(sublane, 2 * step) == step
        for n, (c, _, _) in enumerate(sides):
            for x in range(width):
                left, right = lefts[n][x], rights[n][x]
                through = tree[x, level, 3] * left - tree[x, level, 4] * right
                if c is not None:
                    through = tree[x, level, c] + through
                lefts[n][x] = jnp.where(second, pltpu.roll(through, step, 0), left)
                rights[n][x] = jnp.where(second, pltpu.roll(right, step, 0), -through)
    values = rights
    for j in range(length - 1, -1, -1):
        rows = pl.ds(j, SEGMENTS, stride=length)
        for n, (c, _, _) in enumerate(sides):
            for x in range(width):
                value = factors[x, j, 3] * lefts[n][x] + factors[x, j, 4] * values[n][x]
                if c is not None:
                    value = factors[x, j, c] + value
                    particular[c, x, rows, :] = value - velocity[c, x, rows, :]
                else:
                    response[n - 3, x, rows, :] = value
                values[n][x] = value
    write.wait()


def sources_of(step, count):
    ring = [0, *range(1, count, 2), *range(count - 2 + count % 2, 0, -2)]
    return [ring[(ring.index(i) - step) % count] for i in range(count)]


def exchange_order(count):
    return range(count - 1, 0, -1)


def spread_kernel(factors, tree, velocity, eddy, particular, response, eddy_out, sent):
    write = pltpu.make_async_copy(eddy, eddy_out, sent)
    write.start()
    width, length = factors.shape[:2]
    levels = tree.shape[1]
    sublane = lax.broadcasted_iota(jnp.int32, (SEGMENTS, LANES), 0)
    one, zero = (jnp.full((SEGMENTS, LANES), v, jnp.float32) for v in (1.0, 0.0))
    sides = [(c, zero, zero) for c in range(3)] + [(None, one, zero), (None, zero, one)]
    lefts = [[side[1]] * width for side in sides]
    rights = [[side[2]] * width for side in sides]
    for level in range(levels - 1, -1, -1):
        step = 2**level
        second = lax.rem(sublane, 2 * step) == step
        for n, (c, _, _) in enumerate(sides):
            for x in range(width):
                left, right = lefts[n][x], rights[n][x]
                through = tree[x, level, 3] * left - tree[x, level, 4] * right
                if c is not None:
                    through = tree[x, level, c] + through
                lefts[n][x] = jnp.where(second, pltpu.roll(through, step, 0), left)
                rights[n][x] = jnp.where(second, pltpu.roll(right, step, 0), -through)
    values = rights
    for j in range(length - 1, -1, -1):
        rows = pl.ds(j, SEGMENTS, stride=length)
        for n, (c, _, _) in enumerate(sides):
            for x in range(width):
                value = factors[x, j, 3] * lefts[n][x] + factors[x, j, 4] * values[n][x]
                if c is not None:
                    value = factors[x, j, c] + value
                    particular[c, x, rows, :] = value - velocity[c, x, rows, :]
                else:
                    response[n - 3, x, rows, :] = value
                values[n][x] = value
    write.wait()


def partner(i, step, count):
    if count & (count - 1) == 0:
        return i ^ step
    return (i - step + count) % count


def finish_kernel(devices, position, particular, response, *rest):
    reduced, (result, gathered, fluxes, out, sent) = rest[:devices], rest[devices:]
    width = particular.shape[1]
    here = position[0]
    for step, ref in zip([0, *exchange_order(devices)], reduced):
        source = sum(jnp.where(here == i, s, 0) for i, s in enumerate(sources_of(step, devices)))
        gathered[source] = ref[...]

    def part(device, i):
        return gathered[device, i * width : (i + 1) * width, :]

    pivots, sources = [], []
    for i in range(devices + 1):
        visc = [part(i - 1, 10)] if i > 0 else []
        total = [part(i - 1, 8)] if i > 0 else []
        source = [part(i - 1, 3 + c) for c in range(3)] if i > 0 else [0.0] * 3
        if i < devices:
            visc.append(part(i, 9))
            total.append(part(i, 6))
            source = [s - part(i, c) for c, s in enumerate(source)]
        pivots.append(sum(total) + 1.0 / (750.0 * sum(visc)))
        sources.append(source)
    across = [part(i, 7) for i in range(devices)]
    minors = [jnp.ones_like(pivots[0]), pivots[0]]
    for i in range(1, devices + 1):
        minors.append(pivots[i] * minors[i] - (across[i - 1] * across[i - 1]) * minors[i - 1])
    inverses = [minors[i] / minors[i + 1] for i in range(devices + 1)]
    ratios = [b * r for b, r in zip(across, inverses)]
    for i in range(1, devices + 1):
        sources[i] = [s + ratios[i - 1] * t for s, t in zip(sources[i], sources[i - 1])]
    for i in range(devices, -1, -1):
        flux_here = [inverses[i] * s for s in sources[i]]
        flux = flux_here if i == devices else [f + ratios[i] * g for f, g in zip(flux_here, flux)]
        for c in range(3):
            fluxes[i, c * width : (c + 1) * width, :] = flux[c]

    writes = []
    for c in range(3):
        for x in range(width):
            r = c * width + x
            left, right = fluxes[here, r : r + 1, :], fluxes[here + 1, r : r + 1, :]
            out[c, x] = particular[c, x] + (response[0, x] * left - response[1, x] * right)
            writes.append(pltpu.make_async_copy(out.at[c, x], result.at[c, x], sent.at[r]))
            writes[-1].start()
    for write in writes:
        write.wait()


def in_vmem(count):
    return [pl.BlockSpec(memory_space=pltpu.VMEM)] * count


def in_hbm(count):
    return [pl.BlockSpec(memory_space=pltpu.HBM)] * count


def in_smem(count):
    return [pl.BlockSpec(memory_space=pltpu.SMEM)] * count


def params():
    return pltpu.CompilerParams(vmem_limit_bytes=VMEM_BYTES)


def body(velocity, tendency):
    _, width, cells, lanes = velocity.shape
    nz_parts = lax.axis_size("gz")
    count = lax.axis_size("gx") * nz_parts
    walls = lax.axis_size("gy")
    rows = cells // count
    nx = lax.axis_size("gx") * width
    padded = 16 + aligned(rows)
    f32 = jnp.float32

    planes = 3 * width
    depth = aligned(planes * rows + 2 * aligned(planes))
    position = lax.axis_index("gy").astype(jnp.int32).reshape(1)
    parity = lax.rem(position, 2)
    chunks = pl.pallas_call(
        functools.partial(pack_kernel, rows),
        out_shape=jax.ShapeDtypeStruct((count, depth, lanes), f32),
        in_specs=in_smem(1) + in_vmem(1),
        out_specs=pl.BlockSpec(memory_space=pltpu.VMEM),
        compiler_params=params(),
        name="pack",
    )(parity, velocity)
    recv = lax.all_to_all(chunks, ("gx", "gz"), split_axis=0, concat_axis=0, tiled=True)
    slot = lax.slice_in_dim(recv, planes * rows, planes * rows + aligned(planes), axis=1)
    swapped = lax.ppermute(slot, ("gy", "gx", "gz"), swap_pairs(walls, count))
    rank = lax.axis_index(("gx", "gz")).astype(jnp.int32).reshape(1)
    chunk_shape = jax.ShapeDtypeStruct((count, width, rows, lanes), f32)
    cells_here = nx * nz_parts * rows * lanes
    provisional = pl.pallas_call(
        functools.partial(germano_kernel, nz_parts, width, rows),
        out_shape=chunk_shape,
        in_specs=in_smem(2) + in_vmem(1),
        out_specs=pl.BlockSpec(memory_space=pltpu.VMEM),
        scratch_shapes=[
            pltpu.VMEM((3, nx, nz_parts, padded, lanes), f32),
            pltpu.VMEM((3, nx, nz_parts, padded, lanes), f32),
            pltpu.VMEM((3, nx, nz_parts, 8, lanes), f32),
            pltpu.VMEM((7, nx, nz_parts, rows, lanes), f32),
            pltpu.VMEM((7, nx, nz_parts, rows, lanes), f32),
            pltpu.VMEM((15, nx, nz_parts, rows, lanes), f32),
        ],
        compiler_params=params(),
        cost_estimate=pl.CostEstimate(
            flops=300 * cells_here, bytes_accessed=16 * cells_here, transcendentals=2 * cells_here
        ),
        name="germano",
    )(rank, parity, recv)
    eddy_chunks = pl.pallas_call(
        functools.partial(edge_kernel, nz_parts, width, rows, walls),
        out_shape=chunk_shape,
        in_specs=in_smem(2) + in_vmem(3),
        out_specs=pl.BlockSpec(memory_space=pltpu.VMEM),
        scratch_shapes=[pltpu.VMEM((3, 3, nx, nz_parts * lanes), f32)],
        input_output_aliases={4: 0},
        compiler_params=params(),
        name="edge",
    )(rank, position, recv, swapped, provisional)
    back = lax.all_to_all(eddy_chunks, ("gx", "gz"), split_axis=0, concat_axis=0, tiled=True)

    length = cells // SEGMENTS
    levels = SEGMENTS.bit_length() - 1
    packed = aligned(11 * width)
    eddy_here, reduced, factors, tree = pl.pallas_call(
        sweep_kernel,
        out_shape=(
            jax.ShapeDtypeStruct((width, cells, lanes), f32),
            jax.ShapeDtypeStruct((packed, lanes), f32),
            jax.ShapeDtypeStruct((width, length, 5, SEGMENTS, lanes), f32),
            jax.ShapeDtypeStruct((width, levels, 5, SEGMENTS, lanes), f32),
        ),
        in_specs=in_smem(1) + in_vmem(3),
        out_specs=tuple(in_vmem(4)),
        compiler_params=params(),
        name="sweep",
    )(parity, back, velocity, tendency)

    others = [
        lax.ppermute(reduced, "gy", [(s, i) for i, s in enumerate(sources_of(step, walls))])
        for step in exchange_order(walls)
    ]
    particular, response, eddy = pl.pallas_call(
        spread_kernel,
        out_shape=(
            jax.ShapeDtypeStruct(velocity.shape, f32),
            jax.ShapeDtypeStruct((2, *velocity.shape[1:]), f32),
            jax.ShapeDtypeStruct(eddy_here.shape, f32),
        ),
        in_specs=in_vmem(4),
        out_specs=tuple(in_vmem(2) + in_hbm(1)),
        scratch_shapes=[pltpu.SemaphoreType.DMA],
        compiler_params=params(),
        cost_estimate=pl.CostEstimate(
            flops=20 * velocity.size, bytes_accessed=16 * velocity.size, transcendentals=0
        ),
        name="spread",
    )(factors, tree, velocity, eddy_here)
    new_velocity = pl.pallas_call(
        functools.partial(finish_kernel, walls),
        out_shape=jax.ShapeDtypeStruct(velocity.shape, f32),
        in_specs=in_smem(1) + in_vmem(2 + walls),
        out_specs=in_hbm(1)[0],
        scratch_shapes=[
            pltpu.VMEM((walls, packed, lanes), f32),
            pltpu.VMEM((walls + 1, aligned(3 * width), lanes), f32),
            pltpu.VMEM(velocity.shape, f32),
            pltpu.SemaphoreType.DMA((planes,)),
        ],
        compiler_params=params(),
        name="finish",
    )(position, particular, response, reduced, *others)
    return (new_velocity, eddy)


def solution(mesh):
    return jax.shard_map(
        body,
        mesh=mesh,
        in_specs=(P(None, "gx", "gy", "gz"), P(None, "gx", "gy", "gz")),
        out_specs=(P(None, "gx", "gy", "gz"), P("gx", "gy", "gz")),
        check_vma=False,
    )
```

```python
import functools

import jax
import jax.numpy as jnp
from jax import lax
from jax.experimental import pallas as pl
from jax.experimental.pallas import tpu as pltpu
from jax.sharding import PartitionSpec as P

LANES = 128
SEGMENTS = 8
VMEM_BYTES = 24 * 2**20


def strain_parts(grad_x, grad_y, grad_z):
    return (
        grad_x[0],
        grad_y[1],
        grad_z[2],
        grad_y[0] + grad_x[1],
        grad_z[0] + grad_x[2],
        grad_z[1] + grad_y[2],
    )


def strain_size(parts):
    diagonal = parts[0] * parts[0] + parts[1] * parts[1] + parts[2] * parts[2]
    mixed = parts[3] * parts[3] + parts[4] * parts[4] + parts[5] * parts[5]
    return jnp.sqrt(0.5 * diagonal + 0.25 * mixed)


def beside(blocks):
    count = len(blocks)
    lanes = blocks[0].shape[1]
    down = [pltpu.roll(f, 1, 1) for f in blocks]
    up = [pltpu.roll(f, lanes - 1, 1) for f in blocks]
    if count > 1:
        lane = lax.broadcasted_iota(jnp.int32, blocks[0].shape, 1)
        first, last = lane == 0, lane == lanes - 1
        down, up = (
            [jnp.where(first, down[i - 1], down[i]) for i in range(count)],
            [jnp.where(last, up[(i + 1) % count], up[i]) for i in range(count)],
        )
    return down, up


def slope_z(blocks):
    down, up = beside(blocks)
    return [u - d for u, d in zip(up, down)]


def smooth_z(blocks):
    down, up = beside(blocks)
    return [(u + d) + 2.0 * f for f, u, d in zip(blocks, up, down)]


def band_matrix(n):
    shape = (n, n)
    apart = lax.broadcasted_iota(jnp.int32, shape, 0) - lax.broadcasted_iota(jnp.int32, shape, 1)
    apart = jnp.abs(apart)
    near = jnp.logical_or(apart == 1, apart == n - 1)
    return jnp.where(apart == 0, 2.0, jnp.where(near, 1.0, 0.0)).astype(jnp.bfloat16)


def times_band(f, band):
    total = None
    for i in range(3):
        piece = f.astype(jnp.bfloat16)
        product = jnp.dot(piece, band, preferred_element_type=jnp.float32)
        total = product if total is None else total + product
        if i < 2:
            f = f - piece.astype(jnp.float32)
    return total


def products(v):
    return (v[0] * v[0], v[1] * v[1], v[2] * v[2], v[0] * v[1], v[0] * v[2], v[1] * v[2])


def outer_ranks(count):
    return (count - 3, count - 1)


def places(parity, count):
    outer = outer_ranks(count)
    inner = iter(range(1, count - 1))
    return [
        (0 if outer[parity] == rank else count - 1) if rank in outer else next(inner)
        for rank in range(count)
    ]


def swap_pairs(walls, count):
    odd, even = outer_ranks(count)
    partners = {}

    def join(a, b):
        partners[a], partners[b] = b, a

    for core in range(0, count, 2):
        here = (core, core + 1)
        if odd in here or even in here:
            first = 1 if odd in here else 0
            for wall in range(first, walls - 1, 2):
                for rank in here:
                    join((wall, rank), (wall + 1, rank))
        for wall in range(walls):
            if (wall, core) not in partners:
                join((wall, core), (wall, core + 1))
    return [
        (wall * count + rank, to[0] * count + to[1])
        for wall in range(walls)
        for rank in range(count)
        for to in [partners.get((wall, rank), (wall, rank))]
    ]


def by_parity(parity, count, fill):
    outer = outer_ranks(count)
    for rank, place in enumerate(places(0, count)):
        if rank not in outer:
            fill(rank, place)
    for turn in range(2):

        @pl.when(parity[0] == turn)
        def _():
            for rank in outer:
                fill(rank, places(turn, count)[rank])


def aligned(n):
    return -(-n // 8) * 8


def pack_kernel(rows, parity, velocity, out):
    _, width, cells, _ = velocity.shape
    count, depth, lanes = out.shape
    planes = 3 * width
    slots = planes * rows

    def fill(rank, place):
        first = place * rows
        beside = [first - 1, first + rows]
        if place == 0:
            beside = [first, first + rows]
        if place == count - 1:
            beside = [first + rows - 1, first - 1]
        for i in range(planes):
            c, x = divmod(i, width)
            out[rank, i * rows : (i + 1) * rows, :] = velocity[c, x, first : first + rows, :]
            for slot, row in enumerate(beside):
                at = slots + slot * aligned(planes) + i
                out[rank, at : at + 1, :] = velocity[c, x, row : row + 1, :]

    by_parity(parity, count, fill)
    blank = aligned(planes) - planes
    for rank in range(count):
        for slot in range(2):
            at = slots + slot * aligned(planes) + planes
            out[rank, at : at + blank, :] = jnp.zeros((blank, lanes), jnp.float32)
        at = slots + 2 * aligned(planes)
        if at < depth:
            out[rank, at:, :] = jnp.zeros((depth - at, lanes), jnp.float32)


def outer_sides(rank, parity, count):
    outer = outer_ranks(count)
    even = parity[0] == 0
    bottom = rank[0] == jnp.where(even, outer[0], outer[1])
    top = rank[0] == jnp.where(even, outer[1], outer[0])
    return bottom, top


def edge_kernel(nz_parts, width, rows, walls, rank, position, recv, swapped, given, out, vel):
    count, _, lanes = recv.shape
    planes = 3 * width
    nx = (count // nz_parts) * width
    nz = nz_parts * lanes
    bottom, top = outer_sides(rank, [lax.rem(position[0], 2)], count)
    at_wall = jnp.logical_or(
        jnp.logical_and(bottom, position[0] == 0), jnp.logical_and(top, position[0] == walls - 1)
    )

    def rows_of(k, i):
        first = i * rows
        own = [recv[k, first + j : first + j + 1, :] for j in (0, 1, rows - 2, rows - 1)]
        far = jnp.where(at_wall, 0.0, swapped[k, i : i + 1, :])
        return (
            jnp.where(bottom, far, own[2]),
            jnp.where(bottom, own[0], own[3]),
            jnp.where(bottom, own[1], far),
        )

    def roll_x(f, shift):
        return pltpu.roll(f, shift % nx, 0)

    def roll_z(f, shift):
        return pltpu.roll(f, shift % nz, 1)

    def smooth_x(f):
        return (roll_x(f, 1) + roll_x(f, -1)) + 2.0 * f

    def smooth(f):
        f = smooth_x(f)
        return (roll_z(f, 1) + roll_z(f, -1)) + 2.0 * f

    def slopes(below, centre, above):
        return strain_parts(
            [roll_x(f, -1) - roll_x(f, 1) for f in centre],
            [a - b for a, b in zip(above, below)],
            [roll_z(f, -1) - roll_z(f, 1) for f in centre],
        )

    @pl.when(jnp.logical_or(bottom, top))
    def _():
        for k in range(count):
            x0, zb = (k // nz_parts) * width, k % nz_parts
            for i in range(planes):
                c, x = divmod(i, width)
                for j, row in enumerate(rows_of(k, i)):
                    vel[j, c, x0 + x : x0 + x + 1, zb * lanes : (zb + 1) * lanes] = row
        u = [[vel[j, c] for c in range(3)] for j in range(3)]
        v = [[smooth(f) for f in row] for row in u]
        strain = slopes(*u)
        size = strain_size(strain)
        mean_strain = slopes(*v)
        mean_size = 0.25 * strain_size(mean_strain)
        scaled = [0.0625 * f for f in v[1]]
        pairs = [v[1][i] * scaled[j] for i, j in ((0, 0), (1, 1), (2, 2), (0, 1), (0, 2), (1, 2))]
        leonard = [smooth(p) - q for p, q in zip(products(u[1]), pairs)]
        model = [smooth(size * s) - mean_size * f for s, f in zip(strain, mean_strain)]
        lm, mm = contracted(leonard, model)
        coefficient = coefficient_of(
            *(jnp.sum(f, axis=(0, 1), keepdims=True) for f in (lm, mm)), nx * nz
        )
        eddy = coefficient * size

        def put(at):
            for k in range(count):
                x0, zb = (k // nz_parts) * width, k % nz_parts
                for x in range(width):
                    out[count - 1 - k, x, at : at + 1, :] = eddy[x0 + x : x0 + x + 1, zb * lanes : (zb + 1) * lanes]

        pl.when(bottom)(lambda: put(0))
        pl.when(top)(lambda: put(rows - 1))


def contracted(leonard, model):
    lm = mm = None
    for i in range(6):
        square = model[i] * model[i] if i < 3 else (0.5 * model[i]) * model[i]
        product = leonard[i] * model[i]
        lm = product if lm is None else lm + product
        mm = square if mm is None else mm + square
    return lm, mm


def coefficient_of(plane_lm, plane_mm, cells):
    scale = 1.0 / (256.0 * cells)
    return jnp.maximum(plane_lm * scale / (plane_mm * scale + 1e-06), 0.0)


def germano_kernel(nz_parts, width, rows, rank, parity, recv, out, vel, filt, ends, strains, means, part):
    count, _, lanes = recv.shape
    planes = 3 * width
    _, top = outer_sides(rank, parity, count)
    nx = (count // nz_parts) * width
    nz = nz_parts * lanes
    blocks = range(nz_parts)
    lead = 8
    inner = slice(lead, lead + rows)
    for k in range(count):
        x0, zb = (k // nz_parts) * width, k % nz_parts
        for c in range(3):
            for x in range(width):
                i = c * width + x
                vel[c, x0 + x, zb, inner, :] = recv[k, i * rows : (i + 1) * rows, :]
                slots = planes * rows + i
                near = recv[k, slots : slots + 1, :]
                slots += aligned(planes)
                other = recv[k, slots : slots + 1, :]
                below = jnp.where(top, other, near)
                for side, (edge, at) in enumerate(((below, lead - 1), (other, lead + rows))):
                    vel[c, x0 + x, zb, at : at + 1, :] = edge
                    ends[c, x0 + x, zb, side : side + 1, :] = edge

    lower = slice(lead - 1, lead - 1 + rows)
    upper = slice(lead + 1, lead + 1 + rows)

    def smooth_x(read, x):
        return (read((x - 1) % nx) + read((x + 1) % nx)) + 2.0 * read(x)

    def keep_strain(field, x, kept, scale):
        left, right = (x - 1) % nx, (x + 1) % nx
        grad_z = [slope_z([field[c, x, zb, inner, :] for zb in blocks]) for c in range(3)]
        for zb in blocks:
            grad_x = [field[c, right, zb, inner, :] - field[c, left, zb, inner, :] for c in range(3)]
            grad_y = [field[c, x, zb, upper, :] - field[c, x, zb, lower, :] for c in range(3)]
            parts = strain_parts(grad_x, grad_y, [grad_z[c][zb] for c in range(3)])
            for i in range(6):
                kept[i, x, zb] = parts[i]
            kept[6, x, zb] = scale * strain_size(parts) if scale != 1.0 else strain_size(parts)

    for x in range(nx):
        keep_strain(vel, x, strains, 1.0)
        for c in range(3):
            for zb, f in enumerate(smooth_z([vel[c, x, zb, inner, :] for zb in blocks])):
                part[c, x, zb] = f
    for c in range(3):
        rims = [smooth_z([ends[c, x, zb] for zb in blocks]) for x in range(nx)]
        for x in range(nx):
            for zb in blocks:
                rim = smooth_x(lambda at: rims[at][zb], x)
                filt[c, x, zb, lead - 1 : lead, :] = rim[0:1, :]
                filt[c, x, zb, lead + rows : lead + rows + 1, :] = rim[1:2, :]
                filt[c, x, zb, inner, :] = smooth_x(lambda at: part[c, at, zb], x)
    def filter_z(read, kept):
        if not on_matrix_unit:
            for x in range(nx):
                for zb, f in enumerate(smooth_z([read(x, zb) for zb in blocks])):
                    part[kept, x, zb] = f
            return
        half = nx // 2
        for x0 in (0, half):
            planes_here = [
                jnp.concatenate([read(x, zb) for zb in blocks], axis=1) for x in range(x0, x0 + half)
            ]
            total = times_band(jnp.concatenate(planes_here, axis=0), band)
            for x in range(half):
                for zb in blocks:
                    part[kept, x0 + x, zb] = total[x * rows : (x + 1) * rows, zb * lanes : (zb + 1) * lanes]

    on_matrix_unit = nz <= 256 and rows * nx % 32 == 0 and rows % 8 == 0
    band = band_matrix(nz) if on_matrix_unit else None
    for i, (a, b) in enumerate(((0, 0), (1, 1), (2, 2), (0, 1), (0, 2), (1, 2))):
        filter_z(lambda x, zb: vel[a, x, zb, inner, :] * vel[b, x, zb, inner, :], 3 + i)
        filter_z(lambda x, zb: strains[6, x, zb] * strains[i, x, zb], 9 + i)
    for x in range(nx):
        keep_strain(filt, x, means, 0.25)

    sum_lm = sum_mm = None
    for x in range(nx):
        for zb in blocks:
            v = [filt[c, x, zb, inner, :] for c in range(3)]
            scaled = [0.0625 * f for f in v]
            size = means[6, x, zb]
            for i, (a, b) in enumerate(((0, 0), (1, 1), (2, 2), (0, 1), (0, 2), (1, 2))):
                leonard = smooth_x(lambda at: part[3 + i, at, zb], x) - v[a] * scaled[b]
                model = smooth_x(lambda at: part[9 + i, at, zb], x) - size * means[i, x, zb]
                square = model * model if i < 3 else (0.5 * model) * model
                sum_lm = leonard * model if sum_lm is None else sum_lm + leonard * model
                sum_mm = square if sum_mm is None else sum_mm + square

    coefficient = coefficient_of(
        *(jnp.sum(total, axis=1, keepdims=True) for total in (sum_lm, sum_mm)), nx * nz
    )
    for k in range(count):
        x0, zb = (k // nz_parts) * width, k % nz_parts
        for x in range(width):
            out[count - 1 - k, x] = coefficient * strains[6, x0 + x, zb]


def sweep_kernel(parity, back, velocity, tendency, eddy, reduced, factors, tree):
    count, width, rows, _ = back.shape
    length = count * rows // SEGMENTS

    def fill(rank, place):
        for x in range(width):
            eddy[x, place * rows : (place + 1) * rows, :] = back[count - 1 - rank, x]

    by_parity(parity, count, fill)

    def row(ref, index, j):
        return ref[(*index, pl.ds(j, SEGMENTS, stride=length), slice(None))]

    planes = range(width)
    last_row = length - 1
    visc = [[1.0 + row(eddy, (x,), j) for x in planes] for j in range(length)]
    links = [[750.0 * (v + w) for v, w in zip(visc[j], visc[j + 1])] for j in range(last_row)]

    over = [jnp.ones_like(v) for v in visc[0]]
    under = [jnp.ones_like(v) for v in visc[0]]
    inverses = []
    for j in range(last_row):
        inverses.append([u / (o + e * u) for o, u, e in zip(over, under, links[j])])
        steps = [o * (1.0 / e) for o, e in zip(over, links[j])]
        under, over = (
            [u + t for u, t in zip(under, steps)],
            [(o + u) + t for o, u, t in zip(over, under, steps)],
        )
    inverses.append([u / o for o, u in zip(over, under)])

    value = first = corner = left = None
    reach = [jnp.ones_like(v) for v in visc[0]]
    for j in range(length):
        inverse = inverses[j]
        before = value
        source = [[2.0 * row(velocity, (c, x), j) + row(tendency, (c, x), j) for x in planes] for c in range(3)]
        value = [[f * r for f, r in zip(source[c], inverse)] for c in range(3)]
        if j > 0:
            carry = [e * r for e, r in zip(links[j - 1], inverse)]
            value = [[v + k * w for v, k, w in zip(value[c], carry, before[c])] for c in range(3)]
        left = [m * r for m, r in zip(reach, inverse)]
        if j == 0:
            first, corner = value, left
        else:
            first = [[f + m * v for f, m, v in zip(first[c], reach, value[c])] for c in range(3)]
            corner = [a + m * v for a, m, v in zip(corner, reach, left)]
        ratio = inverse
        if j < last_row:
            ratio = [e * r for e, r in zip(links[j], inverse)]
            reach = [m * r for m, r in zip(reach, ratio)]
        for x in planes:
            for c in range(3):
                factors[x, j, c] = value[c][x]
            factors[x, j, 3] = left[x]
            factors[x, j, 4] = ratio[x]

    def other(fields, step):
        return [pltpu.roll(f, (SEGMENTS - step) % SEGMENTS, 0) if step else f for f in fields]

    last, across, end = value, left, inverse
    seams = [750.0 * (v + w) for v, w in zip(visc[last_row], other(visc[0], 1))]
    level, step = 0, 1
    while step < SEGMENTS:
        link = other(seams, step - 1)
        first_b = [other(f, step) for f in first]
        last_b = [other(f, step) for f in last]
        corner_b, end_b, across_b = other(corner, step), other(end, step), other(across, step)
        stiff = [e / (1.0 + e * (d + a)) for e, d, a in zip(link, end, corner_b)]
        flux = [[k * (g - f) for k, g, f in zip(stiff, last[c], first_b[c])] for c in range(3)]
        from_left = [k * b for k, b in zip(stiff, across)]
        from_right = [k * b for k, b in zip(stiff, across_b)]
        for x in planes:
            for c in range(3):
                tree[x, level, c] = flux[c][x]
            tree[x, level, 3] = from_left[x]
            tree[x, level, 4] = from_right[x]
        first = [[f - b * t for f, b, t in zip(first[c], across, flux[c])] for c in range(3)]
        last = [[g + b * t for g, b, t in zip(last_b[c], across_b, flux[c])] for c in range(3)]
        corner = [a - b * k for a, b, k in zip(corner, across, from_left)]
        end = [d - b * k for d, b, k in zip(end_b, across_b, from_right)]
        across = [k * b for k, b in zip(from_left, across_b)]
        level, step = level + 1, step * 2
    for x in planes:
        rows_out = [f[x][0:1, :] for f in (*first, *last, corner, across, end, visc[0])]
        rows_out.append(visc[last_row][x][SEGMENTS - 1 :, :])
        for i, v in enumerate(rows_out):
            reduced[i * width + x : i * width + x + 1, :] = v


def spread_kernel(factors, tree, velocity, eddy, particular, response, eddy_out, sent):
    write = pltpu.make_async_copy(eddy, eddy_out, sent)
    write.start()
    width, length = factors.shape[:2]
    levels = tree.shape[1]
    sublane = lax.broadcasted_iota(jnp.int32, (SEGMENTS, LANES), 0)
    one, zero = (jnp.full((SEGMENTS, LANES), v, jnp.float32) for v in (1.0, 0.0))
    sides = [(c, zero, zero) for c in range(3)] + [(None, one, zero), (None, zero, one)]
    lefts = [[side[1]] * width for side in sides]
    rights = [[side[2]] * width for side in sides]
    for level in range(levels - 1, -1, -1):
        step = 2**level
        second = lax.rem(sublane, 2 * step) == step
        for n, (c, _, _) in enumerate(sides):
            for x in range(width):
                left, right = lefts[n][x], rights[n][x]
                through = tree[x, level, 3] * left - tree[x, level, 4] * right
                if c is not None:
                    through = tree[x, level, c] + through
                lefts[n][x] = jnp.where(second, pltpu.roll(through, step, 0), left)
                rights[n][x] = jnp.where(second, pltpu.roll(right, step, 0), -through)
    values = rights
    for j in range(length - 1, -1, -1):
        rows = pl.ds(j, SEGMENTS, stride=length)
        for n, (c, _, _) in enumerate(sides):
            for x in range(width):
                value = factors[x, j, 3] * lefts[n][x] + factors[x, j, 4] * values[n][x]
                if c is not None:
                    value = factors[x, j, c] + value
                    particular[c, x, rows, :] = value - velocity[c, x, rows, :]
                else:
                    response[n - 3, x, rows, :] = value
                values[n][x] = value
    write.wait()


def sources_of(step, count):
    ring = [0, *range(1, count, 2), *range(count - 2 + count % 2, 0, -2)]
    return [ring[(ring.index(i) - step) % count] for i in range(count)]


def exchange_order(count):
    return range(count - 1, 0, -1)


def spread_kernel(factors, tree, velocity, eddy, particular, response, eddy_out, sent):
    write = pltpu.make_async_copy(eddy, eddy_out, sent)
    write.start()
    width, length = factors.shape[:2]
    levels = tree.shape[1]
    sublane = lax.broadcasted_iota(jnp.int32, (SEGMENTS, LANES), 0)
    one, zero = (jnp.full((SEGMENTS, LANES), v, jnp.float32) for v in (1.0, 0.0))
    sides = [(c, zero, zero) for c in range(3)] + [(None, one, zero), (None, zero, one)]
    lefts = [[side[1]] * width for side in sides]
    rights = [[side[2]] * width for side in sides]
    for level in range(levels - 1, -1, -1):
        step = 2**level
        second = lax.rem(sublane, 2 * step) == step
        for n, (c, _, _) in enumerate(sides):
            for x in range(width):
                left, right = lefts[n][x], rights[n][x]
                through = tree[x, level, 3] * left - tree[x, level, 4] * right
                if c is not None:
                    through = tree[x, level, c] + through
                lefts[n][x] = jnp.where(second, pltpu.roll(through, step, 0), left)
                rights[n][x] = jnp.where(second, pltpu.roll(right, step, 0), -through)
    values = rights
    for j in range(length - 1, -1, -1):
        rows = pl.ds(j, SEGMENTS, stride=length)
        for n, (c, _, _) in enumerate(sides):
            for x in range(width):
                value = factors[x, j, 3] * lefts[n][x] + factors[x, j, 4] * values[n][x]
                if c is not None:
                    value = factors[x, j, c] + value
                    particular[c, x, rows, :] = value - velocity[c, x, rows, :]
                else:
                    response[n - 3, x, rows, :] = value
                values[n][x] = value
    write.wait()


def partner(i, step, count):
    if count & (count - 1) == 0:
        return i ^ step
    return (i - step + count) % count


def finish_kernel(devices, position, particular, response, *rest):
    reduced, (result, gathered, fluxes, out, sent) = rest[:devices], rest[devices:]
    width = particular.shape[1]
    here = position[0]
    for step, ref in zip([0, *exchange_order(devices)], reduced):
        source = sum(jnp.where(here == i, s, 0) for i, s in enumerate(sources_of(step, devices)))
        gathered[source] = ref[...]

    def part(device, i):
        return gathered[device, i * width : (i + 1) * width, :]

    pivots, sources = [], []
    for i in range(devices + 1):
        visc = [part(i - 1, 10)] if i > 0 else []
        total = [part(i - 1, 8)] if i > 0 else []
        source = [part(i - 1, 3 + c) for c in range(3)] if i > 0 else [0.0] * 3
        if i < devices:
            visc.append(part(i, 9))
            total.append(part(i, 6))
            source = [s - part(i, c) for c, s in enumerate(source)]
        pivots.append(sum(total) + 1.0 / (750.0 * sum(visc)))
        sources.append(source)
    across = [part(i, 7) for i in range(devices)]
    minors = [jnp.ones_like(pivots[0]), pivots[0]]
    for i in range(1, devices + 1):
        minors.append(pivots[i] * minors[i] - (across[i - 1] * across[i - 1]) * minors[i - 1])
    inverses = [minors[i] / minors[i + 1] for i in range(devices + 1)]
    ratios = [b * r for b, r in zip(across, inverses)]
    for i in range(1, devices + 1):
        sources[i] = [s + ratios[i - 1] * t for s, t in zip(sources[i], sources[i - 1])]
    for i in range(devices, -1, -1):
        flux_here = [inverses[i] * s for s in sources[i]]
        flux = flux_here if i == devices else [f + ratios[i] * g for f, g in zip(flux_here, flux)]
        for c in range(3):
            fluxes[i, c * width : (c + 1) * width, :] = flux[c]

    writes = []
    for c in range(3):
        for x in range(width):
            r = c * width + x
            left, right = fluxes[here, r : r + 1, :], fluxes[here + 1, r : r + 1, :]
            out[c, x] = particular[c, x] + (response[0, x] * left - response[1, x] * right)
            writes.append(pltpu.make_async_copy(out.at[c, x], result.at[c, x], sent.at[r]))
            writes[-1].start()
    for write in writes:
        write.wait()


def in_vmem(count):
    return [pl.BlockSpec(memory_space=pltpu.VMEM)] * count


def in_hbm(count):
    return [pl.BlockSpec(memory_space=pltpu.HBM)] * count


def in_smem(count):
    return [pl.BlockSpec(memory_space=pltpu.SMEM)] * count


def params():
    return pltpu.CompilerParams(vmem_limit_bytes=VMEM_BYTES)


def body(velocity, tendency):
    _, width, cells, lanes = velocity.shape
    nz_parts = lax.axis_size("gz")
    count = lax.axis_size("gx") * nz_parts
    walls = lax.axis_size("gy")
    rows = cells // count
    nx = lax.axis_size("gx") * width
    padded = 16 + aligned(rows)
    f32 = jnp.float32

    planes = 3 * width
    depth = aligned(planes * rows + 2 * aligned(planes))
    position = lax.axis_index("gy").astype(jnp.int32).reshape(1)
    parity = lax.rem(position, 2)
    chunks = pl.pallas_call(
        functools.partial(pack_kernel, rows),
        out_shape=jax.ShapeDtypeStruct((count, depth, lanes), f32),
        in_specs=in_smem(1) + in_vmem(1),
        out_specs=pl.BlockSpec(memory_space=pltpu.VMEM),
        compiler_params=params(),
        name="pack",
    )(parity, velocity)
    recv = lax.all_to_all(chunks, ("gx", "gz"), split_axis=0, concat_axis=0, tiled=True)
    slot = lax.slice_in_dim(recv, planes * rows, planes * rows + aligned(planes), axis=1)
    swapped = lax.ppermute(slot, ("gy", "gx", "gz"), swap_pairs(walls, count))
    rank = lax.axis_index(("gx", "gz")).astype(jnp.int32).reshape(1)
    chunk_shape = jax.ShapeDtypeStruct((count, width, rows, lanes), f32)
    cells_here = nx * nz_parts * rows * lanes
    provisional = pl.pallas_call(
        functools.partial(germano_kernel, nz_parts, width, rows),
        out_shape=chunk_shape,
        in_specs=in_smem(2) + in_vmem(1),
        out_specs=pl.BlockSpec(memory_space=pltpu.VMEM),
        scratch_shapes=[
            pltpu.VMEM((3, nx, nz_parts, padded, lanes), f32),
            pltpu.VMEM((3, nx, nz_parts, padded, lanes), f32),
            pltpu.VMEM((3, nx, nz_parts, 8, lanes), f32),
            pltpu.VMEM((7, nx, nz_parts, rows, lanes), f32),
            pltpu.VMEM((7, nx, nz_parts, rows, lanes), f32),
            pltpu.VMEM((15, nx, nz_parts, rows, lanes), f32),
        ],
        compiler_params=params(),
        cost_estimate=pl.CostEstimate(
            flops=300 * cells_here, bytes_accessed=16 * cells_here, transcendentals=2 * cells_here
        ),
        name="germano",
    )(rank, parity, recv)
    eddy_chunks = pl.pallas_call(
        functools.partial(edge_kernel, nz_parts, width, rows, walls),
        out_shape=chunk_shape,
        in_specs=in_smem(2) + in_vmem(3),
        out_specs=pl.BlockSpec(memory_space=pltpu.VMEM),
        scratch_shapes=[pltpu.VMEM((3, 3, nx, nz_parts * lanes), f32)],
        input_output_aliases={4: 0},
        compiler_params=params(),
        name="edge",
    )(rank, position, recv, swapped, provisional)
    back = lax.all_to_all(
        eddy_chunks,
        ("gx", "gz"),
        split_axis=0,
        concat_axis=0,
        tiled=True,
        axis_index_groups=[list(range(count - 1, -1, -1))],
    )

    length = cells // SEGMENTS
    levels = SEGMENTS.bit_length() - 1
    packed = aligned(11 * width)
    eddy_here, reduced, factors, tree = pl.pallas_call(
        sweep_kernel,
        out_shape=(
            jax.ShapeDtypeStruct((width, cells, lanes), f32),
            jax.ShapeDtypeStruct((packed, lanes), f32),
            jax.ShapeDtypeStruct((width, length, 5, SEGMENTS, lanes), f32),
            jax.ShapeDtypeStruct((width, levels, 5, SEGMENTS, lanes), f32),
        ),
        in_specs=in_smem(1) + in_vmem(3),
        out_specs=tuple(in_vmem(4)),
        compiler_params=params(),
        name="sweep",
    )(parity, back, velocity, tendency)

    others = [
        lax.ppermute(reduced, "gy", [(s, i) for i, s in enumerate(sources_of(step, walls))])
        for step in exchange_order(walls)
    ]
    particular, response, eddy = pl.pallas_call(
        spread_kernel,
        out_shape=(
            jax.ShapeDtypeStruct(velocity.shape, f32),
            jax.ShapeDtypeStruct((2, *velocity.shape[1:]), f32),
            jax.ShapeDtypeStruct(eddy_here.shape, f32),
        ),
        in_specs=in_vmem(4),
        out_specs=tuple(in_vmem(2) + in_hbm(1)),
        scratch_shapes=[pltpu.SemaphoreType.DMA],
        compiler_params=params(),
        cost_estimate=pl.CostEstimate(
            flops=20 * velocity.size, bytes_accessed=16 * velocity.size, transcendentals=0
        ),
        name="spread",
    )(factors, tree, velocity, eddy_here)
    new_velocity = pl.pallas_call(
        functools.partial(finish_kernel, walls),
        out_shape=jax.ShapeDtypeStruct(velocity.shape, f32),
        in_specs=in_smem(1) + in_vmem(2 + walls),
        out_specs=in_hbm(1)[0],
        scratch_shapes=[
            pltpu.VMEM((walls, packed, lanes), f32),
            pltpu.VMEM((walls + 1, aligned(3 * width), lanes), f32),
            pltpu.VMEM(velocity.shape, f32),
            pltpu.SemaphoreType.DMA((planes,)),
        ],
        compiler_params=params(),
        name="finish",
    )(position, particular, response, reduced, *others)
    return (new_velocity, eddy)


def solution(mesh):
    return jax.shard_map(
        body,
        mesh=mesh,
        in_specs=(P(None, "gx", "gy", "gz"), P(None, "gx", "gy", "gz")),
        out_specs=(P(None, "gx", "gy", "gz"), P("gx", "gy", "gz")),
        check_vma=False,
    )
```

```python
import functools

import jax
import jax.numpy as jnp
from jax import lax
from jax.experimental import pallas as pl
from jax.experimental.pallas import tpu as pltpu
from jax.sharding import PartitionSpec as P

LANES = 128
SEGMENTS = 8
VMEM_BYTES = 24 * 2**20


def strain_parts(grad_x, grad_y, grad_z):
    return (
        grad_x[0],
        grad_y[1],
        grad_z[2],
        grad_y[0] + grad_x[1],
        grad_z[0] + grad_x[2],
        grad_z[1] + grad_y[2],
    )


def strain_size(parts):
    diagonal = parts[0] * parts[0] + parts[1] * parts[1] + parts[2] * parts[2]
    mixed = parts[3] * parts[3] + parts[4] * parts[4] + parts[5] * parts[5]
    return jnp.sqrt(0.5 * diagonal + 0.25 * mixed)


def beside(blocks):
    count = len(blocks)
    lanes = blocks[0].shape[1]
    down = [pltpu.roll(f, 1, 1) for f in blocks]
    up = [pltpu.roll(f, lanes - 1, 1) for f in blocks]
    if count > 1:
        lane = lax.broadcasted_iota(jnp.int32, blocks[0].shape, 1)
        first, last = lane == 0, lane == lanes - 1
        down, up = (
            [jnp.where(first, down[i - 1], down[i]) for i in range(count)],
            [jnp.where(last, up[(i + 1) % count], up[i]) for i in range(count)],
        )
    return down, up


def slope_z(blocks):
    down, up = beside(blocks)
    return [u - d for u, d in zip(up, down)]


def smooth_z(blocks):
    down, up = beside(blocks)
    return [(u + d) + 2.0 * f for f, u, d in zip(blocks, up, down)]


def band_matrix(n):
    shape = (n, n)
    apart = lax.broadcasted_iota(jnp.int32, shape, 0) - lax.broadcasted_iota(jnp.int32, shape, 1)
    apart = jnp.abs(apart)
    near = jnp.logical_or(apart == 1, apart == n - 1)
    return jnp.where(apart == 0, 2.0, jnp.where(near, 1.0, 0.0)).astype(jnp.bfloat16)


def times_band(f, band):
    total = None
    for i in range(3):
        piece = f.astype(jnp.bfloat16)
        product = jnp.dot(piece, band, preferred_element_type=jnp.float32)
        total = product if total is None else total + product
        if i < 2:
            f = f - piece.astype(jnp.float32)
    return total


def products(v):
    return (v[0] * v[0], v[1] * v[1], v[2] * v[2], v[0] * v[1], v[0] * v[2], v[1] * v[2])


def outer_ranks(count):
    return (count - 3, count - 1)


def places(parity, count):
    outer = outer_ranks(count)
    inner = iter(range(1, count - 1))
    return [
        (0 if outer[parity] == rank else count - 1) if rank in outer else next(inner)
        for rank in range(count)
    ]


def swap_pairs(walls, count):
    odd, even = outer_ranks(count)
    partners = {}

    def join(a, b):
        partners[a], partners[b] = b, a

    for core in range(0, count, 2):
        here = (core, core + 1)
        if odd in here or even in here:
            first = 1 if odd in here else 0
            for wall in range(first, walls - 1, 2):
                for rank in here:
                    join((wall, rank), (wall + 1, rank))
        for wall in range(walls):
            if (wall, core) not in partners:
                join((wall, core), (wall, core + 1))
    return [
        (wall * count + rank, to[0] * count + to[1])
        for wall in range(walls)
        for rank in range(count)
        for to in [partners.get((wall, rank), (wall, rank))]
    ]


def out_order(count):
    odd, even = outer_ranks(count)
    late = (1, 0, even, odd, even - 1)
    return [r for r in range(count) if r not in late] + list(late)


def back_order(count):
    return [*range(count - 1, 0, -2), *range(count - 2, -1, -2)]


def slots_of(order):
    return [order.index(r) for r in range(len(order))]


def by_parity(parity, count, fill):
    outer = outer_ranks(count)
    for rank, place in enumerate(places(0, count)):
        if rank not in outer:
            fill(rank, place)
    for turn in range(2):

        @pl.when(parity[0] == turn)
        def _():
            for rank in outer:
                fill(rank, places(turn, count)[rank])


def aligned(n):
    return -(-n // 8) * 8


def pack_kernel(rows, parity, velocity, out):
    _, width, cells, _ = velocity.shape
    count, depth, lanes = out.shape
    planes = 3 * width
    slots = planes * rows

    slot_of = slots_of(out_order(count))

    def fill(rank, place):
        rank = slot_of[rank]
        first = place * rows
        beside = [first - 1, first + rows]
        if place == 0:
            beside = [first, first + rows]
        if place == count - 1:
            beside = [first + rows - 1, first - 1]
        for i in range(planes):
            c, x = divmod(i, width)
            out[rank, i * rows : (i + 1) * rows, :] = velocity[c, x, first : first + rows, :]
            for slot, row in enumerate(beside):
                at = slots + slot * aligned(planes) + i
                out[rank, at : at + 1, :] = velocity[c, x, row : row + 1, :]

    by_parity(parity, count, fill)
    blank = aligned(planes) - planes
    for rank in range(count):
        for slot in range(2):
            at = slots + slot * aligned(planes) + planes
            out[rank, at : at + blank, :] = jnp.zeros((blank, lanes), jnp.float32)
        at = slots + 2 * aligned(planes)
        if at < depth:
            out[rank, at:, :] = jnp.zeros((depth - at, lanes), jnp.float32)


def outer_sides(rank, parity, count):
    outer = outer_ranks(count)
    even = parity[0] == 0
    bottom = rank[0] == jnp.where(even, outer[0], outer[1])
    top = rank[0] == jnp.where(even, outer[1], outer[0])
    return bottom, top


def edge_kernel(nz_parts, width, rows, walls, rank, position, recv, swapped, given, out, vel):
    count, _, lanes = recv.shape
    planes = 3 * width
    nx = (count // nz_parts) * width
    nz = nz_parts * lanes
    bottom, top = outer_sides(rank, [lax.rem(position[0], 2)], count)
    came, to = slots_of(out_order(count)), slots_of(back_order(count))
    at_wall = jnp.logical_or(
        jnp.logical_and(bottom, position[0] == 0), jnp.logical_and(top, position[0] == walls - 1)
    )

    def rows_of(k, i):
        k = came[k]
        first = i * rows
        own = [recv[k, first + j : first + j + 1, :] for j in (0, 1, rows - 2, rows - 1)]
        far = jnp.where(at_wall, 0.0, swapped[k, i : i + 1, :])
        return (
            jnp.where(bottom, far, own[2]),
            jnp.where(bottom, own[0], own[3]),
            jnp.where(bottom, own[1], far),
        )

    def roll_x(f, shift):
        return pltpu.roll(f, shift % nx, 0)

    def roll_z(f, shift):
        return pltpu.roll(f, shift % nz, 1)

    def smooth_x(f):
        return (roll_x(f, 1) + roll_x(f, -1)) + 2.0 * f

    def smooth(f):
        f = smooth_x(f)
        return (roll_z(f, 1) + roll_z(f, -1)) + 2.0 * f

    def slopes(below, centre, above):
        return strain_parts(
            [roll_x(f, -1) - roll_x(f, 1) for f in centre],
            [a - b for a, b in zip(above, below)],
            [roll_z(f, -1) - roll_z(f, 1) for f in centre],
        )

    @pl.when(jnp.logical_or(bottom, top))
    def _():
        for k in range(count):
            x0, zb = (k // nz_parts) * width, k % nz_parts
            for i in range(planes):
                c, x = divmod(i, width)
                for j, row in enumerate(rows_of(k, i)):
                    vel[j, c, x0 + x : x0 + x + 1, zb * lanes : (zb + 1) * lanes] = row
        u = [[vel[j, c] for c in range(3)] for j in range(3)]
        v = [[smooth(f) for f in row] for row in u]
        strain = slopes(*u)
        size = strain_size(strain)
        mean_strain = slopes(*v)
        mean_size = 0.25 * strain_size(mean_strain)
        scaled = [0.0625 * f for f in v[1]]
        pairs = [v[1][i] * scaled[j] for i, j in ((0, 0), (1, 1), (2, 2), (0, 1), (0, 2), (1, 2))]
        leonard = [smooth(p) - q for p, q in zip(products(u[1]), pairs)]
        model = [smooth(size * s) - mean_size * f for s, f in zip(strain, mean_strain)]
        lm, mm = contracted(leonard, model)
        coefficient = coefficient_of(
            *(jnp.sum(f, axis=(0, 1), keepdims=True) for f in (lm, mm)), nx * nz
        )
        eddy = coefficient * size

        def put(at):
            for k in range(count):
                x0, zb = (k // nz_parts) * width, k % nz_parts
                for x in range(width):
                    out[to[k], x, at : at + 1, :] = eddy[x0 + x : x0 + x + 1, zb * lanes : (zb + 1) * lanes]

        pl.when(bottom)(lambda: put(0))
        pl.when(top)(lambda: put(rows - 1))


def contracted(leonard, model):
    lm = mm = None
    for i in range(6):
        square = model[i] * model[i] if i < 3 else (0.5 * model[i]) * model[i]
        product = leonard[i] * model[i]
        lm = product if lm is None else lm + product
        mm = square if mm is None else mm + square
    return lm, mm


def coefficient_of(plane_lm, plane_mm, cells):
    scale = 1.0 / (256.0 * cells)
    return jnp.maximum(plane_lm * scale / (plane_mm * scale + 1e-06), 0.0)


def germano_kernel(nz_parts, width, rows, rank, parity, recv, out, vel, filt, ends, strains, means, part):
    count, _, lanes = recv.shape
    planes = 3 * width
    _, top = outer_sides(rank, parity, count)
    came, to = slots_of(out_order(count)), slots_of(back_order(count))
    nx = (count // nz_parts) * width
    nz = nz_parts * lanes
    blocks = range(nz_parts)
    lead = 8
    inner = slice(lead, lead + rows)
    for k in range(count):
        x0, zb = (k // nz_parts) * width, k % nz_parts
        for c in range(3):
            for x in range(width):
                i = c * width + x
                vel[c, x0 + x, zb, inner, :] = recv[came[k], i * rows : (i + 1) * rows, :]
                slots = planes * rows + i
                near = recv[came[k], slots : slots + 1, :]
                slots += aligned(planes)
                other = recv[came[k], slots : slots + 1, :]
                below = jnp.where(top, other, near)
                for side, (edge, at) in enumerate(((below, lead - 1), (other, lead + rows))):
                    vel[c, x0 + x, zb, at : at + 1, :] = edge
                    ends[c, x0 + x, zb, side : side + 1, :] = edge

    lower = slice(lead - 1, lead - 1 + rows)
    upper = slice(lead + 1, lead + 1 + rows)

    def smooth_x(read, x):
        return (read((x - 1) % nx) + read((x + 1) % nx)) + 2.0 * read(x)

    def keep_strain(field, x, kept, scale):
        left, right = (x - 1) % nx, (x + 1) % nx
        grad_z = [slope_z([field[c, x, zb, inner, :] for zb in blocks]) for c in range(3)]
        for zb in blocks:
            grad_x = [field[c, right, zb, inner, :] - field[c, left, zb, inner, :] for c in range(3)]
            grad_y = [field[c, x, zb, upper, :] - field[c, x, zb, lower, :] for c in range(3)]
            parts = strain_parts(grad_x, grad_y, [grad_z[c][zb] for c in range(3)])
            for i in range(6):
                kept[i, x, zb] = parts[i]
            kept[6, x, zb] = scale * strain_size(parts) if scale != 1.0 else strain_size(parts)

    for x in range(nx):
        keep_strain(vel, x, strains, 1.0)
        for c in range(3):
            for zb, f in enumerate(smooth_z([vel[c, x, zb, inner, :] for zb in blocks])):
                part[c, x, zb] = f
    for c in range(3):
        rims = [smooth_z([ends[c, x, zb] for zb in blocks]) for x in range(nx)]
        for x in range(nx):
            for zb in blocks:
                rim = smooth_x(lambda at: rims[at][zb], x)
                filt[c, x, zb, lead - 1 : lead, :] = rim[0:1, :]
                filt[c, x, zb, lead + rows : lead + rows + 1, :] = rim[1:2, :]
                filt[c, x, zb, inner, :] = smooth_x(lambda at: part[c, at, zb], x)
    def filter_z(read, kept):
        if not on_matrix_unit:
            for x in range(nx):
                for zb, f in enumerate(smooth_z([read(x, zb) for zb in blocks])):
                    part[kept, x, zb] = f
            return
        half = nx // 2
        for x0 in (0, half):
            planes_here = [
                jnp.concatenate([read(x, zb) for zb in blocks], axis=1) for x in range(x0, x0 + half)
            ]
            total = times_band(jnp.concatenate(planes_here, axis=0), band)
            for x in range(half):
                for zb in blocks:
                    part[kept, x0 + x, zb] = total[x * rows : (x + 1) * rows, zb * lanes : (zb + 1) * lanes]

    on_matrix_unit = nz <= 256 and rows * nx % 32 == 0 and rows % 8 == 0
    band = band_matrix(nz) if on_matrix_unit else None
    for i, (a, b) in enumerate(((0, 0), (1, 1), (2, 2), (0, 1), (0, 2), (1, 2))):
        filter_z(lambda x, zb: vel[a, x, zb, inner, :] * vel[b, x, zb, inner, :], 3 + i)
        filter_z(lambda x, zb: strains[6, x, zb] * strains[i, x, zb], 9 + i)
    for x in range(nx):
        keep_strain(filt, x, means, 0.25)

    sum_lm = sum_mm = None
    for x in range(nx):
        for zb in blocks:
            v = [filt[c, x, zb, inner, :] for c in range(3)]
            scaled = [0.0625 * f for f in v]
            size = means[6, x, zb]
            for i, (a, b) in enumerate(((0, 0), (1, 1), (2, 2), (0, 1), (0, 2), (1, 2))):
                leonard = smooth_x(lambda at: part[3 + i, at, zb], x) - v[a] * scaled[b]
                model = smooth_x(lambda at: part[9 + i, at, zb], x) - size * means[i, x, zb]
                square = model * model if i < 3 else (0.5 * model) * model
                sum_lm = leonard * model if sum_lm is None else sum_lm + leonard * model
                sum_mm = square if sum_mm is None else sum_mm + square

    coefficient = coefficient_of(
        *(jnp.sum(total, axis=1, keepdims=True) for total in (sum_lm, sum_mm)), nx * nz
    )
    for k in range(count):
        x0, zb = (k // nz_parts) * width, k % nz_parts
        for x in range(width):
            out[to[k], x] = coefficient * strains[6, x0 + x, zb]


def sweep_kernel(parity, back, velocity, tendency, eddy, reduced, factors, tree):
    count, width, rows, _ = back.shape
    length = count * rows // SEGMENTS
    slots = slots_of(back_order(count))

    def fill(rank, place):
        for x in range(width):
            eddy[x, place * rows : (place + 1) * rows, :] = back[slots[rank], x]

    by_parity(parity, count, fill)

    def row(ref, index, j):
        return ref[(*index, pl.ds(j, SEGMENTS, stride=length), slice(None))]

    planes = range(width)
    last_row = length - 1
    visc = [[1.0 + row(eddy, (x,), j) for x in planes] for j in range(length)]
    links = [[750.0 * (v + w) for v, w in zip(visc[j], visc[j + 1])] for j in range(last_row)]

    over = [jnp.ones_like(v) for v in visc[0]]
    under = [jnp.ones_like(v) for v in visc[0]]
    inverses = []
    for j in range(last_row):
        inverses.append([u / (o + e * u) for o, u, e in zip(over, under, links[j])])
        steps = [o * (1.0 / e) for o, e in zip(over, links[j])]
        under, over = (
            [u + t for u, t in zip(under, steps)],
            [(o + u) + t for o, u, t in zip(over, under, steps)],
        )
    inverses.append([u / o for o, u in zip(over, under)])

    value = first = corner = left = None
    reach = [jnp.ones_like(v) for v in visc[0]]
    for j in range(length):
        inverse = inverses[j]
        before = value
        source = [[2.0 * row(velocity, (c, x), j) + row(tendency, (c, x), j) for x in planes] for c in range(3)]
        value = [[f * r for f, r in zip(source[c], inverse)] for c in range(3)]
        if j > 0:
            carry = [e * r for e, r in zip(links[j - 1], inverse)]
            value = [[v + k * w for v, k, w in zip(value[c], carry, before[c])] for c in range(3)]
        left = [m * r for m, r in zip(reach, inverse)]
        if j == 0:
            first, corner = value, left
        else:
            first = [[f + m * v for f, m, v in zip(first[c], reach, value[c])] for c in range(3)]
            corner = [a + m * v for a, m, v in zip(corner, reach, left)]
        ratio = inverse
        if j < last_row:
            ratio = [e * r for e, r in zip(links[j], inverse)]
            reach = [m * r for m, r in zip(reach, ratio)]
        for x in planes:
            for c in range(3):
                factors[x, j, c] = value[c][x]
            factors[x, j, 3] = left[x]
            factors[x, j, 4] = ratio[x]

    def other(fields, step):
        return [pltpu.roll(f, (SEGMENTS - step) % SEGMENTS, 0) if step else f for f in fields]

    last, across, end = value, left, inverse
    seams = [750.0 * (v + w) for v, w in zip(visc[last_row], other(visc[0], 1))]
    level, step = 0, 1
    while step < SEGMENTS:
        link = other(seams, step - 1)
        first_b = [other(f, step) for f in first]
        last_b = [other(f, step) for f in last]
        corner_b, end_b, across_b = other(corner, step), other(end, step), other(across, step)
        stiff = [e / (1.0 + e * (d + a)) for e, d, a in zip(link, end, corner_b)]
        flux = [[k * (g - f) for k, g, f in zip(stiff, last[c], first_b[c])] for c in range(3)]
        from_left = [k * b for k, b in zip(stiff, across)]
        from_right = [k * b for k, b in zip(stiff, across_b)]
        for x in planes:
            for c in range(3):
                tree[x, level, c] = flux[c][x]
            tree[x, level, 3] = from_left[x]
            tree[x, level, 4] = from_right[x]
        first = [[f - b * t for f, b, t in zip(first[c], across, flux[c])] for c in range(3)]
        last = [[g + b * t for g, b, t in zip(last_b[c], across_b, flux[c])] for c in range(3)]
        corner = [a - b * k for a, b, k in zip(corner, across, from_left)]
        end = [d - b * k for d, b, k in zip(end_b, across_b, from_right)]
        across = [k * b for k, b in zip(from_left, across_b)]
        level, step = level + 1, step * 2
    for x in planes:
        rows_out = [f[x][0:1, :] for f in (*first, *last, corner, across, end, visc[0])]
        rows_out.append(visc[last_row][x][SEGMENTS - 1 :, :])
        for i, v in enumerate(rows_out):
            reduced[i * width + x : i * width + x + 1, :] = v


def spread_kernel(factors, tree, velocity, eddy, particular, response, eddy_out, sent):
    write = pltpu.make_async_copy(eddy, eddy_out, sent)
    write.start()
    width, length = factors.shape[:2]
    levels = tree.shape[1]
    sublane = lax.broadcasted_iota(jnp.int32, (SEGMENTS, LANES), 0)
    one, zero = (jnp.full((SEGMENTS, LANES), v, jnp.float32) for v in (1.0, 0.0))
    sides = [(c, zero, zero) for c in range(3)] + [(None, one, zero), (None, zero, one)]
    lefts = [[side[1]] * width for side in sides]
    rights = [[side[2]] * width for side in sides]
    for level in range(levels - 1, -1, -1):
        step = 2**level
        second = lax.rem(sublane, 2 * step) == step
        for n, (c, _, _) in enumerate(sides):
            for x in range(width):
                left, right = lefts[n][x], rights[n][x]
                through = tree[x, level, 3] * left - tree[x, level, 4] * right
                if c is not None:
                    through = tree[x, level, c] + through
                lefts[n][x] = jnp.where(second, pltpu.roll(through, step, 0), left)
                rights[n][x] = jnp.where(second, pltpu.roll(right, step, 0), -through)
    values = rights
    for j in range(length - 1, -1, -1):
        rows = pl.ds(j, SEGMENTS, stride=length)
        for n, (c, _, _) in enumerate(sides):
            for x in range(width):
                value = factors[x, j, 3] * lefts[n][x] + factors[x, j, 4] * values[n][x]
                if c is not None:
                    value = factors[x, j, c] + value
                    particular[c, x, rows, :] = value - velocity[c, x, rows, :]
                else:
                    response[n - 3, x, rows, :] = value
                values[n][x] = value
    write.wait()


def sources_of(step, count):
    ring = [0, *range(1, count, 2), *range(count - 2 + count % 2, 0, -2)]
    return [ring[(ring.index(i) - step) % count] for i in range(count)]


def exchange_order(count):
    return range(count - 1, 0, -1)


def spread_kernel(factors, tree, velocity, eddy, particular, response, eddy_out, sent):
    write = pltpu.make_async_copy(eddy, eddy_out, sent)
    write.start()
    width, length = factors.shape[:2]
    levels = tree.shape[1]
    sublane = lax.broadcasted_iota(jnp.int32, (SEGMENTS, LANES), 0)
    one, zero = (jnp.full((SEGMENTS, LANES), v, jnp.float32) for v in (1.0, 0.0))
    sides = [(c, zero, zero) for c in range(3)] + [(None, one, zero), (None, zero, one)]
    lefts = [[side[1]] * width for side in sides]
    rights = [[side[2]] * width for side in sides]
    for level in range(levels - 1, -1, -1):
        step = 2**level
        second = lax.rem(sublane, 2 * step) == step
        for n, (c, _, _) in enumerate(sides):
            for x in range(width):
                left, right = lefts[n][x], rights[n][x]
                through = tree[x, level, 3] * left - tree[x, level, 4] * right
                if c is not None:
                    through = tree[x, level, c] + through
                lefts[n][x] = jnp.where(second, pltpu.roll(through, step, 0), left)
                rights[n][x] = jnp.where(second, pltpu.roll(right, step, 0), -through)
    values = rights
    for j in range(length - 1, -1, -1):
        rows = pl.ds(j, SEGMENTS, stride=length)
        for n, (c, _, _) in enumerate(sides):
            for x in range(width):
                value = factors[x, j, 3] * lefts[n][x] + factors[x, j, 4] * values[n][x]
                if c is not None:
                    value = factors[x, j, c] + value
                    particular[c, x, rows, :] = value - velocity[c, x, rows, :]
                else:
                    response[n - 3, x, rows, :] = value
                values[n][x] = value
    write.wait()


def partner(i, step, count):
    if count & (count - 1) == 0:
        return i ^ step
    return (i - step + count) % count


def finish_kernel(devices, position, particular, response, *rest):
    reduced, (result, gathered, fluxes, out, sent) = rest[:devices], rest[devices:]
    width = particular.shape[1]
    here = position[0]
    for step, ref in zip([0, *exchange_order(devices)], reduced):
        source = sum(jnp.where(here == i, s, 0) for i, s in enumerate(sources_of(step, devices)))
        gathered[source] = ref[...]

    def part(device, i):
        return gathered[device, i * width : (i + 1) * width, :]

    pivots, sources = [], []
    for i in range(devices + 1):
        visc = [part(i - 1, 10)] if i > 0 else []
        total = [part(i - 1, 8)] if i > 0 else []
        source = [part(i - 1, 3 + c) for c in range(3)] if i > 0 else [0.0] * 3
        if i < devices:
            visc.append(part(i, 9))
            total.append(part(i, 6))
            source = [s - part(i, c) for c, s in enumerate(source)]
        pivots.append(sum(total) + 1.0 / (750.0 * sum(visc)))
        sources.append(source)
    across = [part(i, 7) for i in range(devices)]
    minors = [jnp.ones_like(pivots[0]), pivots[0]]
    for i in range(1, devices + 1):
        minors.append(pivots[i] * minors[i] - (across[i - 1] * across[i - 1]) * minors[i - 1])
    inverses = [minors[i] / minors[i + 1] for i in range(devices + 1)]
    ratios = [b * r for b, r in zip(across, inverses)]
    for i in range(1, devices + 1):
        sources[i] = [s + ratios[i - 1] * t for s, t in zip(sources[i], sources[i - 1])]
    for i in range(devices, -1, -1):
        flux_here = [inverses[i] * s for s in sources[i]]
        flux = flux_here if i == devices else [f + ratios[i] * g for f, g in zip(flux_here, flux)]
        for c in range(3):
            fluxes[i, c * width : (c + 1) * width, :] = flux[c]

    writes = []
    for c in range(3):
        for x in range(width):
            r = c * width + x
            left, right = fluxes[here, r : r + 1, :], fluxes[here + 1, r : r + 1, :]
            out[c, x] = particular[c, x] + (response[0, x] * left - response[1, x] * right)
            writes.append(pltpu.make_async_copy(out.at[c, x], result.at[c, x], sent.at[r]))
            writes[-1].start()
    for write in writes:
        write.wait()


def in_vmem(count):
    return [pl.BlockSpec(memory_space=pltpu.VMEM)] * count


def in_hbm(count):
    return [pl.BlockSpec(memory_space=pltpu.HBM)] * count


def in_smem(count):
    return [pl.BlockSpec(memory_space=pltpu.SMEM)] * count


def params():
    return pltpu.CompilerParams(vmem_limit_bytes=VMEM_BYTES)


def swap_chunks(chunks, order):
    return lax.all_to_all(
        chunks, ("gx", "gz"), split_axis=0, concat_axis=0, tiled=True, axis_index_groups=[order]
    )


def body(velocity, tendency):
    _, width, cells, lanes = velocity.shape
    nz_parts = lax.axis_size("gz")
    count = lax.axis_size("gx") * nz_parts
    walls = lax.axis_size("gy")
    rows = cells // count
    nx = lax.axis_size("gx") * width
    padded = 16 + aligned(rows)
    f32 = jnp.float32

    planes = 3 * width
    depth = aligned(planes * rows + 2 * aligned(planes))
    position = lax.axis_index("gy").astype(jnp.int32).reshape(1)
    parity = lax.rem(position, 2)
    chunks = pl.pallas_call(
        functools.partial(pack_kernel, rows),
        out_shape=jax.ShapeDtypeStruct((count, depth, lanes), f32),
        in_specs=in_smem(1) + in_vmem(1),
        out_specs=pl.BlockSpec(memory_space=pltpu.VMEM),
        compiler_params=params(),
        name="pack",
    )(parity, velocity)
    recv = swap_chunks(chunks, out_order(count))
    slot = lax.slice_in_dim(recv, planes * rows, planes * rows + aligned(planes), axis=1)
    swapped = lax.ppermute(slot, ("gy", "gx", "gz"), swap_pairs(walls, count))
    rank = lax.axis_index(("gx", "gz")).astype(jnp.int32).reshape(1)
    chunk_shape = jax.ShapeDtypeStruct((count, width, rows, lanes), f32)
    cells_here = nx * nz_parts * rows * lanes
    provisional = pl.pallas_call(
        functools.partial(germano_kernel, nz_parts, width, rows),
        out_shape=chunk_shape,
        in_specs=in_smem(2) + in_vmem(1),
        out_specs=pl.BlockSpec(memory_space=pltpu.VMEM),
        scratch_shapes=[
            pltpu.VMEM((3, nx, nz_parts, padded, lanes), f32),
            pltpu.VMEM((3, nx, nz_parts, padded, lanes), f32),
            pltpu.VMEM((3, nx, nz_parts, 8, lanes), f32),
            pltpu.VMEM((7, nx, nz_parts, rows, lanes), f32),
            pltpu.VMEM((7, nx, nz_parts, rows, lanes), f32),
            pltpu.VMEM((15, nx, nz_parts, rows, lanes), f32),
        ],
        compiler_params=params(),
        cost_estimate=pl.CostEstimate(
            flops=300 * cells_here, bytes_accessed=16 * cells_here, transcendentals=2 * cells_here
        ),
        name="germano",
    )(rank, parity, recv)
    eddy_chunks = pl.pallas_call(
        functools.partial(edge_kernel, nz_parts, width, rows, walls),
        out_shape=chunk_shape,
        in_specs=in_smem(2) + in_vmem(3),
        out_specs=pl.BlockSpec(memory_space=pltpu.VMEM),
        scratch_shapes=[pltpu.VMEM((3, 3, nx, nz_parts * lanes), f32)],
        input_output_aliases={4: 0},
        compiler_params=params(),
        name="edge",
    )(rank, position, recv, swapped, provisional)
    back = swap_chunks(eddy_chunks, back_order(count))

    length = cells // SEGMENTS
    levels = SEGMENTS.bit_length() - 1
    packed = aligned(11 * width)
    eddy_here, reduced, factors, tree = pl.pallas_call(
        sweep_kernel,
        out_shape=(
            jax.ShapeDtypeStruct((width, cells, lanes), f32),
            jax.ShapeDtypeStruct((packed, lanes), f32),
            jax.ShapeDtypeStruct((width, length, 5, SEGMENTS, lanes), f32),
            jax.ShapeDtypeStruct((width, levels, 5, SEGMENTS, lanes), f32),
        ),
        in_specs=in_smem(1) + in_vmem(3),
        out_specs=tuple(in_vmem(4)),
        compiler_params=params(),
        name="sweep",
    )(parity, back, velocity, tendency)

    others = [
        lax.ppermute(reduced, "gy", [(s, i) for i, s in enumerate(sources_of(step, walls))])
        for step in exchange_order(walls)
    ]
    particular, response, eddy = pl.pallas_call(
        spread_kernel,
        out_shape=(
            jax.ShapeDtypeStruct(velocity.shape, f32),
            jax.ShapeDtypeStruct((2, *velocity.shape[1:]), f32),
            jax.ShapeDtypeStruct(eddy_here.shape, f32),
        ),
        in_specs=in_vmem(4),
        out_specs=tuple(in_vmem(2) + in_hbm(1)),
        scratch_shapes=[pltpu.SemaphoreType.DMA],
        compiler_params=params(),
        cost_estimate=pl.CostEstimate(
            flops=20 * velocity.size, bytes_accessed=16 * velocity.size, transcendentals=0
        ),
        name="spread",
    )(factors, tree, velocity, eddy_here)
    new_velocity = pl.pallas_call(
        functools.partial(finish_kernel, walls),
        out_shape=jax.ShapeDtypeStruct(velocity.shape, f32),
        in_specs=in_smem(1) + in_vmem(2 + walls),
        out_specs=in_hbm(1)[0],
        scratch_shapes=[
            pltpu.VMEM((walls, packed, lanes), f32),
            pltpu.VMEM((walls + 1, aligned(3 * width), lanes), f32),
            pltpu.VMEM(velocity.shape, f32),
            pltpu.SemaphoreType.DMA((planes,)),
        ],
        compiler_params=params(),
        name="finish",
    )(position, particular, response, reduced, *others)
    return (new_velocity, eddy)


def solution(mesh):
    return jax.shard_map(
        body,
        mesh=mesh,
        in_specs=(P(None, "gx", "gy", "gz"), P(None, "gx", "gy", "gz")),
        out_specs=(P(None, "gx", "gy", "gz"), P("gx", "gy", "gz")),
        check_vma=False,
    )
```

```python
import functools

import jax
import jax.numpy as jnp
from jax import lax
from jax.experimental import pallas as pl
from jax.experimental.pallas import tpu as pltpu
from jax.sharding import PartitionSpec as P

LANES = 128
SEGMENTS = 8
VMEM_BYTES = 24 * 2**20


def strain_parts(grad_x, grad_y, grad_z):
    return (
        grad_x[0],
        grad_y[1],
        grad_z[2],
        grad_y[0] + grad_x[1],
        grad_z[0] + grad_x[2],
        grad_z[1] + grad_y[2],
    )


def strain_size(parts):
    diagonal = parts[0] * parts[0] + parts[1] * parts[1] + parts[2] * parts[2]
    mixed = parts[3] * parts[3] + parts[4] * parts[4] + parts[5] * parts[5]
    return jnp.sqrt(0.5 * diagonal + 0.25 * mixed)


def beside(blocks):
    count = len(blocks)
    lanes = blocks[0].shape[1]
    down = [pltpu.roll(f, 1, 1) for f in blocks]
    up = [pltpu.roll(f, lanes - 1, 1) for f in blocks]
    if count > 1:
        lane = lax.broadcasted_iota(jnp.int32, blocks[0].shape, 1)
        first, last = lane == 0, lane == lanes - 1
        down, up = (
            [jnp.where(first, down[i - 1], down[i]) for i in range(count)],
            [jnp.where(last, up[(i + 1) % count], up[i]) for i in range(count)],
        )
    return down, up


def slope_z(blocks):
    down, up = beside(blocks)
    return [u - d for u, d in zip(up, down)]


def smooth_z(blocks):
    down, up = beside(blocks)
    return [(u + d) + 2.0 * f for f, u, d in zip(blocks, up, down)]


def band_matrix(n):
    shape = (n, n)
    apart = lax.broadcasted_iota(jnp.int32, shape, 0) - lax.broadcasted_iota(jnp.int32, shape, 1)
    apart = jnp.abs(apart)
    near = jnp.logical_or(apart == 1, apart == n - 1)
    return jnp.where(apart == 0, 2.0, jnp.where(near, 1.0, 0.0)).astype(jnp.bfloat16)


def times_band(f, band):
    total = None
    for i in range(3):
        piece = f.astype(jnp.bfloat16)
        product = jnp.dot(piece, band, preferred_element_type=jnp.float32)
        total = product if total is None else total + product
        if i < 2:
            f = f - piece.astype(jnp.float32)
    return total


def products(v):
    return (v[0] * v[0], v[1] * v[1], v[2] * v[2], v[0] * v[1], v[0] * v[2], v[1] * v[2])


def outer_ranks(count):
    return (count - 3, count - 1)


def places(parity, count):
    outer = outer_ranks(count)
    inner = iter(range(1, count - 1))
    return [
        (0 if outer[parity] == rank else count - 1) if rank in outer else next(inner)
        for rank in range(count)
    ]


def swap_pairs(walls, count):
    odd, even = outer_ranks(count)
    partners = {}

    def join(a, b):
        partners[a], partners[b] = b, a

    for core in range(0, count, 2):
        here = (core, core + 1)
        if odd in here or even in here:
            first = 1 if odd in here else 0
            for wall in range(first, walls - 1, 2):
                for rank in here:
                    join((wall, rank), (wall + 1, rank))
        for wall in range(walls):
            if (wall, core) not in partners:
                join((wall, core), (wall, core + 1))
    return [
        (wall * count + rank, to[0] * count + to[1])
        for wall in range(walls)
        for rank in range(count)
        for to in [partners.get((wall, rank), (wall, rank))]
    ]


def ring_of(count):
    return [0, *range(1, count, 2), *range(count - 2 + count % 2, 0, -2)]


def by_core(chips):
    return [2 * chip + 1 for chip in chips] + [2 * chip for chip in chips]


def out_order(count):
    return by_core(ring_of(count // 2))


def back_order(count):
    first, *others = ring_of(count // 2)
    return by_core([*others, first])


def slots_of(order):
    return [order.index(r) for r in range(len(order))]


def by_parity(parity, count, fill):
    outer = outer_ranks(count)
    for rank, place in enumerate(places(0, count)):
        if rank not in outer:
            fill(rank, place)
    for turn in range(2):

        @pl.when(parity[0] == turn)
        def _():
            for rank in outer:
                fill(rank, places(turn, count)[rank])


def aligned(n):
    return -(-n // 8) * 8


def pack_kernel(rows, parity, velocity, out):
    _, width, cells, _ = velocity.shape
    count, depth, lanes = out.shape
    planes = 3 * width
    slots = planes * rows

    slot_of = slots_of(out_order(count))

    def fill(rank, place):
        rank = slot_of[rank]
        first = place * rows
        beside = [first - 1, first + rows]
        if place == 0:
            beside = [first, first + rows]
        if place == count - 1:
            beside = [first + rows - 1, first - 1]
        for i in range(planes):
            c, x = divmod(i, width)
            out[rank, i * rows : (i + 1) * rows, :] = velocity[c, x, first : first + rows, :]
            for slot, row in enumerate(beside):
                at = slots + slot * aligned(planes) + i
                out[rank, at : at + 1, :] = velocity[c, x, row : row + 1, :]

    by_parity(parity, count, fill)
    blank = aligned(planes) - planes
    for rank in range(count):
        for slot in range(2):
            at = slots + slot * aligned(planes) + planes
            out[rank, at : at + blank, :] = jnp.zeros((blank, lanes), jnp.float32)
        at = slots + 2 * aligned(planes)
        if at < depth:
            out[rank, at:, :] = jnp.zeros((depth - at, lanes), jnp.float32)


def outer_sides(rank, parity, count):
    outer = outer_ranks(count)
    even = parity[0] == 0
    bottom = rank[0] == jnp.where(even, outer[0], outer[1])
    top = rank[0] == jnp.where(even, outer[1], outer[0])
    return bottom, top


def edge_kernel(nz_parts, width, rows, walls, rank, position, recv, swapped, given, out, vel):
    count, _, lanes = recv.shape
    planes = 3 * width
    nx = (count // nz_parts) * width
    nz = nz_parts * lanes
    bottom, top = outer_sides(rank, [lax.rem(position[0], 2)], count)
    came, to = slots_of(out_order(count)), slots_of(back_order(count))
    at_wall = jnp.logical_or(
        jnp.logical_and(bottom, position[0] == 0), jnp.logical_and(top, position[0] == walls - 1)
    )

    def rows_of(k, i):
        k = came[k]
        first = i * rows
        own = [recv[k, first + j : first + j + 1, :] for j in (0, 1, rows - 2, rows - 1)]
        far = jnp.where(at_wall, 0.0, swapped[k, i : i + 1, :])
        return (
            jnp.where(bottom, far, own[2]),
            jnp.where(bottom, own[0], own[3]),
            jnp.where(bottom, own[1], far),
        )

    def roll_x(f, shift):
        return pltpu.roll(f, shift % nx, 0)

    def roll_z(f, shift):
        return pltpu.roll(f, shift % nz, 1)

    def smooth_x(f):
        return (roll_x(f, 1) + roll_x(f, -1)) + 2.0 * f

    def smooth(f):
        f = smooth_x(f)
        return (roll_z(f, 1) + roll_z(f, -1)) + 2.0 * f

    def slopes(below, centre, above):
        return strain_parts(
            [roll_x(f, -1) - roll_x(f, 1) for f in centre],
            [a - b for a, b in zip(above, below)],
            [roll_z(f, -1) - roll_z(f, 1) for f in centre],
        )

    @pl.when(jnp.logical_or(bottom, top))
    def _():
        for k in range(count):
            x0, zb = (k // nz_parts) * width, k % nz_parts
            for i in range(planes):
                c, x = divmod(i, width)
                for j, row in enumerate(rows_of(k, i)):
                    vel[j, c, x0 + x : x0 + x + 1, zb * lanes : (zb + 1) * lanes] = row
        u = [[vel[j, c] for c in range(3)] for j in range(3)]
        v = [[smooth(f) for f in row] for row in u]
        strain = slopes(*u)
        size = strain_size(strain)
        mean_strain = slopes(*v)
        mean_size = 0.25 * strain_size(mean_strain)
        scaled = [0.0625 * f for f in v[1]]
        pairs = [v[1][i] * scaled[j] for i, j in ((0, 0), (1, 1), (2, 2), (0, 1), (0, 2), (1, 2))]
        leonard = [smooth(p) - q for p, q in zip(products(u[1]), pairs)]
        model = [smooth(size * s) - mean_size * f for s, f in zip(strain, mean_strain)]
        lm, mm = contracted(leonard, model)
        coefficient = coefficient_of(
            *(jnp.sum(f, axis=(0, 1), keepdims=True) for f in (lm, mm)), nx * nz
        )
        eddy = coefficient * size

        def put(at):
            for k in range(count):
                x0, zb = (k // nz_parts) * width, k % nz_parts
                for x in range(width):
                    out[to[k], x, at : at + 1, :] = eddy[x0 + x : x0 + x + 1, zb * lanes : (zb + 1) * lanes]

        pl.when(bottom)(lambda: put(0))
        pl.when(top)(lambda: put(rows - 1))


def contracted(leonard, model):
    lm = mm = None
    for i in range(6):
        square = model[i] * model[i] if i < 3 else (0.5 * model[i]) * model[i]
        product = leonard[i] * model[i]
        lm = product if lm is None else lm + product
        mm = square if mm is None else mm + square
    return lm, mm


def coefficient_of(plane_lm, plane_mm, cells):
    scale = 1.0 / (256.0 * cells)
    return jnp.maximum(plane_lm * scale / (plane_mm * scale + 1e-06), 0.0)


def germano_kernel(nz_parts, width, rows, rank, parity, recv, out, vel, filt, ends, strains, means, part):
    count, _, lanes = recv.shape
    planes = 3 * width
    _, top = outer_sides(rank, parity, count)
    came, to = slots_of(out_order(count)), slots_of(back_order(count))
    nx = (count // nz_parts) * width
    nz = nz_parts * lanes
    blocks = range(nz_parts)
    lead = 8
    inner = slice(lead, lead + rows)
    for k in range(count):
        x0, zb = (k // nz_parts) * width, k % nz_parts
        for c in range(3):
            for x in range(width):
                i = c * width + x
                vel[c, x0 + x, zb, inner, :] = recv[came[k], i * rows : (i + 1) * rows, :]
                slots = planes * rows + i
                near = recv[came[k], slots : slots + 1, :]
                slots += aligned(planes)
                other = recv[came[k], slots : slots + 1, :]
                below = jnp.where(top, other, near)
                for side, (edge, at) in enumerate(((below, lead - 1), (other, lead + rows))):
                    vel[c, x0 + x, zb, at : at + 1, :] = edge
                    ends[c, x0 + x, zb, side : side + 1, :] = edge

    lower = slice(lead - 1, lead - 1 + rows)
    upper = slice(lead + 1, lead + 1 + rows)

    def smooth_x(read, x):
        return (read((x - 1) % nx) + read((x + 1) % nx)) + 2.0 * read(x)

    def keep_strain(field, x, kept, scale):
        left, right = (x - 1) % nx, (x + 1) % nx
        grad_z = [slope_z([field[c, x, zb, inner, :] for zb in blocks]) for c in range(3)]
        for zb in blocks:
            grad_x = [field[c, right, zb, inner, :] - field[c, left, zb, inner, :] for c in range(3)]
            grad_y = [field[c, x, zb, upper, :] - field[c, x, zb, lower, :] for c in range(3)]
            parts = strain_parts(grad_x, grad_y, [grad_z[c][zb] for c in range(3)])
            for i in range(6):
                kept[i, x, zb] = parts[i]
            kept[6, x, zb] = scale * strain_size(parts) if scale != 1.0 else strain_size(parts)

    for x in range(nx):
        keep_strain(vel, x, strains, 1.0)
        for c in range(3):
            for zb, f in enumerate(smooth_z([vel[c, x, zb, inner, :] for zb in blocks])):
                part[c, x, zb] = f
    for c in range(3):
        rims = [smooth_z([ends[c, x, zb] for zb in blocks]) for x in range(nx)]
        for x in range(nx):
            for zb in blocks:
                rim = smooth_x(lambda at: rims[at][zb], x)
                filt[c, x, zb, lead - 1 : lead, :] = rim[0:1, :]
                filt[c, x, zb, lead + rows : lead + rows + 1, :] = rim[1:2, :]
                filt[c, x, zb, inner, :] = smooth_x(lambda at: part[c, at, zb], x)
    def filter_z(read, kept):
        if not on_matrix_unit:
            for x in range(nx):
                for zb, f in enumerate(smooth_z([read(x, zb) for zb in blocks])):
                    part[kept, x, zb] = f
            return
        half = nx // 2
        for x0 in (0, half):
            planes_here = [
                jnp.concatenate([read(x, zb) for zb in blocks], axis=1) for x in range(x0, x0 + half)
            ]
            total = times_band(jnp.concatenate(planes_here, axis=0), band)
            for x in range(half):
                for zb in blocks:
                    part[kept, x0 + x, zb] = total[x * rows : (x + 1) * rows, zb * lanes : (zb + 1) * lanes]

    on_matrix_unit = nz <= 256 and rows * nx % 32 == 0 and rows % 8 == 0
    band = band_matrix(nz) if on_matrix_unit else None
    for i, (a, b) in enumerate(((0, 0), (1, 1), (2, 2), (0, 1), (0, 2), (1, 2))):
        filter_z(lambda x, zb: vel[a, x, zb, inner, :] * vel[b, x, zb, inner, :], 3 + i)
        filter_z(lambda x, zb: strains[6, x, zb] * strains[i, x, zb], 9 + i)
    for x in range(nx):
        keep_strain(filt, x, means, 0.25)

    sum_lm = sum_mm = None
    for x in range(nx):
        for zb in blocks:
            v = [filt[c, x, zb, inner, :] for c in range(3)]
            scaled = [0.0625 * f for f in v]
            size = means[6, x, zb]
            for i, (a, b) in enumerate(((0, 0), (1, 1), (2, 2), (0, 1), (0, 2), (1, 2))):
                leonard = smooth_x(lambda at: part[3 + i, at, zb], x) - v[a] * scaled[b]
                model = smooth_x(lambda at: part[9 + i, at, zb], x) - size * means[i, x, zb]
                square = model * model if i < 3 else (0.5 * model) * model
                sum_lm = leonard * model if sum_lm is None else sum_lm + leonard * model
                sum_mm = square if sum_mm is None else sum_mm + square

    coefficient = coefficient_of(
        *(jnp.sum(total, axis=1, keepdims=True) for total in (sum_lm, sum_mm)), nx * nz
    )
    for k in range(count):
        x0, zb = (k // nz_parts) * width, k % nz_parts
        for x in range(width):
            out[to[k], x] = coefficient * strains[6, x0 + x, zb]


def sweep_kernel(parity, back, velocity, tendency, eddy, reduced, factors, tree):
    count, width, rows, _ = back.shape
    length = count * rows // SEGMENTS
    slots = slots_of(back_order(count))

    def fill(rank, place):
        for x in range(width):
            eddy[x, place * rows : (place + 1) * rows, :] = back[slots[rank], x]

    by_parity(parity, count, fill)

    def row(ref, index, j):
        return ref[(*index, pl.ds(j, SEGMENTS, stride=length), slice(None))]

    planes = range(width)
    last_row = length - 1
    visc = [[1.0 + row(eddy, (x,), j) for x in planes] for j in range(length)]
    links = [[750.0 * (v + w) for v, w in zip(visc[j], visc[j + 1])] for j in range(last_row)]

    over = [jnp.ones_like(v) for v in visc[0]]
    under = [jnp.ones_like(v) for v in visc[0]]
    inverses = []
    for j in range(last_row):
        inverses.append([u / (o + e * u) for o, u, e in zip(over, under, links[j])])
        steps = [o * (1.0 / e) for o, e in zip(over, links[j])]
        under, over = (
            [u + t for u, t in zip(under, steps)],
            [(o + u) + t for o, u, t in zip(over, under, steps)],
        )
    inverses.append([u / o for o, u in zip(over, under)])

    value = first = corner = left = None
    reach = [jnp.ones_like(v) for v in visc[0]]
    for j in range(length):
        inverse = inverses[j]
        before = value
        source = [[2.0 * row(velocity, (c, x), j) + row(tendency, (c, x), j) for x in planes] for c in range(3)]
        value = [[f * r for f, r in zip(source[c], inverse)] for c in range(3)]
        if j > 0:
            carry = [e * r for e, r in zip(links[j - 1], inverse)]
            value = [[v + k * w for v, k, w in zip(value[c], carry, before[c])] for c in range(3)]
        left = [m * r for m, r in zip(reach, inverse)]
        if j == 0:
            first, corner = value, left
        else:
            first = [[f + m * v for f, m, v in zip(first[c], reach, value[c])] for c in range(3)]
            corner = [a + m * v for a, m, v in zip(corner, reach, left)]
        ratio = inverse
        if j < last_row:
            ratio = [e * r for e, r in zip(links[j], inverse)]
            reach = [m * r for m, r in zip(reach, ratio)]
        for x in planes:
            for c in range(3):
                factors[x, j, c] = value[c][x]
            factors[x, j, 3] = left[x]
            factors[x, j, 4] = ratio[x]

    def other(fields, step):
        return [pltpu.roll(f, (SEGMENTS - step) % SEGMENTS, 0) if step else f for f in fields]

    last, across, end = value, left, inverse
    seams = [750.0 * (v + w) for v, w in zip(visc[last_row], other(visc[0], 1))]
    level, step = 0, 1
    while step < SEGMENTS:
        link = other(seams, step - 1)
        first_b = [other(f, step) for f in first]
        last_b = [other(f, step) for f in last]
        corner_b, end_b, across_b = other(corner, step), other(end, step), other(across, step)
        stiff = [e / (1.0 + e * (d + a)) for e, d, a in zip(link, end, corner_b)]
        flux = [[k * (g - f) for k, g, f in zip(stiff, last[c], first_b[c])] for c in range(3)]
        from_left = [k * b for k, b in zip(stiff, across)]
        from_right = [k * b for k, b in zip(stiff, across_b)]
        for x in planes:
            for c in range(3):
                tree[x, level, c] = flux[c][x]
            tree[x, level, 3] = from_left[x]
            tree[x, level, 4] = from_right[x]
        first = [[f - b * t for f, b, t in zip(first[c], across, flux[c])] for c in range(3)]
        last = [[g + b * t for g, b, t in zip(last_b[c], across_b, flux[c])] for c in range(3)]
        corner = [a - b * k for a, b, k in zip(corner, across, from_left)]
        end = [d - b * k for d, b, k in zip(end_b, across_b, from_right)]
        across = [k * b for k, b in zip(from_left, across_b)]
        level, step = level + 1, step * 2
    for x in planes:
        rows_out = [f[x][0:1, :] for f in (*first, *last, corner, across, end, visc[0])]
        rows_out.append(visc[last_row][x][SEGMENTS - 1 :, :])
        for i, v in enumerate(rows_out):
            reduced[i * width + x : i * width + x + 1, :] = v


def spread_kernel(factors, tree, velocity, eddy, particular, response, eddy_out, sent):
    write = pltpu.make_async_copy(eddy, eddy_out, sent)
    write.start()
    width, length = factors.shape[:2]
    levels = tree.shape[1]
    sublane = lax.broadcasted_iota(jnp.int32, (SEGMENTS, LANES), 0)
    one, zero = (jnp.full((SEGMENTS, LANES), v, jnp.float32) for v in (1.0, 0.0))
    sides = [(c, zero, zero) for c in range(3)] + [(None, one, zero), (None, zero, one)]
    lefts = [[side[1]] * width for side in sides]
    rights = [[side[2]] * width for side in sides]
    for level in range(levels - 1, -1, -1):
        step = 2**level
        second = lax.rem(sublane, 2 * step) == step
        for n, (c, _, _) in enumerate(sides):
            for x in range(width):
                left, right = lefts[n][x], rights[n][x]
                through = tree[x, level, 3] * left - tree[x, level, 4] * right
                if c is not None:
                    through = tree[x, level, c] + through
                lefts[n][x] = jnp.where(second, pltpu.roll(through, step, 0), left)
                rights[n][x] = jnp.where(second, pltpu.roll(right, step, 0), -through)
    values = rights
    for j in range(length - 1, -1, -1):
        rows = pl.ds(j, SEGMENTS, stride=length)
        for n, (c, _, _) in enumerate(sides):
            for x in range(width):
                value = factors[x, j, 3] * lefts[n][x] + factors[x, j, 4] * values[n][x]
                if c is not None:
                    value = factors[x, j, c] + value
                    particular[c, x, rows, :] = value - velocity[c, x, rows, :]
                else:
                    response[n - 3, x, rows, :] = value
                values[n][x] = value
    write.wait()


def sources_of(step, count):
    ring = ring_of(count)
    return [ring[(ring.index(i) - step) % count] for i in range(count)]


def exchange_order(count):
    return range(count - 1, 0, -1)


def spread_kernel(factors, tree, velocity, eddy, particular, response, eddy_out, sent):
    write = pltpu.make_async_copy(eddy, eddy_out, sent)
    write.start()
    width, length = factors.shape[:2]
    levels = tree.shape[1]
    sublane = lax.broadcasted_iota(jnp.int32, (SEGMENTS, LANES), 0)
    one, zero = (jnp.full((SEGMENTS, LANES), v, jnp.float32) for v in (1.0, 0.0))
    sides = [(c, zero, zero) for c in range(3)] + [(None, one, zero), (None, zero, one)]
    lefts = [[side[1]] * width for side in sides]
    rights = [[side[2]] * width for side in sides]
    for level in range(levels - 1, -1, -1):
        step = 2**level
        second = lax.rem(sublane, 2 * step) == step
        for n, (c, _, _) in enumerate(sides):
            for x in range(width):
                left, right = lefts[n][x], rights[n][x]
                through = tree[x, level, 3] * left - tree[x, level, 4] * right
                if c is not None:
                    through = tree[x, level, c] + through
                lefts[n][x] = jnp.where(second, pltpu.roll(through, step, 0), left)
                rights[n][x] = jnp.where(second, pltpu.roll(right, step, 0), -through)
    values = rights
    for j in range(length - 1, -1, -1):
        rows = pl.ds(j, SEGMENTS, stride=length)
        for n, (c, _, _) in enumerate(sides):
            for x in range(width):
                value = factors[x, j, 3] * lefts[n][x] + factors[x, j, 4] * values[n][x]
                if c is not None:
                    value = factors[x, j, c] + value
                    particular[c, x, rows, :] = value - velocity[c, x, rows, :]
                else:
                    response[n - 3, x, rows, :] = value
                values[n][x] = value
    write.wait()


def partner(i, step, count):
    if count & (count - 1) == 0:
        return i ^ step
    return (i - step + count) % count


def finish_kernel(devices, position, particular, response, *rest):
    reduced, (result, gathered, fluxes, out, sent) = rest[:devices], rest[devices:]
    width = particular.shape[1]
    here = position[0]
    for step, ref in zip([0, *exchange_order(devices)], reduced):
        source = sum(jnp.where(here == i, s, 0) for i, s in enumerate(sources_of(step, devices)))
        gathered[source] = ref[...]

    def part(device, i):
        return gathered[device, i * width : (i + 1) * width, :]

    pivots, sources = [], []
    for i in range(devices + 1):
        visc = [part(i - 1, 10)] if i > 0 else []
        total = [part(i - 1, 8)] if i > 0 else []
        source = [part(i - 1, 3 + c) for c in range(3)] if i > 0 else [0.0] * 3
        if i < devices:
            visc.append(part(i, 9))
            total.append(part(i, 6))
            source = [s - part(i, c) for c, s in enumerate(source)]
        pivots.append(sum(total) + 1.0 / (750.0 * sum(visc)))
        sources.append(source)
    across = [part(i, 7) for i in range(devices)]
    minors = [jnp.ones_like(pivots[0]), pivots[0]]
    for i in range(1, devices + 1):
        minors.append(pivots[i] * minors[i] - (across[i - 1] * across[i - 1]) * minors[i - 1])
    inverses = [minors[i] / minors[i + 1] for i in range(devices + 1)]
    ratios = [b * r for b, r in zip(across, inverses)]
    for i in range(1, devices + 1):
        sources[i] = [s + ratios[i - 1] * t for s, t in zip(sources[i], sources[i - 1])]
    for i in range(devices, -1, -1):
        flux_here = [inverses[i] * s for s in sources[i]]
        flux = flux_here if i == devices else [f + ratios[i] * g for f, g in zip(flux_here, flux)]
        for c in range(3):
            fluxes[i, c * width : (c + 1) * width, :] = flux[c]

    writes = []
    for c in range(3):
        for x in range(width):
            r = c * width + x
            left, right = fluxes[here, r : r + 1, :], fluxes[here + 1, r : r + 1, :]
            out[c, x] = particular[c, x] + (response[0, x] * left - response[1, x] * right)
            writes.append(pltpu.make_async_copy(out.at[c, x], result.at[c, x], sent.at[r]))
            writes[-1].start()
    for write in writes:
        write.wait()


def in_vmem(count):
    return [pl.BlockSpec(memory_space=pltpu.VMEM)] * count


def in_hbm(count):
    return [pl.BlockSpec(memory_space=pltpu.HBM)] * count


def in_smem(count):
    return [pl.BlockSpec(memory_space=pltpu.SMEM)] * count


def params():
    return pltpu.CompilerParams(vmem_limit_bytes=VMEM_BYTES)


def swap_chunks(chunks, order):
    return lax.all_to_all(
        chunks, ("gx", "gz"), split_axis=0, concat_axis=0, tiled=True, axis_index_groups=[order]
    )


def body(velocity, tendency):
    _, width, cells, lanes = velocity.shape
    nz_parts = lax.axis_size("gz")
    count = lax.axis_size("gx") * nz_parts
    walls = lax.axis_size("gy")
    rows = cells // count
    nx = lax.axis_size("gx") * width
    padded = 16 + aligned(rows)
    f32 = jnp.float32

    planes = 3 * width
    depth = aligned(planes * rows + 2 * aligned(planes))
    position = lax.axis_index("gy").astype(jnp.int32).reshape(1)
    parity = lax.rem(position, 2)
    chunks = pl.pallas_call(
        functools.partial(pack_kernel, rows),
        out_shape=jax.ShapeDtypeStruct((count, depth, lanes), f32),
        in_specs=in_smem(1) + in_vmem(1),
        out_specs=pl.BlockSpec(memory_space=pltpu.VMEM),
        compiler_params=params(),
        name="pack",
    )(parity, velocity)
    recv = swap_chunks(chunks, out_order(count))
    slot = lax.slice_in_dim(recv, planes * rows, planes * rows + aligned(planes), axis=1)
    swapped = lax.ppermute(slot, ("gy", "gx", "gz"), swap_pairs(walls, count))
    rank = lax.axis_index(("gx", "gz")).astype(jnp.int32).reshape(1)
    chunk_shape = jax.ShapeDtypeStruct((count, width, rows, lanes), f32)
    cells_here = nx * nz_parts * rows * lanes
    provisional = pl.pallas_call(
        functools.partial(germano_kernel, nz_parts, width, rows),
        out_shape=chunk_shape,
        in_specs=in_smem(2) + in_vmem(1),
        out_specs=pl.BlockSpec(memory_space=pltpu.VMEM),
        scratch_shapes=[
            pltpu.VMEM((3, nx, nz_parts, padded, lanes), f32),
            pltpu.VMEM((3, nx, nz_parts, padded, lanes), f32),
            pltpu.VMEM((3, nx, nz_parts, 8, lanes), f32),
            pltpu.VMEM((7, nx, nz_parts, rows, lanes), f32),
            pltpu.VMEM((7, nx, nz_parts, rows, lanes), f32),
            pltpu.VMEM((15, nx, nz_parts, rows, lanes), f32),
        ],
        compiler_params=params(),
        cost_estimate=pl.CostEstimate(
            flops=300 * cells_here, bytes_accessed=16 * cells_here, transcendentals=2 * cells_here
        ),
        name="germano",
    )(rank, parity, recv)
    eddy_chunks = pl.pallas_call(
        functools.partial(edge_kernel, nz_parts, width, rows, walls),
        out_shape=chunk_shape,
        in_specs=in_smem(2) + in_vmem(3),
        out_specs=pl.BlockSpec(memory_space=pltpu.VMEM),
        scratch_shapes=[pltpu.VMEM((3, 3, nx, nz_parts * lanes), f32)],
        input_output_aliases={4: 0},
        compiler_params=params(),
        name="edge",
    )(rank, position, recv, swapped, provisional)
    back = swap_chunks(eddy_chunks, back_order(count))

    length = cells // SEGMENTS
    levels = SEGMENTS.bit_length() - 1
    packed = aligned(11 * width)
    eddy_here, reduced, factors, tree = pl.pallas_call(
        sweep_kernel,
        out_shape=(
            jax.ShapeDtypeStruct((width, cells, lanes), f32),
            jax.ShapeDtypeStruct((packed, lanes), f32),
            jax.ShapeDtypeStruct((width, length, 5, SEGMENTS, lanes), f32),
            jax.ShapeDtypeStruct((width, levels, 5, SEGMENTS, lanes), f32),
        ),
        in_specs=in_smem(1) + in_vmem(3),
        out_specs=tuple(in_vmem(4)),
        compiler_params=params(),
        name="sweep",
    )(parity, back, velocity, tendency)

    others = [
        lax.ppermute(reduced, "gy", [(s, i) for i, s in enumerate(sources_of(step, walls))])
        for step in exchange_order(walls)
    ]
    particular, response, eddy = pl.pallas_call(
        spread_kernel,
        out_shape=(
            jax.ShapeDtypeStruct(velocity.shape, f32),
            jax.ShapeDtypeStruct((2, *velocity.shape[1:]), f32),
            jax.ShapeDtypeStruct(eddy_here.shape, f32),
        ),
        in_specs=in_vmem(4),
        out_specs=tuple(in_vmem(2) + in_hbm(1)),
        scratch_shapes=[pltpu.SemaphoreType.DMA],
        compiler_params=params(),
        cost_estimate=pl.CostEstimate(
            flops=20 * velocity.size, bytes_accessed=16 * velocity.size, transcendentals=0
        ),
        name="spread",
    )(factors, tree, velocity, eddy_here)
    new_velocity = pl.pallas_call(
        functools.partial(finish_kernel, walls),
        out_shape=jax.ShapeDtypeStruct(velocity.shape, f32),
        in_specs=in_smem(1) + in_vmem(2 + walls),
        out_specs=in_hbm(1)[0],
        scratch_shapes=[
            pltpu.VMEM((walls, packed, lanes), f32),
            pltpu.VMEM((walls + 1, aligned(3 * width), lanes), f32),
            pltpu.VMEM(velocity.shape, f32),
            pltpu.SemaphoreType.DMA((planes,)),
        ],
        compiler_params=params(),
        name="finish",
    )(position, particular, response, reduced, *others)
    return (new_velocity, eddy)


def solution(mesh):
    return jax.shard_map(
        body,
        mesh=mesh,
        in_specs=(P(None, "gx", "gy", "gz"), P(None, "gx", "gy", "gz")),
        out_specs=(P(None, "gx", "gy", "gz"), P("gx", "gy", "gz")),
        check_vma=False,
    )
```

```python
import functools

import jax
import jax.numpy as jnp
from jax import lax
from jax.experimental import pallas as pl
from jax.experimental.pallas import tpu as pltpu
from jax.sharding import PartitionSpec as P

LANES = 128
SEGMENTS = 8
VMEM_BYTES = 24 * 2**20


def strain_parts(grad_x, grad_y, grad_z):
    return (
        grad_x[0],
        grad_y[1],
        grad_z[2],
        grad_y[0] + grad_x[1],
        grad_z[0] + grad_x[2],
        grad_z[1] + grad_y[2],
    )


def strain_size(parts):
    diagonal = parts[0] * parts[0] + parts[1] * parts[1] + parts[2] * parts[2]
    mixed = parts[3] * parts[3] + parts[4] * parts[4] + parts[5] * parts[5]
    return jnp.sqrt(0.5 * diagonal + 0.25 * mixed)


def beside(blocks):
    count = len(blocks)
    lanes = blocks[0].shape[1]
    down = [pltpu.roll(f, 1, 1) for f in blocks]
    up = [pltpu.roll(f, lanes - 1, 1) for f in blocks]
    if count > 1:
        lane = lax.broadcasted_iota(jnp.int32, blocks[0].shape, 1)
        first, last = lane == 0, lane == lanes - 1
        down, up = (
            [jnp.where(first, down[i - 1], down[i]) for i in range(count)],
            [jnp.where(last, up[(i + 1) % count], up[i]) for i in range(count)],
        )
    return down, up


def slope_z(blocks):
    down, up = beside(blocks)
    return [u - d for u, d in zip(up, down)]


def smooth_z(blocks):
    down, up = beside(blocks)
    return [(u + d) + 2.0 * f for f, u, d in zip(blocks, up, down)]


def band_matrix(n):
    shape = (n, n)
    apart = lax.broadcasted_iota(jnp.int32, shape, 0) - lax.broadcasted_iota(jnp.int32, shape, 1)
    apart = jnp.abs(apart)
    near = jnp.logical_or(apart == 1, apart == n - 1)
    return jnp.where(apart == 0, 2.0, jnp.where(near, 1.0, 0.0)).astype(jnp.bfloat16)


def times_band(f, band):
    total = None
    for i in range(3):
        piece = f.astype(jnp.bfloat16)
        product = jnp.dot(piece, band, preferred_element_type=jnp.float32)
        total = product if total is None else total + product
        if i < 2:
            f = f - piece.astype(jnp.float32)
    return total


def products(v):
    return (v[0] * v[0], v[1] * v[1], v[2] * v[2], v[0] * v[1], v[0] * v[2], v[1] * v[2])


def outer_ranks(count):
    return (count - 3, count - 1)


def places(parity, count):
    outer = outer_ranks(count)
    inner = iter(range(1, count - 1))
    return [
        (0 if outer[parity] == rank else count - 1) if rank in outer else next(inner)
        for rank in range(count)
    ]


def swap_pairs(walls, count):
    odd, even = outer_ranks(count)
    partners = {}

    def join(a, b):
        partners[a], partners[b] = b, a

    for core in range(0, count, 2):
        here = (core, core + 1)
        if odd in here or even in here:
            first = 1 if odd in here else 0
            for wall in range(first, walls - 1, 2):
                for rank in here:
                    join((wall, rank), (wall + 1, rank))
        for wall in range(walls):
            if (wall, core) not in partners:
                join((wall, core), (wall, core + 1))
    return [
        (wall * count + rank, to[0] * count + to[1])
        for wall in range(walls)
        for rank in range(count)
        for to in [partners.get((wall, rank), (wall, rank))]
    ]


def ring_of(count):
    return [0, *range(1, count, 2), *range(count - 2 + count % 2, 0, -2)]


def by_core(chips):
    return [2 * chip + 1 for chip in chips] + [2 * chip for chip in chips]


def out_order(count):
    return by_core(ring_of(count // 2))


def back_order(count):
    return by_core(range(count // 2 - 1, -1, -1))


def slots_of(order):
    return [order.index(r) for r in range(len(order))]


def by_parity(parity, count, fill):
    outer = outer_ranks(count)
    for rank, place in enumerate(places(0, count)):
        if rank not in outer:
            fill(rank, place)
    for turn in range(2):

        @pl.when(parity[0] == turn)
        def _():
            for rank in outer:
                fill(rank, places(turn, count)[rank])


def aligned(n):
    return -(-n // 8) * 8


def pack_kernel(rows, parity, velocity, out):
    _, width, cells, _ = velocity.shape
    count, depth, lanes = out.shape
    planes = 3 * width
    slots = planes * rows

    slot_of = slots_of(out_order(count))

    def fill(rank, place):
        rank = slot_of[rank]
        first = place * rows
        beside = [first - 1, first + rows]
        if place == 0:
            beside = [first, first + rows]
        if place == count - 1:
            beside = [first + rows - 1, first - 1]
        for i in range(planes):
            c, x = divmod(i, width)
            out[rank, i * rows : (i + 1) * rows, :] = velocity[c, x, first : first + rows, :]
            for slot, row in enumerate(beside):
                at = slots + slot * aligned(planes) + i
                out[rank, at : at + 1, :] = velocity[c, x, row : row + 1, :]

    by_parity(parity, count, fill)
    blank = aligned(planes) - planes
    for rank in range(count):
        for slot in range(2):
            at = slots + slot * aligned(planes) + planes
            out[rank, at : at + blank, :] = jnp.zeros((blank, lanes), jnp.float32)
        at = slots + 2 * aligned(planes)
        if at < depth:
            out[rank, at:, :] = jnp.zeros((depth - at, lanes), jnp.float32)


def outer_sides(rank, parity, count):
    outer = outer_ranks(count)
    even = parity[0] == 0
    bottom = rank[0] == jnp.where(even, outer[0], outer[1])
    top = rank[0] == jnp.where(even, outer[1], outer[0])
    return bottom, top


def edge_kernel(nz_parts, width, rows, walls, rank, position, recv, swapped, given, out, vel):
    count, _, lanes = recv.shape
    planes = 3 * width
    nx = (count // nz_parts) * width
    nz = nz_parts * lanes
    bottom, top = outer_sides(rank, [lax.rem(position[0], 2)], count)
    came, to = slots_of(out_order(count)), slots_of(back_order(count))
    at_wall = jnp.logical_or(
        jnp.logical_and(bottom, position[0] == 0), jnp.logical_and(top, position[0] == walls - 1)
    )

    def rows_of(k, i):
        k = came[k]
        first = i * rows
        own = [recv[k, first + j : first + j + 1, :] for j in (0, 1, rows - 2, rows - 1)]
        far = jnp.where(at_wall, 0.0, swapped[k, i : i + 1, :])
        return (
            jnp.where(bottom, far, own[2]),
            jnp.where(bottom, own[0], own[3]),
            jnp.where(bottom, own[1], far),
        )

    def roll_x(f, shift):
        return pltpu.roll(f, shift % nx, 0)

    def roll_z(f, shift):
        return pltpu.roll(f, shift % nz, 1)

    def smooth_x(f):
        return (roll_x(f, 1) + roll_x(f, -1)) + 2.0 * f

    def smooth(f):
        f = smooth_x(f)
        return (roll_z(f, 1) + roll_z(f, -1)) + 2.0 * f

    def slopes(below, centre, above):
        return strain_parts(
            [roll_x(f, -1) - roll_x(f, 1) for f in centre],
            [a - b for a, b in zip(above, below)],
            [roll_z(f, -1) - roll_z(f, 1) for f in centre],
        )

    @pl.when(jnp.logical_or(bottom, top))
    def _():
        for k in range(count):
            x0, zb = (k // nz_parts) * width, k % nz_parts
            for i in range(planes):
                c, x = divmod(i, width)
                for j, row in enumerate(rows_of(k, i)):
                    vel[j, c, x0 + x : x0 + x + 1, zb * lanes : (zb + 1) * lanes] = row
        u = [[vel[j, c] for c in range(3)] for j in range(3)]
        v = [[smooth(f) for f in row] for row in u]
        strain = slopes(*u)
        size = strain_size(strain)
        mean_strain = slopes(*v)
        mean_size = 0.25 * strain_size(mean_strain)
        scaled = [0.0625 * f for f in v[1]]
        pairs = [v[1][i] * scaled[j] for i, j in ((0, 0), (1, 1), (2, 2), (0, 1), (0, 2), (1, 2))]
        leonard = [smooth(p) - q for p, q in zip(products(u[1]), pairs)]
        model = [smooth(size * s) - mean_size * f for s, f in zip(strain, mean_strain)]
        lm, mm = contracted(leonard, model)
        coefficient = coefficient_of(
            *(jnp.sum(f, axis=(0, 1), keepdims=True) for f in (lm, mm)), nx * nz
        )
        eddy = coefficient * size

        def put(at):
            for k in range(count):
                x0, zb = (k // nz_parts) * width, k % nz_parts
                for x in range(width):
                    out[to[k], x, at : at + 1, :] = eddy[x0 + x : x0 + x + 1, zb * lanes : (zb + 1) * lanes]

        pl.when(bottom)(lambda: put(0))
        pl.when(top)(lambda: put(rows - 1))


def contracted(leonard, model):
    lm = mm = None
    for i in range(6):
        square = model[i] * model[i] if i < 3 else (0.5 * model[i]) * model[i]
        product = leonard[i] * model[i]
        lm = product if lm is None else lm + product
        mm = square if mm is None else mm + square
    return lm, mm


def coefficient_of(plane_lm, plane_mm, cells):
    scale = 1.0 / (256.0 * cells)
    return jnp.maximum(plane_lm * scale / (plane_mm * scale + 1e-06), 0.0)


def germano_kernel(nz_parts, width, rows, rank, parity, recv, out, vel, filt, ends, strains, means, part):
    count, _, lanes = recv.shape
    planes = 3 * width
    _, top = outer_sides(rank, parity, count)
    came, to = slots_of(out_order(count)), slots_of(back_order(count))
    nx = (count // nz_parts) * width
    nz = nz_parts * lanes
    blocks = range(nz_parts)
    lead = 8
    inner = slice(lead, lead + rows)
    for k in range(count):
        x0, zb = (k // nz_parts) * width, k % nz_parts
        for c in range(3):
            for x in range(width):
                i = c * width + x
                vel[c, x0 + x, zb, inner, :] = recv[came[k], i * rows : (i + 1) * rows, :]
                slots = planes * rows + i
                near = recv[came[k], slots : slots + 1, :]
                slots += aligned(planes)
                other = recv[came[k], slots : slots + 1, :]
                below = jnp.where(top, other, near)
                for side, (edge, at) in enumerate(((below, lead - 1), (other, lead + rows))):
                    vel[c, x0 + x, zb, at : at + 1, :] = edge
                    ends[c, x0 + x, zb, side : side + 1, :] = edge

    lower = slice(lead - 1, lead - 1 + rows)
    upper = slice(lead + 1, lead + 1 + rows)

    def smooth_x(read, x):
        return (read((x - 1) % nx) + read((x + 1) % nx)) + 2.0 * read(x)

    def keep_strain(field, x, kept, scale):
        left, right = (x - 1) % nx, (x + 1) % nx
        grad_z = [slope_z([field[c, x, zb, inner, :] for zb in blocks]) for c in range(3)]
        for zb in blocks:
            grad_x = [field[c, right, zb, inner, :] - field[c, left, zb, inner, :] for c in range(3)]
            grad_y = [field[c, x, zb, upper, :] - field[c, x, zb, lower, :] for c in range(3)]
            parts = strain_parts(grad_x, grad_y, [grad_z[c][zb] for c in range(3)])
            for i in range(6):
                kept[i, x, zb] = parts[i]
            kept[6, x, zb] = scale * strain_size(parts) if scale != 1.0 else strain_size(parts)

    for x in range(nx):
        keep_strain(vel, x, strains, 1.0)
        for c in range(3):
            for zb, f in enumerate(smooth_z([vel[c, x, zb, inner, :] for zb in blocks])):
                part[c, x, zb] = f
    for c in range(3):
        rims = [smooth_z([ends[c, x, zb] for zb in blocks]) for x in range(nx)]
        for x in range(nx):
            for zb in blocks:
                rim = smooth_x(lambda at: rims[at][zb], x)
                filt[c, x, zb, lead - 1 : lead, :] = rim[0:1, :]
                filt[c, x, zb, lead + rows : lead + rows + 1, :] = rim[1:2, :]
                filt[c, x, zb, inner, :] = smooth_x(lambda at: part[c, at, zb], x)
    def filter_z(read, kept):
        if not on_matrix_unit:
            for x in range(nx):
                for zb, f in enumerate(smooth_z([read(x, zb) for zb in blocks])):
                    part[kept, x, zb] = f
            return
        half = nx // 2
        for x0 in (0, half):
            planes_here = [
                jnp.concatenate([read(x, zb) for zb in blocks], axis=1) for x in range(x0, x0 + half)
            ]
            total = times_band(jnp.concatenate(planes_here, axis=0), band)
            for x in range(half):
                for zb in blocks:
                    part[kept, x0 + x, zb] = total[x * rows : (x + 1) * rows, zb * lanes : (zb + 1) * lanes]

    on_matrix_unit = nz <= 256 and rows * nx % 32 == 0 and rows % 8 == 0
    band = band_matrix(nz) if on_matrix_unit else None
    for i, (a, b) in enumerate(((0, 0), (1, 1), (2, 2), (0, 1), (0, 2), (1, 2))):
        filter_z(lambda x, zb: vel[a, x, zb, inner, :] * vel[b, x, zb, inner, :], 3 + i)
        filter_z(lambda x, zb: strains[6, x, zb] * strains[i, x, zb], 9 + i)
    for x in range(nx):
        keep_strain(filt, x, means, 0.25)

    sum_lm = sum_mm = None
    for x in range(nx):
        for zb in blocks:
            v = [filt[c, x, zb, inner, :] for c in range(3)]
            scaled = [0.0625 * f for f in v]
            size = means[6, x, zb]
            for i, (a, b) in enumerate(((0, 0), (1, 1), (2, 2), (0, 1), (0, 2), (1, 2))):
                leonard = smooth_x(lambda at: part[3 + i, at, zb], x) - v[a] * scaled[b]
                model = smooth_x(lambda at: part[9 + i, at, zb], x) - size * means[i, x, zb]
                square = model * model if i < 3 else (0.5 * model) * model
                sum_lm = leonard * model if sum_lm is None else sum_lm + leonard * model
                sum_mm = square if sum_mm is None else sum_mm + square

    coefficient = coefficient_of(
        *(jnp.sum(total, axis=1, keepdims=True) for total in (sum_lm, sum_mm)), nx * nz
    )
    for k in range(count):
        x0, zb = (k // nz_parts) * width, k % nz_parts
        for x in range(width):
            out[to[k], x] = coefficient * strains[6, x0 + x, zb]


def sweep_kernel(parity, back, velocity, tendency, eddy, reduced, factors, tree):
    count, width, rows, _ = back.shape
    length = count * rows // SEGMENTS
    slots = slots_of(back_order(count))

    def fill(rank, place):
        for x in range(width):
            eddy[x, place * rows : (place + 1) * rows, :] = back[slots[rank], x]

    by_parity(parity, count, fill)

    def row(ref, index, j):
        return ref[(*index, pl.ds(j, SEGMENTS, stride=length), slice(None))]

    planes = range(width)
    last_row = length - 1
    visc = [[1.0 + row(eddy, (x,), j) for x in planes] for j in range(length)]
    links = [[750.0 * (v + w) for v, w in zip(visc[j], visc[j + 1])] for j in range(last_row)]

    over = [jnp.ones_like(v) for v in visc[0]]
    under = [jnp.ones_like(v) for v in visc[0]]
    inverses = []
    for j in range(last_row):
        inverses.append([u / (o + e * u) for o, u, e in zip(over, under, links[j])])
        steps = [o * (1.0 / e) for o, e in zip(over, links[j])]
        under, over = (
            [u + t for u, t in zip(under, steps)],
            [(o + u) + t for o, u, t in zip(over, under, steps)],
        )
    inverses.append([u / o for o, u in zip(over, under)])

    value = first = corner = left = None
    reach = [jnp.ones_like(v) for v in visc[0]]
    for j in range(length):
        inverse = inverses[j]
        before = value
        source = [[2.0 * row(velocity, (c, x), j) + row(tendency, (c, x), j) for x in planes] for c in range(3)]
        value = [[f * r for f, r in zip(source[c], inverse)] for c in range(3)]
        if j > 0:
            carry = [e * r for e, r in zip(links[j - 1], inverse)]
            value = [[v + k * w for v, k, w in zip(value[c], carry, before[c])] for c in range(3)]
        left = [m * r for m, r in zip(reach, inverse)]
        if j == 0:
            first, corner = value, left
        else:
            first = [[f + m * v for f, m, v in zip(first[c], reach, value[c])] for c in range(3)]
            corner = [a + m * v for a, m, v in zip(corner, reach, left)]
        ratio = inverse
        if j < last_row:
            ratio = [e * r for e, r in zip(links[j], inverse)]
            reach = [m * r for m, r in zip(reach, ratio)]
        for x in planes:
            for c in range(3):
                factors[x, j, c] = value[c][x]
            factors[x, j, 3] = left[x]
            factors[x, j, 4] = ratio[x]

    def other(fields, step):
        return [pltpu.roll(f, (SEGMENTS - step) % SEGMENTS, 0) if step else f for f in fields]

    last, across, end = value, left, inverse
    seams = [750.0 * (v + w) for v, w in zip(visc[last_row], other(visc[0], 1))]
    level, step = 0, 1
    while step < SEGMENTS:
        link = other(seams, step - 1)
        first_b = [other(f, step) for f in first]
        last_b = [other(f, step) for f in last]
        corner_b, end_b, across_b = other(corner, step), other(end, step), other(across, step)
        stiff = [e / (1.0 + e * (d + a)) for e, d, a in zip(link, end, corner_b)]
        flux = [[k * (g - f) for k, g, f in zip(stiff, last[c], first_b[c])] for c in range(3)]
        from_left = [k * b for k, b in zip(stiff, across)]
        from_right = [k * b for k, b in zip(stiff, across_b)]
        for x in planes:
            for c in range(3):
                tree[x, level, c] = flux[c][x]
            tree[x, level, 3] = from_left[x]
            tree[x, level, 4] = from_right[x]
        first = [[f - b * t for f, b, t in zip(first[c], across, flux[c])] for c in range(3)]
        last = [[g + b * t for g, b, t in zip(last_b[c], across_b, flux[c])] for c in range(3)]
        corner = [a - b * k for a, b, k in zip(corner, across, from_left)]
        end = [d - b * k for d, b, k in zip(end_b, across_b, from_right)]
        across = [k * b for k, b in zip(from_left, across_b)]
        level, step = level + 1, step * 2
    for x in planes:
        rows_out = [f[x][0:1, :] for f in (*first, *last, corner, across, end, visc[0])]
        rows_out.append(visc[last_row][x][SEGMENTS - 1 :, :])
        for i, v in enumerate(rows_out):
            reduced[i * width + x : i * width + x + 1, :] = v


def spread_kernel(factors, tree, velocity, eddy, particular, response, eddy_out, sent):
    write = pltpu.make_async_copy(eddy, eddy_out, sent)
    write.start()
    width, length = factors.shape[:2]
    levels = tree.shape[1]
    sublane = lax.broadcasted_iota(jnp.int32, (SEGMENTS, LANES), 0)
    one, zero = (jnp.full((SEGMENTS, LANES), v, jnp.float32) for v in (1.0, 0.0))
    sides = [(c, zero, zero) for c in range(3)] + [(None, one, zero), (None, zero, one)]
    lefts = [[side[1]] * width for side in sides]
    rights = [[side[2]] * width for side in sides]
    for level in range(levels - 1, -1, -1):
        step = 2**level
        second = lax.rem(sublane, 2 * step) == step
        for n, (c, _, _) in enumerate(sides):
            for x in range(width):
                left, right = lefts[n][x], rights[n][x]
                through = tree[x, level, 3] * left - tree[x, level, 4] * right
                if c is not None:
                    through = tree[x, level, c] + through
                lefts[n][x] = jnp.where(second, pltpu.roll(through, step, 0), left)
                rights[n][x] = jnp.where(second, pltpu.roll(right, step, 0), -through)
    values = rights
    for j in range(length - 1, -1, -1):
        rows = pl.ds(j, SEGMENTS, stride=length)
        for n, (c, _, _) in enumerate(sides):
            for x in range(width):
                value = factors[x, j, 3] * lefts[n][x] + factors[x, j, 4] * values[n][x]
                if c is not None:
                    value = factors[x, j, c] + value
                    particular[c, x, rows, :] = value - velocity[c, x, rows, :]
                else:
                    response[n - 3, x, rows, :] = value
                values[n][x] = value
    write.wait()


def sources_of(step, count):
    ring = ring_of(count)
    return [ring[(ring.index(i) - step) % count] for i in range(count)]


def exchange_order(count):
    return range(count - 1, 0, -1)


def spread_kernel(factors, tree, velocity, eddy, particular, response, eddy_out, sent):
    write = pltpu.make_async_copy(eddy, eddy_out, sent)
    write.start()
    width, length = factors.shape[:2]
    levels = tree.shape[1]
    sublane = lax.broadcasted_iota(jnp.int32, (SEGMENTS, LANES), 0)
    one, zero = (jnp.full((SEGMENTS, LANES), v, jnp.float32) for v in (1.0, 0.0))
    sides = [(c, zero, zero) for c in range(3)] + [(None, one, zero), (None, zero, one)]
    lefts = [[side[1]] * width for side in sides]
    rights = [[side[2]] * width for side in sides]
    for level in range(levels - 1, -1, -1):
        step = 2**level
        second = lax.rem(sublane, 2 * step) == step
        for n, (c, _, _) in enumerate(sides):
            for x in range(width):
                left, right = lefts[n][x], rights[n][x]
                through = tree[x, level, 3] * left - tree[x, level, 4] * right
                if c is not None:
                    through = tree[x, level, c] + through
                lefts[n][x] = jnp.where(second, pltpu.roll(through, step, 0), left)
                rights[n][x] = jnp.where(second, pltpu.roll(right, step, 0), -through)
    values = rights
    for j in range(length - 1, -1, -1):
        rows = pl.ds(j, SEGMENTS, stride=length)
        for n, (c, _, _) in enumerate(sides):
            for x in range(width):
                value = factors[x, j, 3] * lefts[n][x] + factors[x, j, 4] * values[n][x]
                if c is not None:
                    value = factors[x, j, c] + value
                    particular[c, x, rows, :] = value - velocity[c, x, rows, :]
                else:
                    response[n - 3, x, rows, :] = value
                values[n][x] = value
    write.wait()


def partner(i, step, count):
    if count & (count - 1) == 0:
        return i ^ step
    return (i - step + count) % count


def finish_kernel(devices, position, particular, response, *rest):
    reduced, (result, gathered, fluxes, out, sent) = rest[:devices], rest[devices:]
    width = particular.shape[1]
    here = position[0]
    for step, ref in zip([0, *exchange_order(devices)], reduced):
        source = sum(jnp.where(here == i, s, 0) for i, s in enumerate(sources_of(step, devices)))
        gathered[source] = ref[...]

    def part(device, i):
        return gathered[device, i * width : (i + 1) * width, :]

    pivots, sources = [], []
    for i in range(devices + 1):
        visc = [part(i - 1, 10)] if i > 0 else []
        total = [part(i - 1, 8)] if i > 0 else []
        source = [part(i - 1, 3 + c) for c in range(3)] if i > 0 else [0.0] * 3
        if i < devices:
            visc.append(part(i, 9))
            total.append(part(i, 6))
            source = [s - part(i, c) for c, s in enumerate(source)]
        pivots.append(sum(total) + 1.0 / (750.0 * sum(visc)))
        sources.append(source)
    across = [part(i, 7) for i in range(devices)]
    minors = [jnp.ones_like(pivots[0]), pivots[0]]
    for i in range(1, devices + 1):
        minors.append(pivots[i] * minors[i] - (across[i - 1] * across[i - 1]) * minors[i - 1])
    inverses = [minors[i] / minors[i + 1] for i in range(devices + 1)]
    ratios = [b * r for b, r in zip(across, inverses)]
    for i in range(1, devices + 1):
        sources[i] = [s + ratios[i - 1] * t for s, t in zip(sources[i], sources[i - 1])]
    for i in range(devices, -1, -1):
        flux_here = [inverses[i] * s for s in sources[i]]
        flux = flux_here if i == devices else [f + ratios[i] * g for f, g in zip(flux_here, flux)]
        for c in range(3):
            fluxes[i, c * width : (c + 1) * width, :] = flux[c]

    writes = []
    for c in range(3):
        for x in range(width):
            r = c * width + x
            left, right = fluxes[here, r : r + 1, :], fluxes[here + 1, r : r + 1, :]
            out[c, x] = particular[c, x] + (response[0, x] * left - response[1, x] * right)
            writes.append(pltpu.make_async_copy(out.at[c, x], result.at[c, x], sent.at[r]))
            writes[-1].start()
    for write in writes:
        write.wait()


def in_vmem(count):
    return [pl.BlockSpec(memory_space=pltpu.VMEM)] * count


def in_hbm(count):
    return [pl.BlockSpec(memory_space=pltpu.HBM)] * count


def in_smem(count):
    return [pl.BlockSpec(memory_space=pltpu.SMEM)] * count


def params():
    return pltpu.CompilerParams(vmem_limit_bytes=VMEM_BYTES)


def swap_chunks(chunks, order):
    return lax.all_to_all(
        chunks, ("gx", "gz"), split_axis=0, concat_axis=0, tiled=True, axis_index_groups=[order]
    )


def body(velocity, tendency):
    _, width, cells, lanes = velocity.shape
    nz_parts = lax.axis_size("gz")
    count = lax.axis_size("gx") * nz_parts
    walls = lax.axis_size("gy")
    rows = cells // count
    nx = lax.axis_size("gx") * width
    padded = 16 + aligned(rows)
    f32 = jnp.float32

    planes = 3 * width
    depth = aligned(planes * rows + 2 * aligned(planes))
    position = lax.axis_index("gy").astype(jnp.int32).reshape(1)
    parity = lax.rem(position, 2)
    chunks = pl.pallas_call(
        functools.partial(pack_kernel, rows),
        out_shape=jax.ShapeDtypeStruct((count, depth, lanes), f32),
        in_specs=in_smem(1) + in_vmem(1),
        out_specs=pl.BlockSpec(memory_space=pltpu.VMEM),
        compiler_params=params(),
        name="pack",
    )(parity, velocity)
    recv = swap_chunks(chunks, out_order(count))
    slot = lax.slice_in_dim(recv, planes * rows, planes * rows + aligned(planes), axis=1)
    swapped = lax.ppermute(slot, ("gy", "gx", "gz"), swap_pairs(walls, count))
    rank = lax.axis_index(("gx", "gz")).astype(jnp.int32).reshape(1)
    chunk_shape = jax.ShapeDtypeStruct((count, width, rows, lanes), f32)
    cells_here = nx * nz_parts * rows * lanes
    provisional = pl.pallas_call(
        functools.partial(germano_kernel, nz_parts, width, rows),
        out_shape=chunk_shape,
        in_specs=in_smem(2) + in_vmem(1),
        out_specs=pl.BlockSpec(memory_space=pltpu.VMEM),
        scratch_shapes=[
            pltpu.VMEM((3, nx, nz_parts, padded, lanes), f32),
            pltpu.VMEM((3, nx, nz_parts, padded, lanes), f32),
            pltpu.VMEM((3, nx, nz_parts, 8, lanes), f32),
            pltpu.VMEM((7, nx, nz_parts, rows, lanes), f32),
            pltpu.VMEM((7, nx, nz_parts, rows, lanes), f32),
            pltpu.VMEM((15, nx, nz_parts, rows, lanes), f32),
        ],
        compiler_params=params(),
        cost_estimate=pl.CostEstimate(
            flops=300 * cells_here, bytes_accessed=16 * cells_here, transcendentals=2 * cells_here
        ),
        name="germano",
    )(rank, parity, recv)
    eddy_chunks = pl.pallas_call(
        functools.partial(edge_kernel, nz_parts, width, rows, walls),
        out_shape=chunk_shape,
        in_specs=in_smem(2) + in_vmem(3),
        out_specs=pl.BlockSpec(memory_space=pltpu.VMEM),
        scratch_shapes=[pltpu.VMEM((3, 3, nx, nz_parts * lanes), f32)],
        input_output_aliases={4: 0},
        compiler_params=params(),
        name="edge",
    )(rank, position, recv, swapped, provisional)
    back = swap_chunks(eddy_chunks, back_order(count))

    length = cells // SEGMENTS
    levels = SEGMENTS.bit_length() - 1
    packed = aligned(11 * width)
    eddy_here, reduced, factors, tree = pl.pallas_call(
        sweep_kernel,
        out_shape=(
            jax.ShapeDtypeStruct((width, cells, lanes), f32),
            jax.ShapeDtypeStruct((packed, lanes), f32),
            jax.ShapeDtypeStruct((width, length, 5, SEGMENTS, lanes), f32),
            jax.ShapeDtypeStruct((width, levels, 5, SEGMENTS, lanes), f32),
        ),
        in_specs=in_smem(1) + in_vmem(3),
        out_specs=tuple(in_vmem(4)),
        compiler_params=params(),
        name="sweep",
    )(parity, back, velocity, tendency)

    others = [
        lax.ppermute(reduced, "gy", [(s, i) for i, s in enumerate(sources_of(step, walls))])
        for step in exchange_order(walls)
    ]
    particular, response, eddy = pl.pallas_call(
        spread_kernel,
        out_shape=(
            jax.ShapeDtypeStruct(velocity.shape, f32),
            jax.ShapeDtypeStruct((2, *velocity.shape[1:]), f32),
            jax.ShapeDtypeStruct(eddy_here.shape, f32),
        ),
        in_specs=in_vmem(4),
        out_specs=tuple(in_vmem(2) + in_hbm(1)),
        scratch_shapes=[pltpu.SemaphoreType.DMA],
        compiler_params=params(),
        cost_estimate=pl.CostEstimate(
            flops=20 * velocity.size, bytes_accessed=16 * velocity.size, transcendentals=0
        ),
        name="spread",
    )(factors, tree, velocity, eddy_here)
    new_velocity = pl.pallas_call(
        functools.partial(finish_kernel, walls),
        out_shape=jax.ShapeDtypeStruct(velocity.shape, f32),
        in_specs=in_smem(1) + in_vmem(2 + walls),
        out_specs=in_hbm(1)[0],
        scratch_shapes=[
            pltpu.VMEM((walls, packed, lanes), f32),
            pltpu.VMEM((walls + 1, aligned(3 * width), lanes), f32),
            pltpu.VMEM(velocity.shape, f32),
            pltpu.SemaphoreType.DMA((planes,)),
        ],
        compiler_params=params(),
        name="finish",
    )(position, particular, response, reduced, *others)
    return (new_velocity, eddy)


def solution(mesh):
    return jax.shard_map(
        body,
        mesh=mesh,
        in_specs=(P(None, "gx", "gy", "gz"), P(None, "gx", "gy", "gz")),
        out_specs=(P(None, "gx", "gy", "gz"), P("gx", "gy", "gz")),
        check_vma=False,
    )
```

```python
import functools

import jax
import jax.numpy as jnp
from jax import lax
from jax.experimental import pallas as pl
from jax.experimental.pallas import tpu as pltpu
from jax.sharding import PartitionSpec as P

LANES = 128
SEGMENTS = 8
VMEM_BYTES = 24 * 2**20


def strain_parts(grad_x, grad_y, grad_z):
    return (
        grad_x[0],
        grad_y[1],
        grad_z[2],
        grad_y[0] + grad_x[1],
        grad_z[0] + grad_x[2],
        grad_z[1] + grad_y[2],
    )


def strain_size(parts):
    diagonal = parts[0] * parts[0] + parts[1] * parts[1] + parts[2] * parts[2]
    mixed = parts[3] * parts[3] + parts[4] * parts[4] + parts[5] * parts[5]
    return jnp.sqrt(0.5 * diagonal + 0.25 * mixed)


def beside(blocks):
    count = len(blocks)
    lanes = blocks[0].shape[1]
    down = [pltpu.roll(f, 1, 1) for f in blocks]
    up = [pltpu.roll(f, lanes - 1, 1) for f in blocks]
    if count > 1:
        lane = lax.broadcasted_iota(jnp.int32, blocks[0].shape, 1)
        first, last = lane == 0, lane == lanes - 1
        down, up = (
            [jnp.where(first, down[i - 1], down[i]) for i in range(count)],
            [jnp.where(last, up[(i + 1) % count], up[i]) for i in range(count)],
        )
    return down, up


def slope_z(blocks):
    down, up = beside(blocks)
    return [u - d for u, d in zip(up, down)]


def smooth_z(blocks):
    down, up = beside(blocks)
    return [(u + d) + 2.0 * f for f, u, d in zip(blocks, up, down)]


def band_matrix(n):
    shape = (n, n)
    apart = lax.broadcasted_iota(jnp.int32, shape, 0) - lax.broadcasted_iota(jnp.int32, shape, 1)
    apart = jnp.abs(apart)
    near = jnp.logical_or(apart == 1, apart == n - 1)
    return jnp.where(apart == 0, 2.0, jnp.where(near, 1.0, 0.0)).astype(jnp.bfloat16)


def times_band(f, band):
    total = None
    for i in range(3):
        piece = f.astype(jnp.bfloat16)
        product = jnp.dot(piece, band, preferred_element_type=jnp.float32)
        total = product if total is None else total + product
        if i < 2:
            f = f - piece.astype(jnp.float32)
    return total


def products(v):
    return (v[0] * v[0], v[1] * v[1], v[2] * v[2], v[0] * v[1], v[0] * v[2], v[1] * v[2])


def outer_ranks(count):
    return (count - 3, count - 1)


def places(parity, count):
    outer = outer_ranks(count)
    inner = iter(range(1, count - 1))
    return [
        (0 if outer[parity] == rank else count - 1) if rank in outer else next(inner)
        for rank in range(count)
    ]


def swap_pairs(walls, count):
    odd, even = outer_ranks(count)
    partners = {}

    def join(a, b):
        partners[a], partners[b] = b, a

    for core in range(0, count, 2):
        here = (core, core + 1)
        if odd in here or even in here:
            first = 1 if odd in here else 0
            for wall in range(first, walls - 1, 2):
                for rank in here:
                    join((wall, rank), (wall + 1, rank))
        for wall in range(walls):
            if (wall, core) not in partners:
                join((wall, core), (wall, core + 1))
    return [
        (wall * count + rank, to[0] * count + to[1])
        for wall in range(walls)
        for rank in range(count)
        for to in [partners.get((wall, rank), (wall, rank))]
    ]


def ring_of(count):
    return [0, *range(1, count, 2), *range(count - 2 + count % 2, 0, -2)]


def by_core(chips):
    return [2 * chip + 1 for chip in chips] + [2 * chip for chip in chips]


def out_order(count):
    return by_core(ring_of(count // 2))


def back_order(count):
    return by_core(range(count // 2 - 1, -1, -1))


def slots_of(order):
    return [order.index(r) for r in range(len(order))]


def by_parity(parity, count, fill):
    outer = outer_ranks(count)
    for rank, place in enumerate(places(0, count)):
        if rank not in outer:
            fill(rank, place)
    for turn in range(2):

        @pl.when(parity[0] == turn)
        def _():
            for rank in outer:
                fill(rank, places(turn, count)[rank])


def aligned(n):
    return -(-n // 8) * 8


def pack_kernel(rows, parity, velocity, out):
    _, width, cells, _ = velocity.shape
    count, depth, lanes = out.shape
    planes = 3 * width
    slots = planes * rows

    slot_of = slots_of(out_order(count))

    def fill(rank, place):
        rank = slot_of[rank]
        first = place * rows
        beside = [first - 1, first + rows]
        if place == 0:
            beside = [first, first + rows]
        if place == count - 1:
            beside = [first + rows - 1, first - 1]
        for i in range(planes):
            c, x = divmod(i, width)
            out[rank, i * rows : (i + 1) * rows, :] = velocity[c, x, first : first + rows, :]
            for slot, row in enumerate(beside):
                at = slots + slot * aligned(planes) + i
                out[rank, at : at + 1, :] = velocity[c, x, row : row + 1, :]

    by_parity(parity, count, fill)
    blank = aligned(planes) - planes
    for rank in range(count):
        for slot in range(2):
            at = slots + slot * aligned(planes) + planes
            out[rank, at : at + blank, :] = jnp.zeros((blank, lanes), jnp.float32)
        at = slots + 2 * aligned(planes)
        if at < depth:
            out[rank, at:, :] = jnp.zeros((depth - at, lanes), jnp.float32)


def outer_sides(rank, parity, count):
    outer = outer_ranks(count)
    even = parity[0] == 0
    bottom = rank[0] == jnp.where(even, outer[0], outer[1])
    top = rank[0] == jnp.where(even, outer[1], outer[0])
    return bottom, top


def edge_kernel(nz_parts, width, rows, walls, rank, position, recv, swapped, given, out, vel):
    count, _, lanes = recv.shape
    planes = 3 * width
    nx = (count // nz_parts) * width
    nz = nz_parts * lanes
    bottom, top = outer_sides(rank, [lax.rem(position[0], 2)], count)
    came, to = slots_of(out_order(count)), slots_of(back_order(count))
    at_wall = jnp.logical_or(
        jnp.logical_and(bottom, position[0] == 0), jnp.logical_and(top, position[0] == walls - 1)
    )

    def rows_of(k, i):
        k = came[k]
        first = i * rows
        own = [recv[k, first + j : first + j + 1, :] for j in (0, 1, rows - 2, rows - 1)]
        far = jnp.where(at_wall, 0.0, swapped[k, i : i + 1, :])
        return (
            jnp.where(bottom, far, own[2]),
            jnp.where(bottom, own[0], own[3]),
            jnp.where(bottom, own[1], far),
        )

    def roll_x(f, shift):
        return pltpu.roll(f, shift % nx, 0)

    def roll_z(f, shift):
        return pltpu.roll(f, shift % nz, 1)

    def smooth_x(f):
        return (roll_x(f, 1) + roll_x(f, -1)) + 2.0 * f

    def smooth(f):
        f = smooth_x(f)
        return (roll_z(f, 1) + roll_z(f, -1)) + 2.0 * f

    def slopes(below, centre, above):
        return strain_parts(
            [roll_x(f, -1) - roll_x(f, 1) for f in centre],
            [a - b for a, b in zip(above, below)],
            [roll_z(f, -1) - roll_z(f, 1) for f in centre],
        )

    @pl.when(jnp.logical_or(bottom, top))
    def _():
        for k in range(count):
            x0, zb = (k // nz_parts) * width, k % nz_parts
            for i in range(planes):
                c, x = divmod(i, width)
                for j, row in enumerate(rows_of(k, i)):
                    vel[j, c, x0 + x : x0 + x + 1, zb * lanes : (zb + 1) * lanes] = row
        u = [[vel[j, c] for c in range(3)] for j in range(3)]
        v = [[smooth(f) for f in row] for row in u]
        strain = slopes(*u)
        size = strain_size(strain)
        mean_strain = slopes(*v)
        mean_size = 0.25 * strain_size(mean_strain)
        scaled = [0.0625 * f for f in v[1]]
        pairs = [v[1][i] * scaled[j] for i, j in ((0, 0), (1, 1), (2, 2), (0, 1), (0, 2), (1, 2))]
        leonard = [smooth(p) - q for p, q in zip(products(u[1]), pairs)]
        model = [smooth(size * s) - mean_size * f for s, f in zip(strain, mean_strain)]
        lm, mm = contracted(leonard, model)
        coefficient = coefficient_of(
            *(jnp.sum(f, axis=(0, 1), keepdims=True) for f in (lm, mm)), nx * nz
        )
        eddy = coefficient * size

        def put(at):
            for k in range(count):
                x0, zb = (k // nz_parts) * width, k % nz_parts
                for x in range(width):
                    out[to[k], x, at : at + 1, :] = eddy[x0 + x : x0 + x + 1, zb * lanes : (zb + 1) * lanes]

        pl.when(bottom)(lambda: put(0))
        pl.when(top)(lambda: put(rows - 1))


def contracted(leonard, model):
    lm = mm = None
    for i in range(6):
        square = model[i] * model[i] if i < 3 else (0.5 * model[i]) * model[i]
        product = leonard[i] * model[i]
        lm = product if lm is None else lm + product
        mm = square if mm is None else mm + square
    return lm, mm


def coefficient_of(plane_lm, plane_mm, cells):
    scale = 1.0 / (256.0 * cells)
    return jnp.maximum(plane_lm * scale / (plane_mm * scale + 1e-06), 0.0)


def germano_kernel(nz_parts, width, rows, rank, parity, recv, out, vel, filt, ends, strains, means, part):
    count, _, lanes = recv.shape
    planes = 3 * width
    _, top = outer_sides(rank, parity, count)
    came, to = slots_of(out_order(count)), slots_of(back_order(count))
    nx = (count // nz_parts) * width
    nz = nz_parts * lanes
    blocks = range(nz_parts)
    lead = 8
    inner = slice(lead, lead + rows)
    for k in range(count):
        x0, zb = (k // nz_parts) * width, k % nz_parts
        for c in range(3):
            for x in range(width):
                i = c * width + x
                vel[c, x0 + x, zb, inner, :] = recv[came[k], i * rows : (i + 1) * rows, :]
                slots = planes * rows + i
                near = recv[came[k], slots : slots + 1, :]
                slots += aligned(planes)
                other = recv[came[k], slots : slots + 1, :]
                below = jnp.where(top, other, near)
                for side, (edge, at) in enumerate(((below, lead - 1), (other, lead + rows))):
                    vel[c, x0 + x, zb, at : at + 1, :] = edge
                    ends[c, x0 + x, zb, side : side + 1, :] = edge

    lower = slice(lead - 1, lead - 1 + rows)
    upper = slice(lead + 1, lead + 1 + rows)

    def smooth_x(read, x):
        return (read((x - 1) % nx) + read((x + 1) % nx)) + 2.0 * read(x)

    def keep_strain(field, x, kept, scale):
        left, right = (x - 1) % nx, (x + 1) % nx
        grad_z = [slope_z([field[c, x, zb, inner, :] for zb in blocks]) for c in range(3)]
        for zb in blocks:
            grad_x = [field[c, right, zb, inner, :] - field[c, left, zb, inner, :] for c in range(3)]
            grad_y = [field[c, x, zb, upper, :] - field[c, x, zb, lower, :] for c in range(3)]
            parts = strain_parts(grad_x, grad_y, [grad_z[c][zb] for c in range(3)])
            for i in range(6):
                kept[i, x, zb] = parts[i]
            kept[6, x, zb] = scale * strain_size(parts) if scale != 1.0 else strain_size(parts)

    for x in range(nx):
        keep_strain(vel, x, strains, 1.0)
        for c in range(3):
            for zb, f in enumerate(smooth_z([vel[c, x, zb, inner, :] for zb in blocks])):
                part[c, x, zb] = f
    for c in range(3):
        rims = [smooth_z([ends[c, x, zb] for zb in blocks]) for x in range(nx)]
        for x in range(nx):
            for zb in blocks:
                rim = smooth_x(lambda at: rims[at][zb], x)
                filt[c, x, zb, lead - 1 : lead, :] = rim[0:1, :]
                filt[c, x, zb, lead + rows : lead + rows + 1, :] = rim[1:2, :]
                filt[c, x, zb, inner, :] = smooth_x(lambda at: part[c, at, zb], x)
    def filter_z(read, kept):
        if not on_matrix_unit:
            for x in range(nx):
                for zb, f in enumerate(smooth_z([read(x, zb) for zb in blocks])):
                    part[kept, x, zb] = f
            return
        half = nx // 2
        for x0 in (0, half):
            planes_here = [
                jnp.concatenate([read(x, zb) for zb in blocks], axis=1) for x in range(x0, x0 + half)
            ]
            total = times_band(jnp.concatenate(planes_here, axis=0), band)
            for x in range(half):
                for zb in blocks:
                    part[kept, x0 + x, zb] = total[x * rows : (x + 1) * rows, zb * lanes : (zb + 1) * lanes]

    on_matrix_unit = nz <= 256 and rows * nx % 32 == 0 and rows % 8 == 0
    band = band_matrix(nz) if on_matrix_unit else None
    for i, (a, b) in enumerate(((0, 0), (1, 1), (2, 2), (0, 1), (0, 2), (1, 2))):
        filter_z(lambda x, zb: vel[a, x, zb, inner, :] * vel[b, x, zb, inner, :], 3 + i)
        filter_z(lambda x, zb: strains[6, x, zb] * strains[i, x, zb], 9 + i)
    for x in range(nx):
        keep_strain(filt, x, means, 0.25)

    sum_lm = sum_mm = None
    for x in range(nx):
        for zb in blocks:
            v = [filt[c, x, zb, inner, :] for c in range(3)]
            scaled = [0.0625 * f for f in v]
            size = means[6, x, zb]
            for i, (a, b) in enumerate(((0, 0), (1, 1), (2, 2), (0, 1), (0, 2), (1, 2))):
                leonard = smooth_x(lambda at: part[3 + i, at, zb], x) - v[a] * scaled[b]
                model = smooth_x(lambda at: part[9 + i, at, zb], x) - size * means[i, x, zb]
                square = model * model if i < 3 else (0.5 * model) * model
                sum_lm = leonard * model if sum_lm is None else sum_lm + leonard * model
                sum_mm = square if sum_mm is None else sum_mm + square

    coefficient = coefficient_of(
        *(jnp.sum(total, axis=1, keepdims=True) for total in (sum_lm, sum_mm)), nx * nz
    )
    for k in range(count):
        x0, zb = (k // nz_parts) * width, k % nz_parts
        for x in range(width):
            out[to[k], x] = coefficient * strains[6, x0 + x, zb]


def sweep_kernel(parity, back, velocity, tendency, eddy, reduced, factors, tree):
    count, width, rows, _ = back.shape
    length = count * rows // SEGMENTS
    slots = slots_of(back_order(count))

    def fill(rank, place):
        for x in range(width):
            eddy[x, place * rows : (place + 1) * rows, :] = back[slots[rank], x]

    by_parity(parity, count, fill)

    def row(ref, index, j):
        return ref[(*index, pl.ds(j, SEGMENTS, stride=length), slice(None))]

    planes = range(width)
    last_row = length - 1
    visc = [[1.0 + row(eddy, (x,), j) for x in planes] for j in range(length)]
    links = [[750.0 * (v + w) for v, w in zip(visc[j], visc[j + 1])] for j in range(last_row)]

    over = [jnp.ones_like(v) for v in visc[0]]
    under = [jnp.ones_like(v) for v in visc[0]]
    inverses = []
    for j in range(last_row):
        inverses.append([u / (o + e * u) for o, u, e in zip(over, under, links[j])])
        steps = [o * (1.0 / e) for o, e in zip(over, links[j])]
        under, over = (
            [u + t for u, t in zip(under, steps)],
            [(o + u) + t for o, u, t in zip(over, under, steps)],
        )
    inverses.append([u / o for o, u in zip(over, under)])

    value = first = corner = left = None
    reach = [jnp.ones_like(v) for v in visc[0]]
    for j in range(length):
        inverse = inverses[j]
        before = value
        source = [[2.0 * row(velocity, (c, x), j) + row(tendency, (c, x), j) for x in planes] for c in range(3)]
        value = [[f * r for f, r in zip(source[c], inverse)] for c in range(3)]
        if j > 0:
            carry = [e * r for e, r in zip(links[j - 1], inverse)]
            value = [[v + k * w for v, k, w in zip(value[c], carry, before[c])] for c in range(3)]
        left = [m * r for m, r in zip(reach, inverse)]
        if j == 0:
            first, corner = value, left
        else:
            first = [[f + m * v for f, m, v in zip(first[c], reach, value[c])] for c in range(3)]
            corner = [a + m * v for a, m, v in zip(corner, reach, left)]
        ratio = inverse
        if j < last_row:
            ratio = [e * r for e, r in zip(links[j], inverse)]
            reach = [m * r for m, r in zip(reach, ratio)]
        for x in planes:
            for c in range(3):
                factors[x, j, c] = value[c][x]
            factors[x, j, 3] = left[x]
            factors[x, j, 4] = ratio[x]

    def other(fields, step):
        return [pltpu.roll(f, (SEGMENTS - step) % SEGMENTS, 0) if step else f for f in fields]

    last, across, end = value, left, inverse
    seams = [750.0 * (v + w) for v, w in zip(visc[last_row], other(visc[0], 1))]
    level, step = 0, 1
    while step < SEGMENTS:
        link = other(seams, step - 1)
        first_b = [other(f, step) for f in first]
        last_b = [other(f, step) for f in last]
        corner_b, end_b, across_b = other(corner, step), other(end, step), other(across, step)
        stiff = [e / (1.0 + e * (d + a)) for e, d, a in zip(link, end, corner_b)]
        flux = [[k * (g - f) for k, g, f in zip(stiff, last[c], first_b[c])] for c in range(3)]
        from_left = [k * b for k, b in zip(stiff, across)]
        from_right = [k * b for k, b in zip(stiff, across_b)]
        for x in planes:
            for c in range(3):
                tree[x, level, c] = flux[c][x]
            tree[x, level, 3] = from_left[x]
            tree[x, level, 4] = from_right[x]
        first = [[f - b * t for f, b, t in zip(first[c], across, flux[c])] for c in range(3)]
        last = [[g + b * t for g, b, t in zip(last_b[c], across_b, flux[c])] for c in range(3)]
        corner = [a - b * k for a, b, k in zip(corner, across, from_left)]
        end = [d - b * k for d, b, k in zip(end_b, across_b, from_right)]
        across = [k * b for k, b in zip(from_left, across_b)]
        level, step = level + 1, step * 2
    for x in planes:
        rows_out = [f[x][0:1, :] for f in (*first, *last, corner, across, end, visc[0])]
        rows_out.append(visc[last_row][x][SEGMENTS - 1 :, :])
        for i, v in enumerate(rows_out):
            reduced[i * width + x : i * width + x + 1, :] = v


def spread_kernel(factors, tree, velocity, eddy, particular, response, eddy_out, sent):
    write = pltpu.make_async_copy(eddy, eddy_out, sent)
    write.start()
    width, length = factors.shape[:2]
    levels = tree.shape[1]
    sublane = lax.broadcasted_iota(jnp.int32, (SEGMENTS, LANES), 0)
    one, zero = (jnp.full((SEGMENTS, LANES), v, jnp.float32) for v in (1.0, 0.0))
    sides = [(c, zero, zero) for c in range(3)] + [(None, one, zero), (None, zero, one)]
    lefts = [[side[1]] * width for side in sides]
    rights = [[side[2]] * width for side in sides]
    for level in range(levels - 1, -1, -1):
        step = 2**level
        second = lax.rem(sublane, 2 * step) == step
        for n, (c, _, _) in enumerate(sides):
            for x in range(width):
                left, right = lefts[n][x], rights[n][x]
                through = tree[x, level, 3] * left - tree[x, level, 4] * right
                if c is not None:
                    through = tree[x, level, c] + through
                lefts[n][x] = jnp.where(second, pltpu.roll(through, step, 0), left)
                rights[n][x] = jnp.where(second, pltpu.roll(right, step, 0), -through)
    values = rights
    for j in range(length - 1, -1, -1):
        rows = pl.ds(j, SEGMENTS, stride=length)
        for n, (c, _, _) in enumerate(sides):
            for x in range(width):
                value = factors[x, j, 3] * lefts[n][x] + factors[x, j, 4] * values[n][x]
                if c is not None:
                    value = factors[x, j, c] + value
                    particular[c, x, rows, :] = value - velocity[c, x, rows, :]
                else:
                    response[n - 3, x, rows, :] = value
                values[n][x] = value
    write.wait()


def sources_of(step, count):
    return [(i - step) % count for i in range(count)]


def exchange_order(count):
    return range(count - 1, 0, -1)


def spread_kernel(factors, tree, velocity, eddy, particular, response, eddy_out, sent):
    write = pltpu.make_async_copy(eddy, eddy_out, sent)
    write.start()
    width, length = factors.shape[:2]
    levels = tree.shape[1]
    sublane = lax.broadcasted_iota(jnp.int32, (SEGMENTS, LANES), 0)
    one, zero = (jnp.full((SEGMENTS, LANES), v, jnp.float32) for v in (1.0, 0.0))
    sides = [(c, zero, zero) for c in range(3)] + [(None, one, zero), (None, zero, one)]
    lefts = [[side[1]] * width for side in sides]
    rights = [[side[2]] * width for side in sides]
    for level in range(levels - 1, -1, -1):
        step = 2**level
        second = lax.rem(sublane, 2 * step) == step
        for n, (c, _, _) in enumerate(sides):
            for x in range(width):
                left, right = lefts[n][x], rights[n][x]
                through = tree[x, level, 3] * left - tree[x, level, 4] * right
                if c is not None:
                    through = tree[x, level, c] + through
                lefts[n][x] = jnp.where(second, pltpu.roll(through, step, 0), left)
                rights[n][x] = jnp.where(second, pltpu.roll(right, step, 0), -through)
    values = rights
    for j in range(length - 1, -1, -1):
        rows = pl.ds(j, SEGMENTS, stride=length)
        for n, (c, _, _) in enumerate(sides):
            for x in range(width):
                value = factors[x, j, 3] * lefts[n][x] + factors[x, j, 4] * values[n][x]
                if c is not None:
                    value = factors[x, j, c] + value
                    particular[c, x, rows, :] = value - velocity[c, x, rows, :]
                else:
                    response[n - 3, x, rows, :] = value
                values[n][x] = value
    write.wait()


def partner(i, step, count):
    if count & (count - 1) == 0:
        return i ^ step
    return (i - step + count) % count


def finish_kernel(devices, position, particular, response, *rest):
    reduced, (result, gathered, fluxes, out, sent) = rest[:devices], rest[devices:]
    width = particular.shape[1]
    here = position[0]
    for step, ref in zip([0, *exchange_order(devices)], reduced):
        source = sum(jnp.where(here == i, s, 0) for i, s in enumerate(sources_of(step, devices)))
        gathered[source] = ref[...]

    def part(device, i):
        return gathered[device, i * width : (i + 1) * width, :]

    pivots, sources = [], []
    for i in range(devices + 1):
        visc = [part(i - 1, 10)] if i > 0 else []
        total = [part(i - 1, 8)] if i > 0 else []
        source = [part(i - 1, 3 + c) for c in range(3)] if i > 0 else [0.0] * 3
        if i < devices:
            visc.append(part(i, 9))
            total.append(part(i, 6))
            source = [s - part(i, c) for c, s in enumerate(source)]
        pivots.append(sum(total) + 1.0 / (750.0 * sum(visc)))
        sources.append(source)
    across = [part(i, 7) for i in range(devices)]
    minors = [jnp.ones_like(pivots[0]), pivots[0]]
    for i in range(1, devices + 1):
        minors.append(pivots[i] * minors[i] - (across[i - 1] * across[i - 1]) * minors[i - 1])
    inverses = [minors[i] / minors[i + 1] for i in range(devices + 1)]
    ratios = [b * r for b, r in zip(across, inverses)]
    for i in range(1, devices + 1):
        sources[i] = [s + ratios[i - 1] * t for s, t in zip(sources[i], sources[i - 1])]
    for i in range(devices, -1, -1):
        flux_here = [inverses[i] * s for s in sources[i]]
        flux = flux_here if i == devices else [f + ratios[i] * g for f, g in zip(flux_here, flux)]
        for c in range(3):
            fluxes[i, c * width : (c + 1) * width, :] = flux[c]

    writes = []
    for c in range(3):
        for x in range(width):
            r = c * width + x
            left, right = fluxes[here, r : r + 1, :], fluxes[here + 1, r : r + 1, :]
            out[c, x] = particular[c, x] + (response[0, x] * left - response[1, x] * right)
            writes.append(pltpu.make_async_copy(out.at[c, x], result.at[c, x], sent.at[r]))
            writes[-1].start()
    for write in writes:
        write.wait()


def in_vmem(count):
    return [pl.BlockSpec(memory_space=pltpu.VMEM)] * count


def in_hbm(count):
    return [pl.BlockSpec(memory_space=pltpu.HBM)] * count


def in_smem(count):
    return [pl.BlockSpec(memory_space=pltpu.SMEM)] * count


def params():
    return pltpu.CompilerParams(vmem_limit_bytes=VMEM_BYTES)


def swap_chunks(chunks, order):
    return lax.all_to_all(
        chunks, ("gx", "gz"), split_axis=0, concat_axis=0, tiled=True, axis_index_groups=[order]
    )


def body(velocity, tendency):
    _, width, cells, lanes = velocity.shape
    nz_parts = lax.axis_size("gz")
    count = lax.axis_size("gx") * nz_parts
    walls = lax.axis_size("gy")
    rows = cells // count
    nx = lax.axis_size("gx") * width
    padded = 16 + aligned(rows)
    f32 = jnp.float32

    planes = 3 * width
    depth = aligned(planes * rows + 2 * aligned(planes))
    position = lax.axis_index("gy").astype(jnp.int32).reshape(1)
    parity = lax.rem(position, 2)
    chunks = pl.pallas_call(
        functools.partial(pack_kernel, rows),
        out_shape=jax.ShapeDtypeStruct((count, depth, lanes), f32),
        in_specs=in_smem(1) + in_vmem(1),
        out_specs=pl.BlockSpec(memory_space=pltpu.VMEM),
        compiler_params=params(),
        name="pack",
    )(parity, velocity)
    recv = swap_chunks(chunks, out_order(count))
    slot = lax.slice_in_dim(recv, planes * rows, planes * rows + aligned(planes), axis=1)
    swapped = lax.ppermute(slot, ("gy", "gx", "gz"), swap_pairs(walls, count))
    rank = lax.axis_index(("gx", "gz")).astype(jnp.int32).reshape(1)
    chunk_shape = jax.ShapeDtypeStruct((count, width, rows, lanes), f32)
    cells_here = nx * nz_parts * rows * lanes
    provisional = pl.pallas_call(
        functools.partial(germano_kernel, nz_parts, width, rows),
        out_shape=chunk_shape,
        in_specs=in_smem(2) + in_vmem(1),
        out_specs=pl.BlockSpec(memory_space=pltpu.VMEM),
        scratch_shapes=[
            pltpu.VMEM((3, nx, nz_parts, padded, lanes), f32),
            pltpu.VMEM((3, nx, nz_parts, padded, lanes), f32),
            pltpu.VMEM((3, nx, nz_parts, 8, lanes), f32),
            pltpu.VMEM((7, nx, nz_parts, rows, lanes), f32),
            pltpu.VMEM((7, nx, nz_parts, rows, lanes), f32),
            pltpu.VMEM((15, nx, nz_parts, rows, lanes), f32),
        ],
        compiler_params=params(),
        cost_estimate=pl.CostEstimate(
            flops=300 * cells_here, bytes_accessed=16 * cells_here, transcendentals=2 * cells_here
        ),
        name="germano",
    )(rank, parity, recv)
    eddy_chunks = pl.pallas_call(
        functools.partial(edge_kernel, nz_parts, width, rows, walls),
        out_shape=chunk_shape,
        in_specs=in_smem(2) + in_vmem(3),
        out_specs=pl.BlockSpec(memory_space=pltpu.VMEM),
        scratch_shapes=[pltpu.VMEM((3, 3, nx, nz_parts * lanes), f32)],
        input_output_aliases={4: 0},
        compiler_params=params(),
        name="edge",
    )(rank, position, recv, swapped, provisional)
    back = swap_chunks(eddy_chunks, back_order(count))

    length = cells // SEGMENTS
    levels = SEGMENTS.bit_length() - 1
    packed = aligned(11 * width)
    eddy_here, reduced, factors, tree = pl.pallas_call(
        sweep_kernel,
        out_shape=(
            jax.ShapeDtypeStruct((width, cells, lanes), f32),
            jax.ShapeDtypeStruct((packed, lanes), f32),
            jax.ShapeDtypeStruct((width, length, 5, SEGMENTS, lanes), f32),
            jax.ShapeDtypeStruct((width, levels, 5, SEGMENTS, lanes), f32),
        ),
        in_specs=in_smem(1) + in_vmem(3),
        out_specs=tuple(in_vmem(4)),
        compiler_params=params(),
        name="sweep",
    )(parity, back, velocity, tendency)

    others = [
        lax.ppermute(reduced, "gy", [(s, i) for i, s in enumerate(sources_of(step, walls))])
        for step in exchange_order(walls)
    ]
    particular, response, eddy = pl.pallas_call(
        spread_kernel,
        out_shape=(
            jax.ShapeDtypeStruct(velocity.shape, f32),
            jax.ShapeDtypeStruct((2, *velocity.shape[1:]), f32),
            jax.ShapeDtypeStruct(eddy_here.shape, f32),
        ),
        in_specs=in_vmem(4),
        out_specs=tuple(in_vmem(2) + in_hbm(1)),
        scratch_shapes=[pltpu.SemaphoreType.DMA],
        compiler_params=params(),
        cost_estimate=pl.CostEstimate(
            flops=20 * velocity.size, bytes_accessed=16 * velocity.size, transcendentals=0
        ),
        name="spread",
    )(factors, tree, velocity, eddy_here)
    new_velocity = pl.pallas_call(
        functools.partial(finish_kernel, walls),
        out_shape=jax.ShapeDtypeStruct(velocity.shape, f32),
        in_specs=in_smem(1) + in_vmem(2 + walls),
        out_specs=in_hbm(1)[0],
        scratch_shapes=[
            pltpu.VMEM((walls, packed, lanes), f32),
            pltpu.VMEM((walls + 1, aligned(3 * width), lanes), f32),
            pltpu.VMEM(velocity.shape, f32),
            pltpu.SemaphoreType.DMA((planes,)),
        ],
        compiler_params=params(),
        name="finish",
    )(position, particular, response, reduced, *others)
    return (new_velocity, eddy)


def solution(mesh):
    return jax.shard_map(
        body,
        mesh=mesh,
        in_specs=(P(None, "gx", "gy", "gz"), P(None, "gx", "gy", "gz")),
        out_specs=(P(None, "gx", "gy", "gz"), P("gx", "gy", "gz")),
        check_vma=False,
    )
```

```python
import functools

import jax
import jax.numpy as jnp
from jax import lax
from jax.experimental import pallas as pl
from jax.experimental.pallas import tpu as pltpu
from jax.sharding import PartitionSpec as P

LANES = 128
SEGMENTS = 8
VMEM_BYTES = 24 * 2**20


def strain_parts(grad_x, grad_y, grad_z):
    return (
        grad_x[0],
        grad_y[1],
        grad_z[2],
        grad_y[0] + grad_x[1],
        grad_z[0] + grad_x[2],
        grad_z[1] + grad_y[2],
    )


def strain_size(parts):
    diagonal = parts[0] * parts[0] + parts[1] * parts[1] + parts[2] * parts[2]
    mixed = parts[3] * parts[3] + parts[4] * parts[4] + parts[5] * parts[5]
    return jnp.sqrt(0.5 * diagonal + 0.25 * mixed)


def beside(blocks):
    count = len(blocks)
    lanes = blocks[0].shape[1]
    down = [pltpu.roll(f, 1, 1) for f in blocks]
    up = [pltpu.roll(f, lanes - 1, 1) for f in blocks]
    if count > 1:
        lane = lax.broadcasted_iota(jnp.int32, blocks[0].shape, 1)
        first, last = lane == 0, lane == lanes - 1
        down, up = (
            [jnp.where(first, down[i - 1], down[i]) for i in range(count)],
            [jnp.where(last, up[(i + 1) % count], up[i]) for i in range(count)],
        )
    return down, up


def slope_z(blocks):
    down, up = beside(blocks)
    return [u - d for u, d in zip(up, down)]


def smooth_z(blocks):
    down, up = beside(blocks)
    return [(u + d) + 2.0 * f for f, u, d in zip(blocks, up, down)]


def band_matrix(n):
    shape = (n, n)
    apart = lax.broadcasted_iota(jnp.int32, shape, 0) - lax.broadcasted_iota(jnp.int32, shape, 1)
    apart = jnp.abs(apart)
    near = jnp.logical_or(apart == 1, apart == n - 1)
    return jnp.where(apart == 0, 2.0, jnp.where(near, 1.0, 0.0)).astype(jnp.bfloat16)


def times_band(f, band):
    total = None
    for i in range(3):
        piece = f.astype(jnp.bfloat16)
        product = jnp.dot(piece, band, preferred_element_type=jnp.float32)
        total = product if total is None else total + product
        if i < 2:
            f = f - piece.astype(jnp.float32)
    return total


def products(v):
    return (v[0] * v[0], v[1] * v[1], v[2] * v[2], v[0] * v[1], v[0] * v[2], v[1] * v[2])


def outer_ranks(count):
    return (count - 3, count - 1)


def places(parity, count):
    outer = outer_ranks(count)
    inner = iter(range(1, count - 1))
    return [
        (0 if outer[parity] == rank else count - 1) if rank in outer else next(inner)
        for rank in range(count)
    ]


def swap_pairs(walls, count):
    odd, even = outer_ranks(count)
    partners = {}

    def join(a, b):
        partners[a], partners[b] = b, a

    for core in range(0, count, 2):
        here = (core, core + 1)
        if odd in here or even in here:
            first = 1 if odd in here else 0
            for wall in range(first, walls - 1, 2):
                for rank in here:
                    join((wall, rank), (wall + 1, rank))
        for wall in range(walls):
            if (wall, core) not in partners:
                join((wall, core), (wall, core + 1))
    return [
        (wall * count + rank, to[0] * count + to[1])
        for wall in range(walls)
        for rank in range(count)
        for to in [partners.get((wall, rank), (wall, rank))]
    ]


def ring_of(count):
    return [0, *range(1, count, 2), *range(count - 2 + count % 2, 0, -2)]


def by_core(chips):
    return [2 * chip + 1 for chip in chips] + [2 * chip for chip in chips]


def out_order(count):
    return by_core(ring_of(count // 2))


def back_order(count):
    return by_core(range(count // 2 - 1, -1, -1))


def slots_of(order):
    return [order.index(r) for r in range(len(order))]


def by_parity(parity, count, fill):
    outer = outer_ranks(count)
    for rank, place in enumerate(places(0, count)):
        if rank not in outer:
            fill(rank, place)
    for turn in range(2):

        @pl.when(parity[0] == turn)
        def _():
            for rank in outer:
                fill(rank, places(turn, count)[rank])


def aligned(n):
    return -(-n // 8) * 8


def pack_kernel(rows, parity, velocity, out):
    _, width, cells, _ = velocity.shape
    count, depth, lanes = out.shape
    planes = 3 * width
    slots = planes * rows

    slot_of = slots_of(out_order(count))

    def fill(rank, place):
        rank = slot_of[rank]
        first = place * rows
        beside = [first - 1, first + rows]
        if place == 0:
            beside = [first, first + rows]
        if place == count - 1:
            beside = [first + rows - 1, first - 1]
        for i in range(planes):
            c, x = divmod(i, width)
            out[rank, i * rows : (i + 1) * rows, :] = velocity[c, x, first : first + rows, :]
            for slot, row in enumerate(beside):
                at = slots + slot * aligned(planes) + i
                out[rank, at : at + 1, :] = velocity[c, x, row : row + 1, :]

    by_parity(parity, count, fill)
    blank = aligned(planes) - planes
    for rank in range(count):
        for slot in range(2):
            at = slots + slot * aligned(planes) + planes
            out[rank, at : at + blank, :] = jnp.zeros((blank, lanes), jnp.float32)
        at = slots + 2 * aligned(planes)
        if at < depth:
            out[rank, at:, :] = jnp.zeros((depth - at, lanes), jnp.float32)


def outer_sides(rank, parity, count):
    outer = outer_ranks(count)
    even = parity[0] == 0
    bottom = rank[0] == jnp.where(even, outer[0], outer[1])
    top = rank[0] == jnp.where(even, outer[1], outer[0])
    return bottom, top


def edge_kernel(nz_parts, width, rows, walls, rank, position, recv, swapped, given, out, vel):
    count, _, lanes = recv.shape
    planes = 3 * width
    nx = (count // nz_parts) * width
    nz = nz_parts * lanes
    bottom, top = outer_sides(rank, [lax.rem(position[0], 2)], count)
    came, to = slots_of(out_order(count)), slots_of(back_order(count))
    at_wall = jnp.logical_or(
        jnp.logical_and(bottom, position[0] == 0), jnp.logical_and(top, position[0] == walls - 1)
    )

    def rows_of(k, i):
        k = came[k]
        first = i * rows
        own = [recv[k, first + j : first + j + 1, :] for j in (0, 1, rows - 2, rows - 1)]
        far = jnp.where(at_wall, 0.0, swapped[k, i : i + 1, :])
        return (
            jnp.where(bottom, far, own[2]),
            jnp.where(bottom, own[0], own[3]),
            jnp.where(bottom, own[1], far),
        )

    def roll_x(f, shift):
        return pltpu.roll(f, shift % nx, 0)

    def roll_z(f, shift):
        return pltpu.roll(f, shift % nz, 1)

    def smooth_x(f):
        return (roll_x(f, 1) + roll_x(f, -1)) + 2.0 * f

    def smooth(f):
        f = smooth_x(f)
        return (roll_z(f, 1) + roll_z(f, -1)) + 2.0 * f

    def slopes(below, centre, above):
        return strain_parts(
            [roll_x(f, -1) - roll_x(f, 1) for f in centre],
            [a - b for a, b in zip(above, below)],
            [roll_z(f, -1) - roll_z(f, 1) for f in centre],
        )

    @pl.when(jnp.logical_or(bottom, top))
    def _():
        for k in range(count):
            x0, zb = (k // nz_parts) * width, k % nz_parts
            for i in range(planes):
                c, x = divmod(i, width)
                for j, row in enumerate(rows_of(k, i)):
                    vel[j, c, x0 + x : x0 + x + 1, zb * lanes : (zb + 1) * lanes] = row
        u = [[vel[j, c] for c in range(3)] for j in range(3)]
        v = [[smooth(f) for f in row] for row in u]
        strain = slopes(*u)
        size = strain_size(strain)
        mean_strain = slopes(*v)
        mean_size = 0.25 * strain_size(mean_strain)
        scaled = [0.0625 * f for f in v[1]]
        pairs = [v[1][i] * scaled[j] for i, j in ((0, 0), (1, 1), (2, 2), (0, 1), (0, 2), (1, 2))]
        leonard = [smooth(p) - q for p, q in zip(products(u[1]), pairs)]
        model = [smooth(size * s) - mean_size * f for s, f in zip(strain, mean_strain)]
        lm, mm = contracted(leonard, model)
        coefficient = coefficient_of(
            *(jnp.sum(f, axis=(0, 1), keepdims=True) for f in (lm, mm)), nx * nz
        )
        eddy = coefficient * size

        def put(at):
            for k in range(count):
                x0, zb = (k // nz_parts) * width, k % nz_parts
                for x in range(width):
                    out[to[k], x, at : at + 1, :] = eddy[x0 + x : x0 + x + 1, zb * lanes : (zb + 1) * lanes]

        pl.when(bottom)(lambda: put(0))
        pl.when(top)(lambda: put(rows - 1))


def contracted(leonard, model):
    lm = mm = None
    for i in range(6):
        square = model[i] * model[i] if i < 3 else (0.5 * model[i]) * model[i]
        product = leonard[i] * model[i]
        lm = product if lm is None else lm + product
        mm = square if mm is None else mm + square
    return lm, mm


def coefficient_of(plane_lm, plane_mm, cells):
    scale = 1.0 / (256.0 * cells)
    return jnp.maximum(plane_lm * scale / (plane_mm * scale + 1e-06), 0.0)


def germano_kernel(nz_parts, width, rows, rank, parity, recv, out, vel, filt, ends, strains, means, part):
    count, _, lanes = recv.shape
    planes = 3 * width
    _, top = outer_sides(rank, parity, count)
    came, to = slots_of(out_order(count)), slots_of(back_order(count))
    nx = (count // nz_parts) * width
    nz = nz_parts * lanes
    blocks = range(nz_parts)
    lead = 8
    inner = slice(lead, lead + rows)
    for k in range(count):
        x0, zb = (k // nz_parts) * width, k % nz_parts
        for c in range(3):
            for x in range(width):
                i = c * width + x
                vel[c, x0 + x, zb, inner, :] = recv[came[k], i * rows : (i + 1) * rows, :]
                slots = planes * rows + i
                near = recv[came[k], slots : slots + 1, :]
                slots += aligned(planes)
                other = recv[came[k], slots : slots + 1, :]
                below = jnp.where(top, other, near)
                for side, (edge, at) in enumerate(((below, lead - 1), (other, lead + rows))):
                    vel[c, x0 + x, zb, at : at + 1, :] = edge
                    ends[c, x0 + x, zb, side : side + 1, :] = edge

    lower = slice(lead - 1, lead - 1 + rows)
    upper = slice(lead + 1, lead + 1 + rows)

    def paired(read, x):
        return read(x) + read((x + 1) % nx)

    def smooth_x(sums, x):
        return sums((x - 1) % nx) + sums(x)

    def keep_strain(field, x, kept, scale):
        left, right = (x - 1) % nx, (x + 1) % nx
        grad_z = [slope_z([field[c, x, zb, inner, :] for zb in blocks]) for c in range(3)]
        for zb in blocks:
            grad_x = [field[c, right, zb, inner, :] - field[c, left, zb, inner, :] for c in range(3)]
            grad_y = [field[c, x, zb, upper, :] - field[c, x, zb, lower, :] for c in range(3)]
            parts = strain_parts(grad_x, grad_y, [grad_z[c][zb] for c in range(3)])
            for i in range(6):
                kept[i, x, zb] = parts[i]
            kept[6, x, zb] = scale * strain_size(parts) if scale != 1.0 else strain_size(parts)

    for x in range(nx):
        keep_strain(vel, x, strains, 1.0)
        for c in range(3):
            fields = [paired(lambda at: vel[c, at, zb, inner, :], x) for zb in blocks]
            for zb, f in enumerate(smooth_z(fields)):
                part[c, x, zb] = f
    for c in range(3):
        rims = [smooth_z([paired(lambda at: ends[c, at, zb], x) for zb in blocks]) for x in range(nx)]
        for x in range(nx):
            for zb in blocks:
                rim = smooth_x(lambda at: rims[at][zb], x)
                filt[c, x, zb, lead - 1 : lead, :] = rim[0:1, :]
                filt[c, x, zb, lead + rows : lead + rows + 1, :] = rim[1:2, :]
                filt[c, x, zb, inner, :] = smooth_x(lambda at: part[c, at, zb], x)
    def filter_z(read, kept):
        if not on_matrix_unit:
            for x in range(nx):
                fields = [paired(lambda at: read(at, zb), x) for zb in blocks]
                for zb, f in enumerate(smooth_z(fields)):
                    part[kept, x, zb] = f
            return
        half = nx // 2
        for x0 in (0, half):
            fields = [[read((x0 + x) % nx, zb) for zb in blocks] for x in range(half + 1)]
            planes_here = [
                jnp.concatenate([f + g for f, g in zip(fields[x], fields[x + 1])], axis=1)
                for x in range(half)
            ]
            total = times_band(jnp.concatenate(planes_here, axis=0), band)
            for x in range(half):
                for zb in blocks:
                    part[kept, x0 + x, zb] = total[x * rows : (x + 1) * rows, zb * lanes : (zb + 1) * lanes]

    on_matrix_unit = nz <= 256 and rows * nx % 32 == 0 and rows % 8 == 0
    band = band_matrix(nz) if on_matrix_unit else None
    for i, (a, b) in enumerate(((0, 0), (1, 1), (2, 2), (0, 1), (0, 2), (1, 2))):
        filter_z(lambda x, zb: vel[a, x, zb, inner, :] * vel[b, x, zb, inner, :], 3 + i)
        filter_z(lambda x, zb: strains[6, x, zb] * strains[i, x, zb], 9 + i)
    for x in range(nx):
        keep_strain(filt, x, means, 0.25)

    sum_lm = sum_mm = None
    for x in range(nx):
        for zb in blocks:
            v = [filt[c, x, zb, inner, :] for c in range(3)]
            scaled = [0.0625 * f for f in v]
            size = means[6, x, zb]
            for i, (a, b) in enumerate(((0, 0), (1, 1), (2, 2), (0, 1), (0, 2), (1, 2))):
                leonard = smooth_x(lambda at: part[3 + i, at, zb], x) - v[a] * scaled[b]
                model = smooth_x(lambda at: part[9 + i, at, zb], x) - size * means[i, x, zb]
                square = model * model if i < 3 else (0.5 * model) * model
                sum_lm = leonard * model if sum_lm is None else sum_lm + leonard * model
                sum_mm = square if sum_mm is None else sum_mm + square

    coefficient = coefficient_of(
        *(jnp.sum(total, axis=1, keepdims=True) for total in (sum_lm, sum_mm)), nx * nz
    )
    for k in range(count):
        x0, zb = (k // nz_parts) * width, k % nz_parts
        for x in range(width):
            out[to[k], x] = coefficient * strains[6, x0 + x, zb]


def sweep_kernel(parity, back, velocity, tendency, eddy, reduced, factors, tree):
    count, width, rows, _ = back.shape
    length = count * rows // SEGMENTS
    slots = slots_of(back_order(count))

    def fill(rank, place):
        for x in range(width):
            eddy[x, place * rows : (place + 1) * rows, :] = back[slots[rank], x]

    by_parity(parity, count, fill)

    def row(ref, index, j):
        return ref[(*index, pl.ds(j, SEGMENTS, stride=length), slice(None))]

    planes = range(width)
    last_row = length - 1
    visc = [[1.0 + row(eddy, (x,), j) for x in planes] for j in range(length)]
    links = [[750.0 * (v + w) for v, w in zip(visc[j], visc[j + 1])] for j in range(last_row)]

    over = [jnp.ones_like(v) for v in visc[0]]
    under = [jnp.ones_like(v) for v in visc[0]]
    inverses = []
    for j in range(last_row):
        inverses.append([u / (o + e * u) for o, u, e in zip(over, under, links[j])])
        steps = [o * (1.0 / e) for o, e in zip(over, links[j])]
        under, over = (
            [u + t for u, t in zip(under, steps)],
            [(o + u) + t for o, u, t in zip(over, under, steps)],
        )
    inverses.append([u / o for o, u in zip(over, under)])

    value = first = corner = left = None
    reach = [jnp.ones_like(v) for v in visc[0]]
    for j in range(length):
        inverse = inverses[j]
        before = value
        source = [[2.0 * row(velocity, (c, x), j) + row(tendency, (c, x), j) for x in planes] for c in range(3)]
        value = [[f * r for f, r in zip(source[c], inverse)] for c in range(3)]
        if j > 0:
            carry = [e * r for e, r in zip(links[j - 1], inverse)]
            value = [[v + k * w for v, k, w in zip(value[c], carry, before[c])] for c in range(3)]
        left = [m * r for m, r in zip(reach, inverse)]
        if j == 0:
            first, corner = value, left
        else:
            first = [[f + m * v for f, m, v in zip(first[c], reach, value[c])] for c in range(3)]
            corner = [a + m * v for a, m, v in zip(corner, reach, left)]
        ratio = inverse
        if j < last_row:
            ratio = [e * r for e, r in zip(links[j], inverse)]
            reach = [m * r for m, r in zip(reach, ratio)]
        for x in planes:
            for c in range(3):
                factors[x, j, c] = value[c][x]
            factors[x, j, 3] = left[x]
            factors[x, j, 4] = ratio[x]

    def other(fields, step):
        return [pltpu.roll(f, (SEGMENTS - step) % SEGMENTS, 0) if step else f for f in fields]

    last, across, end = value, left, inverse
    seams = [750.0 * (v + w) for v, w in zip(visc[last_row], other(visc[0], 1))]
    level, step = 0, 1
    while step < SEGMENTS:
        link = other(seams, step - 1)
        first_b = [other(f, step) for f in first]
        last_b = [other(f, step) for f in last]
        corner_b, end_b, across_b = other(corner, step), other(end, step), other(across, step)
        stiff = [e / (1.0 + e * (d + a)) for e, d, a in zip(link, end, corner_b)]
        flux = [[k * (g - f) for k, g, f in zip(stiff, last[c], first_b[c])] for c in range(3)]
        from_left = [k * b for k, b in zip(stiff, across)]
        from_right = [k * b for k, b in zip(stiff, across_b)]
        for x in planes:
            for c in range(3):
                tree[x, level, c] = flux[c][x]
            tree[x, level, 3] = from_left[x]
            tree[x, level, 4] = from_right[x]
        first = [[f - b * t for f, b, t in zip(first[c], across, flux[c])] for c in range(3)]
        last = [[g + b * t for g, b, t in zip(last_b[c], across_b, flux[c])] for c in range(3)]
        corner = [a - b * k for a, b, k in zip(corner, across, from_left)]
        end = [d - b * k for d, b, k in zip(end_b, across_b, from_right)]
        across = [k * b for k, b in zip(from_left, across_b)]
        level, step = level + 1, step * 2
    for x in planes:
        rows_out = [f[x][0:1, :] for f in (*first, *last, corner, across, end, visc[0])]
        rows_out.append(visc[last_row][x][SEGMENTS - 1 :, :])
        for i, v in enumerate(rows_out):
            reduced[i * width + x : i * width + x + 1, :] = v


def spread_kernel(factors, tree, velocity, eddy, particular, response, eddy_out, sent):
    write = pltpu.make_async_copy(eddy, eddy_out, sent)
    write.start()
    width, length = factors.shape[:2]
    levels = tree.shape[1]
    sublane = lax.broadcasted_iota(jnp.int32, (SEGMENTS, LANES), 0)
    one, zero = (jnp.full((SEGMENTS, LANES), v, jnp.float32) for v in (1.0, 0.0))
    sides = [(c, zero, zero) for c in range(3)] + [(None, one, zero), (None, zero, one)]
    lefts = [[side[1]] * width for side in sides]
    rights = [[side[2]] * width for side in sides]
    for level in range(levels - 1, -1, -1):
        step = 2**level
        second = lax.rem(sublane, 2 * step) == step
        for n, (c, _, _) in enumerate(sides):
            for x in range(width):
                left, right = lefts[n][x], rights[n][x]
                through = tree[x, level, 3] * left - tree[x, level, 4] * right
                if c is not None:
                    through = tree[x, level, c] + through
                lefts[n][x] = jnp.where(second, pltpu.roll(through, step, 0), left)
                rights[n][x] = jnp.where(second, pltpu.roll(right, step, 0), -through)
    values = rights
    for j in range(length - 1, -1, -1):
        rows = pl.ds(j, SEGMENTS, stride=length)
        for n, (c, _, _) in enumerate(sides):
            for x in range(width):
                value = factors[x, j, 3] * lefts[n][x] + factors[x, j, 4] * values[n][x]
                if c is not None:
                    value = factors[x, j, c] + value
                    particular[c, x, rows, :] = value - velocity[c, x, rows, :]
                else:
                    response[n - 3, x, rows, :] = value
                values[n][x] = value
    write.wait()


def sources_of(step, count):
    return [(i - step) % count for i in range(count)]


def exchange_order(count):
    return range(count - 1, 0, -1)


def spread_kernel(factors, tree, velocity, eddy, particular, response, eddy_out, sent):
    write = pltpu.make_async_copy(eddy, eddy_out, sent)
    write.start()
    width, length = factors.shape[:2]
    levels = tree.shape[1]
    sublane = lax.broadcasted_iota(jnp.int32, (SEGMENTS, LANES), 0)
    one, zero = (jnp.full((SEGMENTS, LANES), v, jnp.float32) for v in (1.0, 0.0))
    sides = [(c, zero, zero) for c in range(3)] + [(None, one, zero), (None, zero, one)]
    lefts = [[side[1]] * width for side in sides]
    rights = [[side[2]] * width for side in sides]
    for level in range(levels - 1, -1, -1):
        step = 2**level
        second = lax.rem(sublane, 2 * step) == step
        for n, (c, _, _) in enumerate(sides):
            for x in range(width):
                left, right = lefts[n][x], rights[n][x]
                through = tree[x, level, 3] * left - tree[x, level, 4] * right
                if c is not None:
                    through = tree[x, level, c] + through
                lefts[n][x] = jnp.where(second, pltpu.roll(through, step, 0), left)
                rights[n][x] = jnp.where(second, pltpu.roll(right, step, 0), -through)
    values = rights
    for j in range(length - 1, -1, -1):
        rows = pl.ds(j, SEGMENTS, stride=length)
        for n, (c, _, _) in enumerate(sides):
            for x in range(width):
                value = factors[x, j, 3] * lefts[n][x] + factors[x, j, 4] * values[n][x]
                if c is not None:
                    value = factors[x, j, c] + value
                    particular[c, x, rows, :] = value - velocity[c, x, rows, :]
                else:
                    response[n - 3, x, rows, :] = value
                values[n][x] = value
    write.wait()


def partner(i, step, count):
    if count & (count - 1) == 0:
        return i ^ step
    return (i - step + count) % count


def finish_kernel(devices, position, particular, response, *rest):
    reduced, (result, gathered, fluxes, out, sent) = rest[:devices], rest[devices:]
    width = particular.shape[1]
    here = position[0]
    for step, ref in zip([0, *exchange_order(devices)], reduced):
        source = sum(jnp.where(here == i, s, 0) for i, s in enumerate(sources_of(step, devices)))
        gathered[source] = ref[...]

    def part(device, i):
        return gathered[device, i * width : (i + 1) * width, :]

    pivots, sources = [], []
    for i in range(devices + 1):
        visc = [part(i - 1, 10)] if i > 0 else []
        total = [part(i - 1, 8)] if i > 0 else []
        source = [part(i - 1, 3 + c) for c in range(3)] if i > 0 else [0.0] * 3
        if i < devices:
            visc.append(part(i, 9))
            total.append(part(i, 6))
            source = [s - part(i, c) for c, s in enumerate(source)]
        pivots.append(sum(total) + 1.0 / (750.0 * sum(visc)))
        sources.append(source)
    across = [part(i, 7) for i in range(devices)]
    minors = [jnp.ones_like(pivots[0]), pivots[0]]
    for i in range(1, devices + 1):
        minors.append(pivots[i] * minors[i] - (across[i - 1] * across[i - 1]) * minors[i - 1])
    inverses = [minors[i] / minors[i + 1] for i in range(devices + 1)]
    ratios = [b * r for b, r in zip(across, inverses)]
    for i in range(1, devices + 1):
        sources[i] = [s + ratios[i - 1] * t for s, t in zip(sources[i], sources[i - 1])]
    for i in range(devices, -1, -1):
        flux_here = [inverses[i] * s for s in sources[i]]
        flux = flux_here if i == devices else [f + ratios[i] * g for f, g in zip(flux_here, flux)]
        for c in range(3):
            fluxes[i, c * width : (c + 1) * width, :] = flux[c]

    writes = []
    for c in range(3):
        for x in range(width):
            r = c * width + x
            left, right = fluxes[here, r : r + 1, :], fluxes[here + 1, r : r + 1, :]
            out[c, x] = particular[c, x] + (response[0, x] * left - response[1, x] * right)
            writes.append(pltpu.make_async_copy(out.at[c, x], result.at[c, x], sent.at[r]))
            writes[-1].start()
    for write in writes:
        write.wait()


def in_vmem(count):
    return [pl.BlockSpec(memory_space=pltpu.VMEM)] * count


def in_hbm(count):
    return [pl.BlockSpec(memory_space=pltpu.HBM)] * count


def in_smem(count):
    return [pl.BlockSpec(memory_space=pltpu.SMEM)] * count


def params():
    return pltpu.CompilerParams(vmem_limit_bytes=VMEM_BYTES)


def swap_chunks(chunks, order):
    return lax.all_to_all(
        chunks, ("gx", "gz"), split_axis=0, concat_axis=0, tiled=True, axis_index_groups=[order]
    )


def body(velocity, tendency):
    _, width, cells, lanes = velocity.shape
    nz_parts = lax.axis_size("gz")
    count = lax.axis_size("gx") * nz_parts
    walls = lax.axis_size("gy")
    rows = cells // count
    nx = lax.axis_size("gx") * width
    padded = 16 + aligned(rows)
    f32 = jnp.float32

    planes = 3 * width
    depth = aligned(planes * rows + 2 * aligned(planes))
    position = lax.axis_index("gy").astype(jnp.int32).reshape(1)
    parity = lax.rem(position, 2)
    chunks = pl.pallas_call(
        functools.partial(pack_kernel, rows),
        out_shape=jax.ShapeDtypeStruct((count, depth, lanes), f32),
        in_specs=in_smem(1) + in_vmem(1),
        out_specs=pl.BlockSpec(memory_space=pltpu.VMEM),
        compiler_params=params(),
        name="pack",
    )(parity, velocity)
    recv = swap_chunks(chunks, out_order(count))
    slot = lax.slice_in_dim(recv, planes * rows, planes * rows + aligned(planes), axis=1)
    swapped = lax.ppermute(slot, ("gy", "gx", "gz"), swap_pairs(walls, count))
    rank = lax.axis_index(("gx", "gz")).astype(jnp.int32).reshape(1)
    chunk_shape = jax.ShapeDtypeStruct((count, width, rows, lanes), f32)
    cells_here = nx * nz_parts * rows * lanes
    provisional = pl.pallas_call(
        functools.partial(germano_kernel, nz_parts, width, rows),
        out_shape=chunk_shape,
        in_specs=in_smem(2) + in_vmem(1),
        out_specs=pl.BlockSpec(memory_space=pltpu.VMEM),
        scratch_shapes=[
            pltpu.VMEM((3, nx, nz_parts, padded, lanes), f32),
            pltpu.VMEM((3, nx, nz_parts, padded, lanes), f32),
            pltpu.VMEM((3, nx, nz_parts, 8, lanes), f32),
            pltpu.VMEM((7, nx, nz_parts, rows, lanes), f32),
            pltpu.VMEM((7, nx, nz_parts, rows, lanes), f32),
            pltpu.VMEM((15, nx, nz_parts, rows, lanes), f32),
        ],
        compiler_params=params(),
        cost_estimate=pl.CostEstimate(
            flops=300 * cells_here, bytes_accessed=16 * cells_here, transcendentals=2 * cells_here
        ),
        name="germano",
    )(rank, parity, recv)
    eddy_chunks = pl.pallas_call(
        functools.partial(edge_kernel, nz_parts, width, rows, walls),
        out_shape=chunk_shape,
        in_specs=in_smem(2) + in_vmem(3),
        out_specs=pl.BlockSpec(memory_space=pltpu.VMEM),
        scratch_shapes=[pltpu.VMEM((3, 3, nx, nz_parts * lanes), f32)],
        input_output_aliases={4: 0},
        compiler_params=params(),
        name="edge",
    )(rank, position, recv, swapped, provisional)
    back = swap_chunks(eddy_chunks, back_order(count))

    length = cells // SEGMENTS
    levels = SEGMENTS.bit_length() - 1
    packed = aligned(11 * width)
    eddy_here, reduced, factors, tree = pl.pallas_call(
        sweep_kernel,
        out_shape=(
            jax.ShapeDtypeStruct((width, cells, lanes), f32),
            jax.ShapeDtypeStruct((packed, lanes), f32),
            jax.ShapeDtypeStruct((width, length, 5, SEGMENTS, lanes), f32),
            jax.ShapeDtypeStruct((width, levels, 5, SEGMENTS, lanes), f32),
        ),
        in_specs=in_smem(1) + in_vmem(3),
        out_specs=tuple(in_vmem(4)),
        compiler_params=params(),
        name="sweep",
    )(parity, back, velocity, tendency)

    others = [
        lax.ppermute(reduced, "gy", [(s, i) for i, s in enumerate(sources_of(step, walls))])
        for step in exchange_order(walls)
    ]
    particular, response, eddy = pl.pallas_call(
        spread_kernel,
        out_shape=(
            jax.ShapeDtypeStruct(velocity.shape, f32),
            jax.ShapeDtypeStruct((2, *velocity.shape[1:]), f32),
            jax.ShapeDtypeStruct(eddy_here.shape, f32),
        ),
        in_specs=in_vmem(4),
        out_specs=tuple(in_vmem(2) + in_hbm(1)),
        scratch_shapes=[pltpu.SemaphoreType.DMA],
        compiler_params=params(),
        cost_estimate=pl.CostEstimate(
            flops=20 * velocity.size, bytes_accessed=16 * velocity.size, transcendentals=0
        ),
        name="spread",
    )(factors, tree, velocity, eddy_here)
    new_velocity = pl.pallas_call(
        functools.partial(finish_kernel, walls),
        out_shape=jax.ShapeDtypeStruct(velocity.shape, f32),
        in_specs=in_smem(1) + in_vmem(2 + walls),
        out_specs=in_hbm(1)[0],
        scratch_shapes=[
            pltpu.VMEM((walls, packed, lanes), f32),
            pltpu.VMEM((walls + 1, aligned(3 * width), lanes), f32),
            pltpu.VMEM(velocity.shape, f32),
            pltpu.SemaphoreType.DMA((planes,)),
        ],
        compiler_params=params(),
        name="finish",
    )(position, particular, response, reduced, *others)
    return (new_velocity, eddy)


def solution(mesh):
    return jax.shard_map(
        body,
        mesh=mesh,
        in_specs=(P(None, "gx", "gy", "gz"), P(None, "gx", "gy", "gz")),
        out_specs=(P(None, "gx", "gy", "gz"), P("gx", "gy", "gz")),
        check_vma=False,
    )
```

```python
import functools

import jax
import jax.numpy as jnp
from jax import lax
from jax.experimental import pallas as pl
from jax.experimental.pallas import tpu as pltpu
from jax.sharding import PartitionSpec as P

LANES = 128
SEGMENTS = 8
VMEM_BYTES = 24 * 2**20


def strain_parts(grad_x, grad_y, grad_z):
    return (
        grad_x[0],
        grad_y[1],
        grad_z[2],
        grad_y[0] + grad_x[1],
        grad_z[0] + grad_x[2],
        grad_z[1] + grad_y[2],
    )


def strain_size(parts):
    diagonal = parts[0] * parts[0] + parts[1] * parts[1] + parts[2] * parts[2]
    mixed = parts[3] * parts[3] + parts[4] * parts[4] + parts[5] * parts[5]
    return jnp.sqrt(0.5 * diagonal + 0.25 * mixed)


def beside(blocks):
    count = len(blocks)
    lanes = blocks[0].shape[1]
    down = [pltpu.roll(f, 1, 1) for f in blocks]
    up = [pltpu.roll(f, lanes - 1, 1) for f in blocks]
    if count > 1:
        lane = lax.broadcasted_iota(jnp.int32, blocks[0].shape, 1)
        first, last = lane == 0, lane == lanes - 1
        down, up = (
            [jnp.where(first, down[i - 1], down[i]) for i in range(count)],
            [jnp.where(last, up[(i + 1) % count], up[i]) for i in range(count)],
        )
    return down, up


def slope_z(blocks):
    down, up = beside(blocks)
    return [u - d for u, d in zip(up, down)]


def smooth_z(blocks):
    down, up = beside(blocks)
    return [(u + d) + 2.0 * f for f, u, d in zip(blocks, up, down)]


def band_matrix(n):
    shape = (n, n)
    apart = lax.broadcasted_iota(jnp.int32, shape, 0) - lax.broadcasted_iota(jnp.int32, shape, 1)
    apart = jnp.abs(apart)
    near = jnp.logical_or(apart == 1, apart == n - 1)
    return jnp.where(apart == 0, 2.0, jnp.where(near, 1.0, 0.0)).astype(jnp.bfloat16)


def times_band(f, band):
    total = None
    for i in range(3):
        piece = f.astype(jnp.bfloat16)
        product = jnp.dot(piece, band, preferred_element_type=jnp.float32)
        total = product if total is None else total + product
        if i < 2:
            f = f - piece.astype(jnp.float32)
    return total


def products(v):
    return (v[0] * v[0], v[1] * v[1], v[2] * v[2], v[0] * v[1], v[0] * v[2], v[1] * v[2])


def outer_ranks(count):
    return (count - 3, count - 1)


def places(parity, count):
    outer = outer_ranks(count)
    inner = iter(range(1, count - 1))
    return [
        (0 if outer[parity] == rank else count - 1) if rank in outer else next(inner)
        for rank in range(count)
    ]


def swap_pairs(walls, count):
    odd, even = outer_ranks(count)
    partners = {}

    def join(a, b):
        partners[a], partners[b] = b, a

    for core in range(0, count, 2):
        here = (core, core + 1)
        if odd in here or even in here:
            first = 1 if odd in here else 0
            for wall in range(first, walls - 1, 2):
                for rank in here:
                    join((wall, rank), (wall + 1, rank))
        for wall in range(walls):
            if (wall, core) not in partners:
                join((wall, core), (wall, core + 1))
    return [
        (wall * count + rank, to[0] * count + to[1])
        for wall in range(walls)
        for rank in range(count)
        for to in [partners.get((wall, rank), (wall, rank))]
    ]


def ring_of(count):
    return [0, *range(1, count, 2), *range(count - 2 + count % 2, 0, -2)]


def by_core(chips):
    return [2 * chip + 1 for chip in chips] + [2 * chip for chip in chips]


def out_order(count):
    return by_core(ring_of(count // 2))


def back_order(count):
    return by_core(range(count // 2 - 1, -1, -1))


def slots_of(order):
    return [order.index(r) for r in range(len(order))]


def by_parity(parity, count, fill):
    outer = outer_ranks(count)
    for rank, place in enumerate(places(0, count)):
        if rank not in outer:
            fill(rank, place)
    for turn in range(2):

        @pl.when(parity[0] == turn)
        def _():
            for rank in outer:
                fill(rank, places(turn, count)[rank])


def aligned(n):
    return -(-n // 8) * 8


def pack_kernel(rows, parity, velocity, out):
    _, width, cells, _ = velocity.shape
    count, depth, lanes = out.shape
    planes = 3 * width
    slots = planes * rows

    slot_of = slots_of(out_order(count))

    def fill(rank, place):
        rank = slot_of[rank]
        first = place * rows
        beside = [first - 1, first + rows]
        if place == 0:
            beside = [first, first + rows]
        if place == count - 1:
            beside = [first + rows - 1, first - 1]
        for i in range(planes):
            c, x = divmod(i, width)
            out[rank, i * rows : (i + 1) * rows, :] = velocity[c, x, first : first + rows, :]
            for slot, row in enumerate(beside):
                at = slots + slot * aligned(planes) + i
                out[rank, at : at + 1, :] = velocity[c, x, row : row + 1, :]

    by_parity(parity, count, fill)
    blank = aligned(planes) - planes
    for rank in range(count):
        for slot in range(2):
            at = slots + slot * aligned(planes) + planes
            out[rank, at : at + blank, :] = jnp.zeros((blank, lanes), jnp.float32)
        at = slots + 2 * aligned(planes)
        if at < depth:
            out[rank, at:, :] = jnp.zeros((depth - at, lanes), jnp.float32)


def outer_sides(rank, parity, count):
    outer = outer_ranks(count)
    even = parity[0] == 0
    bottom = rank[0] == jnp.where(even, outer[0], outer[1])
    top = rank[0] == jnp.where(even, outer[1], outer[0])
    return bottom, top


def edge_kernel(nz_parts, width, rows, walls, rank, position, recv, swapped, given, out, vel):
    count, _, lanes = recv.shape
    planes = 3 * width
    nx = (count // nz_parts) * width
    nz = nz_parts * lanes
    bottom, top = outer_sides(rank, [lax.rem(position[0], 2)], count)
    came, to = slots_of(out_order(count)), slots_of(back_order(count))
    at_seam = jnp.logical_or(
        jnp.logical_and(bottom, position[0] > 0), jnp.logical_and(top, position[0] < walls - 1)
    )

    def rows_of(k, i):
        k = came[k]
        first = i * rows
        own = [recv[k, first + j : first + j + 1, :] for j in (0, 1, rows - 2, rows - 1)]
        far = swapped[k, i : i + 1, :]
        return (
            jnp.where(bottom, far, own[2]),
            jnp.where(bottom, own[0], own[3]),
            jnp.where(bottom, own[1], far),
        )

    def roll_x(f, shift):
        return pltpu.roll(f, shift % nx, 0)

    def roll_z(f, shift):
        return pltpu.roll(f, shift % nz, 1)

    def smooth_x(f):
        return (roll_x(f, 1) + roll_x(f, -1)) + 2.0 * f

    def smooth(f):
        f = smooth_x(f)
        return (roll_z(f, 1) + roll_z(f, -1)) + 2.0 * f

    def slopes(below, centre, above):
        return strain_parts(
            [roll_x(f, -1) - roll_x(f, 1) for f in centre],
            [a - b for a, b in zip(above, below)],
            [roll_z(f, -1) - roll_z(f, 1) for f in centre],
        )

    @pl.when(at_seam)
    def _():
        for k in range(count):
            x0, zb = (k // nz_parts) * width, k % nz_parts
            for i in range(planes):
                c, x = divmod(i, width)
                for j, row in enumerate(rows_of(k, i)):
                    vel[j, c, x0 + x : x0 + x + 1, zb * lanes : (zb + 1) * lanes] = row
        u = [[vel[j, c] for c in range(3)] for j in range(3)]
        v = [[smooth(f) for f in row] for row in u]
        strain = slopes(*u)
        size = strain_size(strain)
        mean_strain = slopes(*v)
        mean_size = 0.25 * strain_size(mean_strain)
        scaled = [0.0625 * f for f in v[1]]
        pairs = [v[1][i] * scaled[j] for i, j in ((0, 0), (1, 1), (2, 2), (0, 1), (0, 2), (1, 2))]
        leonard = [smooth(p) - q for p, q in zip(products(u[1]), pairs)]
        model = [smooth(size * s) - mean_size * f for s, f in zip(strain, mean_strain)]
        lm, mm = contracted(leonard, model)
        coefficient = coefficient_of(
            *(jnp.sum(f, axis=(0, 1), keepdims=True) for f in (lm, mm)), nx * nz
        )
        eddy = coefficient * size

        def put(at):
            for k in range(count):
                x0, zb = (k // nz_parts) * width, k % nz_parts
                for x in range(width):
                    out[to[k], x, at : at + 1, :] = eddy[x0 + x : x0 + x + 1, zb * lanes : (zb + 1) * lanes]

        pl.when(bottom)(lambda: put(0))
        pl.when(top)(lambda: put(rows - 1))


def contracted(leonard, model):
    lm = mm = None
    for i in range(6):
        square = model[i] * model[i] if i < 3 else (0.5 * model[i]) * model[i]
        product = leonard[i] * model[i]
        lm = product if lm is None else lm + product
        mm = square if mm is None else mm + square
    return lm, mm


def coefficient_of(plane_lm, plane_mm, cells):
    scale = 1.0 / (256.0 * cells)
    return jnp.maximum(plane_lm * scale / (plane_mm * scale + 1e-06), 0.0)


def germano_kernel(nz_parts, width, rows, walls, rank, position, recv, out, vel, filt, ends, strains, means, part):
    count, _, lanes = recv.shape
    planes = 3 * width
    bottom, top = outer_sides(rank, [lax.rem(position[0], 2)], count)
    floor = jnp.logical_and(bottom, position[0] == 0)
    ceiling = jnp.logical_and(top, position[0] == walls - 1)
    came, to = slots_of(out_order(count)), slots_of(back_order(count))
    nx = (count // nz_parts) * width
    nz = nz_parts * lanes
    blocks = range(nz_parts)
    lead = 8
    inner = slice(lead, lead + rows)
    for k in range(count):
        x0, zb = (k // nz_parts) * width, k % nz_parts
        for c in range(3):
            for x in range(width):
                i = c * width + x
                vel[c, x0 + x, zb, inner, :] = recv[came[k], i * rows : (i + 1) * rows, :]
                slots = planes * rows + i
                near = recv[came[k], slots : slots + 1, :]
                slots += aligned(planes)
                other = recv[came[k], slots : slots + 1, :]
                below = jnp.where(floor, 0.0, jnp.where(top, other, near))
                above = jnp.where(ceiling, 0.0, other)
                for side, (edge, at) in enumerate(((below, lead - 1), (above, lead + rows))):
                    vel[c, x0 + x, zb, at : at + 1, :] = edge
                    ends[c, x0 + x, zb, side : side + 1, :] = edge

    lower = slice(lead - 1, lead - 1 + rows)
    upper = slice(lead + 1, lead + 1 + rows)

    def paired(read, x):
        return read(x) + read((x + 1) % nx)

    def smooth_x(sums, x):
        return sums((x - 1) % nx) + sums(x)

    def keep_strain(field, x, kept, scale):
        left, right = (x - 1) % nx, (x + 1) % nx
        grad_z = [slope_z([field[c, x, zb, inner, :] for zb in blocks]) for c in range(3)]
        for zb in blocks:
            grad_x = [field[c, right, zb, inner, :] - field[c, left, zb, inner, :] for c in range(3)]
            grad_y = [field[c, x, zb, upper, :] - field[c, x, zb, lower, :] for c in range(3)]
            parts = strain_parts(grad_x, grad_y, [grad_z[c][zb] for c in range(3)])
            for i in range(6):
                kept[i, x, zb] = parts[i]
            kept[6, x, zb] = scale * strain_size(parts) if scale != 1.0 else strain_size(parts)

    for x in range(nx):
        keep_strain(vel, x, strains, 1.0)
        for c in range(3):
            fields = [paired(lambda at: vel[c, at, zb, inner, :], x) for zb in blocks]
            for zb, f in enumerate(smooth_z(fields)):
                part[c, x, zb] = f
    for c in range(3):
        rims = [smooth_z([paired(lambda at: ends[c, at, zb], x) for zb in blocks]) for x in range(nx)]
        for x in range(nx):
            for zb in blocks:
                rim = smooth_x(lambda at: rims[at][zb], x)
                filt[c, x, zb, lead - 1 : lead, :] = rim[0:1, :]
                filt[c, x, zb, lead + rows : lead + rows + 1, :] = rim[1:2, :]
                filt[c, x, zb, inner, :] = smooth_x(lambda at: part[c, at, zb], x)
    def filter_z(read, kept):
        if not on_matrix_unit:
            for x in range(nx):
                fields = [paired(lambda at: read(at, zb), x) for zb in blocks]
                for zb, f in enumerate(smooth_z(fields)):
                    part[kept, x, zb] = f
            return
        half = nx // 2
        for x0 in (0, half):
            fields = [[read((x0 + x) % nx, zb) for zb in blocks] for x in range(half + 1)]
            planes_here = [
                jnp.concatenate([f + g for f, g in zip(fields[x], fields[x + 1])], axis=1)
                for x in range(half)
            ]
            total = times_band(jnp.concatenate(planes_here, axis=0), band)
            for x in range(half):
                for zb in blocks:
                    part[kept, x0 + x, zb] = total[x * rows : (x + 1) * rows, zb * lanes : (zb + 1) * lanes]

    on_matrix_unit = nz <= 256 and rows * nx % 32 == 0 and rows % 8 == 0
    band = band_matrix(nz) if on_matrix_unit else None
    for i, (a, b) in enumerate(((0, 0), (1, 1), (2, 2), (0, 1), (0, 2), (1, 2))):
        filter_z(lambda x, zb: vel[a, x, zb, inner, :] * vel[b, x, zb, inner, :], 3 + i)
        filter_z(lambda x, zb: strains[6, x, zb] * strains[i, x, zb], 9 + i)
    for x in range(nx):
        keep_strain(filt, x, means, 0.25)

    sum_lm = sum_mm = None
    for x in range(nx):
        for zb in blocks:
            v = [filt[c, x, zb, inner, :] for c in range(3)]
            scaled = [0.0625 * f for f in v]
            size = means[6, x, zb]
            for i, (a, b) in enumerate(((0, 0), (1, 1), (2, 2), (0, 1), (0, 2), (1, 2))):
                leonard = smooth_x(lambda at: part[3 + i, at, zb], x) - v[a] * scaled[b]
                model = smooth_x(lambda at: part[9 + i, at, zb], x) - size * means[i, x, zb]
                square = model * model if i < 3 else (0.5 * model) * model
                sum_lm = leonard * model if sum_lm is None else sum_lm + leonard * model
                sum_mm = square if sum_mm is None else sum_mm + square

    coefficient = coefficient_of(
        *(jnp.sum(total, axis=1, keepdims=True) for total in (sum_lm, sum_mm)), nx * nz
    )
    for k in range(count):
        x0, zb = (k // nz_parts) * width, k % nz_parts
        for x in range(width):
            out[to[k], x] = coefficient * strains[6, x0 + x, zb]


def sweep_kernel(parity, back, velocity, tendency, eddy, reduced, factors, tree):
    count, width, rows, _ = back.shape
    length = count * rows // SEGMENTS
    slots = slots_of(back_order(count))

    def fill(rank, place):
        for x in range(width):
            eddy[x, place * rows : (place + 1) * rows, :] = back[slots[rank], x]

    by_parity(parity, count, fill)

    def row(ref, index, j):
        return ref[(*index, pl.ds(j, SEGMENTS, stride=length), slice(None))]

    planes = range(width)
    last_row = length - 1
    visc = [[1.0 + row(eddy, (x,), j) for x in planes] for j in range(length)]
    links = [[750.0 * (v + w) for v, w in zip(visc[j], visc[j + 1])] for j in range(last_row)]

    over = [jnp.ones_like(v) for v in visc[0]]
    under = [jnp.ones_like(v) for v in visc[0]]
    inverses = []
    for j in range(last_row):
        inverses.append([u / (o + e * u) for o, u, e in zip(over, under, links[j])])
        steps = [o * (1.0 / e) for o, e in zip(over, links[j])]
        under, over = (
            [u + t for u, t in zip(under, steps)],
            [(o + u) + t for o, u, t in zip(over, under, steps)],
        )
    inverses.append([u / o for o, u in zip(over, under)])

    value = first = corner = left = None
    reach = [jnp.ones_like(v) for v in visc[0]]
    for j in range(length):
        inverse = inverses[j]
        before = value
        source = [[2.0 * row(velocity, (c, x), j) + row(tendency, (c, x), j) for x in planes] for c in range(3)]
        value = [[f * r for f, r in zip(source[c], inverse)] for c in range(3)]
        if j > 0:
            carry = [e * r for e, r in zip(links[j - 1], inverse)]
            value = [[v + k * w for v, k, w in zip(value[c], carry, before[c])] for c in range(3)]
        left = [m * r for m, r in zip(reach, inverse)]
        if j == 0:
            first, corner = value, left
        else:
            first = [[f + m * v for f, m, v in zip(first[c], reach, value[c])] for c in range(3)]
            corner = [a + m * v for a, m, v in zip(corner, reach, left)]
        ratio = inverse
        if j < last_row:
            ratio = [e * r for e, r in zip(links[j], inverse)]
            reach = [m * r for m, r in zip(reach, ratio)]
        for x in planes:
            for c in range(3):
                factors[x, j, c] = value[c][x]
            factors[x, j, 3] = left[x]
            factors[x, j, 4] = ratio[x]

    def other(fields, step):
        return [pltpu.roll(f, (SEGMENTS - step) % SEGMENTS, 0) if step else f for f in fields]

    last, across, end = value, left, inverse
    seams = [750.0 * (v + w) for v, w in zip(visc[last_row], other(visc[0], 1))]
    level, step = 0, 1
    while step < SEGMENTS:
        link = other(seams, step - 1)
        first_b = [other(f, step) for f in first]
        last_b = [other(f, step) for f in last]
        corner_b, end_b, across_b = other(corner, step), other(end, step), other(across, step)
        stiff = [e / (1.0 + e * (d + a)) for e, d, a in zip(link, end, corner_b)]
        flux = [[k * (g - f) for k, g, f in zip(stiff, last[c], first_b[c])] for c in range(3)]
        from_left = [k * b for k, b in zip(stiff, across)]
        from_right = [k * b for k, b in zip(stiff, across_b)]
        for x in planes:
            for c in range(3):
                tree[x, level, c] = flux[c][x]
            tree[x, level, 3] = from_left[x]
            tree[x, level, 4] = from_right[x]
        first = [[f - b * t for f, b, t in zip(first[c], across, flux[c])] for c in range(3)]
        last = [[g + b * t for g, b, t in zip(last_b[c], across_b, flux[c])] for c in range(3)]
        corner = [a - b * k for a, b, k in zip(corner, across, from_left)]
        end = [d - b * k for d, b, k in zip(end_b, across_b, from_right)]
        across = [k * b for k, b in zip(from_left, across_b)]
        level, step = level + 1, step * 2
    for x in planes:
        rows_out = [f[x][0:1, :] for f in (*first, *last, corner, across, end, visc[0])]
        rows_out.append(visc[last_row][x][SEGMENTS - 1 :, :])
        for i, v in enumerate(rows_out):
            reduced[i * width + x : i * width + x + 1, :] = v


def spread_kernel(factors, tree, velocity, eddy, particular, response, eddy_out, sent):
    write = pltpu.make_async_copy(eddy, eddy_out, sent)
    write.start()
    width, length = factors.shape[:2]
    levels = tree.shape[1]
    sublane = lax.broadcasted_iota(jnp.int32, (SEGMENTS, LANES), 0)
    one, zero = (jnp.full((SEGMENTS, LANES), v, jnp.float32) for v in (1.0, 0.0))
    sides = [(c, zero, zero) for c in range(3)] + [(None, one, zero), (None, zero, one)]
    lefts = [[side[1]] * width for side in sides]
    rights = [[side[2]] * width for side in sides]
    for level in range(levels - 1, -1, -1):
        step = 2**level
        second = lax.rem(sublane, 2 * step) == step
        for n, (c, _, _) in enumerate(sides):
            for x in range(width):
                left, right = lefts[n][x], rights[n][x]
                through = tree[x, level, 3] * left - tree[x, level, 4] * right
                if c is not None:
                    through = tree[x, level, c] + through
                lefts[n][x] = jnp.where(second, pltpu.roll(through, step, 0), left)
                rights[n][x] = jnp.where(second, pltpu.roll(right, step, 0), -through)
    values = rights
    for j in range(length - 1, -1, -1):
        rows = pl.ds(j, SEGMENTS, stride=length)
        for n, (c, _, _) in enumerate(sides):
            for x in range(width):
                value = factors[x, j, 3] * lefts[n][x] + factors[x, j, 4] * values[n][x]
                if c is not None:
                    value = factors[x, j, c] + value
                    particular[c, x, rows, :] = value - velocity[c, x, rows, :]
                else:
                    response[n - 3, x, rows, :] = value
                values[n][x] = value
    write.wait()


def sources_of(step, count):
    return [(i - step) % count for i in range(count)]


def exchange_order(count):
    return range(count - 1, 0, -1)


def spread_kernel(factors, tree, velocity, eddy, particular, response, eddy_out, sent):
    write = pltpu.make_async_copy(eddy, eddy_out, sent)
    write.start()
    width, length = factors.shape[:2]
    levels = tree.shape[1]
    sublane = lax.broadcasted_iota(jnp.int32, (SEGMENTS, LANES), 0)
    one, zero = (jnp.full((SEGMENTS, LANES), v, jnp.float32) for v in (1.0, 0.0))
    sides = [(c, zero, zero) for c in range(3)] + [(None, one, zero), (None, zero, one)]
    lefts = [[side[1]] * width for side in sides]
    rights = [[side[2]] * width for side in sides]
    for level in range(levels - 1, -1, -1):
        step = 2**level
        second = lax.rem(sublane, 2 * step) == step
        for n, (c, _, _) in enumerate(sides):
            for x in range(width):
                left, right = lefts[n][x], rights[n][x]
                through = tree[x, level, 3] * left - tree[x, level, 4] * right
                if c is not None:
                    through = tree[x, level, c] + through
                lefts[n][x] = jnp.where(second, pltpu.roll(through, step, 0), left)
                rights[n][x] = jnp.where(second, pltpu.roll(right, step, 0), -through)
    values = rights
    for j in range(length - 1, -1, -1):
        rows = pl.ds(j, SEGMENTS, stride=length)
        for n, (c, _, _) in enumerate(sides):
            for x in range(width):
                value = factors[x, j, 3] * lefts[n][x] + factors[x, j, 4] * values[n][x]
                if c is not None:
                    value = factors[x, j, c] + value
                    particular[c, x, rows, :] = value - velocity[c, x, rows, :]
                else:
                    response[n - 3, x, rows, :] = value
                values[n][x] = value
    write.wait()


def partner(i, step, count):
    if count & (count - 1) == 0:
        return i ^ step
    return (i - step + count) % count


def finish_kernel(devices, position, particular, response, *rest):
    reduced, (result, gathered, fluxes, out, sent) = rest[:devices], rest[devices:]
    width = particular.shape[1]
    here = position[0]
    for step, ref in zip([0, *exchange_order(devices)], reduced):
        source = sum(jnp.where(here == i, s, 0) for i, s in enumerate(sources_of(step, devices)))
        gathered[source] = ref[...]

    def part(device, i):
        return gathered[device, i * width : (i + 1) * width, :]

    pivots, sources = [], []
    for i in range(devices + 1):
        visc = [part(i - 1, 10)] if i > 0 else []
        total = [part(i - 1, 8)] if i > 0 else []
        source = [part(i - 1, 3 + c) for c in range(3)] if i > 0 else [0.0] * 3
        if i < devices:
            visc.append(part(i, 9))
            total.append(part(i, 6))
            source = [s - part(i, c) for c, s in enumerate(source)]
        pivots.append(sum(total) + 1.0 / (750.0 * sum(visc)))
        sources.append(source)
    across = [part(i, 7) for i in range(devices)]
    minors = [jnp.ones_like(pivots[0]), pivots[0]]
    for i in range(1, devices + 1):
        minors.append(pivots[i] * minors[i] - (across[i - 1] * across[i - 1]) * minors[i - 1])
    inverses = [minors[i] / minors[i + 1] for i in range(devices + 1)]
    ratios = [b * r for b, r in zip(across, inverses)]
    for i in range(1, devices + 1):
        sources[i] = [s + ratios[i - 1] * t for s, t in zip(sources[i], sources[i - 1])]
    for i in range(devices, -1, -1):
        flux_here = [inverses[i] * s for s in sources[i]]
        flux = flux_here if i == devices else [f + ratios[i] * g for f, g in zip(flux_here, flux)]
        for c in range(3):
            fluxes[i, c * width : (c + 1) * width, :] = flux[c]

    writes = []
    for c in range(3):
        for x in range(width):
            r = c * width + x
            left, right = fluxes[here, r : r + 1, :], fluxes[here + 1, r : r + 1, :]
            out[c, x] = particular[c, x] + (response[0, x] * left - response[1, x] * right)
            writes.append(pltpu.make_async_copy(out.at[c, x], result.at[c, x], sent.at[r]))
            writes[-1].start()
    for write in writes:
        write.wait()


def in_vmem(count):
    return [pl.BlockSpec(memory_space=pltpu.VMEM)] * count


def in_hbm(count):
    return [pl.BlockSpec(memory_space=pltpu.HBM)] * count


def in_smem(count):
    return [pl.BlockSpec(memory_space=pltpu.SMEM)] * count


def params():
    return pltpu.CompilerParams(vmem_limit_bytes=VMEM_BYTES)


def swap_chunks(chunks, order):
    return lax.all_to_all(
        chunks, ("gx", "gz"), split_axis=0, concat_axis=0, tiled=True, axis_index_groups=[order]
    )


def body(velocity, tendency):
    _, width, cells, lanes = velocity.shape
    nz_parts = lax.axis_size("gz")
    count = lax.axis_size("gx") * nz_parts
    walls = lax.axis_size("gy")
    rows = cells // count
    nx = lax.axis_size("gx") * width
    padded = 16 + aligned(rows)
    f32 = jnp.float32

    planes = 3 * width
    depth = aligned(planes * rows + 2 * aligned(planes))
    position = lax.axis_index("gy").astype(jnp.int32).reshape(1)
    parity = lax.rem(position, 2)
    chunks = pl.pallas_call(
        functools.partial(pack_kernel, rows),
        out_shape=jax.ShapeDtypeStruct((count, depth, lanes), f32),
        in_specs=in_smem(1) + in_vmem(1),
        out_specs=pl.BlockSpec(memory_space=pltpu.VMEM),
        compiler_params=params(),
        name="pack",
    )(parity, velocity)
    recv = swap_chunks(chunks, out_order(count))
    slot = lax.slice_in_dim(recv, planes * rows, planes * rows + aligned(planes), axis=1)
    swapped = lax.ppermute(slot, ("gy", "gx", "gz"), swap_pairs(walls, count))
    rank = lax.axis_index(("gx", "gz")).astype(jnp.int32).reshape(1)
    chunk_shape = jax.ShapeDtypeStruct((count, width, rows, lanes), f32)
    cells_here = nx * nz_parts * rows * lanes
    provisional = pl.pallas_call(
        functools.partial(germano_kernel, nz_parts, width, rows, walls),
        out_shape=chunk_shape,
        in_specs=in_smem(2) + in_vmem(1),
        out_specs=pl.BlockSpec(memory_space=pltpu.VMEM),
        scratch_shapes=[
            pltpu.VMEM((3, nx, nz_parts, padded, lanes), f32),
            pltpu.VMEM((3, nx, nz_parts, padded, lanes), f32),
            pltpu.VMEM((3, nx, nz_parts, 8, lanes), f32),
            pltpu.VMEM((7, nx, nz_parts, rows, lanes), f32),
            pltpu.VMEM((7, nx, nz_parts, rows, lanes), f32),
            pltpu.VMEM((15, nx, nz_parts, rows, lanes), f32),
        ],
        compiler_params=params(),
        cost_estimate=pl.CostEstimate(
            flops=300 * cells_here, bytes_accessed=16 * cells_here, transcendentals=2 * cells_here
        ),
        name="germano",
    )(rank, position, recv)
    eddy_chunks = pl.pallas_call(
        functools.partial(edge_kernel, nz_parts, width, rows, walls),
        out_shape=chunk_shape,
        in_specs=in_smem(2) + in_vmem(3),
        out_specs=pl.BlockSpec(memory_space=pltpu.VMEM),
        scratch_shapes=[pltpu.VMEM((3, 3, nx, nz_parts * lanes), f32)],
        input_output_aliases={4: 0},
        compiler_params=params(),
        name="edge",
    )(rank, position, recv, swapped, provisional)
    back = swap_chunks(eddy_chunks, back_order(count))

    length = cells // SEGMENTS
    levels = SEGMENTS.bit_length() - 1
    packed = aligned(11 * width)
    eddy_here, reduced, factors, tree = pl.pallas_call(
        sweep_kernel,
        out_shape=(
            jax.ShapeDtypeStruct((width, cells, lanes), f32),
            jax.ShapeDtypeStruct((packed, lanes), f32),
            jax.ShapeDtypeStruct((width, length, 5, SEGMENTS, lanes), f32),
            jax.ShapeDtypeStruct((width, levels, 5, SEGMENTS, lanes), f32),
        ),
        in_specs=in_smem(1) + in_vmem(3),
        out_specs=tuple(in_vmem(4)),
        compiler_params=params(),
        name="sweep",
    )(parity, back, velocity, tendency)

    others = [
        lax.ppermute(reduced, "gy", [(s, i) for i, s in enumerate(sources_of(step, walls))])
        for step in exchange_order(walls)
    ]
    particular, response, eddy = pl.pallas_call(
        spread_kernel,
        out_shape=(
            jax.ShapeDtypeStruct(velocity.shape, f32),
            jax.ShapeDtypeStruct((2, *velocity.shape[1:]), f32),
            jax.ShapeDtypeStruct(eddy_here.shape, f32),
        ),
        in_specs=in_vmem(4),
        out_specs=tuple(in_vmem(2) + in_hbm(1)),
        scratch_shapes=[pltpu.SemaphoreType.DMA],
        compiler_params=params(),
        cost_estimate=pl.CostEstimate(
            flops=20 * velocity.size, bytes_accessed=16 * velocity.size, transcendentals=0
        ),
        name="spread",
    )(factors, tree, velocity, eddy_here)
    new_velocity = pl.pallas_call(
        functools.partial(finish_kernel, walls),
        out_shape=jax.ShapeDtypeStruct(velocity.shape, f32),
        in_specs=in_smem(1) + in_vmem(2 + walls),
        out_specs=in_hbm(1)[0],
        scratch_shapes=[
            pltpu.VMEM((walls, packed, lanes), f32),
            pltpu.VMEM((walls + 1, aligned(3 * width), lanes), f32),
            pltpu.VMEM(velocity.shape, f32),
            pltpu.SemaphoreType.DMA((planes,)),
        ],
        compiler_params=params(),
        name="finish",
    )(position, particular, response, reduced, *others)
    return (new_velocity, eddy)


def solution(mesh):
    return jax.shard_map(
        body,
        mesh=mesh,
        in_specs=(P(None, "gx", "gy", "gz"), P(None, "gx", "gy", "gz")),
        out_specs=(P(None, "gx", "gy", "gz"), P("gx", "gy", "gz")),
        check_vma=False,
    )
```

```python
import functools

import jax
import jax.numpy as jnp
from jax import lax
from jax.experimental import pallas as pl
from jax.experimental.pallas import tpu as pltpu
from jax.sharding import PartitionSpec as P

LANES = 128
SEGMENTS = 8
VMEM_BYTES = 24 * 2**20


def strain_parts(grad_x, grad_y, grad_z):
    return (
        grad_x[0],
        grad_y[1],
        grad_z[2],
        grad_y[0] + grad_x[1],
        grad_z[0] + grad_x[2],
        grad_z[1] + grad_y[2],
    )


def strain_size(parts):
    diagonal = parts[0] * parts[0] + parts[1] * parts[1] + parts[2] * parts[2]
    mixed = parts[3] * parts[3] + parts[4] * parts[4] + parts[5] * parts[5]
    return jnp.sqrt(0.5 * diagonal + 0.25 * mixed)


def beside(blocks):
    count = len(blocks)
    lanes = blocks[0].shape[1]
    down = [pltpu.roll(f, 1, 1) for f in blocks]
    up = [pltpu.roll(f, lanes - 1, 1) for f in blocks]
    if count > 1:
        lane = lax.broadcasted_iota(jnp.int32, blocks[0].shape, 1)
        first, last = lane == 0, lane == lanes - 1
        down, up = (
            [jnp.where(first, down[i - 1], down[i]) for i in range(count)],
            [jnp.where(last, up[(i + 1) % count], up[i]) for i in range(count)],
        )
    return down, up


def slope_z(blocks):
    down, up = beside(blocks)
    return [u - d for u, d in zip(up, down)]


def smooth_z(blocks):
    down, up = beside(blocks)
    return [(u + d) + 2.0 * f for f, u, d in zip(blocks, up, down)]


def band_matrix(n):
    shape = (n, n)
    apart = lax.broadcasted_iota(jnp.int32, shape, 0) - lax.broadcasted_iota(jnp.int32, shape, 1)
    apart = jnp.abs(apart)
    near = jnp.logical_or(apart == 1, apart == n - 1)
    return jnp.where(apart == 0, 2.0, jnp.where(near, 1.0, 0.0)).astype(jnp.bfloat16)


def times_band(f, band):
    total = None
    for i in range(3):
        piece = f.astype(jnp.bfloat16)
        product = jnp.dot(piece, band, preferred_element_type=jnp.float32)
        total = product if total is None else total + product
        if i < 2:
            f = f - piece.astype(jnp.float32)
    return total


def products(v):
    return (v[0] * v[0], v[1] * v[1], v[2] * v[2], v[0] * v[1], v[0] * v[2], v[1] * v[2])


def outer_ranks(count):
    return (count - 3, count - 1)


def places(parity, count):
    outer = outer_ranks(count)
    inner = iter(range(1, count - 1))
    return [
        (0 if outer[parity] == rank else count - 1) if rank in outer else next(inner)
        for rank in range(count)
    ]


def swap_pairs(walls, count):
    odd, even = outer_ranks(count)
    partners = {}

    def join(a, b):
        partners[a], partners[b] = b, a

    for core in range(0, count, 2):
        here = (core, core + 1)
        if odd in here or even in here:
            first = 1 if odd in here else 0
            for wall in range(first, walls - 1, 2):
                for rank in here:
                    join((wall, rank), (wall + 1, rank))
        for wall in range(walls):
            if (wall, core) not in partners:
                join((wall, core), (wall, core + 1))
    return [
        (wall * count + rank, to[0] * count + to[1])
        for wall in range(walls)
        for rank in range(count)
        for to in [partners.get((wall, rank), (wall, rank))]
    ]


def ring_of(count):
    return [0, *range(1, count, 2), *range(count - 2 + count % 2, 0, -2)]


def by_core(chips):
    return [2 * chip + 1 for chip in chips] + [2 * chip for chip in chips]


def out_order(count):
    return by_core(ring_of(count // 2))


def back_order(count):
    return by_core(range(count // 2 - 1, -1, -1))


def slots_of(order):
    return [order.index(r) for r in range(len(order))]


def by_parity(parity, count, fill):
    outer = outer_ranks(count)
    for rank, place in enumerate(places(0, count)):
        if rank not in outer:
            fill(rank, place)
    for turn in range(2):

        @pl.when(parity[0] == turn)
        def _():
            for rank in outer:
                fill(rank, places(turn, count)[rank])


def aligned(n):
    return -(-n // 8) * 8


def pack_kernel(rows, parity, velocity, out):
    _, width, cells, _ = velocity.shape
    count, depth, lanes = out.shape
    planes = 3 * width
    slots = planes * rows

    slot_of = slots_of(out_order(count))

    def fill(rank, place):
        rank = slot_of[rank]
        first = place * rows
        beside = [first - 1, first + rows]
        if place == 0:
            beside = [first, first + rows]
        if place == count - 1:
            beside = [first + rows - 1, first - 1]
        for i in range(planes):
            c, x = divmod(i, width)
            out[rank, i * rows : (i + 1) * rows, :] = velocity[c, x, first : first + rows, :]
            for slot, row in enumerate(beside):
                at = slots + slot * aligned(planes) + i
                out[rank, at : at + 1, :] = velocity[c, x, row : row + 1, :]

    by_parity(parity, count, fill)
    blank = aligned(planes) - planes
    for rank in range(count):
        for slot in range(2):
            at = slots + slot * aligned(planes) + planes
            out[rank, at : at + blank, :] = jnp.zeros((blank, lanes), jnp.float32)
        at = slots + 2 * aligned(planes)
        if at < depth:
            out[rank, at:, :] = jnp.zeros((depth - at, lanes), jnp.float32)


def outer_sides(rank, parity, count):
    outer = outer_ranks(count)
    even = parity[0] == 0
    bottom = rank[0] == jnp.where(even, outer[0], outer[1])
    top = rank[0] == jnp.where(even, outer[1], outer[0])
    return bottom, top


def edge_kernel(nz_parts, width, rows, walls, rank, position, recv, swapped, given, out, vel):
    count, _, lanes = recv.shape
    planes = 3 * width
    nx = (count // nz_parts) * width
    nz = nz_parts * lanes
    bottom, top = outer_sides(rank, [lax.rem(position[0], 2)], count)
    came, to = slots_of(out_order(count)), slots_of(back_order(count))
    at_seam = jnp.logical_or(
        jnp.logical_and(bottom, position[0] > 0), jnp.logical_and(top, position[0] < walls - 1)
    )

    def rows_of(k, i):
        k = came[k]
        first = i * rows
        own = [recv[k, first + j : first + j + 1, :] for j in (0, 1, rows - 2, rows - 1)]
        far = swapped[k, i : i + 1, :]
        return (
            jnp.where(bottom, far, own[2]),
            jnp.where(bottom, own[0], own[3]),
            jnp.where(bottom, own[1], far),
        )

    def roll_x(f, shift):
        return pltpu.roll(f, shift % nx, 0)

    def roll_z(f, shift):
        return pltpu.roll(f, shift % nz, 1)

    def smooth_x(f):
        return (roll_x(f, 1) + roll_x(f, -1)) + 2.0 * f

    def smooth(f):
        f = smooth_x(f)
        return (roll_z(f, 1) + roll_z(f, -1)) + 2.0 * f

    def slopes(below, centre, above):
        return strain_parts(
            [roll_x(f, -1) - roll_x(f, 1) for f in centre],
            [a - b for a, b in zip(above, below)],
            [roll_z(f, -1) - roll_z(f, 1) for f in centre],
        )

    @pl.when(at_seam)
    def _():
        for k in range(count):
            x0, zb = (k // nz_parts) * width, k % nz_parts
            for i in range(planes):
                c, x = divmod(i, width)
                for j, row in enumerate(rows_of(k, i)):
                    vel[j, c, x0 + x : x0 + x + 1, zb * lanes : (zb + 1) * lanes] = row
        u = [[vel[j, c] for c in range(3)] for j in range(3)]
        v = [[smooth(f) for f in row] for row in u]
        strain = slopes(*u)
        size = strain_size(strain)
        mean_strain = slopes(*v)
        mean_size = 0.25 * strain_size(mean_strain)
        scaled = [0.0625 * f for f in v[1]]
        pairs = [v[1][i] * scaled[j] for i, j in ((0, 0), (1, 1), (2, 2), (0, 1), (0, 2), (1, 2))]
        leonard = [smooth(p) - q for p, q in zip(products(u[1]), pairs)]
        model = [smooth(size * s) - mean_size * f for s, f in zip(strain, mean_strain)]
        lm, mm = contracted(leonard, model)
        coefficient = coefficient_of(
            *(jnp.sum(f, axis=(0, 1), keepdims=True) for f in (lm, mm)), nx * nz
        )
        eddy = coefficient * size

        def put(at):
            for k in range(count):
                x0, zb = (k // nz_parts) * width, k % nz_parts
                for x in range(width):
                    out[to[k], x, at : at + 1, :] = eddy[x0 + x : x0 + x + 1, zb * lanes : (zb + 1) * lanes]

        pl.when(bottom)(lambda: put(0))
        pl.when(top)(lambda: put(rows - 1))


def contracted(leonard, model):
    lm = mm = None
    for i in range(6):
        square = model[i] * model[i] if i < 3 else (0.5 * model[i]) * model[i]
        product = leonard[i] * model[i]
        lm = product if lm is None else lm + product
        mm = square if mm is None else mm + square
    return lm, mm


def coefficient_of(plane_lm, plane_mm, cells):
    scale = 1.0 / (256.0 * cells)
    return jnp.maximum(plane_lm * scale / (plane_mm * scale + 1e-06), 0.0)


def germano_kernel(nz_parts, width, rows, walls, rank, position, recv, out, vel, filt, ends, strains, means, part):
    count, _, lanes = recv.shape
    planes = 3 * width
    bottom, top = outer_sides(rank, [lax.rem(position[0], 2)], count)
    floor = jnp.logical_and(bottom, position[0] == 0)
    ceiling = jnp.logical_and(top, position[0] == walls - 1)
    came, to = slots_of(out_order(count)), slots_of(back_order(count))
    nx = (count // nz_parts) * width
    nz = nz_parts * lanes
    blocks = range(nz_parts)
    lead = 8
    inner = slice(lead, lead + rows)
    for k in range(count):
        x0, zb = (k // nz_parts) * width, k % nz_parts
        for c in range(3):
            for x in range(width):
                i = c * width + x
                vel[c, x0 + x, zb, inner, :] = recv[came[k], i * rows : (i + 1) * rows, :]
                slots = planes * rows + i
                near = recv[came[k], slots : slots + 1, :]
                slots += aligned(planes)
                other = recv[came[k], slots : slots + 1, :]
                below = jnp.where(floor, 0.0, jnp.where(top, other, near))
                above = jnp.where(ceiling, 0.0, other)
                for side, (edge, at) in enumerate(((below, lead - 1), (above, lead + rows))):
                    vel[c, x0 + x, zb, at : at + 1, :] = edge
                    ends[c, x0 + x, zb, side : side + 1, :] = edge

    lower = slice(lead - 1, lead - 1 + rows)
    upper = slice(lead + 1, lead + 1 + rows)

    def paired(read, x):
        return read(x) + read((x + 1) % nx)

    def smooth_x(sums, x):
        return sums((x - 1) % nx) + sums(x)

    def keep_strain(field, x, kept, scale):
        left, right = (x - 1) % nx, (x + 1) % nx
        grad_z = [slope_z([field[c, x, zb, inner, :] for zb in blocks]) for c in range(3)]
        for zb in blocks:
            grad_x = [field[c, right, zb, inner, :] - field[c, left, zb, inner, :] for c in range(3)]
            grad_y = [field[c, x, zb, upper, :] - field[c, x, zb, lower, :] for c in range(3)]
            parts = strain_parts(grad_x, grad_y, [grad_z[c][zb] for c in range(3)])
            for i in range(6):
                kept[i, x, zb] = parts[i]
            kept[6, x, zb] = scale * strain_size(parts) if scale != 1.0 else strain_size(parts)

    def filter_z(read, kept):
        if not on_matrix_unit:
            for x in range(nx):
                fields = [paired(lambda at: read(at, zb), x) for zb in blocks]
                for zb, f in enumerate(smooth_z(fields)):
                    part[kept, x, zb] = f
            return
        half = nx // 2
        for x0 in (0, half):
            fields = [[read((x0 + x) % nx, zb) for zb in blocks] for x in range(half + 1)]
            planes_here = [
                jnp.concatenate([f + g for f, g in zip(fields[x], fields[x + 1])], axis=1)
                for x in range(half)
            ]
            total = times_band(jnp.concatenate(planes_here, axis=0), band)
            for x in range(half):
                for zb in blocks:
                    part[kept, x0 + x, zb] = total[x * rows : (x + 1) * rows, zb * lanes : (zb + 1) * lanes]

    on_matrix_unit = nz <= 256 and rows * nx % 32 == 0 and rows % 8 == 0
    band = band_matrix(nz) if on_matrix_unit else None

    for c in range(3):
        filter_z(lambda x, zb: vel[c, x, zb, inner, :], c)
    for x in range(nx):
        keep_strain(vel, x, strains, 1.0)
    for c in range(3):
        rims = [smooth_z([paired(lambda at: ends[c, at, zb], x) for zb in blocks]) for x in range(nx)]
        for x in range(nx):
            for zb in blocks:
                rim = smooth_x(lambda at: rims[at][zb], x)
                filt[c, x, zb, lead - 1 : lead, :] = rim[0:1, :]
                filt[c, x, zb, lead + rows : lead + rows + 1, :] = rim[1:2, :]
                filt[c, x, zb, inner, :] = smooth_x(lambda at: part[c, at, zb], x)
    for i, (a, b) in enumerate(((0, 0), (1, 1), (2, 2), (0, 1), (0, 2), (1, 2))):
        filter_z(lambda x, zb: vel[a, x, zb, inner, :] * vel[b, x, zb, inner, :], 3 + i)
        filter_z(lambda x, zb: strains[6, x, zb] * strains[i, x, zb], 9 + i)
    for x in range(nx):
        keep_strain(filt, x, means, 0.25)

    sum_lm = sum_mm = None
    for x in range(nx):
        for zb in blocks:
            v = [filt[c, x, zb, inner, :] for c in range(3)]
            scaled = [0.0625 * f for f in v]
            size = means[6, x, zb]
            for i, (a, b) in enumerate(((0, 0), (1, 1), (2, 2), (0, 1), (0, 2), (1, 2))):
                leonard = smooth_x(lambda at: part[3 + i, at, zb], x) - v[a] * scaled[b]
                model = smooth_x(lambda at: part[9 + i, at, zb], x) - size * means[i, x, zb]
                square = model * model if i < 3 else (0.5 * model) * model
                sum_lm = leonard * model if sum_lm is None else sum_lm + leonard * model
                sum_mm = square if sum_mm is None else sum_mm + square

    coefficient = coefficient_of(
        *(jnp.sum(total, axis=1, keepdims=True) for total in (sum_lm, sum_mm)), nx * nz
    )
    for k in range(count):
        x0, zb = (k // nz_parts) * width, k % nz_parts
        for x in range(width):
            out[to[k], x] = coefficient * strains[6, x0 + x, zb]


def sweep_kernel(parity, back, velocity, tendency, eddy, reduced, factors, tree):
    count, width, rows, _ = back.shape
    length = count * rows // SEGMENTS
    slots = slots_of(back_order(count))

    def fill(rank, place):
        for x in range(width):
            eddy[x, place * rows : (place + 1) * rows, :] = back[slots[rank], x]

    by_parity(parity, count, fill)

    def row(ref, index, j):
        return ref[(*index, pl.ds(j, SEGMENTS, stride=length), slice(None))]

    planes = range(width)
    last_row = length - 1
    visc = [[1.0 + row(eddy, (x,), j) for x in planes] for j in range(length)]
    links = [[750.0 * (v + w) for v, w in zip(visc[j], visc[j + 1])] for j in range(last_row)]

    over = [jnp.ones_like(v) for v in visc[0]]
    under = [jnp.ones_like(v) for v in visc[0]]
    inverses = []
    for j in range(last_row):
        inverses.append([u / (o + e * u) for o, u, e in zip(over, under, links[j])])
        steps = [o * (1.0 / e) for o, e in zip(over, links[j])]
        under, over = (
            [u + t for u, t in zip(under, steps)],
            [(o + u) + t for o, u, t in zip(over, under, steps)],
        )
    inverses.append([u / o for o, u in zip(over, under)])

    value = first = corner = left = None
    reach = [jnp.ones_like(v) for v in visc[0]]
    for j in range(length):
        inverse = inverses[j]
        before = value
        source = [[2.0 * row(velocity, (c, x), j) + row(tendency, (c, x), j) for x in planes] for c in range(3)]
        value = [[f * r for f, r in zip(source[c], inverse)] for c in range(3)]
        if j > 0:
            carry = [e * r for e, r in zip(links[j - 1], inverse)]
            value = [[v + k * w for v, k, w in zip(value[c], carry, before[c])] for c in range(3)]
        left = [m * r for m, r in zip(reach, inverse)]
        if j == 0:
            first, corner = value, left
        else:
            first = [[f + m * v for f, m, v in zip(first[c], reach, value[c])] for c in range(3)]
            corner = [a + m * v for a, m, v in zip(corner, reach, left)]
        ratio = inverse
        if j < last_row:
            ratio = [e * r for e, r in zip(links[j], inverse)]
            reach = [m * r for m, r in zip(reach, ratio)]
        for x in planes:
            for c in range(3):
                factors[x, j, c] = value[c][x]
            factors[x, j, 3] = left[x]
            factors[x, j, 4] = ratio[x]

    def other(fields, step):
        return [pltpu.roll(f, (SEGMENTS - step) % SEGMENTS, 0) if step else f for f in fields]

    last, across, end = value, left, inverse
    seams = [750.0 * (v + w) for v, w in zip(visc[last_row], other(visc[0], 1))]
    level, step = 0, 1
    while step < SEGMENTS:
        link = other(seams, step - 1)
        first_b = [other(f, step) for f in first]
        last_b = [other(f, step) for f in last]
        corner_b, end_b, across_b = other(corner, step), other(end, step), other(across, step)
        stiff = [e / (1.0 + e * (d + a)) for e, d, a in zip(link, end, corner_b)]
        flux = [[k * (g - f) for k, g, f in zip(stiff, last[c], first_b[c])] for c in range(3)]
        from_left = [k * b for k, b in zip(stiff, across)]
        from_right = [k * b for k, b in zip(stiff, across_b)]
        for x in planes:
            for c in range(3):
                tree[x, level, c] = flux[c][x]
            tree[x, level, 3] = from_left[x]
            tree[x, level, 4] = from_right[x]
        first = [[f - b * t for f, b, t in zip(first[c], across, flux[c])] for c in range(3)]
        last = [[g + b * t for g, b, t in zip(last_b[c], across_b, flux[c])] for c in range(3)]
        corner = [a - b * k for a, b, k in zip(corner, across, from_left)]
        end = [d - b * k for d, b, k in zip(end_b, across_b, from_right)]
        across = [k * b for k, b in zip(from_left, across_b)]
        level, step = level + 1, step * 2
    for x in planes:
        rows_out = [f[x][0:1, :] for f in (*first, *last, corner, across, end, visc[0])]
        rows_out.append(visc[last_row][x][SEGMENTS - 1 :, :])
        for i, v in enumerate(rows_out):
            reduced[i * width + x : i * width + x + 1, :] = v


def spread_kernel(factors, tree, velocity, eddy, particular, response, eddy_out, sent):
    write = pltpu.make_async_copy(eddy, eddy_out, sent)
    write.start()
    width, length = factors.shape[:2]
    levels = tree.shape[1]
    sublane = lax.broadcasted_iota(jnp.int32, (SEGMENTS, LANES), 0)
    one, zero = (jnp.full((SEGMENTS, LANES), v, jnp.float32) for v in (1.0, 0.0))
    sides = [(c, zero, zero) for c in range(3)] + [(None, one, zero), (None, zero, one)]
    lefts = [[side[1]] * width for side in sides]
    rights = [[side[2]] * width for side in sides]
    for level in range(levels - 1, -1, -1):
        step = 2**level
        second = lax.rem(sublane, 2 * step) == step
        for n, (c, _, _) in enumerate(sides):
            for x in range(width):
                left, right = lefts[n][x], rights[n][x]
                through = tree[x, level, 3] * left - tree[x, level, 4] * right
                if c is not None:
                    through = tree[x, level, c] + through
                lefts[n][x] = jnp.where(second, pltpu.roll(through, step, 0), left)
                rights[n][x] = jnp.where(second, pltpu.roll(right, step, 0), -through)
    values = rights
    for j in range(length - 1, -1, -1):
        rows = pl.ds(j, SEGMENTS, stride=length)
        for n, (c, _, _) in enumerate(sides):
            for x in range(width):
                value = factors[x, j, 3] * lefts[n][x] + factors[x, j, 4] * values[n][x]
                if c is not None:
                    value = factors[x, j, c] + value
                    particular[c, x, rows, :] = value - velocity[c, x, rows, :]
                else:
                    response[n - 3, x, rows, :] = value
                values[n][x] = value
    write.wait()


def sources_of(step, count):
    return [(i - step) % count for i in range(count)]


def exchange_order(count):
    return range(count - 1, 0, -1)


def spread_kernel(factors, tree, velocity, eddy, particular, response, eddy_out, sent):
    write = pltpu.make_async_copy(eddy, eddy_out, sent)
    write.start()
    width, length = factors.shape[:2]
    levels = tree.shape[1]
    sublane = lax.broadcasted_iota(jnp.int32, (SEGMENTS, LANES), 0)
    one, zero = (jnp.full((SEGMENTS, LANES), v, jnp.float32) for v in (1.0, 0.0))
    sides = [(c, zero, zero) for c in range(3)] + [(None, one, zero), (None, zero, one)]
    lefts = [[side[1]] * width for side in sides]
    rights = [[side[2]] * width for side in sides]
    for level in range(levels - 1, -1, -1):
        step = 2**level
        second = lax.rem(sublane, 2 * step) == step
        for n, (c, _, _) in enumerate(sides):
            for x in range(width):
                left, right = lefts[n][x], rights[n][x]
                through = tree[x, level, 3] * left - tree[x, level, 4] * right
                if c is not None:
                    through = tree[x, level, c] + through
                lefts[n][x] = jnp.where(second, pltpu.roll(through, step, 0), left)
                rights[n][x] = jnp.where(second, pltpu.roll(right, step, 0), -through)
    values = rights
    for j in range(length - 1, -1, -1):
        rows = pl.ds(j, SEGMENTS, stride=length)
        for n, (c, _, _) in enumerate(sides):
            for x in range(width):
                value = factors[x, j, 3] * lefts[n][x] + factors[x, j, 4] * values[n][x]
                if c is not None:
                    value = factors[x, j, c] + value
                    particular[c, x, rows, :] = value - velocity[c, x, rows, :]
                else:
                    response[n - 3, x, rows, :] = value
                values[n][x] = value
    write.wait()


def partner(i, step, count):
    if count & (count - 1) == 0:
        return i ^ step
    return (i - step + count) % count


def finish_kernel(devices, position, particular, response, *rest):
    reduced, (result, gathered, fluxes, out, sent) = rest[:devices], rest[devices:]
    width = particular.shape[1]
    here = position[0]
    for step, ref in zip([0, *exchange_order(devices)], reduced):
        source = sum(jnp.where(here == i, s, 0) for i, s in enumerate(sources_of(step, devices)))
        gathered[source] = ref[...]

    def part(device, i):
        return gathered[device, i * width : (i + 1) * width, :]

    pivots, sources = [], []
    for i in range(devices + 1):
        visc = [part(i - 1, 10)] if i > 0 else []
        total = [part(i - 1, 8)] if i > 0 else []
        source = [part(i - 1, 3 + c) for c in range(3)] if i > 0 else [0.0] * 3
        if i < devices:
            visc.append(part(i, 9))
            total.append(part(i, 6))
            source = [s - part(i, c) for c, s in enumerate(source)]
        pivots.append(sum(total) + 1.0 / (750.0 * sum(visc)))
        sources.append(source)
    across = [part(i, 7) for i in range(devices)]
    minors = [jnp.ones_like(pivots[0]), pivots[0]]
    for i in range(1, devices + 1):
        minors.append(pivots[i] * minors[i] - (across[i - 1] * across[i - 1]) * minors[i - 1])
    inverses = [minors[i] / minors[i + 1] for i in range(devices + 1)]
    ratios = [b * r for b, r in zip(across, inverses)]
    for i in range(1, devices + 1):
        sources[i] = [s + ratios[i - 1] * t for s, t in zip(sources[i], sources[i - 1])]
    for i in range(devices, -1, -1):
        flux_here = [inverses[i] * s for s in sources[i]]
        flux = flux_here if i == devices else [f + ratios[i] * g for f, g in zip(flux_here, flux)]
        for c in range(3):
            fluxes[i, c * width : (c + 1) * width, :] = flux[c]

    writes = []
    for c in range(3):
        for x in range(width):
            r = c * width + x
            left, right = fluxes[here, r : r + 1, :], fluxes[here + 1, r : r + 1, :]
            out[c, x] = particular[c, x] + (response[0, x] * left - response[1, x] * right)
            writes.append(pltpu.make_async_copy(out.at[c, x], result.at[c, x], sent.at[r]))
            writes[-1].start()
    for write in writes:
        write.wait()


def in_vmem(count):
    return [pl.BlockSpec(memory_space=pltpu.VMEM)] * count


def in_hbm(count):
    return [pl.BlockSpec(memory_space=pltpu.HBM)] * count


def in_smem(count):
    return [pl.BlockSpec(memory_space=pltpu.SMEM)] * count


def params():
    return pltpu.CompilerParams(vmem_limit_bytes=VMEM_BYTES)


def swap_chunks(chunks, order):
    return lax.all_to_all(
        chunks, ("gx", "gz"), split_axis=0, concat_axis=0, tiled=True, axis_index_groups=[order]
    )


def body(velocity, tendency):
    _, width, cells, lanes = velocity.shape
    nz_parts = lax.axis_size("gz")
    count = lax.axis_size("gx") * nz_parts
    walls = lax.axis_size("gy")
    rows = cells // count
    nx = lax.axis_size("gx") * width
    padded = 16 + aligned(rows)
    f32 = jnp.float32

    planes = 3 * width
    depth = aligned(planes * rows + 2 * aligned(planes))
    position = lax.axis_index("gy").astype(jnp.int32).reshape(1)
    parity = lax.rem(position, 2)
    chunks = pl.pallas_call(
        functools.partial(pack_kernel, rows),
        out_shape=jax.ShapeDtypeStruct((count, depth, lanes), f32),
        in_specs=in_smem(1) + in_vmem(1),
        out_specs=pl.BlockSpec(memory_space=pltpu.VMEM),
        compiler_params=params(),
        name="pack",
    )(parity, velocity)
    recv = swap_chunks(chunks, out_order(count))
    slot = lax.slice_in_dim(recv, planes * rows, planes * rows + aligned(planes), axis=1)
    swapped = lax.ppermute(slot, ("gy", "gx", "gz"), swap_pairs(walls, count))
    rank = lax.axis_index(("gx", "gz")).astype(jnp.int32).reshape(1)
    chunk_shape = jax.ShapeDtypeStruct((count, width, rows, lanes), f32)
    cells_here = nx * nz_parts * rows * lanes
    provisional = pl.pallas_call(
        functools.partial(germano_kernel, nz_parts, width, rows, walls),
        out_shape=chunk_shape,
        in_specs=in_smem(2) + in_vmem(1),
        out_specs=pl.BlockSpec(memory_space=pltpu.VMEM),
        scratch_shapes=[
            pltpu.VMEM((3, nx, nz_parts, padded, lanes), f32),
            pltpu.VMEM((3, nx, nz_parts, padded, lanes), f32),
            pltpu.VMEM((3, nx, nz_parts, 8, lanes), f32),
            pltpu.VMEM((7, nx, nz_parts, rows, lanes), f32),
            pltpu.VMEM((7, nx, nz_parts, rows, lanes), f32),
            pltpu.VMEM((15, nx, nz_parts, rows, lanes), f32),
        ],
        compiler_params=params(),
        cost_estimate=pl.CostEstimate(
            flops=300 * cells_here, bytes_accessed=16 * cells_here, transcendentals=2 * cells_here
        ),
        name="germano",
    )(rank, position, recv)
    eddy_chunks = pl.pallas_call(
        functools.partial(edge_kernel, nz_parts, width, rows, walls),
        out_shape=chunk_shape,
        in_specs=in_smem(2) + in_vmem(3),
        out_specs=pl.BlockSpec(memory_space=pltpu.VMEM),
        scratch_shapes=[pltpu.VMEM((3, 3, nx, nz_parts * lanes), f32)],
        input_output_aliases={4: 0},
        compiler_params=params(),
        name="edge",
    )(rank, position, recv, swapped, provisional)
    back = swap_chunks(eddy_chunks, back_order(count))

    length = cells // SEGMENTS
    levels = SEGMENTS.bit_length() - 1
    packed = aligned(11 * width)
    eddy_here, reduced, factors, tree = pl.pallas_call(
        sweep_kernel,
        out_shape=(
            jax.ShapeDtypeStruct((width, cells, lanes), f32),
            jax.ShapeDtypeStruct((packed, lanes), f32),
            jax.ShapeDtypeStruct((width, length, 5, SEGMENTS, lanes), f32),
            jax.ShapeDtypeStruct((width, levels, 5, SEGMENTS, lanes), f32),
        ),
        in_specs=in_smem(1) + in_vmem(3),
        out_specs=tuple(in_vmem(4)),
        compiler_params=params(),
        name="sweep",
    )(parity, back, velocity, tendency)

    others = [
        lax.ppermute(reduced, "gy", [(s, i) for i, s in enumerate(sources_of(step, walls))])
        for step in exchange_order(walls)
    ]
    particular, response, eddy = pl.pallas_call(
        spread_kernel,
        out_shape=(
            jax.ShapeDtypeStruct(velocity.shape, f32),
            jax.ShapeDtypeStruct((2, *velocity.shape[1:]), f32),
            jax.ShapeDtypeStruct(eddy_here.shape, f32),
        ),
        in_specs=in_vmem(4),
        out_specs=tuple(in_vmem(2) + in_hbm(1)),
        scratch_shapes=[pltpu.SemaphoreType.DMA],
        compiler_params=params(),
        cost_estimate=pl.CostEstimate(
            flops=20 * velocity.size, bytes_accessed=16 * velocity.size, transcendentals=0
        ),
        name="spread",
    )(factors, tree, velocity, eddy_here)
    new_velocity = pl.pallas_call(
        functools.partial(finish_kernel, walls),
        out_shape=jax.ShapeDtypeStruct(velocity.shape, f32),
        in_specs=in_smem(1) + in_vmem(2 + walls),
        out_specs=in_hbm(1)[0],
        scratch_shapes=[
            pltpu.VMEM((walls, packed, lanes), f32),
            pltpu.VMEM((walls + 1, aligned(3 * width), lanes), f32),
            pltpu.VMEM(velocity.shape, f32),
            pltpu.SemaphoreType.DMA((planes,)),
        ],
        compiler_params=params(),
        name="finish",
    )(position, particular, response, reduced, *others)
    return (new_velocity, eddy)


def solution(mesh):
    return jax.shard_map(
        body,
        mesh=mesh,
        in_specs=(P(None, "gx", "gy", "gz"), P(None, "gx", "gy", "gz")),
        out_specs=(P(None, "gx", "gy", "gz"), P("gx", "gy", "gz")),
        check_vma=False,
    )
```

```python
import functools

import jax
import jax.numpy as jnp
from jax import lax
from jax.experimental import pallas as pl
from jax.experimental.pallas import tpu as pltpu
from jax.sharding import PartitionSpec as P

LANES = 128
SEGMENTS = 8
VMEM_BYTES = 24 * 2**20


def strain_parts(grad_x, grad_y, grad_z):
    return (
        grad_x[0],
        grad_y[1],
        grad_z[2],
        grad_y[0] + grad_x[1],
        grad_z[0] + grad_x[2],
        grad_z[1] + grad_y[2],
    )


def strain_size(parts):
    diagonal = parts[0] * parts[0] + parts[1] * parts[1] + parts[2] * parts[2]
    mixed = parts[3] * parts[3] + parts[4] * parts[4] + parts[5] * parts[5]
    return jnp.sqrt(0.5 * diagonal + 0.25 * mixed)


def beside(blocks):
    count = len(blocks)
    lanes = blocks[0].shape[1]
    down = [pltpu.roll(f, 1, 1) for f in blocks]
    up = [pltpu.roll(f, lanes - 1, 1) for f in blocks]
    if count > 1:
        lane = lax.broadcasted_iota(jnp.int32, blocks[0].shape, 1)
        first, last = lane == 0, lane == lanes - 1
        down, up = (
            [jnp.where(first, down[i - 1], down[i]) for i in range(count)],
            [jnp.where(last, up[(i + 1) % count], up[i]) for i in range(count)],
        )
    return down, up


def slope_z(blocks):
    down, up = beside(blocks)
    return [u - d for u, d in zip(up, down)]


def smooth_z(blocks):
    down, up = beside(blocks)
    return [(u + d) + 2.0 * f for f, u, d in zip(blocks, up, down)]


def band_matrix(n):
    shape = (n, n)
    apart = lax.broadcasted_iota(jnp.int32, shape, 0) - lax.broadcasted_iota(jnp.int32, shape, 1)
    apart = jnp.abs(apart)
    near = jnp.logical_or(apart == 1, apart == n - 1)
    return jnp.where(apart == 0, 2.0, jnp.where(near, 1.0, 0.0)).astype(jnp.bfloat16)


def times_band(f, band):
    total = None
    for i in range(3):
        piece = f.astype(jnp.bfloat16)
        product = jnp.dot(piece, band, preferred_element_type=jnp.float32)
        total = product if total is None else total + product
        if i < 2:
            f = f - piece.astype(jnp.float32)
    return total


def products(v):
    return (v[0] * v[0], v[1] * v[1], v[2] * v[2], v[0] * v[1], v[0] * v[2], v[1] * v[2])


def outer_ranks(count):
    return (count - 3, count - 1)


def places(parity, count):
    outer = outer_ranks(count)
    inner = iter(range(1, count - 1))
    return [
        (0 if outer[parity] == rank else count - 1) if rank in outer else next(inner)
        for rank in range(count)
    ]


def swap_pairs(walls, count):
    odd, even = outer_ranks(count)
    partners = {}

    def join(a, b):
        partners[a], partners[b] = b, a

    for core in range(0, count, 2):
        here = (core, core + 1)
        if odd in here or even in here:
            first = 1 if odd in here else 0
            for wall in range(first, walls - 1, 2):
                for rank in here:
                    join((wall, rank), (wall + 1, rank))
        for wall in range(walls):
            if (wall, core) not in partners:
                join((wall, core), (wall, core + 1))
    return [
        (wall * count + rank, to[0] * count + to[1])
        for wall in range(walls)
        for rank in range(count)
        for to in [partners.get((wall, rank), (wall, rank))]
    ]


def ring_of(count):
    return [0, *range(1, count, 2), *range(count - 2 + count % 2, 0, -2)]


def by_core(chips):
    return [2 * chip + 1 for chip in chips] + [2 * chip for chip in chips]


def out_order(count):
    return by_core(ring_of(count // 2))


def back_order(count):
    return by_core(range(count // 2 - 1, -1, -1))


def slots_of(order):
    return [order.index(r) for r in range(len(order))]


def by_parity(parity, count, fill):
    outer = outer_ranks(count)
    for rank, place in enumerate(places(0, count)):
        if rank not in outer:
            fill(rank, place)
    for turn in range(2):

        @pl.when(parity[0] == turn)
        def _():
            for rank in outer:
                fill(rank, places(turn, count)[rank])


def aligned(n):
    return -(-n // 8) * 8


def pack_kernel(rows, parity, velocity, out):
    _, width, cells, _ = velocity.shape
    count, depth, lanes = out.shape
    planes = 3 * width
    slots = planes * rows

    slot_of = slots_of(out_order(count))

    def fill(rank, place):
        rank = slot_of[rank]
        first = place * rows
        beside = [first - 1, first + rows]
        if place == 0:
            beside = [first, first + rows]
        if place == count - 1:
            beside = [first + rows - 1, first - 1]
        for i in range(planes):
            c, x = divmod(i, width)
            out[rank, i * rows : (i + 1) * rows, :] = velocity[c, x, first : first + rows, :]
            for slot, row in enumerate(beside):
                at = slots + slot * aligned(planes) + i
                out[rank, at : at + 1, :] = velocity[c, x, row : row + 1, :]

    by_parity(parity, count, fill)
    blank = aligned(planes) - planes
    for rank in range(count):
        for slot in range(2):
            at = slots + slot * aligned(planes) + planes
            out[rank, at : at + blank, :] = jnp.zeros((blank, lanes), jnp.float32)
        at = slots + 2 * aligned(planes)
        if at < depth:
            out[rank, at:, :] = jnp.zeros((depth - at, lanes), jnp.float32)


def outer_sides(rank, parity, count):
    outer = outer_ranks(count)
    even = parity[0] == 0
    bottom = rank[0] == jnp.where(even, outer[0], outer[1])
    top = rank[0] == jnp.where(even, outer[1], outer[0])
    return bottom, top


def edge_kernel(nz_parts, width, rows, walls, rank, position, recv, swapped, given, out, vel):
    count, _, lanes = recv.shape
    planes = 3 * width
    nx = (count // nz_parts) * width
    nz = nz_parts * lanes
    bottom, top = outer_sides(rank, [lax.rem(position[0], 2)], count)
    came, to = slots_of(out_order(count)), slots_of(back_order(count))
    at_seam = jnp.logical_or(
        jnp.logical_and(bottom, position[0] > 0), jnp.logical_and(top, position[0] < walls - 1)
    )

    def rows_of(k, i):
        k = came[k]
        first = i * rows
        own = [recv[k, first + j : first + j + 1, :] for j in (0, 1, rows - 2, rows - 1)]
        far = swapped[k, i : i + 1, :]
        return (
            jnp.where(bottom, far, own[2]),
            jnp.where(bottom, own[0], own[3]),
            jnp.where(bottom, own[1], far),
        )

    def roll_x(f, shift):
        return pltpu.roll(f, shift % nx, 0)

    def roll_z(f, shift):
        return pltpu.roll(f, shift % nz, 1)

    def smooth_x(f):
        return (roll_x(f, 1) + roll_x(f, -1)) + 2.0 * f

    def smooth(f):
        f = smooth_x(f)
        return (roll_z(f, 1) + roll_z(f, -1)) + 2.0 * f

    def slopes(below, centre, above):
        return strain_parts(
            [roll_x(f, -1) - roll_x(f, 1) for f in centre],
            [a - b for a, b in zip(above, below)],
            [roll_z(f, -1) - roll_z(f, 1) for f in centre],
        )

    @pl.when(at_seam)
    def _():
        for k in range(count):
            x0, zb = (k // nz_parts) * width, k % nz_parts
            for i in range(planes):
                c, x = divmod(i, width)
                for j, row in enumerate(rows_of(k, i)):
                    vel[j, c, x0 + x : x0 + x + 1, zb * lanes : (zb + 1) * lanes] = row
        u = [[vel[j, c] for c in range(3)] for j in range(3)]
        v = [[smooth(f) for f in row] for row in u]
        strain = slopes(*u)
        size = strain_size(strain)
        mean_strain = slopes(*v)
        mean_size = 0.25 * strain_size(mean_strain)
        scaled = [0.0625 * f for f in v[1]]
        pairs = [v[1][i] * scaled[j] for i, j in ((0, 0), (1, 1), (2, 2), (0, 1), (0, 2), (1, 2))]
        leonard = [smooth(p) - q for p, q in zip(products(u[1]), pairs)]
        model = [smooth(size * s) - mean_size * f for s, f in zip(strain, mean_strain)]
        lm, mm = contracted(leonard, model)
        coefficient = coefficient_of(
            *(jnp.sum(f, axis=(0, 1), keepdims=True) for f in (lm, mm)), nx * nz
        )
        eddy = coefficient * size

        def put(at):
            for k in range(count):
                x0, zb = (k // nz_parts) * width, k % nz_parts
                for x in range(width):
                    out[to[k], x, at : at + 1, :] = eddy[x0 + x : x0 + x + 1, zb * lanes : (zb + 1) * lanes]

        pl.when(bottom)(lambda: put(0))
        pl.when(top)(lambda: put(rows - 1))


def contracted(leonard, model):
    lm = mm = None
    for i in range(6):
        square = model[i] * model[i] if i < 3 else (0.5 * model[i]) * model[i]
        product = leonard[i] * model[i]
        lm = product if lm is None else lm + product
        mm = square if mm is None else mm + square
    return lm, mm


def coefficient_of(plane_lm, plane_mm, cells):
    scale = 1.0 / (256.0 * cells)
    return jnp.maximum(plane_lm * scale / (plane_mm * scale + 1e-06), 0.0)


def germano_kernel(nz_parts, width, rows, walls, rank, position, recv, out, vel, filt, ends, strains, means, part):
    count, _, lanes = recv.shape
    planes = 3 * width
    bottom, top = outer_sides(rank, [lax.rem(position[0], 2)], count)
    floor = jnp.logical_and(bottom, position[0] == 0)
    ceiling = jnp.logical_and(top, position[0] == walls - 1)
    came, to = slots_of(out_order(count)), slots_of(back_order(count))
    nx = (count // nz_parts) * width
    nz = nz_parts * lanes
    blocks = range(nz_parts)
    lead = 8
    inner = slice(lead, lead + rows)
    for k in range(count):
        x0, zb = (k // nz_parts) * width, k % nz_parts
        for c in range(3):
            for x in range(width):
                i = c * width + x
                vel[c, x0 + x, zb, inner, :] = recv[came[k], i * rows : (i + 1) * rows, :]
                slots = planes * rows + i
                near = recv[came[k], slots : slots + 1, :]
                slots += aligned(planes)
                other = recv[came[k], slots : slots + 1, :]
                below = jnp.where(floor, 0.0, jnp.where(top, other, near))
                above = jnp.where(ceiling, 0.0, other)
                for side, (edge, at) in enumerate(((below, lead - 1), (above, lead + rows))):
                    vel[c, x0 + x, zb, at : at + 1, :] = edge
                    ends[c, x0 + x, zb, side : side + 1, :] = edge

    lower = slice(lead - 1, lead - 1 + rows)
    upper = slice(lead + 1, lead + 1 + rows)

    def paired(read, x):
        return read(x) + read((x + 1) % nx)

    def smooth_x(sums, x):
        return sums((x - 1) % nx) + sums(x)

    def keep_strain(field, x, kept, scale):
        left, right = (x - 1) % nx, (x + 1) % nx
        grad_z = [slope_z([field[c, x, zb, inner, :] for zb in blocks]) for c in range(3)]
        for zb in blocks:
            grad_x = [field[c, right, zb, inner, :] - field[c, left, zb, inner, :] for c in range(3)]
            grad_y = [field[c, x, zb, upper, :] - field[c, x, zb, lower, :] for c in range(3)]
            parts = strain_parts(grad_x, grad_y, [grad_z[c][zb] for c in range(3)])
            for i in range(6):
                kept[i, x, zb] = parts[i]
            kept[6, x, zb] = scale * strain_size(parts) if scale != 1.0 else strain_size(parts)

    for x in range(nx):
        keep_strain(vel, x, strains, 1.0)
        for c in range(3):
            fields = [paired(lambda at: vel[c, at, zb, inner, :], x) for zb in blocks]
            for zb, f in enumerate(smooth_z(fields)):
                part[c, x, zb] = f
    for c in range(3):
        rims = [smooth_z([paired(lambda at: ends[c, at, zb], x) for zb in blocks]) for x in range(nx)]
        for x in range(nx):
            for zb in blocks:
                rim = smooth_x(lambda at: rims[at][zb], x)
                filt[c, x, zb, lead - 1 : lead, :] = rim[0:1, :]
                filt[c, x, zb, lead + rows : lead + rows + 1, :] = rim[1:2, :]
                filt[c, x, zb, inner, :] = smooth_x(lambda at: part[c, at, zb], x)
    def filter_z(read, kept, rotate=False):
        if rotate or not on_matrix_unit:
            for x in range(nx):
                fields = [paired(lambda at: read(at, zb), x) for zb in blocks]
                for zb, f in enumerate(smooth_z(fields)):
                    part[kept, x, zb] = f
            return
        half = nx // 2
        for x0 in (0, half):
            fields = [[read((x0 + x) % nx, zb) for zb in blocks] for x in range(half + 1)]
            planes_here = [
                jnp.concatenate([f + g for f, g in zip(fields[x], fields[x + 1])], axis=1)
                for x in range(half)
            ]
            total = times_band(jnp.concatenate(planes_here, axis=0), band)
            for x in range(half):
                for zb in blocks:
                    part[kept, x0 + x, zb] = total[x * rows : (x + 1) * rows, zb * lanes : (zb + 1) * lanes]

    on_matrix_unit = nz <= 256 and rows * nx % 32 == 0 and rows % 8 == 0
    band = band_matrix(nz) if on_matrix_unit else None
    for i, (a, b) in enumerate(((0, 0), (1, 1), (2, 2), (0, 1), (0, 2), (1, 2))):
        filter_z(lambda x, zb: vel[a, x, zb, inner, :] * vel[b, x, zb, inner, :], 3 + i, i % 2 == 1)
        filter_z(lambda x, zb: strains[6, x, zb] * strains[i, x, zb], 9 + i)
    for x in range(nx):
        keep_strain(filt, x, means, 0.25)

    sum_lm = sum_mm = None
    for x in range(nx):
        for zb in blocks:
            v = [filt[c, x, zb, inner, :] for c in range(3)]
            scaled = [0.0625 * f for f in v]
            size = means[6, x, zb]
            for i, (a, b) in enumerate(((0, 0), (1, 1), (2, 2), (0, 1), (0, 2), (1, 2))):
                leonard = smooth_x(lambda at: part[3 + i, at, zb], x) - v[a] * scaled[b]
                model = smooth_x(lambda at: part[9 + i, at, zb], x) - size * means[i, x, zb]
                square = model * model if i < 3 else (0.5 * model) * model
                sum_lm = leonard * model if sum_lm is None else sum_lm + leonard * model
                sum_mm = square if sum_mm is None else sum_mm + square

    coefficient = coefficient_of(
        *(jnp.sum(total, axis=1, keepdims=True) for total in (sum_lm, sum_mm)), nx * nz
    )
    for k in range(count):
        x0, zb = (k // nz_parts) * width, k % nz_parts
        for x in range(width):
            out[to[k], x] = coefficient * strains[6, x0 + x, zb]


def sweep_kernel(parity, back, velocity, tendency, eddy, reduced, factors, tree):
    count, width, rows, _ = back.shape
    length = count * rows // SEGMENTS
    slots = slots_of(back_order(count))

    def fill(rank, place):
        for x in range(width):
            eddy[x, place * rows : (place + 1) * rows, :] = back[slots[rank], x]

    by_parity(parity, count, fill)

    def row(ref, index, j):
        return ref[(*index, pl.ds(j, SEGMENTS, stride=length), slice(None))]

    planes = range(width)
    last_row = length - 1
    visc = [[1.0 + row(eddy, (x,), j) for x in planes] for j in range(length)]
    links = [[750.0 * (v + w) for v, w in zip(visc[j], visc[j + 1])] for j in range(last_row)]

    over = [jnp.ones_like(v) for v in visc[0]]
    under = [jnp.ones_like(v) for v in visc[0]]
    inverses = []
    for j in range(last_row):
        inverses.append([u / (o + e * u) for o, u, e in zip(over, under, links[j])])
        steps = [o * (1.0 / e) for o, e in zip(over, links[j])]
        under, over = (
            [u + t for u, t in zip(under, steps)],
            [(o + u) + t for o, u, t in zip(over, under, steps)],
        )
    inverses.append([u / o for o, u in zip(over, under)])

    value = first = corner = left = None
    reach = [jnp.ones_like(v) for v in visc[0]]
    for j in range(length):
        inverse = inverses[j]
        before = value
        source = [[2.0 * row(velocity, (c, x), j) + row(tendency, (c, x), j) for x in planes] for c in range(3)]
        value = [[f * r for f, r in zip(source[c], inverse)] for c in range(3)]
        if j > 0:
            carry = [e * r for e, r in zip(links[j - 1], inverse)]
            value = [[v + k * w for v, k, w in zip(value[c], carry, before[c])] for c in range(3)]
        left = [m * r for m, r in zip(reach, inverse)]
        if j == 0:
            first, corner = value, left
        else:
            first = [[f + m * v for f, m, v in zip(first[c], reach, value[c])] for c in range(3)]
            corner = [a + m * v for a, m, v in zip(corner, reach, left)]
        ratio = inverse
        if j < last_row:
            ratio = [e * r for e, r in zip(links[j], inverse)]
            reach = [m * r for m, r in zip(reach, ratio)]
        for x in planes:
            for c in range(3):
                factors[x, j, c] = value[c][x]
            factors[x, j, 3] = left[x]
            factors[x, j, 4] = ratio[x]

    def other(fields, step):
        return [pltpu.roll(f, (SEGMENTS - step) % SEGMENTS, 0) if step else f for f in fields]

    last, across, end = value, left, inverse
    seams = [750.0 * (v + w) for v, w in zip(visc[last_row], other(visc[0], 1))]
    level, step = 0, 1
    while step < SEGMENTS:
        link = other(seams, step - 1)
        first_b = [other(f, step) for f in first]
        last_b = [other(f, step) for f in last]
        corner_b, end_b, across_b = other(corner, step), other(end, step), other(across, step)
        stiff = [e / (1.0 + e * (d + a)) for e, d, a in zip(link, end, corner_b)]
        flux = [[k * (g - f) for k, g, f in zip(stiff, last[c], first_b[c])] for c in range(3)]
        from_left = [k * b for k, b in zip(stiff, across)]
        from_right = [k * b for k, b in zip(stiff, across_b)]
        for x in planes:
            for c in range(3):
                tree[x, level, c] = flux[c][x]
            tree[x, level, 3] = from_left[x]
            tree[x, level, 4] = from_right[x]
        first = [[f - b * t for f, b, t in zip(first[c], across, flux[c])] for c in range(3)]
        last = [[g + b * t for g, b, t in zip(last_b[c], across_b, flux[c])] for c in range(3)]
        corner = [a - b * k for a, b, k in zip(corner, across, from_left)]
        end = [d - b * k for d, b, k in zip(end_b, across_b, from_right)]
        across = [k * b for k, b in zip(from_left, across_b)]
        level, step = level + 1, step * 2
    for x in planes:
        rows_out = [f[x][0:1, :] for f in (*first, *last, corner, across, end, visc[0])]
        rows_out.append(visc[last_row][x][SEGMENTS - 1 :, :])
        for i, v in enumerate(rows_out):
            reduced[i * width + x : i * width + x + 1, :] = v


def spread_kernel(factors, tree, velocity, eddy, particular, response, eddy_out, sent):
    write = pltpu.make_async_copy(eddy, eddy_out, sent)
    write.start()
    width, length = factors.shape[:2]
    levels = tree.shape[1]
    sublane = lax.broadcasted_iota(jnp.int32, (SEGMENTS, LANES), 0)
    one, zero = (jnp.full((SEGMENTS, LANES), v, jnp.float32) for v in (1.0, 0.0))
    sides = [(c, zero, zero) for c in range(3)] + [(None, one, zero), (None, zero, one)]
    lefts = [[side[1]] * width for side in sides]
    rights = [[side[2]] * width for side in sides]
    for level in range(levels - 1, -1, -1):
        step = 2**level
        second = lax.rem(sublane, 2 * step) == step
        for n, (c, _, _) in enumerate(sides):
            for x in range(width):
                left, right = lefts[n][x], rights[n][x]
                through = tree[x, level, 3] * left - tree[x, level, 4] * right
                if c is not None:
                    through = tree[x, level, c] + through
                lefts[n][x] = jnp.where(second, pltpu.roll(through, step, 0), left)
                rights[n][x] = jnp.where(second, pltpu.roll(right, step, 0), -through)
    values = rights
    for j in range(length - 1, -1, -1):
        rows = pl.ds(j, SEGMENTS, stride=length)
        for n, (c, _, _) in enumerate(sides):
            for x in range(width):
                value = factors[x, j, 3] * lefts[n][x] + factors[x, j, 4] * values[n][x]
                if c is not None:
                    value = factors[x, j, c] + value
                    particular[c, x, rows, :] = value - velocity[c, x, rows, :]
                else:
                    response[n - 3, x, rows, :] = value
                values[n][x] = value
    write.wait()


def sources_of(step, count):
    return [(i - step) % count for i in range(count)]


def exchange_order(count):
    return range(count - 1, 0, -1)


def spread_kernel(factors, tree, velocity, eddy, particular, response, eddy_out, sent):
    write = pltpu.make_async_copy(eddy, eddy_out, sent)
    write.start()
    width, length = factors.shape[:2]
    levels = tree.shape[1]
    sublane = lax.broadcasted_iota(jnp.int32, (SEGMENTS, LANES), 0)
    one, zero = (jnp.full((SEGMENTS, LANES), v, jnp.float32) for v in (1.0, 0.0))
    sides = [(c, zero, zero) for c in range(3)] + [(None, one, zero), (None, zero, one)]
    lefts = [[side[1]] * width for side in sides]
    rights = [[side[2]] * width for side in sides]
    for level in range(levels - 1, -1, -1):
        step = 2**level
        second = lax.rem(sublane, 2 * step) == step
        for n, (c, _, _) in enumerate(sides):
            for x in range(width):
                left, right = lefts[n][x], rights[n][x]
                through = tree[x, level, 3] * left - tree[x, level, 4] * right
                if c is not None:
                    through = tree[x, level, c] + through
                lefts[n][x] = jnp.where(second, pltpu.roll(through, step, 0), left)
                rights[n][x] = jnp.where(second, pltpu.roll(right, step, 0), -through)
    values = rights
    for j in range(length - 1, -1, -1):
        rows = pl.ds(j, SEGMENTS, stride=length)
        for n, (c, _, _) in enumerate(sides):
            for x in range(width):
                value = factors[x, j, 3] * lefts[n][x] + factors[x, j, 4] * values[n][x]
                if c is not None:
                    value = factors[x, j, c] + value
                    particular[c, x, rows, :] = value - velocity[c, x, rows, :]
                else:
                    response[n - 3, x, rows, :] = value
                values[n][x] = value
    write.wait()


def partner(i, step, count):
    if count & (count - 1) == 0:
        return i ^ step
    return (i - step + count) % count


def finish_kernel(devices, position, particular, response, *rest):
    reduced, (result, gathered, fluxes, out, sent) = rest[:devices], rest[devices:]
    width = particular.shape[1]
    here = position[0]
    for step, ref in zip([0, *exchange_order(devices)], reduced):
        source = sum(jnp.where(here == i, s, 0) for i, s in enumerate(sources_of(step, devices)))
        gathered[source] = ref[...]

    def part(device, i):
        return gathered[device, i * width : (i + 1) * width, :]

    pivots, sources = [], []
    for i in range(devices + 1):
        visc = [part(i - 1, 10)] if i > 0 else []
        total = [part(i - 1, 8)] if i > 0 else []
        source = [part(i - 1, 3 + c) for c in range(3)] if i > 0 else [0.0] * 3
        if i < devices:
            visc.append(part(i, 9))
            total.append(part(i, 6))
            source = [s - part(i, c) for c, s in enumerate(source)]
        pivots.append(sum(total) + 1.0 / (750.0 * sum(visc)))
        sources.append(source)
    across = [part(i, 7) for i in range(devices)]
    minors = [jnp.ones_like(pivots[0]), pivots[0]]
    for i in range(1, devices + 1):
        minors.append(pivots[i] * minors[i] - (across[i - 1] * across[i - 1]) * minors[i - 1])
    inverses = [minors[i] / minors[i + 1] for i in range(devices + 1)]
    ratios = [b * r for b, r in zip(across, inverses)]
    for i in range(1, devices + 1):
        sources[i] = [s + ratios[i - 1] * t for s, t in zip(sources[i], sources[i - 1])]
    for i in range(devices, -1, -1):
        flux_here = [inverses[i] * s for s in sources[i]]
        flux = flux_here if i == devices else [f + ratios[i] * g for f, g in zip(flux_here, flux)]
        for c in range(3):
            fluxes[i, c * width : (c + 1) * width, :] = flux[c]

    writes = []
    for c in range(3):
        for x in range(width):
            r = c * width + x
            left, right = fluxes[here, r : r + 1, :], fluxes[here + 1, r : r + 1, :]
            out[c, x] = particular[c, x] + (response[0, x] * left - response[1, x] * right)
            writes.append(pltpu.make_async_copy(out.at[c, x], result.at[c, x], sent.at[r]))
            writes[-1].start()
    for write in writes:
        write.wait()


def in_vmem(count):
    return [pl.BlockSpec(memory_space=pltpu.VMEM)] * count


def in_hbm(count):
    return [pl.BlockSpec(memory_space=pltpu.HBM)] * count


def in_smem(count):
    return [pl.BlockSpec(memory_space=pltpu.SMEM)] * count


def params():
    return pltpu.CompilerParams(vmem_limit_bytes=VMEM_BYTES)


def swap_chunks(chunks, order):
    return lax.all_to_all(
        chunks, ("gx", "gz"), split_axis=0, concat_axis=0, tiled=True, axis_index_groups=[order]
    )


def body(velocity, tendency):
    _, width, cells, lanes = velocity.shape
    nz_parts = lax.axis_size("gz")
    count = lax.axis_size("gx") * nz_parts
    walls = lax.axis_size("gy")
    rows = cells // count
    nx = lax.axis_size("gx") * width
    padded = 16 + aligned(rows)
    f32 = jnp.float32

    planes = 3 * width
    depth = aligned(planes * rows + 2 * aligned(planes))
    position = lax.axis_index("gy").astype(jnp.int32).reshape(1)
    parity = lax.rem(position, 2)
    chunks = pl.pallas_call(
        functools.partial(pack_kernel, rows),
        out_shape=jax.ShapeDtypeStruct((count, depth, lanes), f32),
        in_specs=in_smem(1) + in_vmem(1),
        out_specs=pl.BlockSpec(memory_space=pltpu.VMEM),
        compiler_params=params(),
        name="pack",
    )(parity, velocity)
    recv = swap_chunks(chunks, out_order(count))
    slot = lax.slice_in_dim(recv, planes * rows, planes * rows + aligned(planes), axis=1)
    swapped = lax.ppermute(slot, ("gy", "gx", "gz"), swap_pairs(walls, count))
    rank = lax.axis_index(("gx", "gz")).astype(jnp.int32).reshape(1)
    chunk_shape = jax.ShapeDtypeStruct((count, width, rows, lanes), f32)
    cells_here = nx * nz_parts * rows * lanes
    provisional = pl.pallas_call(
        functools.partial(germano_kernel, nz_parts, width, rows, walls),
        out_shape=chunk_shape,
        in_specs=in_smem(2) + in_vmem(1),
        out_specs=pl.BlockSpec(memory_space=pltpu.VMEM),
        scratch_shapes=[
            pltpu.VMEM((3, nx, nz_parts, padded, lanes), f32),
            pltpu.VMEM((3, nx, nz_parts, padded, lanes), f32),
            pltpu.VMEM((3, nx, nz_parts, 8, lanes), f32),
            pltpu.VMEM((7, nx, nz_parts, rows, lanes), f32),
            pltpu.VMEM((7, nx, nz_parts, rows, lanes), f32),
            pltpu.VMEM((15, nx, nz_parts, rows, lanes), f32),
        ],
        compiler_params=params(),
        cost_estimate=pl.CostEstimate(
            flops=300 * cells_here, bytes_accessed=16 * cells_here, transcendentals=2 * cells_here
        ),
        name="germano",
    )(rank, position, recv)
    eddy_chunks = pl.pallas_call(
        functools.partial(edge_kernel, nz_parts, width, rows, walls),
        out_shape=chunk_shape,
        in_specs=in_smem(2) + in_vmem(3),
        out_specs=pl.BlockSpec(memory_space=pltpu.VMEM),
        scratch_shapes=[pltpu.VMEM((3, 3, nx, nz_parts * lanes), f32)],
        input_output_aliases={4: 0},
        compiler_params=params(),
        name="edge",
    )(rank, position, recv, swapped, provisional)
    back = swap_chunks(eddy_chunks, back_order(count))

    length = cells // SEGMENTS
    levels = SEGMENTS.bit_length() - 1
    packed = aligned(11 * width)
    eddy_here, reduced, factors, tree = pl.pallas_call(
        sweep_kernel,
        out_shape=(
            jax.ShapeDtypeStruct((width, cells, lanes), f32),
            jax.ShapeDtypeStruct((packed, lanes), f32),
            jax.ShapeDtypeStruct((width, length, 5, SEGMENTS, lanes), f32),
            jax.ShapeDtypeStruct((width, levels, 5, SEGMENTS, lanes), f32),
        ),
        in_specs=in_smem(1) + in_vmem(3),
        out_specs=tuple(in_vmem(4)),
        compiler_params=params(),
        name="sweep",
    )(parity, back, velocity, tendency)

    others = [
        lax.ppermute(reduced, "gy", [(s, i) for i, s in enumerate(sources_of(step, walls))])
        for step in exchange_order(walls)
    ]
    particular, response, eddy = pl.pallas_call(
        spread_kernel,
        out_shape=(
            jax.ShapeDtypeStruct(velocity.shape, f32),
            jax.ShapeDtypeStruct((2, *velocity.shape[1:]), f32),
            jax.ShapeDtypeStruct(eddy_here.shape, f32),
        ),
        in_specs=in_vmem(4),
        out_specs=tuple(in_vmem(2) + in_hbm(1)),
        scratch_shapes=[pltpu.SemaphoreType.DMA],
        compiler_params=params(),
        cost_estimate=pl.CostEstimate(
            flops=20 * velocity.size, bytes_accessed=16 * velocity.size, transcendentals=0
        ),
        name="spread",
    )(factors, tree, velocity, eddy_here)
    new_velocity = pl.pallas_call(
        functools.partial(finish_kernel, walls),
        out_shape=jax.ShapeDtypeStruct(velocity.shape, f32),
        in_specs=in_smem(1) + in_vmem(2 + walls),
        out_specs=in_hbm(1)[0],
        scratch_shapes=[
            pltpu.VMEM((walls, packed, lanes), f32),
            pltpu.VMEM((walls + 1, aligned(3 * width), lanes), f32),
            pltpu.VMEM(velocity.shape, f32),
            pltpu.SemaphoreType.DMA((planes,)),
        ],
        compiler_params=params(),
        name="finish",
    )(position, particular, response, reduced, *others)
    return (new_velocity, eddy)


def solution(mesh):
    return jax.shard_map(
        body,
        mesh=mesh,
        in_specs=(P(None, "gx", "gy", "gz"), P(None, "gx", "gy", "gz")),
        out_specs=(P(None, "gx", "gy", "gz"), P("gx", "gy", "gz")),
        check_vma=False,
    )
```
